32 devices in a mesh: dp: 2 (over y), seq: 4 (over z), tensor: 4 (over x, core).
Axes of the slice: x: 2, y: 2, z: 4, core: 2. Of those that a mesh axis runs over, the one named last changes fastest.
Arguments:
- tokens: bfloat16 [4, 2048, 1536], P('dp', 'seq'), may hold values from -6 to 6
- lengths: int32 [4, 8], P('dp'), may hold values from 1 to 1024, 2048 in all within a row
- cotangent: bfloat16 [4, 2048, 1536], P('dp', 'seq'), may hold values from -6 to 6
- q_weight: bfloat16 [1536, 1536], P(None, 'tensor'), may hold values from -0.15625 to 0.15625
- q_bias: bfloat16 [1536], P('tensor'), may hold values from -3 to 3
- k_weight: bfloat16 [1536, 256], replicated, may hold values from -0.15625 to 0.15625
- k_bias: bfloat16 [256], replicated, may hold values from -3 to 3
- v_weight: bfloat16 [1536, 256], replicated, may hold values from -0.15625 to 0.15625
- v_bias: bfloat16 [256], replicated, may hold values from -3 to 3
- o_weight: bfloat16 [1536, 1536], P(None, 'tensor'), may hold values from -0.625 to 0.625
- attn_gain: bfloat16 [1536], replicated, may hold values from 0.099609375 to 1.8984375
- ffn_gain: bfloat16 [1536], replicated, may hold values from 0.099609375 to 1.8984375
- gate_weight: bfloat16 [1536, 8960], P(None, 'tensor'), may hold values from -0.15625 to 0.15625
- up_weight: bfloat16 [1536, 8960], P(None, 'tensor'), may hold values from -0.15625 to 0.15625
- down_weight: bfloat16 [1536, 8960], P(None, 'tensor'), may hold values from -0.0625 to 0.0625
Outputs:
- layer_out: bfloat16 [4, 2048, 1536], P('dp', 'seq')
- token_grad: float32 [4, 2048, 1536], P('dp', 'seq')
- q_weight_grad: float32 [1536, 1536], P(('dp', 'seq'), 'tensor')
- q_bias_grad: float32 [1536], replicated
- k_weight_grad: float32 [1536, 256], P(('dp', 'seq', 'tensor'))
- k_bias_grad: float32 [256], replicated
- v_weight_grad: float32 [1536, 256], P(('dp', 'seq', 'tensor'))
- v_bias_grad: float32 [256], replicated
- o_weight_grad: float32 [1536, 1536], P(('dp', 'seq'), 'tensor')
- attn_gain_grad: float32 [1536], P(('dp', 'seq'))
- ffn_gain_grad: float32 [1536], P(('dp', 'seq'))
- gate_weight_grad: float32 [1536, 8960], P(('dp', 'seq'), 'tensor')
- up_weight_grad: float32 [1536, 8960], P(('dp', 'seq'), 'tensor')
- down_weight_grad: float32 [1536, 8960], P(('dp', 'seq'), 'tensor')
The draws below stay inside these ranges and needn't reach their ends.
Inputs may be any that keep to these rules, and one draw needn't show every extreme that they name: Each row's entries are its document lengths in order followed by its padding tail; they sum to 2048, and every row's length list contains an entry equal to 1024, its largest.
All inputs are finite; a program needn't handle non-finite values.
Results may differ from the reference program's by a relative error of at most 0.025.
Values may be sent and summed in bfloat16 or wider, within the bound.
No kernel may reach another device: no remote copies, remote signals or barrier semaphores. Data moves between devices by JAX's collectives and lax.ppermute only.
A program may use at most 256 MiB of HBM per device.

```python
import math
import jax
import jax.numpy as jnp
import numpy as np
from jax import lax

D = 1536
H = 12
KVH = 2
HD = 128
FF = 8960
LEN = 2048
SLOTS = 8
MOST = 1024
ROWS = 4


def level_of(own_key, dims, cuts, least, largest):
    factor_of, own = 1.0, jax.random.fold_in(own_key, 6)
    for dim, shards_of in cuts:
        draws = jnp.exp(jax.random.uniform(jax.random.fold_in(own, dim), (shards_of,), jnp.float32, least / len(cuts), largest / len(cuts)))
        factor_of = factor_of * jnp.repeat(draws, dims[dim] // shards_of).reshape([-1 if axis == dim else 1 for axis in range(len(dims))])
    return factor_of


def split_up(count, total, bound, lean):
    portions = [(1 << 20) // math.isqrt(grade ** lean) + 1 for grade in range(2, count + 1)]
    rest, counts = total - bound - (count - 1), [1] * (count - 1)
    while rest > 0:
        free = [i for i in range(count - 1) if counts[i] < bound]
        pool, budget = sum([portions[i] for i in free]), rest
        for i in free:
            extra = min(bound - counts[i], max(1, budget * portions[i] // pool), rest)
            counts[i] = counts[i] + extra
            rest = rest - extra
    return np.array([bound] + counts)


def uneven(own_key, count, total, reach, skew):
    if count == 2:
        one = jax.random.randint(own_key, (), max(1, total - reach), min(reach, total - 1) + 1)
        return jnp.stack([one, total - one])
    tallies = jnp.asarray(split_up(count, total, reach, skew), jnp.int32)
    twos = (count - 1) // 2
    giver, receiver = tallies[1:1 + 2 * twos:2], tallies[2:2 + 2 * twos:2]
    room = jnp.minimum(giver - 1, reach - receiver)
    shifted = jax.random.randint(jax.random.fold_in(own_key, 1), (twos,), 0, 1 << 20) % (room + 1)
    tallies = tallies.at[1:1 + 2 * twos:2].set(giver - shifted).at[2:2 + 2 * twos:2].set(receiver + shifted)
    return tallies[jax.random.permutation(jax.random.fold_in(own_key, 2), count)]


def normal_values(own_key, shape, scale, limit, shards=(), kind=jnp.bfloat16):
    factor_of = level_of(own_key, shape, shards, -0.22, 0.18) if shards else 1.0
    drawn = jax.random.normal(own_key, shape, jnp.float32) * scale * factor_of
    return jnp.minimum(jnp.maximum(drawn, -limit), limit).astype(kind)


def setup_inputs(seed: int = 0) -> dict:
    arg_keys = jax.random.split(jax.random.key(seed), 16)
    return {
        "tokens": normal_values(arg_keys[0], (ROWS, LEN, D), 1.0, 6.0, ((0, 2), (1, 4))),
        "lengths": jax.vmap(lambda own: uneven(own, SLOTS, LEN, MOST, 2))(jax.random.split(arg_keys[1], ROWS)).reshape((ROWS, SLOTS)).astype(jnp.int32),
        "cotangent": normal_values(arg_keys[2], (ROWS, LEN, D), 1.0, 6.0, ((0, 2), (1, 4))),
        "q_weight": normal_values(arg_keys[3], (D, H * HD), D ** -0.5, 0.15625, ((1, 4),)),
        "q_bias": normal_values(arg_keys[4], (H * HD,), 0.5, 3.0, ((0, 4),)),
        "k_weight": normal_values(arg_keys[5], (D, KVH * HD), D ** -0.5, 0.15625),
        "k_bias": normal_values(arg_keys[6], (KVH * HD,), 0.5, 3.0),
        "v_weight": normal_values(arg_keys[7], (D, KVH * HD), D ** -0.5, 0.15625),
        "v_bias": normal_values(arg_keys[8], (KVH * HD,), 0.5, 3.0),
        "o_weight": normal_values(arg_keys[9], (D, H * HD), (H * HD // 16) ** -0.5, 0.625, ((1, 4),)),
        "attn_gain": jnp.clip(1.0 + 0.18 * jax.random.normal(arg_keys[10], (D,), jnp.float32), 0.099609375, 1.8984375).astype(jnp.bfloat16),
        "ffn_gain": jnp.clip(1.0 + 0.18 * jax.random.normal(arg_keys[11], (D,), jnp.float32), 0.099609375, 1.8984375).astype(jnp.bfloat16),
        "gate_weight": normal_values(arg_keys[12], (D, FF), D ** -0.5, 0.15625, ((1, 4),)),
        "up_weight": normal_values(arg_keys[13], (D, FF), D ** -0.5, 0.15625, ((1, 4),)),
        "down_weight": normal_values(arg_keys[14], (D, FF), FF ** -0.5, 0.0625, ((1, 4),)),
    }


EPS = 1e-06
ROPE_BASE = 10000.0
NEG_FILL = -1e+30

@jax.custom_vjp
def low(v):
    return lax.optimization_barrier(v.astype(jnp.bfloat16)).astype(jnp.float32)

@jax.custom_vjp
def low_back(v):
    return v

def low_keep(v):
    return (low(v), None)

def low_pass(kept, grad):
    return (grad,)

def back_keep(v):
    return (v, None)

def back_low(kept, grad):
    return (low(grad),)
low.defvjp(low_keep, low_pass)
low_back.defvjp(back_keep, back_low)

def doc_tables(lengths, span):
    ends = jnp.cumsum(lengths, axis=1).astype(jnp.int32)
    starts = ends - lengths
    places = jnp.arange(span, dtype=jnp.int32)
    segment = lax.optimization_barrier(jnp.sum((places[None, :, None] >= ends[:, None, :]).astype(jnp.int32), axis=2))
    slot_ids = jnp.arange(lengths.shape[1], dtype=jnp.int32)
    member = segment[:, :, None] == slot_ids[None, None, :]
    first = lax.optimization_barrier(jnp.sum(jnp.where(member, starts[:, None, :], jnp.zeros_like(starts[:, None, :])), axis=2))
    position = places[None, :] - first
    valid = (segment < lengths.shape[1] - 1).astype(jnp.float32)
    return (segment, position, valid)

def rope_tables(position):
    half = HD // 2
    freqs = ROPE_BASE ** (-(jnp.arange(half, dtype=jnp.float32) * 2.0) / HD)
    angles = position.astype(jnp.float32)[..., None] * freqs
    cosine = jnp.cos(angles)
    sine = jnp.sin(angles)
    return (jnp.concatenate([cosine, cosine], -1), jnp.concatenate([sine, sine], -1))

def rotate(value, cosine, sine):
    half = value.shape[-1] // 2
    turned = jnp.concatenate([-value[..., half:], value[..., :half]], axis=-1)
    return value * cosine + turned * sine

def highest(left, right):
    return jnp.dot(left, right, precision=lax.Precision.HIGHEST)

def rms(value):
    return value * lax.rsqrt(lax.optimization_barrier(jnp.mean(value * value, axis=-1, keepdims=True)) + EPS)

def attend(item):
    q_row, k_row, v_row, segment = item
    places = jnp.arange(LEN, dtype=jnp.int32)
    allowed = (segment[:, None] == segment[None, :]) & (places[:, None] >= places[None, :])
    keys = jnp.repeat(k_row, H // KVH, axis=1)
    values = jnp.repeat(v_row, H // KVH, axis=1)
    raw = jnp.einsum('qhd,khd->hqk', q_row, keys, precision=lax.Precision.HIGHEST)
    scores = low_back(raw * (1.0 / math.sqrt(HD)))
    scores = jnp.where(allowed[None], scores, NEG_FILL)
    top = lax.optimization_barrier(jnp.max(scores, axis=-1, keepdims=True))
    expo = jnp.exp(scores - top)
    probs = expo / lax.optimization_barrier(jnp.sum(expo, axis=-1, keepdims=True))
    mixed = jnp.einsum('hqk,khd->qhd', low(probs), values, precision=lax.Precision.HIGHEST)
    return low(low_back(mixed))

def layer(inputs, q_weight, q_bias, k_weight, k_bias, v_weight, v_bias, o_weight, attn_gain, ffn_gain, gate_weight, up_weight, down_weight, segment, cosine, sine):
    count = inputs.shape[0]
    h_one = low(rms(inputs) * attn_gain)
    q_lin = low_back(highest(h_one, q_weight) + q_bias)
    k_lin = low_back(highest(h_one, k_weight) + k_bias)
    v_lin = low_back(highest(h_one, v_weight) + v_bias)
    cos_four = cosine[:, :, None, :]
    sin_four = sine[:, :, None, :]
    q_rot = low(rotate(q_lin.reshape(count, LEN, H, HD), cos_four, sin_four))
    k_rot = low(rotate(k_lin.reshape(count, LEN, KVH, HD), cos_four, sin_four))
    v_val = low(v_lin.reshape(count, LEN, KVH, HD))
    mixed = lax.map(jax.checkpoint(attend), (q_rot, k_rot, v_val, segment))
    branch = low_back(highest(mixed.reshape(count, LEN, H * HD), o_weight.T))
    middle = inputs + branch
    h_two = low(rms(middle) * ffn_gain)
    gate_lin = low_back(highest(h_two, gate_weight))
    up_lin = low_back(highest(h_two, up_weight))
    hidden = low(gate_lin * jax.nn.sigmoid(gate_lin) * up_lin)
    return middle + low_back(highest(hidden, down_weight.T))

def reference(tokens, lengths, cotangent, q_weight, q_bias, k_weight, k_bias, v_weight, v_bias, o_weight, attn_gain, ffn_gain, gate_weight, up_weight, down_weight):
    segment, position, valid = doc_tables(lengths, LEN)
    cosine, sine = rope_tables(position)
    floats = [item.astype(jnp.float32) for item in (tokens, q_weight, q_bias, k_weight, k_bias, v_weight, v_bias, o_weight, attn_gain, ffn_gain, gate_weight, up_weight, down_weight)]

    def forward(*params):
        return layer(*params, segment, cosine, sine)
    result, pull = jax.vjp(forward, *floats)
    grads = pull(cotangent.astype(jnp.float32) * valid[:, :, None])
    return (result.astype(jnp.bfloat16), grads[0], grads[1], grads[2], grads[3], grads[4], grads[5], grads[6], grads[7], grads[8], grads[9], grads[10], grads[11], grads[12])
```

```python
import functools
import math

import jax
import jax.numpy as jnp
from jax import lax
from jax.experimental import pallas as pl
from jax.experimental.pallas import tpu as pltpu
from jax.sharding import PartitionSpec as P

KVH = 2
HD = 128
MOST = 1024
EPS = 1e-06
ROPE_BASE = 10000.0
NEG_FILL = -1e30
Q_BLOCK = 256
K_BLOCK = 256
MIB = 1 << 20
SCALE = 1.0 / math.sqrt(HD)


def to_bf(value):
    return value.astype(jnp.bfloat16)


def to_f(value):
    return value.astype(jnp.float32)


def dot(left, right, left_dim=1, right_dim=0):
    return lax.dot_general(
        left,
        right,
        (((left_dim,), (right_dim,)), ((), ())),
        preferred_element_type=jnp.float32,
    )


def flipped(axis, bit):
    return [(i, i ^ (1 << bit)) for i in range(lax.axis_size(axis))]


def core_swap(value):
    return lax.ppermute(value, "tensor", flipped("tensor", 0))


def chip_swap(value):
    return lax.ppermute(value, "tensor", flipped("tensor", 1))


def shifted(value, hops):
    count = lax.axis_size("seq")
    route = [(i, i + hops) for i in range(count) if 0 <= i + hops < count]
    return lax.ppermute(value, "seq", route)


def first_kernel(core_ref, tok_ref, gain_ref, w_ref, b_ref, cos_ref, sin_ref, h_ref, q_ref, kv_ref):
    x = to_f(tok_ref[...])
    factor = lax.rsqrt(jnp.mean(x * x, axis=-1, keepdims=True) + EPS)
    h = to_bf(x * factor * gain_ref[...])
    h_ref[...] = h
    lin = dot(h, w_ref[...]) + b_ref[...]
    cosine = cos_ref[...]
    sine = sin_ref[...]
    heads = q_ref.shape[1] // HD
    for head in range(heads):
        part = lin[:, head * HD : (head + 1) * HD]
        q_ref[:, head * HD : (head + 1) * HD] = to_bf(
            part * cosine + pltpu.roll(part, HD // 2, 1) * sine
        )
    part = lin[:, heads * HD :]
    is_key = core_ref[0] == 0
    kv_ref[...] = to_bf(
        part * jnp.where(is_key, cosine, 1.0)
        + pltpu.roll(part, HD // 2, 1) * jnp.where(is_key, sine, 0.0)
    )


def first(core, tokens, gain, weight, bias, cosine, sine):
    total, width = tokens.shape
    columns = weight.shape[1]
    block = total // 4
    half = 2

    def flip(i, core_ref):
        return (lax.rem(i + core_ref[0] * half, 4), 0)

    def at(i, core_ref):
        return (i, 0)

    def whole(i, core_ref):
        return (0, 0)

    return pl.pallas_call(
        first_kernel,
        grid_spec=pltpu.PrefetchScalarGridSpec(
            num_scalar_prefetch=1,
            grid=(4,),
            in_specs=[
                pl.BlockSpec((block, width), flip),
                pl.BlockSpec((1, width), whole),
                pl.BlockSpec((width, columns), whole),
                pl.BlockSpec((1, columns), whole),
                pl.BlockSpec((block, HD), at),
                pl.BlockSpec((block, HD), at),
            ],
            out_specs=[
                pl.BlockSpec((block, width), at),
                pl.BlockSpec((block, columns - HD), at),
                pl.BlockSpec((block, HD), at),
            ],
        ),
        out_shape=[
            jax.ShapeDtypeStruct((total, width), jnp.bfloat16),
            jax.ShapeDtypeStruct((total, columns - HD), jnp.bfloat16),
            jax.ShapeDtypeStruct((total, HD), jnp.bfloat16),
        ],
        compiler_params=pltpu.CompilerParams(vmem_limit_bytes=24 * MIB),
        cost_estimate=pl.CostEstimate(
            flops=2 * total * width * columns, bytes_accessed=9 * MIB, transcendentals=0
        ),
        name="first",
    )(core, tokens, gain, weight, bias, cosine, sine)


def stacked(ref, start, count, heads):
    return jnp.concatenate(
        [ref[0, pl.ds(start, count), h * HD : (h + 1) * HD] for h in range(heads)], axis=0
    )


def bounds(start_ref, index, heads, reach):
    first_key = jnp.concatenate(
        [start_ref[0, :, pl.ds(index * Q_BLOCK, Q_BLOCK)]] * heads, axis=1
    )
    place = reach + index * Q_BLOCK + lax.broadcasted_iota(jnp.int32, (1, Q_BLOCK), 1)
    return first_key, jnp.concatenate([place] * heads, axis=1)


def attend_kernel(heads, blocks, reach, low_ref, q_ref, k_ref, v_ref, start_ref, o_ref, lse_ref, acc):
    row = pl.program_id(0)
    wide = heads * Q_BLOCK
    for index in range(blocks):
        q = stacked(q_ref, index * Q_BLOCK, Q_BLOCK, heads)
        first_key, place = bounds(start_ref, index, heads, reach)
        acc[...] = jnp.zeros_like(acc)

        def step(j, carry):
            top, total = carry
            keys = pl.ds(pl.multiple_of(j * K_BLOCK, K_BLOCK), K_BLOCK)
            s = dot(k_ref[0, keys], q, 1, 1) * SCALE
            key = j * K_BLOCK + lax.broadcasted_iota(jnp.int32, (K_BLOCK, wide), 0)
            s = jnp.where((key >= first_key) & (key <= place), s, NEG_FILL)
            later = jnp.maximum(top, jnp.max(s, axis=0, keepdims=True))
            p = jnp.exp(s - later)
            fade = jnp.exp(top - later)
            total = total * fade + jnp.sum(p, axis=0, keepdims=True)
            acc[...] = acc[...] * fade + dot(v_ref[0, keys], to_bf(p), 0, 0)
            return later, total

        last = (reach + (index + 1) * Q_BLOCK - 1) // K_BLOCK + 1
        top, total = lax.fori_loop(
            low_ref[row, index],
            last,
            step,
            (jnp.full((1, wide), NEG_FILL, jnp.float32), jnp.zeros((1, wide), jnp.float32)),
        )
        out = to_bf((acc[...] / total).T)
        for h in range(heads):
            o_ref[0, index * Q_BLOCK : (index + 1) * Q_BLOCK, h * HD : (h + 1) * HD] = out[
                h * Q_BLOCK : (h + 1) * Q_BLOCK
            ]
        lse_ref[0, index : index + 1, :] = top + jnp.log(total)


def attend(low, q, k, v, start, reach):
    rows, local, columns = q.shape
    window = k.shape[1]
    heads = columns // HD
    blocks = local // Q_BLOCK

    def at(i, low_ref):
        return (i, 0, 0)

    return pl.pallas_call(
        functools.partial(attend_kernel, heads, blocks, reach),
        grid_spec=pltpu.PrefetchScalarGridSpec(
            num_scalar_prefetch=1,
            grid=(rows,),
            in_specs=[
                pl.BlockSpec((1, local, columns), at),
                pl.BlockSpec((1, window, HD), at),
                pl.BlockSpec((1, window, HD), at),
                pl.BlockSpec((1, 1, local), at),
            ],
            out_specs=[
                pl.BlockSpec((1, local, columns), at),
                pl.BlockSpec((1, blocks, heads * Q_BLOCK), at),
            ],
            scratch_shapes=[pltpu.VMEM((HD, heads * Q_BLOCK), jnp.float32)],
        ),
        out_shape=[
            jax.ShapeDtypeStruct((rows, local, columns), jnp.bfloat16),
            jax.ShapeDtypeStruct((rows, blocks, heads * Q_BLOCK), jnp.float32),
        ],
        compiler_params=pltpu.CompilerParams(vmem_limit_bytes=24 * MIB),
        cost_estimate=pl.CostEstimate(
            flops=12_000_000_000, bytes_accessed=4 * MIB, transcendentals=rows * local * window
        ),
        name="attend",
    )(low, q, k, v, start)


def attend_back_kernel(
    heads, blocks, reach, low_ref, core_ref, q_ref, k_ref, v_ref, g_ref, o_ref, lse_ref, start_ref, cos_ref,
    sin_ref, gq_ref, both_ref, acc, gk, gv
):
    row = pl.program_id(0)
    wide = heads * Q_BLOCK
    gk[...] = jnp.zeros_like(gk)
    gv[...] = jnp.zeros_like(gv)
    for index in range(blocks):
        q = stacked(q_ref, index * Q_BLOCK, Q_BLOCK, heads)
        g = stacked(g_ref, index * Q_BLOCK, Q_BLOCK, heads)
        o = stacked(o_ref, index * Q_BLOCK, Q_BLOCK, heads)
        inner = jnp.sum((to_f(g) * to_f(o)).T, axis=0, keepdims=True)
        lse = lse_ref[0, index : index + 1, :]
        first_key, place = bounds(start_ref, index, heads, reach)
        acc[...] = jnp.zeros_like(acc)

        def step(j, carry):
            keys = pl.ds(pl.multiple_of(j * K_BLOCK, K_BLOCK), K_BLOCK)
            k = k_ref[0, keys]
            s = dot(k, q, 1, 1) * SCALE
            key = j * K_BLOCK + lax.broadcasted_iota(jnp.int32, (K_BLOCK, wide), 0)
            p = jnp.where((key >= first_key) & (key <= place), jnp.exp(s - lse), 0.0)
            gp = dot(v_ref[0, keys], g, 1, 1)
            gs = to_bf(p * (gp - inner))
            gv[keys] += dot(to_bf(p), g)
            gk[keys] += dot(gs, q)
            acc[...] += dot(k, gs, 0, 0)
            return carry

        last = (reach + (index + 1) * Q_BLOCK - 1) // K_BLOCK + 1
        lax.fori_loop(low_ref[row, index], last, step, 0)
        gq = acc[...].T * SCALE
        here = slice(index * Q_BLOCK, (index + 1) * Q_BLOCK)
        cosine, sine = cos_ref[0, here], sin_ref[0, here]
        for h in range(heads):
            part = gq[h * Q_BLOCK : (h + 1) * Q_BLOCK]
            gq_ref[0, here, h * HD : (h + 1) * HD] = to_bf(
                part * cosine + pltpu.roll(part * sine, HD // 2, 1)
            )
    core = core_ref[0]
    both_ref[core, 0] = to_bf(gk[...] * SCALE)
    both_ref[1 - core, 0] = to_bf(gv[...])


def attend_back(low, core, q, k, v, grad, out, lse, start, cosine, sine, reach):
    rows, local, columns = q.shape
    window = k.shape[1]
    heads = columns // HD
    blocks = local // Q_BLOCK

    def at(i, *refs):
        return (i, 0, 0)

    return pl.pallas_call(
        functools.partial(attend_back_kernel, heads, blocks, reach),
        grid_spec=pltpu.PrefetchScalarGridSpec(
            num_scalar_prefetch=2,
            grid=(rows,),
            in_specs=[
                pl.BlockSpec((1, local, columns), at),
                pl.BlockSpec((1, window, HD), at),
                pl.BlockSpec((1, window, HD), at),
                pl.BlockSpec((1, local, columns), at),
                pl.BlockSpec((1, local, columns), at),
                pl.BlockSpec((1, blocks, heads * Q_BLOCK), at),
                pl.BlockSpec((1, 1, local), at),
                pl.BlockSpec((1, local, HD), at),
                pl.BlockSpec((1, local, HD), at),
            ],
            out_specs=[
                pl.BlockSpec((1, local, columns), at),
                pl.BlockSpec((2, 1, window, HD), lambda i, *refs: (0, i, 0, 0)),
            ],
            scratch_shapes=[
                pltpu.VMEM((HD, heads * Q_BLOCK), jnp.float32),
                pltpu.VMEM((window, HD), jnp.float32),
                pltpu.VMEM((window, HD), jnp.float32),
            ],
        ),
        out_shape=[
            jax.ShapeDtypeStruct((rows, local, columns), jnp.bfloat16),
            jax.ShapeDtypeStruct((2, rows, window, HD), jnp.bfloat16),
        ],
        compiler_params=pltpu.CompilerParams(vmem_limit_bytes=24 * MIB),
        cost_estimate=pl.CostEstimate(
            flops=20_000_000_000, bytes_accessed=6 * MIB, transcendentals=rows * local * window
        ),
        name="attend_back",
    )(low, core, q, k, v, grad, out, lse, start, cosine, sine)


def gated_kernel(h_ref, gh_ref, gw_ref, uw_ref, hid_ref, gg_ref, gu_ref):
    h = h_ref[...]
    gate = dot(h, gw_ref[...])
    up = dot(h, uw_ref[...])
    grad = to_f(gh_ref[...])
    sigma = 1.0 / (1.0 + jnp.exp(-gate))
    swish = gate * sigma
    hid_ref[...] = to_bf(swish * up)
    gu_ref[...] = to_bf(grad * swish)
    gg_ref[...] = to_bf(grad * up * sigma * (1.0 + gate * (1.0 - sigma)))


def gated(h, grad_hidden, gate_weight, up_weight):
    total, width = h.shape
    hidden = gate_weight.shape[1]
    tile = 256
    steps = pl.cdiv(hidden, tile)
    column = pl.BlockSpec((total, tile), lambda i: (0, i))
    weight = pl.BlockSpec((width, tile), lambda i: (0, i))
    shape = jax.ShapeDtypeStruct((total, hidden), jnp.bfloat16)
    return pl.pallas_call(
        gated_kernel,
        grid=(steps,),
        in_specs=[pl.BlockSpec((total, width), lambda i: (0, 0)), column, weight, weight],
        out_specs=[column] * 3,
        out_shape=[shape] * 3,
        compiler_params=pltpu.CompilerParams(vmem_limit_bytes=40 * MIB),
        cost_estimate=pl.CostEstimate(
            flops=4 * total * width * hidden, bytes_accessed=45 * MIB, transcendentals=total * hidden
        ),
        name="gated",
    )(h, grad_hidden, gate_weight, up_weight)


def tensor_sum(half_of):
    sent = core_swap(to_bf(half_of(1, None)))
    mine = to_bf(half_of(0, sent))
    return to_f(mine) + to_f(chip_swap(mine))


def rows_sum(left, right, dp_index, extra=None):
    count = lax.axis_size("dp")
    width = left.shape[1]
    if count != 2:
        whole = to_bf(dot(left, right, 0, 0))
        if extra is not None:
            share = jnp.concatenate(
                [whole.reshape(count, width // count, -1), jnp.broadcast_to(extra, (count,) + extra.shape)], axis=1
            )
            return lax.psum_scatter(share, "dp", scatter_dimension=0, tiled=False)
        return lax.psum_scatter(whole, "dp", scatter_dimension=0, tiled=True)
    part = width // 2
    other = lax.dynamic_slice_in_dim(left, (1 - dp_index) * part, part, 1)
    own = lax.dynamic_slice_in_dim(left, dp_index * part, part, 1)
    send = to_bf(dot(other, right, 0, 0))
    if extra is not None:
        send = jnp.concatenate([send, extra], axis=0)
    come = lax.ppermute(send, "dp", flipped("dp", 0))
    total = to_bf(dot(own, right, 0, 0) + to_f(come[:part]))
    if extra is not None:
        total = jnp.concatenate([total, to_bf(to_f(extra) + to_f(come[part:]))], axis=0)
    return total


def seq_scatter(value):
    return to_f(lax.psum_scatter(value, "seq", scatter_dimension=0, tiled=True))


def body(
    tokens,
    lengths,
    cotangent,
    q_weight,
    q_bias,
    k_weight,
    k_bias,
    v_weight,
    v_bias,
    o_weight,
    attn_gain,
    ffn_gain,
    gate_weight,
    up_weight,
    down_weight,
):
    rows, local, width = tokens.shape
    total = rows * local
    half = total // 2
    heads = q_weight.shape[1] // HD
    ranks = lax.axis_size("tensor")
    seqs = lax.axis_size("seq")
    rank = lax.axis_index("tensor")
    dp_index = lax.axis_index("dp")
    seq_index = lax.axis_index("seq")
    core = lax.rem(rank, 2)
    head = lax.div(rank, 2)
    core_one = core.reshape(1)
    hops = min(seqs - 1, -(-(MOST - 1) // local))
    reach = hops * local

    def own_first(value):
        turned = jnp.concatenate([value[rows // 2 :], value[: rows // 2]], axis=0)
        return jnp.where(core == 0, value, turned)

    slots = jnp.arange(lengths.shape[1], dtype=jnp.int32)
    lens = own_first(lengths)
    ends = jnp.sum(jnp.where(slots[None, :] <= slots[:, None], lens[:, None, :], 0), axis=2)
    place = seq_index * local + jnp.arange(local, dtype=jnp.int32)
    begun = jnp.max(
        jnp.where(ends[:, None, :] <= place[None, :, None], ends[:, None, :], 0), axis=2
    )
    valid = to_f(place[None, :] < ends[:, -2:-1])
    position = (place[None, :] - begun).reshape(total, 1)
    freqs = ROPE_BASE ** (-(jnp.arange(HD // 2, dtype=jnp.float32) * 2.0) / HD)
    angles = to_f(position) * freqs[None, :]
    cosine, sine = jnp.cos(angles), jnp.sin(angles)
    cosine = jnp.concatenate([cosine, cosine], axis=1)
    sine = jnp.concatenate([-sine, sine], axis=1)
    start = begun - (seq_index * local - reach)
    low = jnp.maximum(lax.div(jnp.maximum(start[:, ::Q_BLOCK], 0), K_BLOCK), 0)
    start = start.reshape(rows, 1, local)

    key_side = core == 0
    kv_weight = jnp.where(
        key_side,
        lax.dynamic_slice_in_dim(k_weight, head * HD, HD, 1),
        lax.dynamic_slice_in_dim(v_weight, head * HD, HD, 1),
    )
    kv_bias = jnp.where(
        key_side,
        lax.dynamic_slice_in_dim(k_bias, head * HD, HD, 0),
        lax.dynamic_slice_in_dim(v_bias, head * HD, HD, 0),
    )
    weight = jnp.concatenate([q_weight, kv_weight], axis=1)
    bias = to_f(jnp.concatenate([q_bias, kv_bias])).reshape(1, -1)
    gain_one = to_f(attn_gain).reshape(1, width)
    gain_two = to_f(ffn_gain).reshape(1, width)

    h_one, q_rot, kv = first(
        core_one, tokens.reshape(total, width), gain_one, weight, bias, cosine, sine
    )
    kv = kv.reshape(rows, local, HD)
    span = jnp.concatenate([shifted(kv, h) for h in range(hops, 0, -1)] + [kv], axis=1)
    mate = core_swap(span)
    mate = jnp.concatenate([mate[rows // 2 :], mate[: rows // 2]], axis=0)
    k_span = jnp.where(key_side, span, mate)
    v_span = jnp.where(key_side, mate, span)
    q_rows = q_rot.reshape(rows, local, heads * HD)
    mixed_rows, lse = attend(low, q_rows, k_span, v_span, start, reach)
    mixed = mixed_rows.reshape(total, heads * HD)

    grad_out = to_f(cotangent) * valid_rows(valid, core, rows)[:, :, None]
    grad_out = own_first(grad_out).reshape(total, width)
    grad_ffn = to_bf(grad_out)

    def branch_half(index, extra):
        out = dot(mixed[index * half : (index + 1) * half], o_weight, 1, 1)
        return out if extra is None else out + to_f(extra)

    branch = tensor_sum(branch_half)
    mine = to_f(lax.dynamic_slice_in_dim(tokens, core * (rows // 2), rows // 2, 0)).reshape(half, width)
    grad_mine = grad_out[:half]
    middle = mine + branch
    factor_two = lax.rsqrt(jnp.mean(middle * middle, axis=-1, keepdims=True) + EPS)
    normed_two = middle * factor_two
    h_two_mine = to_bf(normed_two * gain_two)
    h_two = jnp.concatenate([h_two_mine, core_swap(h_two_mine)], axis=0)

    grad_hidden = to_bf(dot(grad_ffn, down_weight))
    hidden, grad_gate, grad_up = gated(h_two, grad_hidden, gate_weight, up_weight)

    down_rows = rows_sum(grad_ffn, hidden, dp_index)
    down_grad = seq_scatter(down_rows)

    def grad_half(index, extra):
        here = slice(index * half, (index + 1) * half)
        out = dot(grad_gate[here], gate_weight, 1, 1) + dot(grad_up[here], up_weight, 1, 1)
        return out if extra is None else out + to_f(extra)

    grad_h_two = tensor_sum(grad_half)
    gate_rows = rows_sum(h_two, grad_gate, dp_index)
    up_rows = rows_sum(h_two, grad_up, dp_index)
    gate_grad = seq_scatter(gate_rows)
    up_grad = seq_scatter(up_rows)

    weighted = grad_h_two * gain_two
    inner = jnp.mean(weighted * normed_two, axis=-1, keepdims=True)
    grad_middle = grad_mine + factor_two * (weighted - normed_two * inner)
    branch_mine = to_bf(grad_middle)
    grad_branch = jnp.concatenate([branch_mine, core_swap(branch_mine)], axis=0)
    grad_mixed = to_bf(dot(grad_branch, o_weight)).reshape(rows, local, heads * HD)
    out_rows = rows_sum(grad_branch, mixed, dp_index)
    o_grad = seq_scatter(out_rows)

    grad_q_rows, both = attend_back(
        low,
        core_one,
        q_rows,
        k_span,
        v_span,
        grad_mixed,
        mixed_rows,
        lse,
        start,
        cosine.reshape(rows, local, HD),
        sine.reshape(rows, local, HD),
        reach,
    )
    come = core_swap(both[1])
    come = jnp.concatenate([come[rows // 2 :], come[: rows // 2]], axis=0)
    span_grad = to_f(both[0]) + to_f(come)
    grad_kv = span_grad[:, reach:]
    for h in range(1, hops + 1):
        there = to_bf(span_grad[:, reach - h * local : reach - (h - 1) * local])
        grad_kv = grad_kv + to_f(shifted(there, -h))
    grad_kv = grad_kv.reshape(total, HD)
    turned = grad_kv * sine
    turned = jnp.concatenate([turned[:, HD // 2 :], turned[:, : HD // 2]], axis=1)
    grad_kv = to_bf(jnp.where(key_side, grad_kv * cosine + turned, grad_kv))
    grad_qkv = jnp.concatenate([grad_q_rows.reshape(total, heads * HD), grad_kv], axis=1)

    bias_sum = jnp.sum(to_f(grad_qkv), axis=0, keepdims=True)
    bias_high = to_bf(bias_sum)
    bias_low = to_bf(bias_sum - to_f(bias_high))
    pad = 16
    bias_rows = jnp.concatenate(
        [bias_high, bias_low, jnp.zeros((pad - 2, bias_sum.shape[1]), jnp.bfloat16)], axis=0
    )
    qkv_rows = rows_sum(h_one, grad_qkv, dp_index)
    qkv_grad = seq_scatter(qkv_rows)

    def one_half(index, extra):
        out = dot(grad_qkv[index * half : (index + 1) * half], weight, 1, 1)
        return out if extra is None else out + to_f(extra)

    grad_h_one = tensor_sum(one_half)
    factor_one = lax.rsqrt(jnp.mean(mine * mine, axis=-1, keepdims=True) + EPS)
    normed_one = mine * factor_one
    weighted = grad_h_one * gain_one
    inner = jnp.mean(weighted * normed_one, axis=-1, keepdims=True)
    token_mine = grad_middle + factor_one * (weighted - normed_one * inner)
    token_mate = core_swap(token_mine)
    token_grad = jnp.where(
        key_side,
        jnp.concatenate([token_mine, token_mate], axis=0),
        jnp.concatenate([token_mate, token_mine], axis=0),
    ).reshape(rows, local, width)

    def ffn_half(index, extra):
        out = dot(hidden[index * half : (index + 1) * half], down_weight, 1, 1)
        return out if extra is None else out + to_f(extra)

    layer_mine = to_bf(middle + tensor_sum(ffn_half))
    layer_mate = core_swap(layer_mine)
    layer_out = jnp.where(
        key_side,
        jnp.concatenate([layer_mine, layer_mate], axis=0),
        jnp.concatenate([layer_mate, layer_mine], axis=0),
    ).reshape(rows, local, width)

    share = qkv_grad.shape[0]
    begin = (dp_index * seqs + seq_index) * share

    def rows_of(value):
        return to_f(lax.dynamic_slice_in_dim(value, begin, share, 0))

    attn_term = jnp.sum(rows_of(weight) * qkv_grad, axis=1)
    ffn_term = jnp.sum(rows_of(gate_weight) * gate_grad + rows_of(up_weight) * up_grad, axis=1)
    ffn_gain_grad, attn_gain_grad = lax.psum((ffn_term, attn_term), "tensor")
    attn_gain_grad = attn_gain_grad / lax.dynamic_slice_in_dim(gain_one[0], begin, share, 0)
    ffn_gain_grad = ffn_gain_grad / lax.dynamic_slice_in_dim(gain_two[0], begin, share, 0)
    q_grad = qkv_grad[:, : heads * HD]
    kv_parts = lax.all_to_all(qkv_grad[:, heads * HD :], "tensor", 0, 0, tiled=True)
    kv_parts = kv_parts.reshape(KVH, 2, share // ranks, HD)
    k_grad = jnp.concatenate([kv_parts[i, 0] for i in range(KVH)], axis=1)
    v_grad = jnp.concatenate([kv_parts[i, 1] for i in range(KVH)], axis=1)
    rank_pick = to_f(jnp.arange(ranks, dtype=jnp.int32) == rank)
    bias_all = lax.psum(rank_pick[:, None] * bias_sum, ("dp", "seq", "tensor"))
    q_bias_grad = bias_all[:, : heads * HD].reshape(-1)
    kv_bias = bias_all[:, heads * HD :].reshape(KVH, 2, HD)
    k_bias_grad = kv_bias[:, 0].reshape(-1)
    v_bias_grad = kv_bias[:, 1].reshape(-1)
    return (
        layer_out,
        token_grad,
        q_grad,
        q_bias_grad,
        k_grad,
        k_bias_grad,
        v_grad,
        v_bias_grad,
        o_grad,
        attn_gain_grad,
        ffn_gain_grad,
        gate_grad,
        up_grad,
        down_grad,
    )


def valid_rows(valid, core, rows):
    turned = jnp.concatenate([valid[rows // 2 :], valid[: rows // 2]], axis=0)
    return jnp.where(core == 0, valid, turned)


def solution(mesh):
    in_specs = (
        P("dp", "seq", None),
        P("dp", None),
        P("dp", "seq", None),
        P(None, "tensor"),
        P("tensor"),
        P(),
        P(),
        P(),
        P(),
        P(None, "tensor"),
        P(),
        P(),
        P(None, "tensor"),
        P(None, "tensor"),
        P(None, "tensor"),
    )
    out_specs = (
        P("dp", "seq", None),
        P("dp", "seq", None),
        P(("dp", "seq"), "tensor"),
        P(),
        P(("dp", "seq", "tensor"), None),
        P(),
        P(("dp", "seq", "tensor"), None),
        P(),
        P(("dp", "seq"), "tensor"),
        P(("dp", "seq")),
        P(("dp", "seq")),
        P(("dp", "seq"), "tensor"),
        P(("dp", "seq"), "tensor"),
        P(("dp", "seq"), "tensor"),
    )
    return jax.shard_map(body, mesh=mesh, in_specs=in_specs, out_specs=out_specs, check_vma=False)
```

```python
import functools
import math

import jax
import jax.numpy as jnp
from jax import lax
from jax.experimental import pallas as pl
from jax.experimental.pallas import tpu as pltpu
from jax.sharding import PartitionSpec as P

KVH = 2
HD = 128
MOST = 1024
EPS = 1e-06
ROPE_BASE = 10000.0
NEG_FILL = -1e30
Q_BLOCK = 256
K_BLOCK = 256
MIB = 1 << 20
LIGHT = 1000
TILE = 256
SCALE = 1.0 / math.sqrt(HD)


def to_bf(value):
    return value.astype(jnp.bfloat16)


def to_f(value):
    return value.astype(jnp.float32)


def dot(left, right, left_dim=1, right_dim=0):
    return lax.dot_general(
        left,
        right,
        (((left_dim,), (right_dim,)), ((), ())),
        preferred_element_type=jnp.float32,
    )


def flipped(axis, bit):
    return [(i, i ^ (1 << bit)) for i in range(lax.axis_size(axis))]


def core_swap(value):
    return lax.ppermute(value, "tensor", flipped("tensor", 0))


def chip_swap(value):
    return lax.ppermute(value, "tensor", flipped("tensor", 1))


def shifted(value, hops):
    count = lax.axis_size("seq")
    route = [(i, i + hops) for i in range(count) if 0 <= i + hops < count]
    return lax.ppermute(value, "seq", route)


def cost(flops, read):
    return pl.CostEstimate(flops=flops // LIGHT, bytes_accessed=read // LIGHT, transcendentals=0)


class Order:
    def __init__(self):
        self.mark = None

    def __call__(self, kernel, args, in_specs, out_specs, out_shape, grid, flops, read, name, scalars=(), scratch=()):
        anchor = [] if self.mark is None else [self.mark]
        count = len(scalars) + len(args)
        outs = len(out_shape)

        def run(*refs):
            rest = refs[count + len(anchor) :]
            kernel(*refs[:count], *rest[:outs], *rest[outs + 1 :])
            rest[outs][...] = jnp.zeros(rest[outs].shape, jnp.float32)

        *results, self.mark = pl.pallas_call(
            run,
            grid_spec=pltpu.PrefetchScalarGridSpec(
                num_scalar_prefetch=len(scalars),
                grid=grid,
                in_specs=list(in_specs) + anchors(len(anchor)),
                out_specs=list(out_specs) + [mark_spec()],
                scratch_shapes=list(scratch),
            ),
            out_shape=list(out_shape) + [MARK],
            compiler_params=pltpu.CompilerParams(vmem_limit_bytes=32 * MIB),
            cost_estimate=cost(flops, read),
            name=name,
        )(*scalars, *args, *anchor)
        return results


def first_kernel(core_ref, tok_ref, gain_ref, w_ref, b_ref, cos_ref, sin_ref, h_ref, q_ref, kv_ref):
    x = to_f(tok_ref[...])
    factor = lax.rsqrt(jnp.mean(x * x, axis=-1, keepdims=True) + EPS)
    h = to_bf(x * factor * gain_ref[...])
    h_ref[...] = h
    lin = dot(h, w_ref[...]) + b_ref[...]
    cosine = cos_ref[...]
    sine = sin_ref[...]
    heads = q_ref.shape[1] // HD
    for head in range(heads):
        part = lin[:, head * HD : (head + 1) * HD]
        q_ref[:, head * HD : (head + 1) * HD] = to_bf(
            part * cosine + pltpu.roll(part, HD // 2, 1) * sine
        )
    part = lin[:, heads * HD :]
    is_key = core_ref[0] == 0
    kv_ref[...] = to_bf(
        part * jnp.where(is_key, cosine, 1.0)
        + pltpu.roll(part, HD // 2, 1) * jnp.where(is_key, sine, 0.0)
    )


def first(core, tokens, gain, weight, bias, cosine, sine):
    total, width = tokens.shape
    columns = weight.shape[1]
    block = total // 4
    half = 2

    def flip(i, core_ref):
        return (lax.rem(i + core_ref[0] * half, 4), 0)

    def at(i, core_ref):
        return (i, 0)

    def whole(i, core_ref):
        return (0, 0)

    return pl.pallas_call(
        first_kernel,
        grid_spec=pltpu.PrefetchScalarGridSpec(
            num_scalar_prefetch=1,
            grid=(4,),
            in_specs=[
                pl.BlockSpec((block, width), flip),
                pl.BlockSpec((1, width), whole),
                pl.BlockSpec((width, columns), whole),
                pl.BlockSpec((1, columns), whole),
                pl.BlockSpec((block, HD), at),
                pl.BlockSpec((block, HD), at),
            ],
            out_specs=[
                pl.BlockSpec((block, width), at),
                pl.BlockSpec((block, columns - HD), at),
                pl.BlockSpec((block, HD), at),
            ],
        ),
        out_shape=[
            jax.ShapeDtypeStruct((total, width), jnp.bfloat16),
            jax.ShapeDtypeStruct((total, columns - HD), jnp.bfloat16),
            jax.ShapeDtypeStruct((total, HD), jnp.bfloat16),
        ],
        compiler_params=pltpu.CompilerParams(vmem_limit_bytes=24 * MIB),
        cost_estimate=cost(2 * total * width * columns, 9 * MIB),
        name="first",
    )(core, tokens, gain, weight, bias, cosine, sine)


def stacked(ref, start, count, heads):
    return jnp.concatenate(
        [ref[0, pl.ds(start, count), h * HD : (h + 1) * HD] for h in range(heads)], axis=0
    )


def bounds(start_ref, index, heads, reach):
    first_key = jnp.concatenate(
        [start_ref[0, :, pl.ds(index * Q_BLOCK, Q_BLOCK)]] * heads, axis=1
    )
    place = reach + index * Q_BLOCK + lax.broadcasted_iota(jnp.int32, (1, Q_BLOCK), 1)
    return first_key, jnp.concatenate([place] * heads, axis=1)


def gather_span(core, refs, span):
    count = len(refs) // 2
    local = refs[0].shape[1]
    for i in range(count):
        here = slice(i * local, (i + 1) * local)
        span[core, here] = refs[i][0]
        span[1 - core, here] = refs[count + i][0]


def attend_kernel(heads, blocks, pieces, low_ref, core_ref, q_ref, start_ref, *refs):
    o_ref, lse_ref, acc, span = refs[2 * pieces :]
    row = pl.program_id(0)
    wide = heads * Q_BLOCK
    reach = (pieces - 1) * q_ref.shape[1]
    gather_span(core_ref[0], refs[: 2 * pieces], span)
    for index in range(blocks):
        q = stacked(q_ref, index * Q_BLOCK, Q_BLOCK, heads)
        first_key, place = bounds(start_ref, index, heads, reach)
        acc[...] = jnp.zeros_like(acc)

        def step(j, carry):
            top, total = carry
            keys = pl.ds(pl.multiple_of(j * K_BLOCK, K_BLOCK), K_BLOCK)
            s = dot(span[0, keys], q, 1, 1) * SCALE
            key = j * K_BLOCK + lax.broadcasted_iota(jnp.int32, (K_BLOCK, wide), 0)
            s = jnp.where((key >= first_key) & (key <= place), s, NEG_FILL)
            later = jnp.maximum(top, jnp.max(s, axis=0, keepdims=True))
            p = jnp.exp(s - later)
            fade = jnp.exp(top - later)
            total = total * fade + jnp.sum(p, axis=0, keepdims=True)
            acc[...] = acc[...] * fade + dot(span[1, keys], to_bf(p), 0, 0)
            return later, total

        last = (reach + (index + 1) * Q_BLOCK - 1) // K_BLOCK + 1
        top, total = lax.fori_loop(
            low_ref[row, index],
            last,
            step,
            (jnp.full((1, wide), NEG_FILL, jnp.float32), jnp.zeros((1, wide), jnp.float32)),
        )
        out = to_bf((acc[...] / total).T)
        for h in range(heads):
            o_ref[0, index * Q_BLOCK : (index + 1) * Q_BLOCK, h * HD : (h + 1) * HD] = out[
                h * Q_BLOCK : (h + 1) * Q_BLOCK
            ]
        lse_ref[0, index : index + 1, :] = top + jnp.log(total)


def span_specs(rows, local, pieces):
    near = pl.BlockSpec((1, local, HD), lambda i, *refs: (i, 0, 0))
    far = pl.BlockSpec((1, local, HD), lambda i, *refs: (lax.rem(i + rows // 2, rows), 0, 0))
    return [near] * pieces + [far] * pieces


def attend(low, core, q, start, span, mate):
    rows, local, columns = q.shape
    pieces = len(span)
    heads = columns // HD
    blocks = local // Q_BLOCK

    def at(i, *refs):
        return (i, 0, 0)

    return pl.pallas_call(
        functools.partial(attend_kernel, heads, blocks, pieces),
        grid_spec=pltpu.PrefetchScalarGridSpec(
            num_scalar_prefetch=2,
            grid=(rows,),
            in_specs=[pl.BlockSpec((1, local, columns), at), pl.BlockSpec((1, 1, local), at)]
            + span_specs(rows, local, pieces),
            out_specs=[
                pl.BlockSpec((1, local, columns), at),
                pl.BlockSpec((1, blocks, heads * Q_BLOCK), at),
            ],
            scratch_shapes=[
                pltpu.VMEM((HD, heads * Q_BLOCK), jnp.float32),
                pltpu.VMEM((2, pieces * local, HD), jnp.bfloat16),
            ],
        ),
        out_shape=[
            jax.ShapeDtypeStruct((rows, local, columns), jnp.bfloat16),
            jax.ShapeDtypeStruct((rows, blocks, heads * Q_BLOCK), jnp.float32),
        ],
        compiler_params=pltpu.CompilerParams(vmem_limit_bytes=24 * MIB),
        cost_estimate=cost(8_000_000_000, 4 * MIB),
        name="attend",
    )(low, core, q, start, *span, *mate)


def attend_back_kernel(
    heads, blocks, pieces, low_ref, core_ref, q_ref, start_ref, g_ref, o_ref, lse_ref, cos_ref, sin_ref, *refs
):
    gq_ref, both_ref, acc, gk, gv, span = refs[2 * pieces :]
    row = pl.program_id(0)
    wide = heads * Q_BLOCK
    reach = (pieces - 1) * q_ref.shape[1]
    core = core_ref[0]
    gather_span(core, refs[: 2 * pieces], span)
    gk[...] = jnp.zeros_like(gk)
    gv[...] = jnp.zeros_like(gv)
    for index in range(blocks):
        q = stacked(q_ref, index * Q_BLOCK, Q_BLOCK, heads)
        g = stacked(g_ref, index * Q_BLOCK, Q_BLOCK, heads)
        o = stacked(o_ref, index * Q_BLOCK, Q_BLOCK, heads)
        inner = jnp.sum((to_f(g) * to_f(o)).T, axis=0, keepdims=True)
        lse = lse_ref[0, index : index + 1, :]
        first_key, place = bounds(start_ref, index, heads, reach)
        acc[...] = jnp.zeros_like(acc)

        def step(j, carry):
            keys = pl.ds(pl.multiple_of(j * K_BLOCK, K_BLOCK), K_BLOCK)
            k = span[0, keys]
            s = dot(k, q, 1, 1) * SCALE
            key = j * K_BLOCK + lax.broadcasted_iota(jnp.int32, (K_BLOCK, wide), 0)
            p = jnp.where((key >= first_key) & (key <= place), jnp.exp(s - lse), 0.0)
            gp = dot(span[1, keys], g, 1, 1)
            gs = to_bf(p * (gp - inner))
            gv[keys] += dot(to_bf(p), g)
            gk[keys] += dot(gs, q)
            acc[...] += dot(k, gs, 0, 0)
            return carry

        last = (reach + (index + 1) * Q_BLOCK - 1) // K_BLOCK + 1
        lax.fori_loop(low_ref[row, index], last, step, 0)
        gq = acc[...].T * SCALE
        here = slice(index * Q_BLOCK, (index + 1) * Q_BLOCK)
        cosine, sine = cos_ref[here], sin_ref[here]
        for h in range(heads):
            part = gq[h * Q_BLOCK : (h + 1) * Q_BLOCK]
            gq_ref[0, here, h * HD : (h + 1) * HD] = to_bf(
                part * cosine + pltpu.roll(part * sine, HD // 2, 1)
            )
    both_ref[core, 0] = to_bf(gk[...] * SCALE)
    both_ref[1 - core, 0] = to_bf(gv[...])


def attend_back(order, low, core, q, start, span, mate, grad, out, lse, cosine, sine):
    rows, local, columns = q.shape
    pieces = len(span)
    window = pieces * local
    heads = columns // HD
    blocks = local // Q_BLOCK

    def at(i, *refs):
        return (i, 0, 0)

    table = pl.BlockSpec((local, HD), lambda i, *refs: (i, 0))
    tokens = pl.BlockSpec((1, local, columns), at)
    return order(
        functools.partial(attend_back_kernel, heads, blocks, pieces),
        [q, start, grad, out, lse, cosine, sine, *span, *mate],
        [
            tokens,
            pl.BlockSpec((1, 1, local), at),
            tokens,
            tokens,
            pl.BlockSpec((1, blocks, heads * Q_BLOCK), at),
            table,
            table,
        ]
        + span_specs(rows, local, pieces),
        [tokens, pl.BlockSpec((2, 1, window, HD), lambda i, *refs: (0, i, 0, 0))],
        [
            jax.ShapeDtypeStruct((rows, local, columns), jnp.bfloat16),
            jax.ShapeDtypeStruct((2, rows, window, HD), jnp.bfloat16),
        ],
        (rows,),
        20_000_000_000,
        6 * MIB,
        "attend_back",
        scalars=(low, core),
        scratch=[
            pltpu.VMEM((HD, heads * Q_BLOCK), jnp.float32),
            pltpu.VMEM((window, HD), jnp.float32),
            pltpu.VMEM((window, HD), jnp.float32),
            pltpu.VMEM((2, window, HD), jnp.bfloat16),
        ],
    )


def fold_kernel(both_ref, come_ref, own_ref, *send_refs):
    local = own_ref.shape[1]
    total = to_f(both_ref[0, 0]) + to_f(come_ref[0])
    reach = total.shape[0] - local
    own_ref[0] = total[reach:]
    for hop, ref in enumerate(send_refs, 1):
        ref[0] = to_bf(total[reach - hop * local : reach - (hop - 1) * local])


def fold(order, both, come, local):
    rows, window = both.shape[1:3]
    hops = window // local - 1
    out = pl.BlockSpec((1, local, HD), lambda i: (i, 0, 0))
    return order(
        fold_kernel,
        [both, come],
        [
            pl.BlockSpec((1, 1, window, HD), lambda i: (0, i, 0, 0)),
            pl.BlockSpec((1, window, HD), lambda i: (lax.rem(i + rows // 2, rows), 0, 0)),
        ],
        [out] * (hops + 1),
        [jax.ShapeDtypeStruct((rows, local, HD), jnp.float32)]
        + [jax.ShapeDtypeStruct((rows, local, HD), jnp.bfloat16)] * hops,
        (rows,),
        0,
        4 * MIB,
        "fold",
    )


def join_kernel(hops, core_ref, gq_ref, cos_ref, sin_ref, own_ref, *refs):
    out_ref, sum_ref = refs[-2:]
    columns = gq_ref.shape[2]
    grad = own_ref[0]
    for ref in refs[:hops]:
        grad = grad + to_f(ref[0])
    is_key = core_ref[0] == 0
    cosine = jnp.where(is_key, cos_ref[...], 1.0)
    sine = jnp.where(is_key, sin_ref[...], 0.0)
    kv = to_bf(grad * cosine + pltpu.roll(grad * sine, HD // 2, 1))
    q = gq_ref[0]
    out_ref[:, :columns] = q
    out_ref[:, columns:] = kv

    @pl.when(pl.program_id(0) == 0)
    def _():
        sum_ref[...] = jnp.zeros(sum_ref.shape, jnp.float32)

    sum_ref[:, :columns] += jnp.sum(to_f(q), axis=0, keepdims=True)
    sum_ref[:, columns:] += jnp.sum(to_f(kv), axis=0, keepdims=True)


def join(order, core, grad_q, own, comes, cosine, sine):
    rows, local, columns = grad_q.shape
    wide = columns + HD

    def at(i, *refs):
        return (i, 0, 0)

    piece = pl.BlockSpec((1, local, HD), at)
    table = pl.BlockSpec((local, HD), lambda i, *refs: (i, 0))
    return order(
        functools.partial(join_kernel, len(comes)),
        [grad_q, cosine, sine, own, *comes],
        [pl.BlockSpec((1, local, columns), at), table, table, piece] + [piece] * len(comes),
        [
            pl.BlockSpec((local, wide), lambda i, *refs: (i, 0)),
            pl.BlockSpec((8, wide), lambda i, *refs: (0, 0)),
        ],
        [
            jax.ShapeDtypeStruct((rows * local, wide), jnp.bfloat16),
            jax.ShapeDtypeStruct((8, wide), jnp.float32),
        ],
        (rows,),
        0,
        4 * MIB,
        "join",
        scalars=(core,),
    )


def mixed_back_kernel(near_ref, far_ref, w_ref, out_ref):
    half = near_ref.shape[0]
    out_ref[:half] = to_bf(dot(near_ref[...], w_ref[...]))
    out_ref[half:] = to_bf(dot(far_ref[...], w_ref[...]))


def mixed_back(order, near, far, weight):
    half, width = near.shape
    columns = weight.shape[1]

    def whole(i):
        return (0, 0)

    return order(
        mixed_back_kernel,
        [near, far, weight],
        [
            pl.BlockSpec((half, width), whole),
            pl.BlockSpec((half, width), whole),
            pl.BlockSpec((width, columns), whole),
        ],
        [pl.BlockSpec((2 * half, columns), whole)],
        [jax.ShapeDtypeStruct((2 * half, columns), jnp.bfloat16)],
        (1,),
        4 * half * width * columns,
        6 * MIB,
        "mixed_back",
    )[0]


def place_kernel(core_ref, near_ref, far_ref, out_ref):
    near = pl.program_id(0) < 2

    @pl.when(near)
    def _():
        out_ref[...] = near_ref[...]

    @pl.when(jnp.logical_not(near))
    def _():
        out_ref[...] = far_ref[...]


def place(order, core, near, far):
    half, width = near.shape
    block = half // 2
    return order(
        place_kernel,
        [near, far],
        [
            pl.BlockSpec((block, width), lambda i, core_ref: (jnp.minimum(i, 1), 0)),
            pl.BlockSpec((block, width), lambda i, core_ref: (jnp.maximum(i - 2, 0), 0)),
        ],
        [pl.BlockSpec((block, width), lambda i, core_ref: (lax.rem(i + core_ref[0] * 2, 4), 0))],
        [jax.ShapeDtypeStruct((2 * half, width), near.dtype)],
        (4,),
        0,
        8 * half * width,
        "place",
        scalars=(core,),
    )[0]


def anchors(count):
    return [pl.BlockSpec(memory_space=pl.ANY)] * count


MARK = jax.ShapeDtypeStruct((8, HD), jnp.float32)


def mark_spec():
    return pl.BlockSpec((8, HD), lambda *refs: (0, 0))


def grad_hidden_kernel(g_ref, w_ref, out_ref):
    out_ref[...] = to_bf(dot(g_ref[...], w_ref[...], 1, 1))


def grad_hidden_of(order, grad, weight):
    total, width = grad.shape
    hidden = weight.shape[0]
    return order(
        grad_hidden_kernel,
        [grad, weight],
        [pl.BlockSpec((total, width), lambda i: (0, 0)), pl.BlockSpec((TILE, width), lambda i: (i, 0))],
        [pl.BlockSpec((total, TILE), lambda i: (0, i))],
        [jax.ShapeDtypeStruct((total, hidden), jnp.bfloat16)],
        (pl.cdiv(hidden, TILE),),
        2 * total * width * hidden,
        15 * MIB,
        "grad_hidden",
    )[0]


def gated_kernel(h_ref, far_ref, gh_ref, gw_ref, uw_ref, hid_ref, gg_ref, gu_ref):
    half = h_ref.shape[0]
    for part, ref in enumerate((h_ref, far_ref)):
        here = slice(part * half, (part + 1) * half)
        h = ref[...]
        gate = dot(h, gw_ref[...], 1, 1)
        up = dot(h, uw_ref[...], 1, 1)
        grad = to_f(gh_ref[here])
        sigma = 1.0 / (1.0 + jnp.exp(-gate))
        swish = gate * sigma
        hid_ref[here] = to_bf(swish * up)
        gu_ref[here] = to_bf(grad * swish)
        gg_ref[here] = to_bf(grad * up * sigma * (1.0 + gate * (1.0 - sigma)))


def gated(order, near, far, grad_hidden, gate_weight, up_weight):
    half, width = near.shape
    total = 2 * half
    hidden = gate_weight.shape[0]
    column = pl.BlockSpec((total, TILE), lambda i: (0, i))
    weight = pl.BlockSpec((TILE, width), lambda i: (i, 0))
    whole = pl.BlockSpec((half, width), lambda i: (0, 0))
    shape = jax.ShapeDtypeStruct((total, hidden), jnp.bfloat16)
    return order(
        gated_kernel,
        [near, far, grad_hidden, gate_weight, up_weight],
        [whole, whole, column, weight, weight],
        [column] * 3,
        [shape] * 3,
        (pl.cdiv(hidden, TILE),),
        4 * total * width * hidden,
        30 * MIB,
        "gated",
    )


def share_kernel(columns, skip, extra, halves, pick_ref, blocks_ref, left_ref, right_ref, *refs):
    out = dot(left_ref[...], right_ref[...])
    if extra:
        out = out + to_f(refs[0][...])
        refs = refs[1:]
    tile = out.shape[1]
    spot = (pl.program_id(0) + skip) * tile + lax.broadcasted_iota(jnp.int32, (1, tile), 1)
    out = to_bf(jnp.where(spot < columns, out, 0.0))
    if not halves:
        refs[0][...] = out
        return
    send_ref, keep_ref, rows = refs
    rows[...] = out
    share = send_ref.shape[0] // (2 * halves)
    for i in range(2 * halves):
        here = slice(i * share, (i + 1) * share)
        send_ref[here] = rows[pl.ds(pl.multiple_of(blocks_ref[i] * share, share), share)]
        keep_ref[here] = rows[pl.ds(pl.multiple_of(blocks_ref[2 * halves + i] * share, share), share)]


def share_of(order, left, right, part, pick, span, tile=0, extra=None, blocks=None):
    tokens, columns = right.shape
    tile = tile or TILE
    skip, count = span
    column = pl.BlockSpec((part, tile), lambda i, *refs: (0, i))
    extras = [] if extra is None else [extra]
    scratch = []
    outs, shapes = [column], [jax.ShapeDtypeStruct((part, count * tile), jnp.bfloat16)]
    halves = 0
    if blocks is None:
        blocks = jnp.zeros((1,), jnp.int32)
    else:
        halves = blocks.shape[0] // 4
        outs = [pl.BlockSpec((part // 2, tile), lambda i, *refs: (0, i))] * 2
        shapes = [jax.ShapeDtypeStruct((part // 2, count * tile), jnp.bfloat16)] * 2
        scratch = [pltpu.VMEM((part, tile), jnp.bfloat16)]
    result = order(
        functools.partial(share_kernel, columns, skip, len(extras), halves),
        [left, right, *extras],
        [
            pl.BlockSpec((part, tokens), lambda i, pick_ref, blocks_ref: (pick_ref[0], 0)),
            pl.BlockSpec((tokens, tile), lambda i, *refs: (0, i + skip)),
        ]
        + [column] * len(extras),
        outs,
        shapes,
        (count,),
        2 * part * tokens * count * tile,
        2 * (part * tokens + (part + tokens) * count * tile),
        "share",
        scalars=(jnp.asarray(pick, jnp.int32).reshape(1), blocks),
        scratch=scratch,
    )
    return result if halves else result[0]


def relay_kernel(keep_ref, come_ref, out_ref):
    out_ref[...] = to_bf(to_f(keep_ref[...]) + to_f(come_ref[...]))


def relay(order, keep, come, share):
    rows, columns = keep.shape
    pair = pl.BlockSpec((share, columns), lambda i: (2 * i + 1, 0))
    return order(
        relay_kernel,
        [keep, come],
        [pair, pair],
        [pl.BlockSpec((share, columns), lambda i: (i, 0))],
        [jax.ShapeDtypeStruct((rows // 2, columns), jnp.bfloat16)],
        (rows // (2 * share),),
        0,
        3 * rows * columns,
        "relay",
    )[0]


def settle_kernel(pick_ref, keep_ref, come_ref, last_ref, out_ref):
    out_ref[...] = to_bf(to_f(keep_ref[...]) + to_f(come_ref[...]) + to_f(last_ref[...]))


def settle(order, keep, come, last, pick):
    share = last.shape[0] // 2
    columns = keep.shape[1]
    pair = pl.BlockSpec((share, columns), lambda i, pick_ref: (2 * pick_ref[0], 0))
    return order(
        settle_kernel,
        [keep, come, last],
        [pair, pair, pl.BlockSpec((share, columns), lambda i, pick_ref: (pick_ref[0], 0))],
        [pl.BlockSpec((share, columns), lambda i, pick_ref: (0, 0))],
        [jax.ShapeDtypeStruct((share, columns), jnp.bfloat16)],
        (1,),
        0,
        8 * share * columns,
        "settle",
        scalars=(pick.reshape(1),),
    )[0]


def narrow_kernel(pairs, extra, right_dim, *refs):
    out = dot(refs[0][...], refs[1][...], 1, right_dim)
    for i in range(1, pairs):
        out = out + dot(refs[2 * i][...], refs[2 * i + 1][...], 1, right_dim)
    if extra:
        out = out + to_f(refs[2 * pairs][...])
    refs[-1][...] = to_bf(out)


def narrow(order, pairs, index, extra=None, right_dim=0):
    total, hidden = pairs[0][0].shape
    width = pairs[0][1].shape[1 - right_dim]
    half = total // 2
    column = pl.BlockSpec((half, TILE), lambda i: (0, i))
    extras = [] if extra is None else [extra]
    right = (
        pl.BlockSpec((TILE, hidden), lambda i: (i, 0))
        if right_dim
        else pl.BlockSpec((hidden, TILE), lambda i: (0, i))
    )
    return order(
        functools.partial(narrow_kernel, len(pairs), len(extras), right_dim),
        [item for pair in pairs for item in pair] + extras,
        [pl.BlockSpec((half, hidden), lambda i: (index, 0)), right] * len(pairs) + [column] * len(extras),
        [column],
        [jax.ShapeDtypeStruct((half, width), jnp.bfloat16)],
        (width // TILE,),
        2 * len(pairs) * half * width * hidden,
        2 * len(pairs) * (half + width) * hidden + 2 * half * width,
        "narrow",
    )[0]


def turn_kernel(near_ref, far_ref, out_ref):
    half = near_ref.shape[0]
    out_ref[:, :half] = near_ref[...].T
    out_ref[:, half:] = far_ref[...].T


def turn(order, near, far=None):
    half, width = near.shape
    far_index = 0
    if far is None:
        half, far, far_index = half // 2, near, 1
    return order(
        turn_kernel,
        [near, far],
        [
            pl.BlockSpec((half, TILE), lambda i: (0, i)),
            pl.BlockSpec((half, TILE), lambda i: (far_index, i)),
        ],
        [pl.BlockSpec((TILE, 2 * half), lambda i: (i, 0))],
        [jax.ShapeDtypeStruct((width, 2 * half), jnp.bfloat16)],
        (width // TILE,),
        0,
        8 * half * width,
        "turn",
    )[0]


def grad_out_kernel(core_ref, cot_ref, valid_ref, out_ref, turned_ref):
    out = to_bf(to_f(cot_ref[...]) * valid_ref[...])
    out_ref[...] = out
    turned_ref[...] = out.T


def grad_out_of(order, core, cotangent, valid):
    total, width = cotangent.shape
    block = total // 4
    return order(
        grad_out_kernel,
        [cotangent, valid],
        [
            pl.BlockSpec((block, width), lambda i, core_ref: (lax.rem(i + core_ref[0] * 2, 4), 0)),
            pl.BlockSpec((block, 1), lambda i, core_ref: (i, 0)),
        ],
        [
            pl.BlockSpec((block, width), lambda i, core_ref: (i, 0)),
            pl.BlockSpec((width, block), lambda i, core_ref: (0, i)),
        ],
        [
            jax.ShapeDtypeStruct((total, width), jnp.bfloat16),
            jax.ShapeDtypeStruct((width, total), jnp.bfloat16),
        ],
        (4,),
        0,
        6 * total * width,
        "grad_out",
        scalars=(core,),
    )


def middle_kernel(core_ref, tok_ref, mine_ref, come_ref, gain_ref, mid_ref, h_ref):
    middle = to_f(tok_ref[...]) + (to_f(mine_ref[...]) + to_f(come_ref[...]))
    factor = lax.rsqrt(jnp.mean(middle * middle, axis=-1, keepdims=True) + EPS)
    mid_ref[...] = middle
    h_ref[...] = to_bf(middle * factor * gain_ref[...])


def middle_of(order, core, tokens, mine, come, gain):
    half, width = mine.shape
    block = half // 4
    at = pl.BlockSpec((block, width), lambda i, core_ref: (i, 0))
    return order(
        middle_kernel,
        [tokens, mine, come, gain],
        [
            pl.BlockSpec((block, width), lambda i, core_ref: (core_ref[0] * 4 + i, 0)),
            at,
            at,
            pl.BlockSpec((1, width), lambda i, core_ref: (0, 0)),
        ],
        [at, at],
        [jax.ShapeDtypeStruct((half, width), jnp.float32), jax.ShapeDtypeStruct((half, width), jnp.bfloat16)],
        (4,),
        0,
        9 * MIB,
        "middle",
        scalars=(core,),
    )


def norm_back_kernel(core_ref, mine_ref, come_ref, x_ref, gain_ref, up_ref, *refs):
    grad = to_f(mine_ref[...]) + to_f(come_ref[...])
    x = to_f(x_ref[...])
    factor = lax.rsqrt(jnp.mean(x * x, axis=-1, keepdims=True) + EPS)
    normed = x * factor
    weighted = grad * gain_ref[...]
    inner = jnp.mean(weighted * normed, axis=-1, keepdims=True)
    out = to_f(up_ref[...]) + factor * (weighted - normed * inner)
    refs[0][...] = out
    if len(refs) > 1:
        refs[1][...] = to_bf(out)


def norm_back(order, core, mine, come, x, gain, up, by_core):
    half, width = mine.shape
    block = half // 4
    at = pl.BlockSpec((block, width), lambda i, core_ref: (i, 0))
    picked = pl.BlockSpec((block, width), lambda i, core_ref: (core_ref[0] * 4 + i, 0))
    shapes = [jax.ShapeDtypeStruct((half, width), jnp.float32)]
    if not by_core:
        shapes.append(jax.ShapeDtypeStruct((half, width), jnp.bfloat16))
    return order(
        norm_back_kernel,
        [mine, come, x, gain, up],
        [at, at, picked if by_core else at, pl.BlockSpec((1, width), lambda i, core_ref: (0, 0)), at],
        [at] * len(shapes),
        shapes,
        (4,),
        0,
        10 * MIB,
        "norm_back",
        scalars=(core,),
    )


def layer_kernel(middle_ref, mine_ref, come_ref, out_ref):
    out_ref[...] = to_bf(middle_ref[...] + (to_f(mine_ref[...]) + to_f(come_ref[...])))


def layer_of(order, middle, mine, come):
    half, width = mine.shape
    at = pl.BlockSpec((half // 4, width), lambda i: (i, 0))
    return order(
        layer_kernel,
        [middle, mine, come],
        [at] * 3,
        [at],
        [jax.ShapeDtypeStruct((half, width), jnp.bfloat16)],
        (4,),
        0,
        5 * MIB,
        "layer",
    )[0]


def tensor_gather(value, rank):
    mate = core_swap(value)
    pair = jnp.where(lax.rem(rank, 2) == 0, jnp.stack([value, mate]), jnp.stack([mate, value]))
    come = chip_swap(pair)
    return jnp.where(
        lax.div(rank, 2) == 0,
        jnp.concatenate([pair, come], axis=0),
        jnp.concatenate([come, pair], axis=0),
    )


def body(
    tokens,
    lengths,
    cotangent,
    q_weight,
    q_bias,
    k_weight,
    k_bias,
    v_weight,
    v_bias,
    o_weight,
    attn_gain,
    ffn_gain,
    gate_weight,
    up_weight,
    down_weight,
):
    rows, local, width = tokens.shape
    total = rows * local
    half = total // 2
    heads = q_weight.shape[1] // HD
    ranks = lax.axis_size("tensor")
    seqs = lax.axis_size("seq")
    rank = lax.axis_index("tensor")
    dp_index = lax.axis_index("dp")
    seq_index = lax.axis_index("seq")
    core = lax.rem(rank, 2)
    head = lax.div(rank, 2)
    core_one = core.reshape(1)
    hops = min(seqs - 1, -(-(MOST - 1) // local))
    reach = hops * local

    def own_first(value):
        turned = jnp.concatenate([value[rows // 2 :], value[: rows // 2]], axis=0)
        return jnp.where(core == 0, value, turned)

    slots = jnp.arange(lengths.shape[1], dtype=jnp.int32)
    lens = own_first(lengths)
    ends = jnp.sum(jnp.where(slots[None, :] <= slots[:, None], lens[:, None, :], 0), axis=2)
    spot = seq_index * local + jnp.arange(local, dtype=jnp.int32)
    begun = jnp.max(
        jnp.where(ends[:, None, :] <= spot[None, :, None], ends[:, None, :], 0), axis=2
    )
    valid = to_f(spot[None, :] < ends[:, -2:-1])
    position = (spot[None, :] - begun).reshape(total, 1)
    freqs = ROPE_BASE ** (-(jnp.arange(HD // 2, dtype=jnp.float32) * 2.0) / HD)
    angles = to_f(position) * freqs[None, :]
    cosine, sine = jnp.cos(angles), jnp.sin(angles)
    cosine = jnp.concatenate([cosine, cosine], axis=1)
    sine = jnp.concatenate([-sine, sine], axis=1)
    start = begun - (seq_index * local - reach)
    low = jnp.maximum(lax.div(jnp.maximum(start[:, ::Q_BLOCK], 0), K_BLOCK), 0)
    start = start.reshape(rows, 1, local)

    key_side = core == 0
    kv_weight = jnp.where(
        key_side,
        lax.dynamic_slice_in_dim(k_weight, head * HD, HD, 1),
        lax.dynamic_slice_in_dim(v_weight, head * HD, HD, 1),
    )
    kv_bias = jnp.where(
        key_side,
        lax.dynamic_slice_in_dim(k_bias, head * HD, HD, 0),
        lax.dynamic_slice_in_dim(v_bias, head * HD, HD, 0),
    )
    weight = jnp.concatenate([q_weight, kv_weight], axis=1)
    bias = to_f(jnp.concatenate([q_bias, kv_bias])).reshape(1, -1)
    gain_one = to_f(attn_gain).reshape(1, width)
    gain_two = to_f(ffn_gain).reshape(1, width)

    h_one, q_rot, kv = first(
        core_one, tokens.reshape(total, width), gain_one, weight, bias, cosine, sine
    )
    kv = kv.reshape(rows, local, HD)
    span = [shifted(kv, h) for h in range(hops, 0, -1)] + [kv]
    mate = [core_swap(piece) for piece in span]
    q_rows = q_rot.reshape(rows, local, heads * HD)
    mixed_rows, lse = attend(low, core_one, q_rows, start, span, mate)
    mixed = mixed_rows.reshape(total, heads * HD)

    order = Order()
    flat_tokens = tokens.reshape(total, width)
    dps = lax.axis_size("dp")
    near_pair = dps == 2 and seqs == 4
    part = width // dps
    share = part // seqs
    gate_t, up_t, down_t = gate_weight.T, up_weight.T, down_weight.T
    units = gate_t.shape[0]
    tiles = -(-units // TILE)
    cut = (tiles + 1) // 2
    one, two = seq_index ^ 1, seq_index ^ 2
    three = seq_index ^ 3
    quad = jnp.stack([one, three, seq_index, two])
    wide = jnp.stack([one, three, one + seqs, three + seqs, seq_index, two, seq_index + seqs, two + seqs])

    class Rows:
        def __init__(self, left_t, right, span, tile=TILE):
            self.args = (left_t, right)
            self.span, self.tile = span, tile
            if near_pair:
                sent = share_of(order, left_t, right, part, 1 - dp_index, span, tile)
                self.come = lax.ppermute(sent, "dp", flipped("dp", 0))
            else:
                self.whole = share_of(order, left_t, right, width, 0, span, tile)

        def own(self):
            if near_pair:
                send, self.keep = share_of(
                    order, *self.args, part, dp_index, self.span, self.tile, self.come, quad
                )
                self.come = lax.ppermute(send, "seq", flipped("seq", 0))

        def relay(self):
            if near_pair:
                sent = relay(order, self.keep, self.come, share)
                self.last = lax.ppermute(sent, "seq", flipped("seq", 1))

        def result(self):
            if near_pair:
                return to_f(self.keep[:share]) + to_f(self.come[:share]) + to_f(self.last)
            return to_f(lax.psum_scatter(self.whole, ("dp", "seq"), scatter_dimension=0, tiled=True))

    class SeqFirst(Rows):
        def __init__(self, left_t, right, span, tile=TILE):
            self.near = near_pair
            if near_pair:
                send, self.keep = share_of(order, left_t, right, width, 0, span, tile, None, wide)
                self.come = lax.ppermute(send, "seq", flipped("seq", 0))
            else:
                super().__init__(left_t, right, span, tile)

        def settle(self):
            if near_pair:
                sent = settle(order, self.keep, self.come, self.last, 1 - dp_index)
                self.mine = settle(order, self.keep, self.come, self.last, dp_index)
                self.final = lax.ppermute(sent, "dp", flipped("dp", 0))

        def result(self):
            return to_f(self.mine) + to_f(self.final) if near_pair else super().result()

    sent = narrow(order, [(mixed, o_weight)], 1, None, 1)
    mine = narrow(order, [(mixed, o_weight)], 0, core_swap(sent), 1)
    come = chip_swap(mine)
    grad_ffn, grad_ffn_t = grad_out_of(
        order, core_one, cotangent.reshape(total, width), valid.reshape(total, 1)
    )
    grad_hidden = grad_hidden_of(order, grad_ffn, down_t)
    h_one_t = turn(order, h_one)
    middle, h_two_mine = middle_of(order, core_one, flat_tokens, mine, come, gain_two)
    h_two_mate = core_swap(h_two_mine)
    hidden, grad_gate, grad_up = gated(order, h_two_mine, h_two_mate, grad_hidden, gate_t, up_t)

    down_a = Rows(grad_ffn_t, hidden, (0, cut))
    down_b = SeqFirst(grad_ffn_t, hidden, (cut, tiles - cut))
    pairs = [(grad_gate, gate_t), (grad_up, up_t)]
    sent = narrow(order, pairs, 1)
    mine = narrow(order, pairs, 0, core_swap(sent))
    come = chip_swap(mine)
    h_two_t = turn(order, h_two_mine, h_two_mate)
    gate_a = Rows(h_two_t, grad_gate, (0, cut))
    gate_b = Rows(h_two_t, grad_gate, (cut, tiles - cut))
    up_a = Rows(h_two_t, grad_up, (0, cut))
    ffn_sent = narrow(order, [(hidden, down_t)], 1)
    down_b.relay()
    down_a.own()
    grad_middle, branch_mine = norm_back(order, core_one, mine, come, middle, gain_two, grad_ffn, False)
    branch_mate = core_swap(branch_mine)
    grad_mixed = mixed_back(order, branch_mine, branch_mate, o_weight).reshape(rows, local, heads * HD)
    grad_q_rows, both = attend_back(
        order, low, core_one, q_rows, start, span, mate, grad_mixed, mixed_rows, lse, cosine, sine
    )
    both_come = core_swap(both[1])
    ffn_mine = narrow(order, [(hidden, down_t)], 0, core_swap(ffn_sent))
    ffn_come = chip_swap(ffn_mine)
    own_kv, *kv_sends = fold(order, both, both_come, local)
    kv_comes = [shifted(piece, -hop) for hop, piece in enumerate(kv_sends, 1)]
    branch_t = turn(order, branch_mine, branch_mate)
    out = Rows(branch_t, mixed, (0, heads), HD)
    down_b.settle() if near_pair else None
    down_a.relay()
    gate_a.own()
    grad_qkv, bias_sum = join(order, core_one, grad_q_rows, own_kv, kv_comes, cosine, sine)
    sent = narrow(order, [(grad_qkv, weight)], 1, None, 1)
    mine = narrow(order, [(grad_qkv, weight)], 0, core_swap(sent), 1)
    come = chip_swap(mine)
    qkv = Rows(h_one_t, grad_qkv, (0, grad_qkv.shape[1] // TILE))
    up_b = Rows(h_two_t, grad_up, (cut, tiles - cut))
    gate_b.own()
    gate_a.relay()
    (token_mine,) = norm_back(order, core_one, mine, come, flat_tokens, gain_one, grad_middle, True)
    token_mate = core_swap(token_mine)
    layer_mine = layer_of(order, middle, ffn_mine, ffn_come)
    layer_mate = core_swap(layer_mine)
    up_a.own()
    gate_b.relay()
    out.own()
    token_grad = place(order, core_one, token_mine, token_mate).reshape(rows, local, width)
    layer_out = place(order, core_one, layer_mine, layer_mate).reshape(rows, local, width)
    up_a.relay()
    out.relay()
    qkv.own()
    qkv.relay()
    up_b.own()
    up_b.relay()
    if near_pair:
        bias_all = bias_sum + lax.ppermute(bias_sum, "dp", flipped("dp", 0))
        bias_all = bias_all + lax.ppermute(bias_all, "seq", flipped("seq", 0))
        bias_all = bias_all + lax.ppermute(bias_all, "seq", flipped("seq", 1))
        bias_all = bias_all[:1]
    else:
        bias_all = lax.psum(bias_sum[:1], ("dp", "seq"))
    qkv_grad = qkv.result()
    o_grad = out.result()
    down_grad = jnp.concatenate([down_a.result(), down_b.result()], axis=1)[:, :units]
    gate_grad = jnp.concatenate([gate_a.result(), gate_b.result()], axis=1)[:, :units]
    up_grad = jnp.concatenate([up_a.result(), up_b.result()], axis=1)[:, :units]

    begin = (dp_index * seqs + seq_index) * share

    def rows_of(value):
        return to_f(lax.dynamic_slice_in_dim(value, begin, share, 0))

    attn_term = jnp.sum(rows_of(weight) * qkv_grad, axis=1)
    ffn_term = jnp.sum(rows_of(gate_weight) * gate_grad + rows_of(up_weight) * up_grad, axis=1)
    columns = heads * HD
    room = -(-share // HD) * HD - share
    terms = jnp.pad(jnp.stack([ffn_term, attn_term]), ((0, 0), (0, room))).reshape(-1, HD)
    packed = jnp.concatenate([qkv_grad[:, columns:], bias_all.reshape(-1, HD), terms], axis=0)
    gathered = tensor_gather(packed, rank)
    term_rows = terms.shape[0]
    bias_count = bias_all.shape[1] // HD
    terms = gathered[:, share + bias_count :].reshape(ranks, 2, -1)[:, :, :share]
    ffn_gain_grad, attn_gain_grad = terms[0] + terms[1] + (terms[2] + terms[3])
    attn_gain_grad = attn_gain_grad / lax.dynamic_slice_in_dim(gain_one[0], begin, share, 0)
    ffn_gain_grad = ffn_gain_grad / lax.dynamic_slice_in_dim(gain_two[0], begin, share, 0)
    q_grad = qkv_grad[:, :columns]
    kv_parts = lax.dynamic_slice_in_dim(gathered, rank * (share // ranks), share // ranks, 1)
    k_grad = jnp.concatenate([kv_parts[2 * i] for i in range(KVH)], axis=1)
    v_grad = jnp.concatenate([kv_parts[2 * i + 1] for i in range(KVH)], axis=1)
    biases = gathered[:, share : share + bias_count]
    q_bias_grad = biases[:, :heads].reshape(-1)
    k_bias_grad = biases[0::2, heads].reshape(-1)
    v_bias_grad = biases[1::2, heads].reshape(-1)
    return (
        layer_out,
        token_grad,
        q_grad,
        q_bias_grad,
        k_grad,
        k_bias_grad,
        v_grad,
        v_bias_grad,
        o_grad,
        attn_gain_grad,
        ffn_gain_grad,
        gate_grad,
        up_grad,
        down_grad,
    )


def solution(mesh):
    in_specs = (
        P("dp", "seq", None),
        P("dp", None),
        P("dp", "seq", None),
        P(None, "tensor"),
        P("tensor"),
        P(),
        P(),
        P(),
        P(),
        P(None, "tensor"),
        P(),
        P(),
        P(None, "tensor"),
        P(None, "tensor"),
        P(None, "tensor"),
    )
    out_specs = (
        P("dp", "seq", None),
        P("dp", "seq", None),
        P(("dp", "seq"), "tensor"),
        P(),
        P(("dp", "seq", "tensor"), None),
        P(),
        P(("dp", "seq", "tensor"), None),
        P(),
        P(("dp", "seq"), "tensor"),
        P(("dp", "seq")),
        P(("dp", "seq")),
        P(("dp", "seq"), "tensor"),
        P(("dp", "seq"), "tensor"),
        P(("dp", "seq"), "tensor"),
    )
    return jax.shard_map(body, mesh=mesh, in_specs=in_specs, out_specs=out_specs, check_vma=False)
```

```python
import functools
import math

import jax
import jax.numpy as jnp
from jax import lax
from jax.experimental import pallas as pl
from jax.experimental.pallas import tpu as pltpu
from jax.sharding import PartitionSpec as P

KVH = 2
HD = 128
MOST = 1024
EPS = 1e-06
ROPE_BASE = 10000.0
NEG_FILL = -1e30
Q_BLOCK = 256
K_BLOCK = 256
MIB = 1 << 20
LIGHT = 1000
TILE = 256
PIECES = 2
SCALE = 1.0 / math.sqrt(HD)


def to_bf(value):
    return value.astype(jnp.bfloat16)


def to_f(value):
    return value.astype(jnp.float32)


def dot(left, right, left_dim=1, right_dim=0):
    return lax.dot_general(
        left,
        right,
        (((left_dim,), (right_dim,)), ((), ())),
        preferred_element_type=jnp.float32,
    )


def flipped(axis, bit):
    return [(i, i ^ (1 << bit)) for i in range(lax.axis_size(axis))]


def core_swap(value):
    return lax.ppermute(value, "tensor", flipped("tensor", 0))


def chip_swap(value):
    return lax.ppermute(value, "tensor", flipped("tensor", 1))


def core_swaps(values):
    return [core_swap(value) for value in values]


def chip_swaps(values):
    return [chip_swap(value) for value in values]


def shifted(value, hops):
    count = lax.axis_size("seq")
    route = [(i, i + hops) for i in range(count) if 0 <= i + hops < count]
    return lax.ppermute(value, "seq", route)


def cost(flops, read):
    return pl.CostEstimate(flops=flops // LIGHT, bytes_accessed=read // LIGHT, transcendentals=0)


class Order:
    def __init__(self):
        self.mark = None
        self.touched = []

    def arrived(self, *values):
        self.touched.extend(values)

    def __call__(self, kernel, args, in_specs, out_specs, out_shape, grid, flops, read, name, scalars=(), scratch=()):
        anchor = ([] if self.mark is None else [self.mark]) + self.touched
        self.touched = []
        count = len(scalars) + len(args)
        outs = len(out_shape)

        def run(*refs):
            rest = refs[count + len(anchor) :]
            kernel(*refs[:count], *rest[:outs], *rest[outs + 1 :])
            rest[outs][...] = jnp.zeros(rest[outs].shape, jnp.float32)

        *results, self.mark = pl.pallas_call(
            run,
            grid_spec=pltpu.PrefetchScalarGridSpec(
                num_scalar_prefetch=len(scalars),
                grid=grid,
                in_specs=list(in_specs) + anchors(len(anchor)),
                out_specs=list(out_specs) + [mark_spec()],
                scratch_shapes=list(scratch),
            ),
            out_shape=list(out_shape) + [MARK],
            compiler_params=pltpu.CompilerParams(vmem_limit_bytes=32 * MIB),
            cost_estimate=cost(flops, read),
            name=name,
        )(*scalars, *args, *anchor)
        return results


def first_kernel(core_ref, tok_ref, gain_ref, w_ref, b_ref, cos_ref, sin_ref, h_ref, q_ref, kv_ref):
    x = to_f(tok_ref[...])
    factor = lax.rsqrt(jnp.mean(x * x, axis=-1, keepdims=True) + EPS)
    h = to_bf(x * factor * gain_ref[...])
    h_ref[...] = h
    lin = dot(h, w_ref[...]) + b_ref[...]
    cosine = cos_ref[...]
    sine = sin_ref[...]
    heads = q_ref.shape[1] // HD
    for head in range(heads):
        part = lin[:, head * HD : (head + 1) * HD]
        q_ref[:, head * HD : (head + 1) * HD] = to_bf(
            part * cosine + pltpu.roll(part, HD // 2, 1) * sine
        )
    part = lin[:, heads * HD :]
    is_key = core_ref[0] == 0
    kv_ref[...] = to_bf(
        part * jnp.where(is_key, cosine, 1.0)
        + pltpu.roll(part, HD // 2, 1) * jnp.where(is_key, sine, 0.0)
    )


def first(core, tokens, gain, weight, bias, cosine, sine):
    total, width = tokens.shape
    columns = weight.shape[1]
    block = total // 4
    half = 2

    def flip(i, core_ref):
        return (lax.rem(i + core_ref[0] * half, 4), 0)

    def at(i, core_ref):
        return (i, 0)

    def whole(i, core_ref):
        return (0, 0)

    return pl.pallas_call(
        first_kernel,
        grid_spec=pltpu.PrefetchScalarGridSpec(
            num_scalar_prefetch=1,
            grid=(4,),
            in_specs=[
                pl.BlockSpec((block, width), flip),
                pl.BlockSpec((1, width), whole),
                pl.BlockSpec((width, columns), whole),
                pl.BlockSpec((1, columns), whole),
                pl.BlockSpec((block, HD), at),
                pl.BlockSpec((block, HD), at),
            ],
            out_specs=[
                pl.BlockSpec((block, width), at),
                pl.BlockSpec((block, columns - HD), at),
                pl.BlockSpec((block, HD), at),
            ],
        ),
        out_shape=[
            jax.ShapeDtypeStruct((total, width), jnp.bfloat16),
            jax.ShapeDtypeStruct((total, columns - HD), jnp.bfloat16),
            jax.ShapeDtypeStruct((total, HD), jnp.bfloat16),
        ],
        compiler_params=pltpu.CompilerParams(vmem_limit_bytes=24 * MIB),
        cost_estimate=cost(2 * total * width * columns, 9 * MIB),
        name="first",
    )(core, tokens, gain, weight, bias, cosine, sine)


def stacked(ref, start, count, heads):
    return jnp.concatenate(
        [ref[0, pl.ds(start, count), h * HD : (h + 1) * HD] for h in range(heads)], axis=0
    )


def bounds(start_ref, index, heads, reach):
    first_key = jnp.concatenate(
        [start_ref[0, :, pl.ds(index * Q_BLOCK, Q_BLOCK)]] * heads, axis=1
    )
    place = reach + index * Q_BLOCK + lax.broadcasted_iota(jnp.int32, (1, Q_BLOCK), 1)
    return first_key, jnp.concatenate([place] * heads, axis=1)


def gather_span(core, refs, span):
    count = len(refs) // 2
    local = refs[0].shape[1]
    for i in range(count):
        here = slice(i * local, (i + 1) * local)
        span[core, here] = refs[i][0]
        span[1 - core, here] = refs[count + i][0]


def attend_kernel(heads, blocks, pieces, low_ref, core_ref, q_ref, start_ref, *refs):
    o_ref, lse_ref, acc, span = refs[2 * pieces :]
    row = pl.program_id(0)
    wide = heads * Q_BLOCK
    reach = (pieces - 1) * q_ref.shape[1]
    gather_span(core_ref[0], refs[: 2 * pieces], span)
    for index in range(blocks):
        q = stacked(q_ref, index * Q_BLOCK, Q_BLOCK, heads)
        first_key, place = bounds(start_ref, index, heads, reach)
        acc[...] = jnp.zeros_like(acc)

        def step(j, carry):
            top, total = carry
            keys = pl.ds(pl.multiple_of(j * K_BLOCK, K_BLOCK), K_BLOCK)
            s = dot(span[0, keys], q, 1, 1) * SCALE
            key = j * K_BLOCK + lax.broadcasted_iota(jnp.int32, (K_BLOCK, wide), 0)
            s = jnp.where((key >= first_key) & (key <= place), s, NEG_FILL)
            later = jnp.maximum(top, jnp.max(s, axis=0, keepdims=True))
            p = jnp.exp(s - later)
            fade = jnp.exp(top - later)
            total = total * fade + jnp.sum(p, axis=0, keepdims=True)
            acc[...] = acc[...] * fade + dot(span[1, keys], to_bf(p), 0, 0)
            return later, total

        last = (reach + (index + 1) * Q_BLOCK - 1) // K_BLOCK + 1
        top, total = lax.fori_loop(
            low_ref[row, index],
            last,
            step,
            (jnp.full((1, wide), NEG_FILL, jnp.float32), jnp.zeros((1, wide), jnp.float32)),
        )
        out = to_bf((acc[...] / total).T)
        for h in range(heads):
            o_ref[0, index * Q_BLOCK : (index + 1) * Q_BLOCK, h * HD : (h + 1) * HD] = out[
                h * Q_BLOCK : (h + 1) * Q_BLOCK
            ]
        lse_ref[0, index : index + 1, :] = top + jnp.log(total)


def span_specs(rows, local, pieces):
    near = pl.BlockSpec((1, local, HD), lambda i, *refs: (i, 0, 0))
    far = pl.BlockSpec((1, local, HD), lambda i, *refs: (lax.rem(i + rows // 2, rows), 0, 0))
    return [near] * pieces + [far] * pieces


def attend(low, core, q, start, span, mate):
    rows, local, columns = q.shape
    pieces = len(span)
    heads = columns // HD
    blocks = local // Q_BLOCK

    def at(i, *refs):
        return (i, 0, 0)

    return pl.pallas_call(
        functools.partial(attend_kernel, heads, blocks, pieces),
        grid_spec=pltpu.PrefetchScalarGridSpec(
            num_scalar_prefetch=2,
            grid=(rows,),
            in_specs=[pl.BlockSpec((1, local, columns), at), pl.BlockSpec((1, 1, local), at)]
            + span_specs(rows, local, pieces),
            out_specs=[
                pl.BlockSpec((1, local, columns), at),
                pl.BlockSpec((1, blocks, heads * Q_BLOCK), at),
            ],
            scratch_shapes=[
                pltpu.VMEM((HD, heads * Q_BLOCK), jnp.float32),
                pltpu.VMEM((2, pieces * local, HD), jnp.bfloat16),
            ],
        ),
        out_shape=[
            jax.ShapeDtypeStruct((rows, local, columns), jnp.bfloat16),
            jax.ShapeDtypeStruct((rows, blocks, heads * Q_BLOCK), jnp.float32),
        ],
        compiler_params=pltpu.CompilerParams(vmem_limit_bytes=24 * MIB),
        cost_estimate=cost(8_000_000_000, 4 * MIB),
        name="attend",
    )(low, core, q, start, *span, *mate)


def attend_back_kernel(
    heads, blocks, pieces, low_ref, core_ref, q_ref, start_ref, g_ref, o_ref, lse_ref, cos_ref, sin_ref, *refs
):
    gq_ref, keep_ref, *sends, acc, gk, gv, span = refs[2 * pieces :]
    row = pl.program_id(0)
    wide = heads * Q_BLOCK
    reach = (pieces - 1) * q_ref.shape[1]
    core = core_ref[0]
    gather_span(core, refs[: 2 * pieces], span)
    gk[...] = jnp.zeros_like(gk)
    gv[...] = jnp.zeros_like(gv)
    for index in range(blocks):
        q = stacked(q_ref, index * Q_BLOCK, Q_BLOCK, heads)
        g = stacked(g_ref, index * Q_BLOCK, Q_BLOCK, heads)
        o = stacked(o_ref, index * Q_BLOCK, Q_BLOCK, heads)
        inner = jnp.sum((to_f(g) * to_f(o)).T, axis=0, keepdims=True)
        lse = lse_ref[0, index : index + 1, :]
        first_key, place = bounds(start_ref, index, heads, reach)
        acc[...] = jnp.zeros_like(acc)

        def step(j, carry):
            keys = pl.ds(pl.multiple_of(j * K_BLOCK, K_BLOCK), K_BLOCK)
            k = span[0, keys]
            s = dot(k, q, 1, 1) * SCALE
            key = j * K_BLOCK + lax.broadcasted_iota(jnp.int32, (K_BLOCK, wide), 0)
            p = jnp.where((key >= first_key) & (key <= place), jnp.exp(s - lse), 0.0)
            gp = dot(span[1, keys], g, 1, 1)
            gs = to_bf(p * (gp - inner))
            gv[keys] += dot(to_bf(p), g)
            gk[keys] += dot(gs, q)
            acc[...] += dot(k, gs, 0, 0)
            return carry

        last = (reach + (index + 1) * Q_BLOCK - 1) // K_BLOCK + 1
        lax.fori_loop(low_ref[row, index], last, step, 0)
        gq = acc[...].T * SCALE
        here = slice(index * Q_BLOCK, (index + 1) * Q_BLOCK)
        cosine, sine = cos_ref[here], sin_ref[here]
        for h in range(heads):
            part = gq[h * Q_BLOCK : (h + 1) * Q_BLOCK]
            gq_ref[0, here, h * HD : (h + 1) * HD] = to_bf(
                part * cosine + pltpu.roll(part * sine, HD // 2, 1)
            )
    is_key = core == 0
    keys, values = gk[...] * SCALE, gv[...]
    keep_ref[0] = to_bf(jnp.where(is_key, keys, values))
    sent = to_bf(jnp.where(is_key, values, keys))
    for i, ref in enumerate(sends):

        @pl.when(row == i)
        def _(ref=ref):
            ref[0] = sent


def attend_back(order, low, core, q, start, span, mate, grad, out, lse, cosine, sine):
    rows, local, columns = q.shape
    pieces = len(span)
    window = pieces * local
    heads = columns // HD
    blocks = local // Q_BLOCK

    def at(i, *refs):
        return (i, 0, 0)

    table = pl.BlockSpec((local, HD), lambda i, *refs: (i, 0))
    tokens = pl.BlockSpec((1, local, columns), at)
    return order(
        functools.partial(attend_back_kernel, heads, blocks, pieces),
        [q, start, grad, out, lse, cosine, sine, *span, *mate],
        [
            tokens,
            pl.BlockSpec((1, 1, local), at),
            tokens,
            tokens,
            pl.BlockSpec((1, blocks, heads * Q_BLOCK), at),
            table,
            table,
        ]
        + span_specs(rows, local, pieces),
        [tokens, pl.BlockSpec((1, window, HD), at)]
        + [pl.BlockSpec((1, window, HD), lambda i, *refs: (0, 0, 0))] * rows,
        [
            jax.ShapeDtypeStruct((rows, local, columns), jnp.bfloat16),
            jax.ShapeDtypeStruct((rows, window, HD), jnp.bfloat16),
        ]
        + [jax.ShapeDtypeStruct((1, window, HD), jnp.bfloat16)] * rows,
        (rows,),
        20_000_000_000,
        6 * MIB,
        "attend_back",
        scalars=(low, core),
        scratch=[
            pltpu.VMEM((HD, heads * Q_BLOCK), jnp.float32),
            pltpu.VMEM((window, HD), jnp.float32),
            pltpu.VMEM((window, HD), jnp.float32),
            pltpu.VMEM((2, window, HD), jnp.bfloat16),
        ],
    )


def fold_kernel(rows, keep_ref, *refs):
    comes, own_ref, send_refs = refs[:rows], refs[rows], refs[rows + 1 :]
    local = own_ref.shape[1]
    come = comes[0][0]
    for i in range(1, rows):
        come = jnp.where(pl.program_id(0) == i, comes[i][0], come)
    total = to_f(keep_ref[0]) + to_f(come)
    reach = total.shape[0] - local
    own_ref[0] = total[reach:]
    for hop, ref in enumerate(send_refs, 1):
        ref[0] = to_bf(total[reach - hop * local : reach - (hop - 1) * local])


def fold(order, keep, comes, local):
    rows, window = keep.shape[:2]
    hops = window // local - 1
    out = pl.BlockSpec((1, local, HD), lambda i: (i, 0, 0))
    return order(
        functools.partial(fold_kernel, rows),
        [keep, *comes],
        [pl.BlockSpec((1, window, HD), lambda i: (i, 0, 0))]
        + [pl.BlockSpec((1, window, HD), lambda i: (0, 0, 0))] * rows,
        [out] * (hops + 1),
        [jax.ShapeDtypeStruct((rows, local, HD), jnp.float32)]
        + [jax.ShapeDtypeStruct((rows, local, HD), jnp.bfloat16)] * hops,
        (rows,),
        0,
        4 * MIB,
        "fold",
    )


def carry_kernel(piece_ref, come_ref, out_ref):
    out_ref[...] = to_bf(to_f(piece_ref[...]) + to_f(come_ref[...]))


def carry(order, piece, come):
    rows, local, columns = piece.shape
    at = pl.BlockSpec((1, local, columns), lambda i: (i, 0, 0))
    return order(
        carry_kernel,
        [piece, come],
        [at, at],
        [at],
        [jax.ShapeDtypeStruct(piece.shape, jnp.bfloat16)],
        (rows,),
        0,
        2 * MIB,
        "carry",
    )[0]


def bias_kernel(left_ref, right_ref, out_ref):
    out_ref[...] = left_ref[...] + right_ref[...]


def bias_add(order, left, right):
    whole = pl.BlockSpec(left.shape, lambda i: (0, 0))
    return order(
        bias_kernel,
        [left, right],
        [whole, whole],
        [whole],
        [jax.ShapeDtypeStruct(left.shape, jnp.float32)],
        (1,),
        0,
        MIB,
        "bias",
    )[0]


def join_kernel(hops, core_ref, gq_ref, cos_ref, sin_ref, own_ref, *refs):
    out_ref, sum_ref = refs[-2:]
    columns = gq_ref.shape[2]
    grad = own_ref[0]
    for ref in refs[:hops]:
        grad = grad + to_f(ref[0])
    is_key = core_ref[0] == 0
    cosine = jnp.where(is_key, cos_ref[...], 1.0)
    sine = jnp.where(is_key, sin_ref[...], 0.0)
    kv = to_bf(grad * cosine + pltpu.roll(grad * sine, HD // 2, 1))
    q = gq_ref[0]
    out_ref[:, :columns] = q
    out_ref[:, columns:] = kv

    @pl.when(pl.program_id(0) == 0)
    def _():
        sum_ref[...] = jnp.zeros(sum_ref.shape, jnp.float32)

    sum_ref[:, :columns] += jnp.sum(to_f(q), axis=0, keepdims=True)
    sum_ref[:, columns:] += jnp.sum(to_f(kv), axis=0, keepdims=True)


def join(order, core, grad_q, own, comes, cosine, sine):
    rows, local, columns = grad_q.shape
    wide = columns + HD

    def at(i, *refs):
        return (i, 0, 0)

    piece = pl.BlockSpec((1, local, HD), at)
    table = pl.BlockSpec((local, HD), lambda i, *refs: (i, 0))
    return order(
        functools.partial(join_kernel, len(comes)),
        [grad_q, cosine, sine, own, *comes],
        [pl.BlockSpec((1, local, columns), at), table, table, piece] + [piece] * len(comes),
        [
            pl.BlockSpec((local, wide), lambda i, *refs: (i, 0)),
            pl.BlockSpec((8, wide), lambda i, *refs: (0, 0)),
        ],
        [
            jax.ShapeDtypeStruct((rows * local, wide), jnp.bfloat16),
            jax.ShapeDtypeStruct((8, wide), jnp.float32),
        ],
        (rows,),
        0,
        4 * MIB,
        "join",
        scalars=(core,),
    )


def mixed_back_kernel(w_ref, *refs):
    rows = refs[0].shape[0]
    for i, ref in enumerate(refs[:-1]):
        refs[-1][i * rows : (i + 1) * rows] = to_bf(dot(ref[...], w_ref[...]))


def mixed_back(order, pieces, weight):
    rows, width = pieces[0].shape
    total = rows * len(pieces)
    columns = weight.shape[1]

    def whole(i):
        return (0, 0)

    return order(
        mixed_back_kernel,
        [weight, *pieces],
        [pl.BlockSpec((width, columns), whole)] + [pl.BlockSpec((rows, width), whole)] * len(pieces),
        [pl.BlockSpec((total, columns), whole)],
        [jax.ShapeDtypeStruct((total, columns), jnp.bfloat16)],
        (1,),
        2 * total * width * columns,
        6 * MIB,
        "mixed_back",
    )[0]


def place_kernel(core_ref, *refs):
    for i, ref in enumerate(refs[:-1]):

        @pl.when(pl.program_id(0) == i)
        def _(ref=ref):
            refs[-1][...] = ref[...]


def place(order, core, pieces):
    rows, width = pieces[0].shape
    count = len(pieces)
    return order(
        place_kernel,
        list(pieces),
        [pl.BlockSpec((rows, width), lambda i, core_ref: (0, 0))] * count,
        [pl.BlockSpec((rows, width), lambda i, core_ref: (lax.rem(i + core_ref[0] * (count // 2), count), 0))],
        [jax.ShapeDtypeStruct((rows * count, width), pieces[0].dtype)],
        (count,),
        0,
        8 * rows * width,
        "place",
        scalars=(core,),
    )[0]


def anchors(count):
    return [pl.BlockSpec(memory_space=pl.ANY)] * count


MARK = jax.ShapeDtypeStruct((8, HD), jnp.float32)


def mark_spec():
    return pl.BlockSpec((8, HD), lambda *refs: (0, 0))


def grad_hidden_kernel(g_ref, w_ref, out_ref):
    out_ref[...] = to_bf(dot(g_ref[...], w_ref[...], 1, 1))


def grad_hidden_of(order, grad, weight):
    total, width = grad.shape
    hidden = weight.shape[0]
    return order(
        grad_hidden_kernel,
        [grad, weight],
        [pl.BlockSpec((total, width), lambda i: (0, 0)), pl.BlockSpec((TILE, width), lambda i: (i, 0))],
        [pl.BlockSpec((total, TILE), lambda i: (0, i))],
        [jax.ShapeDtypeStruct((total, hidden), jnp.bfloat16)],
        (pl.cdiv(hidden, TILE),),
        2 * total * width * hidden,
        15 * MIB,
        "grad_hidden",
    )[0]


def gated_kernel(gh_ref, gw_ref, uw_ref, *refs):
    hid_ref, gg_ref, gu_ref = refs[-3:]
    rows = refs[0].shape[0]
    for part, ref in enumerate(refs[:-3]):
        here = slice(part * rows, (part + 1) * rows)
        h = ref[...]
        gate = dot(h, gw_ref[...], 1, 1)
        up = dot(h, uw_ref[...], 1, 1)
        grad = to_f(gh_ref[here])
        sigma = 1.0 / (1.0 + jnp.exp(-gate))
        swish = gate * sigma
        hid_ref[here] = to_bf(swish * up)
        gu_ref[here] = to_bf(grad * swish)
        gg_ref[here] = to_bf(grad * up * sigma * (1.0 + gate * (1.0 - sigma)))


def gated(order, pieces, grad_hidden, gate_weight, up_weight):
    rows, width = pieces[0].shape
    total = rows * len(pieces)
    hidden = gate_weight.shape[0]
    column = pl.BlockSpec((total, TILE), lambda i: (0, i))
    weight = pl.BlockSpec((TILE, width), lambda i: (i, 0))
    shape = jax.ShapeDtypeStruct((total, hidden), jnp.bfloat16)
    return order(
        gated_kernel,
        [grad_hidden, gate_weight, up_weight, *pieces],
        [column, weight, weight] + [pl.BlockSpec((rows, width), lambda i: (0, 0))] * len(pieces),
        [column] * 3,
        [shape] * 3,
        (pl.cdiv(hidden, TILE),),
        4 * total * width * hidden,
        30 * MIB,
        "gated",
    )


def share_kernel(columns, skip, extra, halves, pick_ref, blocks_ref, left_ref, right_ref, *refs):
    out = dot(left_ref[...], right_ref[...])
    if extra:
        out = out + to_f(refs[0][...])
        refs = refs[1:]
    tile = out.shape[1]
    spot = (pl.program_id(0) + skip) * tile + lax.broadcasted_iota(jnp.int32, (1, tile), 1)
    out = to_bf(jnp.where(spot < columns, out, 0.0))
    if not halves:
        refs[0][...] = out
        return
    send_ref, keep_ref, rows = refs
    rows[...] = out
    share = send_ref.shape[0] // (2 * halves)
    for i in range(2 * halves):
        here = slice(i * share, (i + 1) * share)
        send_ref[here] = rows[pl.ds(pl.multiple_of(blocks_ref[i] * share, share), share)]
        keep_ref[here] = rows[pl.ds(pl.multiple_of(blocks_ref[2 * halves + i] * share, share), share)]


def share_of(order, left, right, part, pick, span, tile=0, extra=None, blocks=None):
    tokens, columns = right.shape
    tile = tile or TILE
    skip, count = span
    column = pl.BlockSpec((part, tile), lambda i, *refs: (0, i))
    extras = [] if extra is None else [extra]
    scratch = []
    outs, shapes = [column], [jax.ShapeDtypeStruct((part, count * tile), jnp.bfloat16)]
    halves = 0
    if blocks is None:
        blocks = jnp.zeros((1,), jnp.int32)
    else:
        halves = blocks.shape[0] // 4
        outs = [pl.BlockSpec((part // 2, tile), lambda i, *refs: (0, i))] * 2
        shapes = [jax.ShapeDtypeStruct((part // 2, count * tile), jnp.bfloat16)] * 2
        scratch = [pltpu.VMEM((part, tile), jnp.bfloat16)]
    result = order(
        functools.partial(share_kernel, columns, skip, len(extras), halves),
        [left, right, *extras],
        [
            pl.BlockSpec((part, tokens), lambda i, pick_ref, blocks_ref: (pick_ref[0], 0)),
            pl.BlockSpec((tokens, tile), lambda i, *refs: (0, i + skip)),
        ]
        + [column] * len(extras),
        outs,
        shapes,
        (count,),
        2 * part * tokens * count * tile,
        2 * (part * tokens + (part + tokens) * count * tile),
        "share",
        scalars=(jnp.asarray(pick, jnp.int32).reshape(1), blocks),
        scratch=scratch,
    )
    return result if halves else result[0]


def relay_kernel(keep_ref, come_ref, out_ref):
    out_ref[...] = to_bf(to_f(keep_ref[...]) + to_f(come_ref[...]))


def relay(order, keep, come, share):
    rows, columns = keep.shape
    pair = pl.BlockSpec((share, columns), lambda i: (2 * i + 1, 0))
    return order(
        relay_kernel,
        [keep, come],
        [pair, pair],
        [pl.BlockSpec((share, columns), lambda i: (i, 0))],
        [jax.ShapeDtypeStruct((rows // 2, columns), jnp.bfloat16)],
        (rows // (2 * share),),
        0,
        3 * rows * columns,
        "relay",
    )[0]


def settle_kernel(pick_ref, keep_ref, come_ref, last_ref, out_ref):
    out_ref[...] = to_bf(to_f(keep_ref[...]) + to_f(come_ref[...]) + to_f(last_ref[...]))


def settle(order, keep, come, last, pick):
    share = last.shape[0] // 2
    columns = keep.shape[1]
    pair = pl.BlockSpec((share, columns), lambda i, pick_ref: (2 * pick_ref[0], 0))
    return order(
        settle_kernel,
        [keep, come, last],
        [pair, pair, pl.BlockSpec((share, columns), lambda i, pick_ref: (pick_ref[0], 0))],
        [pl.BlockSpec((share, columns), lambda i, pick_ref: (0, 0))],
        [jax.ShapeDtypeStruct((share, columns), jnp.bfloat16)],
        (1,),
        0,
        8 * share * columns,
        "settle",
        scalars=(pick.reshape(1),),
    )[0]


def narrow_kernel(pairs, extras, right_dim, *refs):
    out = dot(refs[0][...], refs[1][...], 1, right_dim)
    for i in range(1, pairs):
        out = out + dot(refs[2 * i][...], refs[2 * i + 1][...], 1, right_dim)
    extra = refs[2 * pairs : 2 * pairs + extras]
    outs = refs[2 * pairs + extras :]
    if extras:
        out = out + jnp.concatenate([to_f(ref[...]) for ref in extra], axis=0)
    rows = outs[0].shape[0]
    for i, ref in enumerate(outs):
        ref[...] = to_bf(out[i * rows : (i + 1) * rows])


def narrow(order, pairs, index, extra=(), right_dim=0):
    total, hidden = pairs[0][0].shape
    width = pairs[0][1].shape[1 - right_dim]
    half = total // 2
    piece = half // PIECES
    column = pl.BlockSpec((piece, TILE), lambda i: (0, i))
    right = (
        pl.BlockSpec((TILE, hidden), lambda i: (i, 0))
        if right_dim
        else pl.BlockSpec((hidden, TILE), lambda i: (0, i))
    )
    return order(
        functools.partial(narrow_kernel, len(pairs), len(extra), right_dim),
        [item for pair in pairs for item in pair] + list(extra),
        [pl.BlockSpec((half, hidden), lambda i: (index, 0)), right] * len(pairs) + [column] * len(extra),
        [column] * PIECES,
        [jax.ShapeDtypeStruct((piece, width), jnp.bfloat16)] * PIECES,
        (width // TILE,),
        2 * len(pairs) * half * width * hidden,
        2 * len(pairs) * (half + width) * hidden + 2 * half * width,
        "narrow",
    )


def piece_specs(piece, width, block):
    steps = piece // block
    return [
        pl.BlockSpec((block, width), lambda i, *refs, j=j: (jnp.clip(i - j * steps, 0, steps - 1), 0))
        for j in range(PIECES)
    ]


def pick_piece(refs):
    value = refs[0][...]
    for j, ref in enumerate(refs[1:], 1):
        value = jnp.where(pl.program_id(0) >= 4 * j // len(refs), ref[...], value)
    return value


def put_piece(refs, value):
    steps = 4 // len(refs)
    for j, ref in enumerate(refs):

        @pl.when(lax.div(pl.program_id(0), steps) == j)
        def _(ref=ref):
            ref[...] = value


def turn_kernel(*refs):
    rows = refs[0].shape[0]
    for i, ref in enumerate(refs[:-1]):
        refs[-1][:, i * rows : (i + 1) * rows] = ref[...].T


def turn(order, pieces):
    rows, width = pieces[0].shape
    total = rows * len(pieces)
    return order(
        turn_kernel,
        list(pieces),
        [pl.BlockSpec((rows, TILE), lambda i: (0, i))] * len(pieces),
        [pl.BlockSpec((TILE, total), lambda i: (i, 0))],
        [jax.ShapeDtypeStruct((width, total), jnp.bfloat16)],
        (width // TILE,),
        0,
        4 * total * width,
        "turn",
    )[0]


def grad_out_kernel(core_ref, cot_ref, valid_ref, out_ref, turned_ref):
    out = to_bf(to_f(cot_ref[...]) * valid_ref[...])
    out_ref[...] = out
    turned_ref[...] = out.T


def grad_out_of(order, core, cotangent, valid):
    total, width = cotangent.shape
    block = total // 4
    return order(
        grad_out_kernel,
        [cotangent, valid],
        [
            pl.BlockSpec((block, width), lambda i, core_ref: (lax.rem(i + core_ref[0] * 2, 4), 0)),
            pl.BlockSpec((block, 1), lambda i, core_ref: (i, 0)),
        ],
        [
            pl.BlockSpec((block, width), lambda i, core_ref: (i, 0)),
            pl.BlockSpec((width, block), lambda i, core_ref: (0, i)),
        ],
        [
            jax.ShapeDtypeStruct((total, width), jnp.bfloat16),
            jax.ShapeDtypeStruct((width, total), jnp.bfloat16),
        ],
        (4,),
        0,
        6 * total * width,
        "grad_out",
        scalars=(core,),
    )


def middle_kernel(core_ref, tok_ref, gain_ref, *refs):
    mine, come = pick_piece(refs[:PIECES]), pick_piece(refs[PIECES : 2 * PIECES])
    mid_ref, *h_refs = refs[2 * PIECES :]
    middle = to_f(tok_ref[...]) + (to_f(mine) + to_f(come))
    factor = lax.rsqrt(jnp.mean(middle * middle, axis=-1, keepdims=True) + EPS)
    mid_ref[...] = middle
    put_piece(h_refs, to_bf(middle * factor * gain_ref[...]))


def middle_of(order, core, tokens, mine, come, gain):
    piece, width = mine[0].shape
    half = piece * PIECES
    block = half // 4
    specs = piece_specs(piece, width, block)
    middle, *h = order(
        middle_kernel,
        [tokens, gain, *mine, *come],
        [
            pl.BlockSpec((block, width), lambda i, core_ref: (core_ref[0] * 4 + i, 0)),
            pl.BlockSpec((1, width), lambda i, core_ref: (0, 0)),
        ]
        + specs * 2,
        [pl.BlockSpec((block, width), lambda i, core_ref: (i, 0))] + specs,
        [jax.ShapeDtypeStruct((half, width), jnp.float32)]
        + [jax.ShapeDtypeStruct((piece, width), jnp.bfloat16)] * PIECES,
        (4,),
        0,
        9 * MIB,
        "middle",
        scalars=(core,),
    )
    return middle, h


def norm_back_kernel(core_ref, x_ref, gain_ref, up_ref, *refs):
    mine, come = pick_piece(refs[:PIECES]), pick_piece(refs[PIECES : 2 * PIECES])
    outs = refs[2 * PIECES :]
    grad = to_f(mine) + to_f(come)
    x = to_f(x_ref[...])
    factor = lax.rsqrt(jnp.mean(x * x, axis=-1, keepdims=True) + EPS)
    normed = x * factor
    weighted = grad * gain_ref[...]
    inner = jnp.mean(weighted * normed, axis=-1, keepdims=True)
    out = to_f(up_ref[...]) + factor * (weighted - normed * inner)
    if len(outs) > PIECES:
        outs[0][...] = out
        put_piece(outs[1:], to_bf(out))
    else:
        put_piece(outs, out)


def norm_back(order, core, mine, come, x, gain, up, by_core):
    piece, width = mine[0].shape
    half = piece * PIECES
    block = half // 4
    at = pl.BlockSpec((block, width), lambda i, core_ref: (i, 0))
    picked = pl.BlockSpec((block, width), lambda i, core_ref: (core_ref[0] * 4 + i, 0))
    specs = piece_specs(piece, width, block)
    if by_core:
        shapes = [jax.ShapeDtypeStruct((piece, width), jnp.float32)] * PIECES
    else:
        shapes = [jax.ShapeDtypeStruct((half, width), jnp.float32)]
        shapes += [jax.ShapeDtypeStruct((piece, width), jnp.bfloat16)] * PIECES
    return order(
        norm_back_kernel,
        [x, gain, up, *mine, *come],
        [picked if by_core else at, pl.BlockSpec((1, width), lambda i, core_ref: (0, 0)), at] + specs * 2,
        specs if by_core else [at] + specs,
        shapes,
        (4,),
        0,
        10 * MIB,
        "norm_back",
        scalars=(core,),
    )


def layer_kernel(middle_ref, *refs):
    mine, come = pick_piece(refs[:PIECES]), pick_piece(refs[PIECES : 2 * PIECES])
    put_piece(refs[2 * PIECES :], to_bf(middle_ref[...] + (to_f(mine) + to_f(come))))


def layer_of(order, middle, mine, come):
    piece, width = mine[0].shape
    block = piece * PIECES // 4
    specs = piece_specs(piece, width, block)
    return order(
        layer_kernel,
        [middle, *mine, *come],
        [pl.BlockSpec((block, width), lambda i: (i, 0))] + specs * 2,
        specs,
        [jax.ShapeDtypeStruct((piece, width), jnp.bfloat16)] * PIECES,
        (4,),
        0,
        5 * MIB,
        "layer",
    )


def tensor_gather(value, rank):
    mate = core_swap(value)
    pair = jnp.where(lax.rem(rank, 2) == 0, jnp.stack([value, mate]), jnp.stack([mate, value]))
    come = chip_swap(pair)
    return jnp.where(
        lax.div(rank, 2) == 0,
        jnp.concatenate([pair, come], axis=0),
        jnp.concatenate([come, pair], axis=0),
    )


def body(
    tokens,
    lengths,
    cotangent,
    q_weight,
    q_bias,
    k_weight,
    k_bias,
    v_weight,
    v_bias,
    o_weight,
    attn_gain,
    ffn_gain,
    gate_weight,
    up_weight,
    down_weight,
):
    rows, local, width = tokens.shape
    total = rows * local
    half = total // 2
    heads = q_weight.shape[1] // HD
    ranks = lax.axis_size("tensor")
    seqs = lax.axis_size("seq")
    rank = lax.axis_index("tensor")
    dp_index = lax.axis_index("dp")
    seq_index = lax.axis_index("seq")
    core = lax.rem(rank, 2)
    head = lax.div(rank, 2)
    core_one = core.reshape(1)
    hops = min(seqs - 1, -(-(MOST - 1) // local))
    reach = hops * local

    def own_first(value):
        turned = jnp.concatenate([value[rows // 2 :], value[: rows // 2]], axis=0)
        return jnp.where(core == 0, value, turned)

    slots = jnp.arange(lengths.shape[1], dtype=jnp.int32)
    lens = own_first(lengths)
    ends = jnp.sum(jnp.where(slots[None, :] <= slots[:, None], lens[:, None, :], 0), axis=2)
    spot = seq_index * local + jnp.arange(local, dtype=jnp.int32)
    begun = jnp.max(
        jnp.where(ends[:, None, :] <= spot[None, :, None], ends[:, None, :], 0), axis=2
    )
    valid = to_f(spot[None, :] < ends[:, -2:-1])
    position = (spot[None, :] - begun).reshape(total, 1)
    freqs = ROPE_BASE ** (-(jnp.arange(HD // 2, dtype=jnp.float32) * 2.0) / HD)
    angles = to_f(position) * freqs[None, :]
    cosine, sine = jnp.cos(angles), jnp.sin(angles)
    cosine = jnp.concatenate([cosine, cosine], axis=1)
    sine = jnp.concatenate([-sine, sine], axis=1)
    start = begun - (seq_index * local - reach)
    low = jnp.maximum(lax.div(jnp.maximum(start[:, ::Q_BLOCK], 0), K_BLOCK), 0)
    start = start.reshape(rows, 1, local)

    key_side = core == 0
    kv_weight = jnp.where(
        key_side,
        lax.dynamic_slice_in_dim(k_weight, head * HD, HD, 1),
        lax.dynamic_slice_in_dim(v_weight, head * HD, HD, 1),
    )
    kv_bias = jnp.where(
        key_side,
        lax.dynamic_slice_in_dim(k_bias, head * HD, HD, 0),
        lax.dynamic_slice_in_dim(v_bias, head * HD, HD, 0),
    )
    weight = jnp.concatenate([q_weight, kv_weight], axis=1)
    bias = to_f(jnp.concatenate([q_bias, kv_bias])).reshape(1, -1)
    gain_one = to_f(attn_gain).reshape(1, width)
    gain_two = to_f(ffn_gain).reshape(1, width)

    h_one, q_rot, kv = first(
        core_one, tokens.reshape(total, width), gain_one, weight, bias, cosine, sine
    )
    kv = kv.reshape(rows, local, HD)
    span = [shifted(kv, h) for h in range(hops, 0, -1)] + [kv]
    mate = [core_swap(piece) for piece in span]
    q_rows = q_rot.reshape(rows, local, heads * HD)
    mixed_rows, lse = attend(low, core_one, q_rows, start, span, mate)
    mixed = mixed_rows.reshape(total, heads * HD)

    order = Order()
    flat_tokens = tokens.reshape(total, width)
    dps = lax.axis_size("dp")
    near_pair = dps == 2 and seqs == 4
    part = width // dps
    share = part // seqs
    gate_t, up_t, down_t = gate_weight.T, up_weight.T, down_weight.T
    units = gate_t.shape[0]
    tiles = -(-units // TILE)
    cut = (tiles + 1) // 2
    long = cut
    one, two = seq_index ^ 1, seq_index ^ 2
    three = seq_index ^ 3
    quad = jnp.stack([one, three, seq_index, two])
    wide = jnp.stack([one, three, one + seqs, three + seqs, seq_index, two, seq_index + seqs, two + seqs])

    class Rows:
        def __init__(self, left_t, right, span, tile=TILE):
            self.args = (left_t, right)
            self.span, self.tile = span, tile
            if near_pair:
                sent = share_of(order, left_t, right, part, 1 - dp_index, span, tile)
                self.come = lax.ppermute(sent, "dp", flipped("dp", 0))
            else:
                self.whole = share_of(order, left_t, right, width, 0, span, tile)

        def own(self):
            if near_pair:
                send, self.keep = share_of(
                    order, *self.args, part, dp_index, self.span, self.tile, self.come, quad
                )
                self.come = lax.ppermute(send, "seq", flipped("seq", 0))

        def relay(self):
            if near_pair:
                sent = relay(order, self.keep, self.come, share)
                self.last = lax.ppermute(sent, "seq", flipped("seq", 1))

        def settled(self):
            if near_pair:
                order.arrived(self.last)

        def result(self):
            if near_pair:
                return to_f(self.keep[:share]) + to_f(self.come[:share]) + to_f(self.last)
            return to_f(lax.psum_scatter(self.whole, ("dp", "seq"), scatter_dimension=0, tiled=True))

    class SeqFirst(Rows):
        def __init__(self, left_t, right, span, tile=TILE):
            self.near = near_pair
            if near_pair:
                send, self.keep = share_of(order, left_t, right, width, 0, span, tile, None, wide)
                self.come = lax.ppermute(send, "seq", flipped("seq", 0))
            else:
                super().__init__(left_t, right, span, tile)

        def settle(self):
            if near_pair:
                sent = settle(order, self.keep, self.come, self.last, 1 - dp_index)
                self.mine = settle(order, self.keep, self.come, self.last, dp_index)
                self.final = lax.ppermute(sent, "dp", flipped("dp", 0))

        def placed(self):
            if near_pair:
                order.arrived(self.final)

        def result(self):
            return to_f(self.mine) + to_f(self.final) if near_pair else super().result()

    sent = core_swaps(narrow(order, [(mixed, o_weight)], 1, (), 1))
    mine = narrow(order, [(mixed, o_weight)], 0, sent, 1)
    come = chip_swaps(mine)
    grad_ffn, grad_ffn_t = grad_out_of(
        order, core_one, cotangent.reshape(total, width), valid.reshape(total, 1)
    )
    grad_hidden = grad_hidden_of(order, grad_ffn, down_t)
    h_one_t = turn(order, [h_one])
    middle, h_two = middle_of(order, core_one, flat_tokens, mine, come, gain_two)
    h_two += core_swaps(h_two)
    hidden, grad_gate, grad_up = gated(order, h_two, grad_hidden, gate_t, up_t)

    down_a = Rows(grad_ffn_t, hidden, (0, cut))
    down_b = SeqFirst(grad_ffn_t, hidden, (cut, tiles - cut))
    pairs = [(grad_gate, gate_t), (grad_up, up_t)]
    sent = core_swaps(narrow(order, pairs, 1))
    mine = narrow(order, pairs, 0, sent)
    come = chip_swaps(mine)
    h_two_t = turn(order, h_two)
    gate_a = Rows(h_two_t, grad_gate, (0, long))
    down_b.relay()
    down_a.own()
    grad_middle, *branch = norm_back(order, core_one, mine, come, middle, gain_two, grad_ffn, False)
    branch += core_swaps(branch)
    grad_mixed = mixed_back(order, branch, o_weight).reshape(rows, local, heads * HD)
    gate_b = Rows(h_two_t, grad_gate, (long, tiles - long))
    grad_q_rows, keep, *sends = attend_back(
        order, low, core_one, q_rows, start, span, mate, grad_mixed, mixed_rows, lse, cosine, sine
    )
    comes = core_swaps([sends[(i + rows // 2) % rows] for i in range(rows)])
    branch_t = turn(order, branch)
    own_kv, *pieces = fold(order, keep, comes, local)
    moving = shifted(pieces[-1], -1) if pieces else None
    down_b.settled()
    gate_a.own()
    for piece in pieces[-2::-1]:
        moving = shifted(carry(order, piece, moving), -1)
    down_a.relay()
    grad_qkv, bias_sum = join(
        order, core_one, grad_q_rows, own_kv, [] if moving is None else [moving], cosine, sine
    )
    up_a = Rows(h_two_t, grad_up, (0, cut))
    sent = core_swaps(narrow(order, [(grad_qkv, weight)], 1, (), 1))
    gate_a.relay()
    gate_b.own()
    mine = narrow(order, [(grad_qkv, weight)], 0, sent, 1)
    come = chip_swaps(mine)
    up_b = Rows(h_two_t, grad_up, (cut, tiles - cut))
    ffn_sent = core_swaps(narrow(order, [(hidden, down_t)], 1))
    qkv = Rows(h_one_t, grad_qkv, (0, grad_qkv.shape[1] // TILE))
    ffn_mine = narrow(order, [(hidden, down_t)], 0, ffn_sent)
    ffn_come = chip_swaps(ffn_mine)
    out = Rows(branch_t, mixed, (0, heads), HD)
    down_a.settled()
    gate_a.settled()
    gate_b.relay()
    up_a.own()
    token = norm_back(order, core_one, mine, come, flat_tokens, gain_one, grad_middle, True)
    token += core_swaps(token)
    down_b.settle()
    gate_b.settled()
    up_b.own()
    up_a.relay()
    token_grad = place(order, core_one, token).reshape(rows, local, width)
    qkv.own()
    down_b.placed()
    up_b.relay()
    up_a.settled()
    layer = layer_of(order, middle, ffn_mine, ffn_come)
    layer += core_swaps(layer)
    out.own()
    if near_pair:
        bias_come = lax.ppermute(bias_sum, "dp", flipped("dp", 0))
        bias_all = bias_add(order, bias_sum, bias_come)
        bias_come = lax.ppermute(bias_all, "seq", flipped("seq", 0))
    qkv.relay()
    layer_out = place(order, core_one, layer).reshape(rows, local, width)
    up_b.settled()
    out.relay()
    if near_pair:
        bias_all = bias_add(order, bias_all, bias_come)
        bias_come = lax.ppermute(bias_all, "seq", flipped("seq", 1))
        bias_all = (bias_all + bias_come)[:1]
    else:
        bias_all = lax.psum(bias_sum[:1], ("dp", "seq"))
    qkv_grad = qkv.result()
    o_grad = out.result()
    down_grad = jnp.concatenate([down_a.result(), down_b.result()], axis=1)[:, :units]
    gate_grad = jnp.concatenate([gate_a.result(), gate_b.result()], axis=1)[:, :units]
    up_grad = jnp.concatenate([up_a.result(), up_b.result()], axis=1)[:, :units]

    begin = (dp_index * seqs + seq_index) * share

    def rows_of(value):
        return to_f(lax.dynamic_slice_in_dim(value, begin, share, 0))

    attn_term = jnp.sum(rows_of(weight) * qkv_grad, axis=1)
    ffn_term = jnp.sum(rows_of(gate_weight) * gate_grad + rows_of(up_weight) * up_grad, axis=1)
    columns = heads * HD
    room = -(-share // HD) * HD - share
    terms = jnp.pad(jnp.stack([ffn_term, attn_term]), ((0, 0), (0, room))).reshape(-1, HD)
    packed = jnp.concatenate([qkv_grad[:, columns:], bias_all.reshape(-1, HD), terms], axis=0)
    gathered = tensor_gather(packed, rank)
    term_rows = terms.shape[0]
    bias_count = bias_all.shape[1] // HD
    terms = gathered[:, share + bias_count :].reshape(ranks, 2, -1)[:, :, :share]
    ffn_gain_grad, attn_gain_grad = terms[0] + terms[1] + (terms[2] + terms[3])
    attn_gain_grad = attn_gain_grad / lax.dynamic_slice_in_dim(gain_one[0], begin, share, 0)
    ffn_gain_grad = ffn_gain_grad / lax.dynamic_slice_in_dim(gain_two[0], begin, share, 0)
    q_grad = qkv_grad[:, :columns]
    kv_parts = lax.dynamic_slice_in_dim(gathered, rank * (share // ranks), share // ranks, 1)
    k_grad = jnp.concatenate([kv_parts[2 * i] for i in range(KVH)], axis=1)
    v_grad = jnp.concatenate([kv_parts[2 * i + 1] for i in range(KVH)], axis=1)
    biases = gathered[:, share : share + bias_count]
    q_bias_grad = biases[:, :heads].reshape(-1)
    k_bias_grad = biases[0::2, heads].reshape(-1)
    v_bias_grad = biases[1::2, heads].reshape(-1)
    return (
        layer_out,
        token_grad,
        q_grad,
        q_bias_grad,
        k_grad,
        k_bias_grad,
        v_grad,
        v_bias_grad,
        o_grad,
        attn_gain_grad,
        ffn_gain_grad,
        gate_grad,
        up_grad,
        down_grad,
    )


def solution(mesh):
    in_specs = (
        P("dp", "seq", None),
        P("dp", None),
        P("dp", "seq", None),
        P(None, "tensor"),
        P("tensor"),
        P(),
        P(),
        P(),
        P(),
        P(None, "tensor"),
        P(),
        P(),
        P(None, "tensor"),
        P(None, "tensor"),
        P(None, "tensor"),
    )
    out_specs = (
        P("dp", "seq", None),
        P("dp", "seq", None),
        P(("dp", "seq"), "tensor"),
        P(),
        P(("dp", "seq", "tensor"), None),
        P(),
        P(("dp", "seq", "tensor"), None),
        P(),
        P(("dp", "seq"), "tensor"),
        P(("dp", "seq")),
        P(("dp", "seq")),
        P(("dp", "seq"), "tensor"),
        P(("dp", "seq"), "tensor"),
        P(("dp", "seq"), "tensor"),
    )
    return jax.shard_map(body, mesh=mesh, in_specs=in_specs, out_specs=out_specs, check_vma=False)
```

```python
import functools
import math

import jax
import jax.numpy as jnp
from jax import lax
from jax.experimental import pallas as pl
from jax.experimental.pallas import tpu as pltpu
from jax.sharding import PartitionSpec as P

KVH = 2
HD = 128
MOST = 1024
EPS = 1e-06
ROPE_BASE = 10000.0
NEG_FILL = -1e30
Q_BLOCK = 256
K_BLOCK = 256
MIB = 1 << 20
LIGHT = 1000
TILE = 256
PIECES = 2
SCALE = 1.0 / math.sqrt(HD)


def to_bf(value):
    return value.astype(jnp.bfloat16)


def to_f(value):
    return value.astype(jnp.float32)


def dot(left, right, left_dim=1, right_dim=0):
    return lax.dot_general(
        left,
        right,
        (((left_dim,), (right_dim,)), ((), ())),
        preferred_element_type=jnp.float32,
    )


def flipped(axis, bit):
    return [(i, i ^ (1 << bit)) for i in range(lax.axis_size(axis))]


def core_swap(value):
    return lax.ppermute(value, "tensor", flipped("tensor", 0))


def chip_swap(value):
    return lax.ppermute(value, "tensor", flipped("tensor", 1))


def core_swaps(values):
    return [core_swap(value) for value in values]


def chip_swaps(values):
    return [chip_swap(value) for value in values]


def shifted(value, hops):
    count = lax.axis_size("seq")
    route = [(i, i + hops) for i in range(count) if 0 <= i + hops < count]
    return lax.ppermute(value, "seq", route)


def cost(flops, read):
    return pl.CostEstimate(flops=flops // LIGHT, bytes_accessed=read // LIGHT, transcendentals=0)


class Order:
    def __init__(self):
        self.mark = None
        self.touched = []

    def arrived(self, *values):
        self.touched.extend(values)

    def __call__(self, kernel, args, in_specs, out_specs, out_shape, grid, flops, read, name, scalars=(), scratch=()):
        anchor = ([] if self.mark is None else [self.mark]) + self.touched
        self.touched = []
        count = len(scalars) + len(args)
        outs = len(out_shape)

        def run(*refs):
            rest = refs[count + len(anchor) :]
            kernel(*refs[:count], *rest[:outs], *rest[outs + 1 :])
            rest[outs][...] = jnp.zeros(rest[outs].shape, jnp.float32)

        *results, self.mark = pl.pallas_call(
            run,
            grid_spec=pltpu.PrefetchScalarGridSpec(
                num_scalar_prefetch=len(scalars),
                grid=grid,
                in_specs=list(in_specs) + anchors(len(anchor)),
                out_specs=list(out_specs) + [mark_spec()],
                scratch_shapes=list(scratch),
            ),
            out_shape=list(out_shape) + [MARK],
            compiler_params=pltpu.CompilerParams(vmem_limit_bytes=60 * MIB),
            cost_estimate=cost(flops, read),
            name=name,
        )(*scalars, *args, *anchor)
        return results


def first_kernel(core_ref, tok_ref, gain_ref, w_ref, b_ref, cos_ref, sin_ref, h_ref, q_ref, kv_ref):
    x = to_f(tok_ref[...])
    factor = lax.rsqrt(jnp.mean(x * x, axis=-1, keepdims=True) + EPS)
    h = to_bf(x * factor * gain_ref[...])
    h_ref[...] = h
    lin = dot(h, w_ref[...]) + b_ref[...]
    cosine = cos_ref[...]
    sine = sin_ref[...]
    heads = q_ref.shape[1] // HD
    for head in range(heads):
        part = lin[:, head * HD : (head + 1) * HD]
        q_ref[:, head * HD : (head + 1) * HD] = to_bf(
            part * cosine + pltpu.roll(part, HD // 2, 1) * sine
        )
    part = lin[:, heads * HD :]
    is_key = core_ref[0] == 0
    kv_ref[...] = to_bf(
        part * jnp.where(is_key, cosine, 1.0)
        + pltpu.roll(part, HD // 2, 1) * jnp.where(is_key, sine, 0.0)
    )


def first(core, tokens, gain, weight, bias, cosine, sine):
    total, width = tokens.shape
    columns = weight.shape[1]
    block = total // 4
    half = 2

    def flip(i, core_ref):
        return (lax.rem(i + core_ref[0] * half, 4), 0)

    def at(i, core_ref):
        return (i, 0)

    def whole(i, core_ref):
        return (0, 0)

    return pl.pallas_call(
        first_kernel,
        grid_spec=pltpu.PrefetchScalarGridSpec(
            num_scalar_prefetch=1,
            grid=(4,),
            in_specs=[
                pl.BlockSpec((block, width), flip),
                pl.BlockSpec((1, width), whole),
                pl.BlockSpec((width, columns), whole),
                pl.BlockSpec((1, columns), whole),
                pl.BlockSpec((block, HD), at),
                pl.BlockSpec((block, HD), at),
            ],
            out_specs=[
                pl.BlockSpec((block, width), at),
                pl.BlockSpec((block, columns - HD), at),
                pl.BlockSpec((block, HD), at),
            ],
        ),
        out_shape=[
            jax.ShapeDtypeStruct((total, width), jnp.bfloat16),
            jax.ShapeDtypeStruct((total, columns - HD), jnp.bfloat16),
            jax.ShapeDtypeStruct((total, HD), jnp.bfloat16),
        ],
        compiler_params=pltpu.CompilerParams(vmem_limit_bytes=60 * MIB),
        cost_estimate=cost(2 * total * width * columns, 9 * MIB),
        name="first",
    )(core, tokens, gain, weight, bias, cosine, sine)


def stacked(ref, start, count, heads):
    return jnp.concatenate(
        [ref[0, pl.ds(start, count), h * HD : (h + 1) * HD] for h in range(heads)], axis=0
    )


def bounds(start_ref, index, heads, reach):
    first_key = jnp.concatenate(
        [start_ref[0, :, pl.ds(index * Q_BLOCK, Q_BLOCK)]] * heads, axis=1
    )
    place = reach + index * Q_BLOCK + lax.broadcasted_iota(jnp.int32, (1, Q_BLOCK), 1)
    return first_key, jnp.concatenate([place] * heads, axis=1)


def gather_span(core, refs, span):
    count = len(refs) // 2
    local = refs[0].shape[1]
    for i in range(count):
        here = slice(i * local, (i + 1) * local)
        span[core, here] = refs[i][0]
        span[1 - core, here] = refs[count + i][0]


def attend_kernel(heads, blocks, pieces, low_ref, core_ref, q_ref, start_ref, *refs):
    o_ref, lse_ref, acc, span = refs[2 * pieces :]
    row = pl.program_id(0)
    wide = heads * Q_BLOCK
    reach = (pieces - 1) * q_ref.shape[1]
    gather_span(core_ref[0], refs[: 2 * pieces], span)
    for index in range(blocks):
        q = stacked(q_ref, index * Q_BLOCK, Q_BLOCK, heads)
        first_key, place = bounds(start_ref, index, heads, reach)
        acc[...] = jnp.zeros_like(acc)

        def step(j, carry):
            top, total = carry
            keys = pl.ds(pl.multiple_of(j * K_BLOCK, K_BLOCK), K_BLOCK)
            s = dot(span[0, keys], q, 1, 1) * SCALE
            key = j * K_BLOCK + lax.broadcasted_iota(jnp.int32, (K_BLOCK, wide), 0)
            s = jnp.where((key >= first_key) & (key <= place), s, NEG_FILL)
            later = jnp.maximum(top, jnp.max(s, axis=0, keepdims=True))
            p = jnp.exp(s - later)
            fade = jnp.exp(top - later)
            total = total * fade + jnp.sum(p, axis=0, keepdims=True)
            acc[...] = acc[...] * fade + dot(span[1, keys], to_bf(p), 0, 0)
            return later, total

        last = (reach + (index + 1) * Q_BLOCK - 1) // K_BLOCK + 1
        top, total = lax.fori_loop(
            low_ref[row, index],
            last,
            step,
            (jnp.full((1, wide), NEG_FILL, jnp.float32), jnp.zeros((1, wide), jnp.float32)),
        )
        out = to_bf((acc[...] / total).T)
        for h in range(heads):
            o_ref[0, index * Q_BLOCK : (index + 1) * Q_BLOCK, h * HD : (h + 1) * HD] = out[
                h * Q_BLOCK : (h + 1) * Q_BLOCK
            ]
        lse_ref[0, index : index + 1, :] = top + jnp.log(total)


def span_specs(rows, local, pieces):
    near = pl.BlockSpec((1, local, HD), lambda i, *refs: (i, 0, 0))
    far = pl.BlockSpec((1, local, HD), lambda i, *refs: (lax.rem(i + rows // 2, rows), 0, 0))
    return [near] * pieces + [far] * pieces


def attend(low, core, q, start, span, mate):
    rows, local, columns = q.shape
    pieces = len(span)
    heads = columns // HD
    blocks = local // Q_BLOCK

    def at(i, *refs):
        return (i, 0, 0)

    return pl.pallas_call(
        functools.partial(attend_kernel, heads, blocks, pieces),
        grid_spec=pltpu.PrefetchScalarGridSpec(
            num_scalar_prefetch=2,
            grid=(rows,),
            in_specs=[pl.BlockSpec((1, local, columns), at), pl.BlockSpec((1, 1, local), at)]
            + span_specs(rows, local, pieces),
            out_specs=[
                pl.BlockSpec((1, local, columns), at),
                pl.BlockSpec((1, blocks, heads * Q_BLOCK), at),
            ],
            scratch_shapes=[
                pltpu.VMEM((HD, heads * Q_BLOCK), jnp.float32),
                pltpu.VMEM((2, pieces * local, HD), jnp.bfloat16),
            ],
        ),
        out_shape=[
            jax.ShapeDtypeStruct((rows, local, columns), jnp.bfloat16),
            jax.ShapeDtypeStruct((rows, blocks, heads * Q_BLOCK), jnp.float32),
        ],
        compiler_params=pltpu.CompilerParams(vmem_limit_bytes=60 * MIB),
        cost_estimate=cost(8_000_000_000, 4 * MIB),
        name="attend",
    )(low, core, q, start, *span, *mate)


def attend_back_kernel(
    heads, blocks, pieces, low_ref, core_ref, q_ref, start_ref, g_ref, o_ref, lse_ref, cos_ref, sin_ref, *refs
):
    gq_ref, keep_ref, *sends, acc, gk, gv, span = refs[2 * pieces :]
    row = pl.program_id(0)
    wide = heads * Q_BLOCK
    reach = (pieces - 1) * q_ref.shape[1]
    core = core_ref[0]
    gather_span(core, refs[: 2 * pieces], span)
    gk[...] = jnp.zeros_like(gk)
    gv[...] = jnp.zeros_like(gv)
    for index in range(blocks):
        q = stacked(q_ref, index * Q_BLOCK, Q_BLOCK, heads)
        g = stacked(g_ref, index * Q_BLOCK, Q_BLOCK, heads)
        o = stacked(o_ref, index * Q_BLOCK, Q_BLOCK, heads)
        inner = jnp.sum((to_f(g) * to_f(o)).T, axis=0, keepdims=True)
        lse = lse_ref[0, index : index + 1, :]
        first_key, place = bounds(start_ref, index, heads, reach)
        acc[...] = jnp.zeros_like(acc)

        def step(j, carry):
            keys = pl.ds(pl.multiple_of(j * K_BLOCK, K_BLOCK), K_BLOCK)
            k = span[0, keys]
            s = dot(k, q, 1, 1) * SCALE
            key = j * K_BLOCK + lax.broadcasted_iota(jnp.int32, (K_BLOCK, wide), 0)
            p = jnp.where((key >= first_key) & (key <= place), jnp.exp(s - lse), 0.0)
            gp = dot(span[1, keys], g, 1, 1)
            gs = to_bf(p * (gp - inner))
            gv[keys] += dot(to_bf(p), g)
            gk[keys] += dot(gs, q)
            acc[...] += dot(k, gs, 0, 0)
            return carry

        last = (reach + (index + 1) * Q_BLOCK - 1) // K_BLOCK + 1
        lax.fori_loop(low_ref[row, index], last, step, 0)
        gq = acc[...].T * SCALE
        here = slice(index * Q_BLOCK, (index + 1) * Q_BLOCK)
        cosine, sine = cos_ref[here], sin_ref[here]
        for h in range(heads):
            part = gq[h * Q_BLOCK : (h + 1) * Q_BLOCK]
            gq_ref[0, here, h * HD : (h + 1) * HD] = to_bf(
                part * cosine + pltpu.roll(part * sine, HD // 2, 1)
            )
    is_key = core == 0
    keys, values = gk[...] * SCALE, gv[...]
    keep_ref[0] = to_bf(jnp.where(is_key, keys, values))
    sent = to_bf(jnp.where(is_key, values, keys))
    for i, ref in enumerate(sends):

        @pl.when(row == i)
        def _(ref=ref):
            ref[0] = sent


def attend_back(order, low, core, q, start, span, mate, grad, out, lse, cosine, sine):
    rows, local, columns = q.shape
    pieces = len(span)
    window = pieces * local
    heads = columns // HD
    blocks = local // Q_BLOCK

    def at(i, *refs):
        return (i, 0, 0)

    table = pl.BlockSpec((local, HD), lambda i, *refs: (i, 0))
    tokens = pl.BlockSpec((1, local, columns), at)
    return order(
        functools.partial(attend_back_kernel, heads, blocks, pieces),
        [q, start, grad, out, lse, cosine, sine, *span, *mate],
        [
            tokens,
            pl.BlockSpec((1, 1, local), at),
            tokens,
            tokens,
            pl.BlockSpec((1, blocks, heads * Q_BLOCK), at),
            table,
            table,
        ]
        + span_specs(rows, local, pieces),
        [tokens, pl.BlockSpec((1, window, HD), at)]
        + [pl.BlockSpec((1, window, HD), lambda i, *refs: (0, 0, 0))] * rows,
        [
            jax.ShapeDtypeStruct((rows, local, columns), jnp.bfloat16),
            jax.ShapeDtypeStruct((rows, window, HD), jnp.bfloat16),
        ]
        + [jax.ShapeDtypeStruct((1, window, HD), jnp.bfloat16)] * rows,
        (rows,),
        20_000_000_000,
        6 * MIB,
        "attend_back",
        scalars=(low, core),
        scratch=[
            pltpu.VMEM((HD, heads * Q_BLOCK), jnp.float32),
            pltpu.VMEM((window, HD), jnp.float32),
            pltpu.VMEM((window, HD), jnp.float32),
            pltpu.VMEM((2, window, HD), jnp.bfloat16),
        ],
    )


def fold_kernel(rows, keep_ref, *refs):
    comes, own_ref, send_refs = refs[:rows], refs[rows], refs[rows + 1 :]
    local = own_ref.shape[1]
    come = comes[0][0]
    for i in range(1, rows):
        come = jnp.where(pl.program_id(0) == i, comes[i][0], come)
    total = to_f(keep_ref[0]) + to_f(come)
    reach = total.shape[0] - local
    own_ref[0] = total[reach:]
    for hop, ref in enumerate(send_refs, 1):
        ref[0] = to_bf(total[reach - hop * local : reach - (hop - 1) * local])


def fold(order, keep, comes, local):
    rows, window = keep.shape[:2]
    hops = window // local - 1
    out = pl.BlockSpec((1, local, HD), lambda i: (i, 0, 0))
    return order(
        functools.partial(fold_kernel, rows),
        [keep, *comes],
        [pl.BlockSpec((1, window, HD), lambda i: (i, 0, 0))]
        + [pl.BlockSpec((1, window, HD), lambda i: (0, 0, 0))] * rows,
        [out] * (hops + 1),
        [jax.ShapeDtypeStruct((rows, local, HD), jnp.float32)]
        + [jax.ShapeDtypeStruct((rows, local, HD), jnp.bfloat16)] * hops,
        (rows,),
        0,
        4 * MIB,
        "fold",
    )


def carry_kernel(piece_ref, come_ref, out_ref):
    out_ref[...] = to_bf(to_f(piece_ref[...]) + to_f(come_ref[...]))


def carry(order, piece, come):
    rows, local, columns = piece.shape
    at = pl.BlockSpec((1, local, columns), lambda i: (i, 0, 0))
    return order(
        carry_kernel,
        [piece, come],
        [at, at],
        [at],
        [jax.ShapeDtypeStruct(piece.shape, jnp.bfloat16)],
        (rows,),
        0,
        2 * MIB,
        "carry",
    )[0]


def bias_kernel(left_ref, right_ref, out_ref):
    out_ref[...] = left_ref[...] + right_ref[...]


def bias_add(order, left, right):
    whole = pl.BlockSpec(left.shape, lambda i: (0, 0))
    return order(
        bias_kernel,
        [left, right],
        [whole, whole],
        [whole],
        [jax.ShapeDtypeStruct(left.shape, jnp.float32)],
        (1,),
        0,
        MIB,
        "bias",
    )[0]


def join_kernel(hops, core_ref, gq_ref, cos_ref, sin_ref, own_ref, *refs):
    out_ref, sum_ref = refs[-2:]
    columns = gq_ref.shape[2]
    grad = own_ref[0]
    for ref in refs[:hops]:
        grad = grad + to_f(ref[0])
    is_key = core_ref[0] == 0
    cosine = jnp.where(is_key, cos_ref[...], 1.0)
    sine = jnp.where(is_key, sin_ref[...], 0.0)
    kv = to_bf(grad * cosine + pltpu.roll(grad * sine, HD // 2, 1))
    q = gq_ref[0]
    out_ref[:, :columns] = q
    out_ref[:, columns:] = kv

    @pl.when(pl.program_id(0) == 0)
    def _():
        sum_ref[...] = jnp.zeros(sum_ref.shape, jnp.float32)

    sum_ref[:, :columns] += jnp.sum(to_f(q), axis=0, keepdims=True)
    sum_ref[:, columns:] += jnp.sum(to_f(kv), axis=0, keepdims=True)


def join(order, core, grad_q, own, comes, cosine, sine):
    rows, local, columns = grad_q.shape
    wide = columns + HD

    def at(i, *refs):
        return (i, 0, 0)

    piece = pl.BlockSpec((1, local, HD), at)
    table = pl.BlockSpec((local, HD), lambda i, *refs: (i, 0))
    return order(
        functools.partial(join_kernel, len(comes)),
        [grad_q, cosine, sine, own, *comes],
        [pl.BlockSpec((1, local, columns), at), table, table, piece] + [piece] * len(comes),
        [
            pl.BlockSpec((local, wide), lambda i, *refs: (i, 0)),
            pl.BlockSpec((8, wide), lambda i, *refs: (0, 0)),
        ],
        [
            jax.ShapeDtypeStruct((rows * local, wide), jnp.bfloat16),
            jax.ShapeDtypeStruct((8, wide), jnp.float32),
        ],
        (rows,),
        0,
        4 * MIB,
        "join",
        scalars=(core,),
    )


def mixed_back_kernel(w_ref, *refs):
    rows = refs[0].shape[0]
    for i, ref in enumerate(refs[:-1]):
        refs[-1][i * rows : (i + 1) * rows] = to_bf(dot(ref[...], w_ref[...]))


def mixed_back(order, pieces, weight):
    rows, width = pieces[0].shape
    total = rows * len(pieces)
    columns = weight.shape[1]

    def whole(i):
        return (0, 0)

    return order(
        mixed_back_kernel,
        [weight, *pieces],
        [pl.BlockSpec((width, columns), whole)] + [pl.BlockSpec((rows, width), whole)] * len(pieces),
        [pl.BlockSpec((total, columns), whole)],
        [jax.ShapeDtypeStruct((total, columns), jnp.bfloat16)],
        (1,),
        2 * total * width * columns,
        6 * MIB,
        "mixed_back",
    )[0]


def place_kernel(core_ref, *refs):
    for i, ref in enumerate(refs[:-1]):

        @pl.when(pl.program_id(0) == i)
        def _(ref=ref):
            refs[-1][...] = ref[...]


def place(order, core, pieces):
    rows, width = pieces[0].shape
    count = len(pieces)
    return order(
        place_kernel,
        list(pieces),
        [pl.BlockSpec((rows, width), lambda i, core_ref: (0, 0))] * count,
        [pl.BlockSpec((rows, width), lambda i, core_ref: (lax.rem(i + core_ref[0] * (count // 2), count), 0))],
        [jax.ShapeDtypeStruct((rows * count, width), pieces[0].dtype)],
        (count,),
        0,
        8 * rows * width,
        "place",
        scalars=(core,),
    )[0]


def anchors(count):
    return [pl.BlockSpec(memory_space=pl.ANY)] * count


MARK = jax.ShapeDtypeStruct((8, HD), jnp.float32)


def mark_spec():
    return pl.BlockSpec((8, HD), lambda *refs: (0, 0))


def grad_hidden_kernel(g_ref, w_ref, out_ref):
    out_ref[...] = to_bf(dot(g_ref[...], w_ref[...], 1, 1))


def grad_hidden_of(order, grad, weight):
    total, width = grad.shape
    hidden = weight.shape[0]
    return order(
        grad_hidden_kernel,
        [grad, weight],
        [pl.BlockSpec((total, width), lambda i: (0, 0)), pl.BlockSpec((TILE, width), lambda i: (i, 0))],
        [pl.BlockSpec((total, TILE), lambda i: (0, i))],
        [jax.ShapeDtypeStruct((total, hidden), jnp.bfloat16)],
        (pl.cdiv(hidden, TILE),),
        2 * total * width * hidden,
        15 * MIB,
        "grad_hidden",
    )[0]


def gated_kernel(gh_ref, gw_ref, uw_ref, *refs):
    hid_ref, gg_ref, gu_ref = refs[-3:]
    rows = refs[0].shape[0]
    for part, ref in enumerate(refs[:-3]):
        here = slice(part * rows, (part + 1) * rows)
        h = ref[...]
        gate = dot(h, gw_ref[...], 1, 1)
        up = dot(h, uw_ref[...], 1, 1)
        grad = to_f(gh_ref[here])
        sigma = 1.0 / (1.0 + jnp.exp(-gate))
        swish = gate * sigma
        hid_ref[here] = to_bf(swish * up)
        gu_ref[here] = to_bf(grad * swish)
        gg_ref[here] = to_bf(grad * up * sigma * (1.0 + gate * (1.0 - sigma)))


def gated(order, pieces, grad_hidden, gate_weight, up_weight):
    rows, width = pieces[0].shape
    total = rows * len(pieces)
    hidden = gate_weight.shape[0]
    column = pl.BlockSpec((total, TILE), lambda i: (0, i))
    weight = pl.BlockSpec((TILE, width), lambda i: (i, 0))
    shape = jax.ShapeDtypeStruct((total, hidden), jnp.bfloat16)
    return order(
        gated_kernel,
        [grad_hidden, gate_weight, up_weight, *pieces],
        [column, weight, weight] + [pl.BlockSpec((rows, width), lambda i: (0, 0))] * len(pieces),
        [column] * 3,
        [shape] * 3,
        (pl.cdiv(hidden, TILE),),
        4 * total * width * hidden,
        30 * MIB,
        "gated",
    )


def share_kernel(columns, skip, extra, halves, pick_ref, blocks_ref, left_ref, right_ref, *refs):
    out = dot(left_ref[...], right_ref[...])
    if extra:
        out = out + to_f(refs[0][...])
        refs = refs[1:]
    tile = out.shape[1]
    spot = (pl.program_id(0) + skip) * tile + lax.broadcasted_iota(jnp.int32, (1, tile), 1)
    out = to_bf(jnp.where(spot < columns, out, 0.0))
    if not halves:
        refs[0][...] = out
        return
    send_ref, keep_ref, rows = refs
    rows[...] = out
    share = send_ref.shape[0] // (2 * halves)
    for i in range(2 * halves):
        here = slice(i * share, (i + 1) * share)
        send_ref[here] = rows[pl.ds(pl.multiple_of(blocks_ref[i] * share, share), share)]
        keep_ref[here] = rows[pl.ds(pl.multiple_of(blocks_ref[2 * halves + i] * share, share), share)]


def share_of(order, left, right, part, pick, span, tile=0, extra=None, blocks=None):
    tokens, columns = right.shape
    tile = tile or TILE
    skip, count = span
    column = pl.BlockSpec((part, tile), lambda i, *refs: (0, i))
    extras = [] if extra is None else [extra]
    scratch = []
    outs, shapes = [column], [jax.ShapeDtypeStruct((part, count * tile), jnp.bfloat16)]
    halves = 0
    if blocks is None:
        blocks = jnp.zeros((1,), jnp.int32)
    else:
        halves = blocks.shape[0] // 4
        outs = [pl.BlockSpec((part // 2, tile), lambda i, *refs: (0, i))] * 2
        shapes = [jax.ShapeDtypeStruct((part // 2, count * tile), jnp.bfloat16)] * 2
        scratch = [pltpu.VMEM((part, tile), jnp.bfloat16)]
    result = order(
        functools.partial(share_kernel, columns, skip, len(extras), halves),
        [left, right, *extras],
        [
            pl.BlockSpec((part, tokens), lambda i, pick_ref, blocks_ref: (pick_ref[0], 0)),
            pl.BlockSpec((tokens, tile), lambda i, *refs: (0, i + skip)),
        ]
        + [column] * len(extras),
        outs,
        shapes,
        (count,),
        2 * part * tokens * count * tile,
        2 * (part * tokens + (part + tokens) * count * tile),
        "share",
        scalars=(jnp.asarray(pick, jnp.int32).reshape(1), blocks),
        scratch=scratch,
    )
    return result if halves else result[0]


def relay_kernel(keep_ref, come_ref, out_ref):
    out_ref[...] = to_bf(to_f(keep_ref[...]) + to_f(come_ref[...]))


def relay(order, keep, come, share):
    rows, columns = keep.shape
    pair = pl.BlockSpec((share, columns), lambda i: (2 * i + 1, 0))
    return order(
        relay_kernel,
        [keep, come],
        [pair, pair],
        [pl.BlockSpec((share, columns), lambda i: (i, 0))],
        [jax.ShapeDtypeStruct((rows // 2, columns), jnp.bfloat16)],
        (rows // (2 * share),),
        0,
        3 * rows * columns,
        "relay",
    )[0]


def settle_kernel(pick_ref, keep_ref, come_ref, last_ref, out_ref):
    out_ref[...] = to_bf(to_f(keep_ref[...]) + to_f(come_ref[...]) + to_f(last_ref[...]))


def settle(order, keep, come, last, pick):
    share = last.shape[0] // 2
    columns = keep.shape[1]
    pair = pl.BlockSpec((share, columns), lambda i, pick_ref: (2 * pick_ref[0], 0))
    return order(
        settle_kernel,
        [keep, come, last],
        [pair, pair, pl.BlockSpec((share, columns), lambda i, pick_ref: (pick_ref[0], 0))],
        [pl.BlockSpec((share, columns), lambda i, pick_ref: (0, 0))],
        [jax.ShapeDtypeStruct((share, columns), jnp.bfloat16)],
        (1,),
        0,
        8 * share * columns,
        "settle",
        scalars=(pick.reshape(1),),
    )[0]


def narrow_kernel(pairs, extras, right_dim, *refs):
    out = dot(refs[0][...], refs[1][...], 1, right_dim)
    for i in range(1, pairs):
        out = out + dot(refs[2 * i][...], refs[2 * i + 1][...], 1, right_dim)
    extra = refs[2 * pairs : 2 * pairs + extras]
    outs = refs[2 * pairs + extras :]
    if extras:
        out = out + jnp.concatenate([to_f(ref[...]) for ref in extra], axis=0)
    rows = outs[0].shape[0]
    for i, ref in enumerate(outs):
        ref[...] = to_bf(out[i * rows : (i + 1) * rows])


def narrow(order, pairs, index, extra=(), right_dim=0):
    total, hidden = pairs[0][0].shape
    width = pairs[0][1].shape[1 - right_dim]
    half = total // 2
    piece = half // PIECES
    column = pl.BlockSpec((piece, TILE), lambda i: (0, i))
    right = (
        pl.BlockSpec((TILE, hidden), lambda i: (i, 0))
        if right_dim
        else pl.BlockSpec((hidden, TILE), lambda i: (0, i))
    )
    return order(
        functools.partial(narrow_kernel, len(pairs), len(extra), right_dim),
        [item for pair in pairs for item in pair] + list(extra),
        [pl.BlockSpec((half, hidden), lambda i: (index, 0)), right] * len(pairs) + [column] * len(extra),
        [column] * PIECES,
        [jax.ShapeDtypeStruct((piece, width), jnp.bfloat16)] * PIECES,
        (width // TILE,),
        2 * len(pairs) * half * width * hidden,
        2 * len(pairs) * (half + width) * hidden + 2 * half * width,
        "narrow",
    )


def piece_specs(piece, width, block):
    steps = piece // block
    return [
        pl.BlockSpec((block, width), lambda i, *refs, j=j: (jnp.clip(i - j * steps, 0, steps - 1), 0))
        for j in range(PIECES)
    ]


def pick_piece(refs):
    value = refs[0][...]
    for j, ref in enumerate(refs[1:], 1):
        value = jnp.where(pl.program_id(0) >= 4 * j // len(refs), ref[...], value)
    return value


def put_piece(refs, value):
    steps = 4 // len(refs)
    for j, ref in enumerate(refs):

        @pl.when(lax.div(pl.program_id(0), steps) == j)
        def _(ref=ref):
            ref[...] = value


def turn_kernel(*refs):
    rows = refs[0].shape[0]
    for i, ref in enumerate(refs[:-1]):
        refs[-1][:, i * rows : (i + 1) * rows] = ref[...].T


def turn(order, pieces):
    rows, width = pieces[0].shape
    total = rows * len(pieces)
    return order(
        turn_kernel,
        list(pieces),
        [pl.BlockSpec((rows, TILE), lambda i: (0, i))] * len(pieces),
        [pl.BlockSpec((TILE, total), lambda i: (i, 0))],
        [jax.ShapeDtypeStruct((width, total), jnp.bfloat16)],
        (width // TILE,),
        0,
        4 * total * width,
        "turn",
    )[0]


def grad_out_kernel(core_ref, cot_ref, valid_ref, out_ref, turned_ref):
    out = to_bf(to_f(cot_ref[...]) * valid_ref[...])
    out_ref[...] = out
    turned_ref[...] = out.T


def grad_out_of(order, core, cotangent, valid):
    total, width = cotangent.shape
    block = total // 4
    return order(
        grad_out_kernel,
        [cotangent, valid],
        [
            pl.BlockSpec((block, width), lambda i, core_ref: (lax.rem(i + core_ref[0] * 2, 4), 0)),
            pl.BlockSpec((block, 1), lambda i, core_ref: (i, 0)),
        ],
        [
            pl.BlockSpec((block, width), lambda i, core_ref: (i, 0)),
            pl.BlockSpec((width, block), lambda i, core_ref: (0, i)),
        ],
        [
            jax.ShapeDtypeStruct((total, width), jnp.bfloat16),
            jax.ShapeDtypeStruct((width, total), jnp.bfloat16),
        ],
        (4,),
        0,
        6 * total * width,
        "grad_out",
        scalars=(core,),
    )


def middle_kernel(core_ref, tok_ref, gain_ref, *refs):
    mine, come = pick_piece(refs[:PIECES]), pick_piece(refs[PIECES : 2 * PIECES])
    mid_ref, *h_refs = refs[2 * PIECES :]
    middle = to_f(tok_ref[...]) + (to_f(mine) + to_f(come))
    factor = lax.rsqrt(jnp.mean(middle * middle, axis=-1, keepdims=True) + EPS)
    mid_ref[...] = middle
    put_piece(h_refs, to_bf(middle * factor * gain_ref[...]))


def middle_of(order, core, tokens, mine, come, gain):
    piece, width = mine[0].shape
    half = piece * PIECES
    block = half // 4
    specs = piece_specs(piece, width, block)
    middle, *h = order(
        middle_kernel,
        [tokens, gain, *mine, *come],
        [
            pl.BlockSpec((block, width), lambda i, core_ref: (core_ref[0] * 4 + i, 0)),
            pl.BlockSpec((1, width), lambda i, core_ref: (0, 0)),
        ]
        + specs * 2,
        [pl.BlockSpec((block, width), lambda i, core_ref: (i, 0))] + specs,
        [jax.ShapeDtypeStruct((half, width), jnp.float32)]
        + [jax.ShapeDtypeStruct((piece, width), jnp.bfloat16)] * PIECES,
        (4,),
        0,
        9 * MIB,
        "middle",
        scalars=(core,),
    )
    return middle, h


def norm_back_kernel(core_ref, x_ref, gain_ref, up_ref, *refs):
    mine, come = pick_piece(refs[:PIECES]), pick_piece(refs[PIECES : 2 * PIECES])
    outs = refs[2 * PIECES :]
    grad = to_f(mine) + to_f(come)
    x = to_f(x_ref[...])
    factor = lax.rsqrt(jnp.mean(x * x, axis=-1, keepdims=True) + EPS)
    normed = x * factor
    weighted = grad * gain_ref[...]
    inner = jnp.mean(weighted * normed, axis=-1, keepdims=True)
    out = to_f(up_ref[...]) + factor * (weighted - normed * inner)
    if len(outs) > PIECES:
        outs[0][...] = out
        put_piece(outs[1:], to_bf(out))
    else:
        put_piece(outs, out)


def norm_back(order, core, mine, come, x, gain, up, by_core):
    piece, width = mine[0].shape
    half = piece * PIECES
    block = half // 4
    at = pl.BlockSpec((block, width), lambda i, core_ref: (i, 0))
    picked = pl.BlockSpec((block, width), lambda i, core_ref: (core_ref[0] * 4 + i, 0))
    specs = piece_specs(piece, width, block)
    if by_core:
        shapes = [jax.ShapeDtypeStruct((piece, width), jnp.float32)] * PIECES
    else:
        shapes = [jax.ShapeDtypeStruct((half, width), jnp.float32)]
        shapes += [jax.ShapeDtypeStruct((piece, width), jnp.bfloat16)] * PIECES
    return order(
        norm_back_kernel,
        [x, gain, up, *mine, *come],
        [picked if by_core else at, pl.BlockSpec((1, width), lambda i, core_ref: (0, 0)), at] + specs * 2,
        specs if by_core else [at] + specs,
        shapes,
        (4,),
        0,
        10 * MIB,
        "norm_back",
        scalars=(core,),
    )


def layer_kernel(middle_ref, *refs):
    mine, come = pick_piece(refs[:PIECES]), pick_piece(refs[PIECES : 2 * PIECES])
    put_piece(refs[2 * PIECES :], to_bf(middle_ref[...] + (to_f(mine) + to_f(come))))


def layer_of(order, middle, mine, come):
    piece, width = mine[0].shape
    block = piece * PIECES // 4
    specs = piece_specs(piece, width, block)
    return order(
        layer_kernel,
        [middle, *mine, *come],
        [pl.BlockSpec((block, width), lambda i: (i, 0))] + specs * 2,
        specs,
        [jax.ShapeDtypeStruct((piece, width), jnp.bfloat16)] * PIECES,
        (4,),
        0,
        5 * MIB,
        "layer",
    )


def tensor_gather(value, rank):
    mate = core_swap(value)
    pair = jnp.where(lax.rem(rank, 2) == 0, jnp.stack([value, mate]), jnp.stack([mate, value]))
    come = chip_swap(pair)
    return jnp.where(
        lax.div(rank, 2) == 0,
        jnp.concatenate([pair, come], axis=0),
        jnp.concatenate([come, pair], axis=0),
    )


def body(
    tokens,
    lengths,
    cotangent,
    q_weight,
    q_bias,
    k_weight,
    k_bias,
    v_weight,
    v_bias,
    o_weight,
    attn_gain,
    ffn_gain,
    gate_weight,
    up_weight,
    down_weight,
):
    rows, local, width = tokens.shape
    total = rows * local
    half = total // 2
    heads = q_weight.shape[1] // HD
    ranks = lax.axis_size("tensor")
    seqs = lax.axis_size("seq")
    rank = lax.axis_index("tensor")
    dp_index = lax.axis_index("dp")
    seq_index = lax.axis_index("seq")
    core = lax.rem(rank, 2)
    head = lax.div(rank, 2)
    core_one = core.reshape(1)
    hops = min(seqs - 1, -(-(MOST - 1) // local))
    reach = hops * local

    def own_first(value):
        turned = jnp.concatenate([value[rows // 2 :], value[: rows // 2]], axis=0)
        return jnp.where(core == 0, value, turned)

    slots = jnp.arange(lengths.shape[1], dtype=jnp.int32)
    lens = own_first(lengths)
    ends = jnp.sum(jnp.where(slots[None, :] <= slots[:, None], lens[:, None, :], 0), axis=2)
    spot = seq_index * local + jnp.arange(local, dtype=jnp.int32)
    begun = jnp.max(
        jnp.where(ends[:, None, :] <= spot[None, :, None], ends[:, None, :], 0), axis=2
    )
    valid = to_f(spot[None, :] < ends[:, -2:-1])
    position = (spot[None, :] - begun).reshape(total, 1)
    freqs = ROPE_BASE ** (-(jnp.arange(HD // 2, dtype=jnp.float32) * 2.0) / HD)
    angles = to_f(position) * freqs[None, :]
    cosine, sine = jnp.cos(angles), jnp.sin(angles)
    cosine = jnp.concatenate([cosine, cosine], axis=1)
    sine = jnp.concatenate([-sine, sine], axis=1)
    start = begun - (seq_index * local - reach)
    low = jnp.maximum(lax.div(jnp.maximum(start[:, ::Q_BLOCK], 0), K_BLOCK), 0)
    start = start.reshape(rows, 1, local)

    key_side = core == 0
    kv_weight = jnp.where(
        key_side,
        lax.dynamic_slice_in_dim(k_weight, head * HD, HD, 1),
        lax.dynamic_slice_in_dim(v_weight, head * HD, HD, 1),
    )
    kv_bias = jnp.where(
        key_side,
        lax.dynamic_slice_in_dim(k_bias, head * HD, HD, 0),
        lax.dynamic_slice_in_dim(v_bias, head * HD, HD, 0),
    )
    weight = jnp.concatenate([q_weight, kv_weight], axis=1)
    bias = to_f(jnp.concatenate([q_bias, kv_bias])).reshape(1, -1)
    gain_one = to_f(attn_gain).reshape(1, width)
    gain_two = to_f(ffn_gain).reshape(1, width)

    h_one, q_rot, kv = first(
        core_one, tokens.reshape(total, width), gain_one, weight, bias, cosine, sine
    )
    kv = kv.reshape(rows, local, HD)
    span = [shifted(kv, h) for h in range(hops, 0, -1)] + [kv]
    mate = [core_swap(piece) for piece in span]
    q_rows = q_rot.reshape(rows, local, heads * HD)
    mixed_rows, lse = attend(low, core_one, q_rows, start, span, mate)
    mixed = mixed_rows.reshape(total, heads * HD)

    order = Order()
    flat_tokens = tokens.reshape(total, width)
    dps = lax.axis_size("dp")
    near_pair = dps == 2 and seqs == 4
    part = width // dps
    share = part // seqs
    gate_t, up_t, down_t = gate_weight.T, up_weight.T, down_weight.T
    units = gate_t.shape[0]
    tiles = -(-units // TILE)
    cut = (tiles + 1) // 2
    long = -(-2 * tiles // 3)
    one, two = seq_index ^ 1, seq_index ^ 2
    three = seq_index ^ 3
    quad = jnp.stack([one, three, seq_index, two])
    wide = jnp.stack([one, three, one + seqs, three + seqs, seq_index, two, seq_index + seqs, two + seqs])

    class Rows:
        def __init__(self, left_t, right, span, tile=TILE):
            self.args = (left_t, right)
            self.span, self.tile = span, tile
            if near_pair:
                sent = share_of(order, left_t, right, part, 1 - dp_index, span, tile)
                self.come = lax.ppermute(sent, "dp", flipped("dp", 0))
            else:
                self.whole = share_of(order, left_t, right, width, 0, span, tile)

        def own(self):
            if near_pair:
                send, self.keep = share_of(
                    order, *self.args, part, dp_index, self.span, self.tile, self.come, quad
                )
                self.come = lax.ppermute(send, "seq", flipped("seq", 0))

        def relay(self):
            if near_pair:
                sent = relay(order, self.keep, self.come, share)
                self.last = lax.ppermute(sent, "seq", flipped("seq", 1))

        def settled(self):
            if near_pair:
                order.arrived(self.last)

        def result(self):
            if near_pair:
                return to_f(self.keep[:share]) + to_f(self.come[:share]) + to_f(self.last)
            return to_f(lax.psum_scatter(self.whole, ("dp", "seq"), scatter_dimension=0, tiled=True))

    class SeqFirst(Rows):
        def __init__(self, left_t, right, span, tile=TILE):
            self.near = near_pair
            if near_pair:
                send, self.keep = share_of(order, left_t, right, width, 0, span, tile, None, wide)
                self.come = lax.ppermute(send, "seq", flipped("seq", 0))
            else:
                super().__init__(left_t, right, span, tile)

        def settle(self):
            if near_pair:
                sent = settle(order, self.keep, self.come, self.last, 1 - dp_index)
                self.mine = settle(order, self.keep, self.come, self.last, dp_index)
                self.final = lax.ppermute(sent, "dp", flipped("dp", 0))

        def placed(self):
            if near_pair:
                order.arrived(self.final)

        def result(self):
            return to_f(self.mine) + to_f(self.final) if near_pair else super().result()

    sent = core_swaps(narrow(order, [(mixed, o_weight)], 1, (), 1))
    mine = narrow(order, [(mixed, o_weight)], 0, sent, 1)
    come = chip_swaps(mine)
    grad_ffn, grad_ffn_t = grad_out_of(
        order, core_one, cotangent.reshape(total, width), valid.reshape(total, 1)
    )
    grad_hidden = grad_hidden_of(order, grad_ffn, down_t)
    h_one_t = turn(order, [h_one])
    middle, h_two = middle_of(order, core_one, flat_tokens, mine, come, gain_two)
    h_two += core_swaps(h_two)
    hidden, grad_gate, grad_up = gated(order, h_two, grad_hidden, gate_t, up_t)

    down_a = Rows(grad_ffn_t, hidden, (0, long))
    down_b = SeqFirst(grad_ffn_t, hidden, (long, tiles - long))
    pairs = [(grad_gate, gate_t), (grad_up, up_t)]
    sent = core_swaps(narrow(order, pairs, 1))
    mine = narrow(order, pairs, 0, sent)
    come = chip_swaps(mine)
    h_two_t = turn(order, h_two)
    gate_a = Rows(h_two_t, grad_gate, (0, cut))
    down_b.relay()
    down_a.own()
    gate_b = Rows(h_two_t, grad_gate, (cut, tiles - cut))
    grad_middle, *branch = norm_back(order, core_one, mine, come, middle, gain_two, grad_ffn, False)
    branch += core_swaps(branch)
    grad_mixed = mixed_back(order, branch, o_weight).reshape(rows, local, heads * HD)
    grad_q_rows, keep, *sends = attend_back(
        order, low, core_one, q_rows, start, span, mate, grad_mixed, mixed_rows, lse, cosine, sine
    )
    comes = core_swaps([sends[(i + rows // 2) % rows] for i in range(rows)])
    branch_t = turn(order, branch)
    own_kv, *pieces = fold(order, keep, comes, local)
    moving = shifted(pieces[-1], -1) if pieces else None
    up_a = Rows(h_two_t, grad_up, (0, long))
    down_b.settled()
    for piece in pieces[-2::-1]:
        moving = shifted(carry(order, piece, moving), -1)
    gate_a.own()
    grad_qkv, bias_sum = join(
        order, core_one, grad_q_rows, own_kv, [] if moving is None else [moving], cosine, sine
    )
    sent = core_swaps(narrow(order, [(grad_qkv, weight)], 1, (), 1))
    down_a.relay()
    mine = narrow(order, [(grad_qkv, weight)], 0, sent, 1)
    come = chip_swaps(mine)
    up_b = Rows(h_two_t, grad_up, (long, tiles - long))
    gate_b.own()
    gate_a.relay()
    ffn_sent = core_swaps(narrow(order, [(hidden, down_t)], 1))
    qkv = Rows(h_one_t, grad_qkv, (0, grad_qkv.shape[1] // TILE))
    ffn_mine = narrow(order, [(hidden, down_t)], 0, ffn_sent)
    ffn_come = chip_swaps(ffn_mine)
    out = Rows(branch_t, mixed, (0, heads), HD)
    down_b.settle()
    token = norm_back(order, core_one, mine, come, flat_tokens, gain_one, grad_middle, True)
    token += core_swaps(token)
    down_a.settled()
    gate_b.relay()
    up_a.own()
    layer = layer_of(order, middle, ffn_mine, ffn_come)
    layer += core_swaps(layer)
    gate_a.settled()
    up_b.own()
    token_grad = place(order, core_one, token).reshape(rows, local, width)
    up_a.relay()
    gate_b.settled()
    qkv.own()
    layer_out = place(order, core_one, layer).reshape(rows, local, width)
    up_b.relay()
    up_a.settled()
    down_b.placed()
    out.own()
    if near_pair:
        bias_come = lax.ppermute(bias_sum, "dp", flipped("dp", 0))
        bias_all = bias_add(order, bias_sum, bias_come)
        bias_come = lax.ppermute(bias_all, "seq", flipped("seq", 0))
    qkv.relay()
    up_b.settled()
    out.relay()
    if near_pair:
        bias_all = bias_add(order, bias_all, bias_come)
        bias_come = lax.ppermute(bias_all, "seq", flipped("seq", 1))
        bias_all = (bias_all + bias_come)[:1]
    else:
        bias_all = lax.psum(bias_sum[:1], ("dp", "seq"))
    qkv_grad = qkv.result()
    o_grad = out.result()
    down_grad = jnp.concatenate([down_a.result(), down_b.result()], axis=1)[:, :units]
    gate_grad = jnp.concatenate([gate_a.result(), gate_b.result()], axis=1)[:, :units]
    up_grad = jnp.concatenate([up_a.result(), up_b.result()], axis=1)[:, :units]

    begin = (dp_index * seqs + seq_index) * share

    def rows_of(value):
        return to_f(lax.dynamic_slice_in_dim(value, begin, share, 0))

    attn_term = jnp.sum(rows_of(weight) * qkv_grad, axis=1)
    ffn_term = jnp.sum(rows_of(gate_weight) * gate_grad + rows_of(up_weight) * up_grad, axis=1)
    columns = heads * HD
    room = -(-share // HD) * HD - share
    terms = jnp.pad(jnp.stack([ffn_term, attn_term]), ((0, 0), (0, room))).reshape(-1, HD)
    packed = jnp.concatenate([qkv_grad[:, columns:], bias_all.reshape(-1, HD), terms], axis=0)
    gathered = tensor_gather(packed, rank)
    term_rows = terms.shape[0]
    bias_count = bias_all.shape[1] // HD
    terms = gathered[:, share + bias_count :].reshape(ranks, 2, -1)[:, :, :share]
    ffn_gain_grad, attn_gain_grad = terms[0] + terms[1] + (terms[2] + terms[3])
    attn_gain_grad = attn_gain_grad / lax.dynamic_slice_in_dim(gain_one[0], begin, share, 0)
    ffn_gain_grad = ffn_gain_grad / lax.dynamic_slice_in_dim(gain_two[0], begin, share, 0)
    q_grad = qkv_grad[:, :columns]
    kv_parts = lax.dynamic_slice_in_dim(gathered, rank * (share // ranks), share // ranks, 1)
    k_grad = jnp.concatenate([kv_parts[2 * i] for i in range(KVH)], axis=1)
    v_grad = jnp.concatenate([kv_parts[2 * i + 1] for i in range(KVH)], axis=1)
    biases = gathered[:, share : share + bias_count]
    q_bias_grad = biases[:, :heads].reshape(-1)
    k_bias_grad = biases[0::2, heads].reshape(-1)
    v_bias_grad = biases[1::2, heads].reshape(-1)
    return (
        layer_out,
        token_grad,
        q_grad,
        q_bias_grad,
        k_grad,
        k_bias_grad,
        v_grad,
        v_bias_grad,
        o_grad,
        attn_gain_grad,
        ffn_gain_grad,
        gate_grad,
        up_grad,
        down_grad,
    )


def solution(mesh):
    in_specs = (
        P("dp", "seq", None),
        P("dp", None),
        P("dp", "seq", None),
        P(None, "tensor"),
        P("tensor"),
        P(),
        P(),
        P(),
        P(),
        P(None, "tensor"),
        P(),
        P(),
        P(None, "tensor"),
        P(None, "tensor"),
        P(None, "tensor"),
    )
    out_specs = (
        P("dp", "seq", None),
        P("dp", "seq", None),
        P(("dp", "seq"), "tensor"),
        P(),
        P(("dp", "seq", "tensor"), None),
        P(),
        P(("dp", "seq", "tensor"), None),
        P(),
        P(("dp", "seq"), "tensor"),
        P(("dp", "seq")),
        P(("dp", "seq")),
        P(("dp", "seq"), "tensor"),
        P(("dp", "seq"), "tensor"),
        P(("dp", "seq"), "tensor"),
    )
    return jax.shard_map(body, mesh=mesh, in_specs=in_specs, out_specs=out_specs, check_vma=False)
```

```python
import functools
import math

import jax
import jax.numpy as jnp
from jax import lax
from jax.experimental import pallas as pl
from jax.experimental.pallas import tpu as pltpu
from jax.sharding import PartitionSpec as P

KVH = 2
HD = 128
MOST = 1024
EPS = 1e-06
ROPE_BASE = 10000.0
NEG_FILL = -1e30
Q_BLOCK = 256
K_BLOCK = 256
MIB = 1 << 20
LIGHT = 1000
TILE = 256
PIECES = 2
SCALE = 1.0 / math.sqrt(HD)


def to_bf(value):
    return value.astype(jnp.bfloat16)


def to_f(value):
    return value.astype(jnp.float32)


def dot(left, right, left_dim=1, right_dim=0):
    return lax.dot_general(
        left,
        right,
        (((left_dim,), (right_dim,)), ((), ())),
        preferred_element_type=jnp.float32,
    )


def flipped(axis, bit):
    return [(i, i ^ (1 << bit)) for i in range(lax.axis_size(axis))]


def core_swap(value):
    return lax.ppermute(value, "tensor", flipped("tensor", 0))


def chip_swap(value):
    return lax.ppermute(value, "tensor", flipped("tensor", 1))


def core_swaps(values):
    return [core_swap(value) for value in values]


def chip_swaps(values):
    return [chip_swap(value) for value in values]


def shifted(value, hops):
    count = lax.axis_size("seq")
    route = [(i, i + hops) for i in range(count) if 0 <= i + hops < count]
    return lax.ppermute(value, "seq", route)


def cost(flops, read):
    return pl.CostEstimate(flops=flops // LIGHT, bytes_accessed=read // LIGHT, transcendentals=0)


class Order:
    def __init__(self):
        self.mark = None
        self.touched = []

    def arrived(self, *values):
        self.touched.extend(values)

    def __call__(self, kernel, args, in_specs, out_specs, out_shape, grid, flops, read, name, scalars=(), scratch=()):
        anchor = ([] if self.mark is None else [self.mark]) + self.touched
        self.touched = []
        count = len(scalars) + len(args)
        outs = len(out_shape)

        def run(*refs):
            rest = refs[count + len(anchor) :]
            kernel(*refs[:count], *rest[:outs], *rest[outs + 1 :])
            rest[outs][...] = jnp.zeros(rest[outs].shape, jnp.float32)

        *results, self.mark = pl.pallas_call(
            run,
            grid_spec=pltpu.PrefetchScalarGridSpec(
                num_scalar_prefetch=len(scalars),
                grid=grid,
                in_specs=list(in_specs) + anchors(len(anchor)),
                out_specs=list(out_specs) + [mark_spec()],
                scratch_shapes=list(scratch),
            ),
            out_shape=list(out_shape) + [MARK],
            compiler_params=pltpu.CompilerParams(vmem_limit_bytes=32 * MIB),
            cost_estimate=cost(flops, read),
            name=name,
        )(*scalars, *args, *anchor)
        return results


def first_kernel(core_ref, tok_ref, gain_ref, w_ref, b_ref, cos_ref, sin_ref, h_ref, q_ref, kv_ref):
    x = to_f(tok_ref[...])
    factor = lax.rsqrt(jnp.mean(x * x, axis=-1, keepdims=True) + EPS)
    h = to_bf(x * factor * gain_ref[...])
    h_ref[...] = h
    lin = dot(h, w_ref[...]) + b_ref[...]
    cosine = cos_ref[...]
    sine = sin_ref[...]
    heads = q_ref.shape[1] // HD
    for head in range(heads):
        part = lin[:, head * HD : (head + 1) * HD]
        q_ref[:, head * HD : (head + 1) * HD] = to_bf(
            part * cosine + pltpu.roll(part, HD // 2, 1) * sine
        )
    part = lin[:, heads * HD :]
    is_key = core_ref[0] == 0
    kv_ref[...] = to_bf(
        part * jnp.where(is_key, cosine, 1.0)
        + pltpu.roll(part, HD // 2, 1) * jnp.where(is_key, sine, 0.0)
    )


def first(core, tokens, gain, weight, bias, cosine, sine):
    total, width = tokens.shape
    columns = weight.shape[1]
    block = total // 4
    half = 2

    def flip(i, core_ref):
        return (lax.rem(i + core_ref[0] * half, 4), 0)

    def at(i, core_ref):
        return (i, 0)

    def whole(i, core_ref):
        return (0, 0)

    return pl.pallas_call(
        first_kernel,
        grid_spec=pltpu.PrefetchScalarGridSpec(
            num_scalar_prefetch=1,
            grid=(4,),
            in_specs=[
                pl.BlockSpec((block, width), flip),
                pl.BlockSpec((1, width), whole),
                pl.BlockSpec((width, columns), whole),
                pl.BlockSpec((1, columns), whole),
                pl.BlockSpec((block, HD), at),
                pl.BlockSpec((block, HD), at),
            ],
            out_specs=[
                pl.BlockSpec((block, width), at),
                pl.BlockSpec((block, columns - HD), at),
                pl.BlockSpec((block, HD), at),
            ],
        ),
        out_shape=[
            jax.ShapeDtypeStruct((total, width), jnp.bfloat16),
            jax.ShapeDtypeStruct((total, columns - HD), jnp.bfloat16),
            jax.ShapeDtypeStruct((total, HD), jnp.bfloat16),
        ],
        compiler_params=pltpu.CompilerParams(vmem_limit_bytes=32 * MIB),
        cost_estimate=cost(2 * total * width * columns, 9 * MIB),
        name="first",
    )(core, tokens, gain, weight, bias, cosine, sine)


def stacked(ref, start, count, heads):
    return jnp.concatenate(
        [ref[0, pl.ds(start, count), h * HD : (h + 1) * HD] for h in range(heads)], axis=0
    )


def bounds(start_ref, index, heads, reach):
    first_key = jnp.concatenate(
        [start_ref[0, :, pl.ds(index * Q_BLOCK, Q_BLOCK)]] * heads, axis=1
    )
    place = reach + index * Q_BLOCK + lax.broadcasted_iota(jnp.int32, (1, Q_BLOCK), 1)
    return first_key, jnp.concatenate([place] * heads, axis=1)


def gather_span(core, refs, span):
    count = len(refs) // 2
    local = refs[0].shape[1]
    for i in range(count):
        here = slice(i * local, (i + 1) * local)
        span[core, here] = refs[i][0]
        span[1 - core, here] = refs[count + i][0]


def attend_kernel(heads, blocks, pieces, low_ref, core_ref, q_ref, start_ref, *refs):
    o_ref, lse_ref, acc, span = refs[2 * pieces :]
    row = pl.program_id(0)
    wide = heads * Q_BLOCK
    reach = (pieces - 1) * q_ref.shape[1]
    gather_span(core_ref[0], refs[: 2 * pieces], span)
    for index in range(blocks):
        q = stacked(q_ref, index * Q_BLOCK, Q_BLOCK, heads)
        first_key, place = bounds(start_ref, index, heads, reach)
        acc[...] = jnp.zeros_like(acc)

        def step(j, carry):
            top, total = carry
            keys = pl.ds(pl.multiple_of(j * K_BLOCK, K_BLOCK), K_BLOCK)
            s = dot(span[0, keys], q, 1, 1) * SCALE
            key = j * K_BLOCK + lax.broadcasted_iota(jnp.int32, (K_BLOCK, wide), 0)
            s = jnp.where((key >= first_key) & (key <= place), s, NEG_FILL)
            later = jnp.maximum(top, jnp.max(s, axis=0, keepdims=True))
            p = jnp.exp(s - later)
            fade = jnp.exp(top - later)
            total = total * fade + jnp.sum(p, axis=0, keepdims=True)
            acc[...] = acc[...] * fade + dot(span[1, keys], to_bf(p), 0, 0)
            return later, total

        last = (reach + (index + 1) * Q_BLOCK - 1) // K_BLOCK + 1
        top, total = lax.fori_loop(
            low_ref[row, index],
            last,
            step,
            (jnp.full((1, wide), NEG_FILL, jnp.float32), jnp.zeros((1, wide), jnp.float32)),
        )
        out = to_bf((acc[...] / total).T)
        for h in range(heads):
            o_ref[0, index * Q_BLOCK : (index + 1) * Q_BLOCK, h * HD : (h + 1) * HD] = out[
                h * Q_BLOCK : (h + 1) * Q_BLOCK
            ]
        lse_ref[0, index : index + 1, :] = top + jnp.log(total)


def span_specs(rows, local, pieces):
    near = pl.BlockSpec((1, local, HD), lambda i, *refs: (i, 0, 0))
    far = pl.BlockSpec((1, local, HD), lambda i, *refs: (lax.rem(i + rows // 2, rows), 0, 0))
    return [near] * pieces + [far] * pieces


def attend(low, core, q, start, span, mate):
    rows, local, columns = q.shape
    pieces = len(span)
    heads = columns // HD
    blocks = local // Q_BLOCK

    def at(i, *refs):
        return (i, 0, 0)

    return pl.pallas_call(
        functools.partial(attend_kernel, heads, blocks, pieces),
        grid_spec=pltpu.PrefetchScalarGridSpec(
            num_scalar_prefetch=2,
            grid=(rows,),
            in_specs=[pl.BlockSpec((1, local, columns), at), pl.BlockSpec((1, 1, local), at)]
            + span_specs(rows, local, pieces),
            out_specs=[
                pl.BlockSpec((1, local, columns), at),
                pl.BlockSpec((1, blocks, heads * Q_BLOCK), at),
            ],
            scratch_shapes=[
                pltpu.VMEM((HD, heads * Q_BLOCK), jnp.float32),
                pltpu.VMEM((2, pieces * local, HD), jnp.bfloat16),
            ],
        ),
        out_shape=[
            jax.ShapeDtypeStruct((rows, local, columns), jnp.bfloat16),
            jax.ShapeDtypeStruct((rows, blocks, heads * Q_BLOCK), jnp.float32),
        ],
        compiler_params=pltpu.CompilerParams(vmem_limit_bytes=32 * MIB),
        cost_estimate=cost(8_000_000_000, 4 * MIB),
        name="attend",
    )(low, core, q, start, *span, *mate)


def attend_back_kernel(
    heads, blocks, pieces, low_ref, core_ref, q_ref, start_ref, g_ref, o_ref, lse_ref, cos_ref, sin_ref, *refs
):
    gq_ref, keep_ref, *sends, acc, gk, gv, span = refs[2 * pieces :]
    row = pl.program_id(0)
    wide = heads * Q_BLOCK
    reach = (pieces - 1) * q_ref.shape[1]
    core = core_ref[0]
    gather_span(core, refs[: 2 * pieces], span)
    gk[...] = jnp.zeros_like(gk)
    gv[...] = jnp.zeros_like(gv)
    for index in range(blocks):
        q = stacked(q_ref, index * Q_BLOCK, Q_BLOCK, heads)
        g = stacked(g_ref, index * Q_BLOCK, Q_BLOCK, heads)
        o = stacked(o_ref, index * Q_BLOCK, Q_BLOCK, heads)
        inner = jnp.sum((to_f(g) * to_f(o)).T, axis=0, keepdims=True)
        lse = lse_ref[0, index : index + 1, :]
        first_key, place = bounds(start_ref, index, heads, reach)
        acc[...] = jnp.zeros_like(acc)

        def step(j, carry):
            keys = pl.ds(pl.multiple_of(j * K_BLOCK, K_BLOCK), K_BLOCK)
            k = span[0, keys]
            s = dot(k, q, 1, 1) * SCALE
            key = j * K_BLOCK + lax.broadcasted_iota(jnp.int32, (K_BLOCK, wide), 0)
            p = jnp.where((key >= first_key) & (key <= place), jnp.exp(s - lse), 0.0)
            gp = dot(span[1, keys], g, 1, 1)
            gs = to_bf(p * (gp - inner))
            gv[keys] += dot(to_bf(p), g)
            gk[keys] += dot(gs, q)
            acc[...] += dot(k, gs, 0, 0)
            return carry

        last = (reach + (index + 1) * Q_BLOCK - 1) // K_BLOCK + 1
        lax.fori_loop(low_ref[row, index], last, step, 0)
        gq = acc[...].T * SCALE
        here = slice(index * Q_BLOCK, (index + 1) * Q_BLOCK)
        cosine, sine = cos_ref[here], sin_ref[here]
        for h in range(heads):
            part = gq[h * Q_BLOCK : (h + 1) * Q_BLOCK]
            gq_ref[0, here, h * HD : (h + 1) * HD] = to_bf(
                part * cosine + pltpu.roll(part * sine, HD // 2, 1)
            )
    is_key = core == 0
    keys, values = gk[...] * SCALE, gv[...]
    keep_ref[0] = to_bf(jnp.where(is_key, keys, values))
    sent = to_bf(jnp.where(is_key, values, keys))
    for i, ref in enumerate(sends):

        @pl.when(row == i)
        def _(ref=ref):
            ref[0] = sent


def attend_back(order, low, core, q, start, span, mate, grad, out, lse, cosine, sine):
    rows, local, columns = q.shape
    pieces = len(span)
    window = pieces * local
    heads = columns // HD
    blocks = local // Q_BLOCK

    def at(i, *refs):
        return (i, 0, 0)

    table = pl.BlockSpec((local, HD), lambda i, *refs: (i, 0))
    tokens = pl.BlockSpec((1, local, columns), at)
    return order(
        functools.partial(attend_back_kernel, heads, blocks, pieces),
        [q, start, grad, out, lse, cosine, sine, *span, *mate],
        [
            tokens,
            pl.BlockSpec((1, 1, local), at),
            tokens,
            tokens,
            pl.BlockSpec((1, blocks, heads * Q_BLOCK), at),
            table,
            table,
        ]
        + span_specs(rows, local, pieces),
        [tokens, pl.BlockSpec((1, window, HD), at)]
        + [pl.BlockSpec((1, window, HD), lambda i, *refs: (0, 0, 0))] * rows,
        [
            jax.ShapeDtypeStruct((rows, local, columns), jnp.bfloat16),
            jax.ShapeDtypeStruct((rows, window, HD), jnp.bfloat16),
        ]
        + [jax.ShapeDtypeStruct((1, window, HD), jnp.bfloat16)] * rows,
        (rows,),
        20_000_000_000,
        6 * MIB,
        "attend_back",
        scalars=(low, core),
        scratch=[
            pltpu.VMEM((HD, heads * Q_BLOCK), jnp.float32),
            pltpu.VMEM((window, HD), jnp.float32),
            pltpu.VMEM((window, HD), jnp.float32),
            pltpu.VMEM((2, window, HD), jnp.bfloat16),
        ],
    )


def fold_kernel(rows, keep_ref, *refs):
    comes, own_ref, send_refs = refs[:rows], refs[rows], refs[rows + 1 :]
    local = own_ref.shape[1]
    come = comes[0][0]
    for i in range(1, rows):
        come = jnp.where(pl.program_id(0) == i, comes[i][0], come)
    total = to_f(keep_ref[0]) + to_f(come)
    reach = total.shape[0] - local
    own_ref[0] = total[reach:]
    for hop, ref in enumerate(send_refs, 1):
        ref[0] = to_bf(total[reach - hop * local : reach - (hop - 1) * local])


def fold(order, keep, comes, local):
    rows, window = keep.shape[:2]
    hops = window // local - 1
    out = pl.BlockSpec((1, local, HD), lambda i: (i, 0, 0))
    return order(
        functools.partial(fold_kernel, rows),
        [keep, *comes],
        [pl.BlockSpec((1, window, HD), lambda i: (i, 0, 0))]
        + [pl.BlockSpec((1, window, HD), lambda i: (0, 0, 0))] * rows,
        [out] * (hops + 1),
        [jax.ShapeDtypeStruct((rows, local, HD), jnp.float32)]
        + [jax.ShapeDtypeStruct((rows, local, HD), jnp.bfloat16)] * hops,
        (rows,),
        0,
        4 * MIB,
        "fold",
    )


def carry_kernel(piece_ref, come_ref, out_ref):
    out_ref[...] = to_bf(to_f(piece_ref[...]) + to_f(come_ref[...]))


def carry(order, piece, come):
    rows, local, columns = piece.shape
    at = pl.BlockSpec((1, local, columns), lambda i: (i, 0, 0))
    return order(
        carry_kernel,
        [piece, come],
        [at, at],
        [at],
        [jax.ShapeDtypeStruct(piece.shape, jnp.bfloat16)],
        (rows,),
        0,
        2 * MIB,
        "carry",
    )[0]


def bias_kernel(left_ref, right_ref, out_ref):
    out_ref[...] = left_ref[...] + right_ref[...]


def bias_add(order, left, right):
    whole = pl.BlockSpec(left.shape, lambda i: (0, 0))
    return order(
        bias_kernel,
        [left, right],
        [whole, whole],
        [whole],
        [jax.ShapeDtypeStruct(left.shape, jnp.float32)],
        (1,),
        0,
        MIB,
        "bias",
    )[0]


def join_kernel(hops, core_ref, gq_ref, cos_ref, sin_ref, own_ref, *refs):
    out_ref, sum_ref = refs[-2:]
    columns = gq_ref.shape[2]
    grad = own_ref[0]
    for ref in refs[:hops]:
        grad = grad + to_f(ref[0])
    is_key = core_ref[0] == 0
    cosine = jnp.where(is_key, cos_ref[...], 1.0)
    sine = jnp.where(is_key, sin_ref[...], 0.0)
    kv = to_bf(grad * cosine + pltpu.roll(grad * sine, HD // 2, 1))
    q = gq_ref[0]
    out_ref[:, :columns] = q
    out_ref[:, columns:] = kv

    @pl.when(pl.program_id(0) == 0)
    def _():
        sum_ref[...] = jnp.zeros(sum_ref.shape, jnp.float32)

    sum_ref[:, :columns] += jnp.sum(to_f(q), axis=0, keepdims=True)
    sum_ref[:, columns:] += jnp.sum(to_f(kv), axis=0, keepdims=True)


def join(order, core, grad_q, own, comes, cosine, sine):
    rows, local, columns = grad_q.shape
    wide = columns + HD

    def at(i, *refs):
        return (i, 0, 0)

    piece = pl.BlockSpec((1, local, HD), at)
    table = pl.BlockSpec((local, HD), lambda i, *refs: (i, 0))
    return order(
        functools.partial(join_kernel, len(comes)),
        [grad_q, cosine, sine, own, *comes],
        [pl.BlockSpec((1, local, columns), at), table, table, piece] + [piece] * len(comes),
        [
            pl.BlockSpec((local, wide), lambda i, *refs: (i, 0)),
            pl.BlockSpec((8, wide), lambda i, *refs: (0, 0)),
        ],
        [
            jax.ShapeDtypeStruct((rows * local, wide), jnp.bfloat16),
            jax.ShapeDtypeStruct((8, wide), jnp.float32),
        ],
        (rows,),
        0,
        4 * MIB,
        "join",
        scalars=(core,),
    )


def mixed_back_kernel(w_ref, *refs):
    rows = refs[0].shape[0]
    for i, ref in enumerate(refs[:-1]):
        refs[-1][i * rows : (i + 1) * rows] = to_bf(dot(ref[...], w_ref[...]))


def mixed_back(order, pieces, weight):
    rows, width = pieces[0].shape
    total = rows * len(pieces)
    columns = weight.shape[1]

    def whole(i):
        return (0, 0)

    return order(
        mixed_back_kernel,
        [weight, *pieces],
        [pl.BlockSpec((width, columns), whole)] + [pl.BlockSpec((rows, width), whole)] * len(pieces),
        [pl.BlockSpec((total, columns), whole)],
        [jax.ShapeDtypeStruct((total, columns), jnp.bfloat16)],
        (1,),
        2 * total * width * columns,
        6 * MIB,
        "mixed_back",
    )[0]


def place_kernel(core_ref, *refs):
    for i, ref in enumerate(refs[:-1]):

        @pl.when(pl.program_id(0) == i)
        def _(ref=ref):
            refs[-1][...] = ref[...]


def place(order, core, pieces):
    rows, width = pieces[0].shape
    count = len(pieces)
    return order(
        place_kernel,
        list(pieces),
        [pl.BlockSpec((rows, width), lambda i, core_ref: (0, 0))] * count,
        [pl.BlockSpec((rows, width), lambda i, core_ref: (lax.rem(i + core_ref[0] * (count // 2), count), 0))],
        [jax.ShapeDtypeStruct((rows * count, width), pieces[0].dtype)],
        (count,),
        0,
        8 * rows * width,
        "place",
        scalars=(core,),
    )[0]


def anchors(count):
    return [pl.BlockSpec(memory_space=pl.ANY)] * count


MARK = jax.ShapeDtypeStruct((8, HD), jnp.float32)


def mark_spec():
    return pl.BlockSpec((8, HD), lambda *refs: (0, 0))


def grad_hidden_kernel(g_ref, w_ref, out_ref):
    out_ref[...] = to_bf(dot(g_ref[...], w_ref[...], 1, 1))


def grad_hidden_of(order, grad, weight):
    total, width = grad.shape
    hidden = weight.shape[0]
    return order(
        grad_hidden_kernel,
        [grad, weight],
        [pl.BlockSpec((total, width), lambda i: (0, 0)), pl.BlockSpec((TILE, width), lambda i: (i, 0))],
        [pl.BlockSpec((total, TILE), lambda i: (0, i))],
        [jax.ShapeDtypeStruct((total, hidden), jnp.bfloat16)],
        (pl.cdiv(hidden, TILE),),
        2 * total * width * hidden,
        15 * MIB,
        "grad_hidden",
    )[0]


def gated_kernel(gh_ref, gw_ref, uw_ref, *refs):
    hid_ref, gg_ref, gu_ref = refs[-3:]
    rows = refs[0].shape[0]
    for part, ref in enumerate(refs[:-3]):
        here = slice(part * rows, (part + 1) * rows)
        h = ref[...]
        gate = dot(h, gw_ref[...], 1, 1)
        up = dot(h, uw_ref[...], 1, 1)
        grad = to_f(gh_ref[here])
        sigma = 1.0 / (1.0 + jnp.exp(-gate))
        swish = gate * sigma
        hid_ref[here] = to_bf(swish * up)
        gu_ref[here] = to_bf(grad * swish)
        gg_ref[here] = to_bf(grad * up * sigma * (1.0 + gate * (1.0 - sigma)))


def gated(order, pieces, grad_hidden, gate_weight, up_weight):
    rows, width = pieces[0].shape
    total = rows * len(pieces)
    hidden = gate_weight.shape[0]
    column = pl.BlockSpec((total, TILE), lambda i: (0, i))
    weight = pl.BlockSpec((TILE, width), lambda i: (i, 0))
    shape = jax.ShapeDtypeStruct((total, hidden), jnp.bfloat16)
    return order(
        gated_kernel,
        [grad_hidden, gate_weight, up_weight, *pieces],
        [column, weight, weight] + [pl.BlockSpec((rows, width), lambda i: (0, 0))] * len(pieces),
        [column] * 3,
        [shape] * 3,
        (pl.cdiv(hidden, TILE),),
        4 * total * width * hidden,
        30 * MIB,
        "gated",
    )


def share_kernel(plan, lefts, rights, extra, halves, pick_ref, blocks_ref, *refs):
    step = pl.program_id(0)
    left_refs, right_refs = refs[:lefts], refs[lefts : lefts + rights]
    refs = refs[lefts + rights :]
    if extra:
        extra_ref, refs = refs[0], refs[1:]
    for left, right, begin, end, shift, columns, target in plan:

        @pl.when((step >= begin) & (step < end))
        def _(left=left, right=right, shift=shift, columns=columns, target=target):
            out = dot(left_refs[left][...], right_refs[right][...])
            if extra:
                out = out + to_f(extra_ref[...])
            tile = out.shape[1]
            spot = (step + shift) * tile + lax.broadcasted_iota(jnp.int32, (1, tile), 1)
            out = to_bf(jnp.where(spot < columns, out, 0.0))
            if not halves:
                refs[target][...] = out
                return
            send_ref, keep_ref, rows = refs
            rows[...] = out
            share = send_ref.shape[0] // (2 * halves)
            for i in range(2 * halves):
                here = slice(i * share, (i + 1) * share)
                send_ref[here] = rows[pl.ds(pl.multiple_of(blocks_ref[i] * share, share), share)]
                keep_ref[here] = rows[pl.ds(pl.multiple_of(blocks_ref[2 * halves + i] * share, share), share)]


def clipped(rows, tile, begin, count, shift=0):
    return pl.BlockSpec((rows, tile), lambda i, *refs: (0, jnp.clip(i - begin, 0, count - 1) + shift))


def share_of(order, lefts, rights, parts, part, pick, tile, extra=None, blocks=None):
    tokens = lefts[0].shape[1]
    plan, at = [], 0
    starts, sizes, right_at = {}, {}, {}
    for left, right, skip, count, target in parts:
        plan.append((left, right, at, at + count, skip - at, rights[right].shape[1], target))
        starts.setdefault(target, at)
        sizes[target] = sizes.get(target, 0) + count
        first, tiles, low = right_at.get(right, (at, 0, skip))
        right_at[right] = (first, tiles + count, low)
        at += count
    halves = 0
    extras = [] if extra is None else [extra]
    scratch = []
    if blocks is None:
        blocks = jnp.zeros((1,), jnp.int32)
        outs = [clipped(part, tile, starts[t], sizes[t]) for t in sorted(sizes)]
        shapes = [jax.ShapeDtypeStruct((part, sizes[t] * tile), jnp.bfloat16) for t in sorted(sizes)]
    else:
        halves = blocks.shape[0] // 4
        outs = [clipped(part // 2, tile, 0, at)] * 2
        shapes = [jax.ShapeDtypeStruct((part // 2, at * tile), jnp.bfloat16)] * 2
        scratch = [pltpu.VMEM((part, tile), jnp.bfloat16)]
    return order(
        functools.partial(share_kernel, plan, len(lefts), len(rights), len(extras), halves),
        [*lefts, *rights, *extras],
        [pl.BlockSpec((part, tokens), lambda i, pick_ref, blocks_ref: (pick_ref[0], 0))] * len(lefts)
        + [clipped(tokens, tile, *right_at[r]) for r in range(len(rights))]
        + [clipped(part, tile, 0, at)] * len(extras),
        outs,
        shapes,
        (at,),
        2 * part * tokens * at * tile,
        2 * (part * tokens + (part + tokens) * at * tile),
        "share",
        scalars=(jnp.asarray(pick, jnp.int32).reshape(1), blocks),
        scratch=scratch,
    )


def relay_kernel(keep_ref, come_ref, out_ref):
    out_ref[...] = to_bf(to_f(keep_ref[...]) + to_f(come_ref[...]))


def relay(order, keep, come, share):
    rows, columns = keep.shape
    pair = pl.BlockSpec((share, columns), lambda i: (2 * i + 1, 0))
    return order(
        relay_kernel,
        [keep, come],
        [pair, pair],
        [pl.BlockSpec((share, columns), lambda i: (i, 0))],
        [jax.ShapeDtypeStruct((rows // 2, columns), jnp.bfloat16)],
        (rows // (2 * share),),
        0,
        3 * rows * columns,
        "relay",
    )[0]


def settle_kernel(pick_ref, keep_ref, come_ref, last_ref, sent_ref, mine_ref):
    out = to_bf(to_f(keep_ref[...]) + to_f(come_ref[...]) + to_f(last_ref[...]))

    @pl.when(pl.program_id(0) == 0)
    def _():
        sent_ref[...] = out

    @pl.when(pl.program_id(0) == 1)
    def _():
        mine_ref[...] = out


def settle(order, keep, come, last, picks):
    share = last.shape[0] // 2
    columns = keep.shape[1]
    pair = pl.BlockSpec((share, columns), lambda i, pick_ref: (2 * pick_ref[i], 0))
    whole = pl.BlockSpec((share, columns), lambda i, pick_ref: (0, 0))
    return order(
        settle_kernel,
        [keep, come, last],
        [pair, pair, pl.BlockSpec((share, columns), lambda i, pick_ref: (pick_ref[i], 0))],
        [whole] * 2,
        [jax.ShapeDtypeStruct((share, columns), jnp.bfloat16)] * 2,
        (2,),
        0,
        16 * share * columns,
        "settle",
        scalars=(picks,),
    )


def finish_kernel(plan, columns, gains, *refs):
    out_ref = refs[-2] if gains else refs[-1]
    step = pl.program_id(0)
    tile = out_ref.shape[1]
    for begin, end, first, count in plan:

        @pl.when((step >= begin) & (step < end))
        def _(first=first, count=count):
            out = to_f(refs[first][...])
            for ref in refs[first + 1 : first + count]:
                out = out + to_f(ref[...])
            out_ref[...] = out
            if gains:
                spot = step * tile + lax.broadcasted_iota(jnp.int32, (1, tile), 1)
                terms = jnp.where(spot < columns, out * to_f(refs[-3][...]), 0.0)
                total = terms[:, :HD]
                for i in range(HD, tile, HD):
                    total = total + terms[:, i : i + HD]

                @pl.when(step == 0)
                def _():
                    refs[-1][...] = total

                @pl.when(step > 0)
                def _():
                    refs[-1][...] += total


def finish(order, chunks, share, columns, tile, weight=None):
    plan, specs, args, at = [], [], [], 0
    for chunk in chunks:
        count = chunk[0].shape[1] // tile
        plan.append((at, at + count, len(args), len(chunk)))
        specs += [clipped(share, tile, at, count)] * len(chunk)
        args += chunk
        at += count
    column = pl.BlockSpec((share, tile), lambda i: (0, i))
    outs, shapes = [column], [jax.ShapeDtypeStruct((share, columns), jnp.float32)]
    if weight is not None:
        args.append(weight)
        specs.append(column)
        outs.append(pl.BlockSpec((share, HD), lambda i: (0, 0)))
        shapes.append(jax.ShapeDtypeStruct((share, HD), jnp.float32))
    return order(
        functools.partial(finish_kernel, plan, columns, weight is not None),
        args,
        specs,
        outs,
        shapes,
        (at,),
        0,
        14 * share * columns,
        "finish",
    )


def narrow_kernel(pairs, extras, right_dim, *refs):
    out = dot(refs[0][...], refs[1][...], 1, right_dim)
    for i in range(1, pairs):
        out = out + dot(refs[2 * i][...], refs[2 * i + 1][...], 1, right_dim)
    extra = refs[2 * pairs : 2 * pairs + extras]
    outs = refs[2 * pairs + extras :]
    if extras:
        out = out + jnp.concatenate([to_f(ref[...]) for ref in extra], axis=0)
    rows = outs[0].shape[0]
    for i, ref in enumerate(outs):
        ref[...] = to_bf(out[i * rows : (i + 1) * rows])


def narrow(order, pairs, index, extra=(), right_dim=0):
    total, hidden = pairs[0][0].shape
    width = pairs[0][1].shape[1 - right_dim]
    half = total // 2
    piece = half // PIECES
    column = pl.BlockSpec((piece, TILE), lambda i: (0, i))
    right = (
        pl.BlockSpec((TILE, hidden), lambda i: (i, 0))
        if right_dim
        else pl.BlockSpec((hidden, TILE), lambda i: (0, i))
    )
    return order(
        functools.partial(narrow_kernel, len(pairs), len(extra), right_dim),
        [item for pair in pairs for item in pair] + list(extra),
        [pl.BlockSpec((half, hidden), lambda i: (index, 0)), right] * len(pairs) + [column] * len(extra),
        [column] * PIECES,
        [jax.ShapeDtypeStruct((piece, width), jnp.bfloat16)] * PIECES,
        (width // TILE,),
        2 * len(pairs) * half * width * hidden,
        2 * len(pairs) * (half + width) * hidden + 2 * half * width,
        "narrow",
    )


def piece_specs(piece, width, block):
    steps = piece // block
    return [
        pl.BlockSpec((block, width), lambda i, *refs, j=j: (jnp.clip(i - j * steps, 0, steps - 1), 0))
        for j in range(PIECES)
    ]


def pick_piece(refs):
    value = refs[0][...]
    for j, ref in enumerate(refs[1:], 1):
        value = jnp.where(pl.program_id(0) >= 4 * j // len(refs), ref[...], value)
    return value


def put_piece(refs, value):
    steps = 4 // len(refs)
    for j, ref in enumerate(refs):

        @pl.when(lax.div(pl.program_id(0), steps) == j)
        def _(ref=ref):
            ref[...] = value


def turn_kernel(*refs):
    rows = refs[0].shape[0]
    for i, ref in enumerate(refs[:-1]):
        refs[-1][:, i * rows : (i + 1) * rows] = ref[...].T


def turn(order, pieces):
    rows, width = pieces[0].shape
    total = rows * len(pieces)
    return order(
        turn_kernel,
        list(pieces),
        [pl.BlockSpec((rows, TILE), lambda i: (0, i))] * len(pieces),
        [pl.BlockSpec((TILE, total), lambda i: (i, 0))],
        [jax.ShapeDtypeStruct((width, total), jnp.bfloat16)],
        (width // TILE,),
        0,
        4 * total * width,
        "turn",
    )[0]


def grad_out_kernel(core_ref, cot_ref, valid_ref, out_ref, turned_ref):
    out = to_bf(to_f(cot_ref[...]) * valid_ref[...])
    out_ref[...] = out
    turned_ref[...] = out.T


def grad_out_of(order, core, cotangent, valid):
    total, width = cotangent.shape
    block = total // 4
    return order(
        grad_out_kernel,
        [cotangent, valid],
        [
            pl.BlockSpec((block, width), lambda i, core_ref: (lax.rem(i + core_ref[0] * 2, 4), 0)),
            pl.BlockSpec((block, 1), lambda i, core_ref: (i, 0)),
        ],
        [
            pl.BlockSpec((block, width), lambda i, core_ref: (i, 0)),
            pl.BlockSpec((width, block), lambda i, core_ref: (0, i)),
        ],
        [
            jax.ShapeDtypeStruct((total, width), jnp.bfloat16),
            jax.ShapeDtypeStruct((width, total), jnp.bfloat16),
        ],
        (4,),
        0,
        6 * total * width,
        "grad_out",
        scalars=(core,),
    )


def middle_kernel(core_ref, tok_ref, gain_ref, *refs):
    mine, come = pick_piece(refs[:PIECES]), pick_piece(refs[PIECES : 2 * PIECES])
    mid_ref, *h_refs = refs[2 * PIECES :]
    middle = to_f(tok_ref[...]) + (to_f(mine) + to_f(come))
    factor = lax.rsqrt(jnp.mean(middle * middle, axis=-1, keepdims=True) + EPS)
    mid_ref[...] = middle
    put_piece(h_refs, to_bf(middle * factor * gain_ref[...]))


def middle_of(order, core, tokens, mine, come, gain):
    piece, width = mine[0].shape
    half = piece * PIECES
    block = half // 4
    specs = piece_specs(piece, width, block)
    middle, *h = order(
        middle_kernel,
        [tokens, gain, *mine, *come],
        [
            pl.BlockSpec((block, width), lambda i, core_ref: (core_ref[0] * 4 + i, 0)),
            pl.BlockSpec((1, width), lambda i, core_ref: (0, 0)),
        ]
        + specs * 2,
        [pl.BlockSpec((block, width), lambda i, core_ref: (i, 0))] + specs,
        [jax.ShapeDtypeStruct((half, width), jnp.float32)]
        + [jax.ShapeDtypeStruct((piece, width), jnp.bfloat16)] * PIECES,
        (4,),
        0,
        9 * MIB,
        "middle",
        scalars=(core,),
    )
    return middle, h


def norm_back_kernel(core_ref, x_ref, gain_ref, up_ref, *refs):
    mine, come = pick_piece(refs[:PIECES]), pick_piece(refs[PIECES : 2 * PIECES])
    outs = refs[2 * PIECES :]
    grad = to_f(mine) + to_f(come)
    x = to_f(x_ref[...])
    factor = lax.rsqrt(jnp.mean(x * x, axis=-1, keepdims=True) + EPS)
    normed = x * factor
    weighted = grad * gain_ref[...]
    inner = jnp.mean(weighted * normed, axis=-1, keepdims=True)
    out = to_f(up_ref[...]) + factor * (weighted - normed * inner)
    if len(outs) > PIECES:
        outs[0][...] = out
        put_piece(outs[1:], to_bf(out))
    else:
        put_piece(outs, out)


def norm_back(order, core, mine, come, x, gain, up, by_core):
    piece, width = mine[0].shape
    half = piece * PIECES
    block = half // 4
    at = pl.BlockSpec((block, width), lambda i, core_ref: (i, 0))
    picked = pl.BlockSpec((block, width), lambda i, core_ref: (core_ref[0] * 4 + i, 0))
    specs = piece_specs(piece, width, block)
    if by_core:
        shapes = [jax.ShapeDtypeStruct((piece, width), jnp.float32)] * PIECES
    else:
        shapes = [jax.ShapeDtypeStruct((half, width), jnp.float32)]
        shapes += [jax.ShapeDtypeStruct((piece, width), jnp.bfloat16)] * PIECES
    return order(
        norm_back_kernel,
        [x, gain, up, *mine, *come],
        [picked if by_core else at, pl.BlockSpec((1, width), lambda i, core_ref: (0, 0)), at] + specs * 2,
        specs if by_core else [at] + specs,
        shapes,
        (4,),
        0,
        10 * MIB,
        "norm_back",
        scalars=(core,),
    )


def layer_kernel(middle_ref, *refs):
    mine, come = pick_piece(refs[:PIECES]), pick_piece(refs[PIECES : 2 * PIECES])
    put_piece(refs[2 * PIECES :], to_bf(middle_ref[...] + (to_f(mine) + to_f(come))))


def layer_of(order, middle, mine, come):
    piece, width = mine[0].shape
    block = piece * PIECES // 4
    specs = piece_specs(piece, width, block)
    return order(
        layer_kernel,
        [middle, *mine, *come],
        [pl.BlockSpec((block, width), lambda i: (i, 0))] + specs * 2,
        specs,
        [jax.ShapeDtypeStruct((piece, width), jnp.bfloat16)] * PIECES,
        (4,),
        0,
        5 * MIB,
        "layer",
    )


def tensor_gather(value, rank):
    mate = core_swap(value)
    pair = jnp.where(lax.rem(rank, 2) == 0, jnp.stack([value, mate]), jnp.stack([mate, value]))
    come = chip_swap(pair)
    return jnp.where(
        lax.div(rank, 2) == 0,
        jnp.concatenate([pair, come], axis=0),
        jnp.concatenate([come, pair], axis=0),
    )


def body(
    tokens,
    lengths,
    cotangent,
    q_weight,
    q_bias,
    k_weight,
    k_bias,
    v_weight,
    v_bias,
    o_weight,
    attn_gain,
    ffn_gain,
    gate_weight,
    up_weight,
    down_weight,
):
    rows, local, width = tokens.shape
    total = rows * local
    half = total // 2
    heads = q_weight.shape[1] // HD
    ranks = lax.axis_size("tensor")
    seqs = lax.axis_size("seq")
    rank = lax.axis_index("tensor")
    dp_index = lax.axis_index("dp")
    seq_index = lax.axis_index("seq")
    core = lax.rem(rank, 2)
    head = lax.div(rank, 2)
    core_one = core.reshape(1)
    hops = min(seqs - 1, -(-(MOST - 1) // local))
    reach = hops * local

    def own_first(value):
        turned = jnp.concatenate([value[rows // 2 :], value[: rows // 2]], axis=0)
        return jnp.where(core == 0, value, turned)

    slots = jnp.arange(lengths.shape[1], dtype=jnp.int32)
    lens = own_first(lengths)
    ends = jnp.sum(jnp.where(slots[None, :] <= slots[:, None], lens[:, None, :], 0), axis=2)
    spot = seq_index * local + jnp.arange(local, dtype=jnp.int32)
    begun = jnp.max(
        jnp.where(ends[:, None, :] <= spot[None, :, None], ends[:, None, :], 0), axis=2
    )
    valid = to_f(spot[None, :] < ends[:, -2:-1])
    position = (spot[None, :] - begun).reshape(total, 1)
    freqs = ROPE_BASE ** (-(jnp.arange(HD // 2, dtype=jnp.float32) * 2.0) / HD)
    angles = to_f(position) * freqs[None, :]
    cosine, sine = jnp.cos(angles), jnp.sin(angles)
    cosine = jnp.concatenate([cosine, cosine], axis=1)
    sine = jnp.concatenate([-sine, sine], axis=1)
    start = begun - (seq_index * local - reach)
    low = jnp.maximum(lax.div(jnp.maximum(start[:, ::Q_BLOCK], 0), K_BLOCK), 0)
    start = start.reshape(rows, 1, local)

    key_side = core == 0
    kv_weight = jnp.where(
        key_side,
        lax.dynamic_slice_in_dim(k_weight, head * HD, HD, 1),
        lax.dynamic_slice_in_dim(v_weight, head * HD, HD, 1),
    )
    kv_bias = jnp.where(
        key_side,
        lax.dynamic_slice_in_dim(k_bias, head * HD, HD, 0),
        lax.dynamic_slice_in_dim(v_bias, head * HD, HD, 0),
    )
    weight = jnp.concatenate([q_weight, kv_weight], axis=1)
    bias = to_f(jnp.concatenate([q_bias, kv_bias])).reshape(1, -1)
    gain_one = to_f(attn_gain).reshape(1, width)
    gain_two = to_f(ffn_gain).reshape(1, width)

    h_one, q_rot, kv = first(
        core_one, tokens.reshape(total, width), gain_one, weight, bias, cosine, sine
    )
    kv = kv.reshape(rows, local, HD)
    span = [shifted(kv, h) for h in range(hops, 0, -1)] + [kv]
    mate = [core_swap(piece) for piece in span]
    q_rows = q_rot.reshape(rows, local, heads * HD)
    mixed_rows, lse = attend(low, core_one, q_rows, start, span, mate)
    mixed = mixed_rows.reshape(total, heads * HD)

    order = Order()
    flat_tokens = tokens.reshape(total, width)
    dps = lax.axis_size("dp")
    near_pair = dps == 2 and seqs == 4
    part = width // dps
    share = part // seqs
    gate_t, up_t, down_t = gate_weight.T, up_weight.T, down_weight.T
    units = gate_t.shape[0]
    tiles = -(-units // TILE)
    cut = (tiles + 1) // 2
    long = -(-2 * tiles // 3)
    one, two = seq_index ^ 1, seq_index ^ 2
    three = seq_index ^ 3
    quad = jnp.stack([one, three, seq_index, two])
    wide = jnp.stack([one, three, one + seqs, three + seqs, seq_index, two, seq_index + seqs, two + seqs])

    begin = (dp_index * seqs + seq_index) * share

    def rows_of(value):
        return lax.dynamic_slice_in_dim(value, begin, share, 0)

    class Rows:
        def __init__(self, lefts, rights, parts, tile=TILE, sent=None):
            self.args = (order, lefts, rights, parts)
            self.tile = tile
            if not near_pair:
                (whole,) = share_of(*self.args, width, 0, tile)
                self.whole = lax.psum_scatter(whole, ("dp", "seq"), scatter_dimension=0, tiled=True)
                return
            if sent is None:
                (sent,) = share_of(*self.args, part, 1 - dp_index, tile)
            self.come = lax.ppermute(sent, "dp", flipped("dp", 0))

        def own(self):
            if near_pair:
                send, self.keep = share_of(*self.args, part, dp_index, self.tile, self.come, quad)
                self.come = lax.ppermute(send, "seq", flipped("seq", 0))

        def relay(self):
            if near_pair:
                sent = relay(order, self.keep, self.come, share)
                self.last = lax.ppermute(sent, "seq", flipped("seq", 1))

        def settled(self):
            if near_pair:
                order.arrived(self.last)

        def result(self):
            return [self.keep, self.come, self.last] if near_pair else [self.whole]

    class SeqFirst(Rows):
        def __init__(self, lefts, rights, parts, tile=TILE):
            if not near_pair:
                super().__init__(lefts, rights, parts, tile)
                return
            send, self.keep = share_of(order, lefts, rights, parts, width, 0, tile, None, wide)
            self.come = lax.ppermute(send, "seq", flipped("seq", 0))

        def settle(self):
            if near_pair:
                sent, self.mine = settle(
                    order, self.keep, self.come, self.last, jnp.stack([1 - dp_index, dp_index])
                )
                self.final = lax.ppermute(sent, "dp", flipped("dp", 0))

        def result(self):
            return [self.mine, self.final] if near_pair else [self.whole]

    sent = core_swaps(narrow(order, [(mixed, o_weight)], 1, (), 1))
    mine = narrow(order, [(mixed, o_weight)], 0, sent, 1)
    come = chip_swaps(mine)
    grad_ffn, grad_ffn_t = grad_out_of(
        order, core_one, cotangent.reshape(total, width), valid.reshape(total, 1)
    )
    gate_rows, up_rows = rows_of(gate_weight), rows_of(up_weight)
    order.arrived(gate_rows, up_rows)
    grad_hidden = grad_hidden_of(order, grad_ffn, down_t)
    h_one_t = turn(order, [h_one])
    middle, h_two = middle_of(order, core_one, flat_tokens, mine, come, gain_two)
    h_two += core_swaps(h_two)
    hidden, grad_gate, grad_up = gated(order, h_two, grad_hidden, gate_t, up_t)

    down_a = Rows([grad_ffn_t], [hidden], [(0, 0, 0, long, 0)])
    down_b = SeqFirst([grad_ffn_t], [hidden], [(0, 0, long, tiles - long, 0)])
    pairs = [(grad_gate, gate_t), (grad_up, up_t)]
    sent = core_swaps(narrow(order, pairs, 1))
    mine = narrow(order, pairs, 0, sent)
    come = chip_swaps(mine)
    h_two_t = turn(order, h_two)
    up_cut = long
    if near_pair:
        sends = share_of(
            order,
            [h_two_t],
            [grad_gate, grad_up],
            [
                (0, 0, 0, tiles, 0),
                (0, 1, 0, up_cut, 1),
                (0, 1, up_cut, tiles - up_cut, 2),
            ],
            part,
            1 - dp_index,
            TILE,
        )
    else:
        sends = [None] * 3

    def half_rows(right, begin, end, sent):
        return Rows([h_two_t], [right], [(0, 0, begin, end - begin, 0)], TILE, sent)

    gate = half_rows(grad_gate, 0, tiles, sends[0])
    down_b.relay()
    down_a.own()
    up_a = half_rows(grad_up, 0, up_cut, sends[1])
    up_b = half_rows(grad_up, up_cut, tiles, sends[2])
    grad_middle, *branch = norm_back(order, core_one, mine, come, middle, gain_two, grad_ffn, False)
    branch += core_swaps(branch)
    grad_mixed = mixed_back(order, branch, o_weight).reshape(rows, local, heads * HD)
    grad_q_rows, keep, *sends = attend_back(
        order, low, core_one, q_rows, start, span, mate, grad_mixed, mixed_rows, lse, cosine, sine
    )
    comes = core_swaps([sends[(i + rows // 2) % rows] for i in range(rows)])
    branch_t = turn(order, branch)
    own_kv, *pieces = fold(order, keep, comes, local)
    moving = shifted(pieces[-1], -1) if pieces else None
    down_b.settled()
    for piece in pieces[-2::-1]:
        moving = shifted(carry(order, piece, moving), -1)
    grad_qkv, bias_sum = join(
        order, core_one, grad_q_rows, own_kv, [] if moving is None else [moving], cosine, sine
    )
    sent = core_swaps(narrow(order, [(grad_qkv, weight)], 1, (), 1))
    down_a.relay()
    mine = narrow(order, [(grad_qkv, weight)], 0, sent, 1)
    come = chip_swaps(mine)
    last_parts = [(0, 0, 0, grad_qkv.shape[1] // HD, 0), (1, 1, 0, heads, 0)]
    last = Rows([h_one_t, branch_t], [grad_qkv, mixed], last_parts, HD)
    gate.own()
    token = norm_back(order, core_one, mine, come, flat_tokens, gain_one, grad_middle, True)
    token += core_swaps(token)
    token_grad = place(order, core_one, token).reshape(rows, local, width)
    gate.relay()
    up_a.own()
    ffn_sent = core_swaps(narrow(order, [(hidden, down_t)], 1))
    if near_pair:
        down_b.settle()
    ffn_mine = narrow(order, [(hidden, down_t)], 0, ffn_sent)
    ffn_come = chip_swaps(ffn_mine)
    up_b.own()
    (down_grad,) = finish(order, [down_a.result(), down_b.result()], share, units, TILE)
    up_a.relay()
    last.own()
    gate_grad, gate_term = finish(order, [gate.result()], share, units, TILE, gate_rows)
    up_b.relay()
    layer = layer_of(order, middle, ffn_mine, ffn_come)
    layer += core_swaps(layer)
    if near_pair:
        bias_come = lax.ppermute(bias_sum, "dp", flipped("dp", 0))
        bias_all = bias_add(order, bias_sum, bias_come)
        bias_come = lax.ppermute(bias_all, "seq", flipped("seq", 0))
    last.relay()
    layer_out = place(order, core_one, layer).reshape(rows, local, width)
    if near_pair:
        bias_all = bias_add(order, bias_all, bias_come)
        bias_come = lax.ppermute(bias_all, "seq", flipped("seq", 1))
        bias_all = (bias_all + bias_come)[:1]
    else:
        bias_all = lax.psum(bias_sum[:1], ("dp", "seq"))
    up_grad, up_term = finish(order, [up_a.result(), up_b.result()], share, units, TILE, up_rows)
    wide_columns = grad_qkv.shape[1]
    (last_grad,) = finish(order, [last.result()], share, wide_columns + heads * HD, HD)
    qkv_grad, o_grad = last_grad[:, :wide_columns], last_grad[:, wide_columns:]

    attn_term = jnp.sum(to_f(rows_of(weight)) * qkv_grad, axis=1)
    ffn_term = jnp.sum(gate_term + up_term, axis=1)
    columns = heads * HD
    room = -(-share // HD) * HD - share
    terms = jnp.pad(jnp.stack([ffn_term, attn_term]), ((0, 0), (0, room))).reshape(-1, HD)
    packed = jnp.concatenate([qkv_grad[:, columns:], bias_all.reshape(-1, HD), terms], axis=0)
    gathered = tensor_gather(packed, rank)
    term_rows = terms.shape[0]
    bias_count = bias_all.shape[1] // HD
    terms = gathered[:, share + bias_count :].reshape(ranks, 2, -1)[:, :, :share]
    ffn_gain_grad, attn_gain_grad = terms[0] + terms[1] + (terms[2] + terms[3])
    attn_gain_grad = attn_gain_grad / lax.dynamic_slice_in_dim(gain_one[0], begin, share, 0)
    ffn_gain_grad = ffn_gain_grad / lax.dynamic_slice_in_dim(gain_two[0], begin, share, 0)
    q_grad = qkv_grad[:, :columns]
    kv_parts = lax.dynamic_slice_in_dim(gathered, rank * (share // ranks), share // ranks, 1)
    k_grad = jnp.concatenate([kv_parts[2 * i] for i in range(KVH)], axis=1)
    v_grad = jnp.concatenate([kv_parts[2 * i + 1] for i in range(KVH)], axis=1)
    biases = gathered[:, share : share + bias_count]
    q_bias_grad = biases[:, :heads].reshape(-1)
    k_bias_grad = biases[0::2, heads].reshape(-1)
    v_bias_grad = biases[1::2, heads].reshape(-1)
    return (
        layer_out,
        token_grad,
        q_grad,
        q_bias_grad,
        k_grad,
        k_bias_grad,
        v_grad,
        v_bias_grad,
        o_grad,
        attn_gain_grad,
        ffn_gain_grad,
        gate_grad,
        up_grad,
        down_grad,
    )


def solution(mesh):
    in_specs = (
        P("dp", "seq", None),
        P("dp", None),
        P("dp", "seq", None),
        P(None, "tensor"),
        P("tensor"),
        P(),
        P(),
        P(),
        P(),
        P(None, "tensor"),
        P(),
        P(),
        P(None, "tensor"),
        P(None, "tensor"),
        P(None, "tensor"),
    )
    out_specs = (
        P("dp", "seq", None),
        P("dp", "seq", None),
        P(("dp", "seq"), "tensor"),
        P(),
        P(("dp", "seq", "tensor"), None),
        P(),
        P(("dp", "seq", "tensor"), None),
        P(),
        P(("dp", "seq"), "tensor"),
        P(("dp", "seq")),
        P(("dp", "seq")),
        P(("dp", "seq"), "tensor"),
        P(("dp", "seq"), "tensor"),
        P(("dp", "seq"), "tensor"),
    )
    return jax.shard_map(body, mesh=mesh, in_specs=in_specs, out_specs=out_specs, check_vma=False)
```

```python
import functools
import math

import jax
import jax.numpy as jnp
from jax import lax
from jax.experimental import pallas as pl
from jax.experimental.pallas import tpu as pltpu
from jax.sharding import PartitionSpec as P

KVH = 2
HD = 128
MOST = 1024
EPS = 1e-06
ROPE_BASE = 10000.0
NEG_FILL = -1e30
Q_BLOCK = 256
K_BLOCK = 256
MIB = 1 << 20
LIGHT = 1000
TILE = 256
PIECES = 2
SCALE = 1.0 / math.sqrt(HD)


def to_bf(value):
    return value.astype(jnp.bfloat16)


def to_f(value):
    return value.astype(jnp.float32)


def dot(left, right, left_dim=1, right_dim=0):
    return lax.dot_general(
        left,
        right,
        (((left_dim,), (right_dim,)), ((), ())),
        preferred_element_type=jnp.float32,
    )


def flipped(axis, bit):
    return [(i, i ^ (1 << bit)) for i in range(lax.axis_size(axis))]


def core_swap(value):
    return lax.ppermute(value, "tensor", flipped("tensor", 0))


def chip_swap(value):
    return lax.ppermute(value, "tensor", flipped("tensor", 1))


def core_swaps(values):
    return [core_swap(value) for value in values]


def chip_swaps(values):
    return [chip_swap(value) for value in values]


def shifted(value, hops):
    count = lax.axis_size("seq")
    route = [(i, i + hops) for i in range(count) if 0 <= i + hops < count]
    return lax.ppermute(value, "seq", route)


def cost(flops, read):
    return pl.CostEstimate(flops=flops // LIGHT, bytes_accessed=read // LIGHT, transcendentals=0)


class Order:
    def __init__(self):
        self.mark = None
        self.touched = []

    def arrived(self, *values):
        self.touched.extend(values)

    def __call__(self, kernel, args, in_specs, out_specs, out_shape, grid, flops, read, name, scalars=(), scratch=()):
        anchor = ([] if self.mark is None else [self.mark]) + self.touched
        self.touched = []
        count = len(scalars) + len(args)
        outs = len(out_shape)

        def run(*refs):
            rest = refs[count + len(anchor) :]
            kernel(*refs[:count], *rest[:outs], *rest[outs + 1 :])
            rest[outs][...] = jnp.zeros(rest[outs].shape, jnp.float32)

        *results, self.mark = pl.pallas_call(
            run,
            grid_spec=pltpu.PrefetchScalarGridSpec(
                num_scalar_prefetch=len(scalars),
                grid=grid,
                in_specs=list(in_specs) + anchors(len(anchor)),
                out_specs=list(out_specs) + [mark_spec()],
                scratch_shapes=list(scratch),
            ),
            out_shape=list(out_shape) + [MARK],
            compiler_params=pltpu.CompilerParams(vmem_limit_bytes=32 * MIB),
            cost_estimate=cost(flops, read),
            name=name,
        )(*scalars, *args, *anchor)
        return results


def first_kernel(core_ref, tok_ref, gain_ref, w_ref, b_ref, cos_ref, sin_ref, h_ref, q_ref, kv_ref):
    x = to_f(tok_ref[...])
    factor = lax.rsqrt(jnp.mean(x * x, axis=-1, keepdims=True) + EPS)
    h = to_bf(x * factor * gain_ref[...])
    h_ref[...] = h
    lin = dot(h, w_ref[...]) + b_ref[...]
    cosine = cos_ref[...]
    sine = sin_ref[...]
    heads = q_ref.shape[1] // HD
    for head in range(heads):
        part = lin[:, head * HD : (head + 1) * HD]
        q_ref[:, head * HD : (head + 1) * HD] = to_bf(
            part * cosine + pltpu.roll(part, HD // 2, 1) * sine
        )
    part = lin[:, heads * HD :]
    is_key = core_ref[0] == 0
    kv_ref[...] = to_bf(
        part * jnp.where(is_key, cosine, 1.0)
        + pltpu.roll(part, HD // 2, 1) * jnp.where(is_key, sine, 0.0)
    )


def first(core, tokens, gain, weight, bias, cosine, sine):
    total, width = tokens.shape
    columns = weight.shape[1]
    block = total // 4
    half = 2

    def flip(i, core_ref):
        return (lax.rem(i + core_ref[0] * half, 4), 0)

    def at(i, core_ref):
        return (i, 0)

    def whole(i, core_ref):
        return (0, 0)

    return pl.pallas_call(
        first_kernel,
        grid_spec=pltpu.PrefetchScalarGridSpec(
            num_scalar_prefetch=1,
            grid=(4,),
            in_specs=[
                pl.BlockSpec((block, width), flip),
                pl.BlockSpec((1, width), whole),
                pl.BlockSpec((width, columns), whole),
                pl.BlockSpec((1, columns), whole),
                pl.BlockSpec((block, HD), at),
                pl.BlockSpec((block, HD), at),
            ],
            out_specs=[
                pl.BlockSpec((block, width), at),
                pl.BlockSpec((block, columns - HD), at),
                pl.BlockSpec((block, HD), at),
            ],
        ),
        out_shape=[
            jax.ShapeDtypeStruct((total, width), jnp.bfloat16),
            jax.ShapeDtypeStruct((total, columns - HD), jnp.bfloat16),
            jax.ShapeDtypeStruct((total, HD), jnp.bfloat16),
        ],
        compiler_params=pltpu.CompilerParams(vmem_limit_bytes=32 * MIB),
        cost_estimate=cost(2 * total * width * columns, 9 * MIB),
        name="first",
    )(core, tokens, gain, weight, bias, cosine, sine)


def stacked(ref, start, count, heads):
    return jnp.concatenate(
        [ref[0, pl.ds(start, count), h * HD : (h + 1) * HD] for h in range(heads)], axis=0
    )


def bounds(start_ref, index, heads, reach):
    first_key = jnp.concatenate(
        [start_ref[0, :, pl.ds(index * Q_BLOCK, Q_BLOCK)]] * heads, axis=1
    )
    place = reach + index * Q_BLOCK + lax.broadcasted_iota(jnp.int32, (1, Q_BLOCK), 1)
    return first_key, jnp.concatenate([place] * heads, axis=1)


def gather_span(core, refs, span):
    count = len(refs) // 2
    local = refs[0].shape[1]
    for i in range(count):
        here = slice(i * local, (i + 1) * local)
        span[core, here] = refs[i][0]
        span[1 - core, here] = refs[count + i][0]


def attend_kernel(heads, blocks, pieces, low_ref, core_ref, q_ref, start_ref, *refs):
    o_ref, lse_ref, acc, span = refs[2 * pieces :]
    row = pl.program_id(0)
    wide = heads * Q_BLOCK
    reach = (pieces - 1) * q_ref.shape[1]
    gather_span(core_ref[0], refs[: 2 * pieces], span)
    for index in range(blocks):
        q = stacked(q_ref, index * Q_BLOCK, Q_BLOCK, heads)
        first_key, place = bounds(start_ref, index, heads, reach)
        acc[...] = jnp.zeros_like(acc)

        def step(j, carry):
            top, total = carry
            keys = pl.ds(pl.multiple_of(j * K_BLOCK, K_BLOCK), K_BLOCK)
            s = dot(span[0, keys], q, 1, 1) * SCALE
            key = j * K_BLOCK + lax.broadcasted_iota(jnp.int32, (K_BLOCK, wide), 0)
            s = jnp.where((key >= first_key) & (key <= place), s, NEG_FILL)
            later = jnp.maximum(top, jnp.max(s, axis=0, keepdims=True))
            p = jnp.exp(s - later)
            fade = jnp.exp(top - later)
            total = total * fade + jnp.sum(p, axis=0, keepdims=True)
            acc[...] = acc[...] * fade + dot(span[1, keys], to_bf(p), 0, 0)
            return later, total

        last = (reach + (index + 1) * Q_BLOCK - 1) // K_BLOCK + 1
        top, total = lax.fori_loop(
            low_ref[row, index],
            last,
            step,
            (jnp.full((1, wide), NEG_FILL, jnp.float32), jnp.zeros((1, wide), jnp.float32)),
        )
        out = to_bf((acc[...] / total).T)
        for h in range(heads):
            o_ref[0, index * Q_BLOCK : (index + 1) * Q_BLOCK, h * HD : (h + 1) * HD] = out[
                h * Q_BLOCK : (h + 1) * Q_BLOCK
            ]
        lse_ref[0, index : index + 1, :] = top + jnp.log(total)


def span_specs(rows, local, pieces):
    near = pl.BlockSpec((1, local, HD), lambda i, *refs: (i, 0, 0))
    far = pl.BlockSpec((1, local, HD), lambda i, *refs: (lax.rem(i + rows // 2, rows), 0, 0))
    return [near] * pieces + [far] * pieces


def attend(low, core, q, start, span, mate):
    rows, local, columns = q.shape
    pieces = len(span)
    heads = columns // HD
    blocks = local // Q_BLOCK

    def at(i, *refs):
        return (i, 0, 0)

    return pl.pallas_call(
        functools.partial(attend_kernel, heads, blocks, pieces),
        grid_spec=pltpu.PrefetchScalarGridSpec(
            num_scalar_prefetch=2,
            grid=(rows,),
            in_specs=[pl.BlockSpec((1, local, columns), at), pl.BlockSpec((1, 1, local), at)]
            + span_specs(rows, local, pieces),
            out_specs=[
                pl.BlockSpec((1, local, columns), at),
                pl.BlockSpec((1, blocks, heads * Q_BLOCK), at),
            ],
            scratch_shapes=[
                pltpu.VMEM((HD, heads * Q_BLOCK), jnp.float32),
                pltpu.VMEM((2, pieces * local, HD), jnp.bfloat16),
            ],
        ),
        out_shape=[
            jax.ShapeDtypeStruct((rows, local, columns), jnp.bfloat16),
            jax.ShapeDtypeStruct((rows, blocks, heads * Q_BLOCK), jnp.float32),
        ],
        compiler_params=pltpu.CompilerParams(vmem_limit_bytes=32 * MIB),
        cost_estimate=cost(8_000_000_000, 4 * MIB),
        name="attend",
    )(low, core, q, start, *span, *mate)


def attend_back_kernel(
    heads, blocks, pieces, low_ref, core_ref, q_ref, start_ref, g_ref, o_ref, lse_ref, cos_ref, sin_ref, *refs
):
    gq_ref, keep_ref, *sends, acc, gk, gv, span = refs[2 * pieces :]
    row = pl.program_id(0)
    wide = heads * Q_BLOCK
    reach = (pieces - 1) * q_ref.shape[1]
    core = core_ref[0]
    gather_span(core, refs[: 2 * pieces], span)
    gk[...] = jnp.zeros_like(gk)
    gv[...] = jnp.zeros_like(gv)
    for index in range(blocks):
        q = stacked(q_ref, index * Q_BLOCK, Q_BLOCK, heads)
        g = stacked(g_ref, index * Q_BLOCK, Q_BLOCK, heads)
        o = stacked(o_ref, index * Q_BLOCK, Q_BLOCK, heads)
        inner = jnp.sum((to_f(g) * to_f(o)).T, axis=0, keepdims=True)
        lse = lse_ref[0, index : index + 1, :]
        first_key, place = bounds(start_ref, index, heads, reach)
        acc[...] = jnp.zeros_like(acc)

        def step(j, carry):
            keys = pl.ds(pl.multiple_of(j * K_BLOCK, K_BLOCK), K_BLOCK)
            k = span[0, keys]
            s = dot(k, q, 1, 1) * SCALE
            key = j * K_BLOCK + lax.broadcasted_iota(jnp.int32, (K_BLOCK, wide), 0)
            p = jnp.where((key >= first_key) & (key <= place), jnp.exp(s - lse), 0.0)
            gp = dot(span[1, keys], g, 1, 1)
            gs = to_bf(p * (gp - inner))
            gv[keys] += dot(to_bf(p), g)
            gk[keys] += dot(gs, q)
            acc[...] += dot(k, gs, 0, 0)
            return carry

        last = (reach + (index + 1) * Q_BLOCK - 1) // K_BLOCK + 1
        lax.fori_loop(low_ref[row, index], last, step, 0)
        gq = acc[...].T * SCALE
        here = slice(index * Q_BLOCK, (index + 1) * Q_BLOCK)
        cosine, sine = cos_ref[here], sin_ref[here]
        for h in range(heads):
            part = gq[h * Q_BLOCK : (h + 1) * Q_BLOCK]
            gq_ref[0, here, h * HD : (h + 1) * HD] = to_bf(
                part * cosine + pltpu.roll(part * sine, HD // 2, 1)
            )
    is_key = core == 0
    keys, values = gk[...] * SCALE, gv[...]
    keep_ref[0] = to_bf(jnp.where(is_key, keys, values))
    sent = to_bf(jnp.where(is_key, values, keys))
    for i, ref in enumerate(sends):

        @pl.when(row == i)
        def _(ref=ref):
            ref[0] = sent


def attend_back(order, low, core, q, start, span, mate, grad, out, lse, cosine, sine):
    rows, local, columns = q.shape
    pieces = len(span)
    window = pieces * local
    heads = columns // HD
    blocks = local // Q_BLOCK

    def at(i, *refs):
        return (i, 0, 0)

    table = pl.BlockSpec((local, HD), lambda i, *refs: (i, 0))
    tokens = pl.BlockSpec((1, local, columns), at)
    return order(
        functools.partial(attend_back_kernel, heads, blocks, pieces),
        [q, start, grad, out, lse, cosine, sine, *span, *mate],
        [
            tokens,
            pl.BlockSpec((1, 1, local), at),
            tokens,
            tokens,
            pl.BlockSpec((1, blocks, heads * Q_BLOCK), at),
            table,
            table,
        ]
        + span_specs(rows, local, pieces),
        [tokens, pl.BlockSpec((1, window, HD), at)]
        + [pl.BlockSpec((1, window, HD), lambda i, *refs: (0, 0, 0))] * rows,
        [
            jax.ShapeDtypeStruct((rows, local, columns), jnp.bfloat16),
            jax.ShapeDtypeStruct((rows, window, HD), jnp.bfloat16),
        ]
        + [jax.ShapeDtypeStruct((1, window, HD), jnp.bfloat16)] * rows,
        (rows,),
        20_000_000_000,
        6 * MIB,
        "attend_back",
        scalars=(low, core),
        scratch=[
            pltpu.VMEM((HD, heads * Q_BLOCK), jnp.float32),
            pltpu.VMEM((window, HD), jnp.float32),
            pltpu.VMEM((window, HD), jnp.float32),
            pltpu.VMEM((2, window, HD), jnp.bfloat16),
        ],
    )


def fold_kernel(rows, keep_ref, *refs):
    comes, own_ref, send_refs = refs[:rows], refs[rows], refs[rows + 1 :]
    local = own_ref.shape[1]
    come = comes[0][0]
    for i in range(1, rows):
        come = jnp.where(pl.program_id(0) == i, comes[i][0], come)
    total = to_f(keep_ref[0]) + to_f(come)
    reach = total.shape[0] - local
    own_ref[0] = total[reach:]
    for hop, ref in enumerate(send_refs, 1):
        ref[0] = to_bf(total[reach - hop * local : reach - (hop - 1) * local])


def fold(order, keep, comes, local):
    rows, window = keep.shape[:2]
    hops = window // local - 1
    out = pl.BlockSpec((1, local, HD), lambda i: (i, 0, 0))
    return order(
        functools.partial(fold_kernel, rows),
        [keep, *comes],
        [pl.BlockSpec((1, window, HD), lambda i: (i, 0, 0))]
        + [pl.BlockSpec((1, window, HD), lambda i: (0, 0, 0))] * rows,
        [out] * (hops + 1),
        [jax.ShapeDtypeStruct((rows, local, HD), jnp.float32)]
        + [jax.ShapeDtypeStruct((rows, local, HD), jnp.bfloat16)] * hops,
        (rows,),
        0,
        4 * MIB,
        "fold",
    )


def carry_kernel(piece_ref, come_ref, out_ref):
    out_ref[...] = to_bf(to_f(piece_ref[...]) + to_f(come_ref[...]))


def carry(order, piece, come):
    rows, local, columns = piece.shape
    at = pl.BlockSpec((1, local, columns), lambda i: (i, 0, 0))
    return order(
        carry_kernel,
        [piece, come],
        [at, at],
        [at],
        [jax.ShapeDtypeStruct(piece.shape, jnp.bfloat16)],
        (rows,),
        0,
        2 * MIB,
        "carry",
    )[0]


def bias_kernel(left_ref, right_ref, out_ref):
    out_ref[...] = left_ref[...] + right_ref[...]


def bias_add(order, left, right):
    whole = pl.BlockSpec(left.shape, lambda i: (0, 0))
    return order(
        bias_kernel,
        [left, right],
        [whole, whole],
        [whole],
        [jax.ShapeDtypeStruct(left.shape, jnp.float32)],
        (1,),
        0,
        MIB,
        "bias",
    )[0]


def join_kernel(hops, core_ref, gq_ref, cos_ref, sin_ref, own_ref, *refs):
    out_ref, sum_ref = refs[-2:]
    columns = gq_ref.shape[2]
    grad = own_ref[0]
    for ref in refs[:hops]:
        grad = grad + to_f(ref[0])
    is_key = core_ref[0] == 0
    cosine = jnp.where(is_key, cos_ref[...], 1.0)
    sine = jnp.where(is_key, sin_ref[...], 0.0)
    kv = to_bf(grad * cosine + pltpu.roll(grad * sine, HD // 2, 1))
    q = gq_ref[0]
    out_ref[:, :columns] = q
    out_ref[:, columns:] = kv

    @pl.when(pl.program_id(0) == 0)
    def _():
        sum_ref[...] = jnp.zeros(sum_ref.shape, jnp.float32)

    sum_ref[:, :columns] += jnp.sum(to_f(q), axis=0, keepdims=True)
    sum_ref[:, columns:] += jnp.sum(to_f(kv), axis=0, keepdims=True)


def join(order, core, grad_q, own, comes, cosine, sine):
    rows, local, columns = grad_q.shape
    wide = columns + HD

    def at(i, *refs):
        return (i, 0, 0)

    piece = pl.BlockSpec((1, local, HD), at)
    table = pl.BlockSpec((local, HD), lambda i, *refs: (i, 0))
    return order(
        functools.partial(join_kernel, len(comes)),
        [grad_q, cosine, sine, own, *comes],
        [pl.BlockSpec((1, local, columns), at), table, table, piece] + [piece] * len(comes),
        [
            pl.BlockSpec((local, wide), lambda i, *refs: (i, 0)),
            pl.BlockSpec((8, wide), lambda i, *refs: (0, 0)),
        ],
        [
            jax.ShapeDtypeStruct((rows * local, wide), jnp.bfloat16),
            jax.ShapeDtypeStruct((8, wide), jnp.float32),
        ],
        (rows,),
        0,
        4 * MIB,
        "join",
        scalars=(core,),
    )


def mixed_back_kernel(w_ref, *refs):
    rows = refs[0].shape[0]
    for i, ref in enumerate(refs[:-1]):
        refs[-1][i * rows : (i + 1) * rows] = to_bf(dot(ref[...], w_ref[...]))


def mixed_back(order, pieces, weight):
    rows, width = pieces[0].shape
    total = rows * len(pieces)
    columns = weight.shape[1]

    def whole(i):
        return (0, 0)

    return order(
        mixed_back_kernel,
        [weight, *pieces],
        [pl.BlockSpec((width, columns), whole)] + [pl.BlockSpec((rows, width), whole)] * len(pieces),
        [pl.BlockSpec((total, columns), whole)],
        [jax.ShapeDtypeStruct((total, columns), jnp.bfloat16)],
        (1,),
        2 * total * width * columns,
        6 * MIB,
        "mixed_back",
    )[0]


def place_kernel(core_ref, *refs):
    for i, ref in enumerate(refs[:-1]):

        @pl.when(pl.program_id(0) == i)
        def _(ref=ref):
            refs[-1][...] = ref[...]


def place(order, core, pieces):
    rows, width = pieces[0].shape
    count = len(pieces)
    return order(
        place_kernel,
        list(pieces),
        [pl.BlockSpec((rows, width), lambda i, core_ref: (0, 0))] * count,
        [pl.BlockSpec((rows, width), lambda i, core_ref: (lax.rem(i + core_ref[0] * (count // 2), count), 0))],
        [jax.ShapeDtypeStruct((rows * count, width), pieces[0].dtype)],
        (count,),
        0,
        8 * rows * width,
        "place",
        scalars=(core,),
    )[0]


def anchors(count):
    return [pl.BlockSpec(memory_space=pl.ANY)] * count


MARK = jax.ShapeDtypeStruct((8, HD), jnp.float32)


def mark_spec():
    return pl.BlockSpec((8, HD), lambda *refs: (0, 0))


def grad_hidden_kernel(g_ref, w_ref, out_ref):
    out_ref[...] = to_bf(dot(g_ref[...], w_ref[...], 1, 1))


def grad_hidden_of(order, grad, weight):
    total, width = grad.shape
    hidden = weight.shape[0]
    return order(
        grad_hidden_kernel,
        [grad, weight],
        [pl.BlockSpec((total, width), lambda i: (0, 0)), pl.BlockSpec((TILE, width), lambda i: (i, 0))],
        [pl.BlockSpec((total, TILE), lambda i: (0, i))],
        [jax.ShapeDtypeStruct((total, hidden), jnp.bfloat16)],
        (pl.cdiv(hidden, TILE),),
        2 * total * width * hidden,
        15 * MIB,
        "grad_hidden",
    )[0]


def gated_kernel(gh_ref, gw_ref, uw_ref, *refs):
    hid_ref, gg_ref, gu_ref = refs[-3:]
    rows = refs[0].shape[0]
    for part, ref in enumerate(refs[:-3]):
        here = slice(part * rows, (part + 1) * rows)
        h = ref[...]
        gate = dot(h, gw_ref[...], 1, 1)
        up = dot(h, uw_ref[...], 1, 1)
        grad = to_f(gh_ref[here])
        sigma = 1.0 / (1.0 + jnp.exp(-gate))
        swish = gate * sigma
        hid_ref[here] = to_bf(swish * up)
        gu_ref[here] = to_bf(grad * swish)
        gg_ref[here] = to_bf(grad * up * sigma * (1.0 + gate * (1.0 - sigma)))


def gated(order, pieces, grad_hidden, gate_weight, up_weight):
    rows, width = pieces[0].shape
    total = rows * len(pieces)
    hidden = gate_weight.shape[0]
    column = pl.BlockSpec((total, TILE), lambda i: (0, i))
    weight = pl.BlockSpec((TILE, width), lambda i: (i, 0))
    shape = jax.ShapeDtypeStruct((total, hidden), jnp.bfloat16)
    return order(
        gated_kernel,
        [grad_hidden, gate_weight, up_weight, *pieces],
        [column, weight, weight] + [pl.BlockSpec((rows, width), lambda i: (0, 0))] * len(pieces),
        [column] * 3,
        [shape] * 3,
        (pl.cdiv(hidden, TILE),),
        4 * total * width * hidden,
        30 * MIB,
        "gated",
    )


def share_kernel(plan, lefts, rights, extra, halves, pick_ref, blocks_ref, *refs):
    step = pl.program_id(0)
    left_refs, right_refs = refs[:lefts], refs[lefts : lefts + rights]
    refs = refs[lefts + rights :]
    if extra:
        extra_ref, refs = refs[0], refs[1:]
    for left, right, begin, end, shift, columns, target in plan:

        @pl.when((step >= begin) & (step < end))
        def _(left=left, right=right, shift=shift, columns=columns, target=target):
            out = dot(left_refs[left][...], right_refs[right][...])
            if extra:
                out = out + to_f(extra_ref[...])
            tile = out.shape[1]
            spot = (step + shift) * tile + lax.broadcasted_iota(jnp.int32, (1, tile), 1)
            out = to_bf(jnp.where(spot < columns, out, 0.0))
            if not halves:
                refs[target][...] = out
                return
            send_ref, keep_ref, rows = refs
            rows[...] = out
            share = send_ref.shape[0] // (2 * halves)
            for i in range(2 * halves):
                here = slice(i * share, (i + 1) * share)
                send_ref[here] = rows[pl.ds(pl.multiple_of(blocks_ref[i] * share, share), share)]
                keep_ref[here] = rows[pl.ds(pl.multiple_of(blocks_ref[2 * halves + i] * share, share), share)]


def clipped(rows, tile, begin, count, shift=0):
    return pl.BlockSpec((rows, tile), lambda i, *refs: (0, jnp.clip(i - begin, 0, count - 1) + shift))


def share_of(order, lefts, rights, parts, part, pick, tile, extra=None, blocks=None):
    tokens = lefts[0].shape[1]
    plan, at = [], 0
    starts, sizes, right_at = {}, {}, {}
    for left, right, skip, count, target in parts:
        plan.append((left, right, at, at + count, skip - at, rights[right].shape[1], target))
        starts.setdefault(target, at)
        sizes[target] = sizes.get(target, 0) + count
        first, tiles, low = right_at.get(right, (at, 0, skip))
        right_at[right] = (first, tiles + count, low)
        at += count
    halves = 0
    extras = [] if extra is None else [extra]
    scratch = []
    if blocks is None:
        blocks = jnp.zeros((1,), jnp.int32)
        outs = [clipped(part, tile, starts[t], sizes[t]) for t in sorted(sizes)]
        shapes = [jax.ShapeDtypeStruct((part, sizes[t] * tile), jnp.bfloat16) for t in sorted(sizes)]
    else:
        halves = blocks.shape[0] // 4
        outs = [clipped(part // 2, tile, 0, at)] * 2
        shapes = [jax.ShapeDtypeStruct((part // 2, at * tile), jnp.bfloat16)] * 2
        scratch = [pltpu.VMEM((part, tile), jnp.bfloat16)]
    return order(
        functools.partial(share_kernel, plan, len(lefts), len(rights), len(extras), halves),
        [*lefts, *rights, *extras],
        [pl.BlockSpec((part, tokens), lambda i, pick_ref, blocks_ref: (pick_ref[0], 0))] * len(lefts)
        + [clipped(tokens, tile, *right_at[r]) for r in range(len(rights))]
        + [clipped(part, tile, 0, at)] * len(extras),
        outs,
        shapes,
        (at,),
        2 * part * tokens * at * tile,
        2 * (part * tokens + (part + tokens) * at * tile),
        "share",
        scalars=(jnp.asarray(pick, jnp.int32).reshape(1), blocks),
        scratch=scratch,
    )


def relay_kernel(keep_ref, come_ref, out_ref):
    out_ref[...] = to_bf(to_f(keep_ref[...]) + to_f(come_ref[...]))


def relay(order, keep, come, share):
    rows, columns = keep.shape
    pair = pl.BlockSpec((share, columns), lambda i: (2 * i + 1, 0))
    return order(
        relay_kernel,
        [keep, come],
        [pair, pair],
        [pl.BlockSpec((share, columns), lambda i: (i, 0))],
        [jax.ShapeDtypeStruct((rows // 2, columns), jnp.bfloat16)],
        (rows // (2 * share),),
        0,
        3 * rows * columns,
        "relay",
    )[0]


def finish_kernel(plan, columns, gains, *refs):
    out_ref = refs[-2] if gains else refs[-1]
    step = pl.program_id(0)
    tile = out_ref.shape[1]
    for begin, end, first, count in plan:

        @pl.when((step >= begin) & (step < end))
        def _(first=first, count=count):
            out = to_f(refs[first][...])
            for ref in refs[first + 1 : first + count]:
                out = out + to_f(ref[...])
            out_ref[...] = out
            if gains:
                spot = step * tile + lax.broadcasted_iota(jnp.int32, (1, tile), 1)
                terms = jnp.where(spot < columns, out * to_f(refs[-3][...]), 0.0)
                total = terms[:, :HD]
                for i in range(HD, tile, HD):
                    total = total + terms[:, i : i + HD]

                @pl.when(step == 0)
                def _():
                    refs[-1][...] = total

                @pl.when(step > 0)
                def _():
                    refs[-1][...] += total


def finish(order, chunks, share, columns, tile, weight=None):
    plan, specs, args, at = [], [], [], 0
    for chunk in chunks:
        count = chunk[0].shape[1] // tile
        plan.append((at, at + count, len(args), len(chunk)))
        specs += [clipped(share, tile, at, count)] * len(chunk)
        args += chunk
        at += count
    column = pl.BlockSpec((share, tile), lambda i: (0, i))
    outs, shapes = [column], [jax.ShapeDtypeStruct((share, columns), jnp.float32)]
    if weight is not None:
        args.append(weight)
        specs.append(column)
        outs.append(pl.BlockSpec((share, HD), lambda i: (0, 0)))
        shapes.append(jax.ShapeDtypeStruct((share, HD), jnp.float32))
    return order(
        functools.partial(finish_kernel, plan, columns, weight is not None),
        args,
        specs,
        outs,
        shapes,
        (at,),
        0,
        14 * share * columns,
        "finish",
    )


def narrow_kernel(pairs, extras, right_dim, *refs):
    out = dot(refs[0][...], refs[1][...], 1, right_dim)
    for i in range(1, pairs):
        out = out + dot(refs[2 * i][...], refs[2 * i + 1][...], 1, right_dim)
    extra = refs[2 * pairs : 2 * pairs + extras]
    outs = refs[2 * pairs + extras :]
    if extras:
        out = out + jnp.concatenate([to_f(ref[...]) for ref in extra], axis=0)
    rows = outs[0].shape[0]
    for i, ref in enumerate(outs):
        ref[...] = to_bf(out[i * rows : (i + 1) * rows])


def narrow(order, pairs, index, extra=(), right_dim=0):
    total, hidden = pairs[0][0].shape
    width = pairs[0][1].shape[1 - right_dim]
    half = total // 2
    piece = half // PIECES
    column = pl.BlockSpec((piece, TILE), lambda i: (0, i))
    right = (
        pl.BlockSpec((TILE, hidden), lambda i: (i, 0))
        if right_dim
        else pl.BlockSpec((hidden, TILE), lambda i: (0, i))
    )
    return order(
        functools.partial(narrow_kernel, len(pairs), len(extra), right_dim),
        [item for pair in pairs for item in pair] + list(extra),
        [pl.BlockSpec((half, hidden), lambda i: (index, 0)), right] * len(pairs) + [column] * len(extra),
        [column] * PIECES,
        [jax.ShapeDtypeStruct((piece, width), jnp.bfloat16)] * PIECES,
        (width // TILE,),
        2 * len(pairs) * half * width * hidden,
        2 * len(pairs) * (half + width) * hidden + 2 * half * width,
        "narrow",
    )


def piece_specs(piece, width, block):
    steps = piece // block
    return [
        pl.BlockSpec((block, width), lambda i, *refs, j=j: (jnp.clip(i - j * steps, 0, steps - 1), 0))
        for j in range(PIECES)
    ]


def pick_piece(refs):
    value = refs[0][...]
    for j, ref in enumerate(refs[1:], 1):
        value = jnp.where(pl.program_id(0) >= 4 * j // len(refs), ref[...], value)
    return value


def put_piece(refs, value):
    steps = 4 // len(refs)
    for j, ref in enumerate(refs):

        @pl.when(lax.div(pl.program_id(0), steps) == j)
        def _(ref=ref):
            ref[...] = value


def turn_kernel(*refs):
    rows = refs[0].shape[0]
    for i, ref in enumerate(refs[:-1]):
        refs[-1][:, i * rows : (i + 1) * rows] = ref[...].T


def turn(order, pieces):
    rows, width = pieces[0].shape
    total = rows * len(pieces)
    return order(
        turn_kernel,
        list(pieces),
        [pl.BlockSpec((rows, TILE), lambda i: (0, i))] * len(pieces),
        [pl.BlockSpec((TILE, total), lambda i: (i, 0))],
        [jax.ShapeDtypeStruct((width, total), jnp.bfloat16)],
        (width // TILE,),
        0,
        4 * total * width,
        "turn",
    )[0]


def grad_out_kernel(core_ref, cot_ref, valid_ref, out_ref, turned_ref):
    out = to_bf(to_f(cot_ref[...]) * valid_ref[...])
    out_ref[...] = out
    turned_ref[...] = out.T


def grad_out_of(order, core, cotangent, valid):
    total, width = cotangent.shape
    block = total // 4
    return order(
        grad_out_kernel,
        [cotangent, valid],
        [
            pl.BlockSpec((block, width), lambda i, core_ref: (lax.rem(i + core_ref[0] * 2, 4), 0)),
            pl.BlockSpec((block, 1), lambda i, core_ref: (i, 0)),
        ],
        [
            pl.BlockSpec((block, width), lambda i, core_ref: (i, 0)),
            pl.BlockSpec((width, block), lambda i, core_ref: (0, i)),
        ],
        [
            jax.ShapeDtypeStruct((total, width), jnp.bfloat16),
            jax.ShapeDtypeStruct((width, total), jnp.bfloat16),
        ],
        (4,),
        0,
        6 * total * width,
        "grad_out",
        scalars=(core,),
    )


def middle_kernel(core_ref, tok_ref, gain_ref, *refs):
    mine, come = pick_piece(refs[:PIECES]), pick_piece(refs[PIECES : 2 * PIECES])
    mid_ref, *h_refs = refs[2 * PIECES :]
    middle = to_f(tok_ref[...]) + (to_f(mine) + to_f(come))
    factor = lax.rsqrt(jnp.mean(middle * middle, axis=-1, keepdims=True) + EPS)
    mid_ref[...] = middle
    put_piece(h_refs, to_bf(middle * factor * gain_ref[...]))


def middle_of(order, core, tokens, mine, come, gain):
    piece, width = mine[0].shape
    half = piece * PIECES
    block = half // 4
    specs = piece_specs(piece, width, block)
    middle, *h = order(
        middle_kernel,
        [tokens, gain, *mine, *come],
        [
            pl.BlockSpec((block, width), lambda i, core_ref: (core_ref[0] * 4 + i, 0)),
            pl.BlockSpec((1, width), lambda i, core_ref: (0, 0)),
        ]
        + specs * 2,
        [pl.BlockSpec((block, width), lambda i, core_ref: (i, 0))] + specs,
        [jax.ShapeDtypeStruct((half, width), jnp.float32)]
        + [jax.ShapeDtypeStruct((piece, width), jnp.bfloat16)] * PIECES,
        (4,),
        0,
        9 * MIB,
        "middle",
        scalars=(core,),
    )
    return middle, h


def norm_back_kernel(core_ref, x_ref, gain_ref, up_ref, *refs):
    mine, come = pick_piece(refs[:PIECES]), pick_piece(refs[PIECES : 2 * PIECES])
    outs = refs[2 * PIECES :]
    grad = to_f(mine) + to_f(come)
    x = to_f(x_ref[...])
    factor = lax.rsqrt(jnp.mean(x * x, axis=-1, keepdims=True) + EPS)
    normed = x * factor
    weighted = grad * gain_ref[...]
    inner = jnp.mean(weighted * normed, axis=-1, keepdims=True)
    out = to_f(up_ref[...]) + factor * (weighted - normed * inner)
    if len(outs) > PIECES:
        outs[0][...] = out
        put_piece(outs[1:], to_bf(out))
    else:
        put_piece(outs, out)


def norm_back(order, core, mine, come, x, gain, up, by_core):
    piece, width = mine[0].shape
    half = piece * PIECES
    block = half // 4
    at = pl.BlockSpec((block, width), lambda i, core_ref: (i, 0))
    picked = pl.BlockSpec((block, width), lambda i, core_ref: (core_ref[0] * 4 + i, 0))
    specs = piece_specs(piece, width, block)
    if by_core:
        shapes = [jax.ShapeDtypeStruct((piece, width), jnp.float32)] * PIECES
    else:
        shapes = [jax.ShapeDtypeStruct((half, width), jnp.float32)]
        shapes += [jax.ShapeDtypeStruct((piece, width), jnp.bfloat16)] * PIECES
    return order(
        norm_back_kernel,
        [x, gain, up, *mine, *come],
        [picked if by_core else at, pl.BlockSpec((1, width), lambda i, core_ref: (0, 0)), at] + specs * 2,
        specs if by_core else [at] + specs,
        shapes,
        (4,),
        0,
        10 * MIB,
        "norm_back",
        scalars=(core,),
    )


def layer_kernel(middle_ref, *refs):
    mine, come = pick_piece(refs[:PIECES]), pick_piece(refs[PIECES : 2 * PIECES])
    put_piece(refs[2 * PIECES :], to_bf(middle_ref[...] + (to_f(mine) + to_f(come))))


def layer_of(order, middle, mine, come):
    piece, width = mine[0].shape
    block = piece * PIECES // 4
    specs = piece_specs(piece, width, block)
    return order(
        layer_kernel,
        [middle, *mine, *come],
        [pl.BlockSpec((block, width), lambda i: (i, 0))] + specs * 2,
        specs,
        [jax.ShapeDtypeStruct((piece, width), jnp.bfloat16)] * PIECES,
        (4,),
        0,
        5 * MIB,
        "layer",
    )


def tensor_gather(value, rank):
    mate = core_swap(value)
    pair = jnp.where(lax.rem(rank, 2) == 0, jnp.stack([value, mate]), jnp.stack([mate, value]))
    come = chip_swap(pair)
    return jnp.where(
        lax.div(rank, 2) == 0,
        jnp.concatenate([pair, come], axis=0),
        jnp.concatenate([come, pair], axis=0),
    )


def body(
    tokens,
    lengths,
    cotangent,
    q_weight,
    q_bias,
    k_weight,
    k_bias,
    v_weight,
    v_bias,
    o_weight,
    attn_gain,
    ffn_gain,
    gate_weight,
    up_weight,
    down_weight,
):
    rows, local, width = tokens.shape
    total = rows * local
    half = total // 2
    heads = q_weight.shape[1] // HD
    ranks = lax.axis_size("tensor")
    seqs = lax.axis_size("seq")
    rank = lax.axis_index("tensor")
    dp_index = lax.axis_index("dp")
    seq_index = lax.axis_index("seq")
    core = lax.rem(rank, 2)
    head = lax.div(rank, 2)
    core_one = core.reshape(1)
    hops = min(seqs - 1, -(-(MOST - 1) // local))
    reach = hops * local

    def own_first(value):
        turned = jnp.concatenate([value[rows // 2 :], value[: rows // 2]], axis=0)
        return jnp.where(core == 0, value, turned)

    slots = jnp.arange(lengths.shape[1], dtype=jnp.int32)
    lens = own_first(lengths)
    ends = jnp.sum(jnp.where(slots[None, :] <= slots[:, None], lens[:, None, :], 0), axis=2)
    spot = seq_index * local + jnp.arange(local, dtype=jnp.int32)
    begun = jnp.max(
        jnp.where(ends[:, None, :] <= spot[None, :, None], ends[:, None, :], 0), axis=2
    )
    valid = to_f(spot[None, :] < ends[:, -2:-1])
    position = (spot[None, :] - begun).reshape(total, 1)
    freqs = ROPE_BASE ** (-(jnp.arange(HD // 2, dtype=jnp.float32) * 2.0) / HD)
    angles = to_f(position) * freqs[None, :]
    cosine, sine = jnp.cos(angles), jnp.sin(angles)
    cosine = jnp.concatenate([cosine, cosine], axis=1)
    sine = jnp.concatenate([-sine, sine], axis=1)
    start = begun - (seq_index * local - reach)
    low = jnp.maximum(lax.div(jnp.maximum(start[:, ::Q_BLOCK], 0), K_BLOCK), 0)
    start = start.reshape(rows, 1, local)

    key_side = core == 0
    kv_weight = jnp.where(
        key_side,
        lax.dynamic_slice_in_dim(k_weight, head * HD, HD, 1),
        lax.dynamic_slice_in_dim(v_weight, head * HD, HD, 1),
    )
    kv_bias = jnp.where(
        key_side,
        lax.dynamic_slice_in_dim(k_bias, head * HD, HD, 0),
        lax.dynamic_slice_in_dim(v_bias, head * HD, HD, 0),
    )
    weight = jnp.concatenate([q_weight, kv_weight], axis=1)
    bias = to_f(jnp.concatenate([q_bias, kv_bias])).reshape(1, -1)
    gain_one = to_f(attn_gain).reshape(1, width)
    gain_two = to_f(ffn_gain).reshape(1, width)

    h_one, q_rot, kv = first(
        core_one, tokens.reshape(total, width), gain_one, weight, bias, cosine, sine
    )
    kv = kv.reshape(rows, local, HD)
    span = [shifted(kv, h) for h in range(hops, 0, -1)] + [kv]
    mate = [core_swap(piece) for piece in span]
    q_rows = q_rot.reshape(rows, local, heads * HD)
    mixed_rows, lse = attend(low, core_one, q_rows, start, span, mate)
    mixed = mixed_rows.reshape(total, heads * HD)

    order = Order()
    flat_tokens = tokens.reshape(total, width)
    dps = lax.axis_size("dp")
    near_pair = dps == 2 and seqs == 4
    part = width // dps
    share = part // seqs
    gate_t, up_t, down_t = gate_weight.T, up_weight.T, down_weight.T
    units = gate_t.shape[0]
    tiles = -(-units // TILE)
    cut = (tiles + 1) // 2
    long = -(-2 * tiles // 3)
    one, two = seq_index ^ 1, seq_index ^ 2
    three = seq_index ^ 3
    quad = jnp.stack([one, three, seq_index, two])

    begin = (dp_index * seqs + seq_index) * share

    def rows_of(value):
        return lax.dynamic_slice_in_dim(value, begin, share, 0)

    class Rows:
        def __init__(self, lefts, rights, parts, tile=TILE, sent=None):
            self.args = (order, lefts, rights, parts)
            self.tile = tile
            if not near_pair:
                (whole,) = share_of(*self.args, width, 0, tile)
                self.whole = lax.psum_scatter(whole, ("dp", "seq"), scatter_dimension=0, tiled=True)
                return
            if sent is None:
                (sent,) = share_of(*self.args, part, 1 - dp_index, tile)
            self.come = lax.ppermute(sent, "dp", flipped("dp", 0))

        def own(self):
            if near_pair:
                send, self.keep = share_of(*self.args, part, dp_index, self.tile, self.come, quad)
                self.come = lax.ppermute(send, "seq", flipped("seq", 0))

        def relay(self):
            if near_pair:
                sent = relay(order, self.keep, self.come, share)
                self.last = lax.ppermute(sent, "seq", flipped("seq", 1))

        def settled(self):
            if near_pair:
                order.arrived(self.last)

        def result(self):
            return [self.keep, self.come, self.last] if near_pair else [self.whole]

    class Scattered(Rows):
        def own(self):
            if near_pair:
                (mine,) = share_of(*self.args, part, dp_index, self.tile, self.come)
                self.whole = lax.psum_scatter(mine, "seq", scatter_dimension=0, tiled=True)

        def settled(self):
            order.arrived(self.whole)

        def result(self):
            return [self.whole]

    sent = core_swaps(narrow(order, [(mixed, o_weight)], 1, (), 1))
    mine = narrow(order, [(mixed, o_weight)], 0, sent, 1)
    come = chip_swaps(mine)
    grad_ffn, grad_ffn_t = grad_out_of(
        order, core_one, cotangent.reshape(total, width), valid.reshape(total, 1)
    )
    gate_rows, up_rows = rows_of(gate_weight), rows_of(up_weight)
    order.arrived(gate_rows, up_rows)
    grad_hidden = grad_hidden_of(order, grad_ffn, down_t)
    h_one_t = turn(order, [h_one])
    middle, h_two = middle_of(order, core_one, flat_tokens, mine, come, gain_two)
    h_two += core_swaps(h_two)
    hidden, grad_gate, grad_up = gated(order, h_two, grad_hidden, gate_t, up_t)

    down = Rows([grad_ffn_t], [hidden], [(0, 0, 0, tiles, 0)])
    pairs = [(grad_gate, gate_t), (grad_up, up_t)]
    sent = core_swaps(narrow(order, pairs, 1))
    mine = narrow(order, pairs, 0, sent)
    come = chip_swaps(mine)
    h_two_t = turn(order, h_two)
    if near_pair:
        sends = share_of(
            order,
            [h_two_t],
            [grad_gate, grad_up],
            [(0, 0, 0, tiles, 0), (0, 1, 0, long, 1), (0, 1, long, tiles - long, 2)],
            part,
            1 - dp_index,
            TILE,
        )
    else:
        sends = [None] * 3

    def half_rows(kind, right, begin, end, sent):
        return kind([h_two_t], [right], [(0, 0, begin, end - begin, 0)], TILE, sent)

    gate = half_rows(Scattered, grad_gate, 0, tiles, sends[0])
    up_a = half_rows(Rows, grad_up, 0, long, sends[1])
    up_b = half_rows(Rows, grad_up, long, tiles, sends[2])
    down.own()
    grad_middle, *branch = norm_back(order, core_one, mine, come, middle, gain_two, grad_ffn, False)
    branch += core_swaps(branch)
    grad_mixed = mixed_back(order, branch, o_weight).reshape(rows, local, heads * HD)
    grad_q_rows, keep, *sends = attend_back(
        order, low, core_one, q_rows, start, span, mate, grad_mixed, mixed_rows, lse, cosine, sine
    )
    comes = core_swaps([sends[(i + rows // 2) % rows] for i in range(rows)])
    branch_t = turn(order, branch)
    own_kv, *pieces = fold(order, keep, comes, local)
    moving = shifted(pieces[-1], -1) if pieces else None
    ffn_sent = core_swaps(narrow(order, [(hidden, down_t)], 1))
    down.relay()
    for piece in pieces[-2::-1]:
        moving = shifted(carry(order, piece, moving), -1)
    ffn_mine = narrow(order, [(hidden, down_t)], 0, ffn_sent)
    grad_qkv, bias_sum = join(
        order, core_one, grad_q_rows, own_kv, [] if moving is None else [moving], cosine, sine
    )
    sent = core_swaps(narrow(order, [(grad_qkv, weight)], 1, (), 1))
    last_parts = [(0, 0, 0, grad_qkv.shape[1] // HD, 0), (1, 1, 0, heads, 0)]
    last = Rows([h_one_t, branch_t], [grad_qkv, mixed], last_parts, HD)
    mine = narrow(order, [(grad_qkv, weight)], 0, sent, 1)
    come = chip_swaps(mine)
    gate.own()
    token = norm_back(order, core_one, mine, come, flat_tokens, gain_one, grad_middle, True)
    token += core_swaps(token)
    ffn_come = chip_swaps(ffn_mine)
    token_grad = place(order, core_one, token).reshape(rows, local, width)
    up_a.own()
    (down_grad,) = finish(order, [down.result()], share, units, TILE)
    layer = layer_of(order, middle, ffn_mine, ffn_come)
    layer += core_swaps(layer)
    last.own()
    layer_out = place(order, core_one, layer).reshape(rows, local, width)
    up_a.relay()
    up_b.own()
    last.relay()
    if near_pair:
        bias_come = lax.ppermute(bias_sum, "dp", flipped("dp", 0))
        bias_all = bias_add(order, bias_sum, bias_come)
        bias_come = lax.ppermute(bias_all, "seq", flipped("seq", 0))
    up_b.relay()
    gate_grad, gate_term = finish(order, [gate.result()], share, units, TILE, gate_rows)
    wide_columns = grad_qkv.shape[1]
    (last_grad,) = finish(order, [last.result()], share, wide_columns + heads * HD, HD)
    if near_pair:
        bias_all = bias_add(order, bias_all, bias_come)
        bias_come = lax.ppermute(bias_all, "seq", flipped("seq", 1))
        bias_all = (bias_all + bias_come)[:1]
    else:
        bias_all = lax.psum(bias_sum[:1], ("dp", "seq"))
    up_grad, up_term = finish(order, [up_a.result(), up_b.result()], share, units, TILE, up_rows)
    qkv_grad, o_grad = last_grad[:, :wide_columns], last_grad[:, wide_columns:]

    attn_term = jnp.sum(to_f(rows_of(weight)) * qkv_grad, axis=1)
    ffn_term = jnp.sum(gate_term + up_term, axis=1)
    columns = heads * HD
    room = -(-share // HD) * HD - share
    terms = jnp.pad(jnp.stack([ffn_term, attn_term]), ((0, 0), (0, room))).reshape(-1, HD)
    packed = jnp.concatenate([qkv_grad[:, columns:], bias_all.reshape(-1, HD), terms], axis=0)
    gathered = tensor_gather(packed, rank)
    term_rows = terms.shape[0]
    bias_count = bias_all.shape[1] // HD
    terms = gathered[:, share + bias_count :].reshape(ranks, 2, -1)[:, :, :share]
    ffn_gain_grad, attn_gain_grad = terms[0] + terms[1] + (terms[2] + terms[3])
    attn_gain_grad = attn_gain_grad / lax.dynamic_slice_in_dim(gain_one[0], begin, share, 0)
    ffn_gain_grad = ffn_gain_grad / lax.dynamic_slice_in_dim(gain_two[0], begin, share, 0)
    q_grad = qkv_grad[:, :columns]
    kv_parts = lax.dynamic_slice_in_dim(gathered, rank * (share // ranks), share // ranks, 1)
    k_grad = jnp.concatenate([kv_parts[2 * i] for i in range(KVH)], axis=1)
    v_grad = jnp.concatenate([kv_parts[2 * i + 1] for i in range(KVH)], axis=1)
    biases = gathered[:, share : share + bias_count]
    q_bias_grad = biases[:, :heads].reshape(-1)
    k_bias_grad = biases[0::2, heads].reshape(-1)
    v_bias_grad = biases[1::2, heads].reshape(-1)
    return (
        layer_out,
        token_grad,
        q_grad,
        q_bias_grad,
        k_grad,
        k_bias_grad,
        v_grad,
        v_bias_grad,
        o_grad,
        attn_gain_grad,
        ffn_gain_grad,
        gate_grad,
        up_grad,
        down_grad,
    )


def solution(mesh):
    in_specs = (
        P("dp", "seq", None),
        P("dp", None),
        P("dp", "seq", None),
        P(None, "tensor"),
        P("tensor"),
        P(),
        P(),
        P(),
        P(),
        P(None, "tensor"),
        P(),
        P(),
        P(None, "tensor"),
        P(None, "tensor"),
        P(None, "tensor"),
    )
    out_specs = (
        P("dp", "seq", None),
        P("dp", "seq", None),
        P(("dp", "seq"), "tensor"),
        P(),
        P(("dp", "seq", "tensor"), None),
        P(),
        P(("dp", "seq", "tensor"), None),
        P(),
        P(("dp", "seq"), "tensor"),
        P(("dp", "seq")),
        P(("dp", "seq")),
        P(("dp", "seq"), "tensor"),
        P(("dp", "seq"), "tensor"),
        P(("dp", "seq"), "tensor"),
    )
    return jax.shard_map(body, mesh=mesh, in_specs=in_specs, out_specs=out_specs, check_vma=False)
```

```python
import functools
import math

import jax
import jax.numpy as jnp
from jax import lax
from jax.experimental import pallas as pl
from jax.experimental.pallas import tpu as pltpu
from jax.sharding import PartitionSpec as P

KVH = 2
HD = 128
MOST = 1024
EPS = 1e-06
ROPE_BASE = 10000.0
NEG_FILL = -1e30
Q_BLOCK = 256
K_BLOCK = 256
MIB = 1 << 20
LIGHT = 1000
TILE = 256
PIECES = 2
SCALE = 1.0 / math.sqrt(HD)


def to_bf(value):
    return value.astype(jnp.bfloat16)


def to_f(value):
    return value.astype(jnp.float32)


def dot(left, right, left_dim=1, right_dim=0):
    return lax.dot_general(
        left,
        right,
        (((left_dim,), (right_dim,)), ((), ())),
        preferred_element_type=jnp.float32,
    )


def flipped(axis, bit):
    return [(i, i ^ (1 << bit)) for i in range(lax.axis_size(axis))]


def core_swap(value):
    return lax.ppermute(value, "tensor", flipped("tensor", 0))


def chip_swap(value):
    return lax.ppermute(value, "tensor", flipped("tensor", 1))


def core_swaps(values):
    return [core_swap(value) for value in values]


def chip_swaps(values):
    return [chip_swap(value) for value in values]


def shifted(value, hops):
    count = lax.axis_size("seq")
    route = [(i, i + hops) for i in range(count) if 0 <= i + hops < count]
    return lax.ppermute(value, "seq", route)


def cost(flops, read):
    return pl.CostEstimate(flops=flops // LIGHT, bytes_accessed=read // LIGHT, transcendentals=0)


class Order:
    def __init__(self):
        self.mark = None
        self.touched = []

    def arrived(self, *values):
        self.touched.extend(values)

    def __call__(self, kernel, args, in_specs, out_specs, out_shape, grid, flops, read, name, scalars=(), scratch=()):
        anchor = ([] if self.mark is None else [self.mark]) + self.touched
        self.touched = []
        count = len(scalars) + len(args)
        outs = len(out_shape)

        def run(*refs):
            rest = refs[count + len(anchor) :]
            kernel(*refs[:count], *rest[:outs], *rest[outs + 1 :])
            rest[outs][...] = jnp.zeros(rest[outs].shape, jnp.float32)

        *results, self.mark = pl.pallas_call(
            run,
            grid_spec=pltpu.PrefetchScalarGridSpec(
                num_scalar_prefetch=len(scalars),
                grid=grid,
                in_specs=list(in_specs) + anchors(len(anchor)),
                out_specs=list(out_specs) + [mark_spec()],
                scratch_shapes=list(scratch),
            ),
            out_shape=list(out_shape) + [MARK],
            compiler_params=pltpu.CompilerParams(vmem_limit_bytes=32 * MIB),
            cost_estimate=cost(flops, read),
            name=name,
        )(*scalars, *args, *anchor)
        return results


def first_kernel(core_ref, tok_ref, gain_ref, w_ref, b_ref, cos_ref, sin_ref, h_ref, q_ref, kv_ref):
    x = to_f(tok_ref[...])
    factor = lax.rsqrt(jnp.mean(x * x, axis=-1, keepdims=True) + EPS)
    h = to_bf(x * factor * gain_ref[...])
    h_ref[...] = h
    lin = dot(h, w_ref[...]) + b_ref[...]
    cosine = cos_ref[...]
    sine = sin_ref[...]
    heads = q_ref.shape[1] // HD
    for head in range(heads):
        part = lin[:, head * HD : (head + 1) * HD]
        q_ref[:, head * HD : (head + 1) * HD] = to_bf(
            part * cosine + pltpu.roll(part, HD // 2, 1) * sine
        )
    part = lin[:, heads * HD :]
    is_key = core_ref[0] == 0
    kv_ref[...] = to_bf(
        part * jnp.where(is_key, cosine, 1.0)
        + pltpu.roll(part, HD // 2, 1) * jnp.where(is_key, sine, 0.0)
    )


def first(core, tokens, gain, weight, bias, cosine, sine):
    total, width = tokens.shape
    columns = weight.shape[1]
    block = total // 4
    half = 2

    def flip(i, core_ref):
        return (lax.rem(i + core_ref[0] * half, 4), 0)

    def at(i, core_ref):
        return (i, 0)

    def whole(i, core_ref):
        return (0, 0)

    return pl.pallas_call(
        first_kernel,
        grid_spec=pltpu.PrefetchScalarGridSpec(
            num_scalar_prefetch=1,
            grid=(4,),
            in_specs=[
                pl.BlockSpec((block, width), flip),
                pl.BlockSpec((1, width), whole),
                pl.BlockSpec((width, columns), whole),
                pl.BlockSpec((1, columns), whole),
                pl.BlockSpec((block, HD), at),
                pl.BlockSpec((block, HD), at),
            ],
            out_specs=[
                pl.BlockSpec((block, width), at),
                pl.BlockSpec((block, columns - HD), at),
                pl.BlockSpec((block, HD), at),
            ],
        ),
        out_shape=[
            jax.ShapeDtypeStruct((total, width), jnp.bfloat16),
            jax.ShapeDtypeStruct((total, columns - HD), jnp.bfloat16),
            jax.ShapeDtypeStruct((total, HD), jnp.bfloat16),
        ],
        compiler_params=pltpu.CompilerParams(vmem_limit_bytes=32 * MIB),
        cost_estimate=cost(2 * total * width * columns, 9 * MIB),
        name="first",
    )(core, tokens, gain, weight, bias, cosine, sine)


def stacked(ref, start, count, heads):
    return jnp.concatenate(
        [ref[0, pl.ds(start, count), h * HD : (h + 1) * HD] for h in range(heads)], axis=0
    )


def bounds(start_ref, index, heads, reach):
    first_key = jnp.concatenate(
        [start_ref[0, :, pl.ds(index * Q_BLOCK, Q_BLOCK)]] * heads, axis=1
    )
    place = reach + index * Q_BLOCK + lax.broadcasted_iota(jnp.int32, (1, Q_BLOCK), 1)
    return first_key, jnp.concatenate([place] * heads, axis=1)


def gather_span(core, refs, span):
    count = len(refs) // 2
    local = refs[0].shape[1]
    for i in range(count):
        here = slice(i * local, (i + 1) * local)
        span[core, here] = refs[i][0]
        span[1 - core, here] = refs[count + i][0]


def attend_kernel(heads, blocks, pieces, low_ref, core_ref, q_ref, start_ref, *refs):
    o_ref, lse_ref, acc, span = refs[2 * pieces :]
    row = pl.program_id(0)
    wide = heads * Q_BLOCK
    reach = (pieces - 1) * q_ref.shape[1]
    gather_span(core_ref[0], refs[: 2 * pieces], span)
    for index in range(blocks):
        q = stacked(q_ref, index * Q_BLOCK, Q_BLOCK, heads)
        first_key, place = bounds(start_ref, index, heads, reach)
        acc[...] = jnp.zeros_like(acc)

        def step(j, carry):
            top, total = carry
            keys = pl.ds(pl.multiple_of(j * K_BLOCK, K_BLOCK), K_BLOCK)
            s = dot(span[0, keys], q, 1, 1) * SCALE
            key = j * K_BLOCK + lax.broadcasted_iota(jnp.int32, (K_BLOCK, wide), 0)
            s = jnp.where((key >= first_key) & (key <= place), s, NEG_FILL)
            later = jnp.maximum(top, jnp.max(s, axis=0, keepdims=True))
            p = jnp.exp(s - later)
            fade = jnp.exp(top - later)
            total = total * fade + jnp.sum(p, axis=0, keepdims=True)
            acc[...] = acc[...] * fade + dot(span[1, keys], to_bf(p), 0, 0)
            return later, total

        last = (reach + (index + 1) * Q_BLOCK - 1) // K_BLOCK + 1
        top, total = lax.fori_loop(
            low_ref[row, index],
            last,
            step,
            (jnp.full((1, wide), NEG_FILL, jnp.float32), jnp.zeros((1, wide), jnp.float32)),
        )
        out = to_bf((acc[...] / total).T)
        for h in range(heads):
            o_ref[0, index * Q_BLOCK : (index + 1) * Q_BLOCK, h * HD : (h + 1) * HD] = out[
                h * Q_BLOCK : (h + 1) * Q_BLOCK
            ]
        lse_ref[0, index : index + 1, :] = top + jnp.log(total)


def span_specs(rows, local, pieces):
    near = pl.BlockSpec((1, local, HD), lambda i, *refs: (i, 0, 0))
    far = pl.BlockSpec((1, local, HD), lambda i, *refs: (lax.rem(i + rows // 2, rows), 0, 0))
    return [near] * pieces + [far] * pieces


def attend(low, core, q, start, span, mate):
    rows, local, columns = q.shape
    pieces = len(span)
    heads = columns // HD
    blocks = local // Q_BLOCK

    def at(i, *refs):
        return (i, 0, 0)

    return pl.pallas_call(
        functools.partial(attend_kernel, heads, blocks, pieces),
        grid_spec=pltpu.PrefetchScalarGridSpec(
            num_scalar_prefetch=2,
            grid=(rows,),
            in_specs=[pl.BlockSpec((1, local, columns), at), pl.BlockSpec((1, 1, local), at)]
            + span_specs(rows, local, pieces),
            out_specs=[
                pl.BlockSpec((1, local, columns), at),
                pl.BlockSpec((1, blocks, heads * Q_BLOCK), at),
            ],
            scratch_shapes=[
                pltpu.VMEM((HD, heads * Q_BLOCK), jnp.float32),
                pltpu.VMEM((2, pieces * local, HD), jnp.bfloat16),
            ],
        ),
        out_shape=[
            jax.ShapeDtypeStruct((rows, local, columns), jnp.bfloat16),
            jax.ShapeDtypeStruct((rows, blocks, heads * Q_BLOCK), jnp.float32),
        ],
        compiler_params=pltpu.CompilerParams(vmem_limit_bytes=32 * MIB),
        cost_estimate=cost(8_000_000_000, 4 * MIB),
        name="attend",
    )(low, core, q, start, *span, *mate)


def attend_back_kernel(
    heads, blocks, pieces, low_ref, core_ref, q_ref, start_ref, g_ref, o_ref, lse_ref, cos_ref, sin_ref, *refs
):
    gq_ref, keep_ref, send_ref, acc, gk, gv, span = refs[2 * pieces :]
    row = pl.program_id(0)
    wide = heads * Q_BLOCK
    reach = (pieces - 1) * q_ref.shape[1]
    core = core_ref[0]
    gather_span(core, refs[: 2 * pieces], span)
    gk[...] = jnp.zeros_like(gk)
    gv[...] = jnp.zeros_like(gv)
    for index in range(blocks):
        q = stacked(q_ref, index * Q_BLOCK, Q_BLOCK, heads)
        g = stacked(g_ref, index * Q_BLOCK, Q_BLOCK, heads)
        o = stacked(o_ref, index * Q_BLOCK, Q_BLOCK, heads)
        inner = jnp.sum((to_f(g) * to_f(o)).T, axis=0, keepdims=True)
        lse = lse_ref[0, index : index + 1, :]
        first_key, place = bounds(start_ref, index, heads, reach)
        acc[...] = jnp.zeros_like(acc)

        def step(j, carry):
            keys = pl.ds(pl.multiple_of(j * K_BLOCK, K_BLOCK), K_BLOCK)
            k = span[0, keys]
            s = dot(k, q, 1, 1) * SCALE
            key = j * K_BLOCK + lax.broadcasted_iota(jnp.int32, (K_BLOCK, wide), 0)
            p = jnp.where((key >= first_key) & (key <= place), jnp.exp(s - lse), 0.0)
            gp = dot(span[1, keys], g, 1, 1)
            gs = to_bf(p * (gp - inner))
            gv[keys] += dot(to_bf(p), g)
            gk[keys] += dot(gs, q)
            acc[...] += dot(k, gs, 0, 0)
            return carry

        last = (reach + (index + 1) * Q_BLOCK - 1) // K_BLOCK + 1
        lax.fori_loop(low_ref[row, index], last, step, 0)
        gq = acc[...].T * SCALE
        here = slice(index * Q_BLOCK, (index + 1) * Q_BLOCK)
        cosine, sine = cos_ref[here], sin_ref[here]
        for h in range(heads):
            part = gq[h * Q_BLOCK : (h + 1) * Q_BLOCK]
            gq_ref[0, here, h * HD : (h + 1) * HD] = to_bf(
                part * cosine + pltpu.roll(part * sine, HD // 2, 1)
            )
    is_key = core == 0
    keys, values = gk[...] * SCALE, gv[...]
    keep_ref[0] = to_bf(jnp.where(is_key, keys, values))
    send_ref[0] = to_bf(jnp.where(is_key, values, keys))


def attend_back(order, low, core, q, start, span, mate, grad, out, lse, cosine, sine):
    rows, local, columns = q.shape
    pieces = len(span)
    window = pieces * local
    heads = columns // HD
    blocks = local // Q_BLOCK

    def at(i, *refs):
        return (i, 0, 0)

    table = pl.BlockSpec((local, HD), lambda i, *refs: (i, 0))
    tokens = pl.BlockSpec((1, local, columns), at)
    return order(
        functools.partial(attend_back_kernel, heads, blocks, pieces),
        [q, start, grad, out, lse, cosine, sine, *span, *mate],
        [
            tokens,
            pl.BlockSpec((1, 1, local), at),
            tokens,
            tokens,
            pl.BlockSpec((1, blocks, heads * Q_BLOCK), at),
            table,
            table,
        ]
        + span_specs(rows, local, pieces),
        [tokens, pl.BlockSpec((1, window, HD), at), pl.BlockSpec((1, window, HD), at)],
        [
            jax.ShapeDtypeStruct((rows, local, columns), jnp.bfloat16),
            jax.ShapeDtypeStruct((rows, window, HD), jnp.bfloat16),
            jax.ShapeDtypeStruct((rows, window, HD), jnp.bfloat16),
        ],
        (rows,),
        20_000_000_000,
        6 * MIB,
        "attend_back",
        scalars=(low, core),
        scratch=[
            pltpu.VMEM((HD, heads * Q_BLOCK), jnp.float32),
            pltpu.VMEM((window, HD), jnp.float32),
            pltpu.VMEM((window, HD), jnp.float32),
            pltpu.VMEM((2, window, HD), jnp.bfloat16),
        ],
    )


def fold_kernel(keep_ref, come_ref, own_ref, *send_refs):
    local = own_ref.shape[1]
    total = to_f(keep_ref[0]) + to_f(come_ref[0])
    reach = total.shape[0] - local
    own_ref[0] = total[reach:]
    for hop, ref in enumerate(send_refs, 1):
        ref[0] = to_bf(total[reach - hop * local : reach - (hop - 1) * local])


def fold(order, keep, come, local):
    rows, window = keep.shape[:2]
    hops = window // local - 1
    out = pl.BlockSpec((1, local, HD), lambda i: (i, 0, 0))
    return order(
        fold_kernel,
        [keep, come],
        [
            pl.BlockSpec((1, window, HD), lambda i: (i, 0, 0)),
            pl.BlockSpec((1, window, HD), lambda i: (lax.rem(i + rows // 2, rows), 0, 0)),
        ],
        [out] * (hops + 1),
        [jax.ShapeDtypeStruct((rows, local, HD), jnp.float32)]
        + [jax.ShapeDtypeStruct((rows, local, HD), jnp.bfloat16)] * hops,
        (rows,),
        0,
        4 * MIB,
        "fold",
    )


def carry_kernel(piece_ref, come_ref, out_ref):
    out_ref[...] = to_bf(to_f(piece_ref[...]) + to_f(come_ref[...]))


def carry(order, piece, come):
    rows, local, columns = piece.shape
    at = pl.BlockSpec((1, local, columns), lambda i: (i, 0, 0))
    return order(
        carry_kernel,
        [piece, come],
        [at, at],
        [at],
        [jax.ShapeDtypeStruct(piece.shape, jnp.bfloat16)],
        (rows,),
        0,
        2 * MIB,
        "carry",
    )[0]


def bias_kernel(left_ref, right_ref, out_ref):
    out_ref[...] = left_ref[...] + right_ref[...]


def bias_add(order, left, right):
    whole = pl.BlockSpec(left.shape, lambda i: (0, 0))
    return order(
        bias_kernel,
        [left, right],
        [whole, whole],
        [whole],
        [jax.ShapeDtypeStruct(left.shape, jnp.float32)],
        (1,),
        0,
        MIB,
        "bias",
    )[0]


def join_kernel(hops, core_ref, gq_ref, cos_ref, sin_ref, own_ref, *refs):
    out_ref, sum_ref = refs[-2:]
    columns = gq_ref.shape[2]
    grad = own_ref[0]
    for ref in refs[:hops]:
        grad = grad + to_f(ref[0])
    is_key = core_ref[0] == 0
    cosine = jnp.where(is_key, cos_ref[...], 1.0)
    sine = jnp.where(is_key, sin_ref[...], 0.0)
    kv = to_bf(grad * cosine + pltpu.roll(grad * sine, HD // 2, 1))
    q = gq_ref[0]
    out_ref[:, :columns] = q
    out_ref[:, columns:] = kv

    @pl.when(pl.program_id(0) == 0)
    def _():
        sum_ref[...] = jnp.zeros(sum_ref.shape, jnp.float32)

    sum_ref[:, :columns] += jnp.sum(to_f(q), axis=0, keepdims=True)
    sum_ref[:, columns:] += jnp.sum(to_f(kv), axis=0, keepdims=True)


def join(order, core, grad_q, own, comes, cosine, sine):
    rows, local, columns = grad_q.shape
    wide = columns + HD

    def at(i, *refs):
        return (i, 0, 0)

    piece = pl.BlockSpec((1, local, HD), at)
    table = pl.BlockSpec((local, HD), lambda i, *refs: (i, 0))
    return order(
        functools.partial(join_kernel, len(comes)),
        [grad_q, cosine, sine, own, *comes],
        [pl.BlockSpec((1, local, columns), at), table, table, piece] + [piece] * len(comes),
        [
            pl.BlockSpec((local, wide), lambda i, *refs: (i, 0)),
            pl.BlockSpec((8, wide), lambda i, *refs: (0, 0)),
        ],
        [
            jax.ShapeDtypeStruct((rows * local, wide), jnp.bfloat16),
            jax.ShapeDtypeStruct((8, wide), jnp.float32),
        ],
        (rows,),
        0,
        4 * MIB,
        "join",
        scalars=(core,),
    )


def mixed_back_kernel(w_ref, *refs):
    rows = refs[0].shape[0]
    for i, ref in enumerate(refs[:-1]):
        refs[-1][i * rows : (i + 1) * rows] = to_bf(dot(ref[...], w_ref[...]))


def mixed_back(order, pieces, weight):
    rows, width = pieces[0].shape
    total = rows * len(pieces)
    columns = weight.shape[1]

    def whole(i):
        return (0, 0)

    return order(
        mixed_back_kernel,
        [weight, *pieces],
        [pl.BlockSpec((width, columns), whole)] + [pl.BlockSpec((rows, width), whole)] * len(pieces),
        [pl.BlockSpec((total, columns), whole)],
        [jax.ShapeDtypeStruct((total, columns), jnp.bfloat16)],
        (1,),
        2 * total * width * columns,
        6 * MIB,
        "mixed_back",
    )[0]


def place_kernel(core_ref, *refs):
    for i, ref in enumerate(refs[:-1]):

        @pl.when(pl.program_id(0) == i)
        def _(ref=ref):
            refs[-1][...] = ref[...]


def place(order, core, pieces):
    rows, width = pieces[0].shape
    count = len(pieces)
    return order(
        place_kernel,
        list(pieces),
        [pl.BlockSpec((rows, width), lambda i, core_ref: (0, 0))] * count,
        [pl.BlockSpec((rows, width), lambda i, core_ref: (lax.rem(i + core_ref[0] * (count // 2), count), 0))],
        [jax.ShapeDtypeStruct((rows * count, width), pieces[0].dtype)],
        (count,),
        0,
        8 * rows * width,
        "place",
        scalars=(core,),
    )[0]


def anchors(count):
    return [pl.BlockSpec(memory_space=pl.ANY)] * count


MARK = jax.ShapeDtypeStruct((8, HD), jnp.float32)


def mark_spec():
    return pl.BlockSpec((8, HD), lambda *refs: (0, 0))


def grad_hidden_kernel(g_ref, w_ref, out_ref):
    out_ref[...] = to_bf(dot(g_ref[...], w_ref[...], 1, 1))


def grad_hidden_of(order, grad, weight):
    total, width = grad.shape
    hidden = weight.shape[0]
    return order(
        grad_hidden_kernel,
        [grad, weight],
        [pl.BlockSpec((total, width), lambda i: (0, 0)), pl.BlockSpec((TILE, width), lambda i: (i, 0))],
        [pl.BlockSpec((total, TILE), lambda i: (0, i))],
        [jax.ShapeDtypeStruct((total, hidden), jnp.bfloat16)],
        (pl.cdiv(hidden, TILE),),
        2 * total * width * hidden,
        15 * MIB,
        "grad_hidden",
    )[0]


def gated_kernel(gh_ref, gw_ref, uw_ref, *refs):
    hid_ref, gg_ref, gu_ref = refs[-3:]
    rows = refs[0].shape[0]
    for part, ref in enumerate(refs[:-3]):
        here = slice(part * rows, (part + 1) * rows)
        h = ref[...]
        gate = dot(h, gw_ref[...], 1, 1)
        up = dot(h, uw_ref[...], 1, 1)
        grad = to_f(gh_ref[here])
        sigma = 1.0 / (1.0 + jnp.exp(-gate))
        swish = gate * sigma
        hid_ref[here] = to_bf(swish * up)
        gu_ref[here] = to_bf(grad * swish)
        gg_ref[here] = to_bf(grad * up * sigma * (1.0 + gate * (1.0 - sigma)))


def gated(order, pieces, grad_hidden, gate_weight, up_weight):
    rows, width = pieces[0].shape
    total = rows * len(pieces)
    hidden = gate_weight.shape[0]
    column = pl.BlockSpec((total, TILE), lambda i: (0, i))
    weight = pl.BlockSpec((TILE, width), lambda i: (i, 0))
    shape = jax.ShapeDtypeStruct((total, hidden), jnp.bfloat16)
    return order(
        gated_kernel,
        [grad_hidden, gate_weight, up_weight, *pieces],
        [column, weight, weight] + [pl.BlockSpec((rows, width), lambda i: (0, 0))] * len(pieces),
        [column] * 3,
        [shape] * 3,
        (pl.cdiv(hidden, TILE),),
        4 * total * width * hidden,
        30 * MIB,
        "gated",
    )


def share_kernel(plan, lefts, rights, extra, halves, groups, pick_ref, blocks_ref, *refs):
    step = pl.program_id(0)
    left_refs, right_refs = refs[:lefts], refs[lefts : lefts + rights]
    refs = refs[lefts + rights :]
    if extra:
        extra_ref, refs = refs[0], refs[1:]
    for left, right, begin, end, shift, columns, target in plan:

        @pl.when((step >= begin) & (step < end))
        def _(left=left, right=right, shift=shift, columns=columns, target=target):
            out = dot(left_refs[left][...], right_refs[right][...])
            if extra:
                out = out + to_f(extra_ref[...])
            tile = out.shape[1]
            spot = (step + shift) * tile + lax.broadcasted_iota(jnp.int32, (1, tile), 1)
            out = to_bf(jnp.where(spot < columns, out, 0.0))
            if groups:
                share = out.shape[0] // (groups[0] * groups[1])
                for i in range(groups[0]):
                    for j in range(groups[1]):
                        here = (j * groups[0] + i) * share
                        there = (i * groups[1] + j) * share
                        refs[target][here : here + share] = out[there : there + share]
                return
            if not halves:
                refs[target][...] = out
                return
            send_ref, keep_ref, rows = refs
            rows[...] = out
            share = send_ref.shape[0] // (2 * halves)
            for i in range(2 * halves):
                here = slice(i * share, (i + 1) * share)
                send_ref[here] = rows[pl.ds(pl.multiple_of(blocks_ref[i] * share, share), share)]
                keep_ref[here] = rows[pl.ds(pl.multiple_of(blocks_ref[2 * halves + i] * share, share), share)]


def clipped(rows, tile, begin, count, shift=0):
    return pl.BlockSpec((rows, tile), lambda i, *refs: (0, jnp.clip(i - begin, 0, count - 1) + shift))


def share_of(order, lefts, rights, parts, part, pick, tile, extra=None, blocks=None, groups=None):
    tokens = lefts[0].shape[1]
    plan, at = [], 0
    starts, sizes, right_at = {}, {}, {}
    for left, right, skip, count, target in parts:
        plan.append((left, right, at, at + count, skip - at, rights[right].shape[1], target))
        starts.setdefault(target, at)
        sizes[target] = sizes.get(target, 0) + count
        first, tiles, low = right_at.get(right, (at, 0, skip))
        right_at[right] = (first, tiles + count, low)
        at += count
    halves = 0
    extras = [] if extra is None else [extra]
    scratch = []
    if blocks is None:
        blocks = jnp.zeros((1,), jnp.int32)
        outs = [clipped(part, tile, starts[t], sizes[t]) for t in sorted(sizes)]
        shapes = [jax.ShapeDtypeStruct((part, sizes[t] * tile), jnp.bfloat16) for t in sorted(sizes)]
    else:
        halves = blocks.shape[0] // 4
        outs = [clipped(part // 2, tile, 0, at)] * 2
        shapes = [jax.ShapeDtypeStruct((part // 2, at * tile), jnp.bfloat16)] * 2
        scratch = [pltpu.VMEM((part, tile), jnp.bfloat16)]
    return order(
        functools.partial(share_kernel, plan, len(lefts), len(rights), len(extras), halves, groups),
        [*lefts, *rights, *extras],
        [pl.BlockSpec((part, tokens), lambda i, pick_ref, blocks_ref: (pick_ref[0], 0))] * len(lefts)
        + [clipped(tokens, tile, *right_at[r]) for r in range(len(rights))]
        + [clipped(part, tile, 0, at)] * len(extras),
        outs,
        shapes,
        (at,),
        2 * part * tokens * at * tile,
        2 * (part * tokens + (part + tokens) * at * tile),
        "share",
        scalars=(jnp.asarray(pick, jnp.int32).reshape(1), blocks),
        scratch=scratch,
    )


def relay_kernel(keep_ref, come_ref, out_ref):
    out_ref[...] = to_bf(to_f(keep_ref[...]) + to_f(come_ref[...]))


def relay(order, keep, come, share):
    rows, columns = keep.shape
    pair = pl.BlockSpec((share, columns), lambda i: (2 * i + 1, 0))
    return order(
        relay_kernel,
        [keep, come],
        [pair, pair],
        [pl.BlockSpec((share, columns), lambda i: (i, 0))],
        [jax.ShapeDtypeStruct((rows // 2, columns), jnp.bfloat16)],
        (rows // (2 * share),),
        0,
        3 * rows * columns,
        "relay",
    )[0]


def finish_kernel(plan, columns, gains, *refs):
    out_ref = refs[-2] if gains else refs[-1]
    step = pl.program_id(0)
    tile = out_ref.shape[1]
    for begin, end, first, count in plan:

        @pl.when((step >= begin) & (step < end))
        def _(first=first, count=count):
            out = to_f(refs[first][...])
            for ref in refs[first + 1 : first + count]:
                out = out + to_f(ref[...])
            out_ref[...] = out
            if gains:
                spot = step * tile + lax.broadcasted_iota(jnp.int32, (1, tile), 1)
                terms = jnp.where(spot < columns, out * to_f(refs[-3][...]), 0.0)
                total = terms[:, :HD]
                for i in range(HD, tile, HD):
                    total = total + terms[:, i : i + HD]

                @pl.when(step == 0)
                def _():
                    refs[-1][...] = total

                @pl.when(step > 0)
                def _():
                    refs[-1][...] += total


def finish(order, chunks, share, columns, tile, weight=None):
    plan, specs, args, at = [], [], [], 0
    for chunk in chunks:
        count = chunk[0].shape[1] // tile
        plan.append((at, at + count, len(args), len(chunk)))
        specs += [clipped(share, tile, at, count)] * len(chunk)
        args += chunk
        at += count
    column = pl.BlockSpec((share, tile), lambda i: (0, i))
    outs, shapes = [column], [jax.ShapeDtypeStruct((share, columns), jnp.float32)]
    if weight is not None:
        args.append(weight)
        specs.append(column)
        outs.append(pl.BlockSpec((share, HD), lambda i: (0, 0)))
        shapes.append(jax.ShapeDtypeStruct((share, HD), jnp.float32))
    return order(
        functools.partial(finish_kernel, plan, columns, weight is not None),
        args,
        specs,
        outs,
        shapes,
        (at,),
        0,
        14 * share * columns,
        "finish",
    )


def narrow_kernel(pairs, extras, right_dim, *refs):
    out = dot(refs[0][...], refs[1][...], 1, right_dim)
    for i in range(1, pairs):
        out = out + dot(refs[2 * i][...], refs[2 * i + 1][...], 1, right_dim)
    extra = refs[2 * pairs : 2 * pairs + extras]
    outs = refs[2 * pairs + extras :]
    if extras:
        out = out + jnp.concatenate([to_f(ref[...]) for ref in extra], axis=0)
    rows = outs[0].shape[0]
    for i, ref in enumerate(outs):
        ref[...] = to_bf(out[i * rows : (i + 1) * rows])


def narrow(order, pairs, index, extra=(), right_dim=0):
    total, hidden = pairs[0][0].shape
    width = pairs[0][1].shape[1 - right_dim]
    half = total // 2
    piece = half // PIECES
    column = pl.BlockSpec((piece, TILE), lambda i: (0, i))
    right = (
        pl.BlockSpec((TILE, hidden), lambda i: (i, 0))
        if right_dim
        else pl.BlockSpec((hidden, TILE), lambda i: (0, i))
    )
    return order(
        functools.partial(narrow_kernel, len(pairs), len(extra), right_dim),
        [item for pair in pairs for item in pair] + list(extra),
        [pl.BlockSpec((half, hidden), lambda i: (index, 0)), right] * len(pairs) + [column] * len(extra),
        [column] * PIECES,
        [jax.ShapeDtypeStruct((piece, width), jnp.bfloat16)] * PIECES,
        (width // TILE,),
        2 * len(pairs) * half * width * hidden,
        2 * len(pairs) * (half + width) * hidden + 2 * half * width,
        "narrow",
    )


def piece_specs(piece, width, block):
    steps = piece // block
    return [
        pl.BlockSpec((block, width), lambda i, *refs, j=j: (jnp.clip(i - j * steps, 0, steps - 1), 0))
        for j in range(PIECES)
    ]


def pick_piece(refs):
    value = refs[0][...]
    for j, ref in enumerate(refs[1:], 1):
        value = jnp.where(pl.program_id(0) >= 4 * j // len(refs), ref[...], value)
    return value


def put_piece(refs, value):
    steps = 4 // len(refs)
    for j, ref in enumerate(refs):

        @pl.when(lax.div(pl.program_id(0), steps) == j)
        def _(ref=ref):
            ref[...] = value


def turn_kernel(*refs):
    rows = refs[0].shape[0]
    for i, ref in enumerate(refs[:-1]):
        refs[-1][:, i * rows : (i + 1) * rows] = ref[...].T


def turn(order, pieces):
    rows, width = pieces[0].shape
    total = rows * len(pieces)
    return order(
        turn_kernel,
        list(pieces),
        [pl.BlockSpec((rows, TILE), lambda i: (0, i))] * len(pieces),
        [pl.BlockSpec((TILE, total), lambda i: (i, 0))],
        [jax.ShapeDtypeStruct((width, total), jnp.bfloat16)],
        (width // TILE,),
        0,
        4 * total * width,
        "turn",
    )[0]


def grad_out_kernel(core_ref, cot_ref, valid_ref, out_ref, turned_ref):
    out = to_bf(to_f(cot_ref[...]) * valid_ref[...])
    out_ref[...] = out
    turned_ref[...] = out.T


def grad_out_of(order, core, cotangent, valid):
    total, width = cotangent.shape
    block = total // 4
    return order(
        grad_out_kernel,
        [cotangent, valid],
        [
            pl.BlockSpec((block, width), lambda i, core_ref: (lax.rem(i + core_ref[0] * 2, 4), 0)),
            pl.BlockSpec((block, 1), lambda i, core_ref: (i, 0)),
        ],
        [
            pl.BlockSpec((block, width), lambda i, core_ref: (i, 0)),
            pl.BlockSpec((width, block), lambda i, core_ref: (0, i)),
        ],
        [
            jax.ShapeDtypeStruct((total, width), jnp.bfloat16),
            jax.ShapeDtypeStruct((width, total), jnp.bfloat16),
        ],
        (4,),
        0,
        6 * total * width,
        "grad_out",
        scalars=(core,),
    )


def middle_kernel(core_ref, tok_ref, gain_ref, *refs):
    mine, come = pick_piece(refs[:PIECES]), pick_piece(refs[PIECES : 2 * PIECES])
    mid_ref, *h_refs = refs[2 * PIECES :]
    middle = to_f(tok_ref[...]) + (to_f(mine) + to_f(come))
    factor = lax.rsqrt(jnp.mean(middle * middle, axis=-1, keepdims=True) + EPS)
    mid_ref[...] = middle
    put_piece(h_refs, to_bf(middle * factor * gain_ref[...]))


def middle_of(order, core, tokens, mine, come, gain):
    piece, width = mine[0].shape
    half = piece * PIECES
    block = half // 4
    specs = piece_specs(piece, width, block)
    middle, *h = order(
        middle_kernel,
        [tokens, gain, *mine, *come],
        [
            pl.BlockSpec((block, width), lambda i, core_ref: (core_ref[0] * 4 + i, 0)),
            pl.BlockSpec((1, width), lambda i, core_ref: (0, 0)),
        ]
        + specs * 2,
        [pl.BlockSpec((block, width), lambda i, core_ref: (i, 0))] + specs,
        [jax.ShapeDtypeStruct((half, width), jnp.float32)]
        + [jax.ShapeDtypeStruct((piece, width), jnp.bfloat16)] * PIECES,
        (4,),
        0,
        9 * MIB,
        "middle",
        scalars=(core,),
    )
    return middle, h


def norm_back_kernel(core_ref, x_ref, gain_ref, up_ref, *refs):
    mine, come = pick_piece(refs[:PIECES]), pick_piece(refs[PIECES : 2 * PIECES])
    outs = refs[2 * PIECES :]
    grad = to_f(mine) + to_f(come)
    x = to_f(x_ref[...])
    factor = lax.rsqrt(jnp.mean(x * x, axis=-1, keepdims=True) + EPS)
    normed = x * factor
    weighted = grad * gain_ref[...]
    inner = jnp.mean(weighted * normed, axis=-1, keepdims=True)
    out = to_f(up_ref[...]) + factor * (weighted - normed * inner)
    if len(outs) > PIECES:
        outs[0][...] = out
        put_piece(outs[1:], to_bf(out))
    else:
        put_piece(outs, out)


def norm_back(order, core, mine, come, x, gain, up, by_core):
    piece, width = mine[0].shape
    half = piece * PIECES
    block = half // 4
    at = pl.BlockSpec((block, width), lambda i, core_ref: (i, 0))
    picked = pl.BlockSpec((block, width), lambda i, core_ref: (core_ref[0] * 4 + i, 0))
    specs = piece_specs(piece, width, block)
    if by_core:
        shapes = [jax.ShapeDtypeStruct((piece, width), jnp.float32)] * PIECES
    else:
        shapes = [jax.ShapeDtypeStruct((half, width), jnp.float32)]
        shapes += [jax.ShapeDtypeStruct((piece, width), jnp.bfloat16)] * PIECES
    return order(
        norm_back_kernel,
        [x, gain, up, *mine, *come],
        [picked if by_core else at, pl.BlockSpec((1, width), lambda i, core_ref: (0, 0)), at] + specs * 2,
        specs if by_core else [at] + specs,
        shapes,
        (4,),
        0,
        10 * MIB,
        "norm_back",
        scalars=(core,),
    )


def layer_kernel(middle_ref, *refs):
    mine, come = pick_piece(refs[:PIECES]), pick_piece(refs[PIECES : 2 * PIECES])
    put_piece(refs[2 * PIECES :], to_bf(middle_ref[...] + (to_f(mine) + to_f(come))))


def layer_of(order, middle, mine, come):
    piece, width = mine[0].shape
    block = piece * PIECES // 4
    specs = piece_specs(piece, width, block)
    return order(
        layer_kernel,
        [middle, *mine, *come],
        [pl.BlockSpec((block, width), lambda i: (i, 0))] + specs * 2,
        specs,
        [jax.ShapeDtypeStruct((piece, width), jnp.bfloat16)] * PIECES,
        (4,),
        0,
        5 * MIB,
        "layer",
    )


def tensor_gather(value, rank):
    mate = core_swap(value)
    pair = jnp.where(lax.rem(rank, 2) == 0, jnp.stack([value, mate]), jnp.stack([mate, value]))
    come = chip_swap(pair)
    return jnp.where(
        lax.div(rank, 2) == 0,
        jnp.concatenate([pair, come], axis=0),
        jnp.concatenate([come, pair], axis=0),
    )


def body(
    tokens,
    lengths,
    cotangent,
    q_weight,
    q_bias,
    k_weight,
    k_bias,
    v_weight,
    v_bias,
    o_weight,
    attn_gain,
    ffn_gain,
    gate_weight,
    up_weight,
    down_weight,
):
    rows, local, width = tokens.shape
    total = rows * local
    half = total // 2
    heads = q_weight.shape[1] // HD
    ranks = lax.axis_size("tensor")
    seqs = lax.axis_size("seq")
    rank = lax.axis_index("tensor")
    dp_index = lax.axis_index("dp")
    seq_index = lax.axis_index("seq")
    core = lax.rem(rank, 2)
    head = lax.div(rank, 2)
    core_one = core.reshape(1)
    hops = min(seqs - 1, -(-(MOST - 1) // local))
    reach = hops * local

    def own_first(value):
        turned = jnp.concatenate([value[rows // 2 :], value[: rows // 2]], axis=0)
        return jnp.where(core == 0, value, turned)

    slots = jnp.arange(lengths.shape[1], dtype=jnp.int32)
    lens = own_first(lengths)
    ends = jnp.sum(jnp.where(slots[None, :] <= slots[:, None], lens[:, None, :], 0), axis=2)
    spot = seq_index * local + jnp.arange(local, dtype=jnp.int32)
    begun = jnp.max(
        jnp.where(ends[:, None, :] <= spot[None, :, None], ends[:, None, :], 0), axis=2
    )
    valid = to_f(spot[None, :] < ends[:, -2:-1])
    position = (spot[None, :] - begun).reshape(total, 1)
    freqs = ROPE_BASE ** (-(jnp.arange(HD // 2, dtype=jnp.float32) * 2.0) / HD)
    angles = to_f(position) * freqs[None, :]
    cosine, sine = jnp.cos(angles), jnp.sin(angles)
    cosine = jnp.concatenate([cosine, cosine], axis=1)
    sine = jnp.concatenate([-sine, sine], axis=1)
    start = begun - (seq_index * local - reach)
    low = jnp.maximum(lax.div(jnp.maximum(start[:, ::Q_BLOCK], 0), K_BLOCK), 0)
    start = start.reshape(rows, 1, local)

    key_side = core == 0
    kv_weight = jnp.where(
        key_side,
        lax.dynamic_slice_in_dim(k_weight, head * HD, HD, 1),
        lax.dynamic_slice_in_dim(v_weight, head * HD, HD, 1),
    )
    kv_bias = jnp.where(
        key_side,
        lax.dynamic_slice_in_dim(k_bias, head * HD, HD, 0),
        lax.dynamic_slice_in_dim(v_bias, head * HD, HD, 0),
    )
    weight = jnp.concatenate([q_weight, kv_weight], axis=1)
    bias = to_f(jnp.concatenate([q_bias, kv_bias])).reshape(1, -1)
    gain_one = to_f(attn_gain).reshape(1, width)
    gain_two = to_f(ffn_gain).reshape(1, width)

    h_one, q_rot, kv = first(
        core_one, tokens.reshape(total, width), gain_one, weight, bias, cosine, sine
    )
    kv = kv.reshape(rows, local, HD)
    span = [shifted(kv, h) for h in range(hops, 0, -1)] + [kv]
    mate = [core_swap(piece) for piece in span]
    q_rows = q_rot.reshape(rows, local, heads * HD)
    mixed_rows, lse = attend(low, core_one, q_rows, start, span, mate)
    mixed = mixed_rows.reshape(total, heads * HD)

    order = Order()
    flat_tokens = tokens.reshape(total, width)
    dps = lax.axis_size("dp")
    near_pair = dps == 2 and seqs == 4
    part = width // dps
    share = part // seqs
    gate_t, up_t, down_t = gate_weight.T, up_weight.T, down_weight.T
    units = gate_t.shape[0]
    tiles = -(-units // TILE)
    cut = (tiles + 1) // 2
    long = -(-2 * tiles // 3)
    one, two = seq_index ^ 1, seq_index ^ 2
    three = seq_index ^ 3
    quad = jnp.stack([one, three, seq_index, two])

    begin = (dp_index * seqs + seq_index) * share

    def rows_of(value):
        return lax.dynamic_slice_in_dim(value, begin, share, 0)

    class Rows:
        def __init__(self, lefts, rights, parts, tile=TILE, sent=None):
            self.args = (order, lefts, rights, parts)
            self.tile = tile
            if not near_pair:
                (whole,) = share_of(*self.args, width, 0, tile)
                self.whole = lax.psum_scatter(whole, ("dp", "seq"), scatter_dimension=0, tiled=True)
                return
            if sent is None:
                (sent,) = share_of(*self.args, part, 1 - dp_index, tile)
            self.come = lax.ppermute(sent, "dp", flipped("dp", 0))

        def own(self):
            if near_pair:
                send, self.keep = share_of(*self.args, part, dp_index, self.tile, self.come, quad)
                self.come = lax.ppermute(send, "seq", flipped("seq", 0))

        def relay(self):
            if near_pair:
                sent = relay(order, self.keep, self.come, share)
                self.last = lax.ppermute(sent, "seq", flipped("seq", 1))

        def settled(self):
            if near_pair:
                order.arrived(self.last)

        def result(self):
            return [self.keep, self.come, self.last] if near_pair else [self.whole]

    class SeqFirst(Rows):
        def __init__(self, lefts, rights, parts, tile=TILE):
            if not near_pair:
                super().__init__(lefts, rights, parts, tile)
                return
            (whole,) = share_of(order, lefts, rights, parts, width, 0, tile, None, None, (dps, seqs))
            self.mine = lax.psum_scatter(whole, "seq", scatter_dimension=0, tiled=True)

        def across(self):
            if near_pair:
                sent = lax.dynamic_slice_in_dim(self.mine, (1 - dp_index) * share, share, 0)
                self.mine = lax.dynamic_slice_in_dim(self.mine, dp_index * share, share, 0)
                self.come = lax.ppermute(sent, "dp", flipped("dp", 0))

        def settled(self):
            if near_pair:
                order.arrived(self.come)

        def result(self):
            return [self.mine, self.come] if near_pair else [self.whole]

    class Scattered(Rows):
        def own(self):
            if near_pair:
                (mine,) = share_of(*self.args, part, dp_index, self.tile, self.come)
                self.whole = lax.psum_scatter(mine, "seq", scatter_dimension=0, tiled=True)

        def settled(self):
            order.arrived(self.whole)

        def result(self):
            return [self.whole]

    sent = core_swaps(narrow(order, [(mixed, o_weight)], 1, (), 1))
    mine = narrow(order, [(mixed, o_weight)], 0, sent, 1)
    come = chip_swaps(mine)
    grad_ffn, grad_ffn_t = grad_out_of(
        order, core_one, cotangent.reshape(total, width), valid.reshape(total, 1)
    )
    gate_rows, up_rows = rows_of(gate_weight), rows_of(up_weight)
    order.arrived(gate_rows, up_rows)
    grad_hidden = grad_hidden_of(order, grad_ffn, down_t)
    h_one_t = turn(order, [h_one])
    middle, h_two = middle_of(order, core_one, flat_tokens, mine, come, gain_two)
    h_two += core_swaps(h_two)
    hidden, grad_gate, grad_up = gated(order, h_two, grad_hidden, gate_t, up_t)

    down_b = SeqFirst([grad_ffn_t], [hidden], [(0, 0, cut, tiles - cut, 0)])
    down_a = Rows([grad_ffn_t], [hidden], [(0, 0, 0, cut, 0)])
    pairs = [(grad_gate, gate_t), (grad_up, up_t)]
    sent = core_swaps(narrow(order, pairs, 1))
    mine = narrow(order, pairs, 0, sent)
    come = chip_swaps(mine)
    h_two_t = turn(order, h_two)
    if near_pair:
        sends = share_of(
            order,
            [h_two_t],
            [grad_gate, grad_up],
            [(0, 0, 0, tiles, 0), (0, 1, 0, long, 1), (0, 1, long, tiles - long, 2)],
            part,
            1 - dp_index,
            TILE,
        )
    else:
        sends = [None] * 3

    def half_rows(kind, right, begin, end, sent):
        return kind([h_two_t], [right], [(0, 0, begin, end - begin, 0)], TILE, sent)

    gate = half_rows(Scattered, grad_gate, 0, tiles, sends[0])
    up_a = half_rows(Rows, grad_up, 0, long, sends[1])
    up_b = half_rows(Rows, grad_up, long, tiles, sends[2])
    down_a.own()
    grad_middle, *branch = norm_back(order, core_one, mine, come, middle, gain_two, grad_ffn, False)
    branch += core_swaps(branch)
    grad_mixed = mixed_back(order, branch, o_weight).reshape(rows, local, heads * HD)
    grad_q_rows, keep, sent = attend_back(
        order, low, core_one, q_rows, start, span, mate, grad_mixed, mixed_rows, lse, cosine, sine
    )
    both_come = core_swap(sent)
    branch_t = turn(order, branch)
    own_kv, *pieces = fold(order, keep, both_come, local)
    moving = shifted(pieces[-1], -1) if pieces else None
    ffn_sent = core_swaps(narrow(order, [(hidden, down_t)], 1))
    for piece in pieces[-2::-1]:
        moving = shifted(carry(order, piece, moving), -1)
    grad_qkv, bias_sum = join(
        order, core_one, grad_q_rows, own_kv, [] if moving is None else [moving], cosine, sine
    )
    sent = core_swaps(narrow(order, [(grad_qkv, weight)], 1, (), 1))
    last_parts = [(0, 0, 0, grad_qkv.shape[1] // HD, 0), (1, 1, 0, heads, 0)]
    last = Rows([h_one_t, branch_t], [grad_qkv, mixed], last_parts, HD)
    mine = narrow(order, [(grad_qkv, weight)], 0, sent, 1)
    come = chip_swaps(mine)
    down_a.relay()
    gate.own()
    ffn_mine = narrow(order, [(hidden, down_t)], 0, ffn_sent)
    token = norm_back(order, core_one, mine, come, flat_tokens, gain_one, grad_middle, True)
    token += core_swaps(token)
    ffn_come = chip_swaps(ffn_mine)
    token_grad = place(order, core_one, token).reshape(rows, local, width)
    up_a.own()
    down_a.settled()
    layer = layer_of(order, middle, ffn_mine, ffn_come)
    layer += core_swaps(layer)
    down_b.across()
    last.own()
    layer_out = place(order, core_one, layer).reshape(rows, local, width)
    up_a.relay()
    down_b.settled()
    up_b.own()
    last.relay()
    (down_grad,) = finish(order, [down_a.result(), down_b.result()], share, units, TILE)
    if near_pair:
        bias_come = lax.ppermute(bias_sum, "dp", flipped("dp", 0))
        bias_all = bias_add(order, bias_sum, bias_come)
        bias_come = lax.ppermute(bias_all, "seq", flipped("seq", 0))
    up_b.relay()
    gate_grad, gate_term = finish(order, [gate.result()], share, units, TILE, gate_rows)
    wide_columns = grad_qkv.shape[1]
    (last_grad,) = finish(order, [last.result()], share, wide_columns + heads * HD, HD)
    if near_pair:
        bias_all = bias_add(order, bias_all, bias_come)
        bias_come = lax.ppermute(bias_all, "seq", flipped("seq", 1))
        bias_all = (bias_all + bias_come)[:1]
    else:
        bias_all = lax.psum(bias_sum[:1], ("dp", "seq"))
    up_grad, up_term = finish(order, [up_a.result(), up_b.result()], share, units, TILE, up_rows)
    qkv_grad, o_grad = last_grad[:, :wide_columns], last_grad[:, wide_columns:]

    attn_term = jnp.sum(to_f(rows_of(weight)) * qkv_grad, axis=1)
    ffn_term = jnp.sum(gate_term + up_term, axis=1)
    columns = heads * HD
    room = -(-share // HD) * HD - share
    terms = jnp.pad(jnp.stack([ffn_term, attn_term]), ((0, 0), (0, room))).reshape(-1, HD)
    packed = jnp.concatenate([qkv_grad[:, columns:], bias_all.reshape(-1, HD), terms], axis=0)
    gathered = tensor_gather(packed, rank)
    term_rows = terms.shape[0]
    bias_count = bias_all.shape[1] // HD
    terms = gathered[:, share + bias_count :].reshape(ranks, 2, -1)[:, :, :share]
    ffn_gain_grad, attn_gain_grad = terms[0] + terms[1] + (terms[2] + terms[3])
    attn_gain_grad = attn_gain_grad / lax.dynamic_slice_in_dim(gain_one[0], begin, share, 0)
    ffn_gain_grad = ffn_gain_grad / lax.dynamic_slice_in_dim(gain_two[0], begin, share, 0)
    q_grad = qkv_grad[:, :columns]
    kv_parts = lax.dynamic_slice_in_dim(gathered, rank * (share // ranks), share // ranks, 1)
    k_grad = jnp.concatenate([kv_parts[2 * i] for i in range(KVH)], axis=1)
    v_grad = jnp.concatenate([kv_parts[2 * i + 1] for i in range(KVH)], axis=1)
    biases = gathered[:, share : share + bias_count]
    q_bias_grad = biases[:, :heads].reshape(-1)
    k_bias_grad = biases[0::2, heads].reshape(-1)
    v_bias_grad = biases[1::2, heads].reshape(-1)
    return (
        layer_out,
        token_grad,
        q_grad,
        q_bias_grad,
        k_grad,
        k_bias_grad,
        v_grad,
        v_bias_grad,
        o_grad,
        attn_gain_grad,
        ffn_gain_grad,
        gate_grad,
        up_grad,
        down_grad,
    )


def solution(mesh):
    in_specs = (
        P("dp", "seq", None),
        P("dp", None),
        P("dp", "seq", None),
        P(None, "tensor"),
        P("tensor"),
        P(),
        P(),
        P(),
        P(),
        P(None, "tensor"),
        P(),
        P(),
        P(None, "tensor"),
        P(None, "tensor"),
        P(None, "tensor"),
    )
    out_specs = (
        P("dp", "seq", None),
        P("dp", "seq", None),
        P(("dp", "seq"), "tensor"),
        P(),
        P(("dp", "seq", "tensor"), None),
        P(),
        P(("dp", "seq", "tensor"), None),
        P(),
        P(("dp", "seq"), "tensor"),
        P(("dp", "seq")),
        P(("dp", "seq")),
        P(("dp", "seq"), "tensor"),
        P(("dp", "seq"), "tensor"),
        P(("dp", "seq"), "tensor"),
    )
    return jax.shard_map(body, mesh=mesh, in_specs=in_specs, out_specs=out_specs, check_vma=False)
```

```python
import functools
import math

import jax
import jax.numpy as jnp
from jax import lax
from jax.experimental import pallas as pl
from jax.experimental.pallas import tpu as pltpu
from jax.sharding import PartitionSpec as P

KVH = 2
HD = 128
MOST = 1024
EPS = 1e-06
ROPE_BASE = 10000.0
NEG_FILL = -1e30
Q_BLOCK = 256
K_BLOCK = 256
MIB = 1 << 20
LIGHT = 1000
TILE = 256
PIECES = 2
LARGE = MIB
SCALE = 1.0 / math.sqrt(HD)


def to_bf(value):
    return value.astype(jnp.bfloat16)


def to_f(value):
    return value.astype(jnp.float32)


def dot(left, right, left_dim=1, right_dim=0):
    return lax.dot_general(
        left,
        right,
        (((left_dim,), (right_dim,)), ((), ())),
        preferred_element_type=jnp.float32,
    )


def flipped(axis, bit):
    return [(i, i ^ (1 << bit)) for i in range(lax.axis_size(axis))]


def core_swap(value):
    return lax.ppermute(value, "tensor", flipped("tensor", 0))


def chip_swap(value):
    return lax.ppermute(value, "tensor", flipped("tensor", 1))


def core_swaps(values):
    return [core_swap(value) for value in values]


def chip_swaps(values):
    return [chip_swap(value) for value in values]


def shifted(value, hops):
    count = lax.axis_size("seq")
    route = [(i, i + hops) for i in range(count) if 0 <= i + hops < count]
    return lax.ppermute(value, "seq", route)


def cost(flops, read):
    return pl.CostEstimate(flops=flops // LIGHT, bytes_accessed=read // LIGHT, transcendentals=0)


def placed(shape):
    if math.prod(shape.shape) * shape.dtype.itemsize < LARGE:
        return shape
    return pltpu.HBM(shape.shape, shape.dtype)


class Order:
    def __init__(self):
        self.mark = None
        self.touched = []

    def arrived(self, *values):
        self.touched.extend(values)

    def __call__(self, kernel, args, in_specs, out_specs, out_shape, grid, flops, read, name, scalars=(), scratch=()):
        anchor = ([] if self.mark is None else [self.mark]) + self.touched
        self.touched = []
        count = len(scalars) + len(args)
        outs = len(out_shape)

        def run(*refs):
            rest = refs[count + len(anchor) :]
            kernel(*refs[:count], *rest[:outs], *rest[outs + 1 :])
            rest[outs][...] = jnp.zeros(rest[outs].shape, jnp.float32)

        *results, self.mark = pl.pallas_call(
            run,
            grid_spec=pltpu.PrefetchScalarGridSpec(
                num_scalar_prefetch=len(scalars),
                grid=grid,
                in_specs=list(in_specs) + anchors(len(anchor)),
                out_specs=list(out_specs) + [mark_spec()],
                scratch_shapes=list(scratch),
            ),
            out_shape=[placed(shape) for shape in out_shape] + [MARK],
            compiler_params=pltpu.CompilerParams(vmem_limit_bytes=32 * MIB),
            cost_estimate=cost(flops, read),
            name=name,
        )(*scalars, *args, *anchor)
        return results


def first_kernel(core_ref, tok_ref, gain_ref, w_ref, b_ref, cos_ref, sin_ref, h_ref, q_ref, kv_ref):
    x = to_f(tok_ref[...])
    factor = lax.rsqrt(jnp.mean(x * x, axis=-1, keepdims=True) + EPS)
    h = to_bf(x * factor * gain_ref[...])
    h_ref[...] = h
    lin = dot(h, w_ref[...]) + b_ref[...]
    cosine = cos_ref[...]
    sine = sin_ref[...]
    heads = q_ref.shape[1] // HD
    for head in range(heads):
        part = lin[:, head * HD : (head + 1) * HD]
        q_ref[:, head * HD : (head + 1) * HD] = to_bf(
            part * cosine + pltpu.roll(part, HD // 2, 1) * sine
        )
    part = lin[:, heads * HD :]
    is_key = core_ref[0] == 0
    kv_ref[...] = to_bf(
        part * jnp.where(is_key, cosine, 1.0)
        + pltpu.roll(part, HD // 2, 1) * jnp.where(is_key, sine, 0.0)
    )


def first(core, tokens, gain, weight, bias, cosine, sine):
    total, width = tokens.shape
    columns = weight.shape[1]
    block = total // 4
    half = 2

    def flip(i, core_ref):
        return (lax.rem(i + core_ref[0] * half, 4), 0)

    def at(i, core_ref):
        return (i, 0)

    def whole(i, core_ref):
        return (0, 0)

    return pl.pallas_call(
        first_kernel,
        grid_spec=pltpu.PrefetchScalarGridSpec(
            num_scalar_prefetch=1,
            grid=(4,),
            in_specs=[
                pl.BlockSpec((block, width), flip),
                pl.BlockSpec((1, width), whole),
                pl.BlockSpec((width, columns), whole),
                pl.BlockSpec((1, columns), whole),
                pl.BlockSpec((block, HD), at),
                pl.BlockSpec((block, HD), at),
            ],
            out_specs=[
                pl.BlockSpec((block, width), at),
                pl.BlockSpec((block, columns - HD), at),
                pl.BlockSpec((block, HD), at),
            ],
        ),
        out_shape=[
            jax.ShapeDtypeStruct((total, width), jnp.bfloat16),
            jax.ShapeDtypeStruct((total, columns - HD), jnp.bfloat16),
            jax.ShapeDtypeStruct((total, HD), jnp.bfloat16),
        ],
        compiler_params=pltpu.CompilerParams(vmem_limit_bytes=32 * MIB),
        cost_estimate=cost(2 * total * width * columns, 9 * MIB),
        name="first",
    )(core, tokens, gain, weight, bias, cosine, sine)


def stacked(ref, start, count, heads):
    return jnp.concatenate(
        [ref[0, pl.ds(start, count), h * HD : (h + 1) * HD] for h in range(heads)], axis=0
    )


def bounds(start_ref, index, heads, reach):
    first_key = jnp.concatenate(
        [start_ref[0, :, pl.ds(index * Q_BLOCK, Q_BLOCK)]] * heads, axis=1
    )
    place = reach + index * Q_BLOCK + lax.broadcasted_iota(jnp.int32, (1, Q_BLOCK), 1)
    return first_key, jnp.concatenate([place] * heads, axis=1)


def gather_span(core, refs, span):
    count = len(refs) // 2
    local = refs[0].shape[1]
    for i in range(count):
        here = slice(i * local, (i + 1) * local)
        span[core, here] = refs[i][0]
        span[1 - core, here] = refs[count + i][0]


def attend_kernel(heads, blocks, pieces, low_ref, core_ref, q_ref, start_ref, *refs):
    o_ref, lse_ref, acc, span = refs[2 * pieces :]
    row = pl.program_id(0)
    wide = heads * Q_BLOCK
    reach = (pieces - 1) * q_ref.shape[1]
    gather_span(core_ref[0], refs[: 2 * pieces], span)
    for index in range(blocks):
        q = stacked(q_ref, index * Q_BLOCK, Q_BLOCK, heads)
        first_key, place = bounds(start_ref, index, heads, reach)
        acc[...] = jnp.zeros_like(acc)

        def step(j, carry):
            top, total = carry
            keys = pl.ds(pl.multiple_of(j * K_BLOCK, K_BLOCK), K_BLOCK)
            s = dot(span[0, keys], q, 1, 1) * SCALE
            key = j * K_BLOCK + lax.broadcasted_iota(jnp.int32, (K_BLOCK, wide), 0)
            s = jnp.where((key >= first_key) & (key <= place), s, NEG_FILL)
            later = jnp.maximum(top, jnp.max(s, axis=0, keepdims=True))
            p = jnp.exp(s - later)
            fade = jnp.exp(top - later)
            total = total * fade + jnp.sum(p, axis=0, keepdims=True)
            acc[...] = acc[...] * fade + dot(span[1, keys], to_bf(p), 0, 0)
            return later, total

        last = (reach + (index + 1) * Q_BLOCK - 1) // K_BLOCK + 1
        top, total = lax.fori_loop(
            low_ref[row, index],
            last,
            step,
            (jnp.full((1, wide), NEG_FILL, jnp.float32), jnp.zeros((1, wide), jnp.float32)),
        )
        out = to_bf((acc[...] / total).T)
        for h in range(heads):
            o_ref[0, index * Q_BLOCK : (index + 1) * Q_BLOCK, h * HD : (h + 1) * HD] = out[
                h * Q_BLOCK : (h + 1) * Q_BLOCK
            ]
        lse_ref[0, index : index + 1, :] = top + jnp.log(total)


def span_specs(rows, local, pieces):
    near = pl.BlockSpec((1, local, HD), lambda i, *refs: (i, 0, 0))
    far = pl.BlockSpec((1, local, HD), lambda i, *refs: (lax.rem(i + rows // 2, rows), 0, 0))
    return [near] * pieces + [far] * pieces


def attend(order, low, core, q, start, span, mate):
    rows, local, columns = q.shape
    pieces = len(span)
    heads = columns // HD
    blocks = local // Q_BLOCK

    def at(i, *refs):
        return (i, 0, 0)

    return order(
        functools.partial(attend_kernel, heads, blocks, pieces),
        [q, start, *span, *mate],
        [pl.BlockSpec((1, local, columns), at), pl.BlockSpec((1, 1, local), at)]
        + span_specs(rows, local, pieces),
        [pl.BlockSpec((1, local, columns), at), pl.BlockSpec((1, blocks, heads * Q_BLOCK), at)],
        [
            jax.ShapeDtypeStruct((rows, local, columns), jnp.bfloat16),
            jax.ShapeDtypeStruct((rows, blocks, heads * Q_BLOCK), jnp.float32),
        ],
        (rows,),
        8_000_000_000,
        4 * MIB,
        "attend",
        scalars=(low, core),
        scratch=[
            pltpu.VMEM((HD, heads * Q_BLOCK), jnp.float32),
            pltpu.VMEM((2, pieces * local, HD), jnp.bfloat16),
        ],
    )


def attend_back_kernel(
    heads, blocks, pieces, low_ref, core_ref, q_ref, start_ref, g_ref, o_ref, lse_ref, cos_ref, sin_ref, *refs
):
    gq_ref, keep_ref, send_ref, acc, gk, gv, span = refs[2 * pieces :]
    row = pl.program_id(0)
    wide = heads * Q_BLOCK
    reach = (pieces - 1) * q_ref.shape[1]
    core = core_ref[0]
    gather_span(core, refs[: 2 * pieces], span)
    gk[...] = jnp.zeros_like(gk)
    gv[...] = jnp.zeros_like(gv)
    for index in range(blocks):
        q = stacked(q_ref, index * Q_BLOCK, Q_BLOCK, heads)
        g = stacked(g_ref, index * Q_BLOCK, Q_BLOCK, heads)
        o = stacked(o_ref, index * Q_BLOCK, Q_BLOCK, heads)
        inner = jnp.sum((to_f(g) * to_f(o)).T, axis=0, keepdims=True)
        lse = lse_ref[0, index : index + 1, :]
        first_key, place = bounds(start_ref, index, heads, reach)
        acc[...] = jnp.zeros_like(acc)

        def step(j, carry):
            keys = pl.ds(pl.multiple_of(j * K_BLOCK, K_BLOCK), K_BLOCK)
            k = span[0, keys]
            s = dot(k, q, 1, 1) * SCALE
            key = j * K_BLOCK + lax.broadcasted_iota(jnp.int32, (K_BLOCK, wide), 0)
            p = jnp.where((key >= first_key) & (key <= place), jnp.exp(s - lse), 0.0)
            gp = dot(span[1, keys], g, 1, 1)
            gs = to_bf(p * (gp - inner))
            gv[keys] += dot(to_bf(p), g)
            gk[keys] += dot(gs, q)
            acc[...] += dot(k, gs, 0, 0)
            return carry

        last = (reach + (index + 1) * Q_BLOCK - 1) // K_BLOCK + 1
        lax.fori_loop(low_ref[row, index], last, step, 0)
        gq = acc[...].T * SCALE
        here = slice(index * Q_BLOCK, (index + 1) * Q_BLOCK)
        cosine, sine = cos_ref[here], sin_ref[here]
        for h in range(heads):
            part = gq[h * Q_BLOCK : (h + 1) * Q_BLOCK]
            gq_ref[0, here, h * HD : (h + 1) * HD] = to_bf(
                part * cosine + pltpu.roll(part * sine, HD // 2, 1)
            )
    is_key = core == 0
    keys, values = gk[...] * SCALE, gv[...]
    keep_ref[0] = to_bf(jnp.where(is_key, keys, values))
    send_ref[0] = to_bf(jnp.where(is_key, values, keys))


def attend_back(order, low, core, q, start, span, mate, grad, out, lse, cosine, sine):
    rows, local, columns = q.shape
    pieces = len(span)
    window = pieces * local
    heads = columns // HD
    blocks = local // Q_BLOCK

    def at(i, *refs):
        return (i, 0, 0)

    table = pl.BlockSpec((local, HD), lambda i, *refs: (i, 0))
    tokens = pl.BlockSpec((1, local, columns), at)
    return order(
        functools.partial(attend_back_kernel, heads, blocks, pieces),
        [q, start, grad, out, lse, cosine, sine, *span, *mate],
        [
            tokens,
            pl.BlockSpec((1, 1, local), at),
            tokens,
            tokens,
            pl.BlockSpec((1, blocks, heads * Q_BLOCK), at),
            table,
            table,
        ]
        + span_specs(rows, local, pieces),
        [tokens, pl.BlockSpec((1, window, HD), at), pl.BlockSpec((1, window, HD), at)],
        [
            jax.ShapeDtypeStruct((rows, local, columns), jnp.bfloat16),
            jax.ShapeDtypeStruct((rows, window, HD), jnp.bfloat16),
            jax.ShapeDtypeStruct((rows, window, HD), jnp.bfloat16),
        ],
        (rows,),
        20_000_000_000,
        6 * MIB,
        "attend_back",
        scalars=(low, core),
        scratch=[
            pltpu.VMEM((HD, heads * Q_BLOCK), jnp.float32),
            pltpu.VMEM((window, HD), jnp.float32),
            pltpu.VMEM((window, HD), jnp.float32),
            pltpu.VMEM((2, window, HD), jnp.bfloat16),
        ],
    )


def fold_kernel(keep_ref, come_ref, own_ref, *send_refs):
    local = own_ref.shape[1]
    total = to_f(keep_ref[0]) + to_f(come_ref[0])
    reach = total.shape[0] - local
    own_ref[0] = total[reach:]
    for hop, ref in enumerate(send_refs, 1):
        ref[0] = to_bf(total[reach - hop * local : reach - (hop - 1) * local])


def fold(order, keep, come, local):
    rows, window = keep.shape[:2]
    hops = window // local - 1
    out = pl.BlockSpec((1, local, HD), lambda i: (i, 0, 0))
    return order(
        fold_kernel,
        [keep, come],
        [
            pl.BlockSpec((1, window, HD), lambda i: (i, 0, 0)),
            pl.BlockSpec((1, window, HD), lambda i: (lax.rem(i + rows // 2, rows), 0, 0)),
        ],
        [out] * (hops + 1),
        [jax.ShapeDtypeStruct((rows, local, HD), jnp.float32)]
        + [jax.ShapeDtypeStruct((rows, local, HD), jnp.bfloat16)] * hops,
        (rows,),
        0,
        4 * MIB,
        "fold",
    )


def carry_kernel(piece_ref, come_ref, out_ref):
    out_ref[...] = to_bf(to_f(piece_ref[...]) + to_f(come_ref[...]))


def carry(order, piece, come):
    rows, local, columns = piece.shape
    at = pl.BlockSpec((1, local, columns), lambda i: (i, 0, 0))
    return order(
        carry_kernel,
        [piece, come],
        [at, at],
        [at],
        [jax.ShapeDtypeStruct(piece.shape, jnp.bfloat16)],
        (rows,),
        0,
        2 * MIB,
        "carry",
    )[0]


def bias_kernel(left_ref, right_ref, out_ref):
    out_ref[...] = left_ref[...] + right_ref[...]


def bias_add(order, left, right):
    whole = pl.BlockSpec(left.shape, lambda i: (0, 0))
    return order(
        bias_kernel,
        [left, right],
        [whole, whole],
        [whole],
        [jax.ShapeDtypeStruct(left.shape, jnp.float32)],
        (1,),
        0,
        MIB,
        "bias",
    )[0]


def join_kernel(hops, core_ref, gq_ref, cos_ref, sin_ref, own_ref, *refs):
    out_ref, sum_ref = refs[-2:]
    columns = gq_ref.shape[2]
    grad = own_ref[0]
    for ref in refs[:hops]:
        grad = grad + to_f(ref[0])
    is_key = core_ref[0] == 0
    cosine = jnp.where(is_key, cos_ref[...], 1.0)
    sine = jnp.where(is_key, sin_ref[...], 0.0)
    kv = to_bf(grad * cosine + pltpu.roll(grad * sine, HD // 2, 1))
    q = gq_ref[0]
    out_ref[:, :columns] = q
    out_ref[:, columns:] = kv

    @pl.when(pl.program_id(0) == 0)
    def _():
        sum_ref[...] = jnp.zeros(sum_ref.shape, jnp.float32)

    sum_ref[:, :columns] += jnp.sum(to_f(q), axis=0, keepdims=True)
    sum_ref[:, columns:] += jnp.sum(to_f(kv), axis=0, keepdims=True)


def join(order, core, grad_q, own, comes, cosine, sine):
    rows, local, columns = grad_q.shape
    wide = columns + HD

    def at(i, *refs):
        return (i, 0, 0)

    piece = pl.BlockSpec((1, local, HD), at)
    table = pl.BlockSpec((local, HD), lambda i, *refs: (i, 0))
    return order(
        functools.partial(join_kernel, len(comes)),
        [grad_q, cosine, sine, own, *comes],
        [pl.BlockSpec((1, local, columns), at), table, table, piece] + [piece] * len(comes),
        [
            pl.BlockSpec((local, wide), lambda i, *refs: (i, 0)),
            pl.BlockSpec((8, wide), lambda i, *refs: (0, 0)),
        ],
        [
            jax.ShapeDtypeStruct((rows * local, wide), jnp.bfloat16),
            jax.ShapeDtypeStruct((8, wide), jnp.float32),
        ],
        (rows,),
        0,
        4 * MIB,
        "join",
        scalars=(core,),
    )


def mixed_back_kernel(w_ref, *refs):
    rows = refs[0].shape[0]
    for i, ref in enumerate(refs[:-1]):
        refs[-1][i * rows : (i + 1) * rows] = to_bf(dot(ref[...], w_ref[...]))


def mixed_back(order, pieces, weight):
    rows, width = pieces[0].shape
    total = rows * len(pieces)
    columns = weight.shape[1]

    def whole(i):
        return (0, 0)

    return order(
        mixed_back_kernel,
        [weight, *pieces],
        [pl.BlockSpec((width, columns), whole)] + [pl.BlockSpec((rows, width), whole)] * len(pieces),
        [pl.BlockSpec((total, columns), whole)],
        [jax.ShapeDtypeStruct((total, columns), jnp.bfloat16)],
        (1,),
        2 * total * width * columns,
        6 * MIB,
        "mixed_back",
    )[0]


def place_kernel(core_ref, *refs):
    for i, ref in enumerate(refs[:-1]):

        @pl.when(pl.program_id(0) == i)
        def _(ref=ref):
            refs[-1][...] = ref[...]


def place(order, core, pieces):
    rows, width = pieces[0].shape
    count = len(pieces)
    return order(
        place_kernel,
        list(pieces),
        [pl.BlockSpec((rows, width), lambda i, core_ref: (0, 0))] * count,
        [pl.BlockSpec((rows, width), lambda i, core_ref: (lax.rem(i + core_ref[0] * (count // 2), count), 0))],
        [jax.ShapeDtypeStruct((rows * count, width), pieces[0].dtype)],
        (count,),
        0,
        8 * rows * width,
        "place",
        scalars=(core,),
    )[0]


def anchors(count):
    return [pl.BlockSpec(memory_space=pl.ANY)] * count


MARK = jax.ShapeDtypeStruct((8, HD), jnp.float32)


def mark_spec():
    return pl.BlockSpec((8, HD), lambda *refs: (0, 0))


def grad_hidden_kernel(g_ref, w_ref, out_ref):
    out_ref[...] = to_bf(dot(g_ref[...], w_ref[...], 1, 1))


def grad_hidden_of(order, grad, weight):
    total, width = grad.shape
    hidden = weight.shape[0]
    return order(
        grad_hidden_kernel,
        [grad, weight],
        [pl.BlockSpec((total, width), lambda i: (0, 0)), pl.BlockSpec((TILE, width), lambda i: (i, 0))],
        [pl.BlockSpec((total, TILE), lambda i: (0, i))],
        [jax.ShapeDtypeStruct((total, hidden), jnp.bfloat16)],
        (pl.cdiv(hidden, TILE),),
        2 * total * width * hidden,
        15 * MIB,
        "grad_hidden",
    )[0]


def gated_kernel(gh_ref, gw_ref, uw_ref, *refs):
    hid_ref, gg_ref, gu_ref = refs[-3:]
    for here in (slice(0, hid_ref.shape[0]),):
        h = jnp.concatenate([ref[...] for ref in refs[:-3]], axis=0)
        gate = dot(h, gw_ref[...], 1, 1)
        up = dot(h, uw_ref[...], 1, 1)
        grad = to_f(gh_ref[here])
        sigma = 1.0 / (1.0 + jnp.exp(-gate))
        swish = gate * sigma
        hid_ref[here] = to_bf(swish * up)
        gu_ref[here] = to_bf(grad * swish)
        gg_ref[here] = to_bf(grad * up * sigma * (1.0 + gate * (1.0 - sigma)))


def gated(order, pieces, grad_hidden, index, gate_weight, up_weight):
    rows, width = pieces[0].shape
    total = rows * len(pieces)
    hidden = gate_weight.shape[0]
    column = pl.BlockSpec((total, TILE), lambda i: (0, i))
    weight = pl.BlockSpec((TILE, width), lambda i: (i, 0))
    shape = jax.ShapeDtypeStruct((total, hidden), jnp.bfloat16)
    return order(
        gated_kernel,
        [grad_hidden, gate_weight, up_weight, *pieces],
        [pl.BlockSpec((total, TILE), lambda i: (index, i)), weight, weight]
        + [pl.BlockSpec((rows, width), lambda i: (0, 0))] * len(pieces),
        [column] * 3,
        [shape] * 3,
        (pl.cdiv(hidden, TILE),),
        4 * total * width * hidden,
        30 * MIB,
        "gated",
    )


def share_kernel(plan, lefts, rights, extra, halves, groups, pick_ref, blocks_ref, *refs):
    step = pl.program_id(0)
    left_refs, refs = refs[:lefts], refs[lefts:]
    right_refs = []
    for count in rights:
        right_refs.append(refs[:count])
        refs = refs[count:]
    if extra:
        extra_ref, refs = refs[0], refs[1:]
    for left, right, begin, end, shift, columns, target in plan:

        @pl.when((step >= begin) & (step < end))
        def _(left=left, right=right, shift=shift, columns=columns, target=target):
            out = dot(
                left_refs[left][...], jnp.concatenate([ref[...] for ref in right_refs[right]], axis=0)
            )
            if extra:
                out = out + to_f(extra_ref[...])
            tile = out.shape[1]
            spot = (step + shift) * tile + lax.broadcasted_iota(jnp.int32, (1, tile), 1)
            out = to_bf(jnp.where(spot < columns, out, 0.0))
            if groups:
                share = out.shape[0] // (groups[0] * groups[1])
                for i in range(groups[0]):
                    for j in range(groups[1]):
                        here = (j * groups[0] + i) * share
                        there = (i * groups[1] + j) * share
                        refs[target][here : here + share] = out[there : there + share]
                return
            if not halves:
                refs[target][...] = out
                return
            send_ref, keep_ref, rows = refs
            rows[...] = out
            share = send_ref.shape[0] // (2 * halves)
            for i in range(2 * halves):
                here = slice(i * share, (i + 1) * share)
                send_ref[here] = rows[pl.ds(pl.multiple_of(blocks_ref[i] * share, share), share)]
                keep_ref[here] = rows[pl.ds(pl.multiple_of(blocks_ref[2 * halves + i] * share, share), share)]


def clipped(rows, tile, begin, count, shift=0):
    return pl.BlockSpec((rows, tile), lambda i, *refs: (0, jnp.clip(i - begin, 0, count - 1) + shift))


def share_of(order, lefts, rights, parts, part, pick, tile, extra=None, blocks=None, groups=None):
    tokens = lefts[0].shape[1]
    plan, at = [], 0
    starts, sizes, right_at = {}, {}, {}
    for left, right, skip, count, target in parts:
        plan.append((left, right, at, at + count, skip - at, rights[right][0].shape[1], target))
        starts.setdefault(target, at)
        sizes[target] = sizes.get(target, 0) + count
        first, tiles, low = right_at.get(right, (at, 0, skip))
        right_at[right] = (first, tiles + count, low)
        at += count
    halves = 0
    extras = [] if extra is None else [extra]
    scratch = []
    if blocks is None:
        blocks = jnp.zeros((1,), jnp.int32)
        outs = [clipped(part, tile, starts[t], sizes[t]) for t in sorted(sizes)]
        shapes = [jax.ShapeDtypeStruct((part, sizes[t] * tile), jnp.bfloat16) for t in sorted(sizes)]
    else:
        halves = blocks.shape[0] // 4
        outs = [clipped(part // 2, tile, 0, at)] * 2
        shapes = [jax.ShapeDtypeStruct((part // 2, at * tile), jnp.bfloat16)] * 2
        scratch = [pltpu.VMEM((part, tile), jnp.bfloat16)]
    return order(
        functools.partial(share_kernel, plan, len(lefts), [len(r) for r in rights], len(extras), halves, groups),
        [*lefts, *[block for right in rights for block in right], *extras],
        [pl.BlockSpec((part, tokens), lambda i, pick_ref, blocks_ref: (pick_ref[0], 0))] * len(lefts)
        + [clipped(block.shape[0], tile, *right_at[r]) for r, right in enumerate(rights) for block in right]
        + [clipped(part, tile, 0, at)] * len(extras),
        outs,
        shapes,
        (at,),
        2 * part * tokens * at * tile,
        2 * (part * tokens + (part + tokens) * at * tile),
        "share",
        scalars=(jnp.asarray(pick, jnp.int32).reshape(1), blocks),
        scratch=scratch,
    )


def relay_kernel(keep_ref, come_ref, out_ref):
    out_ref[...] = to_bf(to_f(keep_ref[...]) + to_f(come_ref[...]))


def relay(order, keep, come, share):
    rows, columns = keep.shape
    pair = pl.BlockSpec((share, columns), lambda i: (2 * i + 1, 0))
    return order(
        relay_kernel,
        [keep, come],
        [pair, pair],
        [pl.BlockSpec((share, columns), lambda i: (i, 0))],
        [jax.ShapeDtypeStruct((rows // 2, columns), jnp.bfloat16)],
        (rows // (2 * share),),
        0,
        3 * rows * columns,
        "relay",
    )[0]


def finish_kernel(plan, columns, gains, *refs):
    out_ref = refs[-2] if gains else refs[-1]
    step = pl.program_id(0)
    tile = out_ref.shape[1]
    for begin, end, first, count in plan:

        @pl.when((step >= begin) & (step < end))
        def _(first=first, count=count):
            out = to_f(refs[first][...])
            for ref in refs[first + 1 : first + count]:
                out = out + to_f(ref[...])
            out_ref[...] = out
            if gains:
                spot = step * tile + lax.broadcasted_iota(jnp.int32, (1, tile), 1)
                terms = jnp.where(spot < columns, out * to_f(refs[-3][...]), 0.0)
                total = terms[:, :HD]
                for i in range(HD, tile, HD):
                    total = total + terms[:, i : i + HD]

                @pl.when(step == 0)
                def _():
                    refs[-1][...] = total

                @pl.when(step > 0)
                def _():
                    refs[-1][...] += total


def finish(order, chunks, share, columns, tile, weight=None):
    plan, specs, args, at = [], [], [], 0
    for chunk in chunks:
        count = chunk[0].shape[1] // tile
        plan.append((at, at + count, len(args), len(chunk)))
        specs += [clipped(share, tile, at, count)] * len(chunk)
        args += chunk
        at += count
    column = pl.BlockSpec((share, tile), lambda i: (0, i))
    outs, shapes = [column], [jax.ShapeDtypeStruct((share, columns), jnp.float32)]
    if weight is not None:
        args.append(weight)
        specs.append(column)
        outs.append(pl.BlockSpec((share, HD), lambda i: (0, 0)))
        shapes.append(jax.ShapeDtypeStruct((share, HD), jnp.float32))
    return order(
        functools.partial(finish_kernel, plan, columns, weight is not None),
        args,
        specs,
        outs,
        shapes,
        (at,),
        0,
        14 * share * columns,
        "finish",
    )


def narrow_kernel(pairs, extras, right_dim, *refs):
    out = 0.0
    for i in range(pairs):
        left = jnp.concatenate([ref[...] for ref in refs[:PIECES]], axis=0)
        out = out + dot(left, refs[PIECES][...], 1, right_dim)
        refs = refs[PIECES + 1 :]
    outs = refs[extras:]
    if extras:
        out = out + jnp.concatenate([to_f(ref[...]) for ref in refs[:extras]], axis=0)
    rows = outs[0].shape[0]
    for i, ref in enumerate(outs):
        ref[...] = to_bf(out[i * rows : (i + 1) * rows])


def narrow(order, pairs, extra=(), right_dim=0):
    piece = pairs[0][0][0][1]
    hidden = pairs[0][0][0][0].shape[1]
    width = pairs[0][1].shape[1 - right_dim]
    half = piece * PIECES
    column = pl.BlockSpec((piece, TILE), lambda i: (0, i))
    right = (
        pl.BlockSpec((TILE, hidden), lambda i: (i, 0))
        if right_dim
        else pl.BlockSpec((hidden, TILE), lambda i: (0, i))
    )
    args, specs = [], []
    for lefts, weight in pairs:
        for array, rows, index in lefts:
            args.append(array)
            specs.append(pl.BlockSpec((rows, hidden), lambda i, index=index: (index, 0)))
        args.append(weight)
        specs.append(right)
    return order(
        functools.partial(narrow_kernel, len(pairs), len(extra), right_dim),
        args + list(extra),
        specs + [column] * len(extra),
        [column] * PIECES,
        [jax.ShapeDtypeStruct((piece, width), jnp.bfloat16)] * PIECES,
        (width // TILE,),
        2 * len(pairs) * half * width * hidden,
        2 * len(pairs) * (half + width) * hidden + 2 * half * width,
        "narrow",
    )


def half_of(array, index):
    rows = array.shape[0] // (2 * PIECES)
    return [(array, rows, index * PIECES + j) for j in range(PIECES)]


def sides_of(arrays, index):
    return [(array, array.shape[0] // 2, index) for array in arrays]


def piece_specs(piece, width, block):
    steps = piece // block
    return [
        pl.BlockSpec((block, width), lambda i, *refs, j=j: (jnp.clip(i - j * steps, 0, steps - 1), 0))
        for j in range(PIECES)
    ]


def pick_piece(refs):
    value = refs[0][...]
    for j, ref in enumerate(refs[1:], 1):
        value = jnp.where(pl.program_id(0) >= 4 * j // len(refs), ref[...], value)
    return value


def put_piece(refs, value):
    steps = 4 // len(refs)
    for j, ref in enumerate(refs):

        @pl.when(lax.div(pl.program_id(0), steps) == j)
        def _(ref=ref):
            ref[...] = value


def turn_kernel(*refs):
    rows = refs[0].shape[0]
    for i, ref in enumerate(refs[:-1]):
        refs[-1][:, i * rows : (i + 1) * rows] = ref[...].T


def turn(order, pieces):
    rows, width = pieces[0].shape
    total = rows * len(pieces)
    return order(
        turn_kernel,
        list(pieces),
        [pl.BlockSpec((rows, TILE), lambda i: (0, i))] * len(pieces),
        [pl.BlockSpec((TILE, total), lambda i: (i, 0))],
        [jax.ShapeDtypeStruct((width, total), jnp.bfloat16)],
        (width // TILE,),
        0,
        4 * total * width,
        "turn",
    )[0]


def grad_out_kernel(core_ref, cot_ref, valid_ref, out_ref, turned_ref):
    out = to_bf(to_f(cot_ref[...]) * valid_ref[...])
    out_ref[...] = out
    turned_ref[...] = out.T


def grad_out_of(order, core, cotangent, valid):
    total, width = cotangent.shape
    block = total // 4
    return order(
        grad_out_kernel,
        [cotangent, valid],
        [
            pl.BlockSpec(
                (block, width),
                lambda i, core_ref: (lax.rem(i + core_ref[0], 2) * 2 + lax.div(i, 2), 0),
            ),
            pl.BlockSpec((block, 1), lambda i, core_ref: (lax.rem(i, 2) * 2 + lax.div(i, 2), 0)),
        ],
        [
            pl.BlockSpec((block, width), lambda i, core_ref: (i, 0)),
            pl.BlockSpec((width, block), lambda i, core_ref: (0, i)),
        ],
        [
            jax.ShapeDtypeStruct((total, width), jnp.bfloat16),
            jax.ShapeDtypeStruct((width, total), jnp.bfloat16),
        ],
        (4,),
        0,
        6 * total * width,
        "grad_out",
        scalars=(core,),
    )


def middle_kernel(core_ref, tok_ref, gain_ref, mine_ref, come_ref, mid_ref, *h_refs):
    middle = to_f(tok_ref[...]) + (to_f(mine_ref[...]) + to_f(come_ref[...]))
    factor = lax.rsqrt(jnp.mean(middle * middle, axis=-1, keepdims=True) + EPS)
    mid_ref[...] = middle
    h = to_bf(middle * factor * gain_ref[...])
    for i, ref in enumerate(h_refs):

        @pl.when(pl.program_id(0) == i)
        def _(ref=ref):
            ref[...] = h


def middle_of(order, core, tokens, mine, come, gain, index):
    piece, width = mine.shape
    block = piece // 2
    at = pl.BlockSpec((block, width), lambda i, core_ref: (i, 0))
    return order(
        middle_kernel,
        [tokens, gain, mine, come],
        [
            pl.BlockSpec((block, width), lambda i, core_ref: ((core_ref[0] * PIECES + index) * 2 + i, 0)),
            pl.BlockSpec((1, width), lambda i, core_ref: (0, 0)),
            at,
            at,
        ],
        [at] + [pl.BlockSpec((block, width), lambda i, core_ref: (0, 0))] * 2,
        [jax.ShapeDtypeStruct((piece, width), jnp.float32)]
        + [jax.ShapeDtypeStruct((block, width), jnp.bfloat16)] * 2,
        (2,),
        0,
        5 * MIB,
        "middle",
        scalars=(core,),
    )


def norm_back_kernel(last, core_ref, gain_ref, up_ref, *refs):
    xs = 1 if last else PIECES
    x, refs = to_f(pick_piece(refs[:xs])), refs[xs:]
    mine, come = pick_piece(refs[:PIECES]), pick_piece(refs[PIECES : 2 * PIECES])
    outs = refs[2 * PIECES :]
    grad = to_f(mine) + to_f(come)
    factor = lax.rsqrt(jnp.mean(x * x, axis=-1, keepdims=True) + EPS)
    normed = x * factor
    weighted = grad * gain_ref[...]
    inner = jnp.mean(weighted * normed, axis=-1, keepdims=True)
    out = to_f(up_ref[...]) + factor * (weighted - normed * inner)
    if last:
        put_piece(outs, out)
    else:
        outs[0][...] = out
        put_piece(outs[1:], to_bf(out))


def norm_back(order, core, mine, come, x, gain, up, last):
    piece, width = mine[0].shape
    half = piece * PIECES
    block = half // 4
    at = pl.BlockSpec((block, width), lambda i, core_ref: (i, 0))
    gain_at = pl.BlockSpec((1, width), lambda i, core_ref: (0, 0))
    specs = piece_specs(piece, width, block)
    steps = piece // block
    if last:
        args = [gain, up, x]
        front = [gain_at, at, pl.BlockSpec((block, width), lambda i, core_ref: (core_ref[0] * 4 + i, 0))]
        shapes = [jax.ShapeDtypeStruct((piece, width), jnp.float32)] * PIECES
    else:
        args = [gain, up, *x]
        between = pl.BlockSpec((block, width), lambda i, core_ref: (i + lax.div(i, steps) * steps, 0))
        front = [gain_at, between] + specs
        shapes = [jax.ShapeDtypeStruct((half, width), jnp.float32)]
        shapes += [jax.ShapeDtypeStruct((piece, width), jnp.bfloat16)] * PIECES
    return order(
        functools.partial(norm_back_kernel, last),
        [*args, *mine, *come],
        front + specs * 2,
        specs if last else [at] + specs,
        shapes,
        (4,),
        0,
        10 * MIB,
        "norm_back",
        scalars=(core,),
    )


def layer_kernel(*refs):
    middle, mine, come = (pick_piece(refs[i * PIECES : (i + 1) * PIECES]) for i in range(3))
    put_piece(refs[3 * PIECES :], to_bf(middle + (to_f(mine) + to_f(come))))


def layer_of(order, middle, mine, come):
    piece, width = mine[0].shape
    block = piece * PIECES // 4
    specs = piece_specs(piece, width, block)
    return order(
        layer_kernel,
        [*middle, *mine, *come],
        specs * 3,
        specs,
        [jax.ShapeDtypeStruct((piece, width), jnp.bfloat16)] * PIECES,
        (4,),
        0,
        5 * MIB,
        "layer",
    )


def tensor_gather(value, rank):
    mate = core_swap(value)
    pair = jnp.where(lax.rem(rank, 2) == 0, jnp.stack([value, mate]), jnp.stack([mate, value]))
    come = chip_swap(pair)
    return jnp.where(
        lax.div(rank, 2) == 0,
        jnp.concatenate([pair, come], axis=0),
        jnp.concatenate([come, pair], axis=0),
    )


def body(
    tokens,
    lengths,
    cotangent,
    q_weight,
    q_bias,
    k_weight,
    k_bias,
    v_weight,
    v_bias,
    o_weight,
    attn_gain,
    ffn_gain,
    gate_weight,
    up_weight,
    down_weight,
):
    rows, local, width = tokens.shape
    total = rows * local
    half = total // 2
    heads = q_weight.shape[1] // HD
    ranks = lax.axis_size("tensor")
    seqs = lax.axis_size("seq")
    rank = lax.axis_index("tensor")
    dp_index = lax.axis_index("dp")
    seq_index = lax.axis_index("seq")
    core = lax.rem(rank, 2)
    head = lax.div(rank, 2)
    core_one = core.reshape(1)
    hops = min(seqs - 1, -(-(MOST - 1) // local))
    reach = hops * local

    def own_first(value):
        turned = jnp.concatenate([value[rows // 2 :], value[: rows // 2]], axis=0)
        return jnp.where(core == 0, value, turned)

    slots = jnp.arange(lengths.shape[1], dtype=jnp.int32)
    lens = own_first(lengths)
    ends = jnp.sum(jnp.where(slots[None, :] <= slots[:, None], lens[:, None, :], 0), axis=2)
    spot = seq_index * local + jnp.arange(local, dtype=jnp.int32)
    begun = jnp.max(
        jnp.where(ends[:, None, :] <= spot[None, :, None], ends[:, None, :], 0), axis=2
    )
    valid = to_f(spot[None, :] < ends[:, -2:-1])
    position = (spot[None, :] - begun).reshape(total, 1)
    freqs = ROPE_BASE ** (-(jnp.arange(HD // 2, dtype=jnp.float32) * 2.0) / HD)
    angles = to_f(position) * freqs[None, :]
    cosine, sine = jnp.cos(angles), jnp.sin(angles)
    cosine = jnp.concatenate([cosine, cosine], axis=1)
    sine = jnp.concatenate([-sine, sine], axis=1)
    start = begun - (seq_index * local - reach)
    low = jnp.maximum(lax.div(jnp.maximum(start[:, ::Q_BLOCK], 0), K_BLOCK), 0)
    start = start.reshape(rows, 1, local)

    key_side = core == 0
    kv_weight = jnp.where(
        key_side,
        lax.dynamic_slice_in_dim(k_weight, head * HD, HD, 1),
        lax.dynamic_slice_in_dim(v_weight, head * HD, HD, 1),
    )
    kv_bias = jnp.where(
        key_side,
        lax.dynamic_slice_in_dim(k_bias, head * HD, HD, 0),
        lax.dynamic_slice_in_dim(v_bias, head * HD, HD, 0),
    )
    weight = jnp.concatenate([q_weight, kv_weight], axis=1)
    bias = to_f(jnp.concatenate([q_bias, kv_bias])).reshape(1, -1)
    gain_one = to_f(attn_gain).reshape(1, width)
    gain_two = to_f(ffn_gain).reshape(1, width)

    h_one, q_rot, kv = first(
        core_one, tokens.reshape(total, width), gain_one, weight, bias, cosine, sine
    )
    kv = kv.reshape(rows, local, HD)
    span = [shifted(kv, h) for h in range(hops, 0, -1)] + [kv]
    mate = [core_swap(piece) for piece in span]
    q_rows = q_rot.reshape(rows, local, heads * HD)
    order = Order()
    flat_tokens = tokens.reshape(total, width)
    dps = lax.axis_size("dp")
    near_pair = dps == 2 and seqs == 4
    part = width // dps
    share = part // seqs
    gate_t, up_t, down_t = gate_weight.T, up_weight.T, down_weight.T
    units = gate_t.shape[0]
    tiles = -(-units // TILE)
    cut = (tiles + 1) // 2
    long = -(-2 * tiles // 3)
    one, two = seq_index ^ 1, seq_index ^ 2
    three = seq_index ^ 3
    quad = jnp.stack([one, three, seq_index, two])

    begin = (dp_index * seqs + seq_index) * share

    def rows_of(value):
        return lax.dynamic_slice_in_dim(value, begin, share, 0)

    class Rows:
        def __init__(self, lefts, rights, parts, tile=TILE, sent=None):
            self.args = (order, lefts, rights, parts)
            self.tile = tile
            if not near_pair:
                (whole,) = share_of(*self.args, width, 0, tile)
                self.whole = lax.psum_scatter(whole, ("dp", "seq"), scatter_dimension=0, tiled=True)
                return
            if sent is None:
                (sent,) = share_of(*self.args, part, 1 - dp_index, tile)
            self.come = lax.ppermute(sent, "dp", flipped("dp", 0))

        def own(self):
            if near_pair:
                send, self.keep = share_of(*self.args, part, dp_index, self.tile, self.come, quad)
                self.come = lax.ppermute(send, "seq", flipped("seq", 0))

        def relay(self):
            if near_pair:
                sent = relay(order, self.keep, self.come, share)
                self.last = lax.ppermute(sent, "seq", flipped("seq", 1))

        def settled(self):
            if near_pair:
                order.arrived(self.last)

        def result(self):
            return [self.keep, self.come, self.last] if near_pair else [self.whole]

    class SeqFirst(Rows):
        def __init__(self, lefts, rights, parts, tile=TILE):
            if not near_pair:
                super().__init__(lefts, rights, parts, tile)
                return
            (whole,) = share_of(order, lefts, rights, parts, width, 0, tile, None, None, (dps, seqs))
            self.mine = lax.psum_scatter(whole, "seq", scatter_dimension=0, tiled=True)

        def across(self):
            if near_pair:
                sent = lax.dynamic_slice_in_dim(self.mine, (1 - dp_index) * share, share, 0)
                self.mine = lax.dynamic_slice_in_dim(self.mine, dp_index * share, share, 0)
                self.come = lax.ppermute(sent, "dp", flipped("dp", 0))

        def settled(self):
            if near_pair:
                order.arrived(self.come)

        def result(self):
            return [self.mine, self.come] if near_pair else [self.whole]

    class Scattered(Rows):
        def own(self):
            if near_pair:
                (mine,) = share_of(*self.args, part, dp_index, self.tile, self.come)
                self.whole = lax.psum_scatter(mine, "seq", scatter_dimension=0, tiled=True)

        def settled(self):
            order.arrived(self.whole)

        def result(self):
            return [self.whole]

    gate_rows, up_rows = rows_of(gate_weight), rows_of(up_weight)
    order.arrived(kv)
    grad_ffn, grad_ffn_t = grad_out_of(
        order, core_one, cotangent.reshape(total, width), valid.reshape(total, 1)
    )
    grad_hidden = grad_hidden_of(order, grad_ffn, down_t)
    h_one_t = turn(order, [h_one])
    mixed_rows, lse = attend(order, low, core_one, q_rows, start, span, mate)
    mixed = mixed_rows.reshape(total, heads * HD)
    sent = core_swaps(narrow(order, [(half_of(mixed, 1), o_weight)], (), 1))
    mine = narrow(order, [(half_of(mixed, 0), o_weight)], sent, 1)
    come = chip_swaps(mine)
    order.arrived(gate_rows, up_rows)
    middle, h_two, ffn = [], [], []
    for i in range(PIECES):
        middle_part, *h_pair = middle_of(order, core_one, flat_tokens, mine[i], come[i], gain_two, i)
        middle.append(middle_part)
        h_pair += core_swaps(h_pair)
        h_two += h_pair
        ffn.append(gated(order, h_pair, grad_hidden, i, gate_t, up_t))
    hidden, grad_gate, grad_up = (list(parts) for parts in zip(*ffn))

    down_b = SeqFirst([grad_ffn_t], [hidden], [(0, 0, cut, tiles - cut, 0)])
    down_a = Rows([grad_ffn_t], [hidden], [(0, 0, 0, cut, 0)])
    sent = core_swaps(
        narrow(order, [(sides_of(grad_gate, 1), gate_t), (sides_of(grad_up, 1), up_t)])
    )
    mine = narrow(order, [(sides_of(grad_gate, 0), gate_t), (sides_of(grad_up, 0), up_t)], sent)
    come = chip_swaps(mine)
    h_two_t = turn(order, h_two)
    if near_pair:
        sends = share_of(
            order,
            [h_two_t],
            [grad_gate, grad_up],
            [(0, 0, 0, tiles, 0), (0, 1, 0, long, 1), (0, 1, long, tiles - long, 2)],
            part,
            1 - dp_index,
            TILE,
        )
    else:
        sends = [None] * 3

    def half_rows(kind, right, begin, end, sent):
        return kind([h_two_t], [right], [(0, 0, begin, end - begin, 0)], TILE, sent)

    gate = half_rows(Scattered, grad_gate, 0, tiles, sends[0])
    up_a = half_rows(Rows, grad_up, 0, long, sends[1])
    up_b = half_rows(Rows, grad_up, long, tiles, sends[2])
    down_a.own()
    grad_middle, *branch = norm_back(order, core_one, mine, come, middle, gain_two, grad_ffn, False)
    branch += core_swaps(branch)
    grad_mixed = mixed_back(order, branch, o_weight).reshape(rows, local, heads * HD)
    grad_q_rows, keep, sent = attend_back(
        order, low, core_one, q_rows, start, span, mate, grad_mixed, mixed_rows, lse, cosine, sine
    )
    both_come = core_swap(sent)
    branch_t = turn(order, branch)
    own_kv, *pieces = fold(order, keep, both_come, local)
    moving = shifted(pieces[-1], -1) if pieces else None
    ffn_sent = core_swaps(narrow(order, [(sides_of(hidden, 1), down_t)]))
    for piece in pieces[-2::-1]:
        moving = shifted(carry(order, piece, moving), -1)
    grad_qkv, bias_sum = join(
        order, core_one, grad_q_rows, own_kv, [] if moving is None else [moving], cosine, sine
    )
    sent = core_swaps(narrow(order, [(half_of(grad_qkv, 1), weight)], (), 1))
    last_parts = [(0, 0, 0, grad_qkv.shape[1] // HD, 0), (1, 1, 0, heads, 0)]
    last = Rows([h_one_t, branch_t], [[grad_qkv], [mixed]], last_parts, HD)
    mine = narrow(order, [(half_of(grad_qkv, 0), weight)], sent, 1)
    come = chip_swaps(mine)
    gate.own()
    ffn_mine = narrow(order, [(sides_of(hidden, 0), down_t)], ffn_sent)
    down_a.relay()
    token = norm_back(order, core_one, mine, come, flat_tokens, gain_one, grad_middle, True)
    token += core_swaps(token)
    ffn_come = chip_swaps(ffn_mine)
    token_grad = place(order, core_one, token).reshape(rows, local, width)
    up_a.own()
    layer = layer_of(order, middle, ffn_mine, ffn_come)
    layer += core_swaps(layer)
    down_b.across()
    down_a.settled()
    last.own()
    layer_out = place(order, core_one, layer).reshape(rows, local, width)
    up_a.relay()
    down_b.settled()
    up_b.own()
    last.relay()
    (down_grad,) = finish(order, [down_a.result(), down_b.result()], share, units, TILE)
    if near_pair:
        bias_come = lax.ppermute(bias_sum, "dp", flipped("dp", 0))
        bias_all = bias_add(order, bias_sum, bias_come)
        bias_come = lax.ppermute(bias_all, "seq", flipped("seq", 0))
    up_b.relay()
    gate_grad, gate_term = finish(order, [gate.result()], share, units, TILE, gate_rows)
    wide_columns = grad_qkv.shape[1]
    (last_grad,) = finish(order, [last.result()], share, wide_columns + heads * HD, HD)
    if near_pair:
        bias_all = bias_add(order, bias_all, bias_come)
        bias_come = lax.ppermute(bias_all, "seq", flipped("seq", 1))
        bias_all = (bias_all + bias_come)[:1]
    else:
        bias_all = lax.psum(bias_sum[:1], ("dp", "seq"))
    up_grad, up_term = finish(order, [up_a.result(), up_b.result()], share, units, TILE, up_rows)
    qkv_grad, o_grad = last_grad[:, :wide_columns], last_grad[:, wide_columns:]

    attn_term = jnp.sum(to_f(rows_of(weight)) * qkv_grad, axis=1)
    ffn_term = jnp.sum(gate_term + up_term, axis=1)
    columns = heads * HD
    room = -(-share // HD) * HD - share
    terms = jnp.pad(jnp.stack([ffn_term, attn_term]), ((0, 0), (0, room))).reshape(-1, HD)
    packed = jnp.concatenate([qkv_grad[:, columns:], bias_all.reshape(-1, HD), terms], axis=0)
    gathered = tensor_gather(packed, rank)
    term_rows = terms.shape[0]
    bias_count = bias_all.shape[1] // HD
    terms = gathered[:, share + bias_count :].reshape(ranks, 2, -1)[:, :, :share]
    ffn_gain_grad, attn_gain_grad = terms[0] + terms[1] + (terms[2] + terms[3])
    attn_gain_grad = attn_gain_grad / lax.dynamic_slice_in_dim(gain_one[0], begin, share, 0)
    ffn_gain_grad = ffn_gain_grad / lax.dynamic_slice_in_dim(gain_two[0], begin, share, 0)
    q_grad = qkv_grad[:, :columns]
    kv_parts = lax.dynamic_slice_in_dim(gathered, rank * (share // ranks), share // ranks, 1)
    k_grad = jnp.concatenate([kv_parts[2 * i] for i in range(KVH)], axis=1)
    v_grad = jnp.concatenate([kv_parts[2 * i + 1] for i in range(KVH)], axis=1)
    biases = gathered[:, share : share + bias_count]
    q_bias_grad = biases[:, :heads].reshape(-1)
    k_bias_grad = biases[0::2, heads].reshape(-1)
    v_bias_grad = biases[1::2, heads].reshape(-1)
    return (
        layer_out,
        token_grad,
        q_grad,
        q_bias_grad,
        k_grad,
        k_bias_grad,
        v_grad,
        v_bias_grad,
        o_grad,
        attn_gain_grad,
        ffn_gain_grad,
        gate_grad,
        up_grad,
        down_grad,
    )


def solution(mesh):
    in_specs = (
        P("dp", "seq", None),
        P("dp", None),
        P("dp", "seq", None),
        P(None, "tensor"),
        P("tensor"),
        P(),
        P(),
        P(),
        P(),
        P(None, "tensor"),
        P(),
        P(),
        P(None, "tensor"),
        P(None, "tensor"),
        P(None, "tensor"),
    )
    out_specs = (
        P("dp", "seq", None),
        P("dp", "seq", None),
        P(("dp", "seq"), "tensor"),
        P(),
        P(("dp", "seq", "tensor"), None),
        P(),
        P(("dp", "seq", "tensor"), None),
        P(),
        P(("dp", "seq"), "tensor"),
        P(("dp", "seq")),
        P(("dp", "seq")),
        P(("dp", "seq"), "tensor"),
        P(("dp", "seq"), "tensor"),
        P(("dp", "seq"), "tensor"),
    )
    return jax.shard_map(body, mesh=mesh, in_specs=in_specs, out_specs=out_specs, check_vma=False)
```

```python
import functools
import math

import jax
import jax.numpy as jnp
from jax import lax
from jax.experimental import pallas as pl
from jax.experimental.pallas import tpu as pltpu
from jax.sharding import PartitionSpec as P

KVH = 2
HD = 128
MOST = 1024
EPS = 1e-06
ROPE_BASE = 10000.0
NEG_FILL = -1e30
Q_BLOCK = 256
K_BLOCK = 256
MIB = 1 << 20
LIGHT = 1000
TILE = 256
PIECES = 2
LARGE = MIB
SCALE = 1.0 / math.sqrt(HD)


def to_bf(value):
    return value.astype(jnp.bfloat16)


def to_f(value):
    return value.astype(jnp.float32)


def dot(left, right, left_dim=1, right_dim=0):
    return lax.dot_general(
        left,
        right,
        (((left_dim,), (right_dim,)), ((), ())),
        preferred_element_type=jnp.float32,
    )


def flipped(axis, bit):
    return [(i, i ^ (1 << bit)) for i in range(lax.axis_size(axis))]


def core_swap(value):
    return lax.ppermute(value, "tensor", flipped("tensor", 0))


def chip_swap(value):
    return lax.ppermute(value, "tensor", flipped("tensor", 1))


def core_swaps(values):
    return [core_swap(value) for value in values]


def chip_swaps(values):
    return [chip_swap(value) for value in values]


def shifted(value, hops):
    count = lax.axis_size("seq")
    route = [(i, i + hops) for i in range(count) if 0 <= i + hops < count]
    return lax.ppermute(value, "seq", route)


def cost(flops, read):
    return pl.CostEstimate(flops=flops // LIGHT, bytes_accessed=read // LIGHT, transcendentals=0)


def placed(shape):
    if math.prod(shape.shape) * shape.dtype.itemsize < LARGE:
        return shape
    return pltpu.HBM(shape.shape, shape.dtype)


class Order:
    def __init__(self):
        self.mark = None
        self.touched = []

    def arrived(self, *values):
        self.touched.extend(values)

    def __call__(self, kernel, args, in_specs, out_specs, out_shape, grid, flops, read, name, scalars=(), scratch=()):
        anchor = ([] if self.mark is None else [self.mark]) + self.touched
        self.touched = []
        count = len(scalars) + len(args)
        outs = len(out_shape)

        def run(*refs):
            rest = refs[count + len(anchor) :]
            kernel(*refs[:count], *rest[:outs], *rest[outs + 1 :])
            rest[outs][...] = jnp.zeros(rest[outs].shape, jnp.float32)

        *results, self.mark = pl.pallas_call(
            run,
            grid_spec=pltpu.PrefetchScalarGridSpec(
                num_scalar_prefetch=len(scalars),
                grid=grid,
                in_specs=list(in_specs) + anchors(len(anchor)),
                out_specs=list(out_specs) + [mark_spec()],
                scratch_shapes=list(scratch),
            ),
            out_shape=[placed(shape) for shape in out_shape] + [MARK],
            compiler_params=pltpu.CompilerParams(vmem_limit_bytes=32 * MIB),
            cost_estimate=cost(flops, read),
            name=name,
        )(*scalars, *args, *anchor)
        return results


def first_kernel(core_ref, tok_ref, gain_ref, w_ref, b_ref, cos_ref, sin_ref, h_ref, q_ref, kv_ref):
    x = to_f(tok_ref[...])
    factor = lax.rsqrt(jnp.mean(x * x, axis=-1, keepdims=True) + EPS)
    h = to_bf(x * factor * gain_ref[...])
    h_ref[...] = h
    lin = dot(h, w_ref[...]) + b_ref[...]
    cosine = cos_ref[...]
    sine = sin_ref[...]
    heads = q_ref.shape[1] // HD
    for head in range(heads):
        part = lin[:, head * HD : (head + 1) * HD]
        q_ref[:, head * HD : (head + 1) * HD] = to_bf(
            part * cosine + pltpu.roll(part, HD // 2, 1) * sine
        )
    part = lin[:, heads * HD :]
    is_key = core_ref[0] == 0
    kv_ref[...] = to_bf(
        part * jnp.where(is_key, cosine, 1.0)
        + pltpu.roll(part, HD // 2, 1) * jnp.where(is_key, sine, 0.0)
    )


def first(core, tokens, gain, weight, bias, cosine, sine):
    total, width = tokens.shape
    columns = weight.shape[1]
    block = total // 4
    half = 2

    def flip(i, core_ref):
        return (lax.rem(i + core_ref[0] * half, 4), 0)

    def at(i, core_ref):
        return (i, 0)

    def whole(i, core_ref):
        return (0, 0)

    return pl.pallas_call(
        first_kernel,
        grid_spec=pltpu.PrefetchScalarGridSpec(
            num_scalar_prefetch=1,
            grid=(4,),
            in_specs=[
                pl.BlockSpec((block, width), flip),
                pl.BlockSpec((1, width), whole),
                pl.BlockSpec((width, columns), whole),
                pl.BlockSpec((1, columns), whole),
                pl.BlockSpec((block, HD), at),
                pl.BlockSpec((block, HD), at),
            ],
            out_specs=[
                pl.BlockSpec((block, width), at),
                pl.BlockSpec((block, columns - HD), at),
                pl.BlockSpec((block, HD), at),
            ],
        ),
        out_shape=[
            jax.ShapeDtypeStruct((total, width), jnp.bfloat16),
            jax.ShapeDtypeStruct((total, columns - HD), jnp.bfloat16),
            jax.ShapeDtypeStruct((total, HD), jnp.bfloat16),
        ],
        compiler_params=pltpu.CompilerParams(vmem_limit_bytes=32 * MIB),
        cost_estimate=cost(2 * total * width * columns, 9 * MIB),
        name="first",
    )(core, tokens, gain, weight, bias, cosine, sine)


def stacked(ref, start, count, heads):
    return jnp.concatenate(
        [ref[0, pl.ds(start, count), h * HD : (h + 1) * HD] for h in range(heads)], axis=0
    )


def bounds(start_ref, index, heads, reach):
    first_key = jnp.concatenate(
        [start_ref[0, :, pl.ds(index * Q_BLOCK, Q_BLOCK)]] * heads, axis=1
    )
    place = reach + index * Q_BLOCK + lax.broadcasted_iota(jnp.int32, (1, Q_BLOCK), 1)
    return first_key, jnp.concatenate([place] * heads, axis=1)


def pass_kernel(*refs):
    for i, ref in enumerate(refs[:-1]):
        refs[-1][i] = ref[...]


def pass_on(order, pieces):
    rows, local, columns = pieces[0].shape
    count = len(pieces)
    return order(
        pass_kernel,
        list(pieces),
        [pl.BlockSpec((1, local, columns), lambda i: (i, 0, 0))] * count,
        [pl.BlockSpec((count, 1, local, columns), lambda i: (0, i, 0, 0))],
        [jax.ShapeDtypeStruct((count, rows, local, columns), pieces[0].dtype)],
        (rows,),
        0,
        2 * MIB,
        "pass",
    )[0]


def gather_span(core, refs, span):
    for side, (moved, own) in ((core, refs[:2]), (1 - core, refs[2:])):
        local = own.shape[1]
        hops = moved.shape[0]
        for i in range(hops):
            span[side, i * local : (i + 1) * local] = moved[i, 0]
        span[side, hops * local :] = own[0]


def attend_kernel(heads, blocks, pieces, low_ref, core_ref, q_ref, start_ref, *refs):
    o_ref, lse_ref, acc, span = refs[4:]
    row = pl.program_id(0)
    wide = heads * Q_BLOCK
    reach = (pieces - 1) * q_ref.shape[1]
    gather_span(core_ref[0], refs[:4], span)
    for index in range(blocks):
        q = stacked(q_ref, index * Q_BLOCK, Q_BLOCK, heads)
        first_key, place = bounds(start_ref, index, heads, reach)
        acc[...] = jnp.zeros_like(acc)

        def step(j, carry):
            top, total = carry
            keys = pl.ds(pl.multiple_of(j * K_BLOCK, K_BLOCK), K_BLOCK)
            s = dot(span[0, keys], q, 1, 1) * SCALE
            key = j * K_BLOCK + lax.broadcasted_iota(jnp.int32, (K_BLOCK, wide), 0)
            s = jnp.where((key >= first_key) & (key <= place), s, NEG_FILL)
            later = jnp.maximum(top, jnp.max(s, axis=0, keepdims=True))
            p = jnp.exp(s - later)
            fade = jnp.exp(top - later)
            total = total * fade + jnp.sum(p, axis=0, keepdims=True)
            acc[...] = acc[...] * fade + dot(span[1, keys], to_bf(p), 0, 0)
            return later, total

        last = (reach + (index + 1) * Q_BLOCK - 1) // K_BLOCK + 1
        top, total = lax.fori_loop(
            low_ref[row, index],
            last,
            step,
            (jnp.full((1, wide), NEG_FILL, jnp.float32), jnp.zeros((1, wide), jnp.float32)),
        )
        out = to_bf((acc[...] / total).T)
        for h in range(heads):
            o_ref[0, index * Q_BLOCK : (index + 1) * Q_BLOCK, h * HD : (h + 1) * HD] = out[
                h * Q_BLOCK : (h + 1) * Q_BLOCK
            ]
        lse_ref[0, index : index + 1, :] = top + jnp.log(total)


def span_specs(rows, local, pieces):
    def at(turned):
        def row(i):
            return lax.rem(i + turned, rows)

        return [
            pl.BlockSpec((pieces - 1, 1, local, HD), lambda i, *refs: (0, row(i), 0, 0)),
            pl.BlockSpec((1, local, HD), lambda i, *refs: (row(i), 0, 0)),
        ]

    return at(0) + at(rows // 2)


def attend(order, low, core, q, start, span, mate):
    rows, local, columns = q.shape
    pieces = span[0].shape[0] + 1
    heads = columns // HD
    blocks = local // Q_BLOCK

    def at(i, *refs):
        return (i, 0, 0)

    return order(
        functools.partial(attend_kernel, heads, blocks, pieces),
        [q, start, *span, *mate],
        [pl.BlockSpec((1, local, columns), at), pl.BlockSpec((1, 1, local), at)]
        + span_specs(rows, local, pieces),
        [pl.BlockSpec((1, local, columns), at), pl.BlockSpec((1, blocks, heads * Q_BLOCK), at)],
        [
            jax.ShapeDtypeStruct((rows, local, columns), jnp.bfloat16),
            jax.ShapeDtypeStruct((rows, blocks, heads * Q_BLOCK), jnp.float32),
        ],
        (rows,),
        8_000_000_000,
        4 * MIB,
        "attend",
        scalars=(low, core),
        scratch=[
            pltpu.VMEM((HD, heads * Q_BLOCK), jnp.float32),
            pltpu.VMEM((2, pieces * local, HD), jnp.bfloat16),
        ],
    )


def attend_back_kernel(
    heads, blocks, pieces, low_ref, core_ref, q_ref, start_ref, g_ref, o_ref, lse_ref, cos_ref, sin_ref, *refs
):
    gq_ref, keep_ref, send_ref, acc, gk, gv, span = refs[4:]
    row = pl.program_id(0)
    wide = heads * Q_BLOCK
    reach = (pieces - 1) * q_ref.shape[1]
    core = core_ref[0]
    gather_span(core, refs[:4], span)
    gk[...] = jnp.zeros_like(gk)
    gv[...] = jnp.zeros_like(gv)
    for index in range(blocks):
        q = stacked(q_ref, index * Q_BLOCK, Q_BLOCK, heads)
        g = stacked(g_ref, index * Q_BLOCK, Q_BLOCK, heads)
        o = stacked(o_ref, index * Q_BLOCK, Q_BLOCK, heads)
        inner = jnp.sum((to_f(g) * to_f(o)).T, axis=0, keepdims=True)
        lse = lse_ref[0, index : index + 1, :]
        first_key, place = bounds(start_ref, index, heads, reach)
        acc[...] = jnp.zeros_like(acc)

        def step(j, carry):
            keys = pl.ds(pl.multiple_of(j * K_BLOCK, K_BLOCK), K_BLOCK)
            k = span[0, keys]
            s = dot(k, q, 1, 1) * SCALE
            key = j * K_BLOCK + lax.broadcasted_iota(jnp.int32, (K_BLOCK, wide), 0)
            p = jnp.where((key >= first_key) & (key <= place), jnp.exp(s - lse), 0.0)
            gp = dot(span[1, keys], g, 1, 1)
            gs = to_bf(p * (gp - inner))
            gv[keys] += dot(to_bf(p), g)
            gk[keys] += dot(gs, q)
            acc[...] += dot(k, gs, 0, 0)
            return carry

        last = (reach + (index + 1) * Q_BLOCK - 1) // K_BLOCK + 1
        lax.fori_loop(low_ref[row, index], last, step, 0)
        gq = acc[...].T * SCALE
        here = slice(index * Q_BLOCK, (index + 1) * Q_BLOCK)
        cosine, sine = cos_ref[here], sin_ref[here]
        for h in range(heads):
            part = gq[h * Q_BLOCK : (h + 1) * Q_BLOCK]
            gq_ref[0, here, h * HD : (h + 1) * HD] = to_bf(
                part * cosine + pltpu.roll(part * sine, HD // 2, 1)
            )
    is_key = core == 0
    keys, values = gk[...] * SCALE, gv[...]
    keep_ref[0] = to_bf(jnp.where(is_key, keys, values))
    send_ref[0] = to_bf(jnp.where(is_key, values, keys))


def attend_back(order, low, core, q, start, span, mate, grad, out, lse, cosine, sine):
    rows, local, columns = q.shape
    pieces = span[0].shape[0] + 1
    window = pieces * local
    heads = columns // HD
    blocks = local // Q_BLOCK

    def at(i, *refs):
        return (i, 0, 0)

    table = pl.BlockSpec((local, HD), lambda i, *refs: (i, 0))
    tokens = pl.BlockSpec((1, local, columns), at)
    return order(
        functools.partial(attend_back_kernel, heads, blocks, pieces),
        [q, start, grad, out, lse, cosine, sine, *span, *mate],
        [
            tokens,
            pl.BlockSpec((1, 1, local), at),
            tokens,
            tokens,
            pl.BlockSpec((1, blocks, heads * Q_BLOCK), at),
            table,
            table,
        ]
        + span_specs(rows, local, pieces),
        [tokens, pl.BlockSpec((1, window, HD), at), pl.BlockSpec((1, window, HD), at)],
        [
            jax.ShapeDtypeStruct((rows, local, columns), jnp.bfloat16),
            jax.ShapeDtypeStruct((rows, window, HD), jnp.bfloat16),
            jax.ShapeDtypeStruct((rows, window, HD), jnp.bfloat16),
        ],
        (rows,),
        20_000_000_000,
        6 * MIB,
        "attend_back",
        scalars=(low, core),
        scratch=[
            pltpu.VMEM((HD, heads * Q_BLOCK), jnp.float32),
            pltpu.VMEM((window, HD), jnp.float32),
            pltpu.VMEM((window, HD), jnp.float32),
            pltpu.VMEM((2, window, HD), jnp.bfloat16),
        ],
    )


def fold_kernel(keep_ref, come_ref, own_ref, *send_refs):
    local = own_ref.shape[1]
    total = to_f(keep_ref[0]) + to_f(come_ref[0])
    reach = total.shape[0] - local
    own_ref[0] = total[reach:]
    for hop, ref in enumerate(send_refs, 1):
        ref[0] = to_bf(total[reach - hop * local : reach - (hop - 1) * local])


def fold(order, keep, come, local):
    rows, window = keep.shape[:2]
    hops = window // local - 1
    out = pl.BlockSpec((1, local, HD), lambda i: (i, 0, 0))
    return order(
        fold_kernel,
        [keep, come],
        [
            pl.BlockSpec((1, window, HD), lambda i: (i, 0, 0)),
            pl.BlockSpec((1, window, HD), lambda i: (lax.rem(i + rows // 2, rows), 0, 0)),
        ],
        [out] * (hops + 1),
        [jax.ShapeDtypeStruct((rows, local, HD), jnp.float32)]
        + [jax.ShapeDtypeStruct((rows, local, HD), jnp.bfloat16)] * hops,
        (rows,),
        0,
        4 * MIB,
        "fold",
    )


def carry_kernel(piece_ref, come_ref, out_ref):
    out_ref[...] = to_bf(to_f(piece_ref[...]) + to_f(come_ref[...]))


def carry(order, piece, come):
    rows, local, columns = piece.shape
    at = pl.BlockSpec((1, local, columns), lambda i: (i, 0, 0))
    return order(
        carry_kernel,
        [piece, come],
        [at, at],
        [at],
        [jax.ShapeDtypeStruct(piece.shape, jnp.bfloat16)],
        (rows,),
        0,
        2 * MIB,
        "carry",
    )[0]


def bias_kernel(left_ref, right_ref, out_ref):
    out_ref[...] = left_ref[...] + right_ref[...]


def bias_add(order, left, right):
    whole = pl.BlockSpec(left.shape, lambda i: (0, 0))
    return order(
        bias_kernel,
        [left, right],
        [whole, whole],
        [whole],
        [jax.ShapeDtypeStruct(left.shape, jnp.float32)],
        (1,),
        0,
        MIB,
        "bias",
    )[0]


def join_kernel(hops, core_ref, gq_ref, cos_ref, sin_ref, own_ref, *refs):
    out_ref, sum_ref = refs[-2:]
    columns = gq_ref.shape[2]
    grad = own_ref[0]
    for ref in refs[:hops]:
        grad = grad + to_f(ref[0])
    is_key = core_ref[0] == 0
    cosine = jnp.where(is_key, cos_ref[...], 1.0)
    sine = jnp.where(is_key, sin_ref[...], 0.0)
    kv = to_bf(grad * cosine + pltpu.roll(grad * sine, HD // 2, 1))
    q = gq_ref[0]
    out_ref[:, :columns] = q
    out_ref[:, columns:] = kv

    @pl.when(pl.program_id(0) == 0)
    def _():
        sum_ref[...] = jnp.zeros(sum_ref.shape, jnp.float32)

    sum_ref[:, :columns] += jnp.sum(to_f(q), axis=0, keepdims=True)
    sum_ref[:, columns:] += jnp.sum(to_f(kv), axis=0, keepdims=True)


def join(order, core, grad_q, own, comes, cosine, sine):
    rows, local, columns = grad_q.shape
    wide = columns + HD

    def at(i, *refs):
        return (i, 0, 0)

    piece = pl.BlockSpec((1, local, HD), at)
    table = pl.BlockSpec((local, HD), lambda i, *refs: (i, 0))
    return order(
        functools.partial(join_kernel, len(comes)),
        [grad_q, cosine, sine, own, *comes],
        [pl.BlockSpec((1, local, columns), at), table, table, piece] + [piece] * len(comes),
        [
            pl.BlockSpec((local, wide), lambda i, *refs: (i, 0)),
            pl.BlockSpec((8, wide), lambda i, *refs: (0, 0)),
        ],
        [
            jax.ShapeDtypeStruct((rows * local, wide), jnp.bfloat16),
            jax.ShapeDtypeStruct((8, wide), jnp.float32),
        ],
        (rows,),
        0,
        4 * MIB,
        "join",
        scalars=(core,),
    )


def mixed_back_kernel(w_ref, *refs):
    rows = refs[0].shape[0]
    for i, ref in enumerate(refs[:-1]):
        refs[-1][i * rows : (i + 1) * rows] = to_bf(dot(ref[...], w_ref[...]))


def mixed_back(order, pieces, weight):
    rows, width = pieces[0].shape
    total = rows * len(pieces)
    columns = weight.shape[1]

    def whole(i):
        return (0, 0)

    return order(
        mixed_back_kernel,
        [weight, *pieces],
        [pl.BlockSpec((width, columns), whole)] + [pl.BlockSpec((rows, width), whole)] * len(pieces),
        [pl.BlockSpec((total, columns), whole)],
        [jax.ShapeDtypeStruct((total, columns), jnp.bfloat16)],
        (1,),
        2 * total * width * columns,
        6 * MIB,
        "mixed_back",
    )[0]


def place_kernel(core_ref, *refs):
    for i, ref in enumerate(refs[:-1]):

        @pl.when(pl.program_id(0) == i)
        def _(ref=ref):
            refs[-1][...] = ref[...]


def place(order, core, pieces):
    rows, width = pieces[0].shape
    count = len(pieces)
    return order(
        place_kernel,
        list(pieces),
        [pl.BlockSpec((rows, width), lambda i, core_ref: (0, 0))] * count,
        [pl.BlockSpec((rows, width), lambda i, core_ref: (lax.rem(i + core_ref[0] * (count // 2), count), 0))],
        [jax.ShapeDtypeStruct((rows * count, width), pieces[0].dtype)],
        (count,),
        0,
        8 * rows * width,
        "place",
        scalars=(core,),
    )[0]


def anchors(count):
    return [pl.BlockSpec(memory_space=pl.ANY)] * count


MARK = jax.ShapeDtypeStruct((8, HD), jnp.float32)


def mark_spec():
    return pl.BlockSpec((8, HD), lambda *refs: (0, 0))


def grad_hidden_kernel(g_ref, w_ref, out_ref):
    out_ref[...] = to_bf(dot(g_ref[...], w_ref[...], 1, 1))


def grad_hidden_of(order, grad, weight):
    total, width = grad.shape
    hidden = weight.shape[0]
    return order(
        grad_hidden_kernel,
        [grad, weight],
        [pl.BlockSpec((total, width), lambda i: (0, 0)), pl.BlockSpec((TILE, width), lambda i: (i, 0))],
        [pl.BlockSpec((total, TILE), lambda i: (0, i))],
        [jax.ShapeDtypeStruct((total, hidden), jnp.bfloat16)],
        (pl.cdiv(hidden, TILE),),
        2 * total * width * hidden,
        15 * MIB,
        "grad_hidden",
    )[0]


def gated_kernel(gh_ref, gw_ref, uw_ref, *refs):
    hid_ref, gg_ref, gu_ref = refs[-3:]
    for here in (slice(0, hid_ref.shape[0]),):
        h = jnp.concatenate([ref[...] for ref in refs[:-3]], axis=0)
        gate = dot(h, gw_ref[...], 1, 1)
        up = dot(h, uw_ref[...], 1, 1)
        grad = to_f(gh_ref[here])
        sigma = 1.0 / (1.0 + jnp.exp(-gate))
        swish = gate * sigma
        hid_ref[here] = to_bf(swish * up)
        gu_ref[here] = to_bf(grad * swish)
        gg_ref[here] = to_bf(grad * up * sigma * (1.0 + gate * (1.0 - sigma)))


def gated(order, pieces, grad_hidden, index, gate_weight, up_weight):
    rows, width = pieces[0].shape
    total = rows * len(pieces)
    hidden = gate_weight.shape[0]
    column = pl.BlockSpec((total, TILE), lambda i: (0, i))
    weight = pl.BlockSpec((TILE, width), lambda i: (i, 0))
    shape = jax.ShapeDtypeStruct((total, hidden), jnp.bfloat16)
    return order(
        gated_kernel,
        [grad_hidden, gate_weight, up_weight, *pieces],
        [pl.BlockSpec((total, TILE), lambda i: (index, i)), weight, weight]
        + [pl.BlockSpec((rows, width), lambda i: (0, 0))] * len(pieces),
        [column] * 3,
        [shape] * 3,
        (pl.cdiv(hidden, TILE),),
        4 * total * width * hidden,
        30 * MIB,
        "gated",
    )


def share_kernel(plan, lefts, rights, extra, halves, groups, pick_ref, blocks_ref, *refs):
    step = pl.program_id(0)
    left_refs, refs = refs[:lefts], refs[lefts:]
    right_refs = []
    for count in rights:
        right_refs.append(refs[:count])
        refs = refs[count:]
    if extra:
        extra_ref, refs = refs[0], refs[1:]
    for left, right, begin, end, shift, columns, target in plan:

        @pl.when((step >= begin) & (step < end))
        def _(left=left, right=right, shift=shift, columns=columns, target=target):
            out = dot(
                left_refs[left][...], jnp.concatenate([ref[...] for ref in right_refs[right]], axis=0)
            )
            if extra:
                out = out + to_f(extra_ref[...])
            tile = out.shape[1]
            spot = (step + shift) * tile + lax.broadcasted_iota(jnp.int32, (1, tile), 1)
            out = to_bf(jnp.where(spot < columns, out, 0.0))
            if groups:
                share = out.shape[0] // (groups[0] * groups[1])
                for i in range(groups[0]):
                    for j in range(groups[1]):
                        here = (j * groups[0] + i) * share
                        there = (i * groups[1] + j) * share
                        refs[target][here : here + share] = out[there : there + share]
                return
            if not halves:
                refs[target][...] = out
                return
            send_ref, keep_ref, rows = refs
            rows[...] = out
            share = send_ref.shape[0] // (2 * halves)
            for i in range(2 * halves):
                here = slice(i * share, (i + 1) * share)
                send_ref[here] = rows[pl.ds(pl.multiple_of(blocks_ref[i] * share, share), share)]
                keep_ref[here] = rows[pl.ds(pl.multiple_of(blocks_ref[2 * halves + i] * share, share), share)]


def clipped(rows, tile, begin, count, shift=0):
    return pl.BlockSpec((rows, tile), lambda i, *refs: (0, jnp.clip(i - begin, 0, count - 1) + shift))


def share_of(order, lefts, rights, parts, part, pick, tile, extra=None, blocks=None, groups=None):
    tokens = lefts[0].shape[1]
    plan, at = [], 0
    starts, sizes, right_at = {}, {}, {}
    for left, right, skip, count, target in parts:
        plan.append((left, right, at, at + count, skip - at, rights[right][0].shape[1], target))
        starts.setdefault(target, at)
        sizes[target] = sizes.get(target, 0) + count
        first, tiles, low = right_at.get(right, (at, 0, skip))
        right_at[right] = (first, tiles + count, low)
        at += count
    halves = 0
    extras = [] if extra is None else [extra]
    scratch = []
    if blocks is None:
        blocks = jnp.zeros((1,), jnp.int32)
        outs = [clipped(part, tile, starts[t], sizes[t]) for t in sorted(sizes)]
        shapes = [jax.ShapeDtypeStruct((part, sizes[t] * tile), jnp.bfloat16) for t in sorted(sizes)]
    else:
        halves = blocks.shape[0] // 4
        outs = [clipped(part // 2, tile, 0, at)] * 2
        shapes = [jax.ShapeDtypeStruct((part // 2, at * tile), jnp.bfloat16)] * 2
        scratch = [pltpu.VMEM((part, tile), jnp.bfloat16)]
    return order(
        functools.partial(share_kernel, plan, len(lefts), [len(r) for r in rights], len(extras), halves, groups),
        [*lefts, *[block for right in rights for block in right], *extras],
        [pl.BlockSpec((part, tokens), lambda i, pick_ref, blocks_ref: (pick_ref[0], 0))] * len(lefts)
        + [clipped(block.shape[0], tile, *right_at[r]) for r, right in enumerate(rights) for block in right]
        + [clipped(part, tile, 0, at)] * len(extras),
        outs,
        shapes,
        (at,),
        2 * part * tokens * at * tile,
        2 * (part * tokens + (part + tokens) * at * tile),
        "share",
        scalars=(jnp.asarray(pick, jnp.int32).reshape(1), blocks),
        scratch=scratch,
    )


def relay_kernel(keep_ref, come_ref, out_ref):
    out_ref[...] = to_bf(to_f(keep_ref[...]) + to_f(come_ref[...]))


def relay(order, keep, come, share):
    rows, columns = keep.shape
    pair = pl.BlockSpec((share, columns), lambda i: (2 * i + 1, 0))
    return order(
        relay_kernel,
        [keep, come],
        [pair, pair],
        [pl.BlockSpec((share, columns), lambda i: (i, 0))],
        [jax.ShapeDtypeStruct((rows // 2, columns), jnp.bfloat16)],
        (rows // (2 * share),),
        0,
        3 * rows * columns,
        "relay",
    )[0]


def finish_kernel(plan, columns, gains, *refs):
    out_ref = refs[-2] if gains else refs[-1]
    step = pl.program_id(0)
    tile = out_ref.shape[1]
    for begin, end, first, count in plan:

        @pl.when((step >= begin) & (step < end))
        def _(first=first, count=count):
            out = to_f(refs[first][...])
            for ref in refs[first + 1 : first + count]:
                out = out + to_f(ref[...])
            out_ref[...] = out
            if gains:
                spot = step * tile + lax.broadcasted_iota(jnp.int32, (1, tile), 1)
                terms = jnp.where(spot < columns, out * to_f(refs[-3][...]), 0.0)
                total = terms[:, :HD]
                for i in range(HD, tile, HD):
                    total = total + terms[:, i : i + HD]

                @pl.when(step == 0)
                def _():
                    refs[-1][...] = total

                @pl.when(step > 0)
                def _():
                    refs[-1][...] += total


def finish(order, chunks, share, columns, tile, weight=None):
    plan, specs, args, at = [], [], [], 0
    for chunk in chunks:
        count = chunk[0].shape[1] // tile
        plan.append((at, at + count, len(args), len(chunk)))
        specs += [clipped(share, tile, at, count)] * len(chunk)
        args += chunk
        at += count
    column = pl.BlockSpec((share, tile), lambda i: (0, i))
    outs, shapes = [column], [jax.ShapeDtypeStruct((share, columns), jnp.float32)]
    if weight is not None:
        args.append(weight)
        specs.append(column)
        outs.append(pl.BlockSpec((share, HD), lambda i: (0, 0)))
        shapes.append(jax.ShapeDtypeStruct((share, HD), jnp.float32))
    return order(
        functools.partial(finish_kernel, plan, columns, weight is not None),
        args,
        specs,
        outs,
        shapes,
        (at,),
        0,
        14 * share * columns,
        "finish",
    )


def narrow_kernel(pairs, extras, right_dim, *refs):
    out = 0.0
    for i in range(pairs):
        left = jnp.concatenate([ref[...] for ref in refs[:PIECES]], axis=0)
        out = out + dot(left, refs[PIECES][...], 1, right_dim)
        refs = refs[PIECES + 1 :]
    outs = refs[extras:]
    if extras:
        out = out + jnp.concatenate([to_f(ref[...]) for ref in refs[:extras]], axis=0)
    rows = outs[0].shape[0]
    for i, ref in enumerate(outs):
        ref[...] = to_bf(out[i * rows : (i + 1) * rows])


def narrow(order, pairs, extra=(), right_dim=0):
    piece = pairs[0][0][0][1]
    hidden = pairs[0][0][0][0].shape[1]
    width = pairs[0][1].shape[1 - right_dim]
    half = piece * PIECES
    column = pl.BlockSpec((piece, TILE), lambda i: (0, i))
    right = (
        pl.BlockSpec((TILE, hidden), lambda i: (i, 0))
        if right_dim
        else pl.BlockSpec((hidden, TILE), lambda i: (0, i))
    )
    args, specs = [], []
    for lefts, weight in pairs:
        for array, rows, index in lefts:
            args.append(array)
            specs.append(pl.BlockSpec((rows, hidden), lambda i, index=index: (index, 0)))
        args.append(weight)
        specs.append(right)
    return order(
        functools.partial(narrow_kernel, len(pairs), len(extra), right_dim),
        args + list(extra),
        specs + [column] * len(extra),
        [column] * PIECES,
        [jax.ShapeDtypeStruct((piece, width), jnp.bfloat16)] * PIECES,
        (width // TILE,),
        2 * len(pairs) * half * width * hidden,
        2 * len(pairs) * (half + width) * hidden + 2 * half * width,
        "narrow",
    )


def half_of(array, index):
    rows = array.shape[0] // (2 * PIECES)
    return [(array, rows, index * PIECES + j) for j in range(PIECES)]


def sides_of(arrays, index):
    return [(array, array.shape[0] // 2, index) for array in arrays]


def piece_specs(piece, width, block):
    steps = piece // block
    return [
        pl.BlockSpec((block, width), lambda i, *refs, j=j: (jnp.clip(i - j * steps, 0, steps - 1), 0))
        for j in range(PIECES)
    ]


def pick_piece(refs):
    value = refs[0][...]
    for j, ref in enumerate(refs[1:], 1):
        value = jnp.where(pl.program_id(0) >= 4 * j // len(refs), ref[...], value)
    return value


def put_piece(refs, value):
    steps = 4 // len(refs)
    for j, ref in enumerate(refs):

        @pl.when(lax.div(pl.program_id(0), steps) == j)
        def _(ref=ref):
            ref[...] = value


def turn_kernel(*refs):
    rows = refs[0].shape[0]
    for i, ref in enumerate(refs[:-1]):
        refs[-1][:, i * rows : (i + 1) * rows] = ref[...].T


def turn(order, pieces):
    rows, width = pieces[0].shape
    total = rows * len(pieces)
    return order(
        turn_kernel,
        list(pieces),
        [pl.BlockSpec((rows, TILE), lambda i: (0, i))] * len(pieces),
        [pl.BlockSpec((TILE, total), lambda i: (i, 0))],
        [jax.ShapeDtypeStruct((width, total), jnp.bfloat16)],
        (width // TILE,),
        0,
        4 * total * width,
        "turn",
    )[0]


def grad_out_kernel(core_ref, cot_ref, valid_ref, out_ref, turned_ref):
    out = to_bf(to_f(cot_ref[...]) * valid_ref[...])
    out_ref[...] = out
    turned_ref[...] = out.T


def grad_out_of(order, core, cotangent, valid):
    total, width = cotangent.shape
    block = total // 4
    return order(
        grad_out_kernel,
        [cotangent, valid],
        [
            pl.BlockSpec(
                (block, width),
                lambda i, core_ref: (lax.rem(i + core_ref[0], 2) * 2 + lax.div(i, 2), 0),
            ),
            pl.BlockSpec((block, 1), lambda i, core_ref: (lax.rem(i, 2) * 2 + lax.div(i, 2), 0)),
        ],
        [
            pl.BlockSpec((block, width), lambda i, core_ref: (i, 0)),
            pl.BlockSpec((width, block), lambda i, core_ref: (0, i)),
        ],
        [
            jax.ShapeDtypeStruct((total, width), jnp.bfloat16),
            jax.ShapeDtypeStruct((width, total), jnp.bfloat16),
        ],
        (4,),
        0,
        6 * total * width,
        "grad_out",
        scalars=(core,),
    )


def middle_kernel(core_ref, tok_ref, gain_ref, mine_ref, come_ref, mid_ref, *h_refs):
    middle = to_f(tok_ref[...]) + (to_f(mine_ref[...]) + to_f(come_ref[...]))
    factor = lax.rsqrt(jnp.mean(middle * middle, axis=-1, keepdims=True) + EPS)
    mid_ref[...] = middle
    h = to_bf(middle * factor * gain_ref[...])
    for i, ref in enumerate(h_refs):

        @pl.when(pl.program_id(0) == i)
        def _(ref=ref):
            ref[...] = h


def middle_of(order, core, tokens, mine, come, gain, index):
    piece, width = mine.shape
    block = piece // 2
    at = pl.BlockSpec((block, width), lambda i, core_ref: (i, 0))
    return order(
        middle_kernel,
        [tokens, gain, mine, come],
        [
            pl.BlockSpec((block, width), lambda i, core_ref: ((core_ref[0] * PIECES + index) * 2 + i, 0)),
            pl.BlockSpec((1, width), lambda i, core_ref: (0, 0)),
            at,
            at,
        ],
        [at] + [pl.BlockSpec((block, width), lambda i, core_ref: (0, 0))] * 2,
        [jax.ShapeDtypeStruct((piece, width), jnp.float32)]
        + [jax.ShapeDtypeStruct((block, width), jnp.bfloat16)] * 2,
        (2,),
        0,
        5 * MIB,
        "middle",
        scalars=(core,),
    )


def norm_back_kernel(last, core_ref, gain_ref, up_ref, *refs):
    xs = 1 if last else PIECES
    x, refs = to_f(pick_piece(refs[:xs])), refs[xs:]
    mine, come = pick_piece(refs[:PIECES]), pick_piece(refs[PIECES : 2 * PIECES])
    outs = refs[2 * PIECES :]
    grad = to_f(mine) + to_f(come)
    factor = lax.rsqrt(jnp.mean(x * x, axis=-1, keepdims=True) + EPS)
    normed = x * factor
    weighted = grad * gain_ref[...]
    inner = jnp.mean(weighted * normed, axis=-1, keepdims=True)
    out = to_f(up_ref[...]) + factor * (weighted - normed * inner)
    if last:
        put_piece(outs, out)
    else:
        outs[0][...] = out
        put_piece(outs[1:], to_bf(out))


def norm_back(order, core, mine, come, x, gain, up, last):
    piece, width = mine[0].shape
    half = piece * PIECES
    block = half // 4
    at = pl.BlockSpec((block, width), lambda i, core_ref: (i, 0))
    gain_at = pl.BlockSpec((1, width), lambda i, core_ref: (0, 0))
    specs = piece_specs(piece, width, block)
    steps = piece // block
    if last:
        args = [gain, up, x]
        front = [gain_at, at, pl.BlockSpec((block, width), lambda i, core_ref: (core_ref[0] * 4 + i, 0))]
        shapes = [jax.ShapeDtypeStruct((piece, width), jnp.float32)] * PIECES
    else:
        args = [gain, up, *x]
        between = pl.BlockSpec((block, width), lambda i, core_ref: (i + lax.div(i, steps) * steps, 0))
        front = [gain_at, between] + specs
        shapes = [jax.ShapeDtypeStruct((half, width), jnp.float32)]
        shapes += [jax.ShapeDtypeStruct((piece, width), jnp.bfloat16)] * PIECES
    return order(
        functools.partial(norm_back_kernel, last),
        [*args, *mine, *come],
        front + specs * 2,
        specs if last else [at] + specs,
        shapes,
        (4,),
        0,
        10 * MIB,
        "norm_back",
        scalars=(core,),
    )


def layer_kernel(*refs):
    middle, mine, come = (pick_piece(refs[i * PIECES : (i + 1) * PIECES]) for i in range(3))
    put_piece(refs[3 * PIECES :], to_bf(middle + (to_f(mine) + to_f(come))))


def layer_of(order, middle, mine, come):
    piece, width = mine[0].shape
    block = piece * PIECES // 4
    specs = piece_specs(piece, width, block)
    return order(
        layer_kernel,
        [*middle, *mine, *come],
        specs * 3,
        specs,
        [jax.ShapeDtypeStruct((piece, width), jnp.bfloat16)] * PIECES,
        (4,),
        0,
        5 * MIB,
        "layer",
    )


def tensor_gather(value, rank):
    mate = core_swap(value)
    pair = jnp.where(lax.rem(rank, 2) == 0, jnp.stack([value, mate]), jnp.stack([mate, value]))
    come = chip_swap(pair)
    return jnp.where(
        lax.div(rank, 2) == 0,
        jnp.concatenate([pair, come], axis=0),
        jnp.concatenate([come, pair], axis=0),
    )


def body(
    tokens,
    lengths,
    cotangent,
    q_weight,
    q_bias,
    k_weight,
    k_bias,
    v_weight,
    v_bias,
    o_weight,
    attn_gain,
    ffn_gain,
    gate_weight,
    up_weight,
    down_weight,
):
    rows, local, width = tokens.shape
    total = rows * local
    half = total // 2
    heads = q_weight.shape[1] // HD
    ranks = lax.axis_size("tensor")
    seqs = lax.axis_size("seq")
    rank = lax.axis_index("tensor")
    dp_index = lax.axis_index("dp")
    seq_index = lax.axis_index("seq")
    core = lax.rem(rank, 2)
    head = lax.div(rank, 2)
    core_one = core.reshape(1)
    hops = min(seqs - 1, -(-(MOST - 1) // local))
    reach = hops * local

    def own_first(value):
        turned = jnp.concatenate([value[rows // 2 :], value[: rows // 2]], axis=0)
        return jnp.where(core == 0, value, turned)

    slots = jnp.arange(lengths.shape[1], dtype=jnp.int32)
    lens = own_first(lengths)
    ends = jnp.sum(jnp.where(slots[None, :] <= slots[:, None], lens[:, None, :], 0), axis=2)
    spot = seq_index * local + jnp.arange(local, dtype=jnp.int32)
    begun = jnp.max(
        jnp.where(ends[:, None, :] <= spot[None, :, None], ends[:, None, :], 0), axis=2
    )
    valid = to_f(spot[None, :] < ends[:, -2:-1])
    position = (spot[None, :] - begun).reshape(total, 1)
    freqs = ROPE_BASE ** (-(jnp.arange(HD // 2, dtype=jnp.float32) * 2.0) / HD)
    angles = to_f(position) * freqs[None, :]
    cosine, sine = jnp.cos(angles), jnp.sin(angles)
    cosine = jnp.concatenate([cosine, cosine], axis=1)
    sine = jnp.concatenate([-sine, sine], axis=1)
    start = begun - (seq_index * local - reach)
    low = jnp.maximum(lax.div(jnp.maximum(start[:, ::Q_BLOCK], 0), K_BLOCK), 0)
    start = start.reshape(rows, 1, local)

    key_side = core == 0
    kv_weight = jnp.where(
        key_side,
        lax.dynamic_slice_in_dim(k_weight, head * HD, HD, 1),
        lax.dynamic_slice_in_dim(v_weight, head * HD, HD, 1),
    )
    kv_bias = jnp.where(
        key_side,
        lax.dynamic_slice_in_dim(k_bias, head * HD, HD, 0),
        lax.dynamic_slice_in_dim(v_bias, head * HD, HD, 0),
    )
    weight = jnp.concatenate([q_weight, kv_weight], axis=1)
    bias = to_f(jnp.concatenate([q_bias, kv_bias])).reshape(1, -1)
    gain_one = to_f(attn_gain).reshape(1, width)
    gain_two = to_f(ffn_gain).reshape(1, width)

    h_one, q_rot, kv = first(
        core_one, tokens.reshape(total, width), gain_one, weight, bias, cosine, sine
    )
    kv = kv.reshape(rows, local, HD)
    moved = [shifted(kv, h) for h in range(hops, 0, -1)]
    kv_mate = core_swap(kv)
    q_rows = q_rot.reshape(rows, local, heads * HD)
    order = Order()
    flat_tokens = tokens.reshape(total, width)
    dps = lax.axis_size("dp")
    near_pair = dps == 2 and seqs == 4
    part = width // dps
    share = part // seqs
    gate_t, up_t, down_t = gate_weight.T, up_weight.T, down_weight.T
    units = gate_t.shape[0]
    tiles = -(-units // TILE)
    cut = (tiles + 1) // 2
    long = -(-2 * tiles // 3)
    one, two = seq_index ^ 1, seq_index ^ 2
    three = seq_index ^ 3
    quad = jnp.stack([one, three, seq_index, two])

    begin = (dp_index * seqs + seq_index) * share

    def rows_of(value):
        return lax.dynamic_slice_in_dim(value, begin, share, 0)

    class Rows:
        def __init__(self, lefts, rights, parts, tile=TILE, sent=None):
            self.args = (order, lefts, rights, parts)
            self.tile = tile
            if not near_pair:
                (whole,) = share_of(*self.args, width, 0, tile)
                self.whole = lax.psum_scatter(whole, ("dp", "seq"), scatter_dimension=0, tiled=True)
                return
            if sent is None:
                (sent,) = share_of(*self.args, part, 1 - dp_index, tile)
            self.come = lax.ppermute(sent, "dp", flipped("dp", 0))

        def own(self):
            if near_pair:
                send, self.keep = share_of(*self.args, part, dp_index, self.tile, self.come, quad)
                self.come = lax.ppermute(send, "seq", flipped("seq", 0))

        def relay(self):
            if near_pair:
                sent = relay(order, self.keep, self.come, share)
                self.last = lax.ppermute(sent, "seq", flipped("seq", 1))

        def settled(self):
            if near_pair:
                order.arrived(self.last)

        def result(self):
            return [self.keep, self.come, self.last] if near_pair else [self.whole]

    class SeqFirst(Rows):
        def __init__(self, lefts, rights, parts, tile=TILE):
            if not near_pair:
                super().__init__(lefts, rights, parts, tile)
                return
            (whole,) = share_of(order, lefts, rights, parts, width, 0, tile, None, None, (dps, seqs))
            self.mine = lax.psum_scatter(whole, "seq", scatter_dimension=0, tiled=True)

        def across(self):
            if near_pair:
                sent = lax.dynamic_slice_in_dim(self.mine, (1 - dp_index) * share, share, 0)
                self.mine = lax.dynamic_slice_in_dim(self.mine, dp_index * share, share, 0)
                order.arrived(sent, self.mine)
                self.come = lax.ppermute(sent, "dp", flipped("dp", 0))

        def settled(self):
            if near_pair:
                order.arrived(self.come)

        def result(self):
            return [self.mine, self.come] if near_pair else [self.whole]

    class Scattered(Rows):
        def own(self):
            if near_pair:
                (mine,) = share_of(*self.args, part, dp_index, self.tile, self.come)
                self.whole = lax.psum_scatter(mine, "seq", scatter_dimension=0, tiled=True)

        def settled(self):
            order.arrived(self.whole)

        def result(self):
            return [self.whole]

    gate_rows, up_rows = rows_of(gate_weight), rows_of(up_weight)
    order.arrived(kv)
    grad_ffn, grad_ffn_t = grad_out_of(
        order, core_one, cotangent.reshape(total, width), valid.reshape(total, 1)
    )
    grad_hidden = grad_hidden_of(order, grad_ffn, down_t)
    h_one_t = turn(order, [h_one])
    moved = pass_on(order, moved)
    span, mate = [moved, kv], [core_swap(moved), kv_mate]
    mixed_rows, lse = attend(order, low, core_one, q_rows, start, span, mate)
    mixed = mixed_rows.reshape(total, heads * HD)
    sent = core_swaps(narrow(order, [(half_of(mixed, 1), o_weight)], (), 1))
    mine = narrow(order, [(half_of(mixed, 0), o_weight)], sent, 1)
    come = chip_swaps(mine)
    order.arrived(gate_rows, up_rows)
    middle, h_two, ffn = [], [], []
    for i in range(PIECES):
        middle_part, *h_pair = middle_of(order, core_one, flat_tokens, mine[i], come[i], gain_two, i)
        middle.append(middle_part)
        h_pair += core_swaps(h_pair)
        h_two += h_pair
        ffn.append(gated(order, h_pair, grad_hidden, i, gate_t, up_t))
    hidden, grad_gate, grad_up = (list(parts) for parts in zip(*ffn))

    down_b = SeqFirst([grad_ffn_t], [hidden], [(0, 0, cut, tiles - cut, 0)])
    down_a = Rows([grad_ffn_t], [hidden], [(0, 0, 0, cut, 0)])
    sent = core_swaps(
        narrow(order, [(sides_of(grad_gate, 1), gate_t), (sides_of(grad_up, 1), up_t)])
    )
    mine = narrow(order, [(sides_of(grad_gate, 0), gate_t), (sides_of(grad_up, 0), up_t)], sent)
    come = chip_swaps(mine)
    h_two_t = turn(order, h_two)
    if near_pair:
        sends = share_of(
            order,
            [h_two_t],
            [grad_gate, grad_up],
            [(0, 0, 0, tiles, 0), (0, 1, 0, long, 1), (0, 1, long, tiles - long, 2)],
            part,
            1 - dp_index,
            TILE,
        )
    else:
        sends = [None] * 3

    def half_rows(kind, right, begin, end, sent):
        return kind([h_two_t], [right], [(0, 0, begin, end - begin, 0)], TILE, sent)

    gate = half_rows(Scattered, grad_gate, 0, tiles, sends[0])
    up_a = half_rows(Rows, grad_up, 0, long, sends[1])
    up_b = half_rows(Rows, grad_up, long, tiles, sends[2])
    down_a.own()
    grad_middle, *branch = norm_back(order, core_one, mine, come, middle, gain_two, grad_ffn, False)
    branch += core_swaps(branch)
    grad_mixed = mixed_back(order, branch, o_weight).reshape(rows, local, heads * HD)
    grad_q_rows, keep, sent = attend_back(
        order, low, core_one, q_rows, start, span, mate, grad_mixed, mixed_rows, lse, cosine, sine
    )
    both_come = core_swap(sent)
    branch_t = turn(order, branch)
    own_kv, *pieces = fold(order, keep, both_come, local)
    moving = shifted(pieces[-1], -1) if pieces else None
    ffn_sent = core_swaps(narrow(order, [(sides_of(hidden, 1), down_t)]))
    for piece in pieces[-2::-1]:
        moving = shifted(carry(order, piece, moving), -1)
    grad_qkv, bias_sum = join(
        order, core_one, grad_q_rows, own_kv, [] if moving is None else [moving], cosine, sine
    )
    sent = core_swaps(narrow(order, [(half_of(grad_qkv, 1), weight)], (), 1))
    last_parts = [(0, 0, 0, grad_qkv.shape[1] // HD, 0), (1, 1, 0, heads, 0)]
    last = Rows([h_one_t, branch_t], [[grad_qkv], [mixed]], last_parts, HD)
    mine = narrow(order, [(half_of(grad_qkv, 0), weight)], sent, 1)
    come = chip_swaps(mine)
    down_b.across()
    down_a.relay()
    gate.own()
    ffn_mine = narrow(order, [(sides_of(hidden, 0), down_t)], ffn_sent)
    token = norm_back(order, core_one, mine, come, flat_tokens, gain_one, grad_middle, True)
    token += core_swaps(token)
    ffn_come = chip_swaps(ffn_mine)
    up_a.own()
    token_grad = place(order, core_one, token).reshape(rows, local, width)
    down_a.settled()
    layer = layer_of(order, middle, ffn_mine, ffn_come)
    layer += core_swaps(layer)
    last.own()
    layer_out = place(order, core_one, layer).reshape(rows, local, width)
    up_a.relay()
    up_b.own()
    down_b.settled()
    last.relay()
    (down_grad,) = finish(order, [down_a.result(), down_b.result()], share, units, TILE)
    if near_pair:
        bias_come = lax.ppermute(bias_sum, "dp", flipped("dp", 0))
        bias_all = bias_add(order, bias_sum, bias_come)
        bias_come = lax.ppermute(bias_all, "seq", flipped("seq", 0))
    up_b.relay()
    gate_grad, gate_term = finish(order, [gate.result()], share, units, TILE, gate_rows)
    wide_columns = grad_qkv.shape[1]
    (last_grad,) = finish(order, [last.result()], share, wide_columns + heads * HD, HD)
    if near_pair:
        bias_all = bias_add(order, bias_all, bias_come)
        bias_come = lax.ppermute(bias_all, "seq", flipped("seq", 1))
        bias_all = (bias_all + bias_come)[:1]
    else:
        bias_all = lax.psum(bias_sum[:1], ("dp", "seq"))
    up_grad, up_term = finish(order, [up_a.result(), up_b.result()], share, units, TILE, up_rows)
    qkv_grad, o_grad = last_grad[:, :wide_columns], last_grad[:, wide_columns:]

    attn_term = jnp.sum(to_f(rows_of(weight)) * qkv_grad, axis=1)
    ffn_term = jnp.sum(gate_term + up_term, axis=1)
    columns = heads * HD
    room = -(-share // HD) * HD - share
    terms = jnp.pad(jnp.stack([ffn_term, attn_term]), ((0, 0), (0, room))).reshape(-1, HD)
    packed = jnp.concatenate([qkv_grad[:, columns:], bias_all.reshape(-1, HD), terms], axis=0)
    gathered = tensor_gather(packed, rank)
    term_rows = terms.shape[0]
    bias_count = bias_all.shape[1] // HD
    terms = gathered[:, share + bias_count :].reshape(ranks, 2, -1)[:, :, :share]
    ffn_gain_grad, attn_gain_grad = terms[0] + terms[1] + (terms[2] + terms[3])
    attn_gain_grad = attn_gain_grad / lax.dynamic_slice_in_dim(gain_one[0], begin, share, 0)
    ffn_gain_grad = ffn_gain_grad / lax.dynamic_slice_in_dim(gain_two[0], begin, share, 0)
    q_grad = qkv_grad[:, :columns]
    kv_parts = lax.dynamic_slice_in_dim(gathered, rank * (share // ranks), share // ranks, 1)
    k_grad = jnp.concatenate([kv_parts[2 * i] for i in range(KVH)], axis=1)
    v_grad = jnp.concatenate([kv_parts[2 * i + 1] for i in range(KVH)], axis=1)
    biases = gathered[:, share : share + bias_count]
    q_bias_grad = biases[:, :heads].reshape(-1)
    k_bias_grad = biases[0::2, heads].reshape(-1)
    v_bias_grad = biases[1::2, heads].reshape(-1)
    return (
        layer_out,
        token_grad,
        q_grad,
        q_bias_grad,
        k_grad,
        k_bias_grad,
        v_grad,
        v_bias_grad,
        o_grad,
        attn_gain_grad,
        ffn_gain_grad,
        gate_grad,
        up_grad,
        down_grad,
    )


def solution(mesh):
    in_specs = (
        P("dp", "seq", None),
        P("dp", None),
        P("dp", "seq", None),
        P(None, "tensor"),
        P("tensor"),
        P(),
        P(),
        P(),
        P(),
        P(None, "tensor"),
        P(),
        P(),
        P(None, "tensor"),
        P(None, "tensor"),
        P(None, "tensor"),
    )
    out_specs = (
        P("dp", "seq", None),
        P("dp", "seq", None),
        P(("dp", "seq"), "tensor"),
        P(),
        P(("dp", "seq", "tensor"), None),
        P(),
        P(("dp", "seq", "tensor"), None),
        P(),
        P(("dp", "seq"), "tensor"),
        P(("dp", "seq")),
        P(("dp", "seq")),
        P(("dp", "seq"), "tensor"),
        P(("dp", "seq"), "tensor"),
        P(("dp", "seq"), "tensor"),
    )
    return jax.shard_map(body, mesh=mesh, in_specs=in_specs, out_specs=out_specs, check_vma=False)
```

```python
import functools
import math

import jax
import jax.numpy as jnp
from jax import lax
from jax.experimental import pallas as pl
from jax.experimental.pallas import tpu as pltpu
from jax.sharding import PartitionSpec as P

KVH = 2
HD = 128
MOST = 1024
EPS = 1e-06
ROPE_BASE = 10000.0
NEG_FILL = -1e30
Q_BLOCK = 256
K_BLOCK = 256
MIB = 1 << 20
LIGHT = 1000
TILE = 256
PIECES = 2
SCALE = 1.0 / math.sqrt(HD)


def to_bf(value):
    return value.astype(jnp.bfloat16)


def to_f(value):
    return value.astype(jnp.float32)


def dot(left, right, left_dim=1, right_dim=0):
    return lax.dot_general(
        left,
        right,
        (((left_dim,), (right_dim,)), ((), ())),
        preferred_element_type=jnp.float32,
    )


def flipped(axis, bit):
    return [(i, i ^ (1 << bit)) for i in range(lax.axis_size(axis))]


def core_swap(value):
    return lax.ppermute(value, "tensor", flipped("tensor", 0))


def chip_swap(value):
    return lax.ppermute(value, "tensor", flipped("tensor", 1))


def core_swaps(values):
    return [core_swap(value) for value in values]


def chip_swaps(values):
    return [chip_swap(value) for value in values]


def shifted(value, hops):
    count = lax.axis_size("seq")
    route = [(i, i + hops) for i in range(count) if 0 <= i + hops < count]
    return lax.ppermute(value, "seq", route)


def cost(flops, read):
    return pl.CostEstimate(flops=flops // LIGHT, bytes_accessed=read // LIGHT, transcendentals=0)


class Order:
    def __init__(self):
        self.mark = None
        self.touched = []

    def arrived(self, *values):
        self.touched.extend(values)

    def __call__(self, kernel, args, in_specs, out_specs, out_shape, grid, flops, read, name, scalars=(), scratch=()):
        anchor = ([] if self.mark is None else [self.mark]) + self.touched
        self.touched = []
        count = len(scalars) + len(args)
        outs = len(out_shape)

        def run(*refs):
            rest = refs[count + len(anchor) :]
            kernel(*refs[:count], *rest[:outs], *rest[outs + 1 :])
            rest[outs][...] = jnp.zeros(rest[outs].shape, jnp.float32)

        *results, self.mark = pl.pallas_call(
            run,
            grid_spec=pltpu.PrefetchScalarGridSpec(
                num_scalar_prefetch=len(scalars),
                grid=grid,
                in_specs=list(in_specs) + anchors(len(anchor)),
                out_specs=list(out_specs) + [mark_spec()],
                scratch_shapes=list(scratch),
            ),
            out_shape=list(out_shape) + [MARK],
            compiler_params=pltpu.CompilerParams(vmem_limit_bytes=32 * MIB),
            cost_estimate=cost(flops, read),
            name=name,
        )(*scalars, *args, *anchor)
        return results


def first_kernel(core_ref, tok_ref, gain_ref, w_ref, b_ref, cos_ref, sin_ref, h_ref, q_ref, kv_ref):
    x = to_f(tok_ref[...])
    factor = lax.rsqrt(jnp.mean(x * x, axis=-1, keepdims=True) + EPS)
    h = to_bf(x * factor * gain_ref[...])
    h_ref[...] = h
    lin = dot(h, w_ref[...]) + b_ref[...]
    cosine = cos_ref[...]
    sine = sin_ref[...]
    heads = q_ref.shape[1] // HD
    for head in range(heads):
        part = lin[:, head * HD : (head + 1) * HD]
        q_ref[:, head * HD : (head + 1) * HD] = to_bf(
            part * cosine + pltpu.roll(part, HD // 2, 1) * sine
        )
    part = lin[:, heads * HD :]
    is_key = core_ref[0] == 0
    kv_ref[...] = to_bf(
        part * jnp.where(is_key, cosine, 1.0)
        + pltpu.roll(part, HD // 2, 1) * jnp.where(is_key, sine, 0.0)
    )


def first(core, tokens, gain, weight, bias, cosine, sine):
    total, width = tokens.shape
    columns = weight.shape[1]
    block = total // 4
    half = 2

    def flip(i, core_ref):
        return (lax.rem(i + core_ref[0] * half, 4), 0)

    def at(i, core_ref):
        return (i, 0)

    def whole(i, core_ref):
        return (0, 0)

    return pl.pallas_call(
        first_kernel,
        grid_spec=pltpu.PrefetchScalarGridSpec(
            num_scalar_prefetch=1,
            grid=(4,),
            in_specs=[
                pl.BlockSpec((block, width), flip),
                pl.BlockSpec((1, width), whole),
                pl.BlockSpec((width, columns), whole),
                pl.BlockSpec((1, columns), whole),
                pl.BlockSpec((block, HD), at),
                pl.BlockSpec((block, HD), at),
            ],
            out_specs=[
                pl.BlockSpec((block, width), at),
                pl.BlockSpec((block, columns - HD), at),
                pl.BlockSpec((block, HD), at),
            ],
        ),
        out_shape=[
            jax.ShapeDtypeStruct((total, width), jnp.bfloat16),
            jax.ShapeDtypeStruct((total, columns - HD), jnp.bfloat16),
            jax.ShapeDtypeStruct((total, HD), jnp.bfloat16),
        ],
        compiler_params=pltpu.CompilerParams(vmem_limit_bytes=32 * MIB),
        cost_estimate=cost(2 * total * width * columns, 9 * MIB),
        name="first",
    )(core, tokens, gain, weight, bias, cosine, sine)


def stacked(ref, start, count, heads):
    return jnp.concatenate(
        [ref[0, pl.ds(start, count), h * HD : (h + 1) * HD] for h in range(heads)], axis=0
    )


def bounds(start_ref, index, heads, reach):
    first_key = jnp.concatenate(
        [start_ref[0, :, pl.ds(index * Q_BLOCK, Q_BLOCK)]] * heads, axis=1
    )
    place = reach + index * Q_BLOCK + lax.broadcasted_iota(jnp.int32, (1, Q_BLOCK), 1)
    return first_key, jnp.concatenate([place] * heads, axis=1)


def gather_span(core, refs, span):
    count = len(refs) // 2
    local = refs[0].shape[1]
    for i in range(count):
        here = slice(i * local, (i + 1) * local)
        span[core, here] = refs[i][0]
        span[1 - core, here] = refs[count + i][0]


def attend_kernel(heads, blocks, pieces, low_ref, core_ref, q_ref, start_ref, *refs):
    o_ref, lse_ref, acc, span = refs[2 * pieces :]
    row = pl.program_id(0)
    wide = heads * Q_BLOCK
    reach = (pieces - 1) * q_ref.shape[1]
    gather_span(core_ref[0], refs[: 2 * pieces], span)
    for index in range(blocks):
        q = stacked(q_ref, index * Q_BLOCK, Q_BLOCK, heads)
        first_key, place = bounds(start_ref, index, heads, reach)
        acc[...] = jnp.zeros_like(acc)

        def step(j, carry):
            top, total = carry
            keys = pl.ds(pl.multiple_of(j * K_BLOCK, K_BLOCK), K_BLOCK)
            s = dot(span[0, keys], q, 1, 1) * SCALE
            key = j * K_BLOCK + lax.broadcasted_iota(jnp.int32, (K_BLOCK, wide), 0)
            s = jnp.where((key >= first_key) & (key <= place), s, NEG_FILL)
            later = jnp.maximum(top, jnp.max(s, axis=0, keepdims=True))
            p = jnp.exp(s - later)
            fade = jnp.exp(top - later)
            total = total * fade + jnp.sum(p, axis=0, keepdims=True)
            acc[...] = acc[...] * fade + dot(span[1, keys], to_bf(p), 0, 0)
            return later, total

        last = (reach + (index + 1) * Q_BLOCK - 1) // K_BLOCK + 1
        top, total = lax.fori_loop(
            low_ref[row, index],
            last,
            step,
            (jnp.full((1, wide), NEG_FILL, jnp.float32), jnp.zeros((1, wide), jnp.float32)),
        )
        out = to_bf((acc[...] / total).T)
        for h in range(heads):
            o_ref[0, index * Q_BLOCK : (index + 1) * Q_BLOCK, h * HD : (h + 1) * HD] = out[
                h * Q_BLOCK : (h + 1) * Q_BLOCK
            ]
        lse_ref[0, index : index + 1, :] = top + jnp.log(total)


def span_specs(rows, local, pieces):
    near = pl.BlockSpec((1, local, HD), lambda i, *refs: (i, 0, 0))
    far = pl.BlockSpec((1, local, HD), lambda i, *refs: (lax.rem(i + rows // 2, rows), 0, 0))
    return [near] * pieces + [far] * pieces


def attend(low, core, q, start, span, mate):
    rows, local, columns = q.shape
    pieces = len(span)
    heads = columns // HD
    blocks = local // Q_BLOCK

    def at(i, *refs):
        return (i, 0, 0)

    return pl.pallas_call(
        functools.partial(attend_kernel, heads, blocks, pieces),
        grid_spec=pltpu.PrefetchScalarGridSpec(
            num_scalar_prefetch=2,
            grid=(rows,),
            in_specs=[pl.BlockSpec((1, local, columns), at), pl.BlockSpec((1, 1, local), at)]
            + span_specs(rows, local, pieces),
            out_specs=[
                pl.BlockSpec((1, local, columns), at),
                pl.BlockSpec((1, blocks, heads * Q_BLOCK), at),
            ],
            scratch_shapes=[
                pltpu.VMEM((HD, heads * Q_BLOCK), jnp.float32),
                pltpu.VMEM((2, pieces * local, HD), jnp.bfloat16),
            ],
        ),
        out_shape=[
            jax.ShapeDtypeStruct((rows, local, columns), jnp.bfloat16),
            jax.ShapeDtypeStruct((rows, blocks, heads * Q_BLOCK), jnp.float32),
        ],
        compiler_params=pltpu.CompilerParams(vmem_limit_bytes=32 * MIB),
        cost_estimate=cost(8_000_000_000, 4 * MIB),
        name="attend",
    )(low, core, q, start, *span, *mate)


def attend_back_kernel(
    heads, blocks, pieces, low_ref, core_ref, q_ref, start_ref, g_ref, o_ref, lse_ref, cos_ref, sin_ref, *refs
):
    gq_ref, keep_ref, send_ref, acc, gk, gv, span = refs[2 * pieces :]
    row = pl.program_id(0)
    wide = heads * Q_BLOCK
    reach = (pieces - 1) * q_ref.shape[1]
    core = core_ref[0]
    gather_span(core, refs[: 2 * pieces], span)
    gk[...] = jnp.zeros_like(gk)
    gv[...] = jnp.zeros_like(gv)
    for index in range(blocks):
        q = stacked(q_ref, index * Q_BLOCK, Q_BLOCK, heads)
        g = stacked(g_ref, index * Q_BLOCK, Q_BLOCK, heads)
        o = stacked(o_ref, index * Q_BLOCK, Q_BLOCK, heads)
        inner = jnp.sum((to_f(g) * to_f(o)).T, axis=0, keepdims=True)
        lse = lse_ref[0, index : index + 1, :]
        first_key, place = bounds(start_ref, index, heads, reach)
        acc[...] = jnp.zeros_like(acc)

        def step(j, carry):
            keys = pl.ds(pl.multiple_of(j * K_BLOCK, K_BLOCK), K_BLOCK)
            k = span[0, keys]
            s = dot(k, q, 1, 1) * SCALE
            key = j * K_BLOCK + lax.broadcasted_iota(jnp.int32, (K_BLOCK, wide), 0)
            p = jnp.where((key >= first_key) & (key <= place), jnp.exp(s - lse), 0.0)
            gp = dot(span[1, keys], g, 1, 1)
            gs = to_bf(p * (gp - inner))
            gv[keys] += dot(to_bf(p), g)
            gk[keys] += dot(gs, q)
            acc[...] += dot(k, gs, 0, 0)
            return carry

        last = (reach + (index + 1) * Q_BLOCK - 1) // K_BLOCK + 1
        lax.fori_loop(low_ref[row, index], last, step, 0)
        gq = acc[...].T * SCALE
        here = slice(index * Q_BLOCK, (index + 1) * Q_BLOCK)
        cosine, sine = cos_ref[here], sin_ref[here]
        for h in range(heads):
            part = gq[h * Q_BLOCK : (h + 1) * Q_BLOCK]
            gq_ref[0, here, h * HD : (h + 1) * HD] = to_bf(
                part * cosine + pltpu.roll(part * sine, HD // 2, 1)
            )
    is_key = core == 0
    keys, values = gk[...] * SCALE, gv[...]
    keep_ref[0] = to_bf(jnp.where(is_key, keys, values))
    send_ref[0] = to_bf(jnp.where(is_key, values, keys))


def attend_back(order, low, core, q, start, span, mate, grad, out, lse, cosine, sine):
    rows, local, columns = q.shape
    pieces = len(span)
    window = pieces * local
    heads = columns // HD
    blocks = local // Q_BLOCK

    def at(i, *refs):
        return (i, 0, 0)

    table = pl.BlockSpec((local, HD), lambda i, *refs: (i, 0))
    tokens = pl.BlockSpec((1, local, columns), at)
    return order(
        functools.partial(attend_back_kernel, heads, blocks, pieces),
        [q, start, grad, out, lse, cosine, sine, *span, *mate],
        [
            tokens,
            pl.BlockSpec((1, 1, local), at),
            tokens,
            tokens,
            pl.BlockSpec((1, blocks, heads * Q_BLOCK), at),
            table,
            table,
        ]
        + span_specs(rows, local, pieces),
        [tokens, pl.BlockSpec((1, window, HD), at), pl.BlockSpec((1, window, HD), at)],
        [
            jax.ShapeDtypeStruct((rows, local, columns), jnp.bfloat16),
            jax.ShapeDtypeStruct((rows, window, HD), jnp.bfloat16),
            jax.ShapeDtypeStruct((rows, window, HD), jnp.bfloat16),
        ],
        (rows,),
        20_000_000_000,
        6 * MIB,
        "attend_back",
        scalars=(low, core),
        scratch=[
            pltpu.VMEM((HD, heads * Q_BLOCK), jnp.float32),
            pltpu.VMEM((window, HD), jnp.float32),
            pltpu.VMEM((window, HD), jnp.float32),
            pltpu.VMEM((2, window, HD), jnp.bfloat16),
        ],
    )


def fold_kernel(keep_ref, come_ref, own_ref, *send_refs):
    local = own_ref.shape[1]
    total = to_f(keep_ref[0]) + to_f(come_ref[0])
    reach = total.shape[0] - local
    own_ref[0] = total[reach:]
    for hop, ref in enumerate(send_refs, 1):
        ref[0] = to_bf(total[reach - hop * local : reach - (hop - 1) * local])


def fold(order, keep, come, local):
    rows, window = keep.shape[:2]
    hops = window // local - 1
    out = pl.BlockSpec((1, local, HD), lambda i: (i, 0, 0))
    return order(
        fold_kernel,
        [keep, come],
        [
            pl.BlockSpec((1, window, HD), lambda i: (i, 0, 0)),
            pl.BlockSpec((1, window, HD), lambda i: (lax.rem(i + rows // 2, rows), 0, 0)),
        ],
        [out] * (hops + 1),
        [jax.ShapeDtypeStruct((rows, local, HD), jnp.float32)]
        + [jax.ShapeDtypeStruct((rows, local, HD), jnp.bfloat16)] * hops,
        (rows,),
        0,
        4 * MIB,
        "fold",
    )


def carry_kernel(piece_ref, come_ref, out_ref):
    out_ref[...] = to_bf(to_f(piece_ref[...]) + to_f(come_ref[...]))


def carry(order, piece, come):
    rows, local, columns = piece.shape
    at = pl.BlockSpec((1, local, columns), lambda i: (i, 0, 0))
    return order(
        carry_kernel,
        [piece, come],
        [at, at],
        [at],
        [jax.ShapeDtypeStruct(piece.shape, jnp.bfloat16)],
        (rows,),
        0,
        2 * MIB,
        "carry",
    )[0]


def bias_kernel(left_ref, right_ref, out_ref):
    out_ref[...] = left_ref[...] + right_ref[...]


def bias_add(order, left, right):
    whole = pl.BlockSpec(left.shape, lambda i: (0, 0))
    return order(
        bias_kernel,
        [left, right],
        [whole, whole],
        [whole],
        [jax.ShapeDtypeStruct(left.shape, jnp.float32)],
        (1,),
        0,
        MIB,
        "bias",
    )[0]


def join_kernel(hops, core_ref, gq_ref, cos_ref, sin_ref, own_ref, *refs):
    out_ref, sum_ref = refs[-2:]
    columns = gq_ref.shape[2]
    grad = own_ref[0]
    for ref in refs[:hops]:
        grad = grad + to_f(ref[0])
    is_key = core_ref[0] == 0
    cosine = jnp.where(is_key, cos_ref[...], 1.0)
    sine = jnp.where(is_key, sin_ref[...], 0.0)
    kv = to_bf(grad * cosine + pltpu.roll(grad * sine, HD // 2, 1))
    q = gq_ref[0]
    out_ref[:, :columns] = q
    out_ref[:, columns:] = kv

    @pl.when(pl.program_id(0) == 0)
    def _():
        sum_ref[...] = jnp.zeros(sum_ref.shape, jnp.float32)

    sum_ref[:, :columns] += jnp.sum(to_f(q), axis=0, keepdims=True)
    sum_ref[:, columns:] += jnp.sum(to_f(kv), axis=0, keepdims=True)


def join(order, core, grad_q, own, comes, cosine, sine):
    rows, local, columns = grad_q.shape
    wide = columns + HD

    def at(i, *refs):
        return (i, 0, 0)

    piece = pl.BlockSpec((1, local, HD), at)
    table = pl.BlockSpec((local, HD), lambda i, *refs: (i, 0))
    return order(
        functools.partial(join_kernel, len(comes)),
        [grad_q, cosine, sine, own, *comes],
        [pl.BlockSpec((1, local, columns), at), table, table, piece] + [piece] * len(comes),
        [
            pl.BlockSpec((local, wide), lambda i, *refs: (i, 0)),
            pl.BlockSpec((8, wide), lambda i, *refs: (0, 0)),
        ],
        [
            jax.ShapeDtypeStruct((rows * local, wide), jnp.bfloat16),
            jax.ShapeDtypeStruct((8, wide), jnp.float32),
        ],
        (rows,),
        0,
        4 * MIB,
        "join",
        scalars=(core,),
    )


def mixed_back_kernel(w_ref, *refs):
    rows = refs[0].shape[0]
    for i, ref in enumerate(refs[:-1]):
        refs[-1][i * rows : (i + 1) * rows] = to_bf(dot(ref[...], w_ref[...]))


def mixed_back(order, pieces, weight):
    rows, width = pieces[0].shape
    total = rows * len(pieces)
    columns = weight.shape[1]

    def whole(i):
        return (0, 0)

    return order(
        mixed_back_kernel,
        [weight, *pieces],
        [pl.BlockSpec((width, columns), whole)] + [pl.BlockSpec((rows, width), whole)] * len(pieces),
        [pl.BlockSpec((total, columns), whole)],
        [jax.ShapeDtypeStruct((total, columns), jnp.bfloat16)],
        (1,),
        2 * total * width * columns,
        6 * MIB,
        "mixed_back",
    )[0]


def place_kernel(core_ref, *refs):
    for i, ref in enumerate(refs[:-1]):

        @pl.when(pl.program_id(0) == i)
        def _(ref=ref):
            refs[-1][...] = ref[...]


def place(order, core, pieces):
    rows, width = pieces[0].shape
    count = len(pieces)
    return order(
        place_kernel,
        list(pieces),
        [pl.BlockSpec((rows, width), lambda i, core_ref: (0, 0))] * count,
        [pl.BlockSpec((rows, width), lambda i, core_ref: (lax.rem(i + core_ref[0] * (count // 2), count), 0))],
        [jax.ShapeDtypeStruct((rows * count, width), pieces[0].dtype)],
        (count,),
        0,
        8 * rows * width,
        "place",
        scalars=(core,),
    )[0]


def anchors(count):
    return [pl.BlockSpec(memory_space=pl.ANY)] * count


MARK = jax.ShapeDtypeStruct((8, HD), jnp.float32)


def mark_spec():
    return pl.BlockSpec((8, HD), lambda *refs: (0, 0))


def grad_hidden_kernel(g_ref, w_ref, out_ref):
    out_ref[...] = to_bf(dot(g_ref[...], w_ref[...], 1, 1))


def grad_hidden_of(order, grad, weight):
    total, width = grad.shape
    hidden = weight.shape[0]
    return order(
        grad_hidden_kernel,
        [grad, weight],
        [pl.BlockSpec((total, width), lambda i: (0, 0)), pl.BlockSpec((TILE, width), lambda i: (i, 0))],
        [pl.BlockSpec((total, TILE), lambda i: (0, i))],
        [jax.ShapeDtypeStruct((total, hidden), jnp.bfloat16)],
        (pl.cdiv(hidden, TILE),),
        2 * total * width * hidden,
        15 * MIB,
        "grad_hidden",
    )[0]


def gated_kernel(gh_ref, gw_ref, uw_ref, *refs):
    hid_ref, gg_ref, gu_ref = refs[-3:]
    rows = refs[0].shape[0]
    for part, ref in enumerate(refs[:-3]):
        here = slice(part * rows, (part + 1) * rows)
        h = ref[...]
        gate = dot(h, gw_ref[...], 1, 1)
        up = dot(h, uw_ref[...], 1, 1)
        grad = to_f(gh_ref[here])
        sigma = 1.0 / (1.0 + jnp.exp(-gate))
        swish = gate * sigma
        hid_ref[here] = to_bf(swish * up)
        gu_ref[here] = to_bf(grad * swish)
        gg_ref[here] = to_bf(grad * up * sigma * (1.0 + gate * (1.0 - sigma)))


def gated(order, pieces, grad_hidden, gate_weight, up_weight):
    rows, width = pieces[0].shape
    total = rows * len(pieces)
    hidden = gate_weight.shape[0]
    column = pl.BlockSpec((total, TILE), lambda i: (0, i))
    weight = pl.BlockSpec((TILE, width), lambda i: (i, 0))
    shape = jax.ShapeDtypeStruct((total, hidden), jnp.bfloat16)
    return order(
        gated_kernel,
        [grad_hidden, gate_weight, up_weight, *pieces],
        [column, weight, weight] + [pl.BlockSpec((rows, width), lambda i: (0, 0))] * len(pieces),
        [column] * 3,
        [shape] * 3,
        (pl.cdiv(hidden, TILE),),
        4 * total * width * hidden,
        30 * MIB,
        "gated",
    )


def share_kernel(plan, lefts, rights, extra, halves, groups, pick_ref, blocks_ref, *refs):
    step = pl.program_id(0)
    left_refs, right_refs = refs[:lefts], refs[lefts : lefts + rights]
    refs = refs[lefts + rights :]
    if extra:
        extra_ref, refs = refs[0], refs[1:]
    for left, right, begin, end, shift, columns, target in plan:

        @pl.when((step >= begin) & (step < end))
        def _(left=left, right=right, shift=shift, columns=columns, target=target):
            out = dot(left_refs[left][...], right_refs[right][...])
            if extra:
                out = out + to_f(extra_ref[...])
            tile = out.shape[1]
            spot = (step + shift) * tile + lax.broadcasted_iota(jnp.int32, (1, tile), 1)
            out = to_bf(jnp.where(spot < columns, out, 0.0))
            if groups:
                share = out.shape[0] // (groups[0] * groups[1])
                for i in range(groups[0]):
                    for j in range(groups[1]):
                        here = (j * groups[0] + i) * share
                        there = (i * groups[1] + j) * share
                        refs[target][here : here + share] = out[there : there + share]
                return
            if not halves:
                refs[target][...] = out
                return
            send_ref, keep_ref, rows = refs
            rows[...] = out
            share = send_ref.shape[0] // (2 * halves)
            for i in range(2 * halves):
                here = slice(i * share, (i + 1) * share)
                send_ref[here] = rows[pl.ds(pl.multiple_of(blocks_ref[i] * share, share), share)]
                keep_ref[here] = rows[pl.ds(pl.multiple_of(blocks_ref[2 * halves + i] * share, share), share)]


def clipped(rows, tile, begin, count, shift=0):
    return pl.BlockSpec((rows, tile), lambda i, *refs: (0, jnp.clip(i - begin, 0, count - 1) + shift))


def share_of(order, lefts, rights, parts, part, pick, tile, extra=None, blocks=None, groups=None):
    tokens = lefts[0].shape[1]
    plan, at = [], 0
    starts, sizes, right_at = {}, {}, {}
    for left, right, skip, count, target in parts:
        plan.append((left, right, at, at + count, skip - at, rights[right].shape[1], target))
        starts.setdefault(target, at)
        sizes[target] = sizes.get(target, 0) + count
        first, tiles, low = right_at.get(right, (at, 0, skip))
        right_at[right] = (first, tiles + count, low)
        at += count
    halves = 0
    extras = [] if extra is None else [extra]
    scratch = []
    if blocks is None:
        blocks = jnp.zeros((1,), jnp.int32)
        outs = [clipped(part, tile, starts[t], sizes[t]) for t in sorted(sizes)]
        shapes = [jax.ShapeDtypeStruct((part, sizes[t] * tile), jnp.bfloat16) for t in sorted(sizes)]
    else:
        halves = blocks.shape[0] // 4
        outs = [clipped(part // 2, tile, 0, at)] * 2
        shapes = [jax.ShapeDtypeStruct((part // 2, at * tile), jnp.bfloat16)] * 2
        scratch = [pltpu.VMEM((part, tile), jnp.bfloat16)]
    return order(
        functools.partial(share_kernel, plan, len(lefts), len(rights), len(extras), halves, groups),
        [*lefts, *rights, *extras],
        [pl.BlockSpec((part, tokens), lambda i, pick_ref, blocks_ref: (pick_ref[0], 0))] * len(lefts)
        + [clipped(tokens, tile, *right_at[r]) for r in range(len(rights))]
        + [clipped(part, tile, 0, at)] * len(extras),
        outs,
        shapes,
        (at,),
        2 * part * tokens * at * tile,
        2 * (part * tokens + (part + tokens) * at * tile),
        "share",
        scalars=(jnp.asarray(pick, jnp.int32).reshape(1), blocks),
        scratch=scratch,
    )


def relay_kernel(keep_ref, come_ref, out_ref):
    out_ref[...] = to_bf(to_f(keep_ref[...]) + to_f(come_ref[...]))


def relay(order, keep, come, share):
    rows, columns = keep.shape
    pair = pl.BlockSpec((share, columns), lambda i: (2 * i + 1, 0))
    return order(
        relay_kernel,
        [keep, come],
        [pair, pair],
        [pl.BlockSpec((share, columns), lambda i: (i, 0))],
        [jax.ShapeDtypeStruct((rows // 2, columns), jnp.bfloat16)],
        (rows // (2 * share),),
        0,
        3 * rows * columns,
        "relay",
    )[0]


def finish_kernel(plan, columns, gains, *refs):
    out_ref = refs[-2] if gains else refs[-1]
    step = pl.program_id(0)
    tile = out_ref.shape[1]
    for begin, end, first, count in plan:

        @pl.when((step >= begin) & (step < end))
        def _(first=first, count=count):
            out = to_f(refs[first][...])
            for ref in refs[first + 1 : first + count]:
                out = out + to_f(ref[...])
            out_ref[...] = out
            if gains:
                spot = step * tile + lax.broadcasted_iota(jnp.int32, (1, tile), 1)
                terms = jnp.where(spot < columns, out * to_f(refs[-3][...]), 0.0)
                total = terms[:, :HD]
                for i in range(HD, tile, HD):
                    total = total + terms[:, i : i + HD]

                @pl.when(step == 0)
                def _():
                    refs[-1][...] = total

                @pl.when(step > 0)
                def _():
                    refs[-1][...] += total


def finish(order, chunks, share, columns, tile, weight=None):
    plan, specs, args, at = [], [], [], 0
    for chunk in chunks:
        count = chunk[0].shape[1] // tile
        plan.append((at, at + count, len(args), len(chunk)))
        specs += [clipped(share, tile, at, count)] * len(chunk)
        args += chunk
        at += count
    column = pl.BlockSpec((share, tile), lambda i: (0, i))
    outs, shapes = [column], [jax.ShapeDtypeStruct((share, columns), jnp.float32)]
    if weight is not None:
        args.append(weight)
        specs.append(column)
        outs.append(pl.BlockSpec((share, HD), lambda i: (0, 0)))
        shapes.append(jax.ShapeDtypeStruct((share, HD), jnp.float32))
    return order(
        functools.partial(finish_kernel, plan, columns, weight is not None),
        args,
        specs,
        outs,
        shapes,
        (at,),
        0,
        14 * share * columns,
        "finish",
    )


def narrow_kernel(pairs, extras, right_dim, *refs):
    out = dot(refs[0][...], refs[1][...], 1, right_dim)
    for i in range(1, pairs):
        out = out + dot(refs[2 * i][...], refs[2 * i + 1][...], 1, right_dim)
    extra = refs[2 * pairs : 2 * pairs + extras]
    outs = refs[2 * pairs + extras :]
    if extras:
        out = out + jnp.concatenate([to_f(ref[...]) for ref in extra], axis=0)
    rows = outs[0].shape[0]
    for i, ref in enumerate(outs):
        ref[...] = to_bf(out[i * rows : (i + 1) * rows])


def narrow(order, pairs, index, extra=(), right_dim=0):
    total, hidden = pairs[0][0].shape
    width = pairs[0][1].shape[1 - right_dim]
    half = total // 2
    piece = half // PIECES
    column = pl.BlockSpec((piece, TILE), lambda i: (0, i))
    right = (
        pl.BlockSpec((TILE, hidden), lambda i: (i, 0))
        if right_dim
        else pl.BlockSpec((hidden, TILE), lambda i: (0, i))
    )
    return order(
        functools.partial(narrow_kernel, len(pairs), len(extra), right_dim),
        [item for pair in pairs for item in pair] + list(extra),
        [pl.BlockSpec((half, hidden), lambda i: (index, 0)), right] * len(pairs) + [column] * len(extra),
        [column] * PIECES,
        [jax.ShapeDtypeStruct((piece, width), jnp.bfloat16)] * PIECES,
        (width // TILE,),
        2 * len(pairs) * half * width * hidden,
        2 * len(pairs) * (half + width) * hidden + 2 * half * width,
        "narrow",
    )


def piece_specs(piece, width, block):
    steps = piece // block
    return [
        pl.BlockSpec((block, width), lambda i, *refs, j=j: (jnp.clip(i - j * steps, 0, steps - 1), 0))
        for j in range(PIECES)
    ]


def pick_piece(refs):
    value = refs[0][...]
    for j, ref in enumerate(refs[1:], 1):
        value = jnp.where(pl.program_id(0) >= 4 * j // len(refs), ref[...], value)
    return value


def put_piece(refs, value):
    steps = 4 // len(refs)
    for j, ref in enumerate(refs):

        @pl.when(lax.div(pl.program_id(0), steps) == j)
        def _(ref=ref):
            ref[...] = value


def turn_kernel(*refs):
    rows = refs[0].shape[0]
    for i, ref in enumerate(refs[:-1]):
        refs[-1][:, i * rows : (i + 1) * rows] = ref[...].T


def turn(order, pieces):
    rows, width = pieces[0].shape
    total = rows * len(pieces)
    return order(
        turn_kernel,
        list(pieces),
        [pl.BlockSpec((rows, TILE), lambda i: (0, i))] * len(pieces),
        [pl.BlockSpec((TILE, total), lambda i: (i, 0))],
        [jax.ShapeDtypeStruct((width, total), jnp.bfloat16)],
        (width // TILE,),
        0,
        4 * total * width,
        "turn",
    )[0]


def grad_out_kernel(core_ref, cot_ref, valid_ref, out_ref, turned_ref):
    out = to_bf(to_f(cot_ref[...]) * valid_ref[...])
    out_ref[...] = out
    turned_ref[...] = out.T


def grad_out_of(order, core, cotangent, valid):
    total, width = cotangent.shape
    block = total // 4
    return order(
        grad_out_kernel,
        [cotangent, valid],
        [
            pl.BlockSpec((block, width), lambda i, core_ref: (lax.rem(i + core_ref[0] * 2, 4), 0)),
            pl.BlockSpec((block, 1), lambda i, core_ref: (i, 0)),
        ],
        [
            pl.BlockSpec((block, width), lambda i, core_ref: (i, 0)),
            pl.BlockSpec((width, block), lambda i, core_ref: (0, i)),
        ],
        [
            jax.ShapeDtypeStruct((total, width), jnp.bfloat16),
            jax.ShapeDtypeStruct((width, total), jnp.bfloat16),
        ],
        (4,),
        0,
        6 * total * width,
        "grad_out",
        scalars=(core,),
    )


def middle_kernel(core_ref, tok_ref, gain_ref, *refs):
    mine, come = pick_piece(refs[:PIECES]), pick_piece(refs[PIECES : 2 * PIECES])
    mid_ref, *h_refs = refs[2 * PIECES :]
    middle = to_f(tok_ref[...]) + (to_f(mine) + to_f(come))
    factor = lax.rsqrt(jnp.mean(middle * middle, axis=-1, keepdims=True) + EPS)
    mid_ref[...] = middle
    put_piece(h_refs, to_bf(middle * factor * gain_ref[...]))


def middle_of(order, core, tokens, mine, come, gain):
    piece, width = mine[0].shape
    half = piece * PIECES
    block = half // 4
    specs = piece_specs(piece, width, block)
    middle, *h = order(
        middle_kernel,
        [tokens, gain, *mine, *come],
        [
            pl.BlockSpec((block, width), lambda i, core_ref: (core_ref[0] * 4 + i, 0)),
            pl.BlockSpec((1, width), lambda i, core_ref: (0, 0)),
        ]
        + specs * 2,
        [pl.BlockSpec((block, width), lambda i, core_ref: (i, 0))] + specs,
        [jax.ShapeDtypeStruct((half, width), jnp.float32)]
        + [jax.ShapeDtypeStruct((piece, width), jnp.bfloat16)] * PIECES,
        (4,),
        0,
        9 * MIB,
        "middle",
        scalars=(core,),
    )
    return middle, h


def norm_back_kernel(core_ref, x_ref, gain_ref, up_ref, *refs):
    mine, come = pick_piece(refs[:PIECES]), pick_piece(refs[PIECES : 2 * PIECES])
    outs = refs[2 * PIECES :]
    grad = to_f(mine) + to_f(come)
    x = to_f(x_ref[...])
    factor = lax.rsqrt(jnp.mean(x * x, axis=-1, keepdims=True) + EPS)
    normed = x * factor
    weighted = grad * gain_ref[...]
    inner = jnp.mean(weighted * normed, axis=-1, keepdims=True)
    out = to_f(up_ref[...]) + factor * (weighted - normed * inner)
    if len(outs) > PIECES:
        outs[0][...] = out
        put_piece(outs[1:], to_bf(out))
    else:
        put_piece(outs, out)


def norm_back(order, core, mine, come, x, gain, up, by_core):
    piece, width = mine[0].shape
    half = piece * PIECES
    block = half // 4
    at = pl.BlockSpec((block, width), lambda i, core_ref: (i, 0))
    picked = pl.BlockSpec((block, width), lambda i, core_ref: (core_ref[0] * 4 + i, 0))
    specs = piece_specs(piece, width, block)
    if by_core:
        shapes = [jax.ShapeDtypeStruct((piece, width), jnp.float32)] * PIECES
    else:
        shapes = [jax.ShapeDtypeStruct((half, width), jnp.float32)]
        shapes += [jax.ShapeDtypeStruct((piece, width), jnp.bfloat16)] * PIECES
    return order(
        norm_back_kernel,
        [x, gain, up, *mine, *come],
        [picked if by_core else at, pl.BlockSpec((1, width), lambda i, core_ref: (0, 0)), at] + specs * 2,
        specs if by_core else [at] + specs,
        shapes,
        (4,),
        0,
        10 * MIB,
        "norm_back",
        scalars=(core,),
    )


def layer_kernel(middle_ref, *refs):
    mine, come = pick_piece(refs[:PIECES]), pick_piece(refs[PIECES : 2 * PIECES])
    put_piece(refs[2 * PIECES :], to_bf(middle_ref[...] + (to_f(mine) + to_f(come))))


def layer_of(order, middle, mine, come):
    piece, width = mine[0].shape
    block = piece * PIECES // 4
    specs = piece_specs(piece, width, block)
    return order(
        layer_kernel,
        [middle, *mine, *come],
        [pl.BlockSpec((block, width), lambda i: (i, 0))] + specs * 2,
        specs,
        [jax.ShapeDtypeStruct((piece, width), jnp.bfloat16)] * PIECES,
        (4,),
        0,
        5 * MIB,
        "layer",
    )


def tensor_gather(value, rank):
    mate = core_swap(value)
    pair = jnp.where(lax.rem(rank, 2) == 0, jnp.stack([value, mate]), jnp.stack([mate, value]))
    come = chip_swap(pair)
    return jnp.where(
        lax.div(rank, 2) == 0,
        jnp.concatenate([pair, come], axis=0),
        jnp.concatenate([come, pair], axis=0),
    )


def body(
    tokens,
    lengths,
    cotangent,
    q_weight,
    q_bias,
    k_weight,
    k_bias,
    v_weight,
    v_bias,
    o_weight,
    attn_gain,
    ffn_gain,
    gate_weight,
    up_weight,
    down_weight,
):
    rows, local, width = tokens.shape
    total = rows * local
    half = total // 2
    heads = q_weight.shape[1] // HD
    ranks = lax.axis_size("tensor")
    seqs = lax.axis_size("seq")
    rank = lax.axis_index("tensor")
    dp_index = lax.axis_index("dp")
    seq_index = lax.axis_index("seq")
    core = lax.rem(rank, 2)
    head = lax.div(rank, 2)
    core_one = core.reshape(1)
    hops = min(seqs - 1, -(-(MOST - 1) // local))
    reach = hops * local

    def own_first(value):
        turned = jnp.concatenate([value[rows // 2 :], value[: rows // 2]], axis=0)
        return jnp.where(core == 0, value, turned)

    slots = jnp.arange(lengths.shape[1], dtype=jnp.int32)
    lens = own_first(lengths)
    ends = jnp.sum(jnp.where(slots[None, :] <= slots[:, None], lens[:, None, :], 0), axis=2)
    spot = seq_index * local + jnp.arange(local, dtype=jnp.int32)
    begun = jnp.max(
        jnp.where(ends[:, None, :] <= spot[None, :, None], ends[:, None, :], 0), axis=2
    )
    valid = to_f(spot[None, :] < ends[:, -2:-1])
    position = (spot[None, :] - begun).reshape(total, 1)
    freqs = ROPE_BASE ** (-(jnp.arange(HD // 2, dtype=jnp.float32) * 2.0) / HD)
    angles = to_f(position) * freqs[None, :]
    cosine, sine = jnp.cos(angles), jnp.sin(angles)
    cosine = jnp.concatenate([cosine, cosine], axis=1)
    sine = jnp.concatenate([-sine, sine], axis=1)
    start = begun - (seq_index * local - reach)
    low = jnp.maximum(lax.div(jnp.maximum(start[:, ::Q_BLOCK], 0), K_BLOCK), 0)
    start = start.reshape(rows, 1, local)

    key_side = core == 0
    kv_weight = jnp.where(
        key_side,
        lax.dynamic_slice_in_dim(k_weight, head * HD, HD, 1),
        lax.dynamic_slice_in_dim(v_weight, head * HD, HD, 1),
    )
    kv_bias = jnp.where(
        key_side,
        lax.dynamic_slice_in_dim(k_bias, head * HD, HD, 0),
        lax.dynamic_slice_in_dim(v_bias, head * HD, HD, 0),
    )
    weight = jnp.concatenate([q_weight, kv_weight], axis=1)
    bias = to_f(jnp.concatenate([q_bias, kv_bias])).reshape(1, -1)
    gain_one = to_f(attn_gain).reshape(1, width)
    gain_two = to_f(ffn_gain).reshape(1, width)

    h_one, q_rot, kv = first(
        core_one, tokens.reshape(total, width), gain_one, weight, bias, cosine, sine
    )
    kv = kv.reshape(rows, local, HD)
    span = [shifted(kv, h) for h in range(hops, 0, -1)] + [kv]
    mate = [core_swap(piece) for piece in span]
    q_rows = q_rot.reshape(rows, local, heads * HD)
    mixed_rows, lse = attend(low, core_one, q_rows, start, span, mate)
    mixed = mixed_rows.reshape(total, heads * HD)

    order = Order()
    flat_tokens = tokens.reshape(total, width)
    dps = lax.axis_size("dp")
    near_pair = dps == 2 and seqs == 4
    part = width // dps
    share = part // seqs
    gate_t, up_t, down_t = gate_weight.T, up_weight.T, down_weight.T
    units = gate_t.shape[0]
    tiles = -(-units // TILE)
    cut = (tiles + 1) // 2
    long = -(-2 * tiles // 3)
    one, two = seq_index ^ 1, seq_index ^ 2
    three = seq_index ^ 3
    quad = jnp.stack([one, three, seq_index, two])

    begin = (dp_index * seqs + seq_index) * share

    def rows_of(value):
        return lax.dynamic_slice_in_dim(value, begin, share, 0)

    class Rows:
        def __init__(self, lefts, rights, parts, tile=TILE, sent=None):
            self.args = (order, lefts, rights, parts)
            self.tile = tile
            if not near_pair:
                (whole,) = share_of(*self.args, width, 0, tile)
                self.whole = lax.psum_scatter(whole, ("dp", "seq"), scatter_dimension=0, tiled=True)
                return
            if sent is None:
                (sent,) = share_of(*self.args, part, 1 - dp_index, tile)
            self.come = lax.ppermute(sent, "dp", flipped("dp", 0))

        def own(self):
            if near_pair:
                send, self.keep = share_of(*self.args, part, dp_index, self.tile, self.come, quad)
                self.come = lax.ppermute(send, "seq", flipped("seq", 0))

        def relay(self):
            if near_pair:
                sent = relay(order, self.keep, self.come, share)
                self.last = lax.ppermute(sent, "seq", flipped("seq", 1))

        def settled(self):
            if near_pair:
                order.arrived(self.last)

        def result(self):
            return [self.keep, self.come, self.last] if near_pair else [self.whole]

    class SeqFirst(Rows):
        def __init__(self, lefts, rights, parts, tile=TILE):
            if not near_pair:
                super().__init__(lefts, rights, parts, tile)
                return
            (whole,) = share_of(order, lefts, rights, parts, width, 0, tile, None, None, (dps, seqs))
            self.mine = lax.psum_scatter(whole, "seq", scatter_dimension=0, tiled=True)

        def across(self):
            if near_pair:
                sent = lax.dynamic_slice_in_dim(self.mine, (1 - dp_index) * share, share, 0)
                self.mine = lax.dynamic_slice_in_dim(self.mine, dp_index * share, share, 0)
                order.arrived(sent, self.mine)
                self.come = lax.ppermute(sent, "dp", flipped("dp", 0))

        def settled(self):
            if near_pair:
                order.arrived(self.come)

        def result(self):
            return [self.mine, self.come] if near_pair else [self.whole]

    class Scattered(Rows):
        def own(self):
            if near_pair:
                (mine,) = share_of(*self.args, part, dp_index, self.tile, self.come)
                self.whole = lax.psum_scatter(mine, "seq", scatter_dimension=0, tiled=True)

        def settled(self):
            order.arrived(self.whole)

        def result(self):
            return [self.whole]

    sent = core_swaps(narrow(order, [(mixed, o_weight)], 1, (), 1))
    mine = narrow(order, [(mixed, o_weight)], 0, sent, 1)
    come = chip_swaps(mine)
    grad_ffn, grad_ffn_t = grad_out_of(
        order, core_one, cotangent.reshape(total, width), valid.reshape(total, 1)
    )
    gate_rows, up_rows = rows_of(gate_weight), rows_of(up_weight)
    order.arrived(gate_rows, up_rows)
    grad_hidden = grad_hidden_of(order, grad_ffn, down_t)
    h_one_t = turn(order, [h_one])
    middle, h_two = middle_of(order, core_one, flat_tokens, mine, come, gain_two)
    h_two += core_swaps(h_two)
    hidden, grad_gate, grad_up = gated(order, h_two, grad_hidden, gate_t, up_t)

    down_b = SeqFirst([grad_ffn_t], [hidden], [(0, 0, cut, tiles - cut, 0)])
    down_a = Rows([grad_ffn_t], [hidden], [(0, 0, 0, cut, 0)])
    pairs = [(grad_gate, gate_t), (grad_up, up_t)]
    sent = core_swaps(narrow(order, pairs, 1))
    mine = narrow(order, pairs, 0, sent)
    come = chip_swaps(mine)
    h_two_t = turn(order, h_two)
    if near_pair:
        sends = share_of(
            order,
            [h_two_t],
            [grad_gate, grad_up],
            [(0, 0, 0, tiles, 0), (0, 1, 0, long, 1), (0, 1, long, tiles - long, 2)],
            part,
            1 - dp_index,
            TILE,
        )
    else:
        sends = [None] * 3

    def half_rows(kind, right, begin, end, sent):
        return kind([h_two_t], [right], [(0, 0, begin, end - begin, 0)], TILE, sent)

    gate = half_rows(Scattered, grad_gate, 0, tiles, sends[0])
    up_a = half_rows(Rows, grad_up, 0, long, sends[1])
    up_b = half_rows(Rows, grad_up, long, tiles, sends[2])
    down_a.own()
    grad_middle, *branch = norm_back(order, core_one, mine, come, middle, gain_two, grad_ffn, False)
    branch += core_swaps(branch)
    grad_mixed = mixed_back(order, branch, o_weight).reshape(rows, local, heads * HD)
    grad_q_rows, keep, sent = attend_back(
        order, low, core_one, q_rows, start, span, mate, grad_mixed, mixed_rows, lse, cosine, sine
    )
    both_come = core_swap(sent)
    branch_t = turn(order, branch)
    down_a.relay()
    own_kv, *pieces = fold(order, keep, both_come, local)
    moving = shifted(pieces[-1], -1) if pieces else None
    ffn_sent = core_swaps(narrow(order, [(hidden, down_t)], 1))
    for piece in pieces[-2::-1]:
        moving = shifted(carry(order, piece, moving), -1)
    grad_qkv, bias_sum = join(
        order, core_one, grad_q_rows, own_kv, [] if moving is None else [moving], cosine, sine
    )
    sent = core_swaps(narrow(order, [(grad_qkv, weight)], 1, (), 1))
    last_parts = [(0, 0, 0, grad_qkv.shape[1] // HD, 0), (1, 1, 0, heads, 0)]
    last = Rows([h_one_t, branch_t], [grad_qkv, mixed], last_parts, HD)
    mine = narrow(order, [(grad_qkv, weight)], 0, sent, 1)
    come = chip_swaps(mine)
    down_b.across()
    down_a.settled()
    gate.own()
    ffn_mine = narrow(order, [(hidden, down_t)], 0, ffn_sent)
    token = norm_back(order, core_one, mine, come, flat_tokens, gain_one, grad_middle, True)
    token += core_swaps(token)
    ffn_come = chip_swaps(ffn_mine)
    token_grad = place(order, core_one, token).reshape(rows, local, width)
    up_a.own()
    layer = layer_of(order, middle, ffn_mine, ffn_come)
    layer += core_swaps(layer)
    last.own()
    layer_out = place(order, core_one, layer).reshape(rows, local, width)
    up_a.relay()
    up_b.own()
    down_b.settled()
    up_a.settled()
    last.relay()
    (down_grad,) = finish(order, [down_a.result(), down_b.result()], share, units, TILE)
    if near_pair:
        bias_come = lax.ppermute(bias_sum, "dp", flipped("dp", 0))
        bias_all = bias_add(order, bias_sum, bias_come)
        bias_come = lax.ppermute(bias_all, "seq", flipped("seq", 0))
    up_b.relay()
    gate_grad, gate_term = finish(order, [gate.result()], share, units, TILE, gate_rows)
    wide_columns = grad_qkv.shape[1]
    (last_grad,) = finish(order, [last.result()], share, wide_columns + heads * HD, HD)
    if near_pair:
        bias_all = bias_add(order, bias_all, bias_come)
        bias_come = lax.ppermute(bias_all, "seq", flipped("seq", 1))
        bias_all = (bias_all + bias_come)[:1]
    else:
        bias_all = lax.psum(bias_sum[:1], ("dp", "seq"))
    up_grad, up_term = finish(order, [up_a.result(), up_b.result()], share, units, TILE, up_rows)
    qkv_grad, o_grad = last_grad[:, :wide_columns], last_grad[:, wide_columns:]

    attn_term = jnp.sum(to_f(rows_of(weight)) * qkv_grad, axis=1)
    ffn_term = jnp.sum(gate_term + up_term, axis=1)
    columns = heads * HD
    room = -(-share // HD) * HD - share
    terms = jnp.pad(jnp.stack([ffn_term, attn_term]), ((0, 0), (0, room))).reshape(-1, HD)
    packed = jnp.concatenate([qkv_grad[:, columns:], bias_all.reshape(-1, HD), terms], axis=0)
    gathered = tensor_gather(packed, rank)
    term_rows = terms.shape[0]
    bias_count = bias_all.shape[1] // HD
    terms = gathered[:, share + bias_count :].reshape(ranks, 2, -1)[:, :, :share]
    ffn_gain_grad, attn_gain_grad = terms[0] + terms[1] + (terms[2] + terms[3])
    attn_gain_grad = attn_gain_grad / lax.dynamic_slice_in_dim(gain_one[0], begin, share, 0)
    ffn_gain_grad = ffn_gain_grad / lax.dynamic_slice_in_dim(gain_two[0], begin, share, 0)
    q_grad = qkv_grad[:, :columns]
    kv_parts = lax.dynamic_slice_in_dim(gathered, rank * (share // ranks), share // ranks, 1)
    k_grad = jnp.concatenate([kv_parts[2 * i] for i in range(KVH)], axis=1)
    v_grad = jnp.concatenate([kv_parts[2 * i + 1] for i in range(KVH)], axis=1)
    biases = gathered[:, share : share + bias_count]
    q_bias_grad = biases[:, :heads].reshape(-1)
    k_bias_grad = biases[0::2, heads].reshape(-1)
    v_bias_grad = biases[1::2, heads].reshape(-1)
    return (
        layer_out,
        token_grad,
        q_grad,
        q_bias_grad,
        k_grad,
        k_bias_grad,
        v_grad,
        v_bias_grad,
        o_grad,
        attn_gain_grad,
        ffn_gain_grad,
        gate_grad,
        up_grad,
        down_grad,
    )


def solution(mesh):
    in_specs = (
        P("dp", "seq", None),
        P("dp", None),
        P("dp", "seq", None),
        P(None, "tensor"),
        P("tensor"),
        P(),
        P(),
        P(),
        P(),
        P(None, "tensor"),
        P(),
        P(),
        P(None, "tensor"),
        P(None, "tensor"),
        P(None, "tensor"),
    )
    out_specs = (
        P("dp", "seq", None),
        P("dp", "seq", None),
        P(("dp", "seq"), "tensor"),
        P(),
        P(("dp", "seq", "tensor"), None),
        P(),
        P(("dp", "seq", "tensor"), None),
        P(),
        P(("dp", "seq"), "tensor"),
        P(("dp", "seq")),
        P(("dp", "seq")),
        P(("dp", "seq"), "tensor"),
        P(("dp", "seq"), "tensor"),
        P(("dp", "seq"), "tensor"),
    )
    return jax.shard_map(body, mesh=mesh, in_specs=in_specs, out_specs=out_specs, check_vma=False)
```

```python
import functools
import math

import jax
import jax.numpy as jnp
from jax import lax
from jax.experimental import pallas as pl
from jax.experimental.pallas import tpu as pltpu
from jax.sharding import PartitionSpec as P

KVH = 2
HD = 128
MOST = 1024
EPS = 1e-06
ROPE_BASE = 10000.0
NEG_FILL = -1e30
Q_BLOCK = 256
K_BLOCK = 256
MIB = 1 << 20
LIGHT = 1000
TILE = 256
PIECES = 2
SCALE = 1.0 / math.sqrt(HD)


def to_bf(value):
    return value.astype(jnp.bfloat16)


def to_f(value):
    return value.astype(jnp.float32)


def dot(left, right, left_dim=1, right_dim=0):
    return lax.dot_general(
        left,
        right,
        (((left_dim,), (right_dim,)), ((), ())),
        preferred_element_type=jnp.float32,
    )


def flipped(axis, bit):
    return [(i, i ^ (1 << bit)) for i in range(lax.axis_size(axis))]


def core_swap(value):
    return lax.ppermute(value, "tensor", flipped("tensor", 0))


def chip_swap(value):
    return lax.ppermute(value, "tensor", flipped("tensor", 1))


def core_swaps(values):
    return [core_swap(value) for value in values]


def chip_swaps(values):
    return [chip_swap(value) for value in values]


def shifted(value, hops):
    count = lax.axis_size("seq")
    route = [(i, i + hops) for i in range(count) if 0 <= i + hops < count]
    return lax.ppermute(value, "seq", route)


def cost(flops, read):
    return pl.CostEstimate(flops=flops // LIGHT, bytes_accessed=read // LIGHT, transcendentals=0)


class Order:
    def __init__(self):
        self.mark = None
        self.touched = []

    def arrived(self, *values):
        self.touched.extend(values)

    def __call__(self, kernel, args, in_specs, out_specs, out_shape, grid, flops, read, name, scalars=(), scratch=()):
        anchor = ([] if self.mark is None else [self.mark]) + self.touched
        self.touched = []
        count = len(scalars) + len(args)
        outs = len(out_shape)

        def run(*refs):
            rest = refs[count + len(anchor) :]
            kernel(*refs[:count], *rest[:outs], *rest[outs + 1 :])
            rest[outs][...] = jnp.zeros(rest[outs].shape, jnp.float32)

        *results, self.mark = pl.pallas_call(
            run,
            grid_spec=pltpu.PrefetchScalarGridSpec(
                num_scalar_prefetch=len(scalars),
                grid=grid,
                in_specs=list(in_specs) + anchors(len(anchor)),
                out_specs=list(out_specs) + [mark_spec()],
                scratch_shapes=list(scratch),
            ),
            out_shape=list(out_shape) + [MARK],
            compiler_params=pltpu.CompilerParams(vmem_limit_bytes=32 * MIB),
            cost_estimate=cost(flops, read),
            name=name,
        )(*scalars, *args, *anchor)
        return results


def first_kernel(core_ref, tok_ref, gain_ref, w_ref, b_ref, cos_ref, sin_ref, h_ref, q_ref, kv_ref):
    x = to_f(tok_ref[...])
    factor = lax.rsqrt(jnp.mean(x * x, axis=-1, keepdims=True) + EPS)
    h = to_bf(x * factor * gain_ref[...])
    h_ref[...] = h
    lin = dot(h, w_ref[...]) + b_ref[...]
    cosine = cos_ref[...]
    sine = sin_ref[...]
    heads = q_ref.shape[1] // HD
    for head in range(heads):
        part = lin[:, head * HD : (head + 1) * HD]
        q_ref[:, head * HD : (head + 1) * HD] = to_bf(
            part * cosine + pltpu.roll(part, HD // 2, 1) * sine
        )
    part = lin[:, heads * HD :]
    is_key = core_ref[0] == 0
    kv_ref[...] = to_bf(
        part * jnp.where(is_key, cosine, 1.0)
        + pltpu.roll(part, HD // 2, 1) * jnp.where(is_key, sine, 0.0)
    )


def first(core, tokens, gain, weight, bias, cosine, sine):
    total, width = tokens.shape
    columns = weight.shape[1]
    block = total // 4
    half = 2

    def flip(i, core_ref):
        return (lax.rem(i + core_ref[0] * half, 4), 0)

    def at(i, core_ref):
        return (i, 0)

    def whole(i, core_ref):
        return (0, 0)

    return pl.pallas_call(
        first_kernel,
        grid_spec=pltpu.PrefetchScalarGridSpec(
            num_scalar_prefetch=1,
            grid=(4,),
            in_specs=[
                pl.BlockSpec((block, width), flip),
                pl.BlockSpec((1, width), whole),
                pl.BlockSpec((width, columns), whole),
                pl.BlockSpec((1, columns), whole),
                pl.BlockSpec((block, HD), at),
                pl.BlockSpec((block, HD), at),
            ],
            out_specs=[
                pl.BlockSpec((block, width), at),
                pl.BlockSpec((block, columns - HD), at),
                pl.BlockSpec((block, HD), at),
            ],
        ),
        out_shape=[
            jax.ShapeDtypeStruct((total, width), jnp.bfloat16),
            jax.ShapeDtypeStruct((total, columns - HD), jnp.bfloat16),
            jax.ShapeDtypeStruct((total, HD), jnp.bfloat16),
        ],
        compiler_params=pltpu.CompilerParams(vmem_limit_bytes=32 * MIB),
        cost_estimate=cost(2 * total * width * columns, 9 * MIB),
        name="first",
    )(core, tokens, gain, weight, bias, cosine, sine)


def stacked(ref, start, count, heads):
    return jnp.concatenate(
        [ref[0, pl.ds(start, count), h * HD : (h + 1) * HD] for h in range(heads)], axis=0
    )


def bounds(start_ref, index, heads, reach):
    first_key = jnp.concatenate(
        [start_ref[0, :, pl.ds(index * Q_BLOCK, Q_BLOCK)]] * heads, axis=1
    )
    place = reach + index * Q_BLOCK + lax.broadcasted_iota(jnp.int32, (1, Q_BLOCK), 1)
    return first_key, jnp.concatenate([place] * heads, axis=1)


def gather_span(core, refs, span):
    count = len(refs) // 2
    local = refs[0].shape[1]
    for i in range(count):
        here = slice(i * local, (i + 1) * local)
        span[core, here] = refs[i][0]
        span[1 - core, here] = refs[count + i][0]


def attend_kernel(heads, blocks, pieces, low_ref, core_ref, q_ref, start_ref, *refs):
    o_ref, lse_ref, acc, span = refs[2 * pieces :]
    row = pl.program_id(0)
    wide = heads * Q_BLOCK
    reach = (pieces - 1) * q_ref.shape[1]
    gather_span(core_ref[0], refs[: 2 * pieces], span)
    for index in range(blocks):
        q = stacked(q_ref, index * Q_BLOCK, Q_BLOCK, heads)
        first_key, place = bounds(start_ref, index, heads, reach)
        acc[...] = jnp.zeros_like(acc)

        def step(j, carry):
            top, total = carry
            keys = pl.ds(pl.multiple_of(j * K_BLOCK, K_BLOCK), K_BLOCK)
            s = dot(span[0, keys], q, 1, 1) * SCALE
            key = j * K_BLOCK + lax.broadcasted_iota(jnp.int32, (K_BLOCK, wide), 0)
            s = jnp.where((key >= first_key) & (key <= place), s, NEG_FILL)
            later = jnp.maximum(top, jnp.max(s, axis=0, keepdims=True))
            p = jnp.exp(s - later)
            fade = jnp.exp(top - later)
            total = total * fade + jnp.sum(p, axis=0, keepdims=True)
            acc[...] = acc[...] * fade + dot(span[1, keys], to_bf(p), 0, 0)
            return later, total

        last = (reach + (index + 1) * Q_BLOCK - 1) // K_BLOCK + 1
        top, total = lax.fori_loop(
            low_ref[row, index],
            last,
            step,
            (jnp.full((1, wide), NEG_FILL, jnp.float32), jnp.zeros((1, wide), jnp.float32)),
        )
        out = to_bf((acc[...] / total).T)
        for h in range(heads):
            o_ref[0, index * Q_BLOCK : (index + 1) * Q_BLOCK, h * HD : (h + 1) * HD] = out[
                h * Q_BLOCK : (h + 1) * Q_BLOCK
            ]
        lse_ref[0, index : index + 1, :] = top + jnp.log(total)


def span_specs(rows, local, pieces):
    near = pl.BlockSpec((1, local, HD), lambda i, *refs: (i, 0, 0))
    far = pl.BlockSpec((1, local, HD), lambda i, *refs: (lax.rem(i + rows // 2, rows), 0, 0))
    return [near] * pieces + [far] * pieces


def attend(low, core, q, start, span, mate):
    rows, local, columns = q.shape
    pieces = len(span)
    heads = columns // HD
    blocks = local // Q_BLOCK

    def at(i, *refs):
        return (i, 0, 0)

    return pl.pallas_call(
        functools.partial(attend_kernel, heads, blocks, pieces),
        grid_spec=pltpu.PrefetchScalarGridSpec(
            num_scalar_prefetch=2,
            grid=(rows,),
            in_specs=[pl.BlockSpec((1, local, columns), at), pl.BlockSpec((1, 1, local), at)]
            + span_specs(rows, local, pieces),
            out_specs=[
                pl.BlockSpec((1, local, columns), at),
                pl.BlockSpec((1, blocks, heads * Q_BLOCK), at),
            ],
            scratch_shapes=[
                pltpu.VMEM((HD, heads * Q_BLOCK), jnp.float32),
                pltpu.VMEM((2, pieces * local, HD), jnp.bfloat16),
            ],
        ),
        out_shape=[
            jax.ShapeDtypeStruct((rows, local, columns), jnp.bfloat16),
            jax.ShapeDtypeStruct((rows, blocks, heads * Q_BLOCK), jnp.float32),
        ],
        compiler_params=pltpu.CompilerParams(vmem_limit_bytes=32 * MIB),
        cost_estimate=cost(8_000_000_000, 4 * MIB),
        name="attend",
    )(low, core, q, start, *span, *mate)


def attend_back_kernel(
    heads, blocks, pieces, low_ref, core_ref, q_ref, start_ref, g_ref, o_ref, lse_ref, cos_ref, sin_ref, *refs
):
    gq_ref, keep_ref, send_ref, acc, gk, gv, span = refs[2 * pieces :]
    row = pl.program_id(0)
    wide = heads * Q_BLOCK
    reach = (pieces - 1) * q_ref.shape[1]
    core = core_ref[0]
    gather_span(core, refs[: 2 * pieces], span)
    gk[...] = jnp.zeros_like(gk)
    gv[...] = jnp.zeros_like(gv)
    for index in range(blocks):
        q = stacked(q_ref, index * Q_BLOCK, Q_BLOCK, heads)
        g = stacked(g_ref, index * Q_BLOCK, Q_BLOCK, heads)
        o = stacked(o_ref, index * Q_BLOCK, Q_BLOCK, heads)
        inner = jnp.sum((to_f(g) * to_f(o)).T, axis=0, keepdims=True)
        lse = lse_ref[0, index : index + 1, :]
        first_key, place = bounds(start_ref, index, heads, reach)
        acc[...] = jnp.zeros_like(acc)

        def step(j, carry):
            keys = pl.ds(pl.multiple_of(j * K_BLOCK, K_BLOCK), K_BLOCK)
            k = span[0, keys]
            s = dot(k, q, 1, 1) * SCALE
            key = j * K_BLOCK + lax.broadcasted_iota(jnp.int32, (K_BLOCK, wide), 0)
            p = jnp.where((key >= first_key) & (key <= place), jnp.exp(s - lse), 0.0)
            gp = dot(span[1, keys], g, 1, 1)
            gs = to_bf(p * (gp - inner))
            gv[keys] += dot(to_bf(p), g)
            gk[keys] += dot(gs, q)
            acc[...] += dot(k, gs, 0, 0)
            return carry

        last = (reach + (index + 1) * Q_BLOCK - 1) // K_BLOCK + 1
        lax.fori_loop(low_ref[row, index], last, step, 0)
        gq = acc[...].T * SCALE
        here = slice(index * Q_BLOCK, (index + 1) * Q_BLOCK)
        cosine, sine = cos_ref[here], sin_ref[here]
        for h in range(heads):
            part = gq[h * Q_BLOCK : (h + 1) * Q_BLOCK]
            gq_ref[0, here, h * HD : (h + 1) * HD] = to_bf(
                part * cosine + pltpu.roll(part * sine, HD // 2, 1)
            )
    is_key = core == 0
    keys, values = gk[...] * SCALE, gv[...]
    keep_ref[0] = to_bf(jnp.where(is_key, keys, values))
    send_ref[0] = to_bf(jnp.where(is_key, values, keys))


def attend_back(order, low, core, q, start, span, mate, grad, out, lse, cosine, sine):
    rows, local, columns = q.shape
    pieces = len(span)
    window = pieces * local
    heads = columns // HD
    blocks = local // Q_BLOCK

    def at(i, *refs):
        return (i, 0, 0)

    table = pl.BlockSpec((local, HD), lambda i, *refs: (i, 0))
    tokens = pl.BlockSpec((1, local, columns), at)
    return order(
        functools.partial(attend_back_kernel, heads, blocks, pieces),
        [q, start, grad, out, lse, cosine, sine, *span, *mate],
        [
            tokens,
            pl.BlockSpec((1, 1, local), at),
            tokens,
            tokens,
            pl.BlockSpec((1, blocks, heads * Q_BLOCK), at),
            table,
            table,
        ]
        + span_specs(rows, local, pieces),
        [tokens, pl.BlockSpec((1, window, HD), at), pl.BlockSpec((1, window, HD), at)],
        [
            jax.ShapeDtypeStruct((rows, local, columns), jnp.bfloat16),
            jax.ShapeDtypeStruct((rows, window, HD), jnp.bfloat16),
            jax.ShapeDtypeStruct((rows, window, HD), jnp.bfloat16),
        ],
        (rows,),
        20_000_000_000,
        6 * MIB,
        "attend_back",
        scalars=(low, core),
        scratch=[
            pltpu.VMEM((HD, heads * Q_BLOCK), jnp.float32),
            pltpu.VMEM((window, HD), jnp.float32),
            pltpu.VMEM((window, HD), jnp.float32),
            pltpu.VMEM((2, window, HD), jnp.bfloat16),
        ],
    )


def fold_kernel(keep_ref, come_ref, own_ref, *send_refs):
    local = own_ref.shape[1]
    total = to_f(keep_ref[0]) + to_f(come_ref[0])
    reach = total.shape[0] - local
    own_ref[0] = total[reach:]
    for hop, ref in enumerate(send_refs, 1):
        ref[0] = to_bf(total[reach - hop * local : reach - (hop - 1) * local])


def fold(order, keep, come, local):
    rows, window = keep.shape[:2]
    hops = window // local - 1
    out = pl.BlockSpec((1, local, HD), lambda i: (i, 0, 0))
    return order(
        fold_kernel,
        [keep, come],
        [
            pl.BlockSpec((1, window, HD), lambda i: (i, 0, 0)),
            pl.BlockSpec((1, window, HD), lambda i: (lax.rem(i + rows // 2, rows), 0, 0)),
        ],
        [out] * (hops + 1),
        [jax.ShapeDtypeStruct((rows, local, HD), jnp.float32)]
        + [jax.ShapeDtypeStruct((rows, local, HD), jnp.bfloat16)] * hops,
        (rows,),
        0,
        4 * MIB,
        "fold",
    )


def carry_kernel(piece_ref, come_ref, out_ref):
    out_ref[...] = to_bf(to_f(piece_ref[...]) + to_f(come_ref[...]))


def carry(order, piece, come):
    rows, local, columns = piece.shape
    at = pl.BlockSpec((1, local, columns), lambda i: (i, 0, 0))
    return order(
        carry_kernel,
        [piece, come],
        [at, at],
        [at],
        [jax.ShapeDtypeStruct(piece.shape, jnp.bfloat16)],
        (rows,),
        0,
        2 * MIB,
        "carry",
    )[0]


def bias_kernel(left_ref, right_ref, out_ref):
    out_ref[...] = left_ref[...] + right_ref[...]


def bias_add(order, left, right):
    whole = pl.BlockSpec(left.shape, lambda i: (0, 0))
    return order(
        bias_kernel,
        [left, right],
        [whole, whole],
        [whole],
        [jax.ShapeDtypeStruct(left.shape, jnp.float32)],
        (1,),
        0,
        MIB,
        "bias",
    )[0]


def join_kernel(hops, core_ref, gq_ref, cos_ref, sin_ref, own_ref, *refs):
    out_ref, sum_ref = refs[-2:]
    columns = gq_ref.shape[2]
    grad = own_ref[0]
    for ref in refs[:hops]:
        grad = grad + to_f(ref[0])
    is_key = core_ref[0] == 0
    cosine = jnp.where(is_key, cos_ref[...], 1.0)
    sine = jnp.where(is_key, sin_ref[...], 0.0)
    kv = to_bf(grad * cosine + pltpu.roll(grad * sine, HD // 2, 1))
    q = gq_ref[0]
    out_ref[:, :columns] = q
    out_ref[:, columns:] = kv

    @pl.when(pl.program_id(0) == 0)
    def _():
        sum_ref[...] = jnp.zeros(sum_ref.shape, jnp.float32)

    sum_ref[:, :columns] += jnp.sum(to_f(q), axis=0, keepdims=True)
    sum_ref[:, columns:] += jnp.sum(to_f(kv), axis=0, keepdims=True)


def join(order, core, grad_q, own, comes, cosine, sine):
    rows, local, columns = grad_q.shape
    wide = columns + HD

    def at(i, *refs):
        return (i, 0, 0)

    piece = pl.BlockSpec((1, local, HD), at)
    table = pl.BlockSpec((local, HD), lambda i, *refs: (i, 0))
    return order(
        functools.partial(join_kernel, len(comes)),
        [grad_q, cosine, sine, own, *comes],
        [pl.BlockSpec((1, local, columns), at), table, table, piece] + [piece] * len(comes),
        [
            pl.BlockSpec((local, wide), lambda i, *refs: (i, 0)),
            pl.BlockSpec((8, wide), lambda i, *refs: (0, 0)),
        ],
        [
            jax.ShapeDtypeStruct((rows * local, wide), jnp.bfloat16),
            jax.ShapeDtypeStruct((8, wide), jnp.float32),
        ],
        (rows,),
        0,
        4 * MIB,
        "join",
        scalars=(core,),
    )


def mixed_back_kernel(w_ref, *refs):
    rows = refs[0].shape[0]
    for i, ref in enumerate(refs[:-1]):
        refs[-1][i * rows : (i + 1) * rows] = to_bf(dot(ref[...], w_ref[...]))


def mixed_back(order, pieces, weight):
    rows, width = pieces[0].shape
    total = rows * len(pieces)
    columns = weight.shape[1]

    def whole(i):
        return (0, 0)

    return order(
        mixed_back_kernel,
        [weight, *pieces],
        [pl.BlockSpec((width, columns), whole)] + [pl.BlockSpec((rows, width), whole)] * len(pieces),
        [pl.BlockSpec((total, columns), whole)],
        [jax.ShapeDtypeStruct((total, columns), jnp.bfloat16)],
        (1,),
        2 * total * width * columns,
        6 * MIB,
        "mixed_back",
    )[0]


def place_kernel(core_ref, *refs):
    for i, ref in enumerate(refs[:-1]):

        @pl.when(pl.program_id(0) == i)
        def _(ref=ref):
            refs[-1][...] = ref[...]


def place(order, core, pieces):
    rows, width = pieces[0].shape
    count = len(pieces)
    return order(
        place_kernel,
        list(pieces),
        [pl.BlockSpec((rows, width), lambda i, core_ref: (0, 0))] * count,
        [pl.BlockSpec((rows, width), lambda i, core_ref: (lax.rem(i + core_ref[0] * (count // 2), count), 0))],
        [jax.ShapeDtypeStruct((rows * count, width), pieces[0].dtype)],
        (count,),
        0,
        8 * rows * width,
        "place",
        scalars=(core,),
    )[0]


def anchors(count):
    return [pl.BlockSpec(memory_space=pl.ANY)] * count


MARK = jax.ShapeDtypeStruct((8, HD), jnp.float32)


def mark_spec():
    return pl.BlockSpec((8, HD), lambda *refs: (0, 0))


def grad_hidden_kernel(g_ref, w_ref, out_ref):
    out_ref[...] = to_bf(dot(g_ref[...], w_ref[...], 1, 1))


def grad_hidden_of(order, grad, weight):
    total, width = grad.shape
    hidden = weight.shape[0]
    return order(
        grad_hidden_kernel,
        [grad, weight],
        [pl.BlockSpec((total, width), lambda i: (0, 0)), pl.BlockSpec((TILE, width), lambda i: (i, 0))],
        [pl.BlockSpec((total, TILE), lambda i: (0, i))],
        [jax.ShapeDtypeStruct((total, hidden), jnp.bfloat16)],
        (pl.cdiv(hidden, TILE),),
        2 * total * width * hidden,
        15 * MIB,
        "grad_hidden",
    )[0]


def gated_kernel(gh_ref, gw_ref, uw_ref, *refs):
    hid_ref, gg_ref, gu_ref = refs[-3:]
    rows = refs[0].shape[0]
    for part, ref in enumerate(refs[:-3]):
        here = slice(part * rows, (part + 1) * rows)
        h = ref[...]
        gate = dot(h, gw_ref[...], 1, 1)
        up = dot(h, uw_ref[...], 1, 1)
        grad = to_f(gh_ref[here])
        sigma = 1.0 / (1.0 + jnp.exp(-gate))
        swish = gate * sigma
        hid_ref[here] = to_bf(swish * up)
        gu_ref[here] = to_bf(grad * swish)
        gg_ref[here] = to_bf(grad * up * sigma * (1.0 + gate * (1.0 - sigma)))


def gated(order, pieces, grad_hidden, gate_weight, up_weight):
    rows, width = pieces[0].shape
    total = rows * len(pieces)
    hidden = gate_weight.shape[0]
    column = pl.BlockSpec((total, TILE), lambda i: (0, i))
    weight = pl.BlockSpec((TILE, width), lambda i: (i, 0))
    shape = jax.ShapeDtypeStruct((total, hidden), jnp.bfloat16)
    return order(
        gated_kernel,
        [grad_hidden, gate_weight, up_weight, *pieces],
        [column, weight, weight] + [pl.BlockSpec((rows, width), lambda i: (0, 0))] * len(pieces),
        [column] * 3,
        [shape] * 3,
        (pl.cdiv(hidden, TILE),),
        4 * total * width * hidden,
        30 * MIB,
        "gated",
    )


def share_kernel(plan, lefts, rights, extra, halves, groups, pick_ref, blocks_ref, *refs):
    step = pl.program_id(0)
    left_refs, right_refs = refs[:lefts], refs[lefts : lefts + rights]
    refs = refs[lefts + rights :]
    if extra:
        extra_ref, refs = refs[0], refs[1:]
    for left, right, begin, end, shift, columns, target in plan:

        @pl.when((step >= begin) & (step < end))
        def _(left=left, right=right, shift=shift, columns=columns, target=target):
            out = dot(left_refs[left][...], right_refs[right][...])
            if extra:
                out = out + to_f(extra_ref[...])
            tile = out.shape[1]
            spot = (step + shift) * tile + lax.broadcasted_iota(jnp.int32, (1, tile), 1)
            out = to_bf(jnp.where(spot < columns, out, 0.0))
            if groups:
                share = out.shape[0] // (groups[0] * groups[1])
                for i in range(groups[0]):
                    for j in range(groups[1]):
                        here = (j * groups[0] + i) * share
                        there = (i * groups[1] + j) * share
                        refs[target][here : here + share] = out[there : there + share]
                return
            if not halves:
                refs[target][...] = out
                return
            send_ref, keep_ref, rows = refs
            rows[...] = out
            share = send_ref.shape[0] // (2 * halves)
            for i in range(2 * halves):
                here = slice(i * share, (i + 1) * share)
                send_ref[here] = rows[pl.ds(pl.multiple_of(blocks_ref[i] * share, share), share)]
                keep_ref[here] = rows[pl.ds(pl.multiple_of(blocks_ref[2 * halves + i] * share, share), share)]


def clipped(rows, tile, begin, count, shift=0):
    return pl.BlockSpec((rows, tile), lambda i, *refs: (0, jnp.clip(i - begin, 0, count - 1) + shift))


def share_of(order, lefts, rights, parts, part, pick, tile, extra=None, blocks=None, groups=None):
    tokens = lefts[0].shape[1]
    plan, at = [], 0
    starts, sizes, right_at = {}, {}, {}
    for left, right, skip, count, target in parts:
        plan.append((left, right, at, at + count, skip - at, rights[right].shape[1], target))
        starts.setdefault(target, at)
        sizes[target] = sizes.get(target, 0) + count
        first, tiles, low = right_at.get(right, (at, 0, skip))
        right_at[right] = (first, tiles + count, low)
        at += count
    halves = 0
    extras = [] if extra is None else [extra]
    scratch = []
    if blocks is None:
        blocks = jnp.zeros((1,), jnp.int32)
        outs = [clipped(part, tile, starts[t], sizes[t]) for t in sorted(sizes)]
        shapes = [jax.ShapeDtypeStruct((part, sizes[t] * tile), jnp.bfloat16) for t in sorted(sizes)]
    else:
        halves = blocks.shape[0] // 4
        outs = [clipped(part // 2, tile, 0, at)] * 2
        shapes = [jax.ShapeDtypeStruct((part // 2, at * tile), jnp.bfloat16)] * 2
        scratch = [pltpu.VMEM((part, tile), jnp.bfloat16)]
    return order(
        functools.partial(share_kernel, plan, len(lefts), len(rights), len(extras), halves, groups),
        [*lefts, *rights, *extras],
        [pl.BlockSpec((part, tokens), lambda i, pick_ref, blocks_ref: (pick_ref[0], 0))] * len(lefts)
        + [clipped(tokens, tile, *right_at[r]) for r in range(len(rights))]
        + [clipped(part, tile, 0, at)] * len(extras),
        outs,
        shapes,
        (at,),
        2 * part * tokens * at * tile,
        2 * (part * tokens + (part + tokens) * at * tile),
        "share",
        scalars=(jnp.asarray(pick, jnp.int32).reshape(1), blocks),
        scratch=scratch,
    )


def relay_kernel(keep_ref, come_ref, out_ref):
    out_ref[...] = to_bf(to_f(keep_ref[...]) + to_f(come_ref[...]))


def relay(order, keep, come, share):
    rows, columns = keep.shape
    pair = pl.BlockSpec((share, columns), lambda i: (2 * i + 1, 0))
    return order(
        relay_kernel,
        [keep, come],
        [pair, pair],
        [pl.BlockSpec((share, columns), lambda i: (i, 0))],
        [jax.ShapeDtypeStruct((rows // 2, columns), jnp.bfloat16)],
        (rows // (2 * share),),
        0,
        3 * rows * columns,
        "relay",
    )[0]


def finish_kernel(plan, columns, gains, *refs):
    out_ref = refs[-2] if gains else refs[-1]
    step = pl.program_id(0)
    tile = out_ref.shape[1]
    for begin, end, first, count in plan:

        @pl.when((step >= begin) & (step < end))
        def _(first=first, count=count):
            out = to_f(refs[first][...])
            for ref in refs[first + 1 : first + count]:
                out = out + to_f(ref[...])
            out_ref[...] = out
            if gains:
                spot = step * tile + lax.broadcasted_iota(jnp.int32, (1, tile), 1)
                terms = jnp.where(spot < columns, out * to_f(refs[-3][...]), 0.0)
                total = terms[:, :HD]
                for i in range(HD, tile, HD):
                    total = total + terms[:, i : i + HD]

                @pl.when(step == 0)
                def _():
                    refs[-1][...] = total

                @pl.when(step > 0)
                def _():
                    refs[-1][...] += total


def finish(order, chunks, share, columns, tile, weight=None):
    plan, specs, args, at = [], [], [], 0
    for chunk in chunks:
        count = chunk[0].shape[1] // tile
        plan.append((at, at + count, len(args), len(chunk)))
        specs += [clipped(share, tile, at, count)] * len(chunk)
        args += chunk
        at += count
    column = pl.BlockSpec((share, tile), lambda i: (0, i))
    outs, shapes = [column], [jax.ShapeDtypeStruct((share, columns), jnp.float32)]
    if weight is not None:
        args.append(weight)
        specs.append(column)
        outs.append(pl.BlockSpec((share, HD), lambda i: (0, 0)))
        shapes.append(jax.ShapeDtypeStruct((share, HD), jnp.float32))
    return order(
        functools.partial(finish_kernel, plan, columns, weight is not None),
        args,
        specs,
        outs,
        shapes,
        (at,),
        0,
        14 * share * columns,
        "finish",
    )


def narrow_kernel(pairs, extras, right_dim, *refs):
    out = dot(refs[0][...], refs[1][...], 1, right_dim)
    for i in range(1, pairs):
        out = out + dot(refs[2 * i][...], refs[2 * i + 1][...], 1, right_dim)
    extra = refs[2 * pairs : 2 * pairs + extras]
    outs = refs[2 * pairs + extras :]
    if extras:
        out = out + jnp.concatenate([to_f(ref[...]) for ref in extra], axis=0)
    rows = outs[0].shape[0]
    for i, ref in enumerate(outs):
        ref[...] = to_bf(out[i * rows : (i + 1) * rows])


def narrow(order, pairs, index, extra=(), right_dim=0):
    total, hidden = pairs[0][0].shape
    width = pairs[0][1].shape[1 - right_dim]
    half = total // 2
    piece = half // PIECES
    column = pl.BlockSpec((piece, TILE), lambda i: (0, i))
    right = (
        pl.BlockSpec((TILE, hidden), lambda i: (i, 0))
        if right_dim
        else pl.BlockSpec((hidden, TILE), lambda i: (0, i))
    )
    return order(
        functools.partial(narrow_kernel, len(pairs), len(extra), right_dim),
        [item for pair in pairs for item in pair] + list(extra),
        [pl.BlockSpec((half, hidden), lambda i: (index, 0)), right] * len(pairs) + [column] * len(extra),
        [column] * PIECES,
        [jax.ShapeDtypeStruct((piece, width), jnp.bfloat16)] * PIECES,
        (width // TILE,),
        2 * len(pairs) * half * width * hidden,
        2 * len(pairs) * (half + width) * hidden + 2 * half * width,
        "narrow",
    )


def piece_specs(piece, width, block):
    steps = piece // block
    return [
        pl.BlockSpec((block, width), lambda i, *refs, j=j: (jnp.clip(i - j * steps, 0, steps - 1), 0))
        for j in range(PIECES)
    ]


def pick_piece(refs):
    value = refs[0][...]
    for j, ref in enumerate(refs[1:], 1):
        value = jnp.where(pl.program_id(0) >= 4 * j // len(refs), ref[...], value)
    return value


def put_piece(refs, value):
    steps = 4 // len(refs)
    for j, ref in enumerate(refs):

        @pl.when(lax.div(pl.program_id(0), steps) == j)
        def _(ref=ref):
            ref[...] = value


def turn_kernel(*refs):
    rows = refs[0].shape[0]
    for i, ref in enumerate(refs[:-1]):
        refs[-1][:, i * rows : (i + 1) * rows] = ref[...].T


def turn(order, pieces):
    rows, width = pieces[0].shape
    total = rows * len(pieces)
    return order(
        turn_kernel,
        list(pieces),
        [pl.BlockSpec((rows, TILE), lambda i: (0, i))] * len(pieces),
        [pl.BlockSpec((TILE, total), lambda i: (i, 0))],
        [jax.ShapeDtypeStruct((width, total), jnp.bfloat16)],
        (width // TILE,),
        0,
        4 * total * width,
        "turn",
    )[0]


def grad_out_kernel(core_ref, cot_ref, valid_ref, out_ref, turned_ref):
    out = to_bf(to_f(cot_ref[...]) * valid_ref[...])
    out_ref[...] = out
    turned_ref[...] = out.T


def grad_out_of(order, core, cotangent, valid):
    total, width = cotangent.shape
    block = total // 4
    return order(
        grad_out_kernel,
        [cotangent, valid],
        [
            pl.BlockSpec((block, width), lambda i, core_ref: (lax.rem(i + core_ref[0] * 2, 4), 0)),
            pl.BlockSpec((block, 1), lambda i, core_ref: (i, 0)),
        ],
        [
            pl.BlockSpec((block, width), lambda i, core_ref: (i, 0)),
            pl.BlockSpec((width, block), lambda i, core_ref: (0, i)),
        ],
        [
            jax.ShapeDtypeStruct((total, width), jnp.bfloat16),
            jax.ShapeDtypeStruct((width, total), jnp.bfloat16),
        ],
        (4,),
        0,
        6 * total * width,
        "grad_out",
        scalars=(core,),
    )


def middle_kernel(core_ref, tok_ref, gain_ref, *refs):
    mine, come = pick_piece(refs[:PIECES]), pick_piece(refs[PIECES : 2 * PIECES])
    mid_ref, *h_refs = refs[2 * PIECES :]
    middle = to_f(tok_ref[...]) + (to_f(mine) + to_f(come))
    factor = lax.rsqrt(jnp.mean(middle * middle, axis=-1, keepdims=True) + EPS)
    mid_ref[...] = middle
    put_piece(h_refs, to_bf(middle * factor * gain_ref[...]))


def middle_of(order, core, tokens, mine, come, gain):
    piece, width = mine[0].shape
    half = piece * PIECES
    block = half // 4
    specs = piece_specs(piece, width, block)
    middle, *h = order(
        middle_kernel,
        [tokens, gain, *mine, *come],
        [
            pl.BlockSpec((block, width), lambda i, core_ref: (core_ref[0] * 4 + i, 0)),
            pl.BlockSpec((1, width), lambda i, core_ref: (0, 0)),
        ]
        + specs * 2,
        [pl.BlockSpec((block, width), lambda i, core_ref: (i, 0))] + specs,
        [jax.ShapeDtypeStruct((half, width), jnp.float32)]
        + [jax.ShapeDtypeStruct((piece, width), jnp.bfloat16)] * PIECES,
        (4,),
        0,
        9 * MIB,
        "middle",
        scalars=(core,),
    )
    return middle, h


def norm_back_kernel(core_ref, x_ref, gain_ref, up_ref, *refs):
    mine, come = pick_piece(refs[:PIECES]), pick_piece(refs[PIECES : 2 * PIECES])
    outs = refs[2 * PIECES :]
    grad = to_f(mine) + to_f(come)
    x = to_f(x_ref[...])
    factor = lax.rsqrt(jnp.mean(x * x, axis=-1, keepdims=True) + EPS)
    normed = x * factor
    weighted = grad * gain_ref[...]
    inner = jnp.mean(weighted * normed, axis=-1, keepdims=True)
    out = to_f(up_ref[...]) + factor * (weighted - normed * inner)
    if len(outs) > PIECES:
        outs[0][...] = out
        put_piece(outs[1:], to_bf(out))
    else:
        put_piece(outs, out)


def norm_back(order, core, mine, come, x, gain, up, by_core):
    piece, width = mine[0].shape
    half = piece * PIECES
    block = half // 4
    at = pl.BlockSpec((block, width), lambda i, core_ref: (i, 0))
    picked = pl.BlockSpec((block, width), lambda i, core_ref: (core_ref[0] * 4 + i, 0))
    specs = piece_specs(piece, width, block)
    if by_core:
        shapes = [jax.ShapeDtypeStruct((piece, width), jnp.float32)] * PIECES
    else:
        shapes = [jax.ShapeDtypeStruct((half, width), jnp.float32)]
        shapes += [jax.ShapeDtypeStruct((piece, width), jnp.bfloat16)] * PIECES
    return order(
        norm_back_kernel,
        [x, gain, up, *mine, *come],
        [picked if by_core else at, pl.BlockSpec((1, width), lambda i, core_ref: (0, 0)), at] + specs * 2,
        specs if by_core else [at] + specs,
        shapes,
        (4,),
        0,
        10 * MIB,
        "norm_back",
        scalars=(core,),
    )


def layer_kernel(middle_ref, *refs):
    mine, come = pick_piece(refs[:PIECES]), pick_piece(refs[PIECES : 2 * PIECES])
    put_piece(refs[2 * PIECES :], to_bf(middle_ref[...] + (to_f(mine) + to_f(come))))


def layer_of(order, middle, mine, come):
    piece, width = mine[0].shape
    block = piece * PIECES // 4
    specs = piece_specs(piece, width, block)
    return order(
        layer_kernel,
        [middle, *mine, *come],
        [pl.BlockSpec((block, width), lambda i: (i, 0))] + specs * 2,
        specs,
        [jax.ShapeDtypeStruct((piece, width), jnp.bfloat16)] * PIECES,
        (4,),
        0,
        5 * MIB,
        "layer",
    )


def tensor_gather(value, rank):
    mate = core_swap(value)
    pair = jnp.where(lax.rem(rank, 2) == 0, jnp.stack([value, mate]), jnp.stack([mate, value]))
    come = chip_swap(pair)
    return jnp.where(
        lax.div(rank, 2) == 0,
        jnp.concatenate([pair, come], axis=0),
        jnp.concatenate([come, pair], axis=0),
    )


def body(
    tokens,
    lengths,
    cotangent,
    q_weight,
    q_bias,
    k_weight,
    k_bias,
    v_weight,
    v_bias,
    o_weight,
    attn_gain,
    ffn_gain,
    gate_weight,
    up_weight,
    down_weight,
):
    rows, local, width = tokens.shape
    total = rows * local
    half = total // 2
    heads = q_weight.shape[1] // HD
    ranks = lax.axis_size("tensor")
    seqs = lax.axis_size("seq")
    rank = lax.axis_index("tensor")
    dp_index = lax.axis_index("dp")
    seq_index = lax.axis_index("seq")
    core = lax.rem(rank, 2)
    head = lax.div(rank, 2)
    core_one = core.reshape(1)
    hops = min(seqs - 1, -(-(MOST - 1) // local))
    reach = hops * local

    def own_first(value):
        turned = jnp.concatenate([value[rows // 2 :], value[: rows // 2]], axis=0)
        return jnp.where(core == 0, value, turned)

    slots = jnp.arange(lengths.shape[1], dtype=jnp.int32)
    lens = own_first(lengths)
    ends = jnp.sum(jnp.where(slots[None, :] <= slots[:, None], lens[:, None, :], 0), axis=2)
    spot = seq_index * local + jnp.arange(local, dtype=jnp.int32)
    begun = jnp.max(
        jnp.where(ends[:, None, :] <= spot[None, :, None], ends[:, None, :], 0), axis=2
    )
    valid = to_f(spot[None, :] < ends[:, -2:-1])
    position = (spot[None, :] - begun).reshape(total, 1)
    freqs = ROPE_BASE ** (-(jnp.arange(HD // 2, dtype=jnp.float32) * 2.0) / HD)
    angles = to_f(position) * freqs[None, :]
    cosine, sine = jnp.cos(angles), jnp.sin(angles)
    cosine = jnp.concatenate([cosine, cosine], axis=1)
    sine = jnp.concatenate([-sine, sine], axis=1)
    start = begun - (seq_index * local - reach)
    low = jnp.maximum(lax.div(jnp.maximum(start[:, ::Q_BLOCK], 0), K_BLOCK), 0)
    start = start.reshape(rows, 1, local)

    key_side = core == 0
    kv_weight = jnp.where(
        key_side,
        lax.dynamic_slice_in_dim(k_weight, head * HD, HD, 1),
        lax.dynamic_slice_in_dim(v_weight, head * HD, HD, 1),
    )
    kv_bias = jnp.where(
        key_side,
        lax.dynamic_slice_in_dim(k_bias, head * HD, HD, 0),
        lax.dynamic_slice_in_dim(v_bias, head * HD, HD, 0),
    )
    weight = jnp.concatenate([q_weight, kv_weight], axis=1)
    bias = to_f(jnp.concatenate([q_bias, kv_bias])).reshape(1, -1)
    gain_one = to_f(attn_gain).reshape(1, width)
    gain_two = to_f(ffn_gain).reshape(1, width)

    h_one, q_rot, kv = first(
        core_one, tokens.reshape(total, width), gain_one, weight, bias, cosine, sine
    )
    kv = kv.reshape(rows, local, HD)
    span = [shifted(kv, h) for h in range(hops, 0, -1)] + [kv]
    mate = [core_swap(piece) for piece in span]
    q_rows = q_rot.reshape(rows, local, heads * HD)
    mixed_rows, lse = attend(low, core_one, q_rows, start, span, mate)
    mixed = mixed_rows.reshape(total, heads * HD)

    order = Order()
    flat_tokens = tokens.reshape(total, width)
    dps = lax.axis_size("dp")
    near_pair = dps == 2 and seqs == 4
    part = width // dps
    share = part // seqs
    gate_t, up_t, down_t = gate_weight.T, up_weight.T, down_weight.T
    units = gate_t.shape[0]
    tiles = -(-units // TILE)
    cut = (tiles + 1) // 2
    long = -(-2 * tiles // 3)
    one, two = seq_index ^ 1, seq_index ^ 2
    three = seq_index ^ 3
    quad = jnp.stack([one, three, seq_index, two])

    begin = (dp_index * seqs + seq_index) * share

    def rows_of(value):
        return lax.dynamic_slice_in_dim(value, begin, share, 0)

    class Rows:
        def __init__(self, lefts, rights, parts, tile=TILE, sent=None):
            self.args = (order, lefts, rights, parts)
            self.tile = tile
            if not near_pair:
                (whole,) = share_of(*self.args, width, 0, tile)
                self.whole = lax.psum_scatter(whole, ("dp", "seq"), scatter_dimension=0, tiled=True)
                return
            if sent is None:
                (sent,) = share_of(*self.args, part, 1 - dp_index, tile)
            self.come = lax.ppermute(sent, "dp", flipped("dp", 0))

        def own(self):
            if near_pair:
                send, self.keep = share_of(*self.args, part, dp_index, self.tile, self.come, quad)
                self.come = lax.ppermute(send, "seq", flipped("seq", 0))

        def relay(self):
            if near_pair:
                sent = relay(order, self.keep, self.come, share)
                self.last = lax.ppermute(sent, "seq", flipped("seq", 1))

        def settled(self):
            if near_pair:
                order.arrived(self.last)

        def result(self):
            return [self.keep, self.come, self.last] if near_pair else [self.whole]

    class SeqFirst(Rows):
        def __init__(self, lefts, rights, parts, tile=TILE):
            if not near_pair:
                super().__init__(lefts, rights, parts, tile)
                return
            (whole,) = share_of(order, lefts, rights, parts, width, 0, tile, None, None, (dps, seqs))
            self.mine = lax.psum_scatter(whole, "seq", scatter_dimension=0, tiled=True)

        def across(self):
            if near_pair:
                sent = lax.dynamic_slice_in_dim(self.mine, (1 - dp_index) * share, share, 0)
                self.mine = lax.dynamic_slice_in_dim(self.mine, dp_index * share, share, 0)
                order.arrived(sent, self.mine)
                self.come = lax.ppermute(sent, "dp", flipped("dp", 0))

        def settled(self):
            if near_pair:
                order.arrived(self.come)

        def result(self):
            return [self.mine, self.come] if near_pair else [self.whole]

    class Scattered(Rows):
        def own(self):
            if near_pair:
                (mine,) = share_of(*self.args, part, dp_index, self.tile, self.come)
                self.whole = lax.psum_scatter(mine, "seq", scatter_dimension=0, tiled=True)

        def settled(self):
            order.arrived(self.whole)

        def result(self):
            return [self.whole]

    sent = core_swaps(narrow(order, [(mixed, o_weight)], 1, (), 1))
    mine = narrow(order, [(mixed, o_weight)], 0, sent, 1)
    come = chip_swaps(mine)
    grad_ffn, grad_ffn_t = grad_out_of(
        order, core_one, cotangent.reshape(total, width), valid.reshape(total, 1)
    )
    gate_rows, up_rows = rows_of(gate_weight), rows_of(up_weight)
    order.arrived(gate_rows, up_rows)
    grad_hidden = grad_hidden_of(order, grad_ffn, down_t)
    h_one_t = turn(order, [h_one])
    middle, h_two = middle_of(order, core_one, flat_tokens, mine, come, gain_two)
    h_two += core_swaps(h_two)
    hidden, grad_gate, grad_up = gated(order, h_two, grad_hidden, gate_t, up_t)

    down_b = SeqFirst([grad_ffn_t], [hidden], [(0, 0, cut, tiles - cut, 0)])
    down_a = Rows([grad_ffn_t], [hidden], [(0, 0, 0, cut, 0)])
    pairs = [(grad_gate, gate_t), (grad_up, up_t)]
    sent = core_swaps(narrow(order, pairs, 1))
    mine = narrow(order, pairs, 0, sent)
    come = chip_swaps(mine)
    h_two_t = turn(order, h_two)
    if near_pair:
        sends = share_of(
            order,
            [h_two_t],
            [grad_gate, grad_up],
            [(0, 0, 0, tiles, 0), (0, 1, 0, long, 1), (0, 1, long, tiles - long, 2)],
            part,
            1 - dp_index,
            TILE,
        )
    else:
        sends = [None] * 3

    def half_rows(kind, right, begin, end, sent):
        return kind([h_two_t], [right], [(0, 0, begin, end - begin, 0)], TILE, sent)

    gate = half_rows(Scattered, grad_gate, 0, tiles, sends[0])
    up_a = half_rows(Rows, grad_up, 0, long, sends[1])
    up_b = half_rows(Rows, grad_up, long, tiles, sends[2])
    down_a.own()
    grad_middle, *branch = norm_back(order, core_one, mine, come, middle, gain_two, grad_ffn, False)
    branch += core_swaps(branch)
    grad_mixed = mixed_back(order, branch, o_weight).reshape(rows, local, heads * HD)
    grad_q_rows, keep, sent = attend_back(
        order, low, core_one, q_rows, start, span, mate, grad_mixed, mixed_rows, lse, cosine, sine
    )
    both_come = core_swap(sent)
    branch_t = turn(order, branch)
    down_a.relay()
    own_kv, *pieces = fold(order, keep, both_come, local)
    moving = shifted(pieces[-1], -1) if pieces else None
    ffn_sent = core_swaps(narrow(order, [(hidden, down_t)], 1))
    for piece in pieces[-2::-1]:
        moving = shifted(carry(order, piece, moving), -1)
    grad_qkv, bias_sum = join(
        order, core_one, grad_q_rows, own_kv, [] if moving is None else [moving], cosine, sine
    )
    sent = core_swaps(narrow(order, [(grad_qkv, weight)], 1, (), 1))
    down_b.across()
    gate.own()
    mine = narrow(order, [(grad_qkv, weight)], 0, sent, 1)
    come = chip_swaps(mine)
    last_parts = [(0, 0, 0, grad_qkv.shape[1] // HD, 0), (1, 1, 0, heads, 0)]
    last = Rows([h_one_t, branch_t], [grad_qkv, mixed], last_parts, HD)
    ffn_mine = narrow(order, [(hidden, down_t)], 0, ffn_sent)
    token = norm_back(order, core_one, mine, come, flat_tokens, gain_one, grad_middle, True)
    token += core_swaps(token)
    ffn_come = chip_swaps(ffn_mine)
    up_a.own()
    token_grad = place(order, core_one, token).reshape(rows, local, width)
    layer = layer_of(order, middle, ffn_mine, ffn_come)
    layer += core_swaps(layer)
    last.own()
    layer_out = place(order, core_one, layer).reshape(rows, local, width)
    up_a.relay()
    down_a.settled()
    up_b.own()
    down_b.settled()
    up_a.settled()
    last.relay()
    (down_grad,) = finish(order, [down_a.result(), down_b.result()], share, units, TILE)
    if near_pair:
        bias_come = lax.ppermute(bias_sum, "dp", flipped("dp", 0))
        bias_all = bias_add(order, bias_sum, bias_come)
        bias_come = lax.ppermute(bias_all, "seq", flipped("seq", 0))
    up_b.relay()
    gate_grad, gate_term = finish(order, [gate.result()], share, units, TILE, gate_rows)
    wide_columns = grad_qkv.shape[1]
    (last_grad,) = finish(order, [last.result()], share, wide_columns + heads * HD, HD)
    if near_pair:
        bias_all = bias_add(order, bias_all, bias_come)
        bias_come = lax.ppermute(bias_all, "seq", flipped("seq", 1))
        bias_all = (bias_all + bias_come)[:1]
    else:
        bias_all = lax.psum(bias_sum[:1], ("dp", "seq"))
    up_grad, up_term = finish(order, [up_a.result(), up_b.result()], share, units, TILE, up_rows)
    qkv_grad, o_grad = last_grad[:, :wide_columns], last_grad[:, wide_columns:]

    attn_term = jnp.sum(to_f(rows_of(weight)) * qkv_grad, axis=1)
    ffn_term = jnp.sum(gate_term + up_term, axis=1)
    columns = heads * HD
    room = -(-share // HD) * HD - share
    terms = jnp.pad(jnp.stack([ffn_term, attn_term]), ((0, 0), (0, room))).reshape(-1, HD)
    packed = jnp.concatenate([qkv_grad[:, columns:], bias_all.reshape(-1, HD), terms], axis=0)
    gathered = tensor_gather(packed, rank)
    term_rows = terms.shape[0]
    bias_count = bias_all.shape[1] // HD
    terms = gathered[:, share + bias_count :].reshape(ranks, 2, -1)[:, :, :share]
    ffn_gain_grad, attn_gain_grad = terms[0] + terms[1] + (terms[2] + terms[3])
    attn_gain_grad = attn_gain_grad / lax.dynamic_slice_in_dim(gain_one[0], begin, share, 0)
    ffn_gain_grad = ffn_gain_grad / lax.dynamic_slice_in_dim(gain_two[0], begin, share, 0)
    q_grad = qkv_grad[:, :columns]
    kv_parts = lax.dynamic_slice_in_dim(gathered, rank * (share // ranks), share // ranks, 1)
    k_grad = jnp.concatenate([kv_parts[2 * i] for i in range(KVH)], axis=1)
    v_grad = jnp.concatenate([kv_parts[2 * i + 1] for i in range(KVH)], axis=1)
    biases = gathered[:, share : share + bias_count]
    q_bias_grad = biases[:, :heads].reshape(-1)
    k_bias_grad = biases[0::2, heads].reshape(-1)
    v_bias_grad = biases[1::2, heads].reshape(-1)
    return (
        layer_out,
        token_grad,
        q_grad,
        q_bias_grad,
        k_grad,
        k_bias_grad,
        v_grad,
        v_bias_grad,
        o_grad,
        attn_gain_grad,
        ffn_gain_grad,
        gate_grad,
        up_grad,
        down_grad,
    )


def solution(mesh):
    in_specs = (
        P("dp", "seq", None),
        P("dp", None),
        P("dp", "seq", None),
        P(None, "tensor"),
        P("tensor"),
        P(),
        P(),
        P(),
        P(),
        P(None, "tensor"),
        P(),
        P(),
        P(None, "tensor"),
        P(None, "tensor"),
        P(None, "tensor"),
    )
    out_specs = (
        P("dp", "seq", None),
        P("dp", "seq", None),
        P(("dp", "seq"), "tensor"),
        P(),
        P(("dp", "seq", "tensor"), None),
        P(),
        P(("dp", "seq", "tensor"), None),
        P(),
        P(("dp", "seq"), "tensor"),
        P(("dp", "seq")),
        P(("dp", "seq")),
        P(("dp", "seq"), "tensor"),
        P(("dp", "seq"), "tensor"),
        P(("dp", "seq"), "tensor"),
    )
    return jax.shard_map(body, mesh=mesh, in_specs=in_specs, out_specs=out_specs, check_vma=False)
```

```python
import functools
import math

import jax
import jax.numpy as jnp
from jax import lax
from jax.experimental import pallas as pl
from jax.experimental.pallas import tpu as pltpu
from jax.sharding import PartitionSpec as P

KVH = 2
HD = 128
MOST = 1024
EPS = 1e-06
ROPE_BASE = 10000.0
NEG_FILL = -1e30
Q_BLOCK = 256
K_BLOCK = 256
MIB = 1 << 20
LIGHT = 1000
TILE = 256
PIECES = 2
SCALE = 1.0 / math.sqrt(HD)


def to_bf(value):
    return value.astype(jnp.bfloat16)


def to_f(value):
    return value.astype(jnp.float32)


def dot(left, right, left_dim=1, right_dim=0):
    return lax.dot_general(
        left,
        right,
        (((left_dim,), (right_dim,)), ((), ())),
        preferred_element_type=jnp.float32,
    )


def flipped(axis, bit):
    return [(i, i ^ (1 << bit)) for i in range(lax.axis_size(axis))]


def core_swap(value):
    return lax.ppermute(value, "tensor", flipped("tensor", 0))


def chip_swap(value):
    return lax.ppermute(value, "tensor", flipped("tensor", 1))


def core_swaps(values):
    return [core_swap(value) for value in values]


def chip_swaps(values):
    return [chip_swap(value) for value in values]


def shifted(value, hops):
    count = lax.axis_size("seq")
    route = [(i, i + hops) for i in range(count) if 0 <= i + hops < count]
    return lax.ppermute(value, "seq", route)


def cost(flops, read):
    return pl.CostEstimate(flops=flops // LIGHT, bytes_accessed=read // LIGHT, transcendentals=0)


class Order:
    def __init__(self):
        self.mark = None
        self.touched = []

    def arrived(self, *values):
        self.touched.extend(values)

    def __call__(self, kernel, args, in_specs, out_specs, out_shape, grid, flops, read, name, scalars=(), scratch=()):
        anchor = ([] if self.mark is None else [self.mark]) + self.touched
        self.touched = []
        count = len(scalars) + len(args)
        outs = len(out_shape)

        def run(*refs):
            rest = refs[count + len(anchor) :]
            kernel(*refs[:count], *rest[:outs], *rest[outs + 1 :])
            rest[outs][...] = jnp.zeros(rest[outs].shape, jnp.float32)

        *results, self.mark = pl.pallas_call(
            run,
            grid_spec=pltpu.PrefetchScalarGridSpec(
                num_scalar_prefetch=len(scalars),
                grid=grid,
                in_specs=list(in_specs) + anchors(len(anchor)),
                out_specs=list(out_specs) + [mark_spec()],
                scratch_shapes=list(scratch),
            ),
            out_shape=list(out_shape) + [MARK],
            compiler_params=pltpu.CompilerParams(vmem_limit_bytes=32 * MIB),
            cost_estimate=cost(flops, read),
            name=name,
        )(*scalars, *args, *anchor)
        return results


def first_kernel(core_ref, tok_ref, gain_ref, w_ref, b_ref, cos_ref, sin_ref, h_ref, q_ref, kv_ref):
    x = to_f(tok_ref[...])
    factor = lax.rsqrt(jnp.mean(x * x, axis=-1, keepdims=True) + EPS)
    h = to_bf(x * factor * gain_ref[...])
    h_ref[...] = h
    lin = dot(h, w_ref[...]) + b_ref[...]
    cosine = cos_ref[...]
    sine = sin_ref[...]
    heads = q_ref.shape[1] // HD
    for head in range(heads):
        part = lin[:, head * HD : (head + 1) * HD]
        q_ref[:, head * HD : (head + 1) * HD] = to_bf(
            part * cosine + pltpu.roll(part, HD // 2, 1) * sine
        )
    part = lin[:, heads * HD :]
    is_key = core_ref[0] == 0
    kv_ref[...] = to_bf(
        part * jnp.where(is_key, cosine, 1.0)
        + pltpu.roll(part, HD // 2, 1) * jnp.where(is_key, sine, 0.0)
    )


def first(core, tokens, gain, weight, bias, cosine, sine):
    total, width = tokens.shape
    columns = weight.shape[1]
    block = total // 4
    half = 2

    def flip(i, core_ref):
        return (lax.rem(i + core_ref[0] * half, 4), 0)

    def at(i, core_ref):
        return (i, 0)

    def whole(i, core_ref):
        return (0, 0)

    return pl.pallas_call(
        first_kernel,
        grid_spec=pltpu.PrefetchScalarGridSpec(
            num_scalar_prefetch=1,
            grid=(4,),
            in_specs=[
                pl.BlockSpec((block, width), flip),
                pl.BlockSpec((1, width), whole),
                pl.BlockSpec((width, columns), whole),
                pl.BlockSpec((1, columns), whole),
                pl.BlockSpec((block, HD), at),
                pl.BlockSpec((block, HD), at),
            ],
            out_specs=[
                pl.BlockSpec((block, width), at),
                pl.BlockSpec((block, columns - HD), at),
                pl.BlockSpec((block, HD), at),
            ],
        ),
        out_shape=[
            jax.ShapeDtypeStruct((total, width), jnp.bfloat16),
            jax.ShapeDtypeStruct((total, columns - HD), jnp.bfloat16),
            jax.ShapeDtypeStruct((total, HD), jnp.bfloat16),
        ],
        compiler_params=pltpu.CompilerParams(vmem_limit_bytes=32 * MIB),
        cost_estimate=cost(2 * total * width * columns, 9 * MIB),
        name="first",
    )(core, tokens, gain, weight, bias, cosine, sine)


def stacked(ref, start, count, heads):
    return jnp.concatenate(
        [ref[0, pl.ds(start, count), h * HD : (h + 1) * HD] for h in range(heads)], axis=0
    )


def bounds(start_ref, index, heads, reach):
    first_key = jnp.concatenate(
        [start_ref[0, :, pl.ds(index * Q_BLOCK, Q_BLOCK)]] * heads, axis=1
    )
    place = reach + index * Q_BLOCK + lax.broadcasted_iota(jnp.int32, (1, Q_BLOCK), 1)
    return first_key, jnp.concatenate([place] * heads, axis=1)


def gather_span(core, refs, span):
    count = len(refs) // 2
    local = refs[0].shape[1]
    for i in range(count):
        here = slice(i * local, (i + 1) * local)
        span[core, here] = refs[i][0]
        span[1 - core, here] = refs[count + i][0]


def attend_kernel(heads, blocks, pieces, low_ref, core_ref, q_ref, start_ref, *refs):
    o_ref, lse_ref, acc, span = refs[2 * pieces :]
    row = pl.program_id(0)
    wide = heads * Q_BLOCK
    reach = (pieces - 1) * q_ref.shape[1]
    gather_span(core_ref[0], refs[: 2 * pieces], span)
    for index in range(blocks):
        q = stacked(q_ref, index * Q_BLOCK, Q_BLOCK, heads)
        first_key, place = bounds(start_ref, index, heads, reach)
        acc[...] = jnp.zeros_like(acc)

        def step(j, carry):
            top, total = carry
            keys = pl.ds(pl.multiple_of(j * K_BLOCK, K_BLOCK), K_BLOCK)
            s = dot(span[0, keys], q, 1, 1) * SCALE
            key = j * K_BLOCK + lax.broadcasted_iota(jnp.int32, (K_BLOCK, wide), 0)
            s = jnp.where((key >= first_key) & (key <= place), s, NEG_FILL)
            later = jnp.maximum(top, jnp.max(s, axis=0, keepdims=True))
            p = jnp.exp(s - later)
            fade = jnp.exp(top - later)
            total = total * fade + jnp.sum(p, axis=0, keepdims=True)
            acc[...] = acc[...] * fade + dot(span[1, keys], to_bf(p), 0, 0)
            return later, total

        last = (reach + (index + 1) * Q_BLOCK - 1) // K_BLOCK + 1
        top, total = lax.fori_loop(
            low_ref[row, index],
            last,
            step,
            (jnp.full((1, wide), NEG_FILL, jnp.float32), jnp.zeros((1, wide), jnp.float32)),
        )
        out = to_bf((acc[...] / total).T)
        for h in range(heads):
            o_ref[0, index * Q_BLOCK : (index + 1) * Q_BLOCK, h * HD : (h + 1) * HD] = out[
                h * Q_BLOCK : (h + 1) * Q_BLOCK
            ]
        lse_ref[0, index : index + 1, :] = top + jnp.log(total)


def span_specs(rows, local, pieces):
    near = pl.BlockSpec((1, local, HD), lambda i, *refs: (i, 0, 0))
    far = pl.BlockSpec((1, local, HD), lambda i, *refs: (lax.rem(i + rows // 2, rows), 0, 0))
    return [near] * pieces + [far] * pieces


def attend(low, core, q, start, span, mate):
    rows, local, columns = q.shape
    pieces = len(span)
    heads = columns // HD
    blocks = local // Q_BLOCK

    def at(i, *refs):
        return (i, 0, 0)

    return pl.pallas_call(
        functools.partial(attend_kernel, heads, blocks, pieces),
        grid_spec=pltpu.PrefetchScalarGridSpec(
            num_scalar_prefetch=2,
            grid=(rows,),
            in_specs=[pl.BlockSpec((1, local, columns), at), pl.BlockSpec((1, 1, local), at)]
            + span_specs(rows, local, pieces),
            out_specs=[
                pl.BlockSpec((1, local, columns), at),
                pl.BlockSpec((1, blocks, heads * Q_BLOCK), at),
            ],
            scratch_shapes=[
                pltpu.VMEM((HD, heads * Q_BLOCK), jnp.float32),
                pltpu.VMEM((2, pieces * local, HD), jnp.bfloat16),
            ],
        ),
        out_shape=[
            jax.ShapeDtypeStruct((rows, local, columns), jnp.bfloat16),
            jax.ShapeDtypeStruct((rows, blocks, heads * Q_BLOCK), jnp.float32),
        ],
        compiler_params=pltpu.CompilerParams(vmem_limit_bytes=32 * MIB),
        cost_estimate=cost(8_000_000_000, 4 * MIB),
        name="attend",
    )(low, core, q, start, *span, *mate)


def attend_back_kernel(
    heads, blocks, pieces, low_ref, core_ref, q_ref, start_ref, g_ref, o_ref, lse_ref, cos_ref, sin_ref, *refs
):
    gq_ref, keep_ref, send_ref, acc, gk, gv, span = refs[2 * pieces :]
    row = pl.program_id(0)
    wide = heads * Q_BLOCK
    reach = (pieces - 1) * q_ref.shape[1]
    core = core_ref[0]
    gather_span(core, refs[: 2 * pieces], span)
    gk[...] = jnp.zeros_like(gk)
    gv[...] = jnp.zeros_like(gv)
    for index in range(blocks):
        q = stacked(q_ref, index * Q_BLOCK, Q_BLOCK, heads)
        g = stacked(g_ref, index * Q_BLOCK, Q_BLOCK, heads)
        o = stacked(o_ref, index * Q_BLOCK, Q_BLOCK, heads)
        inner = jnp.sum((to_f(g) * to_f(o)).T, axis=0, keepdims=True)
        lse = lse_ref[0, index : index + 1, :]
        first_key, place = bounds(start_ref, index, heads, reach)
        acc[...] = jnp.zeros_like(acc)

        def step(j, carry):
            keys = pl.ds(pl.multiple_of(j * K_BLOCK, K_BLOCK), K_BLOCK)
            k = span[0, keys]
            s = dot(k, q, 1, 1) * SCALE
            key = j * K_BLOCK + lax.broadcasted_iota(jnp.int32, (K_BLOCK, wide), 0)
            p = jnp.where((key >= first_key) & (key <= place), jnp.exp(s - lse), 0.0)
            gp = dot(span[1, keys], g, 1, 1)
            gs = to_bf(p * (gp - inner))
            gv[keys] += dot(to_bf(p), g)
            gk[keys] += dot(gs, q)
            acc[...] += dot(k, gs, 0, 0)
            return carry

        last = (reach + (index + 1) * Q_BLOCK - 1) // K_BLOCK + 1
        lax.fori_loop(low_ref[row, index], last, step, 0)
        gq = acc[...].T * SCALE
        here = slice(index * Q_BLOCK, (index + 1) * Q_BLOCK)
        cosine, sine = cos_ref[here], sin_ref[here]
        for h in range(heads):
            part = gq[h * Q_BLOCK : (h + 1) * Q_BLOCK]
            gq_ref[0, here, h * HD : (h + 1) * HD] = to_bf(
                part * cosine + pltpu.roll(part * sine, HD // 2, 1)
            )
    is_key = core == 0
    keys, values = gk[...] * SCALE, gv[...]
    keep_ref[0] = to_bf(jnp.where(is_key, keys, values))
    send_ref[0] = to_bf(jnp.where(is_key, values, keys))


def attend_back(order, low, core, q, start, span, mate, grad, out, lse, cosine, sine):
    rows, local, columns = q.shape
    pieces = len(span)
    window = pieces * local
    heads = columns // HD
    blocks = local // Q_BLOCK

    def at(i, *refs):
        return (i, 0, 0)

    table = pl.BlockSpec((local, HD), lambda i, *refs: (i, 0))
    tokens = pl.BlockSpec((1, local, columns), at)
    return order(
        functools.partial(attend_back_kernel, heads, blocks, pieces),
        [q, start, grad, out, lse, cosine, sine, *span, *mate],
        [
            tokens,
            pl.BlockSpec((1, 1, local), at),
            tokens,
            tokens,
            pl.BlockSpec((1, blocks, heads * Q_BLOCK), at),
            table,
            table,
        ]
        + span_specs(rows, local, pieces),
        [tokens, pl.BlockSpec((1, window, HD), at), pl.BlockSpec((1, window, HD), at)],
        [
            jax.ShapeDtypeStruct((rows, local, columns), jnp.bfloat16),
            jax.ShapeDtypeStruct((rows, window, HD), jnp.bfloat16),
            jax.ShapeDtypeStruct((rows, window, HD), jnp.bfloat16),
        ],
        (rows,),
        20_000_000_000,
        6 * MIB,
        "attend_back",
        scalars=(low, core),
        scratch=[
            pltpu.VMEM((HD, heads * Q_BLOCK), jnp.float32),
            pltpu.VMEM((window, HD), jnp.float32),
            pltpu.VMEM((window, HD), jnp.float32),
            pltpu.VMEM((2, window, HD), jnp.bfloat16),
        ],
    )


def fold_kernel(keep_ref, come_ref, own_ref, *send_refs):
    local = own_ref.shape[1]
    total = to_f(keep_ref[0]) + to_f(come_ref[0])
    reach = total.shape[0] - local
    own_ref[0] = total[reach:]
    for hop, ref in enumerate(send_refs, 1):
        ref[0] = to_bf(total[reach - hop * local : reach - (hop - 1) * local])


def fold(order, keep, come, local):
    rows, window = keep.shape[:2]
    hops = window // local - 1
    out = pl.BlockSpec((1, local, HD), lambda i: (i, 0, 0))
    return order(
        fold_kernel,
        [keep, come],
        [
            pl.BlockSpec((1, window, HD), lambda i: (i, 0, 0)),
            pl.BlockSpec((1, window, HD), lambda i: (lax.rem(i + rows // 2, rows), 0, 0)),
        ],
        [out] * (hops + 1),
        [jax.ShapeDtypeStruct((rows, local, HD), jnp.float32)]
        + [jax.ShapeDtypeStruct((rows, local, HD), jnp.bfloat16)] * hops,
        (rows,),
        0,
        4 * MIB,
        "fold",
    )


def carry_kernel(piece_ref, come_ref, out_ref):
    out_ref[...] = to_bf(to_f(piece_ref[...]) + to_f(come_ref[...]))


def carry(order, piece, come):
    rows, local, columns = piece.shape
    at = pl.BlockSpec((1, local, columns), lambda i: (i, 0, 0))
    return order(
        carry_kernel,
        [piece, come],
        [at, at],
        [at],
        [jax.ShapeDtypeStruct(piece.shape, jnp.bfloat16)],
        (rows,),
        0,
        2 * MIB,
        "carry",
    )[0]


def bias_kernel(left_ref, right_ref, out_ref):
    out_ref[...] = left_ref[...] + right_ref[...]


def bias_add(order, left, right):
    whole = pl.BlockSpec(left.shape, lambda i: (0, 0))
    return order(
        bias_kernel,
        [left, right],
        [whole, whole],
        [whole],
        [jax.ShapeDtypeStruct(left.shape, jnp.float32)],
        (1,),
        0,
        MIB,
        "bias",
    )[0]


def join_kernel(hops, core_ref, gq_ref, cos_ref, sin_ref, own_ref, *refs):
    out_ref, sum_ref = refs[-2:]
    columns = gq_ref.shape[2]
    grad = own_ref[0]
    for ref in refs[:hops]:
        grad = grad + to_f(ref[0])
    is_key = core_ref[0] == 0
    cosine = jnp.where(is_key, cos_ref[...], 1.0)
    sine = jnp.where(is_key, sin_ref[...], 0.0)
    kv = to_bf(grad * cosine + pltpu.roll(grad * sine, HD // 2, 1))
    q = gq_ref[0]
    out_ref[:, :columns] = q
    out_ref[:, columns:] = kv

    @pl.when(pl.program_id(0) == 0)
    def _():
        sum_ref[...] = jnp.zeros(sum_ref.shape, jnp.float32)

    sum_ref[:, :columns] += jnp.sum(to_f(q), axis=0, keepdims=True)
    sum_ref[:, columns:] += jnp.sum(to_f(kv), axis=0, keepdims=True)


def join(order, core, grad_q, own, comes, cosine, sine):
    rows, local, columns = grad_q.shape
    wide = columns + HD

    def at(i, *refs):
        return (i, 0, 0)

    piece = pl.BlockSpec((1, local, HD), at)
    table = pl.BlockSpec((local, HD), lambda i, *refs: (i, 0))
    return order(
        functools.partial(join_kernel, len(comes)),
        [grad_q, cosine, sine, own, *comes],
        [pl.BlockSpec((1, local, columns), at), table, table, piece] + [piece] * len(comes),
        [
            pl.BlockSpec((local, wide), lambda i, *refs: (i, 0)),
            pl.BlockSpec((8, wide), lambda i, *refs: (0, 0)),
        ],
        [
            jax.ShapeDtypeStruct((rows * local, wide), jnp.bfloat16),
            jax.ShapeDtypeStruct((8, wide), jnp.float32),
        ],
        (rows,),
        0,
        4 * MIB,
        "join",
        scalars=(core,),
    )


def mixed_back_kernel(w_ref, *refs):
    rows = refs[0].shape[0]
    for i, ref in enumerate(refs[:-1]):
        refs[-1][i * rows : (i + 1) * rows] = to_bf(dot(ref[...], w_ref[...]))


def mixed_back(order, pieces, weight):
    rows, width = pieces[0].shape
    total = rows * len(pieces)
    columns = weight.shape[1]

    def whole(i):
        return (0, 0)

    return order(
        mixed_back_kernel,
        [weight, *pieces],
        [pl.BlockSpec((width, columns), whole)] + [pl.BlockSpec((rows, width), whole)] * len(pieces),
        [pl.BlockSpec((total, columns), whole)],
        [jax.ShapeDtypeStruct((total, columns), jnp.bfloat16)],
        (1,),
        2 * total * width * columns,
        6 * MIB,
        "mixed_back",
    )[0]


def place_kernel(core_ref, *refs):
    for i, ref in enumerate(refs[:-1]):

        @pl.when(pl.program_id(0) == i)
        def _(ref=ref):
            refs[-1][...] = ref[...]


def place(order, core, pieces):
    rows, width = pieces[0].shape
    count = len(pieces)
    return order(
        place_kernel,
        list(pieces),
        [pl.BlockSpec((rows, width), lambda i, core_ref: (0, 0))] * count,
        [pl.BlockSpec((rows, width), lambda i, core_ref: (lax.rem(i + core_ref[0] * (count // 2), count), 0))],
        [jax.ShapeDtypeStruct((rows * count, width), pieces[0].dtype)],
        (count,),
        0,
        8 * rows * width,
        "place",
        scalars=(core,),
    )[0]


def anchors(count):
    return [pl.BlockSpec(memory_space=pl.ANY)] * count


MARK = jax.ShapeDtypeStruct((8, HD), jnp.float32)


def mark_spec():
    return pl.BlockSpec((8, HD), lambda *refs: (0, 0))


def grad_hidden_kernel(g_ref, w_ref, out_ref):
    out_ref[...] = to_bf(dot(g_ref[...], w_ref[...], 1, 1))


def grad_hidden_of(order, grad, weight):
    total, width = grad.shape
    hidden = weight.shape[0]
    return order(
        grad_hidden_kernel,
        [grad, weight],
        [pl.BlockSpec((total, width), lambda i: (0, 0)), pl.BlockSpec((TILE, width), lambda i: (i, 0))],
        [pl.BlockSpec((total, TILE), lambda i: (0, i))],
        [jax.ShapeDtypeStruct((total, hidden), jnp.bfloat16)],
        (pl.cdiv(hidden, TILE),),
        2 * total * width * hidden,
        15 * MIB,
        "grad_hidden",
    )[0]


def gated_kernel(gh_ref, gw_ref, uw_ref, *refs):
    hid_ref, gg_ref, gu_ref = refs[-3:]
    rows = refs[0].shape[0]
    for part, ref in enumerate(refs[:-3]):
        here = slice(part * rows, (part + 1) * rows)
        h = ref[...]
        gate = dot(h, gw_ref[...], 1, 1)
        up = dot(h, uw_ref[...], 1, 1)
        grad = to_f(gh_ref[here])
        sigma = 1.0 / (1.0 + jnp.exp(-gate))
        swish = gate * sigma
        hid_ref[here] = to_bf(swish * up)
        gu_ref[here] = to_bf(grad * swish)
        gg_ref[here] = to_bf(grad * up * sigma * (1.0 + gate * (1.0 - sigma)))


def gated(order, pieces, grad_hidden, gate_weight, up_weight):
    rows, width = pieces[0].shape
    total = rows * len(pieces)
    hidden = gate_weight.shape[0]
    column = pl.BlockSpec((total, TILE), lambda i: (0, i))
    weight = pl.BlockSpec((TILE, width), lambda i: (i, 0))
    shape = jax.ShapeDtypeStruct((total, hidden), jnp.bfloat16)
    return order(
        gated_kernel,
        [grad_hidden, gate_weight, up_weight, *pieces],
        [column, weight, weight] + [pl.BlockSpec((rows, width), lambda i: (0, 0))] * len(pieces),
        [column] * 3,
        [shape] * 3,
        (pl.cdiv(hidden, TILE),),
        4 * total * width * hidden,
        30 * MIB,
        "gated",
    )


def share_kernel(plan, lefts, rights, extra, halves, groups, pick_ref, blocks_ref, *refs):
    step = pl.program_id(0)
    left_refs, right_refs = refs[:lefts], refs[lefts : lefts + rights]
    refs = refs[lefts + rights :]
    if extra:
        extra_ref, refs = refs[0], refs[1:]
    for left, right, begin, end, shift, columns, target in plan:

        @pl.when((step >= begin) & (step < end))
        def _(left=left, right=right, shift=shift, columns=columns, target=target):
            out = dot(left_refs[left][...], right_refs[right][...])
            if extra:
                out = out + to_f(extra_ref[...])
            tile = out.shape[1]
            spot = (step + shift) * tile + lax.broadcasted_iota(jnp.int32, (1, tile), 1)
            out = to_bf(jnp.where(spot < columns, out, 0.0))
            if groups:
                share = out.shape[0] // (groups[0] * groups[1])
                for i in range(groups[0]):
                    for j in range(groups[1]):
                        here = (j * groups[0] + i) * share
                        there = (i * groups[1] + j) * share
                        refs[target][here : here + share] = out[there : there + share]
                return
            if not halves:
                refs[target][...] = out
                return
            send_ref, keep_ref, rows = refs
            rows[...] = out
            share = send_ref.shape[0] // (2 * halves)
            for i in range(2 * halves):
                here = slice(i * share, (i + 1) * share)
                send_ref[here] = rows[pl.ds(pl.multiple_of(blocks_ref[i] * share, share), share)]
                keep_ref[here] = rows[pl.ds(pl.multiple_of(blocks_ref[2 * halves + i] * share, share), share)]


def clipped(rows, tile, begin, count, shift=0):
    return pl.BlockSpec((rows, tile), lambda i, *refs: (0, jnp.clip(i - begin, 0, count - 1) + shift))


def share_of(order, lefts, rights, parts, part, pick, tile, extra=None, blocks=None, groups=None):
    tokens = lefts[0].shape[1]
    plan, at = [], 0
    starts, sizes, right_at = {}, {}, {}
    for left, right, skip, count, target in parts:
        plan.append((left, right, at, at + count, skip - at, rights[right].shape[1], target))
        starts.setdefault(target, at)
        sizes[target] = sizes.get(target, 0) + count
        first, tiles, low = right_at.get(right, (at, 0, skip))
        right_at[right] = (first, tiles + count, low)
        at += count
    halves = 0
    extras = [] if extra is None else [extra]
    scratch = []
    if blocks is None:
        blocks = jnp.zeros((1,), jnp.int32)
        outs = [clipped(part, tile, starts[t], sizes[t]) for t in sorted(sizes)]
        shapes = [jax.ShapeDtypeStruct((part, sizes[t] * tile), jnp.bfloat16) for t in sorted(sizes)]
    else:
        halves = blocks.shape[0] // 4
        outs = [clipped(part // 2, tile, 0, at)] * 2
        shapes = [jax.ShapeDtypeStruct((part // 2, at * tile), jnp.bfloat16)] * 2
        scratch = [pltpu.VMEM((part, tile), jnp.bfloat16)]
    return order(
        functools.partial(share_kernel, plan, len(lefts), len(rights), len(extras), halves, groups),
        [*lefts, *rights, *extras],
        [pl.BlockSpec((part, tokens), lambda i, pick_ref, blocks_ref: (pick_ref[0], 0))] * len(lefts)
        + [clipped(tokens, tile, *right_at[r]) for r in range(len(rights))]
        + [clipped(part, tile, 0, at)] * len(extras),
        outs,
        shapes,
        (at,),
        2 * part * tokens * at * tile,
        2 * (part * tokens + (part + tokens) * at * tile),
        "share",
        scalars=(jnp.asarray(pick, jnp.int32).reshape(1), blocks),
        scratch=scratch,
    )


def relay_kernel(keep_ref, come_ref, out_ref):
    out_ref[...] = to_bf(to_f(keep_ref[...]) + to_f(come_ref[...]))


def relay(order, keep, come, share):
    rows, columns = keep.shape
    pair = pl.BlockSpec((share, columns), lambda i: (2 * i + 1, 0))
    return order(
        relay_kernel,
        [keep, come],
        [pair, pair],
        [pl.BlockSpec((share, columns), lambda i: (i, 0))],
        [jax.ShapeDtypeStruct((rows // 2, columns), jnp.bfloat16)],
        (rows // (2 * share),),
        0,
        3 * rows * columns,
        "relay",
    )[0]


def finish_kernel(plan, columns, gains, *refs):
    out_ref = refs[-2] if gains else refs[-1]
    step = pl.program_id(0)
    tile = out_ref.shape[1]
    for begin, end, first, count in plan:

        @pl.when((step >= begin) & (step < end))
        def _(first=first, count=count):
            out = to_f(refs[first][...])
            for ref in refs[first + 1 : first + count]:
                out = out + to_f(ref[...])
            out_ref[...] = out
            if gains:
                spot = step * tile + lax.broadcasted_iota(jnp.int32, (1, tile), 1)
                terms = jnp.where(spot < columns, out * to_f(refs[-3][...]), 0.0)
                total = terms[:, :HD]
                for i in range(HD, tile, HD):
                    total = total + terms[:, i : i + HD]

                @pl.when(step == 0)
                def _():
                    refs[-1][...] = total

                @pl.when(step > 0)
                def _():
                    refs[-1][...] += total


def finish(order, chunks, share, columns, tile, weight=None):
    plan, specs, args, at = [], [], [], 0
    for chunk in chunks:
        count = chunk[0].shape[1] // tile
        plan.append((at, at + count, len(args), len(chunk)))
        specs += [clipped(share, tile, at, count)] * len(chunk)
        args += chunk
        at += count
    column = pl.BlockSpec((share, tile), lambda i: (0, i))
    outs, shapes = [column], [jax.ShapeDtypeStruct((share, columns), jnp.float32)]
    if weight is not None:
        args.append(weight)
        specs.append(column)
        outs.append(pl.BlockSpec((share, HD), lambda i: (0, 0)))
        shapes.append(jax.ShapeDtypeStruct((share, HD), jnp.float32))
    return order(
        functools.partial(finish_kernel, plan, columns, weight is not None),
        args,
        specs,
        outs,
        shapes,
        (at,),
        0,
        14 * share * columns,
        "finish",
    )


def narrow_kernel(pairs, extras, right_dim, *refs):
    out = dot(refs[0][...], refs[1][...], 1, right_dim)
    for i in range(1, pairs):
        out = out + dot(refs[2 * i][...], refs[2 * i + 1][...], 1, right_dim)
    extra = refs[2 * pairs : 2 * pairs + extras]
    outs = refs[2 * pairs + extras :]
    if extras:
        out = out + jnp.concatenate([to_f(ref[...]) for ref in extra], axis=0)
    rows = outs[0].shape[0]
    for i, ref in enumerate(outs):
        ref[...] = to_bf(out[i * rows : (i + 1) * rows])


def narrow(order, pairs, index, extra=(), right_dim=0):
    total, hidden = pairs[0][0].shape
    width = pairs[0][1].shape[1 - right_dim]
    half = total // 2
    piece = half // PIECES
    column = pl.BlockSpec((piece, TILE), lambda i: (0, i))
    right = (
        pl.BlockSpec((TILE, hidden), lambda i: (i, 0))
        if right_dim
        else pl.BlockSpec((hidden, TILE), lambda i: (0, i))
    )
    return order(
        functools.partial(narrow_kernel, len(pairs), len(extra), right_dim),
        [item for pair in pairs for item in pair] + list(extra),
        [pl.BlockSpec((half, hidden), lambda i: (index, 0)), right] * len(pairs) + [column] * len(extra),
        [column] * PIECES,
        [jax.ShapeDtypeStruct((piece, width), jnp.bfloat16)] * PIECES,
        (width // TILE,),
        2 * len(pairs) * half * width * hidden,
        2 * len(pairs) * (half + width) * hidden + 2 * half * width,
        "narrow",
    )


def piece_specs(piece, width, block):
    steps = piece // block
    return [
        pl.BlockSpec((block, width), lambda i, *refs, j=j: (jnp.clip(i - j * steps, 0, steps - 1), 0))
        for j in range(PIECES)
    ]


def pick_piece(refs):
    value = refs[0][...]
    for j, ref in enumerate(refs[1:], 1):
        value = jnp.where(pl.program_id(0) >= 4 * j // len(refs), ref[...], value)
    return value


def put_piece(refs, value):
    steps = 4 // len(refs)
    for j, ref in enumerate(refs):

        @pl.when(lax.div(pl.program_id(0), steps) == j)
        def _(ref=ref):
            ref[...] = value


def turn_kernel(*refs):
    rows = refs[0].shape[0]
    for i, ref in enumerate(refs[:-1]):
        refs[-1][:, i * rows : (i + 1) * rows] = ref[...].T


def turn(order, pieces):
    rows, width = pieces[0].shape
    total = rows * len(pieces)
    return order(
        turn_kernel,
        list(pieces),
        [pl.BlockSpec((rows, TILE), lambda i: (0, i))] * len(pieces),
        [pl.BlockSpec((TILE, total), lambda i: (i, 0))],
        [jax.ShapeDtypeStruct((width, total), jnp.bfloat16)],
        (width // TILE,),
        0,
        4 * total * width,
        "turn",
    )[0]


def grad_out_kernel(core_ref, cot_ref, valid_ref, out_ref, turned_ref):
    out = to_bf(to_f(cot_ref[...]) * valid_ref[...])
    out_ref[...] = out
    turned_ref[...] = out.T


def grad_out_of(order, core, cotangent, valid):
    total, width = cotangent.shape
    block = total // 4
    return order(
        grad_out_kernel,
        [cotangent, valid],
        [
            pl.BlockSpec((block, width), lambda i, core_ref: (lax.rem(i + core_ref[0] * 2, 4), 0)),
            pl.BlockSpec((block, 1), lambda i, core_ref: (i, 0)),
        ],
        [
            pl.BlockSpec((block, width), lambda i, core_ref: (i, 0)),
            pl.BlockSpec((width, block), lambda i, core_ref: (0, i)),
        ],
        [
            jax.ShapeDtypeStruct((total, width), jnp.bfloat16),
            jax.ShapeDtypeStruct((width, total), jnp.bfloat16),
        ],
        (4,),
        0,
        6 * total * width,
        "grad_out",
        scalars=(core,),
    )


def middle_kernel(core_ref, tok_ref, gain_ref, *refs):
    mine, come = pick_piece(refs[:PIECES]), pick_piece(refs[PIECES : 2 * PIECES])
    mid_ref, *h_refs = refs[2 * PIECES :]
    middle = to_f(tok_ref[...]) + (to_f(mine) + to_f(come))
    factor = lax.rsqrt(jnp.mean(middle * middle, axis=-1, keepdims=True) + EPS)
    mid_ref[...] = middle
    put_piece(h_refs, to_bf(middle * factor * gain_ref[...]))


def middle_of(order, core, tokens, mine, come, gain):
    piece, width = mine[0].shape
    half = piece * PIECES
    block = half // 4
    specs = piece_specs(piece, width, block)
    middle, *h = order(
        middle_kernel,
        [tokens, gain, *mine, *come],
        [
            pl.BlockSpec((block, width), lambda i, core_ref: (core_ref[0] * 4 + i, 0)),
            pl.BlockSpec((1, width), lambda i, core_ref: (0, 0)),
        ]
        + specs * 2,
        [pl.BlockSpec((block, width), lambda i, core_ref: (i, 0))] + specs,
        [jax.ShapeDtypeStruct((half, width), jnp.float32)]
        + [jax.ShapeDtypeStruct((piece, width), jnp.bfloat16)] * PIECES,
        (4,),
        0,
        9 * MIB,
        "middle",
        scalars=(core,),
    )
    return middle, h


def norm_back_kernel(core_ref, x_ref, gain_ref, up_ref, *refs):
    mine, come = pick_piece(refs[:PIECES]), pick_piece(refs[PIECES : 2 * PIECES])
    outs = refs[2 * PIECES :]
    grad = to_f(mine) + to_f(come)
    x = to_f(x_ref[...])
    factor = lax.rsqrt(jnp.mean(x * x, axis=-1, keepdims=True) + EPS)
    normed = x * factor
    weighted = grad * gain_ref[...]
    inner = jnp.mean(weighted * normed, axis=-1, keepdims=True)
    out = to_f(up_ref[...]) + factor * (weighted - normed * inner)
    if len(outs) > PIECES:
        outs[0][...] = out
        put_piece(outs[1:], to_bf(out))
    else:
        put_piece(outs, out)


def norm_back(order, core, mine, come, x, gain, up, by_core):
    piece, width = mine[0].shape
    half = piece * PIECES
    block = half // 4
    at = pl.BlockSpec((block, width), lambda i, core_ref: (i, 0))
    picked = pl.BlockSpec((block, width), lambda i, core_ref: (core_ref[0] * 4 + i, 0))
    specs = piece_specs(piece, width, block)
    if by_core:
        shapes = [jax.ShapeDtypeStruct((piece, width), jnp.float32)] * PIECES
    else:
        shapes = [jax.ShapeDtypeStruct((half, width), jnp.float32)]
        shapes += [jax.ShapeDtypeStruct((piece, width), jnp.bfloat16)] * PIECES
    return order(
        norm_back_kernel,
        [x, gain, up, *mine, *come],
        [picked if by_core else at, pl.BlockSpec((1, width), lambda i, core_ref: (0, 0)), at] + specs * 2,
        specs if by_core else [at] + specs,
        shapes,
        (4,),
        0,
        10 * MIB,
        "norm_back",
        scalars=(core,),
    )


def layer_kernel(middle_ref, *refs):
    mine, come = pick_piece(refs[:PIECES]), pick_piece(refs[PIECES : 2 * PIECES])
    put_piece(refs[2 * PIECES :], to_bf(middle_ref[...] + (to_f(mine) + to_f(come))))


def layer_of(order, middle, mine, come):
    piece, width = mine[0].shape
    block = piece * PIECES // 4
    specs = piece_specs(piece, width, block)
    return order(
        layer_kernel,
        [middle, *mine, *come],
        [pl.BlockSpec((block, width), lambda i: (i, 0))] + specs * 2,
        specs,
        [jax.ShapeDtypeStruct((piece, width), jnp.bfloat16)] * PIECES,
        (4,),
        0,
        5 * MIB,
        "layer",
    )


def tensor_gather(value, rank):
    mate = core_swap(value)
    pair = jnp.where(lax.rem(rank, 2) == 0, jnp.stack([value, mate]), jnp.stack([mate, value]))
    come = chip_swap(pair)
    return jnp.where(
        lax.div(rank, 2) == 0,
        jnp.concatenate([pair, come], axis=0),
        jnp.concatenate([come, pair], axis=0),
    )


def body(
    tokens,
    lengths,
    cotangent,
    q_weight,
    q_bias,
    k_weight,
    k_bias,
    v_weight,
    v_bias,
    o_weight,
    attn_gain,
    ffn_gain,
    gate_weight,
    up_weight,
    down_weight,
):
    rows, local, width = tokens.shape
    total = rows * local
    half = total // 2
    heads = q_weight.shape[1] // HD
    ranks = lax.axis_size("tensor")
    seqs = lax.axis_size("seq")
    rank = lax.axis_index("tensor")
    dp_index = lax.axis_index("dp")
    seq_index = lax.axis_index("seq")
    core = lax.rem(rank, 2)
    head = lax.div(rank, 2)
    core_one = core.reshape(1)
    hops = min(seqs - 1, -(-(MOST - 1) // local))
    reach = hops * local

    def own_first(value):
        turned = jnp.concatenate([value[rows // 2 :], value[: rows // 2]], axis=0)
        return jnp.where(core == 0, value, turned)

    slots = jnp.arange(lengths.shape[1], dtype=jnp.int32)
    lens = own_first(lengths)
    ends = jnp.sum(jnp.where(slots[None, :] <= slots[:, None], lens[:, None, :], 0), axis=2)
    spot = seq_index * local + jnp.arange(local, dtype=jnp.int32)
    begun = jnp.max(
        jnp.where(ends[:, None, :] <= spot[None, :, None], ends[:, None, :], 0), axis=2
    )
    valid = to_f(spot[None, :] < ends[:, -2:-1])
    position = (spot[None, :] - begun).reshape(total, 1)
    freqs = ROPE_BASE ** (-(jnp.arange(HD // 2, dtype=jnp.float32) * 2.0) / HD)
    angles = to_f(position) * freqs[None, :]
    cosine, sine = jnp.cos(angles), jnp.sin(angles)
    cosine = jnp.concatenate([cosine, cosine], axis=1)
    sine = jnp.concatenate([-sine, sine], axis=1)
    start = begun - (seq_index * local - reach)
    low = jnp.maximum(lax.div(jnp.maximum(start[:, ::Q_BLOCK], 0), K_BLOCK), 0)
    start = start.reshape(rows, 1, local)

    key_side = core == 0
    kv_weight = jnp.where(
        key_side,
        lax.dynamic_slice_in_dim(k_weight, head * HD, HD, 1),
        lax.dynamic_slice_in_dim(v_weight, head * HD, HD, 1),
    )
    kv_bias = jnp.where(
        key_side,
        lax.dynamic_slice_in_dim(k_bias, head * HD, HD, 0),
        lax.dynamic_slice_in_dim(v_bias, head * HD, HD, 0),
    )
    weight = jnp.concatenate([q_weight, kv_weight], axis=1)
    bias = to_f(jnp.concatenate([q_bias, kv_bias])).reshape(1, -1)
    gain_one = to_f(attn_gain).reshape(1, width)
    gain_two = to_f(ffn_gain).reshape(1, width)

    h_one, q_rot, kv = first(
        core_one, tokens.reshape(total, width), gain_one, weight, bias, cosine, sine
    )
    kv = kv.reshape(rows, local, HD)
    span = [shifted(kv, h) for h in range(hops, 0, -1)] + [kv]
    mate = [core_swap(piece) for piece in span]
    q_rows = q_rot.reshape(rows, local, heads * HD)
    mixed_rows, lse = attend(low, core_one, q_rows, start, span, mate)
    mixed = mixed_rows.reshape(total, heads * HD)

    order = Order()
    flat_tokens = tokens.reshape(total, width)
    dps = lax.axis_size("dp")
    near_pair = dps == 2 and seqs == 4
    part = width // dps
    share = part // seqs
    gate_t, up_t, down_t = gate_weight.T, up_weight.T, down_weight.T
    units = gate_t.shape[0]
    tiles = -(-units // TILE)
    cut = (tiles + 1) // 2
    long = -(-2 * tiles // 3)
    one, two = seq_index ^ 1, seq_index ^ 2
    three = seq_index ^ 3
    quad = jnp.stack([one, three, seq_index, two])

    begin = (dp_index * seqs + seq_index) * share

    def rows_of(value):
        return lax.dynamic_slice_in_dim(value, begin, share, 0)

    class Rows:
        def __init__(self, lefts, rights, parts, tile=TILE, sent=None):
            self.args = (order, lefts, rights, parts)
            self.tile = tile
            if not near_pair:
                (whole,) = share_of(*self.args, width, 0, tile)
                self.whole = lax.psum_scatter(whole, ("dp", "seq"), scatter_dimension=0, tiled=True)
                return
            if sent is None:
                (sent,) = share_of(*self.args, part, 1 - dp_index, tile)
            self.come = lax.ppermute(sent, "dp", flipped("dp", 0))

        def own(self):
            if near_pair:
                send, self.keep = share_of(*self.args, part, dp_index, self.tile, self.come, quad)
                self.come = lax.ppermute(send, "seq", flipped("seq", 0))

        def relay(self):
            if near_pair:
                sent = relay(order, self.keep, self.come, share)
                self.last = lax.ppermute(sent, "seq", flipped("seq", 1))

        def settled(self):
            if near_pair:
                order.arrived(self.last)

        def result(self):
            return [self.keep, self.come, self.last] if near_pair else [self.whole]

    class SeqFirst(Rows):
        def __init__(self, lefts, rights, parts, tile=TILE):
            if not near_pair:
                super().__init__(lefts, rights, parts, tile)
                return
            (whole,) = share_of(order, lefts, rights, parts, width, 0, tile, None, None, (dps, seqs))
            self.mine = lax.psum_scatter(whole, "seq", scatter_dimension=0, tiled=True)

        def across(self):
            if near_pair:
                sent = lax.dynamic_slice_in_dim(self.mine, (1 - dp_index) * share, share, 0)
                self.mine = lax.dynamic_slice_in_dim(self.mine, dp_index * share, share, 0)
                order.arrived(sent, self.mine)
                self.come = lax.ppermute(sent, "dp", flipped("dp", 0))

        def settled(self):
            if near_pair:
                order.arrived(self.come)

        def result(self):
            return [self.mine, self.come] if near_pair else [self.whole]

    class Scattered(Rows):
        def own(self):
            if near_pair:
                (mine,) = share_of(*self.args, part, dp_index, self.tile, self.come)
                self.whole = lax.psum_scatter(mine, "seq", scatter_dimension=0, tiled=True)

        def settled(self):
            order.arrived(self.whole)

        def result(self):
            return [self.whole]

    sent = core_swaps(narrow(order, [(mixed, o_weight)], 1, (), 1))
    mine = narrow(order, [(mixed, o_weight)], 0, sent, 1)
    come = chip_swaps(mine)
    grad_ffn, grad_ffn_t = grad_out_of(
        order, core_one, cotangent.reshape(total, width), valid.reshape(total, 1)
    )
    gate_rows, up_rows = rows_of(gate_weight), rows_of(up_weight)
    order.arrived(gate_rows, up_rows)
    grad_hidden = grad_hidden_of(order, grad_ffn, down_t)
    h_one_t = turn(order, [h_one])
    middle, h_two = middle_of(order, core_one, flat_tokens, mine, come, gain_two)
    h_two += core_swaps(h_two)
    hidden, grad_gate, grad_up = gated(order, h_two, grad_hidden, gate_t, up_t)

    down_b = SeqFirst([grad_ffn_t], [hidden], [(0, 0, cut, tiles - cut, 0)])
    down_a = Rows([grad_ffn_t], [hidden], [(0, 0, 0, cut, 0)])
    pairs = [(grad_gate, gate_t), (grad_up, up_t)]
    sent = core_swaps(narrow(order, pairs, 1))
    mine = narrow(order, pairs, 0, sent)
    come = chip_swaps(mine)
    h_two_t = turn(order, h_two)
    if near_pair:
        sends = share_of(
            order,
            [h_two_t],
            [grad_gate, grad_up],
            [(0, 0, 0, tiles, 0), (0, 1, 0, long, 1), (0, 1, long, tiles - long, 2)],
            part,
            1 - dp_index,
            TILE,
        )
    else:
        sends = [None] * 3

    def half_rows(kind, right, begin, end, sent):
        return kind([h_two_t], [right], [(0, 0, begin, end - begin, 0)], TILE, sent)

    gate = half_rows(Scattered, grad_gate, 0, tiles, sends[0])
    up_a = half_rows(Rows, grad_up, 0, long, sends[1])
    up_b = half_rows(Rows, grad_up, long, tiles, sends[2])
    down_a.own()
    grad_middle, *branch = norm_back(order, core_one, mine, come, middle, gain_two, grad_ffn, False)
    branch += core_swaps(branch)
    grad_mixed = mixed_back(order, branch, o_weight).reshape(rows, local, heads * HD)
    grad_q_rows, keep, sent = attend_back(
        order, low, core_one, q_rows, start, span, mate, grad_mixed, mixed_rows, lse, cosine, sine
    )
    both_come = core_swap(sent)
    branch_t = turn(order, branch)
    down_a.relay()
    own_kv, *pieces = fold(order, keep, both_come, local)
    moving = shifted(pieces[-1], -1) if pieces else None
    ffn_sent = core_swaps(narrow(order, [(hidden, down_t)], 1))
    for piece in pieces[-2::-1]:
        moving = shifted(carry(order, piece, moving), -1)
    grad_qkv, bias_sum = join(
        order, core_one, grad_q_rows, own_kv, [] if moving is None else [moving], cosine, sine
    )
    sent = core_swaps(narrow(order, [(grad_qkv, weight)], 1, (), 1))
    down_b.across()
    mine = narrow(order, [(grad_qkv, weight)], 0, sent, 1)
    come = chip_swaps(mine)
    gate.own()
    last_parts = [(0, 0, 0, grad_qkv.shape[1] // HD, 0), (1, 1, 0, heads, 0)]
    last = Rows([h_one_t, branch_t], [grad_qkv, mixed], last_parts, HD)
    ffn_mine = narrow(order, [(hidden, down_t)], 0, ffn_sent)
    token = norm_back(order, core_one, mine, come, flat_tokens, gain_one, grad_middle, True)
    token += core_swaps(token)
    ffn_come = chip_swaps(ffn_mine)
    up_a.own()
    token_grad = place(order, core_one, token).reshape(rows, local, width)
    layer = layer_of(order, middle, ffn_mine, ffn_come)
    layer += core_swaps(layer)
    last.own()
    layer_out = place(order, core_one, layer).reshape(rows, local, width)
    up_a.relay()
    down_a.settled()
    up_b.own()
    down_b.settled()
    up_a.settled()
    last.relay()
    (down_grad,) = finish(order, [down_a.result(), down_b.result()], share, units, TILE)
    if near_pair:
        bias_come = lax.ppermute(bias_sum, "dp", flipped("dp", 0))
        bias_all = bias_add(order, bias_sum, bias_come)
        bias_come = lax.ppermute(bias_all, "seq", flipped("seq", 0))
    up_b.relay()
    gate_grad, gate_term = finish(order, [gate.result()], share, units, TILE, gate_rows)
    wide_columns = grad_qkv.shape[1]
    (last_grad,) = finish(order, [last.result()], share, wide_columns + heads * HD, HD)
    if near_pair:
        bias_all = bias_add(order, bias_all, bias_come)
        bias_come = lax.ppermute(bias_all, "seq", flipped("seq", 1))
        bias_all = (bias_all + bias_come)[:1]
    else:
        bias_all = lax.psum(bias_sum[:1], ("dp", "seq"))
    up_grad, up_term = finish(order, [up_a.result(), up_b.result()], share, units, TILE, up_rows)
    qkv_grad, o_grad = last_grad[:, :wide_columns], last_grad[:, wide_columns:]

    attn_term = jnp.sum(to_f(rows_of(weight)) * qkv_grad, axis=1)
    ffn_term = jnp.sum(gate_term + up_term, axis=1)
    columns = heads * HD
    room = -(-share // HD) * HD - share
    terms = jnp.pad(jnp.stack([ffn_term, attn_term]), ((0, 0), (0, room))).reshape(-1, HD)
    packed = jnp.concatenate([qkv_grad[:, columns:], bias_all.reshape(-1, HD), terms], axis=0)
    gathered = tensor_gather(packed, rank)
    term_rows = terms.shape[0]
    bias_count = bias_all.shape[1] // HD
    terms = gathered[:, share + bias_count :].reshape(ranks, 2, -1)[:, :, :share]
    ffn_gain_grad, attn_gain_grad = terms[0] + terms[1] + (terms[2] + terms[3])
    attn_gain_grad = attn_gain_grad / lax.dynamic_slice_in_dim(gain_one[0], begin, share, 0)
    ffn_gain_grad = ffn_gain_grad / lax.dynamic_slice_in_dim(gain_two[0], begin, share, 0)
    q_grad = qkv_grad[:, :columns]
    kv_parts = lax.dynamic_slice_in_dim(gathered, rank * (share // ranks), share // ranks, 1)
    k_grad = jnp.concatenate([kv_parts[2 * i] for i in range(KVH)], axis=1)
    v_grad = jnp.concatenate([kv_parts[2 * i + 1] for i in range(KVH)], axis=1)
    biases = gathered[:, share : share + bias_count]
    q_bias_grad = biases[:, :heads].reshape(-1)
    k_bias_grad = biases[0::2, heads].reshape(-1)
    v_bias_grad = biases[1::2, heads].reshape(-1)
    return (
        layer_out,
        token_grad,
        q_grad,
        q_bias_grad,
        k_grad,
        k_bias_grad,
        v_grad,
        v_bias_grad,
        o_grad,
        attn_gain_grad,
        ffn_gain_grad,
        gate_grad,
        up_grad,
        down_grad,
    )


def solution(mesh):
    in_specs = (
        P("dp", "seq", None),
        P("dp", None),
        P("dp", "seq", None),
        P(None, "tensor"),
        P("tensor"),
        P(),
        P(),
        P(),
        P(),
        P(None, "tensor"),
        P(),
        P(),
        P(None, "tensor"),
        P(None, "tensor"),
        P(None, "tensor"),
    )
    out_specs = (
        P("dp", "seq", None),
        P("dp", "seq", None),
        P(("dp", "seq"), "tensor"),
        P(),
        P(("dp", "seq", "tensor"), None),
        P(),
        P(("dp", "seq", "tensor"), None),
        P(),
        P(("dp", "seq"), "tensor"),
        P(("dp", "seq")),
        P(("dp", "seq")),
        P(("dp", "seq"), "tensor"),
        P(("dp", "seq"), "tensor"),
        P(("dp", "seq"), "tensor"),
    )
    return jax.shard_map(body, mesh=mesh, in_specs=in_specs, out_specs=out_specs, check_vma=False)
```

```python
import functools
import math

import jax
import jax.numpy as jnp
from jax import lax
from jax.experimental import pallas as pl
from jax.experimental.pallas import tpu as pltpu
from jax.sharding import PartitionSpec as P

KVH = 2
HD = 128
MOST = 1024
EPS = 1e-06
ROPE_BASE = 10000.0
NEG_FILL = -1e30
Q_BLOCK = 256
K_BLOCK = 256
MIB = 1 << 20
LIGHT = 1000
TILE = 256
PIECES = 2
SCALE = 1.0 / math.sqrt(HD)


def to_bf(value):
    return value.astype(jnp.bfloat16)


def to_f(value):
    return value.astype(jnp.float32)


def dot(left, right, left_dim=1, right_dim=0):
    return lax.dot_general(
        left,
        right,
        (((left_dim,), (right_dim,)), ((), ())),
        preferred_element_type=jnp.float32,
    )


def flipped(axis, bit):
    return [(i, i ^ (1 << bit)) for i in range(lax.axis_size(axis))]


def core_swap(value):
    return lax.ppermute(value, "tensor", flipped("tensor", 0))


def chip_swap(value):
    return lax.ppermute(value, "tensor", flipped("tensor", 1))


def core_swaps(values):
    return [core_swap(value) for value in values]


def chip_swaps(values):
    return [chip_swap(value) for value in values]


def shifted(value, hops):
    count = lax.axis_size("seq")
    route = [(i, i + hops) for i in range(count) if 0 <= i + hops < count]
    return lax.ppermute(value, "seq", route)


def cost(flops, read):
    return pl.CostEstimate(flops=flops // LIGHT, bytes_accessed=read // LIGHT, transcendentals=0)


class Order:
    def __init__(self):
        self.mark = None
        self.touched = []

    def arrived(self, *values):
        self.touched.extend(values)

    def __call__(self, kernel, args, in_specs, out_specs, out_shape, grid, flops, read, name, scalars=(), scratch=()):
        anchor = ([] if self.mark is None else [self.mark]) + self.touched
        self.touched = []
        count = len(scalars) + len(args)
        outs = len(out_shape)

        def run(*refs):
            rest = refs[count + len(anchor) :]
            kernel(*refs[:count], *rest[:outs], *rest[outs + 1 :])
            rest[outs][...] = jnp.zeros(rest[outs].shape, jnp.float32)

        *results, self.mark = pl.pallas_call(
            run,
            grid_spec=pltpu.PrefetchScalarGridSpec(
                num_scalar_prefetch=len(scalars),
                grid=grid,
                in_specs=list(in_specs) + anchors(len(anchor)),
                out_specs=list(out_specs) + [mark_spec()],
                scratch_shapes=list(scratch),
            ),
            out_shape=list(out_shape) + [MARK],
            compiler_params=pltpu.CompilerParams(vmem_limit_bytes=32 * MIB),
            cost_estimate=cost(flops, read),
            name=name,
        )(*scalars, *args, *anchor)
        return results


def first_kernel(core_ref, tok_ref, gain_ref, w_ref, b_ref, cos_ref, sin_ref, h_ref, q_ref, kv_ref):
    x = to_f(tok_ref[...])
    factor = lax.rsqrt(jnp.mean(x * x, axis=-1, keepdims=True) + EPS)
    h = to_bf(x * factor * gain_ref[...])
    h_ref[...] = h
    lin = dot(h, w_ref[...]) + b_ref[...]
    cosine = cos_ref[...]
    sine = sin_ref[...]
    heads = q_ref.shape[1] // HD
    for head in range(heads):
        part = lin[:, head * HD : (head + 1) * HD]
        q_ref[:, head * HD : (head + 1) * HD] = to_bf(
            part * cosine + pltpu.roll(part, HD // 2, 1) * sine
        )
    part = lin[:, heads * HD :]
    is_key = core_ref[0] == 0
    kv_ref[...] = to_bf(
        part * jnp.where(is_key, cosine, 1.0)
        + pltpu.roll(part, HD // 2, 1) * jnp.where(is_key, sine, 0.0)
    )


def first(core, tokens, gain, weight, bias, cosine, sine):
    total, width = tokens.shape
    columns = weight.shape[1]
    block = total // 4
    half = 2

    def flip(i, core_ref):
        return (lax.rem(i + core_ref[0] * half, 4), 0)

    def at(i, core_ref):
        return (i, 0)

    def whole(i, core_ref):
        return (0, 0)

    return pl.pallas_call(
        first_kernel,
        grid_spec=pltpu.PrefetchScalarGridSpec(
            num_scalar_prefetch=1,
            grid=(4,),
            in_specs=[
                pl.BlockSpec((block, width), flip),
                pl.BlockSpec((1, width), whole),
                pl.BlockSpec((width, columns), whole),
                pl.BlockSpec((1, columns), whole),
                pl.BlockSpec((block, HD), at),
                pl.BlockSpec((block, HD), at),
            ],
            out_specs=[
                pl.BlockSpec((block, width), at),
                pl.BlockSpec((block, columns - HD), at),
                pl.BlockSpec((block, HD), at),
            ],
        ),
        out_shape=[
            jax.ShapeDtypeStruct((total, width), jnp.bfloat16),
            jax.ShapeDtypeStruct((total, columns - HD), jnp.bfloat16),
            jax.ShapeDtypeStruct((total, HD), jnp.bfloat16),
        ],
        compiler_params=pltpu.CompilerParams(vmem_limit_bytes=32 * MIB),
        cost_estimate=cost(2 * total * width * columns, 9 * MIB),
        name="first",
    )(core, tokens, gain, weight, bias, cosine, sine)


def stacked(ref, start, count, heads):
    return jnp.concatenate(
        [ref[0, pl.ds(start, count), h * HD : (h + 1) * HD] for h in range(heads)], axis=0
    )


def bounds(start_ref, index, heads, reach):
    first_key = jnp.concatenate(
        [start_ref[0, :, pl.ds(index * Q_BLOCK, Q_BLOCK)]] * heads, axis=1
    )
    place = reach + index * Q_BLOCK + lax.broadcasted_iota(jnp.int32, (1, Q_BLOCK), 1)
    return first_key, jnp.concatenate([place] * heads, axis=1)


def gather_span(core, refs, span):
    count = len(refs) // 2
    local = refs[0].shape[1]
    for i in range(count):
        here = slice(i * local, (i + 1) * local)
        span[core, here] = refs[i][0]
        span[1 - core, here] = refs[count + i][0]


def attend_kernel(heads, blocks, pieces, low_ref, core_ref, q_ref, start_ref, *refs):
    o_ref, lse_ref, acc, span = refs[2 * pieces :]
    row = pl.program_id(0)
    wide = heads * Q_BLOCK
    reach = (pieces - 1) * q_ref.shape[1]
    gather_span(core_ref[0], refs[: 2 * pieces], span)
    for index in range(blocks):
        q = stacked(q_ref, index * Q_BLOCK, Q_BLOCK, heads)
        first_key, place = bounds(start_ref, index, heads, reach)
        acc[...] = jnp.zeros_like(acc)

        def step(j, carry):
            top, total = carry
            keys = pl.ds(pl.multiple_of(j * K_BLOCK, K_BLOCK), K_BLOCK)
            s = dot(span[0, keys], q, 1, 1) * SCALE
            key = j * K_BLOCK + lax.broadcasted_iota(jnp.int32, (K_BLOCK, wide), 0)
            s = jnp.where((key >= first_key) & (key <= place), s, NEG_FILL)
            later = jnp.maximum(top, jnp.max(s, axis=0, keepdims=True))
            p = jnp.exp(s - later)
            fade = jnp.exp(top - later)
            total = total * fade + jnp.sum(p, axis=0, keepdims=True)
            acc[...] = acc[...] * fade + dot(span[1, keys], to_bf(p), 0, 0)
            return later, total

        last = (reach + (index + 1) * Q_BLOCK - 1) // K_BLOCK + 1
        top, total = lax.fori_loop(
            low_ref[row, index],
            last,
            step,
            (jnp.full((1, wide), NEG_FILL, jnp.float32), jnp.zeros((1, wide), jnp.float32)),
        )
        out = to_bf((acc[...] / total).T)
        for h in range(heads):
            o_ref[0, index * Q_BLOCK : (index + 1) * Q_BLOCK, h * HD : (h + 1) * HD] = out[
                h * Q_BLOCK : (h + 1) * Q_BLOCK
            ]
        lse_ref[0, index : index + 1, :] = top + jnp.log(total)


def span_specs(rows, local, pieces):
    near = pl.BlockSpec((1, local, HD), lambda i, *refs: (i, 0, 0))
    far = pl.BlockSpec((1, local, HD), lambda i, *refs: (lax.rem(i + rows // 2, rows), 0, 0))
    return [near] * pieces + [far] * pieces


def attend(low, core, q, start, span, mate):
    rows, local, columns = q.shape
    pieces = len(span)
    heads = columns // HD
    blocks = local // Q_BLOCK

    def at(i, *refs):
        return (i, 0, 0)

    return pl.pallas_call(
        functools.partial(attend_kernel, heads, blocks, pieces),
        grid_spec=pltpu.PrefetchScalarGridSpec(
            num_scalar_prefetch=2,
            grid=(rows,),
            in_specs=[pl.BlockSpec((1, local, columns), at), pl.BlockSpec((1, 1, local), at)]
            + span_specs(rows, local, pieces),
            out_specs=[
                pl.BlockSpec((1, local, columns), at),
                pl.BlockSpec((1, blocks, heads * Q_BLOCK), at),
            ],
            scratch_shapes=[
                pltpu.VMEM((HD, heads * Q_BLOCK), jnp.float32),
                pltpu.VMEM((2, pieces * local, HD), jnp.bfloat16),
            ],
        ),
        out_shape=[
            jax.ShapeDtypeStruct((rows, local, columns), jnp.bfloat16),
            jax.ShapeDtypeStruct((rows, blocks, heads * Q_BLOCK), jnp.float32),
        ],
        compiler_params=pltpu.CompilerParams(vmem_limit_bytes=32 * MIB),
        cost_estimate=cost(8_000_000_000, 4 * MIB),
        name="attend",
    )(low, core, q, start, *span, *mate)


def attend_back_kernel(
    heads, blocks, pieces, low_ref, core_ref, q_ref, start_ref, g_ref, o_ref, lse_ref, cos_ref, sin_ref, *refs
):
    gq_ref, keep_ref, send_ref, acc, gk, gv, span = refs[2 * pieces :]
    row = pl.program_id(0)
    wide = heads * Q_BLOCK
    reach = (pieces - 1) * q_ref.shape[1]
    core = core_ref[0]
    gather_span(core, refs[: 2 * pieces], span)
    gk[...] = jnp.zeros_like(gk)
    gv[...] = jnp.zeros_like(gv)
    for index in range(blocks):
        q = stacked(q_ref, index * Q_BLOCK, Q_BLOCK, heads)
        g = stacked(g_ref, index * Q_BLOCK, Q_BLOCK, heads)
        o = stacked(o_ref, index * Q_BLOCK, Q_BLOCK, heads)
        inner = jnp.sum((to_f(g) * to_f(o)).T, axis=0, keepdims=True)
        lse = lse_ref[0, index : index + 1, :]
        first_key, place = bounds(start_ref, index, heads, reach)
        acc[...] = jnp.zeros_like(acc)

        def step(j, carry):
            keys = pl.ds(pl.multiple_of(j * K_BLOCK, K_BLOCK), K_BLOCK)
            k = span[0, keys]
            s = dot(k, q, 1, 1) * SCALE
            key = j * K_BLOCK + lax.broadcasted_iota(jnp.int32, (K_BLOCK, wide), 0)
            p = jnp.where((key >= first_key) & (key <= place), jnp.exp(s - lse), 0.0)
            gp = dot(span[1, keys], g, 1, 1)
            gs = to_bf(p * (gp - inner))
            gv[keys] += dot(to_bf(p), g)
            gk[keys] += dot(gs, q)
            acc[...] += dot(k, gs, 0, 0)
            return carry

        last = (reach + (index + 1) * Q_BLOCK - 1) // K_BLOCK + 1
        lax.fori_loop(low_ref[row, index], last, step, 0)
        gq = acc[...].T * SCALE
        here = slice(index * Q_BLOCK, (index + 1) * Q_BLOCK)
        cosine, sine = cos_ref[here], sin_ref[here]
        for h in range(heads):
            part = gq[h * Q_BLOCK : (h + 1) * Q_BLOCK]
            gq_ref[0, here, h * HD : (h + 1) * HD] = to_bf(
                part * cosine + pltpu.roll(part * sine, HD // 2, 1)
            )
    is_key = core == 0
    keys, values = gk[...] * SCALE, gv[...]
    keep_ref[0] = to_bf(jnp.where(is_key, keys, values))
    send_ref[0] = to_bf(jnp.where(is_key, values, keys))


def attend_back(order, low, core, q, start, span, mate, grad, out, lse, cosine, sine):
    rows, local, columns = q.shape
    pieces = len(span)
    window = pieces * local
    heads = columns // HD
    blocks = local // Q_BLOCK

    def at(i, *refs):
        return (i, 0, 0)

    table = pl.BlockSpec((local, HD), lambda i, *refs: (i, 0))
    tokens = pl.BlockSpec((1, local, columns), at)
    return order(
        functools.partial(attend_back_kernel, heads, blocks, pieces),
        [q, start, grad, out, lse, cosine, sine, *span, *mate],
        [
            tokens,
            pl.BlockSpec((1, 1, local), at),
            tokens,
            tokens,
            pl.BlockSpec((1, blocks, heads * Q_BLOCK), at),
            table,
            table,
        ]
        + span_specs(rows, local, pieces),
        [tokens, pl.BlockSpec((1, window, HD), at), pl.BlockSpec((1, window, HD), at)],
        [
            jax.ShapeDtypeStruct((rows, local, columns), jnp.bfloat16),
            jax.ShapeDtypeStruct((rows, window, HD), jnp.bfloat16),
            jax.ShapeDtypeStruct((rows, window, HD), jnp.bfloat16),
        ],
        (rows,),
        20_000_000_000,
        6 * MIB,
        "attend_back",
        scalars=(low, core),
        scratch=[
            pltpu.VMEM((HD, heads * Q_BLOCK), jnp.float32),
            pltpu.VMEM((window, HD), jnp.float32),
            pltpu.VMEM((window, HD), jnp.float32),
            pltpu.VMEM((2, window, HD), jnp.bfloat16),
        ],
    )


def fold_kernel(keep_ref, come_ref, own_ref, *send_refs):
    local = own_ref.shape[1]
    total = to_f(keep_ref[0]) + to_f(come_ref[0])
    reach = total.shape[0] - local
    own_ref[0] = total[reach:]
    for hop, ref in enumerate(send_refs, 1):
        ref[0] = to_bf(total[reach - hop * local : reach - (hop - 1) * local])


def fold(order, keep, come, local):
    rows, window = keep.shape[:2]
    hops = window // local - 1
    out = pl.BlockSpec((1, local, HD), lambda i: (i, 0, 0))
    return order(
        fold_kernel,
        [keep, come],
        [
            pl.BlockSpec((1, window, HD), lambda i: (i, 0, 0)),
            pl.BlockSpec((1, window, HD), lambda i: (lax.rem(i + rows // 2, rows), 0, 0)),
        ],
        [out] * (hops + 1),
        [jax.ShapeDtypeStruct((rows, local, HD), jnp.float32)]
        + [jax.ShapeDtypeStruct((rows, local, HD), jnp.bfloat16)] * hops,
        (rows,),
        0,
        4 * MIB,
        "fold",
    )


def carry_kernel(piece_ref, come_ref, out_ref):
    out_ref[...] = to_bf(to_f(piece_ref[...]) + to_f(come_ref[...]))


def carry(order, piece, come):
    rows, local, columns = piece.shape
    at = pl.BlockSpec((1, local, columns), lambda i: (i, 0, 0))
    return order(
        carry_kernel,
        [piece, come],
        [at, at],
        [at],
        [jax.ShapeDtypeStruct(piece.shape, jnp.bfloat16)],
        (rows,),
        0,
        2 * MIB,
        "carry",
    )[0]


def bias_kernel(left_ref, right_ref, out_ref):
    out_ref[...] = left_ref[...] + right_ref[...]


def bias_add(order, left, right):
    whole = pl.BlockSpec(left.shape, lambda i: (0, 0))
    return order(
        bias_kernel,
        [left, right],
        [whole, whole],
        [whole],
        [jax.ShapeDtypeStruct(left.shape, jnp.float32)],
        (1,),
        0,
        MIB,
        "bias",
    )[0]


def join_kernel(hops, core_ref, gq_ref, cos_ref, sin_ref, own_ref, *refs):
    out_ref, sum_ref = refs[-2:]
    columns = gq_ref.shape[2]
    grad = own_ref[0]
    for ref in refs[:hops]:
        grad = grad + to_f(ref[0])
    is_key = core_ref[0] == 0
    cosine = jnp.where(is_key, cos_ref[...], 1.0)
    sine = jnp.where(is_key, sin_ref[...], 0.0)
    kv = to_bf(grad * cosine + pltpu.roll(grad * sine, HD // 2, 1))
    q = gq_ref[0]
    out_ref[:, :columns] = q
    out_ref[:, columns:] = kv

    @pl.when(pl.program_id(0) == 0)
    def _():
        sum_ref[...] = jnp.zeros(sum_ref.shape, jnp.float32)

    sum_ref[:, :columns] += jnp.sum(to_f(q), axis=0, keepdims=True)
    sum_ref[:, columns:] += jnp.sum(to_f(kv), axis=0, keepdims=True)


def join(order, core, grad_q, own, comes, cosine, sine):
    rows, local, columns = grad_q.shape
    wide = columns + HD

    def at(i, *refs):
        return (i, 0, 0)

    piece = pl.BlockSpec((1, local, HD), at)
    table = pl.BlockSpec((local, HD), lambda i, *refs: (i, 0))
    return order(
        functools.partial(join_kernel, len(comes)),
        [grad_q, cosine, sine, own, *comes],
        [pl.BlockSpec((1, local, columns), at), table, table, piece] + [piece] * len(comes),
        [
            pl.BlockSpec((local, wide), lambda i, *refs: (i, 0)),
            pl.BlockSpec((8, wide), lambda i, *refs: (0, 0)),
        ],
        [
            jax.ShapeDtypeStruct((rows * local, wide), jnp.bfloat16),
            jax.ShapeDtypeStruct((8, wide), jnp.float32),
        ],
        (rows,),
        0,
        4 * MIB,
        "join",
        scalars=(core,),
    )


def mixed_back_kernel(w_ref, *refs):
    rows = refs[0].shape[0]
    for i, ref in enumerate(refs[:-1]):
        refs[-1][i * rows : (i + 1) * rows] = to_bf(dot(ref[...], w_ref[...]))


def mixed_back(order, pieces, weight):
    rows, width = pieces[0].shape
    total = rows * len(pieces)
    columns = weight.shape[1]

    def whole(i):
        return (0, 0)

    return order(
        mixed_back_kernel,
        [weight, *pieces],
        [pl.BlockSpec((width, columns), whole)] + [pl.BlockSpec((rows, width), whole)] * len(pieces),
        [pl.BlockSpec((total, columns), whole)],
        [jax.ShapeDtypeStruct((total, columns), jnp.bfloat16)],
        (1,),
        2 * total * width * columns,
        6 * MIB,
        "mixed_back",
    )[0]


def place_kernel(core_ref, *refs):
    for i, ref in enumerate(refs[:-1]):

        @pl.when(pl.program_id(0) == i)
        def _(ref=ref):
            refs[-1][...] = ref[...]


def place(order, core, pieces):
    rows, width = pieces[0].shape
    count = len(pieces)
    return order(
        place_kernel,
        list(pieces),
        [pl.BlockSpec((rows, width), lambda i, core_ref: (0, 0))] * count,
        [pl.BlockSpec((rows, width), lambda i, core_ref: (lax.rem(i + core_ref[0] * (count // 2), count), 0))],
        [jax.ShapeDtypeStruct((rows * count, width), pieces[0].dtype)],
        (count,),
        0,
        8 * rows * width,
        "place",
        scalars=(core,),
    )[0]


def anchors(count):
    return [pl.BlockSpec(memory_space=pl.ANY)] * count


MARK = jax.ShapeDtypeStruct((8, HD), jnp.float32)


def mark_spec():
    return pl.BlockSpec((8, HD), lambda *refs: (0, 0))


def grad_hidden_kernel(g_ref, w_ref, out_ref):
    out_ref[...] = to_bf(dot(g_ref[...], w_ref[...], 1, 1))


def grad_hidden_of(order, grad, weight):
    total, width = grad.shape
    hidden = weight.shape[0]
    return order(
        grad_hidden_kernel,
        [grad, weight],
        [pl.BlockSpec((total, width), lambda i: (0, 0)), pl.BlockSpec((TILE, width), lambda i: (i, 0))],
        [pl.BlockSpec((total, TILE), lambda i: (0, i))],
        [jax.ShapeDtypeStruct((total, hidden), jnp.bfloat16)],
        (pl.cdiv(hidden, TILE),),
        2 * total * width * hidden,
        15 * MIB,
        "grad_hidden",
    )[0]


def gated_kernel(gh_ref, gw_ref, uw_ref, *refs):
    hid_ref, gg_ref, gu_ref = refs[-3:]
    rows = refs[0].shape[0]
    for part, ref in enumerate(refs[:-3]):
        here = slice(part * rows, (part + 1) * rows)
        h = ref[...]
        gate = dot(h, gw_ref[...], 1, 1)
        up = dot(h, uw_ref[...], 1, 1)
        grad = to_f(gh_ref[here])
        sigma = 1.0 / (1.0 + jnp.exp(-gate))
        swish = gate * sigma
        hid_ref[here] = to_bf(swish * up)
        gu_ref[here] = to_bf(grad * swish)
        gg_ref[here] = to_bf(grad * up * sigma * (1.0 + gate * (1.0 - sigma)))


def gated(order, pieces, grad_hidden, gate_weight, up_weight):
    rows, width = pieces[0].shape
    total = rows * len(pieces)
    hidden = gate_weight.shape[0]
    column = pl.BlockSpec((total, TILE), lambda i: (0, i))
    weight = pl.BlockSpec((TILE, width), lambda i: (i, 0))
    shape = jax.ShapeDtypeStruct((total, hidden), jnp.bfloat16)
    return order(
        gated_kernel,
        [grad_hidden, gate_weight, up_weight, *pieces],
        [column, weight, weight] + [pl.BlockSpec((rows, width), lambda i: (0, 0))] * len(pieces),
        [column] * 3,
        [shape] * 3,
        (pl.cdiv(hidden, TILE),),
        4 * total * width * hidden,
        30 * MIB,
        "gated",
    )


def share_kernel(plan, lefts, rights, extra, halves, groups, pick_ref, blocks_ref, *refs):
    step = pl.program_id(0)
    left_refs, right_refs = refs[:lefts], refs[lefts : lefts + rights]
    refs = refs[lefts + rights :]
    if extra:
        extra_ref, refs = refs[0], refs[1:]
    for left, right, begin, end, shift, columns, target in plan:

        @pl.when((step >= begin) & (step < end))
        def _(left=left, right=right, shift=shift, columns=columns, target=target):
            out = dot(left_refs[left][...], right_refs[right][...])
            if extra:
                out = out + to_f(extra_ref[...])
            tile = out.shape[1]
            spot = (step + shift) * tile + lax.broadcasted_iota(jnp.int32, (1, tile), 1)
            out = to_bf(jnp.where(spot < columns, out, 0.0))
            if groups:
                share = out.shape[0] // (groups[0] * groups[1])
                for i in range(groups[0]):
                    for j in range(groups[1]):
                        here = (j * groups[0] + i) * share
                        there = (i * groups[1] + j) * share
                        refs[target][here : here + share] = out[there : there + share]
                return
            if not halves:
                refs[target][...] = out
                return
            send_ref, keep_ref, rows = refs
            rows[...] = out
            share = send_ref.shape[0] // (2 * halves)
            for i in range(2 * halves):
                here = slice(i * share, (i + 1) * share)
                send_ref[here] = rows[pl.ds(pl.multiple_of(blocks_ref[i] * share, share), share)]
                keep_ref[here] = rows[pl.ds(pl.multiple_of(blocks_ref[2 * halves + i] * share, share), share)]


def clipped(rows, tile, begin, count, shift=0):
    return pl.BlockSpec((rows, tile), lambda i, *refs: (0, jnp.clip(i - begin, 0, count - 1) + shift))


def share_of(order, lefts, rights, parts, part, pick, tile, extra=None, blocks=None, groups=None):
    tokens = lefts[0].shape[1]
    plan, at = [], 0
    starts, sizes, right_at = {}, {}, {}
    for left, right, skip, count, target in parts:
        plan.append((left, right, at, at + count, skip - at, rights[right].shape[1], target))
        starts.setdefault(target, at)
        sizes[target] = sizes.get(target, 0) + count
        first, tiles, low = right_at.get(right, (at, 0, skip))
        right_at[right] = (first, tiles + count, low)
        at += count
    halves = 0
    extras = [] if extra is None else [extra]
    scratch = []
    if blocks is None:
        blocks = jnp.zeros((1,), jnp.int32)
        outs = [clipped(part, tile, starts[t], sizes[t]) for t in sorted(sizes)]
        shapes = [jax.ShapeDtypeStruct((part, sizes[t] * tile), jnp.bfloat16) for t in sorted(sizes)]
    else:
        halves = blocks.shape[0] // 4
        outs = [clipped(part // 2, tile, 0, at)] * 2
        shapes = [jax.ShapeDtypeStruct((part // 2, at * tile), jnp.bfloat16)] * 2
        scratch = [pltpu.VMEM((part, tile), jnp.bfloat16)]
    return order(
        functools.partial(share_kernel, plan, len(lefts), len(rights), len(extras), halves, groups),
        [*lefts, *rights, *extras],
        [pl.BlockSpec((part, tokens), lambda i, pick_ref, blocks_ref: (pick_ref[0], 0))] * len(lefts)
        + [clipped(tokens, tile, *right_at[r]) for r in range(len(rights))]
        + [clipped(part, tile, 0, at)] * len(extras),
        outs,
        shapes,
        (at,),
        2 * part * tokens * at * tile,
        2 * (part * tokens + (part + tokens) * at * tile),
        "share",
        scalars=(jnp.asarray(pick, jnp.int32).reshape(1), blocks),
        scratch=scratch,
    )


def relay_kernel(keep_ref, come_ref, out_ref):
    out_ref[...] = to_bf(to_f(keep_ref[...]) + to_f(come_ref[...]))


def relay(order, keep, come, share):
    rows, columns = keep.shape
    pair = pl.BlockSpec((share, columns), lambda i: (2 * i + 1, 0))
    return order(
        relay_kernel,
        [keep, come],
        [pair, pair],
        [pl.BlockSpec((share, columns), lambda i: (i, 0))],
        [jax.ShapeDtypeStruct((rows // 2, columns), jnp.bfloat16)],
        (rows // (2 * share),),
        0,
        3 * rows * columns,
        "relay",
    )[0]


def finish_kernel(plan, columns, gains, *refs):
    out_ref = refs[-2] if gains else refs[-1]
    step = pl.program_id(0)
    tile = out_ref.shape[1]
    for begin, end, first, count in plan:

        @pl.when((step >= begin) & (step < end))
        def _(first=first, count=count):
            out = to_f(refs[first][...])
            for ref in refs[first + 1 : first + count]:
                out = out + to_f(ref[...])
            out_ref[...] = out
            if gains:
                spot = step * tile + lax.broadcasted_iota(jnp.int32, (1, tile), 1)
                terms = jnp.where(spot < columns, out * to_f(refs[-3][...]), 0.0)
                total = terms[:, :HD]
                for i in range(HD, tile, HD):
                    total = total + terms[:, i : i + HD]

                @pl.when(step == 0)
                def _():
                    refs[-1][...] = total

                @pl.when(step > 0)
                def _():
                    refs[-1][...] += total


def finish(order, chunks, share, columns, tile, weight=None):
    plan, specs, args, at = [], [], [], 0
    for chunk in chunks:
        count = chunk[0].shape[1] // tile
        plan.append((at, at + count, len(args), len(chunk)))
        specs += [clipped(share, tile, at, count)] * len(chunk)
        args += chunk
        at += count
    column = pl.BlockSpec((share, tile), lambda i: (0, i))
    outs, shapes = [column], [jax.ShapeDtypeStruct((share, columns), jnp.float32)]
    if weight is not None:
        args.append(weight)
        specs.append(column)
        outs.append(pl.BlockSpec((share, HD), lambda i: (0, 0)))
        shapes.append(jax.ShapeDtypeStruct((share, HD), jnp.float32))
    return order(
        functools.partial(finish_kernel, plan, columns, weight is not None),
        args,
        specs,
        outs,
        shapes,
        (at,),
        0,
        14 * share * columns,
        "finish",
    )


def narrow_kernel(pairs, extras, right_dim, *refs):
    out = dot(refs[0][...], refs[1][...], 1, right_dim)
    for i in range(1, pairs):
        out = out + dot(refs[2 * i][...], refs[2 * i + 1][...], 1, right_dim)
    extra = refs[2 * pairs : 2 * pairs + extras]
    outs = refs[2 * pairs + extras :]
    if extras:
        out = out + jnp.concatenate([to_f(ref[...]) for ref in extra], axis=0)
    rows = outs[0].shape[0]
    for i, ref in enumerate(outs):
        ref[...] = to_bf(out[i * rows : (i + 1) * rows])


def narrow(order, pairs, index, extra=(), right_dim=0):
    total, hidden = pairs[0][0].shape
    width = pairs[0][1].shape[1 - right_dim]
    half = total // 2
    piece = half // PIECES
    column = pl.BlockSpec((piece, TILE), lambda i: (0, i))
    right = (
        pl.BlockSpec((TILE, hidden), lambda i: (i, 0))
        if right_dim
        else pl.BlockSpec((hidden, TILE), lambda i: (0, i))
    )
    return order(
        functools.partial(narrow_kernel, len(pairs), len(extra), right_dim),
        [item for pair in pairs for item in pair] + list(extra),
        [pl.BlockSpec((half, hidden), lambda i: (index, 0)), right] * len(pairs) + [column] * len(extra),
        [column] * PIECES,
        [jax.ShapeDtypeStruct((piece, width), jnp.bfloat16)] * PIECES,
        (width // TILE,),
        2 * len(pairs) * half * width * hidden,
        2 * len(pairs) * (half + width) * hidden + 2 * half * width,
        "narrow",
    )


def piece_specs(piece, width, block):
    steps = piece // block
    return [
        pl.BlockSpec((block, width), lambda i, *refs, j=j: (jnp.clip(i - j * steps, 0, steps - 1), 0))
        for j in range(PIECES)
    ]


def pick_piece(refs):
    value = refs[0][...]
    for j, ref in enumerate(refs[1:], 1):
        value = jnp.where(pl.program_id(0) >= 4 * j // len(refs), ref[...], value)
    return value


def put_piece(refs, value):
    steps = 4 // len(refs)
    for j, ref in enumerate(refs):

        @pl.when(lax.div(pl.program_id(0), steps) == j)
        def _(ref=ref):
            ref[...] = value


def turn_kernel(*refs):
    rows = refs[0].shape[0]
    for i, ref in enumerate(refs[:-1]):
        refs[-1][:, i * rows : (i + 1) * rows] = ref[...].T


def turn(order, pieces):
    rows, width = pieces[0].shape
    total = rows * len(pieces)
    return order(
        turn_kernel,
        list(pieces),
        [pl.BlockSpec((rows, TILE), lambda i: (0, i))] * len(pieces),
        [pl.BlockSpec((TILE, total), lambda i: (i, 0))],
        [jax.ShapeDtypeStruct((width, total), jnp.bfloat16)],
        (width // TILE,),
        0,
        4 * total * width,
        "turn",
    )[0]


def grad_out_kernel(core_ref, cot_ref, valid_ref, out_ref, turned_ref):
    out = to_bf(to_f(cot_ref[...]) * valid_ref[...])
    out_ref[...] = out
    turned_ref[...] = out.T


def grad_out_of(order, core, cotangent, valid):
    total, width = cotangent.shape
    block = total // 4
    return order(
        grad_out_kernel,
        [cotangent, valid],
        [
            pl.BlockSpec((block, width), lambda i, core_ref: (lax.rem(i + core_ref[0] * 2, 4), 0)),
            pl.BlockSpec((block, 1), lambda i, core_ref: (i, 0)),
        ],
        [
            pl.BlockSpec((block, width), lambda i, core_ref: (i, 0)),
            pl.BlockSpec((width, block), lambda i, core_ref: (0, i)),
        ],
        [
            jax.ShapeDtypeStruct((total, width), jnp.bfloat16),
            jax.ShapeDtypeStruct((width, total), jnp.bfloat16),
        ],
        (4,),
        0,
        6 * total * width,
        "grad_out",
        scalars=(core,),
    )


def middle_kernel(core_ref, tok_ref, gain_ref, *refs):
    mine, come = pick_piece(refs[:PIECES]), pick_piece(refs[PIECES : 2 * PIECES])
    mid_ref, *h_refs = refs[2 * PIECES :]
    middle = to_f(tok_ref[...]) + (to_f(mine) + to_f(come))
    factor = lax.rsqrt(jnp.mean(middle * middle, axis=-1, keepdims=True) + EPS)
    mid_ref[...] = middle
    put_piece(h_refs, to_bf(middle * factor * gain_ref[...]))


def middle_of(order, core, tokens, mine, come, gain):
    piece, width = mine[0].shape
    half = piece * PIECES
    block = half // 4
    specs = piece_specs(piece, width, block)
    middle, *h = order(
        middle_kernel,
        [tokens, gain, *mine, *come],
        [
            pl.BlockSpec((block, width), lambda i, core_ref: (core_ref[0] * 4 + i, 0)),
            pl.BlockSpec((1, width), lambda i, core_ref: (0, 0)),
        ]
        + specs * 2,
        [pl.BlockSpec((block, width), lambda i, core_ref: (i, 0))] + specs,
        [jax.ShapeDtypeStruct((half, width), jnp.float32)]
        + [jax.ShapeDtypeStruct((piece, width), jnp.bfloat16)] * PIECES,
        (4,),
        0,
        9 * MIB,
        "middle",
        scalars=(core,),
    )
    return middle, h


def norm_back_kernel(core_ref, x_ref, gain_ref, up_ref, *refs):
    mine, come = pick_piece(refs[:PIECES]), pick_piece(refs[PIECES : 2 * PIECES])
    outs = refs[2 * PIECES :]
    grad = to_f(mine) + to_f(come)
    x = to_f(x_ref[...])
    factor = lax.rsqrt(jnp.mean(x * x, axis=-1, keepdims=True) + EPS)
    normed = x * factor
    weighted = grad * gain_ref[...]
    inner = jnp.mean(weighted * normed, axis=-1, keepdims=True)
    out = to_f(up_ref[...]) + factor * (weighted - normed * inner)
    if len(outs) > PIECES:
        outs[0][...] = out
        put_piece(outs[1:], to_bf(out))
    else:
        put_piece(outs, out)


def norm_back(order, core, mine, come, x, gain, up, by_core):
    piece, width = mine[0].shape
    half = piece * PIECES
    block = half // 4
    at = pl.BlockSpec((block, width), lambda i, core_ref: (i, 0))
    picked = pl.BlockSpec((block, width), lambda i, core_ref: (core_ref[0] * 4 + i, 0))
    specs = piece_specs(piece, width, block)
    if by_core:
        shapes = [jax.ShapeDtypeStruct((piece, width), jnp.float32)] * PIECES
    else:
        shapes = [jax.ShapeDtypeStruct((half, width), jnp.float32)]
        shapes += [jax.ShapeDtypeStruct((piece, width), jnp.bfloat16)] * PIECES
    return order(
        norm_back_kernel,
        [x, gain, up, *mine, *come],
        [picked if by_core else at, pl.BlockSpec((1, width), lambda i, core_ref: (0, 0)), at] + specs * 2,
        specs if by_core else [at] + specs,
        shapes,
        (4,),
        0,
        10 * MIB,
        "norm_back",
        scalars=(core,),
    )


def layer_kernel(middle_ref, *refs):
    mine, come = pick_piece(refs[:PIECES]), pick_piece(refs[PIECES : 2 * PIECES])
    put_piece(refs[2 * PIECES :], to_bf(middle_ref[...] + (to_f(mine) + to_f(come))))


def layer_of(order, middle, mine, come):
    piece, width = mine[0].shape
    block = piece * PIECES // 4
    specs = piece_specs(piece, width, block)
    return order(
        layer_kernel,
        [middle, *mine, *come],
        [pl.BlockSpec((block, width), lambda i: (i, 0))] + specs * 2,
        specs,
        [jax.ShapeDtypeStruct((piece, width), jnp.bfloat16)] * PIECES,
        (4,),
        0,
        5 * MIB,
        "layer",
    )


def tensor_gather(value, rank):
    mate = core_swap(value)
    pair = jnp.where(lax.rem(rank, 2) == 0, jnp.stack([value, mate]), jnp.stack([mate, value]))
    come = chip_swap(pair)
    return jnp.where(
        lax.div(rank, 2) == 0,
        jnp.concatenate([pair, come], axis=0),
        jnp.concatenate([come, pair], axis=0),
    )


def body(
    tokens,
    lengths,
    cotangent,
    q_weight,
    q_bias,
    k_weight,
    k_bias,
    v_weight,
    v_bias,
    o_weight,
    attn_gain,
    ffn_gain,
    gate_weight,
    up_weight,
    down_weight,
):
    rows, local, width = tokens.shape
    total = rows * local
    half = total // 2
    heads = q_weight.shape[1] // HD
    ranks = lax.axis_size("tensor")
    seqs = lax.axis_size("seq")
    rank = lax.axis_index("tensor")
    dp_index = lax.axis_index("dp")
    seq_index = lax.axis_index("seq")
    core = lax.rem(rank, 2)
    head = lax.div(rank, 2)
    core_one = core.reshape(1)
    hops = min(seqs - 1, -(-(MOST - 1) // local))
    reach = hops * local

    def own_first(value):
        turned = jnp.concatenate([value[rows // 2 :], value[: rows // 2]], axis=0)
        return jnp.where(core == 0, value, turned)

    slots = jnp.arange(lengths.shape[1], dtype=jnp.int32)
    lens = own_first(lengths)
    ends = jnp.sum(jnp.where(slots[None, :] <= slots[:, None], lens[:, None, :], 0), axis=2)
    spot = seq_index * local + jnp.arange(local, dtype=jnp.int32)
    begun = jnp.max(
        jnp.where(ends[:, None, :] <= spot[None, :, None], ends[:, None, :], 0), axis=2
    )
    valid = to_f(spot[None, :] < ends[:, -2:-1])
    position = (spot[None, :] - begun).reshape(total, 1)
    freqs = ROPE_BASE ** (-(jnp.arange(HD // 2, dtype=jnp.float32) * 2.0) / HD)
    angles = to_f(position) * freqs[None, :]
    cosine, sine = jnp.cos(angles), jnp.sin(angles)
    cosine = jnp.concatenate([cosine, cosine], axis=1)
    sine = jnp.concatenate([-sine, sine], axis=1)
    start = begun - (seq_index * local - reach)
    low = jnp.maximum(lax.div(jnp.maximum(start[:, ::Q_BLOCK], 0), K_BLOCK), 0)
    start = start.reshape(rows, 1, local)

    key_side = core == 0
    kv_weight = jnp.where(
        key_side,
        lax.dynamic_slice_in_dim(k_weight, head * HD, HD, 1),
        lax.dynamic_slice_in_dim(v_weight, head * HD, HD, 1),
    )
    kv_bias = jnp.where(
        key_side,
        lax.dynamic_slice_in_dim(k_bias, head * HD, HD, 0),
        lax.dynamic_slice_in_dim(v_bias, head * HD, HD, 0),
    )
    weight = jnp.concatenate([q_weight, kv_weight], axis=1)
    bias = to_f(jnp.concatenate([q_bias, kv_bias])).reshape(1, -1)
    gain_one = to_f(attn_gain).reshape(1, width)
    gain_two = to_f(ffn_gain).reshape(1, width)

    h_one, q_rot, kv = first(
        core_one, tokens.reshape(total, width), gain_one, weight, bias, cosine, sine
    )
    kv = kv.reshape(rows, local, HD)
    span = [shifted(kv, h) for h in range(hops, 0, -1)] + [kv]
    mate = [core_swap(piece) for piece in span]
    q_rows = q_rot.reshape(rows, local, heads * HD)
    mixed_rows, lse = attend(low, core_one, q_rows, start, span, mate)
    mixed = mixed_rows.reshape(total, heads * HD)

    order = Order()
    flat_tokens = tokens.reshape(total, width)
    dps = lax.axis_size("dp")
    near_pair = dps == 2 and seqs == 4
    part = width // dps
    share = part // seqs
    gate_t, up_t, down_t = gate_weight.T, up_weight.T, down_weight.T
    units = gate_t.shape[0]
    tiles = -(-units // TILE)
    cut = (tiles + 1) // 2
    long = max(tiles - 2, 1)
    one, two = seq_index ^ 1, seq_index ^ 2
    three = seq_index ^ 3
    quad = jnp.stack([one, three, seq_index, two])

    begin = (dp_index * seqs + seq_index) * share

    def rows_of(value):
        return lax.dynamic_slice_in_dim(value, begin, share, 0)

    class Rows:
        def __init__(self, lefts, rights, parts, tile=TILE, sent=None):
            self.args = (order, lefts, rights, parts)
            self.tile = tile
            if not near_pair:
                (whole,) = share_of(*self.args, width, 0, tile)
                self.whole = lax.psum_scatter(whole, ("dp", "seq"), scatter_dimension=0, tiled=True)
                return
            if sent is None:
                (sent,) = share_of(*self.args, part, 1 - dp_index, tile)
            self.come = lax.ppermute(sent, "dp", flipped("dp", 0))

        def own(self):
            if near_pair:
                send, self.keep = share_of(*self.args, part, dp_index, self.tile, self.come, quad)
                self.come = lax.ppermute(send, "seq", flipped("seq", 0))

        def relay(self):
            if near_pair:
                sent = relay(order, self.keep, self.come, share)
                self.last = lax.ppermute(sent, "seq", flipped("seq", 1))

        def settled(self):
            if near_pair:
                order.arrived(self.last)

        def result(self):
            return [self.keep, self.come, self.last] if near_pair else [self.whole]

    class SeqFirst(Rows):
        def __init__(self, lefts, rights, parts, tile=TILE):
            if not near_pair:
                super().__init__(lefts, rights, parts, tile)
                return
            (whole,) = share_of(order, lefts, rights, parts, width, 0, tile, None, None, (dps, seqs))
            self.mine = lax.psum_scatter(whole, "seq", scatter_dimension=0, tiled=True)

        def across(self):
            if near_pair:
                sent = lax.dynamic_slice_in_dim(self.mine, (1 - dp_index) * share, share, 0)
                self.mine = lax.dynamic_slice_in_dim(self.mine, dp_index * share, share, 0)
                order.arrived(sent, self.mine)
                self.come = lax.ppermute(sent, "dp", flipped("dp", 0))

        def settled(self):
            if near_pair:
                order.arrived(self.come)

        def result(self):
            return [self.mine, self.come] if near_pair else [self.whole]

    class Scattered(Rows):
        def own(self):
            if near_pair:
                (mine,) = share_of(*self.args, part, dp_index, self.tile, self.come)
                self.whole = lax.psum_scatter(mine, "seq", scatter_dimension=0, tiled=True)

        def settled(self):
            order.arrived(self.whole)

        def result(self):
            return [self.whole]

    sent = core_swaps(narrow(order, [(mixed, o_weight)], 1, (), 1))
    mine = narrow(order, [(mixed, o_weight)], 0, sent, 1)
    come = chip_swaps(mine)
    grad_ffn, grad_ffn_t = grad_out_of(
        order, core_one, cotangent.reshape(total, width), valid.reshape(total, 1)
    )
    gate_rows, up_rows = rows_of(gate_weight), rows_of(up_weight)
    order.arrived(gate_rows, up_rows)
    grad_hidden = grad_hidden_of(order, grad_ffn, down_t)
    h_one_t = turn(order, [h_one])
    middle, h_two = middle_of(order, core_one, flat_tokens, mine, come, gain_two)
    h_two += core_swaps(h_two)
    hidden, grad_gate, grad_up = gated(order, h_two, grad_hidden, gate_t, up_t)

    down_b = SeqFirst([grad_ffn_t], [hidden], [(0, 0, cut, tiles - cut, 0)])
    down_a = Rows([grad_ffn_t], [hidden], [(0, 0, 0, cut, 0)])
    pairs = [(grad_gate, gate_t), (grad_up, up_t)]
    sent = core_swaps(narrow(order, pairs, 1))
    mine = narrow(order, pairs, 0, sent)
    come = chip_swaps(mine)
    h_two_t = turn(order, h_two)
    if near_pair:
        sends = share_of(
            order,
            [h_two_t],
            [grad_gate, grad_up],
            [(0, 0, 0, tiles, 0), (0, 1, 0, long, 1), (0, 1, long, tiles - long, 2)],
            part,
            1 - dp_index,
            TILE,
        )
    else:
        sends = [None] * 3

    def half_rows(kind, right, begin, end, sent):
        return kind([h_two_t], [right], [(0, 0, begin, end - begin, 0)], TILE, sent)

    gate = half_rows(Scattered, grad_gate, 0, tiles, sends[0])
    up_a = half_rows(Rows, grad_up, 0, long, sends[1])
    up_b = half_rows(Rows, grad_up, long, tiles, sends[2])
    down_a.own()
    grad_middle, *branch = norm_back(order, core_one, mine, come, middle, gain_two, grad_ffn, False)
    branch += core_swaps(branch)
    grad_mixed = mixed_back(order, branch, o_weight).reshape(rows, local, heads * HD)
    grad_q_rows, keep, sent = attend_back(
        order, low, core_one, q_rows, start, span, mate, grad_mixed, mixed_rows, lse, cosine, sine
    )
    both_come = core_swap(sent)
    branch_t = turn(order, branch)
    down_a.relay()
    own_kv, *pieces = fold(order, keep, both_come, local)
    moving = shifted(pieces[-1], -1) if pieces else None
    ffn_sent = core_swaps(narrow(order, [(hidden, down_t)], 1))
    for piece in pieces[-2::-1]:
        moving = shifted(carry(order, piece, moving), -1)
    grad_qkv, bias_sum = join(
        order, core_one, grad_q_rows, own_kv, [] if moving is None else [moving], cosine, sine
    )
    sent = core_swaps(narrow(order, [(grad_qkv, weight)], 1, (), 1))
    down_b.across()
    mine = narrow(order, [(grad_qkv, weight)], 0, sent, 1)
    come = chip_swaps(mine)
    gate.own()
    last_parts = [(0, 0, 0, grad_qkv.shape[1] // HD, 0), (1, 1, 0, heads, 0)]
    last = Rows([h_one_t, branch_t], [grad_qkv, mixed], last_parts, HD)
    ffn_mine = narrow(order, [(hidden, down_t)], 0, ffn_sent)
    token = norm_back(order, core_one, mine, come, flat_tokens, gain_one, grad_middle, True)
    token += core_swaps(token)
    ffn_come = chip_swaps(ffn_mine)
    up_a.own()
    token_grad = place(order, core_one, token).reshape(rows, local, width)
    layer = layer_of(order, middle, ffn_mine, ffn_come)
    layer += core_swaps(layer)
    last.own()
    layer_out = place(order, core_one, layer).reshape(rows, local, width)
    up_a.relay()
    down_a.settled()
    up_b.own()
    last.relay()
    if near_pair:
        bias_come = lax.ppermute(bias_sum, "dp", flipped("dp", 0))
        bias_all = bias_add(order, bias_sum, bias_come)
        bias_come = lax.ppermute(bias_all, "seq", flipped("seq", 0))
    up_a.settled()
    up_b.relay()
    (down_grad,) = finish(order, [down_a.result(), down_b.result()], share, units, TILE)
    gate_grad, gate_term = finish(order, [gate.result()], share, units, TILE, gate_rows)
    wide_columns = grad_qkv.shape[1]
    (last_grad,) = finish(order, [last.result()], share, wide_columns + heads * HD, HD)
    if near_pair:
        bias_all = bias_add(order, bias_all, bias_come)
        bias_come = lax.ppermute(bias_all, "seq", flipped("seq", 1))
        bias_all = (bias_all + bias_come)[:1]
    else:
        bias_all = lax.psum(bias_sum[:1], ("dp", "seq"))
    up_grad, up_term = finish(order, [up_a.result(), up_b.result()], share, units, TILE, up_rows)
    qkv_grad, o_grad = last_grad[:, :wide_columns], last_grad[:, wide_columns:]

    attn_term = jnp.sum(to_f(rows_of(weight)) * qkv_grad, axis=1)
    ffn_term = jnp.sum(gate_term + up_term, axis=1)
    columns = heads * HD
    room = -(-share // HD) * HD - share
    terms = jnp.pad(jnp.stack([ffn_term, attn_term]), ((0, 0), (0, room))).reshape(-1, HD)
    packed = jnp.concatenate([qkv_grad[:, columns:], bias_all.reshape(-1, HD), terms], axis=0)
    gathered = tensor_gather(packed, rank)
    term_rows = terms.shape[0]
    bias_count = bias_all.shape[1] // HD
    terms = gathered[:, share + bias_count :].reshape(ranks, 2, -1)[:, :, :share]
    ffn_gain_grad, attn_gain_grad = terms[0] + terms[1] + (terms[2] + terms[3])
    attn_gain_grad = attn_gain_grad / lax.dynamic_slice_in_dim(gain_one[0], begin, share, 0)
    ffn_gain_grad = ffn_gain_grad / lax.dynamic_slice_in_dim(gain_two[0], begin, share, 0)
    q_grad = qkv_grad[:, :columns]
    kv_parts = lax.dynamic_slice_in_dim(gathered, rank * (share // ranks), share // ranks, 1)
    k_grad = jnp.concatenate([kv_parts[2 * i] for i in range(KVH)], axis=1)
    v_grad = jnp.concatenate([kv_parts[2 * i + 1] for i in range(KVH)], axis=1)
    biases = gathered[:, share : share + bias_count]
    q_bias_grad = biases[:, :heads].reshape(-1)
    k_bias_grad = biases[0::2, heads].reshape(-1)
    v_bias_grad = biases[1::2, heads].reshape(-1)
    return (
        layer_out,
        token_grad,
        q_grad,
        q_bias_grad,
        k_grad,
        k_bias_grad,
        v_grad,
        v_bias_grad,
        o_grad,
        attn_gain_grad,
        ffn_gain_grad,
        gate_grad,
        up_grad,
        down_grad,
    )


def solution(mesh):
    in_specs = (
        P("dp", "seq", None),
        P("dp", None),
        P("dp", "seq", None),
        P(None, "tensor"),
        P("tensor"),
        P(),
        P(),
        P(),
        P(),
        P(None, "tensor"),
        P(),
        P(),
        P(None, "tensor"),
        P(None, "tensor"),
        P(None, "tensor"),
    )
    out_specs = (
        P("dp", "seq", None),
        P("dp", "seq", None),
        P(("dp", "seq"), "tensor"),
        P(),
        P(("dp", "seq", "tensor"), None),
        P(),
        P(("dp", "seq", "tensor"), None),
        P(),
        P(("dp", "seq"), "tensor"),
        P(("dp", "seq")),
        P(("dp", "seq")),
        P(("dp", "seq"), "tensor"),
        P(("dp", "seq"), "tensor"),
        P(("dp", "seq"), "tensor"),
    )
    return jax.shard_map(body, mesh=mesh, in_specs=in_specs, out_specs=out_specs, check_vma=False)
```

```python
import functools
import math

import jax
import jax.numpy as jnp
from jax import lax
from jax.experimental import pallas as pl
from jax.experimental.pallas import tpu as pltpu
from jax.sharding import PartitionSpec as P

KVH = 2
HD = 128
MOST = 1024
EPS = 1e-06
ROPE_BASE = 10000.0
NEG_FILL = -1e30
Q_BLOCK = 256
K_BLOCK = 256
MIB = 1 << 20
LIGHT = 1000
TILE = 256
PIECES = 2
SCALE = 1.0 / math.sqrt(HD)


def to_bf(value):
    return value.astype(jnp.bfloat16)


def to_f(value):
    return value.astype(jnp.float32)


def dot(left, right, left_dim=1, right_dim=0):
    return lax.dot_general(
        left,
        right,
        (((left_dim,), (right_dim,)), ((), ())),
        preferred_element_type=jnp.float32,
    )


def flipped(axis, bit):
    return [(i, i ^ (1 << bit)) for i in range(lax.axis_size(axis))]


def core_swap(value):
    return lax.ppermute(value, "tensor", flipped("tensor", 0))


def chip_swap(value):
    return lax.ppermute(value, "tensor", flipped("tensor", 1))


def core_swaps(values):
    return [core_swap(value) for value in values]


def chip_swaps(values):
    return [chip_swap(value) for value in values]


def shifted(value, hops):
    count = lax.axis_size("seq")
    route = [(i, i + hops) for i in range(count) if 0 <= i + hops < count]
    return lax.ppermute(value, "seq", route)


def cost(flops, read):
    return pl.CostEstimate(flops=flops // LIGHT, bytes_accessed=read // LIGHT, transcendentals=0)


class Order:
    def __init__(self):
        self.mark = None
        self.touched = []

    def arrived(self, *values):
        self.touched.extend(values)

    def __call__(self, kernel, args, in_specs, out_specs, out_shape, grid, flops, read, name, scalars=(), scratch=()):
        anchor = ([] if self.mark is None else [self.mark]) + self.touched
        self.touched = []
        count = len(scalars) + len(args)
        outs = len(out_shape)

        def run(*refs):
            rest = refs[count + len(anchor) :]
            kernel(*refs[:count], *rest[:outs], *rest[outs + 1 :])
            rest[outs][...] = jnp.zeros(rest[outs].shape, jnp.float32)

        *results, self.mark = pl.pallas_call(
            run,
            grid_spec=pltpu.PrefetchScalarGridSpec(
                num_scalar_prefetch=len(scalars),
                grid=grid,
                in_specs=list(in_specs) + anchors(len(anchor)),
                out_specs=list(out_specs) + [mark_spec()],
                scratch_shapes=list(scratch),
            ),
            out_shape=list(out_shape) + [MARK],
            compiler_params=pltpu.CompilerParams(vmem_limit_bytes=32 * MIB),
            cost_estimate=cost(flops, read),
            name=name,
        )(*scalars, *args, *anchor)
        return results


def first_kernel(core_ref, tok_ref, gain_ref, w_ref, b_ref, cos_ref, sin_ref, h_ref, q_ref, kv_ref):
    x = to_f(tok_ref[...])
    factor = lax.rsqrt(jnp.mean(x * x, axis=-1, keepdims=True) + EPS)
    h = to_bf(x * factor * gain_ref[...])
    h_ref[...] = h
    lin = dot(h, w_ref[...]) + b_ref[...]
    cosine = cos_ref[...]
    sine = sin_ref[...]
    heads = q_ref.shape[1] // HD
    for head in range(heads):
        part = lin[:, head * HD : (head + 1) * HD]
        q_ref[:, head * HD : (head + 1) * HD] = to_bf(
            part * cosine + pltpu.roll(part, HD // 2, 1) * sine
        )
    part = lin[:, heads * HD :]
    is_key = core_ref[0] == 0
    kv_ref[...] = to_bf(
        part * jnp.where(is_key, cosine, 1.0)
        + pltpu.roll(part, HD // 2, 1) * jnp.where(is_key, sine, 0.0)
    )


def first(core, tokens, gain, weight, bias, cosine, sine):
    total, width = tokens.shape
    columns = weight.shape[1]
    block = total // 4
    half = 2

    def flip(i, core_ref):
        return (lax.rem(i + core_ref[0] * half, 4), 0)

    def at(i, core_ref):
        return (i, 0)

    def whole(i, core_ref):
        return (0, 0)

    return pl.pallas_call(
        first_kernel,
        grid_spec=pltpu.PrefetchScalarGridSpec(
            num_scalar_prefetch=1,
            grid=(4,),
            in_specs=[
                pl.BlockSpec((block, width), flip),
                pl.BlockSpec((1, width), whole),
                pl.BlockSpec((width, columns), whole),
                pl.BlockSpec((1, columns), whole),
                pl.BlockSpec((block, HD), at),
                pl.BlockSpec((block, HD), at),
            ],
            out_specs=[
                pl.BlockSpec((block, width), at),
                pl.BlockSpec((block, columns - HD), at),
                pl.BlockSpec((block, HD), at),
            ],
        ),
        out_shape=[
            jax.ShapeDtypeStruct((total, width), jnp.bfloat16),
            jax.ShapeDtypeStruct((total, columns - HD), jnp.bfloat16),
            jax.ShapeDtypeStruct((total, HD), jnp.bfloat16),
        ],
        compiler_params=pltpu.CompilerParams(vmem_limit_bytes=32 * MIB),
        cost_estimate=cost(2 * total * width * columns, 9 * MIB),
        name="first",
    )(core, tokens, gain, weight, bias, cosine, sine)


def stacked(ref, start, count, heads):
    return jnp.concatenate(
        [ref[0, pl.ds(start, count), h * HD : (h + 1) * HD] for h in range(heads)], axis=0
    )


def bounds(start_ref, index, heads, reach):
    first_key = jnp.concatenate(
        [start_ref[0, :, pl.ds(index * Q_BLOCK, Q_BLOCK)]] * heads, axis=1
    )
    place = reach + index * Q_BLOCK + lax.broadcasted_iota(jnp.int32, (1, Q_BLOCK), 1)
    return first_key, jnp.concatenate([place] * heads, axis=1)


def gather_span(core, refs, span):
    count = len(refs) // 2
    local = refs[0].shape[1]
    for i in range(count):
        here = slice(i * local, (i + 1) * local)
        span[core, here] = refs[i][0]
        span[1 - core, here] = refs[count + i][0]


def attend_kernel(heads, blocks, pieces, low_ref, core_ref, q_ref, start_ref, *refs):
    o_ref, lse_ref, acc, span = refs[2 * pieces :]
    row = pl.program_id(0)
    wide = heads * Q_BLOCK
    reach = (pieces - 1) * q_ref.shape[1]
    gather_span(core_ref[0], refs[: 2 * pieces], span)
    for index in range(blocks):
        q = stacked(q_ref, index * Q_BLOCK, Q_BLOCK, heads)
        first_key, place = bounds(start_ref, index, heads, reach)
        acc[...] = jnp.zeros_like(acc)

        def step(j, carry):
            top, total = carry
            keys = pl.ds(pl.multiple_of(j * K_BLOCK, K_BLOCK), K_BLOCK)
            s = dot(span[0, keys], q, 1, 1) * SCALE
            key = j * K_BLOCK + lax.broadcasted_iota(jnp.int32, (K_BLOCK, wide), 0)
            s = jnp.where((key >= first_key) & (key <= place), s, NEG_FILL)
            later = jnp.maximum(top, jnp.max(s, axis=0, keepdims=True))
            p = jnp.exp(s - later)
            fade = jnp.exp(top - later)
            total = total * fade + jnp.sum(p, axis=0, keepdims=True)
            acc[...] = acc[...] * fade + dot(span[1, keys], to_bf(p), 0, 0)
            return later, total

        last = (reach + (index + 1) * Q_BLOCK - 1) // K_BLOCK + 1
        top, total = lax.fori_loop(
            low_ref[row, index],
            last,
            step,
            (jnp.full((1, wide), NEG_FILL, jnp.float32), jnp.zeros((1, wide), jnp.float32)),
        )
        out = to_bf((acc[...] / total).T)
        for h in range(heads):
            o_ref[0, index * Q_BLOCK : (index + 1) * Q_BLOCK, h * HD : (h + 1) * HD] = out[
                h * Q_BLOCK : (h + 1) * Q_BLOCK
            ]
        lse_ref[0, index : index + 1, :] = top + jnp.log(total)


def span_specs(rows, local, pieces):
    near = pl.BlockSpec((1, local, HD), lambda i, *refs: (i, 0, 0))
    far = pl.BlockSpec((1, local, HD), lambda i, *refs: (lax.rem(i + rows // 2, rows), 0, 0))
    return [near] * pieces + [far] * pieces


def attend(low, core, q, start, span, mate):
    rows, local, columns = q.shape
    pieces = len(span)
    heads = columns // HD
    blocks = local // Q_BLOCK

    def at(i, *refs):
        return (i, 0, 0)

    return pl.pallas_call(
        functools.partial(attend_kernel, heads, blocks, pieces),
        grid_spec=pltpu.PrefetchScalarGridSpec(
            num_scalar_prefetch=2,
            grid=(rows,),
            in_specs=[pl.BlockSpec((1, local, columns), at), pl.BlockSpec((1, 1, local), at)]
            + span_specs(rows, local, pieces),
            out_specs=[
                pl.BlockSpec((1, local, columns), at),
                pl.BlockSpec((1, blocks, heads * Q_BLOCK), at),
            ],
            scratch_shapes=[
                pltpu.VMEM((HD, heads * Q_BLOCK), jnp.float32),
                pltpu.VMEM((2, pieces * local, HD), jnp.bfloat16),
            ],
        ),
        out_shape=[
            jax.ShapeDtypeStruct((rows, local, columns), jnp.bfloat16),
            jax.ShapeDtypeStruct((rows, blocks, heads * Q_BLOCK), jnp.float32),
        ],
        compiler_params=pltpu.CompilerParams(vmem_limit_bytes=32 * MIB),
        cost_estimate=cost(8_000_000_000, 4 * MIB),
        name="attend",
    )(low, core, q, start, *span, *mate)


def attend_back_kernel(
    heads, blocks, pieces, low_ref, core_ref, q_ref, start_ref, g_ref, o_ref, lse_ref, cos_ref, sin_ref, *refs
):
    gq_ref, keep_ref, send_ref, acc, gk, gv, span = refs[2 * pieces :]
    row = pl.program_id(0)
    wide = heads * Q_BLOCK
    reach = (pieces - 1) * q_ref.shape[1]
    core = core_ref[0]
    gather_span(core, refs[: 2 * pieces], span)
    gk[...] = jnp.zeros_like(gk)
    gv[...] = jnp.zeros_like(gv)
    for index in range(blocks):
        q = stacked(q_ref, index * Q_BLOCK, Q_BLOCK, heads)
        g = stacked(g_ref, index * Q_BLOCK, Q_BLOCK, heads)
        o = stacked(o_ref, index * Q_BLOCK, Q_BLOCK, heads)
        inner = jnp.sum((to_f(g) * to_f(o)).T, axis=0, keepdims=True)
        lse = lse_ref[0, index : index + 1, :]
        first_key, place = bounds(start_ref, index, heads, reach)
        acc[...] = jnp.zeros_like(acc)

        def step(j, carry):
            keys = pl.ds(pl.multiple_of(j * K_BLOCK, K_BLOCK), K_BLOCK)
            k = span[0, keys]
            s = dot(k, q, 1, 1) * SCALE
            key = j * K_BLOCK + lax.broadcasted_iota(jnp.int32, (K_BLOCK, wide), 0)
            p = jnp.where((key >= first_key) & (key <= place), jnp.exp(s - lse), 0.0)
            gp = dot(span[1, keys], g, 1, 1)
            gs = to_bf(p * (gp - inner))
            gv[keys] += dot(to_bf(p), g)
            gk[keys] += dot(gs, q)
            acc[...] += dot(k, gs, 0, 0)
            return carry

        last = (reach + (index + 1) * Q_BLOCK - 1) // K_BLOCK + 1
        lax.fori_loop(low_ref[row, index], last, step, 0)
        gq = acc[...].T * SCALE
        here = slice(index * Q_BLOCK, (index + 1) * Q_BLOCK)
        cosine, sine = cos_ref[here], sin_ref[here]
        for h in range(heads):
            part = gq[h * Q_BLOCK : (h + 1) * Q_BLOCK]
            gq_ref[0, here, h * HD : (h + 1) * HD] = to_bf(
                part * cosine + pltpu.roll(part * sine, HD // 2, 1)
            )
    is_key = core == 0
    keys, values = gk[...] * SCALE, gv[...]
    keep_ref[0] = to_bf(jnp.where(is_key, keys, values))
    send_ref[0] = to_bf(jnp.where(is_key, values, keys))


def attend_back(order, low, core, q, start, span, mate, grad, out, lse, cosine, sine):
    rows, local, columns = q.shape
    pieces = len(span)
    window = pieces * local
    heads = columns // HD
    blocks = local // Q_BLOCK

    def at(i, *refs):
        return (i, 0, 0)

    table = pl.BlockSpec((local, HD), lambda i, *refs: (i, 0))
    tokens = pl.BlockSpec((1, local, columns), at)
    return order(
        functools.partial(attend_back_kernel, heads, blocks, pieces),
        [q, start, grad, out, lse, cosine, sine, *span, *mate],
        [
            tokens,
            pl.BlockSpec((1, 1, local), at),
            tokens,
            tokens,
            pl.BlockSpec((1, blocks, heads * Q_BLOCK), at),
            table,
            table,
        ]
        + span_specs(rows, local, pieces),
        [tokens, pl.BlockSpec((1, window, HD), at), pl.BlockSpec((1, window, HD), at)],
        [
            jax.ShapeDtypeStruct((rows, local, columns), jnp.bfloat16),
            jax.ShapeDtypeStruct((rows, window, HD), jnp.bfloat16),
            jax.ShapeDtypeStruct((rows, window, HD), jnp.bfloat16),
        ],
        (rows,),
        20_000_000_000,
        6 * MIB,
        "attend_back",
        scalars=(low, core),
        scratch=[
            pltpu.VMEM((HD, heads * Q_BLOCK), jnp.float32),
            pltpu.VMEM((window, HD), jnp.float32),
            pltpu.VMEM((window, HD), jnp.float32),
            pltpu.VMEM((2, window, HD), jnp.bfloat16),
        ],
    )


def fold_kernel(keep_ref, come_ref, own_ref, *send_refs):
    local = own_ref.shape[1]
    total = to_f(keep_ref[0]) + to_f(come_ref[0])
    reach = total.shape[0] - local
    own_ref[0] = total[reach:]
    for hop, ref in enumerate(send_refs, 1):
        ref[0] = to_bf(total[reach - hop * local : reach - (hop - 1) * local])


def fold(order, keep, come, local):
    rows, window = keep.shape[:2]
    hops = window // local - 1
    out = pl.BlockSpec((1, local, HD), lambda i: (i, 0, 0))
    return order(
        fold_kernel,
        [keep, come],
        [
            pl.BlockSpec((1, window, HD), lambda i: (i, 0, 0)),
            pl.BlockSpec((1, window, HD), lambda i: (lax.rem(i + rows // 2, rows), 0, 0)),
        ],
        [out] * (hops + 1),
        [jax.ShapeDtypeStruct((rows, local, HD), jnp.float32)]
        + [jax.ShapeDtypeStruct((rows, local, HD), jnp.bfloat16)] * hops,
        (rows,),
        0,
        4 * MIB,
        "fold",
    )


def carry_kernel(piece_ref, come_ref, out_ref):
    out_ref[...] = to_bf(to_f(piece_ref[...]) + to_f(come_ref[...]))


def carry(order, piece, come):
    rows, local, columns = piece.shape
    at = pl.BlockSpec((1, local, columns), lambda i: (i, 0, 0))
    return order(
        carry_kernel,
        [piece, come],
        [at, at],
        [at],
        [jax.ShapeDtypeStruct(piece.shape, jnp.bfloat16)],
        (rows,),
        0,
        2 * MIB,
        "carry",
    )[0]


def bias_kernel(left_ref, right_ref, out_ref):
    out_ref[...] = left_ref[...] + right_ref[...]


def bias_add(order, left, right):
    whole = pl.BlockSpec(left.shape, lambda i: (0, 0))
    return order(
        bias_kernel,
        [left, right],
        [whole, whole],
        [whole],
        [jax.ShapeDtypeStruct(left.shape, jnp.float32)],
        (1,),
        0,
        MIB,
        "bias",
    )[0]


def join_kernel(hops, core_ref, gq_ref, cos_ref, sin_ref, own_ref, *refs):
    out_ref, sum_ref = refs[-2:]
    columns = gq_ref.shape[2]
    grad = own_ref[0]
    for ref in refs[:hops]:
        grad = grad + to_f(ref[0])
    is_key = core_ref[0] == 0
    cosine = jnp.where(is_key, cos_ref[...], 1.0)
    sine = jnp.where(is_key, sin_ref[...], 0.0)
    kv = to_bf(grad * cosine + pltpu.roll(grad * sine, HD // 2, 1))
    q = gq_ref[0]
    out_ref[:, :columns] = q
    out_ref[:, columns:] = kv

    @pl.when(pl.program_id(0) == 0)
    def _():
        sum_ref[...] = jnp.zeros(sum_ref.shape, jnp.float32)

    sum_ref[:, :columns] += jnp.sum(to_f(q), axis=0, keepdims=True)
    sum_ref[:, columns:] += jnp.sum(to_f(kv), axis=0, keepdims=True)


def join(order, core, grad_q, own, comes, cosine, sine):
    rows, local, columns = grad_q.shape
    wide = columns + HD

    def at(i, *refs):
        return (i, 0, 0)

    piece = pl.BlockSpec((1, local, HD), at)
    table = pl.BlockSpec((local, HD), lambda i, *refs: (i, 0))
    return order(
        functools.partial(join_kernel, len(comes)),
        [grad_q, cosine, sine, own, *comes],
        [pl.BlockSpec((1, local, columns), at), table, table, piece] + [piece] * len(comes),
        [
            pl.BlockSpec((local, wide), lambda i, *refs: (i, 0)),
            pl.BlockSpec((8, wide), lambda i, *refs: (0, 0)),
        ],
        [
            jax.ShapeDtypeStruct((rows * local, wide), jnp.bfloat16),
            jax.ShapeDtypeStruct((8, wide), jnp.float32),
        ],
        (rows,),
        0,
        4 * MIB,
        "join",
        scalars=(core,),
    )


def mixed_back_kernel(w_ref, *refs):
    rows = refs[0].shape[0]
    for i, ref in enumerate(refs[:-1]):
        refs[-1][i * rows : (i + 1) * rows] = to_bf(dot(ref[...], w_ref[...]))


def mixed_back(order, pieces, weight):
    rows, width = pieces[0].shape
    total = rows * len(pieces)
    columns = weight.shape[1]

    def whole(i):
        return (0, 0)

    return order(
        mixed_back_kernel,
        [weight, *pieces],
        [pl.BlockSpec((width, columns), whole)] + [pl.BlockSpec((rows, width), whole)] * len(pieces),
        [pl.BlockSpec((total, columns), whole)],
        [jax.ShapeDtypeStruct((total, columns), jnp.bfloat16)],
        (1,),
        2 * total * width * columns,
        6 * MIB,
        "mixed_back",
    )[0]


def place_kernel(core_ref, *refs):
    for i, ref in enumerate(refs[:-1]):

        @pl.when(pl.program_id(0) == i)
        def _(ref=ref):
            refs[-1][...] = ref[...]


def place(order, core, pieces):
    rows, width = pieces[0].shape
    count = len(pieces)
    return order(
        place_kernel,
        list(pieces),
        [pl.BlockSpec((rows, width), lambda i, core_ref: (0, 0))] * count,
        [pl.BlockSpec((rows, width), lambda i, core_ref: (lax.rem(i + core_ref[0] * (count // 2), count), 0))],
        [jax.ShapeDtypeStruct((rows * count, width), pieces[0].dtype)],
        (count,),
        0,
        8 * rows * width,
        "place",
        scalars=(core,),
    )[0]


def anchors(count):
    return [pl.BlockSpec(memory_space=pl.ANY)] * count


MARK = jax.ShapeDtypeStruct((8, HD), jnp.float32)


def mark_spec():
    return pl.BlockSpec((8, HD), lambda *refs: (0, 0))


def grad_hidden_kernel(g_ref, w_ref, out_ref):
    out_ref[...] = to_bf(dot(g_ref[...], w_ref[...], 1, 1))


def grad_hidden_of(order, grad, weight):
    total, width = grad.shape
    hidden = weight.shape[0]
    return order(
        grad_hidden_kernel,
        [grad, weight],
        [pl.BlockSpec((total, width), lambda i: (0, 0)), pl.BlockSpec((TILE, width), lambda i: (i, 0))],
        [pl.BlockSpec((total, TILE), lambda i: (0, i))],
        [jax.ShapeDtypeStruct((total, hidden), jnp.bfloat16)],
        (pl.cdiv(hidden, TILE),),
        2 * total * width * hidden,
        15 * MIB,
        "grad_hidden",
    )[0]


def gated_kernel(gh_ref, gw_ref, uw_ref, *refs):
    hid_ref, gg_ref, gu_ref = refs[-3:]
    rows = refs[0].shape[0]
    for part, ref in enumerate(refs[:-3]):
        here = slice(part * rows, (part + 1) * rows)
        h = ref[...]
        gate = dot(h, gw_ref[...], 1, 1)
        up = dot(h, uw_ref[...], 1, 1)
        grad = to_f(gh_ref[here])
        sigma = 1.0 / (1.0 + jnp.exp(-gate))
        swish = gate * sigma
        hid_ref[here] = to_bf(swish * up)
        gu_ref[here] = to_bf(grad * swish)
        gg_ref[here] = to_bf(grad * up * sigma * (1.0 + gate * (1.0 - sigma)))


def gated(order, pieces, grad_hidden, gate_weight, up_weight):
    rows, width = pieces[0].shape
    total = rows * len(pieces)
    hidden = gate_weight.shape[0]
    column = pl.BlockSpec((total, TILE), lambda i: (0, i))
    weight = pl.BlockSpec((TILE, width), lambda i: (i, 0))
    shape = jax.ShapeDtypeStruct((total, hidden), jnp.bfloat16)
    return order(
        gated_kernel,
        [grad_hidden, gate_weight, up_weight, *pieces],
        [column, weight, weight] + [pl.BlockSpec((rows, width), lambda i: (0, 0))] * len(pieces),
        [column] * 3,
        [shape] * 3,
        (pl.cdiv(hidden, TILE),),
        4 * total * width * hidden,
        30 * MIB,
        "gated",
    )


def share_kernel(plan, lefts, rights, extra, halves, groups, pick_ref, blocks_ref, *refs):
    step = pl.program_id(0)
    left_refs, right_refs = refs[:lefts], refs[lefts : lefts + rights]
    refs = refs[lefts + rights :]
    if extra:
        extra_ref, refs = refs[0], refs[1:]
    for left, right, begin, end, shift, columns, target in plan:

        @pl.when((step >= begin) & (step < end))
        def _(left=left, right=right, shift=shift, columns=columns, target=target):
            out = dot(left_refs[left][...], right_refs[right][...])
            if extra:
                out = out + to_f(extra_ref[...])
            tile = out.shape[1]
            spot = (step + shift) * tile + lax.broadcasted_iota(jnp.int32, (1, tile), 1)
            out = to_bf(jnp.where(spot < columns, out, 0.0))
            if groups:
                share = out.shape[0] // (groups[0] * groups[1])
                for i in range(groups[0]):
                    for j in range(groups[1]):
                        here = (j * groups[0] + i) * share
                        there = (i * groups[1] + j) * share
                        refs[target][here : here + share] = out[there : there + share]
                return
            if not halves:
                refs[target][...] = out
                return
            send_ref, keep_ref, rows = refs
            rows[...] = out
            share = send_ref.shape[0] // (2 * halves)
            for i in range(2 * halves):
                here = slice(i * share, (i + 1) * share)
                send_ref[here] = rows[pl.ds(pl.multiple_of(blocks_ref[i] * share, share), share)]
                keep_ref[here] = rows[pl.ds(pl.multiple_of(blocks_ref[2 * halves + i] * share, share), share)]


def clipped(rows, tile, begin, count, shift=0):
    return pl.BlockSpec((rows, tile), lambda i, *refs: (0, jnp.clip(i - begin, 0, count - 1) + shift))


def share_of(order, lefts, rights, parts, part, pick, tile, extra=None, blocks=None, groups=None):
    tokens = lefts[0].shape[1]
    plan, at = [], 0
    starts, sizes, right_at = {}, {}, {}
    for left, right, skip, count, target in parts:
        plan.append((left, right, at, at + count, skip - at, rights[right].shape[1], target))
        starts.setdefault(target, at)
        sizes[target] = sizes.get(target, 0) + count
        first, tiles, low = right_at.get(right, (at, 0, skip))
        right_at[right] = (first, tiles + count, low)
        at += count
    halves = 0
    extras = [] if extra is None else [extra]
    scratch = []
    if blocks is None:
        blocks = jnp.zeros((1,), jnp.int32)
        outs = [clipped(part, tile, starts[t], sizes[t]) for t in sorted(sizes)]
        shapes = [jax.ShapeDtypeStruct((part, sizes[t] * tile), jnp.bfloat16) for t in sorted(sizes)]
    else:
        halves = blocks.shape[0] // 4
        outs = [clipped(part // 2, tile, 0, at)] * 2
        shapes = [jax.ShapeDtypeStruct((part // 2, at * tile), jnp.bfloat16)] * 2
        scratch = [pltpu.VMEM((part, tile), jnp.bfloat16)]
    return order(
        functools.partial(share_kernel, plan, len(lefts), len(rights), len(extras), halves, groups),
        [*lefts, *rights, *extras],
        [pl.BlockSpec((part, tokens), lambda i, pick_ref, blocks_ref: (pick_ref[0], 0))] * len(lefts)
        + [clipped(tokens, tile, *right_at[r]) for r in range(len(rights))]
        + [clipped(part, tile, 0, at)] * len(extras),
        outs,
        shapes,
        (at,),
        2 * part * tokens * at * tile,
        2 * (part * tokens + (part + tokens) * at * tile),
        "share",
        scalars=(jnp.asarray(pick, jnp.int32).reshape(1), blocks),
        scratch=scratch,
    )


def relay_kernel(keep_ref, come_ref, out_ref):
    out_ref[...] = to_bf(to_f(keep_ref[...]) + to_f(come_ref[...]))


def relay(order, keep, come, share):
    rows, columns = keep.shape
    pair = pl.BlockSpec((share, columns), lambda i: (2 * i + 1, 0))
    return order(
        relay_kernel,
        [keep, come],
        [pair, pair],
        [pl.BlockSpec((share, columns), lambda i: (i, 0))],
        [jax.ShapeDtypeStruct((rows // 2, columns), jnp.bfloat16)],
        (rows // (2 * share),),
        0,
        3 * rows * columns,
        "relay",
    )[0]


def finish_kernel(plan, columns, gains, *refs):
    out_ref = refs[-2] if gains else refs[-1]
    step = pl.program_id(0)
    tile = out_ref.shape[1]
    for begin, end, first, count in plan:

        @pl.when((step >= begin) & (step < end))
        def _(first=first, count=count):
            out = to_f(refs[first][...])
            for ref in refs[first + 1 : first + count]:
                out = out + to_f(ref[...])
            out_ref[...] = out
            if gains:
                spot = step * tile + lax.broadcasted_iota(jnp.int32, (1, tile), 1)
                terms = jnp.where(spot < columns, out * to_f(refs[-3][...]), 0.0)
                total = terms[:, :HD]
                for i in range(HD, tile, HD):
                    total = total + terms[:, i : i + HD]

                @pl.when(step == 0)
                def _():
                    refs[-1][...] = total

                @pl.when(step > 0)
                def _():
                    refs[-1][...] += total


def finish(order, chunks, share, columns, tile, weight=None):
    plan, specs, args, at = [], [], [], 0
    for chunk in chunks:
        count = chunk[0].shape[1] // tile
        plan.append((at, at + count, len(args), len(chunk)))
        specs += [clipped(share, tile, at, count)] * len(chunk)
        args += chunk
        at += count
    column = pl.BlockSpec((share, tile), lambda i: (0, i))
    outs, shapes = [column], [jax.ShapeDtypeStruct((share, columns), jnp.float32)]
    if weight is not None:
        args.append(weight)
        specs.append(column)
        outs.append(pl.BlockSpec((share, HD), lambda i: (0, 0)))
        shapes.append(jax.ShapeDtypeStruct((share, HD), jnp.float32))
    return order(
        functools.partial(finish_kernel, plan, columns, weight is not None),
        args,
        specs,
        outs,
        shapes,
        (at,),
        0,
        14 * share * columns,
        "finish",
    )


def narrow_kernel(pairs, extras, right_dim, *refs):
    out = dot(refs[0][...], refs[1][...], 1, right_dim)
    for i in range(1, pairs):
        out = out + dot(refs[2 * i][...], refs[2 * i + 1][...], 1, right_dim)
    extra = refs[2 * pairs : 2 * pairs + extras]
    outs = refs[2 * pairs + extras :]
    if extras:
        out = out + jnp.concatenate([to_f(ref[...]) for ref in extra], axis=0)
    rows = outs[0].shape[0]
    for i, ref in enumerate(outs):
        ref[...] = to_bf(out[i * rows : (i + 1) * rows])


def narrow(order, pairs, index, extra=(), right_dim=0):
    total, hidden = pairs[0][0].shape
    width = pairs[0][1].shape[1 - right_dim]
    half = total // 2
    piece = half // PIECES
    column = pl.BlockSpec((piece, TILE), lambda i: (0, i))
    right = (
        pl.BlockSpec((TILE, hidden), lambda i: (i, 0))
        if right_dim
        else pl.BlockSpec((hidden, TILE), lambda i: (0, i))
    )
    return order(
        functools.partial(narrow_kernel, len(pairs), len(extra), right_dim),
        [item for pair in pairs for item in pair] + list(extra),
        [pl.BlockSpec((half, hidden), lambda i: (index, 0)), right] * len(pairs) + [column] * len(extra),
        [column] * PIECES,
        [jax.ShapeDtypeStruct((piece, width), jnp.bfloat16)] * PIECES,
        (width // TILE,),
        2 * len(pairs) * half * width * hidden,
        2 * len(pairs) * (half + width) * hidden + 2 * half * width,
        "narrow",
    )


def piece_specs(piece, width, block):
    steps = piece // block
    return [
        pl.BlockSpec((block, width), lambda i, *refs, j=j: (jnp.clip(i - j * steps, 0, steps - 1), 0))
        for j in range(PIECES)
    ]


def pick_piece(refs):
    value = refs[0][...]
    for j, ref in enumerate(refs[1:], 1):
        value = jnp.where(pl.program_id(0) >= 4 * j // len(refs), ref[...], value)
    return value


def put_piece(refs, value):
    steps = 4 // len(refs)
    for j, ref in enumerate(refs):

        @pl.when(lax.div(pl.program_id(0), steps) == j)
        def _(ref=ref):
            ref[...] = value


def turn_kernel(*refs):
    rows = refs[0].shape[0]
    for i, ref in enumerate(refs[:-1]):
        refs[-1][:, i * rows : (i + 1) * rows] = ref[...].T


def turn(order, pieces):
    rows, width = pieces[0].shape
    total = rows * len(pieces)
    return order(
        turn_kernel,
        list(pieces),
        [pl.BlockSpec((rows, TILE), lambda i: (0, i))] * len(pieces),
        [pl.BlockSpec((TILE, total), lambda i: (i, 0))],
        [jax.ShapeDtypeStruct((width, total), jnp.bfloat16)],
        (width // TILE,),
        0,
        4 * total * width,
        "turn",
    )[0]


def grad_out_kernel(core_ref, cot_ref, valid_ref, out_ref, turned_ref):
    out = to_bf(to_f(cot_ref[...]) * valid_ref[...])
    out_ref[...] = out
    turned_ref[...] = out.T


def grad_out_of(order, core, cotangent, valid):
    total, width = cotangent.shape
    block = total // 4
    return order(
        grad_out_kernel,
        [cotangent, valid],
        [
            pl.BlockSpec((block, width), lambda i, core_ref: (lax.rem(i + core_ref[0] * 2, 4), 0)),
            pl.BlockSpec((block, 1), lambda i, core_ref: (i, 0)),
        ],
        [
            pl.BlockSpec((block, width), lambda i, core_ref: (i, 0)),
            pl.BlockSpec((width, block), lambda i, core_ref: (0, i)),
        ],
        [
            jax.ShapeDtypeStruct((total, width), jnp.bfloat16),
            jax.ShapeDtypeStruct((width, total), jnp.bfloat16),
        ],
        (4,),
        0,
        6 * total * width,
        "grad_out",
        scalars=(core,),
    )


def middle_kernel(core_ref, tok_ref, gain_ref, *refs):
    mine, come = pick_piece(refs[:PIECES]), pick_piece(refs[PIECES : 2 * PIECES])
    mid_ref, *h_refs = refs[2 * PIECES :]
    middle = to_f(tok_ref[...]) + (to_f(mine) + to_f(come))
    factor = lax.rsqrt(jnp.mean(middle * middle, axis=-1, keepdims=True) + EPS)
    mid_ref[...] = middle
    put_piece(h_refs, to_bf(middle * factor * gain_ref[...]))


def middle_of(order, core, tokens, mine, come, gain):
    piece, width = mine[0].shape
    half = piece * PIECES
    block = half // 4
    specs = piece_specs(piece, width, block)
    middle, *h = order(
        middle_kernel,
        [tokens, gain, *mine, *come],
        [
            pl.BlockSpec((block, width), lambda i, core_ref: (core_ref[0] * 4 + i, 0)),
            pl.BlockSpec((1, width), lambda i, core_ref: (0, 0)),
        ]
        + specs * 2,
        [pl.BlockSpec((block, width), lambda i, core_ref: (i, 0))] + specs,
        [jax.ShapeDtypeStruct((half, width), jnp.float32)]
        + [jax.ShapeDtypeStruct((piece, width), jnp.bfloat16)] * PIECES,
        (4,),
        0,
        9 * MIB,
        "middle",
        scalars=(core,),
    )
    return middle, h


def norm_back_kernel(core_ref, x_ref, gain_ref, up_ref, *refs):
    mine, come = pick_piece(refs[:PIECES]), pick_piece(refs[PIECES : 2 * PIECES])
    outs = refs[2 * PIECES :]
    grad = to_f(mine) + to_f(come)
    x = to_f(x_ref[...])
    factor = lax.rsqrt(jnp.mean(x * x, axis=-1, keepdims=True) + EPS)
    normed = x * factor
    weighted = grad * gain_ref[...]
    inner = jnp.mean(weighted * normed, axis=-1, keepdims=True)
    out = to_f(up_ref[...]) + factor * (weighted - normed * inner)
    if len(outs) > PIECES:
        outs[0][...] = out
        put_piece(outs[1:], to_bf(out))
    else:
        put_piece(outs, out)


def norm_back(order, core, mine, come, x, gain, up, by_core):
    piece, width = mine[0].shape
    half = piece * PIECES
    block = half // 4
    at = pl.BlockSpec((block, width), lambda i, core_ref: (i, 0))
    picked = pl.BlockSpec((block, width), lambda i, core_ref: (core_ref[0] * 4 + i, 0))
    specs = piece_specs(piece, width, block)
    if by_core:
        shapes = [jax.ShapeDtypeStruct((piece, width), jnp.float32)] * PIECES
    else:
        shapes = [jax.ShapeDtypeStruct((half, width), jnp.float32)]
        shapes += [jax.ShapeDtypeStruct((piece, width), jnp.bfloat16)] * PIECES
    return order(
        norm_back_kernel,
        [x, gain, up, *mine, *come],
        [picked if by_core else at, pl.BlockSpec((1, width), lambda i, core_ref: (0, 0)), at] + specs * 2,
        specs if by_core else [at] + specs,
        shapes,
        (4,),
        0,
        10 * MIB,
        "norm_back",
        scalars=(core,),
    )


def layer_kernel(middle_ref, *refs):
    mine, come = pick_piece(refs[:PIECES]), pick_piece(refs[PIECES : 2 * PIECES])
    put_piece(refs[2 * PIECES :], to_bf(middle_ref[...] + (to_f(mine) + to_f(come))))


def layer_of(order, middle, mine, come):
    piece, width = mine[0].shape
    block = piece * PIECES // 4
    specs = piece_specs(piece, width, block)
    return order(
        layer_kernel,
        [middle, *mine, *come],
        [pl.BlockSpec((block, width), lambda i: (i, 0))] + specs * 2,
        specs,
        [jax.ShapeDtypeStruct((piece, width), jnp.bfloat16)] * PIECES,
        (4,),
        0,
        5 * MIB,
        "layer",
    )


def tensor_gather(value, rank):
    mate = core_swap(value)
    pair = jnp.where(lax.rem(rank, 2) == 0, jnp.stack([value, mate]), jnp.stack([mate, value]))
    come = chip_swap(pair)
    return jnp.where(
        lax.div(rank, 2) == 0,
        jnp.concatenate([pair, come], axis=0),
        jnp.concatenate([come, pair], axis=0),
    )


def body(
    tokens,
    lengths,
    cotangent,
    q_weight,
    q_bias,
    k_weight,
    k_bias,
    v_weight,
    v_bias,
    o_weight,
    attn_gain,
    ffn_gain,
    gate_weight,
    up_weight,
    down_weight,
):
    rows, local, width = tokens.shape
    total = rows * local
    half = total // 2
    heads = q_weight.shape[1] // HD
    ranks = lax.axis_size("tensor")
    seqs = lax.axis_size("seq")
    rank = lax.axis_index("tensor")
    dp_index = lax.axis_index("dp")
    seq_index = lax.axis_index("seq")
    core = lax.rem(rank, 2)
    head = lax.div(rank, 2)
    core_one = core.reshape(1)
    hops = min(seqs - 1, -(-(MOST - 1) // local))
    reach = hops * local

    def own_first(value):
        turned = jnp.concatenate([value[rows // 2 :], value[: rows // 2]], axis=0)
        return jnp.where(core == 0, value, turned)

    slots = jnp.arange(lengths.shape[1], dtype=jnp.int32)
    lens = own_first(lengths)
    ends = jnp.sum(jnp.where(slots[None, :] <= slots[:, None], lens[:, None, :], 0), axis=2)
    spot = seq_index * local + jnp.arange(local, dtype=jnp.int32)
    begun = jnp.max(
        jnp.where(ends[:, None, :] <= spot[None, :, None], ends[:, None, :], 0), axis=2
    )
    valid = to_f(spot[None, :] < ends[:, -2:-1])
    position = (spot[None, :] - begun).reshape(total, 1)
    freqs = ROPE_BASE ** (-(jnp.arange(HD // 2, dtype=jnp.float32) * 2.0) / HD)
    angles = to_f(position) * freqs[None, :]
    cosine, sine = jnp.cos(angles), jnp.sin(angles)
    cosine = jnp.concatenate([cosine, cosine], axis=1)
    sine = jnp.concatenate([-sine, sine], axis=1)
    start = begun - (seq_index * local - reach)
    low = jnp.maximum(lax.div(jnp.maximum(start[:, ::Q_BLOCK], 0), K_BLOCK), 0)
    start = start.reshape(rows, 1, local)

    key_side = core == 0
    kv_weight = jnp.where(
        key_side,
        lax.dynamic_slice_in_dim(k_weight, head * HD, HD, 1),
        lax.dynamic_slice_in_dim(v_weight, head * HD, HD, 1),
    )
    kv_bias = jnp.where(
        key_side,
        lax.dynamic_slice_in_dim(k_bias, head * HD, HD, 0),
        lax.dynamic_slice_in_dim(v_bias, head * HD, HD, 0),
    )
    weight = jnp.concatenate([q_weight, kv_weight], axis=1)
    bias = to_f(jnp.concatenate([q_bias, kv_bias])).reshape(1, -1)
    gain_one = to_f(attn_gain).reshape(1, width)
    gain_two = to_f(ffn_gain).reshape(1, width)

    h_one, q_rot, kv = first(
        core_one, tokens.reshape(total, width), gain_one, weight, bias, cosine, sine
    )
    kv = kv.reshape(rows, local, HD)
    span = [shifted(kv, h) for h in range(hops, 0, -1)] + [kv]
    mate = [core_swap(piece) for piece in span]
    q_rows = q_rot.reshape(rows, local, heads * HD)
    mixed_rows, lse = attend(low, core_one, q_rows, start, span, mate)
    mixed = mixed_rows.reshape(total, heads * HD)

    order = Order()
    flat_tokens = tokens.reshape(total, width)
    dps = lax.axis_size("dp")
    near_pair = dps == 2 and seqs == 4
    part = width // dps
    share = part // seqs
    gate_t, up_t, down_t = gate_weight.T, up_weight.T, down_weight.T
    units = gate_t.shape[0]
    tiles = -(-units // TILE)
    cut = (tiles + 1) // 2
    long = max(tiles - 2, 1)
    one, two = seq_index ^ 1, seq_index ^ 2
    three = seq_index ^ 3
    quad = jnp.stack([one, three, seq_index, two])

    begin = (dp_index * seqs + seq_index) * share

    def rows_of(value):
        return lax.dynamic_slice_in_dim(value, begin, share, 0)

    class Rows:
        def __init__(self, lefts, rights, parts, tile=TILE, sent=None):
            self.args = (order, lefts, rights, parts)
            self.tile = tile
            if not near_pair:
                (whole,) = share_of(*self.args, width, 0, tile)
                self.whole = lax.psum_scatter(whole, ("dp", "seq"), scatter_dimension=0, tiled=True)
                return
            if sent is None:
                (sent,) = share_of(*self.args, part, 1 - dp_index, tile)
            self.come = lax.ppermute(sent, "dp", flipped("dp", 0))

        def own(self):
            if near_pair:
                send, self.keep = share_of(*self.args, part, dp_index, self.tile, self.come, quad)
                self.come = lax.ppermute(send, "seq", flipped("seq", 0))

        def relay(self):
            if near_pair:
                sent = relay(order, self.keep, self.come, share)
                self.last = lax.ppermute(sent, "seq", flipped("seq", 1))

        def settled(self):
            if near_pair:
                order.arrived(self.last)

        def result(self):
            return [self.keep, self.come, self.last] if near_pair else [self.whole]

    class SeqFirst(Rows):
        def __init__(self, lefts, rights, parts, tile=TILE):
            if not near_pair:
                super().__init__(lefts, rights, parts, tile)
                return
            (whole,) = share_of(order, lefts, rights, parts, width, 0, tile, None, None, (dps, seqs))
            self.mine = lax.psum_scatter(whole, "seq", scatter_dimension=0, tiled=True)

        def across(self):
            if near_pair:
                sent = lax.dynamic_slice_in_dim(self.mine, (1 - dp_index) * share, share, 0)
                self.mine = lax.dynamic_slice_in_dim(self.mine, dp_index * share, share, 0)
                order.arrived(sent, self.mine)
                self.come = lax.ppermute(sent, "dp", flipped("dp", 0))

        def settled(self):
            if near_pair:
                order.arrived(self.come)

        def result(self):
            return [self.mine, self.come] if near_pair else [self.whole]

    class Scattered(Rows):
        def own(self):
            if near_pair:
                (mine,) = share_of(*self.args, part, dp_index, self.tile, self.come)
                self.whole = lax.psum_scatter(mine, "seq", scatter_dimension=0, tiled=True)

        def settled(self):
            order.arrived(self.whole)

        def result(self):
            return [self.whole]

    sent = core_swaps(narrow(order, [(mixed, o_weight)], 1, (), 1))
    mine = narrow(order, [(mixed, o_weight)], 0, sent, 1)
    come = chip_swaps(mine)
    grad_ffn, grad_ffn_t = grad_out_of(
        order, core_one, cotangent.reshape(total, width), valid.reshape(total, 1)
    )
    gate_rows, up_rows = rows_of(gate_weight), rows_of(up_weight)
    order.arrived(gate_rows, up_rows)
    grad_hidden = grad_hidden_of(order, grad_ffn, down_t)
    h_one_t = turn(order, [h_one])
    middle, h_two = middle_of(order, core_one, flat_tokens, mine, come, gain_two)
    h_two += core_swaps(h_two)
    hidden, grad_gate, grad_up = gated(order, h_two, grad_hidden, gate_t, up_t)

    down_b = SeqFirst([grad_ffn_t], [hidden], [(0, 0, cut, tiles - cut, 0)])
    down_a = Rows([grad_ffn_t], [hidden], [(0, 0, 0, cut, 0)])
    pairs = [(grad_gate, gate_t), (grad_up, up_t)]
    sent = core_swaps(narrow(order, pairs, 1))
    mine = narrow(order, pairs, 0, sent)
    come = chip_swaps(mine)
    h_two_t = turn(order, h_two)
    if near_pair:
        sends = share_of(
            order,
            [h_two_t],
            [grad_gate, grad_up],
            [(0, 0, 0, tiles, 0), (0, 1, 0, long, 1), (0, 1, long, tiles - long, 2)],
            part,
            1 - dp_index,
            TILE,
        )
    else:
        sends = [None] * 3

    def half_rows(kind, right, begin, end, sent):
        return kind([h_two_t], [right], [(0, 0, begin, end - begin, 0)], TILE, sent)

    gate = half_rows(Scattered, grad_gate, 0, tiles, sends[0])
    up_a = half_rows(Rows, grad_up, 0, long, sends[1])
    up_b = half_rows(Rows, grad_up, long, tiles, sends[2])
    down_a.own()
    grad_middle, *branch = norm_back(order, core_one, mine, come, middle, gain_two, grad_ffn, False)
    branch += core_swaps(branch)
    grad_mixed = mixed_back(order, branch, o_weight).reshape(rows, local, heads * HD)
    grad_q_rows, keep, sent = attend_back(
        order, low, core_one, q_rows, start, span, mate, grad_mixed, mixed_rows, lse, cosine, sine
    )
    both_come = core_swap(sent)
    branch_t = turn(order, branch)
    down_a.relay()
    own_kv, *pieces = fold(order, keep, both_come, local)
    moving = shifted(pieces[-1], -1) if pieces else None
    ffn_sent = core_swaps(narrow(order, [(hidden, down_t)], 1))
    for piece in pieces[-2::-1]:
        moving = shifted(carry(order, piece, moving), -1)
    grad_qkv, bias_sum = join(
        order, core_one, grad_q_rows, own_kv, [] if moving is None else [moving], cosine, sine
    )
    sent = core_swaps(narrow(order, [(grad_qkv, weight)], 1, (), 1))
    down_b.across()
    mine = narrow(order, [(grad_qkv, weight)], 0, sent, 1)
    come = chip_swaps(mine)
    gate.own()
    last_parts = [(0, 0, 0, grad_qkv.shape[1] // HD, 0), (1, 1, 0, heads, 0)]
    last = Rows([h_one_t, branch_t], [grad_qkv, mixed], last_parts, HD)
    ffn_mine = narrow(order, [(hidden, down_t)], 0, ffn_sent)
    down_a.settled()
    token = norm_back(order, core_one, mine, come, flat_tokens, gain_one, grad_middle, True)
    token += core_swaps(token)
    ffn_come = chip_swaps(ffn_mine)
    up_a.own()
    token_grad = place(order, core_one, token).reshape(rows, local, width)
    layer = layer_of(order, middle, ffn_mine, ffn_come)
    layer += core_swaps(layer)
    last.own()
    layer_out = place(order, core_one, layer).reshape(rows, local, width)
    up_a.relay()
    up_b.own()
    last.relay()
    if near_pair:
        bias_come = lax.ppermute(bias_sum, "dp", flipped("dp", 0))
        bias_all = bias_add(order, bias_sum, bias_come)
        bias_come = lax.ppermute(bias_all, "seq", flipped("seq", 0))
    up_a.settled()
    up_b.relay()
    (down_grad,) = finish(order, [down_a.result(), down_b.result()], share, units, TILE)
    gate_grad, gate_term = finish(order, [gate.result()], share, units, TILE, gate_rows)
    wide_columns = grad_qkv.shape[1]
    (last_grad,) = finish(order, [last.result()], share, wide_columns + heads * HD, HD)
    if near_pair:
        bias_all = bias_add(order, bias_all, bias_come)
        bias_come = lax.ppermute(bias_all, "seq", flipped("seq", 1))
        bias_all = (bias_all + bias_come)[:1]
    else:
        bias_all = lax.psum(bias_sum[:1], ("dp", "seq"))
    up_grad, up_term = finish(order, [up_a.result(), up_b.result()], share, units, TILE, up_rows)
    qkv_grad, o_grad = last_grad[:, :wide_columns], last_grad[:, wide_columns:]

    attn_term = jnp.sum(to_f(rows_of(weight)) * qkv_grad, axis=1)
    ffn_term = jnp.sum(gate_term + up_term, axis=1)
    columns = heads * HD
    room = -(-share // HD) * HD - share
    terms = jnp.pad(jnp.stack([ffn_term, attn_term]), ((0, 0), (0, room))).reshape(-1, HD)
    packed = jnp.concatenate([qkv_grad[:, columns:], bias_all.reshape(-1, HD), terms], axis=0)
    gathered = tensor_gather(packed, rank)
    term_rows = terms.shape[0]
    bias_count = bias_all.shape[1] // HD
    terms = gathered[:, share + bias_count :].reshape(ranks, 2, -1)[:, :, :share]
    ffn_gain_grad, attn_gain_grad = terms[0] + terms[1] + (terms[2] + terms[3])
    attn_gain_grad = attn_gain_grad / lax.dynamic_slice_in_dim(gain_one[0], begin, share, 0)
    ffn_gain_grad = ffn_gain_grad / lax.dynamic_slice_in_dim(gain_two[0], begin, share, 0)
    q_grad = qkv_grad[:, :columns]
    kv_parts = lax.dynamic_slice_in_dim(gathered, rank * (share // ranks), share // ranks, 1)
    k_grad = jnp.concatenate([kv_parts[2 * i] for i in range(KVH)], axis=1)
    v_grad = jnp.concatenate([kv_parts[2 * i + 1] for i in range(KVH)], axis=1)
    biases = gathered[:, share : share + bias_count]
    q_bias_grad = biases[:, :heads].reshape(-1)
    k_bias_grad = biases[0::2, heads].reshape(-1)
    v_bias_grad = biases[1::2, heads].reshape(-1)
    return (
        layer_out,
        token_grad,
        q_grad,
        q_bias_grad,
        k_grad,
        k_bias_grad,
        v_grad,
        v_bias_grad,
        o_grad,
        attn_gain_grad,
        ffn_gain_grad,
        gate_grad,
        up_grad,
        down_grad,
    )


def solution(mesh):
    in_specs = (
        P("dp", "seq", None),
        P("dp", None),
        P("dp", "seq", None),
        P(None, "tensor"),
        P("tensor"),
        P(),
        P(),
        P(),
        P(),
        P(None, "tensor"),
        P(),
        P(),
        P(None, "tensor"),
        P(None, "tensor"),
        P(None, "tensor"),
    )
    out_specs = (
        P("dp", "seq", None),
        P("dp", "seq", None),
        P(("dp", "seq"), "tensor"),
        P(),
        P(("dp", "seq", "tensor"), None),
        P(),
        P(("dp", "seq", "tensor"), None),
        P(),
        P(("dp", "seq"), "tensor"),
        P(("dp", "seq")),
        P(("dp", "seq")),
        P(("dp", "seq"), "tensor"),
        P(("dp", "seq"), "tensor"),
        P(("dp", "seq"), "tensor"),
    )
    return jax.shard_map(body, mesh=mesh, in_specs=in_specs, out_specs=out_specs, check_vma=False)
```

```python
import functools
import math

import jax
import jax.numpy as jnp
from jax import lax
from jax.experimental import pallas as pl
from jax.experimental.pallas import tpu as pltpu
from jax.sharding import PartitionSpec as P

KVH = 2
HD = 128
MOST = 1024
EPS = 1e-06
ROPE_BASE = 10000.0
NEG_FILL = -1e30
Q_BLOCK = 256
K_BLOCK = 256
MIB = 1 << 20
LIGHT = 1000
TILE = 256
PIECES = 2
SCALE = 1.0 / math.sqrt(HD)


def to_bf(value):
    return value.astype(jnp.bfloat16)


def to_f(value):
    return value.astype(jnp.float32)


def dot(left, right, left_dim=1, right_dim=0):
    return lax.dot_general(
        left,
        right,
        (((left_dim,), (right_dim,)), ((), ())),
        preferred_element_type=jnp.float32,
    )


def flipped(axis, bit):
    return [(i, i ^ (1 << bit)) for i in range(lax.axis_size(axis))]


def core_swap(value):
    return lax.ppermute(value, "tensor", flipped("tensor", 0))


def chip_swap(value):
    return lax.ppermute(value, "tensor", flipped("tensor", 1))


def core_swaps(values):
    return [core_swap(value) for value in values]


def chip_swaps(values):
    return [chip_swap(value) for value in values]


def shifted(value, hops):
    count = lax.axis_size("seq")
    route = [(i, i + hops) for i in range(count) if 0 <= i + hops < count]
    return lax.ppermute(value, "seq", route)


def cost(flops, read):
    return pl.CostEstimate(flops=flops // LIGHT, bytes_accessed=read // LIGHT, transcendentals=0)


class Order:
    def __init__(self):
        self.mark = None
        self.touched = []

    def arrived(self, *values):
        self.touched.extend(values)

    def __call__(self, kernel, args, in_specs, out_specs, out_shape, grid, flops, read, name, scalars=(), scratch=()):
        anchor = ([] if self.mark is None else [self.mark]) + self.touched
        self.touched = []
        count = len(scalars) + len(args)
        outs = len(out_shape)

        def run(*refs):
            rest = refs[count + len(anchor) :]
            kernel(*refs[:count], *rest[:outs], *rest[outs + 1 :])
            rest[outs][...] = jnp.zeros(rest[outs].shape, jnp.float32)

        *results, self.mark = pl.pallas_call(
            run,
            grid_spec=pltpu.PrefetchScalarGridSpec(
                num_scalar_prefetch=len(scalars),
                grid=grid,
                in_specs=list(in_specs) + anchors(len(anchor)),
                out_specs=list(out_specs) + [mark_spec()],
                scratch_shapes=list(scratch),
            ),
            out_shape=list(out_shape) + [MARK],
            compiler_params=pltpu.CompilerParams(vmem_limit_bytes=32 * MIB),
            cost_estimate=cost(flops, read),
            name=name,
        )(*scalars, *args, *anchor)
        return results


def first_kernel(core_ref, tok_ref, gain_ref, w_ref, b_ref, cos_ref, sin_ref, h_ref, q_ref, kv_ref):
    x = to_f(tok_ref[...])
    factor = lax.rsqrt(jnp.mean(x * x, axis=-1, keepdims=True) + EPS)
    h = to_bf(x * factor * gain_ref[...])
    h_ref[...] = h
    lin = dot(h, w_ref[...]) + b_ref[...]
    cosine = cos_ref[...]
    sine = sin_ref[...]
    heads = q_ref.shape[1] // HD
    for head in range(heads):
        part = lin[:, head * HD : (head + 1) * HD]
        q_ref[:, head * HD : (head + 1) * HD] = to_bf(
            part * cosine + pltpu.roll(part, HD // 2, 1) * sine
        )
    part = lin[:, heads * HD :]
    is_key = core_ref[0] == 0
    kv_ref[...] = to_bf(
        part * jnp.where(is_key, cosine, 1.0)
        + pltpu.roll(part, HD // 2, 1) * jnp.where(is_key, sine, 0.0)
    )


def first(core, tokens, gain, weight, bias, cosine, sine):
    total, width = tokens.shape
    columns = weight.shape[1]
    block = total // 4
    half = 2

    def flip(i, core_ref):
        return (lax.rem(i + core_ref[0] * half, 4), 0)

    def at(i, core_ref):
        return (i, 0)

    def whole(i, core_ref):
        return (0, 0)

    return pl.pallas_call(
        first_kernel,
        grid_spec=pltpu.PrefetchScalarGridSpec(
            num_scalar_prefetch=1,
            grid=(4,),
            in_specs=[
                pl.BlockSpec((block, width), flip),
                pl.BlockSpec((1, width), whole),
                pl.BlockSpec((width, columns), whole),
                pl.BlockSpec((1, columns), whole),
                pl.BlockSpec((block, HD), at),
                pl.BlockSpec((block, HD), at),
            ],
            out_specs=[
                pl.BlockSpec((block, width), at),
                pl.BlockSpec((block, columns - HD), at),
                pl.BlockSpec((block, HD), at),
            ],
        ),
        out_shape=[
            jax.ShapeDtypeStruct((total, width), jnp.bfloat16),
            jax.ShapeDtypeStruct((total, columns - HD), jnp.bfloat16),
            jax.ShapeDtypeStruct((total, HD), jnp.bfloat16),
        ],
        compiler_params=pltpu.CompilerParams(vmem_limit_bytes=32 * MIB),
        cost_estimate=cost(2 * total * width * columns, 9 * MIB),
        name="first",
    )(core, tokens, gain, weight, bias, cosine, sine)


def stacked(ref, start, count, heads):
    return jnp.concatenate(
        [ref[0, pl.ds(start, count), h * HD : (h + 1) * HD] for h in range(heads)], axis=0
    )


def bounds(start_ref, index, heads, reach):
    first_key = jnp.concatenate(
        [start_ref[0, :, pl.ds(index * Q_BLOCK, Q_BLOCK)]] * heads, axis=1
    )
    place = reach + index * Q_BLOCK + lax.broadcasted_iota(jnp.int32, (1, Q_BLOCK), 1)
    return first_key, jnp.concatenate([place] * heads, axis=1)


def gather_span(core, refs, span):
    count = len(refs) // 2
    local = refs[0].shape[1]
    for i in range(count):
        here = slice(i * local, (i + 1) * local)
        span[core, here] = refs[i][0]
        span[1 - core, here] = refs[count + i][0]


def attend_kernel(heads, blocks, pieces, low_ref, core_ref, q_ref, start_ref, *refs):
    o_ref, lse_ref, acc, span = refs[2 * pieces :]
    row = pl.program_id(0)
    wide = heads * Q_BLOCK
    reach = (pieces - 1) * q_ref.shape[1]
    gather_span(core_ref[0], refs[: 2 * pieces], span)
    for index in range(blocks):
        q = stacked(q_ref, index * Q_BLOCK, Q_BLOCK, heads)
        first_key, place = bounds(start_ref, index, heads, reach)
        acc[...] = jnp.zeros_like(acc)

        def step(j, carry):
            top, total = carry
            keys = pl.ds(pl.multiple_of(j * K_BLOCK, K_BLOCK), K_BLOCK)
            s = dot(span[0, keys], q, 1, 1) * SCALE
            key = j * K_BLOCK + lax.broadcasted_iota(jnp.int32, (K_BLOCK, wide), 0)
            s = jnp.where((key >= first_key) & (key <= place), s, NEG_FILL)
            later = jnp.maximum(top, jnp.max(s, axis=0, keepdims=True))
            p = jnp.exp(s - later)
            fade = jnp.exp(top - later)
            total = total * fade + jnp.sum(p, axis=0, keepdims=True)
            acc[...] = acc[...] * fade + dot(span[1, keys], to_bf(p), 0, 0)
            return later, total

        last = (reach + (index + 1) * Q_BLOCK - 1) // K_BLOCK + 1
        top, total = lax.fori_loop(
            low_ref[row, index],
            last,
            step,
            (jnp.full((1, wide), NEG_FILL, jnp.float32), jnp.zeros((1, wide), jnp.float32)),
        )
        out = to_bf((acc[...] / total).T)
        for h in range(heads):
            o_ref[0, index * Q_BLOCK : (index + 1) * Q_BLOCK, h * HD : (h + 1) * HD] = out[
                h * Q_BLOCK : (h + 1) * Q_BLOCK
            ]
        lse_ref[0, index : index + 1, :] = top + jnp.log(total)


def span_specs(rows, local, pieces):
    near = pl.BlockSpec((1, local, HD), lambda i, *refs: (i, 0, 0))
    far = pl.BlockSpec((1, local, HD), lambda i, *refs: (lax.rem(i + rows // 2, rows), 0, 0))
    return [near] * pieces + [far] * pieces


def attend(low, core, q, start, span, mate):
    rows, local, columns = q.shape
    pieces = len(span)
    heads = columns // HD
    blocks = local // Q_BLOCK

    def at(i, *refs):
        return (i, 0, 0)

    return pl.pallas_call(
        functools.partial(attend_kernel, heads, blocks, pieces),
        grid_spec=pltpu.PrefetchScalarGridSpec(
            num_scalar_prefetch=2,
            grid=(rows,),
            in_specs=[pl.BlockSpec((1, local, columns), at), pl.BlockSpec((1, 1, local), at)]
            + span_specs(rows, local, pieces),
            out_specs=[
                pl.BlockSpec((1, local, columns), at),
                pl.BlockSpec((1, blocks, heads * Q_BLOCK), at),
            ],
            scratch_shapes=[
                pltpu.VMEM((HD, heads * Q_BLOCK), jnp.float32),
                pltpu.VMEM((2, pieces * local, HD), jnp.bfloat16),
            ],
        ),
        out_shape=[
            jax.ShapeDtypeStruct((rows, local, columns), jnp.bfloat16),
            jax.ShapeDtypeStruct((rows, blocks, heads * Q_BLOCK), jnp.float32),
        ],
        compiler_params=pltpu.CompilerParams(vmem_limit_bytes=32 * MIB),
        cost_estimate=cost(8_000_000_000, 4 * MIB),
        name="attend",
    )(low, core, q, start, *span, *mate)


def attend_back_kernel(
    heads, blocks, pieces, low_ref, core_ref, q_ref, start_ref, g_ref, o_ref, lse_ref, cos_ref, sin_ref, *refs
):
    gq_ref, keep_ref, send_ref, acc, gk, gv, span = refs[2 * pieces :]
    row = pl.program_id(0)
    wide = heads * Q_BLOCK
    reach = (pieces - 1) * q_ref.shape[1]
    core = core_ref[0]
    gather_span(core, refs[: 2 * pieces], span)
    gk[...] = jnp.zeros_like(gk)
    gv[...] = jnp.zeros_like(gv)
    for index in range(blocks):
        q = stacked(q_ref, index * Q_BLOCK, Q_BLOCK, heads)
        g = stacked(g_ref, index * Q_BLOCK, Q_BLOCK, heads)
        o = stacked(o_ref, index * Q_BLOCK, Q_BLOCK, heads)
        inner = jnp.sum((to_f(g) * to_f(o)).T, axis=0, keepdims=True)
        lse = lse_ref[0, index : index + 1, :]
        first_key, place = bounds(start_ref, index, heads, reach)
        acc[...] = jnp.zeros_like(acc)

        def step(j, carry):
            keys = pl.ds(pl.multiple_of(j * K_BLOCK, K_BLOCK), K_BLOCK)
            k = span[0, keys]
            s = dot(k, q, 1, 1) * SCALE
            key = j * K_BLOCK + lax.broadcasted_iota(jnp.int32, (K_BLOCK, wide), 0)
            p = jnp.where((key >= first_key) & (key <= place), jnp.exp(s - lse), 0.0)
            gp = dot(span[1, keys], g, 1, 1)
            gs = to_bf(p * (gp - inner))
            gv[keys] += dot(to_bf(p), g)
            gk[keys] += dot(gs, q)
            acc[...] += dot(k, gs, 0, 0)
            return carry

        last = (reach + (index + 1) * Q_BLOCK - 1) // K_BLOCK + 1
        lax.fori_loop(low_ref[row, index], last, step, 0)
        gq = acc[...].T * SCALE
        here = slice(index * Q_BLOCK, (index + 1) * Q_BLOCK)
        cosine, sine = cos_ref[here], sin_ref[here]
        for h in range(heads):
            part = gq[h * Q_BLOCK : (h + 1) * Q_BLOCK]
            gq_ref[0, here, h * HD : (h + 1) * HD] = to_bf(
                part * cosine + pltpu.roll(part * sine, HD // 2, 1)
            )
    is_key = core == 0
    keys, values = gk[...] * SCALE, gv[...]
    keep_ref[0] = to_bf(jnp.where(is_key, keys, values))
    send_ref[0] = to_bf(jnp.where(is_key, values, keys))


def attend_back(order, low, core, q, start, span, mate, grad, out, lse, cosine, sine):
    rows, local, columns = q.shape
    pieces = len(span)
    window = pieces * local
    heads = columns // HD
    blocks = local // Q_BLOCK

    def at(i, *refs):
        return (i, 0, 0)

    table = pl.BlockSpec((local, HD), lambda i, *refs: (i, 0))
    tokens = pl.BlockSpec((1, local, columns), at)
    return order(
        functools.partial(attend_back_kernel, heads, blocks, pieces),
        [q, start, grad, out, lse, cosine, sine, *span, *mate],
        [
            tokens,
            pl.BlockSpec((1, 1, local), at),
            tokens,
            tokens,
            pl.BlockSpec((1, blocks, heads * Q_BLOCK), at),
            table,
            table,
        ]
        + span_specs(rows, local, pieces),
        [tokens, pl.BlockSpec((1, window, HD), at), pl.BlockSpec((1, window, HD), at)],
        [
            jax.ShapeDtypeStruct((rows, local, columns), jnp.bfloat16),
            jax.ShapeDtypeStruct((rows, window, HD), jnp.bfloat16),
            jax.ShapeDtypeStruct((rows, window, HD), jnp.bfloat16),
        ],
        (rows,),
        20_000_000_000,
        6 * MIB,
        "attend_back",
        scalars=(low, core),
        scratch=[
            pltpu.VMEM((HD, heads * Q_BLOCK), jnp.float32),
            pltpu.VMEM((window, HD), jnp.float32),
            pltpu.VMEM((window, HD), jnp.float32),
            pltpu.VMEM((2, window, HD), jnp.bfloat16),
        ],
    )


def fold_kernel(keep_ref, come_ref, own_ref, *send_refs):
    local = own_ref.shape[1]
    total = to_f(keep_ref[0]) + to_f(come_ref[0])
    reach = total.shape[0] - local
    own_ref[0] = total[reach:]
    for hop, ref in enumerate(send_refs, 1):
        ref[0] = to_bf(total[reach - hop * local : reach - (hop - 1) * local])


def fold(order, keep, come, local):
    rows, window = keep.shape[:2]
    hops = window // local - 1
    out = pl.BlockSpec((1, local, HD), lambda i: (i, 0, 0))
    return order(
        fold_kernel,
        [keep, come],
        [
            pl.BlockSpec((1, window, HD), lambda i: (i, 0, 0)),
            pl.BlockSpec((1, window, HD), lambda i: (lax.rem(i + rows // 2, rows), 0, 0)),
        ],
        [out] * (hops + 1),
        [jax.ShapeDtypeStruct((rows, local, HD), jnp.float32)]
        + [jax.ShapeDtypeStruct((rows, local, HD), jnp.bfloat16)] * hops,
        (rows,),
        0,
        4 * MIB,
        "fold",
    )


def carry_kernel(piece_ref, come_ref, out_ref):
    out_ref[...] = to_bf(to_f(piece_ref[...]) + to_f(come_ref[...]))


def carry(order, piece, come):
    rows, local, columns = piece.shape
    at = pl.BlockSpec((1, local, columns), lambda i: (i, 0, 0))
    return order(
        carry_kernel,
        [piece, come],
        [at, at],
        [at],
        [jax.ShapeDtypeStruct(piece.shape, jnp.bfloat16)],
        (rows,),
        0,
        2 * MIB,
        "carry",
    )[0]


def bias_kernel(left_ref, right_ref, out_ref):
    out_ref[...] = left_ref[...] + right_ref[...]


def bias_add(order, left, right):
    whole = pl.BlockSpec(left.shape, lambda i: (0, 0))
    return order(
        bias_kernel,
        [left, right],
        [whole, whole],
        [whole],
        [jax.ShapeDtypeStruct(left.shape, jnp.float32)],
        (1,),
        0,
        MIB,
        "bias",
    )[0]


def join_kernel(hops, core_ref, gq_ref, cos_ref, sin_ref, own_ref, *refs):
    out_ref, sum_ref = refs[-2:]
    columns = gq_ref.shape[2]
    grad = own_ref[0]
    for ref in refs[:hops]:
        grad = grad + to_f(ref[0])
    is_key = core_ref[0] == 0
    cosine = jnp.where(is_key, cos_ref[...], 1.0)
    sine = jnp.where(is_key, sin_ref[...], 0.0)
    kv = to_bf(grad * cosine + pltpu.roll(grad * sine, HD // 2, 1))
    q = gq_ref[0]
    out_ref[:, :columns] = q
    out_ref[:, columns:] = kv

    @pl.when(pl.program_id(0) == 0)
    def _():
        sum_ref[...] = jnp.zeros(sum_ref.shape, jnp.float32)

    sum_ref[:, :columns] += jnp.sum(to_f(q), axis=0, keepdims=True)
    sum_ref[:, columns:] += jnp.sum(to_f(kv), axis=0, keepdims=True)


def join(order, core, grad_q, own, comes, cosine, sine):
    rows, local, columns = grad_q.shape
    wide = columns + HD

    def at(i, *refs):
        return (i, 0, 0)

    piece = pl.BlockSpec((1, local, HD), at)
    table = pl.BlockSpec((local, HD), lambda i, *refs: (i, 0))
    return order(
        functools.partial(join_kernel, len(comes)),
        [grad_q, cosine, sine, own, *comes],
        [pl.BlockSpec((1, local, columns), at), table, table, piece] + [piece] * len(comes),
        [
            pl.BlockSpec((local, wide), lambda i, *refs: (i, 0)),
            pl.BlockSpec((8, wide), lambda i, *refs: (0, 0)),
        ],
        [
            jax.ShapeDtypeStruct((rows * local, wide), jnp.bfloat16),
            jax.ShapeDtypeStruct((8, wide), jnp.float32),
        ],
        (rows,),
        0,
        4 * MIB,
        "join",
        scalars=(core,),
    )


def mixed_back_kernel(w_ref, *refs):
    rows = refs[0].shape[0]
    for i, ref in enumerate(refs[:-1]):
        refs[-1][i * rows : (i + 1) * rows] = to_bf(dot(ref[...], w_ref[...]))


def mixed_back(order, pieces, weight):
    rows, width = pieces[0].shape
    total = rows * len(pieces)
    columns = weight.shape[1]

    def whole(i):
        return (0, 0)

    return order(
        mixed_back_kernel,
        [weight, *pieces],
        [pl.BlockSpec((width, columns), whole)] + [pl.BlockSpec((rows, width), whole)] * len(pieces),
        [pl.BlockSpec((total, columns), whole)],
        [jax.ShapeDtypeStruct((total, columns), jnp.bfloat16)],
        (1,),
        2 * total * width * columns,
        6 * MIB,
        "mixed_back",
    )[0]


def place_kernel(core_ref, *refs):
    for i, ref in enumerate(refs[:-1]):

        @pl.when(pl.program_id(0) == i)
        def _(ref=ref):
            refs[-1][...] = ref[...]


def place(order, core, pieces):
    rows, width = pieces[0].shape
    count = len(pieces)
    return order(
        place_kernel,
        list(pieces),
        [pl.BlockSpec((rows, width), lambda i, core_ref: (0, 0))] * count,
        [pl.BlockSpec((rows, width), lambda i, core_ref: (lax.rem(i + core_ref[0] * (count // 2), count), 0))],
        [jax.ShapeDtypeStruct((rows * count, width), pieces[0].dtype)],
        (count,),
        0,
        8 * rows * width,
        "place",
        scalars=(core,),
    )[0]


def anchors(count):
    return [pl.BlockSpec(memory_space=pl.ANY)] * count


MARK = jax.ShapeDtypeStruct((8, HD), jnp.float32)


def mark_spec():
    return pl.BlockSpec((8, HD), lambda *refs: (0, 0))


def grad_hidden_kernel(g_ref, w_ref, out_ref):
    out_ref[...] = to_bf(dot(g_ref[...], w_ref[...], 1, 1))


def grad_hidden_of(order, grad, weight):
    total, width = grad.shape
    hidden = weight.shape[0]
    return order(
        grad_hidden_kernel,
        [grad, weight],
        [pl.BlockSpec((total, width), lambda i: (0, 0)), pl.BlockSpec((TILE, width), lambda i: (i, 0))],
        [pl.BlockSpec((total, TILE), lambda i: (0, i))],
        [jax.ShapeDtypeStruct((total, hidden), jnp.bfloat16)],
        (pl.cdiv(hidden, TILE),),
        2 * total * width * hidden,
        15 * MIB,
        "grad_hidden",
    )[0]


def gated_kernel(gh_ref, gw_ref, uw_ref, *refs):
    hid_ref, gg_ref, gu_ref = refs[-3:]
    rows = refs[0].shape[0]
    for part, ref in enumerate(refs[:-3]):
        here = slice(part * rows, (part + 1) * rows)
        h = ref[...]
        gate = dot(h, gw_ref[...], 1, 1)
        up = dot(h, uw_ref[...], 1, 1)
        grad = to_f(gh_ref[here])
        sigma = 1.0 / (1.0 + jnp.exp(-gate))
        swish = gate * sigma
        hid_ref[here] = to_bf(swish * up)
        gu_ref[here] = to_bf(grad * swish)
        gg_ref[here] = to_bf(grad * up * sigma * (1.0 + gate * (1.0 - sigma)))


def gated(order, pieces, grad_hidden, gate_weight, up_weight):
    rows, width = pieces[0].shape
    total = rows * len(pieces)
    hidden = gate_weight.shape[0]
    column = pl.BlockSpec((total, TILE), lambda i: (0, i))
    weight = pl.BlockSpec((TILE, width), lambda i: (i, 0))
    shape = jax.ShapeDtypeStruct((total, hidden), jnp.bfloat16)
    return order(
        gated_kernel,
        [grad_hidden, gate_weight, up_weight, *pieces],
        [column, weight, weight] + [pl.BlockSpec((rows, width), lambda i: (0, 0))] * len(pieces),
        [column] * 3,
        [shape] * 3,
        (pl.cdiv(hidden, TILE),),
        4 * total * width * hidden,
        30 * MIB,
        "gated",
    )


def share_kernel(plan, lefts, rights, extra, halves, groups, pick_ref, blocks_ref, *refs):
    step = pl.program_id(0)
    left_refs, right_refs = refs[:lefts], refs[lefts : lefts + rights]
    refs = refs[lefts + rights :]
    if extra:
        extra_ref, refs = refs[0], refs[1:]
    for left, right, begin, end, shift, columns, target in plan:

        @pl.when((step >= begin) & (step < end))
        def _(left=left, right=right, shift=shift, columns=columns, target=target):
            out = dot(left_refs[left][...], right_refs[right][...])
            if extra:
                out = out + to_f(extra_ref[...])
            tile = out.shape[1]
            spot = (step + shift) * tile + lax.broadcasted_iota(jnp.int32, (1, tile), 1)
            out = to_bf(jnp.where(spot < columns, out, 0.0))
            if groups:
                share = out.shape[0] // (groups[0] * groups[1])
                for i in range(groups[0]):
                    for j in range(groups[1]):
                        here = (j * groups[0] + i) * share
                        there = (i * groups[1] + j) * share
                        refs[target][here : here + share] = out[there : there + share]
                return
            if not halves:
                refs[target][...] = out
                return
            send_ref, keep_ref, rows = refs
            rows[...] = out
            share = send_ref.shape[0] // (2 * halves)
            for i in range(2 * halves):
                here = slice(i * share, (i + 1) * share)
                send_ref[here] = rows[pl.ds(pl.multiple_of(blocks_ref[i] * share, share), share)]
                keep_ref[here] = rows[pl.ds(pl.multiple_of(blocks_ref[2 * halves + i] * share, share), share)]


def clipped(rows, tile, begin, count, shift=0):
    return pl.BlockSpec((rows, tile), lambda i, *refs: (0, jnp.clip(i - begin, 0, count - 1) + shift))


def share_of(order, lefts, rights, parts, part, pick, tile, extra=None, blocks=None, groups=None):
    tokens = lefts[0].shape[1]
    plan, at = [], 0
    starts, sizes, right_at = {}, {}, {}
    for left, right, skip, count, target in parts:
        plan.append((left, right, at, at + count, skip - at, rights[right].shape[1], target))
        starts.setdefault(target, at)
        sizes[target] = sizes.get(target, 0) + count
        first, tiles, low = right_at.get(right, (at, 0, skip))
        right_at[right] = (first, tiles + count, low)
        at += count
    halves = 0
    extras = [] if extra is None else [extra]
    scratch = []
    if blocks is None:
        blocks = jnp.zeros((1,), jnp.int32)
        outs = [clipped(part, tile, starts[t], sizes[t]) for t in sorted(sizes)]
        shapes = [jax.ShapeDtypeStruct((part, sizes[t] * tile), jnp.bfloat16) for t in sorted(sizes)]
    else:
        halves = blocks.shape[0] // 4
        outs = [clipped(part // 2, tile, 0, at)] * 2
        shapes = [jax.ShapeDtypeStruct((part // 2, at * tile), jnp.bfloat16)] * 2
        scratch = [pltpu.VMEM((part, tile), jnp.bfloat16)]
    return order(
        functools.partial(share_kernel, plan, len(lefts), len(rights), len(extras), halves, groups),
        [*lefts, *rights, *extras],
        [pl.BlockSpec((part, tokens), lambda i, pick_ref, blocks_ref: (pick_ref[0], 0))] * len(lefts)
        + [clipped(tokens, tile, *right_at[r]) for r in range(len(rights))]
        + [clipped(part, tile, 0, at)] * len(extras),
        outs,
        shapes,
        (at,),
        2 * part * tokens * at * tile,
        2 * (part * tokens + (part + tokens) * at * tile),
        "share",
        scalars=(jnp.asarray(pick, jnp.int32).reshape(1), blocks),
        scratch=scratch,
    )


def relay_kernel(keep_ref, come_ref, out_ref):
    out_ref[...] = to_bf(to_f(keep_ref[...]) + to_f(come_ref[...]))


def relay(order, keep, come, share):
    rows, columns = keep.shape
    pair = pl.BlockSpec((share, columns), lambda i: (2 * i + 1, 0))
    return order(
        relay_kernel,
        [keep, come],
        [pair, pair],
        [pl.BlockSpec((share, columns), lambda i: (i, 0))],
        [jax.ShapeDtypeStruct((rows // 2, columns), jnp.bfloat16)],
        (rows // (2 * share),),
        0,
        3 * rows * columns,
        "relay",
    )[0]


def finish_kernel(plan, columns, gains, *refs):
    out_ref = refs[-2] if gains else refs[-1]
    step = pl.program_id(0)
    tile = out_ref.shape[1]
    for begin, end, first, count in plan:

        @pl.when((step >= begin) & (step < end))
        def _(first=first, count=count):
            out = to_f(refs[first][...])
            for ref in refs[first + 1 : first + count]:
                out = out + to_f(ref[...])
            out_ref[...] = out
            if gains:
                spot = step * tile + lax.broadcasted_iota(jnp.int32, (1, tile), 1)
                terms = jnp.where(spot < columns, out * to_f(refs[-3][...]), 0.0)
                total = terms[:, :HD]
                for i in range(HD, tile, HD):
                    total = total + terms[:, i : i + HD]

                @pl.when(step == 0)
                def _():
                    refs[-1][...] = total

                @pl.when(step > 0)
                def _():
                    refs[-1][...] += total


def finish(order, chunks, share, columns, tile, weight=None):
    plan, specs, args, at = [], [], [], 0
    for chunk in chunks:
        count = chunk[0].shape[1] // tile
        plan.append((at, at + count, len(args), len(chunk)))
        specs += [clipped(share, tile, at, count)] * len(chunk)
        args += chunk
        at += count
    column = pl.BlockSpec((share, tile), lambda i: (0, i))
    outs, shapes = [column], [jax.ShapeDtypeStruct((share, columns), jnp.float32)]
    if weight is not None:
        args.append(weight)
        specs.append(column)
        outs.append(pl.BlockSpec((share, HD), lambda i: (0, 0)))
        shapes.append(jax.ShapeDtypeStruct((share, HD), jnp.float32))
    return order(
        functools.partial(finish_kernel, plan, columns, weight is not None),
        args,
        specs,
        outs,
        shapes,
        (at,),
        0,
        14 * share * columns,
        "finish",
    )


def narrow_kernel(pairs, extras, right_dim, *refs):
    out = dot(refs[0][...], refs[1][...], 1, right_dim)
    for i in range(1, pairs):
        out = out + dot(refs[2 * i][...], refs[2 * i + 1][...], 1, right_dim)
    extra = refs[2 * pairs : 2 * pairs + extras]
    outs = refs[2 * pairs + extras :]
    if extras:
        out = out + jnp.concatenate([to_f(ref[...]) for ref in extra], axis=0)
    rows = outs[0].shape[0]
    for i, ref in enumerate(outs):
        ref[...] = to_bf(out[i * rows : (i + 1) * rows])


def narrow(order, pairs, index, extra=(), right_dim=0):
    total, hidden = pairs[0][0].shape
    width = pairs[0][1].shape[1 - right_dim]
    half = total // 2
    piece = half // PIECES
    column = pl.BlockSpec((piece, TILE), lambda i: (0, i))
    right = (
        pl.BlockSpec((TILE, hidden), lambda i: (i, 0))
        if right_dim
        else pl.BlockSpec((hidden, TILE), lambda i: (0, i))
    )
    return order(
        functools.partial(narrow_kernel, len(pairs), len(extra), right_dim),
        [item for pair in pairs for item in pair] + list(extra),
        [pl.BlockSpec((half, hidden), lambda i: (index, 0)), right] * len(pairs) + [column] * len(extra),
        [column] * PIECES,
        [jax.ShapeDtypeStruct((piece, width), jnp.bfloat16)] * PIECES,
        (width // TILE,),
        2 * len(pairs) * half * width * hidden,
        2 * len(pairs) * (half + width) * hidden + 2 * half * width,
        "narrow",
    )


def piece_specs(piece, width, block):
    steps = piece // block
    return [
        pl.BlockSpec((block, width), lambda i, *refs, j=j: (jnp.clip(i - j * steps, 0, steps - 1), 0))
        for j in range(PIECES)
    ]


def pick_piece(refs):
    value = refs[0][...]
    for j, ref in enumerate(refs[1:], 1):
        value = jnp.where(pl.program_id(0) >= 4 * j // len(refs), ref[...], value)
    return value


def put_piece(refs, value):
    steps = 4 // len(refs)
    for j, ref in enumerate(refs):

        @pl.when(lax.div(pl.program_id(0), steps) == j)
        def _(ref=ref):
            ref[...] = value


def turn_kernel(*refs):
    rows = refs[0].shape[0]
    for i, ref in enumerate(refs[:-1]):
        refs[-1][:, i * rows : (i + 1) * rows] = ref[...].T


def turn(order, pieces):
    rows, width = pieces[0].shape
    total = rows * len(pieces)
    return order(
        turn_kernel,
        list(pieces),
        [pl.BlockSpec((rows, TILE), lambda i: (0, i))] * len(pieces),
        [pl.BlockSpec((TILE, total), lambda i: (i, 0))],
        [jax.ShapeDtypeStruct((width, total), jnp.bfloat16)],
        (width // TILE,),
        0,
        4 * total * width,
        "turn",
    )[0]


def grad_out_kernel(core_ref, cot_ref, valid_ref, out_ref, turned_ref):
    out = to_bf(to_f(cot_ref[...]) * valid_ref[...])
    out_ref[...] = out
    turned_ref[...] = out.T


def grad_out_of(order, core, cotangent, valid):
    total, width = cotangent.shape
    block = total // 4
    return order(
        grad_out_kernel,
        [cotangent, valid],
        [
            pl.BlockSpec((block, width), lambda i, core_ref: (lax.rem(i + core_ref[0] * 2, 4), 0)),
            pl.BlockSpec((block, 1), lambda i, core_ref: (i, 0)),
        ],
        [
            pl.BlockSpec((block, width), lambda i, core_ref: (i, 0)),
            pl.BlockSpec((width, block), lambda i, core_ref: (0, i)),
        ],
        [
            jax.ShapeDtypeStruct((total, width), jnp.bfloat16),
            jax.ShapeDtypeStruct((width, total), jnp.bfloat16),
        ],
        (4,),
        0,
        6 * total * width,
        "grad_out",
        scalars=(core,),
    )


def middle_kernel(core_ref, tok_ref, gain_ref, *refs):
    mine, come = pick_piece(refs[:PIECES]), pick_piece(refs[PIECES : 2 * PIECES])
    mid_ref, *h_refs = refs[2 * PIECES :]
    middle = to_f(tok_ref[...]) + (to_f(mine) + to_f(come))
    factor = lax.rsqrt(jnp.mean(middle * middle, axis=-1, keepdims=True) + EPS)
    mid_ref[...] = middle
    put_piece(h_refs, to_bf(middle * factor * gain_ref[...]))


def middle_of(order, core, tokens, mine, come, gain):
    piece, width = mine[0].shape
    half = piece * PIECES
    block = half // 4
    specs = piece_specs(piece, width, block)
    middle, *h = order(
        middle_kernel,
        [tokens, gain, *mine, *come],
        [
            pl.BlockSpec((block, width), lambda i, core_ref: (core_ref[0] * 4 + i, 0)),
            pl.BlockSpec((1, width), lambda i, core_ref: (0, 0)),
        ]
        + specs * 2,
        [pl.BlockSpec((block, width), lambda i, core_ref: (i, 0))] + specs,
        [jax.ShapeDtypeStruct((half, width), jnp.float32)]
        + [jax.ShapeDtypeStruct((piece, width), jnp.bfloat16)] * PIECES,
        (4,),
        0,
        9 * MIB,
        "middle",
        scalars=(core,),
    )
    return middle, h


def norm_back_kernel(core_ref, x_ref, gain_ref, up_ref, *refs):
    mine, come = pick_piece(refs[:PIECES]), pick_piece(refs[PIECES : 2 * PIECES])
    outs = refs[2 * PIECES :]
    grad = to_f(mine) + to_f(come)
    x = to_f(x_ref[...])
    factor = lax.rsqrt(jnp.mean(x * x, axis=-1, keepdims=True) + EPS)
    normed = x * factor
    weighted = grad * gain_ref[...]
    inner = jnp.mean(weighted * normed, axis=-1, keepdims=True)
    out = to_f(up_ref[...]) + factor * (weighted - normed * inner)
    if len(outs) > PIECES:
        outs[0][...] = out
        put_piece(outs[1:], to_bf(out))
    else:
        put_piece(outs, out)


def norm_back(order, core, mine, come, x, gain, up, by_core):
    piece, width = mine[0].shape
    half = piece * PIECES
    block = half // 4
    at = pl.BlockSpec((block, width), lambda i, core_ref: (i, 0))
    picked = pl.BlockSpec((block, width), lambda i, core_ref: (core_ref[0] * 4 + i, 0))
    specs = piece_specs(piece, width, block)
    if by_core:
        shapes = [jax.ShapeDtypeStruct((piece, width), jnp.float32)] * PIECES
    else:
        shapes = [jax.ShapeDtypeStruct((half, width), jnp.float32)]
        shapes += [jax.ShapeDtypeStruct((piece, width), jnp.bfloat16)] * PIECES
    return order(
        norm_back_kernel,
        [x, gain, up, *mine, *come],
        [picked if by_core else at, pl.BlockSpec((1, width), lambda i, core_ref: (0, 0)), at] + specs * 2,
        specs if by_core else [at] + specs,
        shapes,
        (4,),
        0,
        10 * MIB,
        "norm_back",
        scalars=(core,),
    )


def layer_kernel(middle_ref, *refs):
    mine, come = pick_piece(refs[:PIECES]), pick_piece(refs[PIECES : 2 * PIECES])
    put_piece(refs[2 * PIECES :], to_bf(middle_ref[...] + (to_f(mine) + to_f(come))))


def layer_of(order, middle, mine, come):
    piece, width = mine[0].shape
    block = piece * PIECES // 4
    specs = piece_specs(piece, width, block)
    return order(
        layer_kernel,
        [middle, *mine, *come],
        [pl.BlockSpec((block, width), lambda i: (i, 0))] + specs * 2,
        specs,
        [jax.ShapeDtypeStruct((piece, width), jnp.bfloat16)] * PIECES,
        (4,),
        0,
        5 * MIB,
        "layer",
    )


def tensor_gather(value, rank):
    mate = core_swap(value)
    pair = jnp.where(lax.rem(rank, 2) == 0, jnp.stack([value, mate]), jnp.stack([mate, value]))
    come = chip_swap(pair)
    return jnp.where(
        lax.div(rank, 2) == 0,
        jnp.concatenate([pair, come], axis=0),
        jnp.concatenate([come, pair], axis=0),
    )


def body(
    tokens,
    lengths,
    cotangent,
    q_weight,
    q_bias,
    k_weight,
    k_bias,
    v_weight,
    v_bias,
    o_weight,
    attn_gain,
    ffn_gain,
    gate_weight,
    up_weight,
    down_weight,
):
    rows, local, width = tokens.shape
    total = rows * local
    half = total // 2
    heads = q_weight.shape[1] // HD
    ranks = lax.axis_size("tensor")
    seqs = lax.axis_size("seq")
    rank = lax.axis_index("tensor")
    dp_index = lax.axis_index("dp")
    seq_index = lax.axis_index("seq")
    core = lax.rem(rank, 2)
    head = lax.div(rank, 2)
    core_one = core.reshape(1)
    hops = min(seqs - 1, -(-(MOST - 1) // local))
    reach = hops * local

    def own_first(value):
        turned = jnp.concatenate([value[rows // 2 :], value[: rows // 2]], axis=0)
        return jnp.where(core == 0, value, turned)

    slots = jnp.arange(lengths.shape[1], dtype=jnp.int32)
    lens = own_first(lengths)
    ends = jnp.sum(jnp.where(slots[None, :] <= slots[:, None], lens[:, None, :], 0), axis=2)
    spot = seq_index * local + jnp.arange(local, dtype=jnp.int32)
    begun = jnp.max(
        jnp.where(ends[:, None, :] <= spot[None, :, None], ends[:, None, :], 0), axis=2
    )
    valid = to_f(spot[None, :] < ends[:, -2:-1])
    position = (spot[None, :] - begun).reshape(total, 1)
    freqs = ROPE_BASE ** (-(jnp.arange(HD // 2, dtype=jnp.float32) * 2.0) / HD)
    angles = to_f(position) * freqs[None, :]
    cosine, sine = jnp.cos(angles), jnp.sin(angles)
    cosine = jnp.concatenate([cosine, cosine], axis=1)
    sine = jnp.concatenate([-sine, sine], axis=1)
    start = begun - (seq_index * local - reach)
    low = jnp.maximum(lax.div(jnp.maximum(start[:, ::Q_BLOCK], 0), K_BLOCK), 0)
    start = start.reshape(rows, 1, local)

    key_side = core == 0
    kv_weight = jnp.where(
        key_side,
        lax.dynamic_slice_in_dim(k_weight, head * HD, HD, 1),
        lax.dynamic_slice_in_dim(v_weight, head * HD, HD, 1),
    )
    kv_bias = jnp.where(
        key_side,
        lax.dynamic_slice_in_dim(k_bias, head * HD, HD, 0),
        lax.dynamic_slice_in_dim(v_bias, head * HD, HD, 0),
    )
    weight = jnp.concatenate([q_weight, kv_weight], axis=1)
    bias = to_f(jnp.concatenate([q_bias, kv_bias])).reshape(1, -1)
    gain_one = to_f(attn_gain).reshape(1, width)
    gain_two = to_f(ffn_gain).reshape(1, width)

    h_one, q_rot, kv = first(
        core_one, tokens.reshape(total, width), gain_one, weight, bias, cosine, sine
    )
    kv = kv.reshape(rows, local, HD)
    span = [shifted(kv, h) for h in range(hops, 0, -1)] + [kv]
    mate = [core_swap(piece) for piece in span]
    q_rows = q_rot.reshape(rows, local, heads * HD)
    mixed_rows, lse = attend(low, core_one, q_rows, start, span, mate)
    mixed = mixed_rows.reshape(total, heads * HD)

    order = Order()
    flat_tokens = tokens.reshape(total, width)
    dps = lax.axis_size("dp")
    near_pair = dps == 2 and seqs == 4
    part = width // dps
    share = part // seqs
    gate_t, up_t, down_t = gate_weight.T, up_weight.T, down_weight.T
    units = gate_t.shape[0]
    tiles = -(-units // TILE)
    cut = (tiles + 1) // 2
    long = max(tiles - 2, 1)
    one, two = seq_index ^ 1, seq_index ^ 2
    three = seq_index ^ 3
    quad = jnp.stack([one, three, seq_index, two])

    begin = (dp_index * seqs + seq_index) * share

    def rows_of(value):
        return lax.dynamic_slice_in_dim(value, begin, share, 0)

    class Rows:
        def __init__(self, lefts, rights, parts, tile=TILE, sent=None):
            self.args = (order, lefts, rights, parts)
            self.tile = tile
            if not near_pair:
                (whole,) = share_of(*self.args, width, 0, tile)
                self.whole = lax.psum_scatter(whole, ("dp", "seq"), scatter_dimension=0, tiled=True)
                return
            if sent is None:
                (sent,) = share_of(*self.args, part, 1 - dp_index, tile)
            self.come = lax.ppermute(sent, "dp", flipped("dp", 0))

        def own(self):
            if near_pair:
                send, self.keep = share_of(*self.args, part, dp_index, self.tile, self.come, quad)
                self.come = lax.ppermute(send, "seq", flipped("seq", 0))

        def relay(self):
            if near_pair:
                sent = relay(order, self.keep, self.come, share)
                self.last = lax.ppermute(sent, "seq", flipped("seq", 1))

        def settled(self):
            if near_pair:
                order.arrived(self.last)

        def result(self):
            return [self.keep, self.come, self.last] if near_pair else [self.whole]

    class SeqFirst(Rows):
        def __init__(self, lefts, rights, parts, tile=TILE):
            if not near_pair:
                super().__init__(lefts, rights, parts, tile)
                return
            (whole,) = share_of(order, lefts, rights, parts, width, 0, tile, None, None, (dps, seqs))
            self.mine = lax.psum_scatter(whole, "seq", scatter_dimension=0, tiled=True)

        def across(self):
            if near_pair:
                sent = lax.dynamic_slice_in_dim(self.mine, (1 - dp_index) * share, share, 0)
                self.mine = lax.dynamic_slice_in_dim(self.mine, dp_index * share, share, 0)
                order.arrived(sent, self.mine)
                self.come = lax.ppermute(sent, "dp", flipped("dp", 0))

        def settled(self):
            if near_pair:
                order.arrived(self.come)

        def result(self):
            return [self.mine, self.come] if near_pair else [self.whole]

    class Scattered(Rows):
        def own(self):
            if near_pair:
                (mine,) = share_of(*self.args, part, dp_index, self.tile, self.come)
                self.whole = lax.psum_scatter(mine, "seq", scatter_dimension=0, tiled=True)

        def settled(self):
            order.arrived(self.whole)

        def result(self):
            return [self.whole]

    sent = core_swaps(narrow(order, [(mixed, o_weight)], 1, (), 1))
    mine = narrow(order, [(mixed, o_weight)], 0, sent, 1)
    come = chip_swaps(mine)
    grad_ffn, grad_ffn_t = grad_out_of(
        order, core_one, cotangent.reshape(total, width), valid.reshape(total, 1)
    )
    gate_rows, up_rows = rows_of(gate_weight), rows_of(up_weight)
    order.arrived(gate_rows, up_rows)
    grad_hidden = grad_hidden_of(order, grad_ffn, down_t)
    h_one_t = turn(order, [h_one])
    middle, h_two = middle_of(order, core_one, flat_tokens, mine, come, gain_two)
    h_two += core_swaps(h_two)
    hidden, grad_gate, grad_up = gated(order, h_two, grad_hidden, gate_t, up_t)

    down_b = SeqFirst([grad_ffn_t], [hidden], [(0, 0, cut, tiles - cut, 0)])
    down_a = Rows([grad_ffn_t], [hidden], [(0, 0, 0, cut, 0)])
    pairs = [(grad_gate, gate_t), (grad_up, up_t)]
    sent = core_swaps(narrow(order, pairs, 1))
    mine = narrow(order, pairs, 0, sent)
    come = chip_swaps(mine)
    h_two_t = turn(order, h_two)
    if near_pair:
        sends = share_of(
            order,
            [h_two_t],
            [grad_gate, grad_up],
            [(0, 0, 0, tiles, 0), (0, 1, 0, long, 1), (0, 1, long, tiles - long, 2)],
            part,
            1 - dp_index,
            TILE,
        )
    else:
        sends = [None] * 3

    def half_rows(kind, right, begin, end, sent):
        return kind([h_two_t], [right], [(0, 0, begin, end - begin, 0)], TILE, sent)

    gate = half_rows(Scattered, grad_gate, 0, tiles, sends[0])
    up_a = half_rows(Rows, grad_up, 0, long, sends[1])
    up_b = half_rows(Rows, grad_up, long, tiles, sends[2])
    down_a.own()
    grad_middle, *branch = norm_back(order, core_one, mine, come, middle, gain_two, grad_ffn, False)
    branch += core_swaps(branch)
    grad_mixed = mixed_back(order, branch, o_weight).reshape(rows, local, heads * HD)
    grad_q_rows, keep, sent = attend_back(
        order, low, core_one, q_rows, start, span, mate, grad_mixed, mixed_rows, lse, cosine, sine
    )
    both_come = core_swap(sent)
    branch_t = turn(order, branch)
    down_a.relay()
    own_kv, *pieces = fold(order, keep, both_come, local)
    moving = shifted(pieces[-1], -1) if pieces else None
    ffn_sent = core_swaps(narrow(order, [(hidden, down_t)], 1))
    for piece in pieces[-2::-1]:
        moving = shifted(carry(order, piece, moving), -1)
    grad_qkv, bias_sum = join(
        order, core_one, grad_q_rows, own_kv, [] if moving is None else [moving], cosine, sine
    )
    sent = core_swaps(narrow(order, [(grad_qkv, weight)], 1, (), 1))
    down_b.across()
    mine = narrow(order, [(grad_qkv, weight)], 0, sent, 1)
    come = chip_swaps(mine)
    down_a.settled()
    gate.own()
    last_parts = [(0, 0, 0, grad_qkv.shape[1] // HD, 0), (1, 1, 0, heads, 0)]
    last = Rows([h_one_t, branch_t], [grad_qkv, mixed], last_parts, HD)
    ffn_mine = narrow(order, [(hidden, down_t)], 0, ffn_sent)
    token = norm_back(order, core_one, mine, come, flat_tokens, gain_one, grad_middle, True)
    token += core_swaps(token)
    ffn_come = chip_swaps(ffn_mine)
    up_a.own()
    token_grad = place(order, core_one, token).reshape(rows, local, width)
    layer = layer_of(order, middle, ffn_mine, ffn_come)
    layer += core_swaps(layer)
    last.own()
    layer_out = place(order, core_one, layer).reshape(rows, local, width)
    up_a.relay()
    up_b.own()
    last.relay()
    if near_pair:
        bias_come = lax.ppermute(bias_sum, "dp", flipped("dp", 0))
        bias_all = bias_add(order, bias_sum, bias_come)
        bias_come = lax.ppermute(bias_all, "seq", flipped("seq", 0))
    up_a.settled()
    up_b.relay()
    (down_grad,) = finish(order, [down_a.result(), down_b.result()], share, units, TILE)
    gate_grad, gate_term = finish(order, [gate.result()], share, units, TILE, gate_rows)
    wide_columns = grad_qkv.shape[1]
    (last_grad,) = finish(order, [last.result()], share, wide_columns + heads * HD, HD)
    if near_pair:
        bias_all = bias_add(order, bias_all, bias_come)
        bias_come = lax.ppermute(bias_all, "seq", flipped("seq", 1))
        bias_all = (bias_all + bias_come)[:1]
    else:
        bias_all = lax.psum(bias_sum[:1], ("dp", "seq"))
    up_grad, up_term = finish(order, [up_a.result(), up_b.result()], share, units, TILE, up_rows)
    qkv_grad, o_grad = last_grad[:, :wide_columns], last_grad[:, wide_columns:]

    attn_term = jnp.sum(to_f(rows_of(weight)) * qkv_grad, axis=1)
    ffn_term = jnp.sum(gate_term + up_term, axis=1)
    columns = heads * HD
    room = -(-share // HD) * HD - share
    terms = jnp.pad(jnp.stack([ffn_term, attn_term]), ((0, 0), (0, room))).reshape(-1, HD)
    packed = jnp.concatenate([qkv_grad[:, columns:], bias_all.reshape(-1, HD), terms], axis=0)
    gathered = tensor_gather(packed, rank)
    term_rows = terms.shape[0]
    bias_count = bias_all.shape[1] // HD
    terms = gathered[:, share + bias_count :].reshape(ranks, 2, -1)[:, :, :share]
    ffn_gain_grad, attn_gain_grad = terms[0] + terms[1] + (terms[2] + terms[3])
    attn_gain_grad = attn_gain_grad / lax.dynamic_slice_in_dim(gain_one[0], begin, share, 0)
    ffn_gain_grad = ffn_gain_grad / lax.dynamic_slice_in_dim(gain_two[0], begin, share, 0)
    q_grad = qkv_grad[:, :columns]
    kv_parts = lax.dynamic_slice_in_dim(gathered, rank * (share // ranks), share // ranks, 1)
    k_grad = jnp.concatenate([kv_parts[2 * i] for i in range(KVH)], axis=1)
    v_grad = jnp.concatenate([kv_parts[2 * i + 1] for i in range(KVH)], axis=1)
    biases = gathered[:, share : share + bias_count]
    q_bias_grad = biases[:, :heads].reshape(-1)
    k_bias_grad = biases[0::2, heads].reshape(-1)
    v_bias_grad = biases[1::2, heads].reshape(-1)
    return (
        layer_out,
        token_grad,
        q_grad,
        q_bias_grad,
        k_grad,
        k_bias_grad,
        v_grad,
        v_bias_grad,
        o_grad,
        attn_gain_grad,
        ffn_gain_grad,
        gate_grad,
        up_grad,
        down_grad,
    )


def solution(mesh):
    in_specs = (
        P("dp", "seq", None),
        P("dp", None),
        P("dp", "seq", None),
        P(None, "tensor"),
        P("tensor"),
        P(),
        P(),
        P(),
        P(),
        P(None, "tensor"),
        P(),
        P(),
        P(None, "tensor"),
        P(None, "tensor"),
        P(None, "tensor"),
    )
    out_specs = (
        P("dp", "seq", None),
        P("dp", "seq", None),
        P(("dp", "seq"), "tensor"),
        P(),
        P(("dp", "seq", "tensor"), None),
        P(),
        P(("dp", "seq", "tensor"), None),
        P(),
        P(("dp", "seq"), "tensor"),
        P(("dp", "seq")),
        P(("dp", "seq")),
        P(("dp", "seq"), "tensor"),
        P(("dp", "seq"), "tensor"),
        P(("dp", "seq"), "tensor"),
    )
    return jax.shard_map(body, mesh=mesh, in_specs=in_specs, out_specs=out_specs, check_vma=False)
```

```python
import functools
import math

import jax
import jax.numpy as jnp
from jax import lax
from jax.experimental import pallas as pl
from jax.experimental.pallas import tpu as pltpu
from jax.sharding import PartitionSpec as P

KVH = 2
HD = 128
MOST = 1024
EPS = 1e-06
ROPE_BASE = 10000.0
NEG_FILL = -1e30
Q_BLOCK = 256
K_BLOCK = 256
MIB = 1 << 20
LIGHT = 1000
TILE = 256
PIECES = 2
SCALE = 1.0 / math.sqrt(HD)


def to_bf(value):
    return value.astype(jnp.bfloat16)


def to_f(value):
    return value.astype(jnp.float32)


def dot(left, right, left_dim=1, right_dim=0):
    return lax.dot_general(
        left,
        right,
        (((left_dim,), (right_dim,)), ((), ())),
        preferred_element_type=jnp.float32,
    )


def flipped(axis, bit):
    return [(i, i ^ (1 << bit)) for i in range(lax.axis_size(axis))]


def core_swap(value):
    return lax.ppermute(value, "tensor", flipped("tensor", 0))


def chip_swap(value):
    return lax.ppermute(value, "tensor", flipped("tensor", 1))


def core_swaps(values):
    return [core_swap(value) for value in values]


def chip_swaps(values):
    return [chip_swap(value) for value in values]


def shifted(value, hops):
    count = lax.axis_size("seq")
    route = [(i, i + hops) for i in range(count) if 0 <= i + hops < count]
    return lax.ppermute(value, "seq", route)


def cost(flops, read):
    return pl.CostEstimate(flops=flops // LIGHT, bytes_accessed=read // LIGHT, transcendentals=0)


class Order:
    def __init__(self):
        self.mark = None
        self.touched = []

    def arrived(self, *values):
        self.touched.extend(values)

    def __call__(self, kernel, args, in_specs, out_specs, out_shape, grid, flops, read, name, scalars=(), scratch=()):
        anchor = ([] if self.mark is None else [self.mark]) + self.touched
        self.touched = []
        count = len(scalars) + len(args)
        outs = len(out_shape)

        def run(*refs):
            rest = refs[count + len(anchor) :]
            kernel(*refs[:count], *rest[:outs], *rest[outs + 1 :])
            rest[outs][...] = jnp.zeros(rest[outs].shape, jnp.float32)

        *results, self.mark = pl.pallas_call(
            run,
            grid_spec=pltpu.PrefetchScalarGridSpec(
                num_scalar_prefetch=len(scalars),
                grid=grid,
                in_specs=list(in_specs) + anchors(len(anchor)),
                out_specs=list(out_specs) + [mark_spec()],
                scratch_shapes=list(scratch),
            ),
            out_shape=list(out_shape) + [MARK],
            compiler_params=pltpu.CompilerParams(vmem_limit_bytes=32 * MIB),
            cost_estimate=cost(flops, read),
            name=name,
        )(*scalars, *args, *anchor)
        return results


def first_kernel(core_ref, tok_ref, gain_ref, w_ref, b_ref, cos_ref, sin_ref, h_ref, q_ref, kv_ref):
    x = to_f(tok_ref[...])
    factor = lax.rsqrt(jnp.mean(x * x, axis=-1, keepdims=True) + EPS)
    h = to_bf(x * factor * gain_ref[...])
    h_ref[...] = h
    lin = dot(h, w_ref[...]) + b_ref[...]
    cosine = cos_ref[...]
    sine = sin_ref[...]
    heads = q_ref.shape[1] // HD
    for head in range(heads):
        part = lin[:, head * HD : (head + 1) * HD]
        q_ref[:, head * HD : (head + 1) * HD] = to_bf(
            part * cosine + pltpu.roll(part, HD // 2, 1) * sine
        )
    part = lin[:, heads * HD :]
    is_key = core_ref[0] == 0
    kv_ref[...] = to_bf(
        part * jnp.where(is_key, cosine, 1.0)
        + pltpu.roll(part, HD // 2, 1) * jnp.where(is_key, sine, 0.0)
    )


def first(core, tokens, gain, weight, bias, cosine, sine):
    total, width = tokens.shape
    columns = weight.shape[1]
    block = total // 4
    half = 2

    def flip(i, core_ref):
        return (lax.rem(i + core_ref[0] * half, 4), 0)

    def at(i, core_ref):
        return (i, 0)

    def whole(i, core_ref):
        return (0, 0)

    return pl.pallas_call(
        first_kernel,
        grid_spec=pltpu.PrefetchScalarGridSpec(
            num_scalar_prefetch=1,
            grid=(4,),
            in_specs=[
                pl.BlockSpec((block, width), flip),
                pl.BlockSpec((1, width), whole),
                pl.BlockSpec((width, columns), whole),
                pl.BlockSpec((1, columns), whole),
                pl.BlockSpec((block, HD), at),
                pl.BlockSpec((block, HD), at),
            ],
            out_specs=[
                pl.BlockSpec((block, width), at),
                pl.BlockSpec((block, columns - HD), at),
                pl.BlockSpec((block, HD), at),
            ],
        ),
        out_shape=[
            jax.ShapeDtypeStruct((total, width), jnp.bfloat16),
            jax.ShapeDtypeStruct((total, columns - HD), jnp.bfloat16),
            jax.ShapeDtypeStruct((total, HD), jnp.bfloat16),
        ],
        compiler_params=pltpu.CompilerParams(vmem_limit_bytes=32 * MIB),
        cost_estimate=cost(2 * total * width * columns, 9 * MIB),
        name="first",
    )(core, tokens, gain, weight, bias, cosine, sine)


def stacked(ref, start, count, heads):
    return jnp.concatenate(
        [ref[0, pl.ds(start, count), h * HD : (h + 1) * HD] for h in range(heads)], axis=0
    )


def bounds(start_ref, index, heads, reach):
    first_key = jnp.concatenate(
        [start_ref[0, :, pl.ds(index * Q_BLOCK, Q_BLOCK)]] * heads, axis=1
    )
    place = reach + index * Q_BLOCK + lax.broadcasted_iota(jnp.int32, (1, Q_BLOCK), 1)
    return first_key, jnp.concatenate([place] * heads, axis=1)


def gather_span(core, refs, span):
    count = len(refs) // 2
    local = refs[0].shape[1]
    for i in range(count):
        here = slice(i * local, (i + 1) * local)
        span[core, here] = refs[i][0]
        span[1 - core, here] = refs[count + i][0]


def attend_kernel(heads, blocks, pieces, low_ref, core_ref, q_ref, start_ref, *refs):
    o_ref, lse_ref, acc, span = refs[2 * pieces :]
    row = pl.program_id(0)
    wide = heads * Q_BLOCK
    reach = (pieces - 1) * q_ref.shape[1]
    gather_span(core_ref[0], refs[: 2 * pieces], span)
    for index in range(blocks):
        q = stacked(q_ref, index * Q_BLOCK, Q_BLOCK, heads)
        first_key, place = bounds(start_ref, index, heads, reach)
        acc[...] = jnp.zeros_like(acc)

        def step(j, carry):
            top, total = carry
            keys = pl.ds(pl.multiple_of(j * K_BLOCK, K_BLOCK), K_BLOCK)
            s = dot(span[0, keys], q, 1, 1) * SCALE
            key = j * K_BLOCK + lax.broadcasted_iota(jnp.int32, (K_BLOCK, wide), 0)
            s = jnp.where((key >= first_key) & (key <= place), s, NEG_FILL)
            later = jnp.maximum(top, jnp.max(s, axis=0, keepdims=True))
            p = jnp.exp(s - later)
            fade = jnp.exp(top - later)
            total = total * fade + jnp.sum(p, axis=0, keepdims=True)
            acc[...] = acc[...] * fade + dot(span[1, keys], to_bf(p), 0, 0)
            return later, total

        last = (reach + (index + 1) * Q_BLOCK - 1) // K_BLOCK + 1
        top, total = lax.fori_loop(
            low_ref[row, index],
            last,
            step,
            (jnp.full((1, wide), NEG_FILL, jnp.float32), jnp.zeros((1, wide), jnp.float32)),
        )
        out = to_bf((acc[...] / total).T)
        for h in range(heads):
            o_ref[0, index * Q_BLOCK : (index + 1) * Q_BLOCK, h * HD : (h + 1) * HD] = out[
                h * Q_BLOCK : (h + 1) * Q_BLOCK
            ]
        lse_ref[0, index : index + 1, :] = top + jnp.log(total)


def span_specs(rows, local, pieces):
    near = pl.BlockSpec((1, local, HD), lambda i, *refs: (i, 0, 0))
    far = pl.BlockSpec((1, local, HD), lambda i, *refs: (lax.rem(i + rows // 2, rows), 0, 0))
    return [near] * pieces + [far] * pieces


def attend(low, core, q, start, span, mate):
    rows, local, columns = q.shape
    pieces = len(span)
    heads = columns // HD
    blocks = local // Q_BLOCK

    def at(i, *refs):
        return (i, 0, 0)

    return pl.pallas_call(
        functools.partial(attend_kernel, heads, blocks, pieces),
        grid_spec=pltpu.PrefetchScalarGridSpec(
            num_scalar_prefetch=2,
            grid=(rows,),
            in_specs=[pl.BlockSpec((1, local, columns), at), pl.BlockSpec((1, 1, local), at)]
            + span_specs(rows, local, pieces),
            out_specs=[
                pl.BlockSpec((1, local, columns), at),
                pl.BlockSpec((1, blocks, heads * Q_BLOCK), at),
            ],
            scratch_shapes=[
                pltpu.VMEM((HD, heads * Q_BLOCK), jnp.float32),
                pltpu.VMEM((2, pieces * local, HD), jnp.bfloat16),
            ],
        ),
        out_shape=[
            jax.ShapeDtypeStruct((rows, local, columns), jnp.bfloat16),
            jax.ShapeDtypeStruct((rows, blocks, heads * Q_BLOCK), jnp.float32),
        ],
        compiler_params=pltpu.CompilerParams(vmem_limit_bytes=32 * MIB),
        cost_estimate=cost(8_000_000_000, 4 * MIB),
        name="attend",
    )(low, core, q, start, *span, *mate)


def attend_back_kernel(
    heads, blocks, pieces, low_ref, core_ref, q_ref, start_ref, g_ref, o_ref, lse_ref, cos_ref, sin_ref, *refs
):
    gq_ref, keep_ref, send_ref, acc, gk, gv, span = refs[2 * pieces :]
    row = pl.program_id(0)
    wide = heads * Q_BLOCK
    reach = (pieces - 1) * q_ref.shape[1]
    core = core_ref[0]
    gather_span(core, refs[: 2 * pieces], span)
    gk[...] = jnp.zeros_like(gk)
    gv[...] = jnp.zeros_like(gv)
    for index in range(blocks):
        q = stacked(q_ref, index * Q_BLOCK, Q_BLOCK, heads)
        g = stacked(g_ref, index * Q_BLOCK, Q_BLOCK, heads)
        o = stacked(o_ref, index * Q_BLOCK, Q_BLOCK, heads)
        inner = jnp.sum((to_f(g) * to_f(o)).T, axis=0, keepdims=True)
        lse = lse_ref[0, index : index + 1, :]
        first_key, place = bounds(start_ref, index, heads, reach)
        acc[...] = jnp.zeros_like(acc)

        def step(j, carry):
            keys = pl.ds(pl.multiple_of(j * K_BLOCK, K_BLOCK), K_BLOCK)
            k = span[0, keys]
            s = dot(k, q, 1, 1) * SCALE
            key = j * K_BLOCK + lax.broadcasted_iota(jnp.int32, (K_BLOCK, wide), 0)
            p = jnp.where((key >= first_key) & (key <= place), jnp.exp(s - lse), 0.0)
            gp = dot(span[1, keys], g, 1, 1)
            gs = to_bf(p * (gp - inner))
            gv[keys] += dot(to_bf(p), g)
            gk[keys] += dot(gs, q)
            acc[...] += dot(k, gs, 0, 0)
            return carry

        last = (reach + (index + 1) * Q_BLOCK - 1) // K_BLOCK + 1
        lax.fori_loop(low_ref[row, index], last, step, 0)
        gq = acc[...].T * SCALE
        here = slice(index * Q_BLOCK, (index + 1) * Q_BLOCK)
        cosine, sine = cos_ref[here], sin_ref[here]
        for h in range(heads):
            part = gq[h * Q_BLOCK : (h + 1) * Q_BLOCK]
            gq_ref[0, here, h * HD : (h + 1) * HD] = to_bf(
                part * cosine + pltpu.roll(part * sine, HD // 2, 1)
            )
    is_key = core == 0
    keys, values = gk[...] * SCALE, gv[...]
    keep_ref[0] = to_bf(jnp.where(is_key, keys, values))
    send_ref[0] = to_bf(jnp.where(is_key, values, keys))


def attend_back(order, low, core, q, start, span, mate, grad, out, lse, cosine, sine):
    rows, local, columns = q.shape
    pieces = len(span)
    window = pieces * local
    heads = columns // HD
    blocks = local // Q_BLOCK

    def at(i, *refs):
        return (i, 0, 0)

    table = pl.BlockSpec((local, HD), lambda i, *refs: (i, 0))
    tokens = pl.BlockSpec((1, local, columns), at)
    return order(
        functools.partial(attend_back_kernel, heads, blocks, pieces),
        [q, start, grad, out, lse, cosine, sine, *span, *mate],
        [
            tokens,
            pl.BlockSpec((1, 1, local), at),
            tokens,
            tokens,
            pl.BlockSpec((1, blocks, heads * Q_BLOCK), at),
            table,
            table,
        ]
        + span_specs(rows, local, pieces),
        [tokens, pl.BlockSpec((1, window, HD), at), pl.BlockSpec((1, window, HD), at)],
        [
            jax.ShapeDtypeStruct((rows, local, columns), jnp.bfloat16),
            jax.ShapeDtypeStruct((rows, window, HD), jnp.bfloat16),
            jax.ShapeDtypeStruct((rows, window, HD), jnp.bfloat16),
        ],
        (rows,),
        20_000_000_000,
        6 * MIB,
        "attend_back",
        scalars=(low, core),
        scratch=[
            pltpu.VMEM((HD, heads * Q_BLOCK), jnp.float32),
            pltpu.VMEM((window, HD), jnp.float32),
            pltpu.VMEM((window, HD), jnp.float32),
            pltpu.VMEM((2, window, HD), jnp.bfloat16),
        ],
    )


def fold_kernel(keep_ref, come_ref, own_ref, *send_refs):
    local = own_ref.shape[1]
    total = to_f(keep_ref[0]) + to_f(come_ref[0])
    reach = total.shape[0] - local
    own_ref[0] = total[reach:]
    for hop, ref in enumerate(send_refs, 1):
        ref[0] = to_bf(total[reach - hop * local : reach - (hop - 1) * local])


def fold(order, keep, come, local):
    rows, window = keep.shape[:2]
    hops = window // local - 1
    out = pl.BlockSpec((1, local, HD), lambda i: (i, 0, 0))
    return order(
        fold_kernel,
        [keep, come],
        [
            pl.BlockSpec((1, window, HD), lambda i: (i, 0, 0)),
            pl.BlockSpec((1, window, HD), lambda i: (lax.rem(i + rows // 2, rows), 0, 0)),
        ],
        [out] * (hops + 1),
        [jax.ShapeDtypeStruct((rows, local, HD), jnp.float32)]
        + [jax.ShapeDtypeStruct((rows, local, HD), jnp.bfloat16)] * hops,
        (rows,),
        0,
        4 * MIB,
        "fold",
    )


def carry_kernel(piece_ref, come_ref, out_ref):
    out_ref[...] = to_bf(to_f(piece_ref[...]) + to_f(come_ref[...]))


def carry(order, piece, come):
    rows, local, columns = piece.shape
    at = pl.BlockSpec((1, local, columns), lambda i: (i, 0, 0))
    return order(
        carry_kernel,
        [piece, come],
        [at, at],
        [at],
        [jax.ShapeDtypeStruct(piece.shape, jnp.bfloat16)],
        (rows,),
        0,
        2 * MIB,
        "carry",
    )[0]


def bias_kernel(left_ref, right_ref, out_ref):
    out_ref[...] = left_ref[...] + right_ref[...]


def bias_add(order, left, right):
    whole = pl.BlockSpec(left.shape, lambda i: (0, 0))
    return order(
        bias_kernel,
        [left, right],
        [whole, whole],
        [whole],
        [jax.ShapeDtypeStruct(left.shape, jnp.float32)],
        (1,),
        0,
        MIB,
        "bias",
    )[0]


def join_kernel(hops, core_ref, gq_ref, cos_ref, sin_ref, own_ref, *refs):
    out_ref, sum_ref = refs[-2:]
    columns = gq_ref.shape[2]
    grad = own_ref[0]
    for ref in refs[:hops]:
        grad = grad + to_f(ref[0])
    is_key = core_ref[0] == 0
    cosine = jnp.where(is_key, cos_ref[...], 1.0)
    sine = jnp.where(is_key, sin_ref[...], 0.0)
    kv = to_bf(grad * cosine + pltpu.roll(grad * sine, HD // 2, 1))
    q = gq_ref[0]
    out_ref[:, :columns] = q
    out_ref[:, columns:] = kv

    @pl.when(pl.program_id(0) == 0)
    def _():
        sum_ref[...] = jnp.zeros(sum_ref.shape, jnp.float32)

    sum_ref[:, :columns] += jnp.sum(to_f(q), axis=0, keepdims=True)
    sum_ref[:, columns:] += jnp.sum(to_f(kv), axis=0, keepdims=True)


def join(order, core, grad_q, own, comes, cosine, sine):
    rows, local, columns = grad_q.shape
    wide = columns + HD

    def at(i, *refs):
        return (i, 0, 0)

    piece = pl.BlockSpec((1, local, HD), at)
    table = pl.BlockSpec((local, HD), lambda i, *refs: (i, 0))
    return order(
        functools.partial(join_kernel, len(comes)),
        [grad_q, cosine, sine, own, *comes],
        [pl.BlockSpec((1, local, columns), at), table, table, piece] + [piece] * len(comes),
        [
            pl.BlockSpec((local, wide), lambda i, *refs: (i, 0)),
            pl.BlockSpec((8, wide), lambda i, *refs: (0, 0)),
        ],
        [
            jax.ShapeDtypeStruct((rows * local, wide), jnp.bfloat16),
            jax.ShapeDtypeStruct((8, wide), jnp.float32),
        ],
        (rows,),
        0,
        4 * MIB,
        "join",
        scalars=(core,),
    )


def mixed_back_kernel(w_ref, *refs):
    rows = refs[0].shape[0]
    for i, ref in enumerate(refs[:-1]):
        refs[-1][i * rows : (i + 1) * rows] = to_bf(dot(ref[...], w_ref[...]))


def mixed_back(order, pieces, weight):
    rows, width = pieces[0].shape
    total = rows * len(pieces)
    columns = weight.shape[1]

    def whole(i):
        return (0, 0)

    return order(
        mixed_back_kernel,
        [weight, *pieces],
        [pl.BlockSpec((width, columns), whole)] + [pl.BlockSpec((rows, width), whole)] * len(pieces),
        [pl.BlockSpec((total, columns), whole)],
        [jax.ShapeDtypeStruct((total, columns), jnp.bfloat16)],
        (1,),
        2 * total * width * columns,
        6 * MIB,
        "mixed_back",
    )[0]


def place_kernel(core_ref, *refs):
    for i, ref in enumerate(refs[:-1]):

        @pl.when(pl.program_id(0) == i)
        def _(ref=ref):
            refs[-1][...] = ref[...]


def place(order, core, pieces):
    rows, width = pieces[0].shape
    count = len(pieces)
    return order(
        place_kernel,
        list(pieces),
        [pl.BlockSpec((rows, width), lambda i, core_ref: (0, 0))] * count,
        [pl.BlockSpec((rows, width), lambda i, core_ref: (lax.rem(i + core_ref[0] * (count // 2), count), 0))],
        [jax.ShapeDtypeStruct((rows * count, width), pieces[0].dtype)],
        (count,),
        0,
        8 * rows * width,
        "place",
        scalars=(core,),
    )[0]


def anchors(count):
    return [pl.BlockSpec(memory_space=pl.ANY)] * count


MARK = jax.ShapeDtypeStruct((8, HD), jnp.float32)


def mark_spec():
    return pl.BlockSpec((8, HD), lambda *refs: (0, 0))


def grad_hidden_kernel(g_ref, w_ref, out_ref):
    out_ref[...] = to_bf(dot(g_ref[...], w_ref[...], 1, 1))


def grad_hidden_of(order, grad, weight):
    total, width = grad.shape
    hidden = weight.shape[0]
    return order(
        grad_hidden_kernel,
        [grad, weight],
        [pl.BlockSpec((total, width), lambda i: (0, 0)), pl.BlockSpec((TILE, width), lambda i: (i, 0))],
        [pl.BlockSpec((total, TILE), lambda i: (0, i))],
        [jax.ShapeDtypeStruct((total, hidden), jnp.bfloat16)],
        (pl.cdiv(hidden, TILE),),
        2 * total * width * hidden,
        15 * MIB,
        "grad_hidden",
    )[0]


def gated_kernel(gh_ref, gw_ref, uw_ref, *refs):
    hid_ref, gg_ref, gu_ref = refs[-3:]
    rows = refs[0].shape[0]
    for part, ref in enumerate(refs[:-3]):
        here = slice(part * rows, (part + 1) * rows)
        h = ref[...]
        gate = dot(h, gw_ref[...], 1, 1)
        up = dot(h, uw_ref[...], 1, 1)
        grad = to_f(gh_ref[here])
        sigma = 1.0 / (1.0 + jnp.exp(-gate))
        swish = gate * sigma
        hid_ref[here] = to_bf(swish * up)
        gu_ref[here] = to_bf(grad * swish)
        gg_ref[here] = to_bf(grad * up * sigma * (1.0 + gate * (1.0 - sigma)))


def gated(order, pieces, grad_hidden, gate_weight, up_weight):
    rows, width = pieces[0].shape
    total = rows * len(pieces)
    hidden = gate_weight.shape[0]
    column = pl.BlockSpec((total, TILE), lambda i: (0, i))
    weight = pl.BlockSpec((TILE, width), lambda i: (i, 0))
    shape = jax.ShapeDtypeStruct((total, hidden), jnp.bfloat16)
    return order(
        gated_kernel,
        [grad_hidden, gate_weight, up_weight, *pieces],
        [column, weight, weight] + [pl.BlockSpec((rows, width), lambda i: (0, 0))] * len(pieces),
        [column] * 3,
        [shape] * 3,
        (pl.cdiv(hidden, TILE),),
        4 * total * width * hidden,
        30 * MIB,
        "gated",
    )


def share_kernel(plan, lefts, rights, extra, halves, groups, pick_ref, blocks_ref, *refs):
    step = pl.program_id(0)
    left_refs, right_refs = refs[:lefts], refs[lefts : lefts + rights]
    refs = refs[lefts + rights :]
    if extra:
        extra_ref, refs = refs[0], refs[1:]
    for left, right, begin, end, shift, columns, target in plan:

        @pl.when((step >= begin) & (step < end))
        def _(left=left, right=right, shift=shift, columns=columns, target=target):
            out = dot(left_refs[left][...], right_refs[right][...])
            if extra:
                out = out + to_f(extra_ref[...])
            tile = out.shape[1]
            spot = (step + shift) * tile + lax.broadcasted_iota(jnp.int32, (1, tile), 1)
            out = to_bf(jnp.where(spot < columns, out, 0.0))
            if groups:
                share = out.shape[0] // (groups[0] * groups[1])
                for i in range(groups[0]):
                    for j in range(groups[1]):
                        here = (j * groups[0] + i) * share
                        there = (i * groups[1] + j) * share
                        refs[target][here : here + share] = out[there : there + share]
                return
            if not halves:
                refs[target][...] = out
                return
            send_ref, keep_ref, rows = refs
            rows[...] = out
            share = send_ref.shape[0] // (2 * halves)
            for i in range(2 * halves):
                here = slice(i * share, (i + 1) * share)
                send_ref[here] = rows[pl.ds(pl.multiple_of(blocks_ref[i] * share, share), share)]
                keep_ref[here] = rows[pl.ds(pl.multiple_of(blocks_ref[2 * halves + i] * share, share), share)]


def clipped(rows, tile, begin, count, shift=0):
    return pl.BlockSpec((rows, tile), lambda i, *refs: (0, jnp.clip(i - begin, 0, count - 1) + shift))


def share_of(order, lefts, rights, parts, part, pick, tile, extra=None, blocks=None, groups=None):
    tokens = lefts[0].shape[1]
    plan, at = [], 0
    starts, sizes, right_at = {}, {}, {}
    for left, right, skip, count, target in parts:
        plan.append((left, right, at, at + count, skip - at, rights[right].shape[1], target))
        starts.setdefault(target, at)
        sizes[target] = sizes.get(target, 0) + count
        first, tiles, low = right_at.get(right, (at, 0, skip))
        right_at[right] = (first, tiles + count, low)
        at += count
    halves = 0
    extras = [] if extra is None else [extra]
    scratch = []
    if blocks is None:
        blocks = jnp.zeros((1,), jnp.int32)
        outs = [clipped(part, tile, starts[t], sizes[t]) for t in sorted(sizes)]
        shapes = [jax.ShapeDtypeStruct((part, sizes[t] * tile), jnp.bfloat16) for t in sorted(sizes)]
    else:
        halves = blocks.shape[0] // 4
        outs = [clipped(part // 2, tile, 0, at)] * 2
        shapes = [jax.ShapeDtypeStruct((part // 2, at * tile), jnp.bfloat16)] * 2
        scratch = [pltpu.VMEM((part, tile), jnp.bfloat16)]
    return order(
        functools.partial(share_kernel, plan, len(lefts), len(rights), len(extras), halves, groups),
        [*lefts, *rights, *extras],
        [pl.BlockSpec((part, tokens), lambda i, pick_ref, blocks_ref: (pick_ref[0], 0))] * len(lefts)
        + [clipped(tokens, tile, *right_at[r]) for r in range(len(rights))]
        + [clipped(part, tile, 0, at)] * len(extras),
        outs,
        shapes,
        (at,),
        2 * part * tokens * at * tile,
        2 * (part * tokens + (part + tokens) * at * tile),
        "share",
        scalars=(jnp.asarray(pick, jnp.int32).reshape(1), blocks),
        scratch=scratch,
    )


def relay_kernel(keep_ref, come_ref, out_ref):
    out_ref[...] = to_bf(to_f(keep_ref[...]) + to_f(come_ref[...]))


def relay(order, keep, come, share):
    rows, columns = keep.shape
    pair = pl.BlockSpec((share, columns), lambda i: (2 * i + 1, 0))
    return order(
        relay_kernel,
        [keep, come],
        [pair, pair],
        [pl.BlockSpec((share, columns), lambda i: (i, 0))],
        [jax.ShapeDtypeStruct((rows // 2, columns), jnp.bfloat16)],
        (rows // (2 * share),),
        0,
        3 * rows * columns,
        "relay",
    )[0]


def finish_kernel(plan, columns, gains, *refs):
    out_ref = refs[-2] if gains else refs[-1]
    step = pl.program_id(0)
    tile = out_ref.shape[1]
    for begin, end, first, count in plan:

        @pl.when((step >= begin) & (step < end))
        def _(first=first, count=count):
            out = to_f(refs[first][...])
            for ref in refs[first + 1 : first + count]:
                out = out + to_f(ref[...])
            out_ref[...] = out
            if gains:
                spot = step * tile + lax.broadcasted_iota(jnp.int32, (1, tile), 1)
                terms = jnp.where(spot < columns, out * to_f(refs[-3][...]), 0.0)
                total = terms[:, :HD]
                for i in range(HD, tile, HD):
                    total = total + terms[:, i : i + HD]

                @pl.when(step == 0)
                def _():
                    refs[-1][...] = total

                @pl.when(step > 0)
                def _():
                    refs[-1][...] += total


def finish(order, chunks, share, columns, tile, weight=None):
    plan, specs, args, at = [], [], [], 0
    for chunk in chunks:
        count = chunk[0].shape[1] // tile
        plan.append((at, at + count, len(args), len(chunk)))
        specs += [clipped(share, tile, at, count)] * len(chunk)
        args += chunk
        at += count
    column = pl.BlockSpec((share, tile), lambda i: (0, i))
    outs, shapes = [column], [jax.ShapeDtypeStruct((share, columns), jnp.float32)]
    if weight is not None:
        args.append(weight)
        specs.append(column)
        outs.append(pl.BlockSpec((share, HD), lambda i: (0, 0)))
        shapes.append(jax.ShapeDtypeStruct((share, HD), jnp.float32))
    return order(
        functools.partial(finish_kernel, plan, columns, weight is not None),
        args,
        specs,
        outs,
        shapes,
        (at,),
        0,
        14 * share * columns,
        "finish",
    )


def narrow_kernel(pairs, extras, right_dim, *refs):
    out = dot(refs[0][...], refs[1][...], 1, right_dim)
    for i in range(1, pairs):
        out = out + dot(refs[2 * i][...], refs[2 * i + 1][...], 1, right_dim)
    extra = refs[2 * pairs : 2 * pairs + extras]
    outs = refs[2 * pairs + extras :]
    if extras:
        out = out + jnp.concatenate([to_f(ref[...]) for ref in extra], axis=0)
    rows = outs[0].shape[0]
    for i, ref in enumerate(outs):
        ref[...] = to_bf(out[i * rows : (i + 1) * rows])


def narrow(order, pairs, index, extra=(), right_dim=0):
    total, hidden = pairs[0][0].shape
    width = pairs[0][1].shape[1 - right_dim]
    half = total // 2
    piece = half // PIECES
    column = pl.BlockSpec((piece, TILE), lambda i: (0, i))
    right = (
        pl.BlockSpec((TILE, hidden), lambda i: (i, 0))
        if right_dim
        else pl.BlockSpec((hidden, TILE), lambda i: (0, i))
    )
    return order(
        functools.partial(narrow_kernel, len(pairs), len(extra), right_dim),
        [item for pair in pairs for item in pair] + list(extra),
        [pl.BlockSpec((half, hidden), lambda i: (index, 0)), right] * len(pairs) + [column] * len(extra),
        [column] * PIECES,
        [jax.ShapeDtypeStruct((piece, width), jnp.bfloat16)] * PIECES,
        (width // TILE,),
        2 * len(pairs) * half * width * hidden,
        2 * len(pairs) * (half + width) * hidden + 2 * half * width,
        "narrow",
    )


def piece_specs(piece, width, block):
    steps = piece // block
    return [
        pl.BlockSpec((block, width), lambda i, *refs, j=j: (jnp.clip(i - j * steps, 0, steps - 1), 0))
        for j in range(PIECES)
    ]


def pick_piece(refs):
    value = refs[0][...]
    for j, ref in enumerate(refs[1:], 1):
        value = jnp.where(pl.program_id(0) >= 4 * j // len(refs), ref[...], value)
    return value


def put_piece(refs, value):
    steps = 4 // len(refs)
    for j, ref in enumerate(refs):

        @pl.when(lax.div(pl.program_id(0), steps) == j)
        def _(ref=ref):
            ref[...] = value


def turn_kernel(*refs):
    rows = refs[0].shape[0]
    for i, ref in enumerate(refs[:-1]):
        refs[-1][:, i * rows : (i + 1) * rows] = ref[...].T


def turn(order, pieces):
    rows, width = pieces[0].shape
    total = rows * len(pieces)
    return order(
        turn_kernel,
        list(pieces),
        [pl.BlockSpec((rows, TILE), lambda i: (0, i))] * len(pieces),
        [pl.BlockSpec((TILE, total), lambda i: (i, 0))],
        [jax.ShapeDtypeStruct((width, total), jnp.bfloat16)],
        (width // TILE,),
        0,
        4 * total * width,
        "turn",
    )[0]


def grad_out_kernel(core_ref, cot_ref, valid_ref, out_ref, turned_ref):
    out = to_bf(to_f(cot_ref[...]) * valid_ref[...])
    out_ref[...] = out
    turned_ref[...] = out.T


def grad_out_of(order, core, cotangent, valid):
    total, width = cotangent.shape
    block = total // 4
    return order(
        grad_out_kernel,
        [cotangent, valid],
        [
            pl.BlockSpec((block, width), lambda i, core_ref: (lax.rem(i + core_ref[0] * 2, 4), 0)),
            pl.BlockSpec((block, 1), lambda i, core_ref: (i, 0)),
        ],
        [
            pl.BlockSpec((block, width), lambda i, core_ref: (i, 0)),
            pl.BlockSpec((width, block), lambda i, core_ref: (0, i)),
        ],
        [
            jax.ShapeDtypeStruct((total, width), jnp.bfloat16),
            jax.ShapeDtypeStruct((width, total), jnp.bfloat16),
        ],
        (4,),
        0,
        6 * total * width,
        "grad_out",
        scalars=(core,),
    )


def middle_kernel(core_ref, tok_ref, gain_ref, *refs):
    mine, come = pick_piece(refs[:PIECES]), pick_piece(refs[PIECES : 2 * PIECES])
    mid_ref, *h_refs = refs[2 * PIECES :]
    middle = to_f(tok_ref[...]) + (to_f(mine) + to_f(come))
    factor = lax.rsqrt(jnp.mean(middle * middle, axis=-1, keepdims=True) + EPS)
    mid_ref[...] = middle
    put_piece(h_refs, to_bf(middle * factor * gain_ref[...]))


def middle_of(order, core, tokens, mine, come, gain):
    piece, width = mine[0].shape
    half = piece * PIECES
    block = half // 4
    specs = piece_specs(piece, width, block)
    middle, *h = order(
        middle_kernel,
        [tokens, gain, *mine, *come],
        [
            pl.BlockSpec((block, width), lambda i, core_ref: (core_ref[0] * 4 + i, 0)),
            pl.BlockSpec((1, width), lambda i, core_ref: (0, 0)),
        ]
        + specs * 2,
        [pl.BlockSpec((block, width), lambda i, core_ref: (i, 0))] + specs,
        [jax.ShapeDtypeStruct((half, width), jnp.float32)]
        + [jax.ShapeDtypeStruct((piece, width), jnp.bfloat16)] * PIECES,
        (4,),
        0,
        9 * MIB,
        "middle",
        scalars=(core,),
    )
    return middle, h


def norm_back_kernel(core_ref, x_ref, gain_ref, up_ref, *refs):
    mine, come = pick_piece(refs[:PIECES]), pick_piece(refs[PIECES : 2 * PIECES])
    outs = refs[2 * PIECES :]
    grad = to_f(mine) + to_f(come)
    x = to_f(x_ref[...])
    factor = lax.rsqrt(jnp.mean(x * x, axis=-1, keepdims=True) + EPS)
    normed = x * factor
    weighted = grad * gain_ref[...]
    inner = jnp.mean(weighted * normed, axis=-1, keepdims=True)
    out = to_f(up_ref[...]) + factor * (weighted - normed * inner)
    if len(outs) > PIECES:
        outs[0][...] = out
        put_piece(outs[1:], to_bf(out))
    else:
        put_piece(outs, out)


def norm_back(order, core, mine, come, x, gain, up, by_core):
    piece, width = mine[0].shape
    half = piece * PIECES
    block = half // 4
    at = pl.BlockSpec((block, width), lambda i, core_ref: (i, 0))
    picked = pl.BlockSpec((block, width), lambda i, core_ref: (core_ref[0] * 4 + i, 0))
    specs = piece_specs(piece, width, block)
    if by_core:
        shapes = [jax.ShapeDtypeStruct((piece, width), jnp.float32)] * PIECES
    else:
        shapes = [jax.ShapeDtypeStruct((half, width), jnp.float32)]
        shapes += [jax.ShapeDtypeStruct((piece, width), jnp.bfloat16)] * PIECES
    return order(
        norm_back_kernel,
        [x, gain, up, *mine, *come],
        [picked if by_core else at, pl.BlockSpec((1, width), lambda i, core_ref: (0, 0)), at] + specs * 2,
        specs if by_core else [at] + specs,
        shapes,
        (4,),
        0,
        10 * MIB,
        "norm_back",
        scalars=(core,),
    )


def layer_kernel(middle_ref, *refs):
    mine, come = pick_piece(refs[:PIECES]), pick_piece(refs[PIECES : 2 * PIECES])
    put_piece(refs[2 * PIECES :], to_bf(middle_ref[...] + (to_f(mine) + to_f(come))))


def layer_of(order, middle, mine, come):
    piece, width = mine[0].shape
    block = piece * PIECES // 4
    specs = piece_specs(piece, width, block)
    return order(
        layer_kernel,
        [middle, *mine, *come],
        [pl.BlockSpec((block, width), lambda i: (i, 0))] + specs * 2,
        specs,
        [jax.ShapeDtypeStruct((piece, width), jnp.bfloat16)] * PIECES,
        (4,),
        0,
        5 * MIB,
        "layer",
    )


def tensor_gather(value, rank):
    mate = core_swap(value)
    pair = jnp.where(lax.rem(rank, 2) == 0, jnp.stack([value, mate]), jnp.stack([mate, value]))
    come = chip_swap(pair)
    return jnp.where(
        lax.div(rank, 2) == 0,
        jnp.concatenate([pair, come], axis=0),
        jnp.concatenate([come, pair], axis=0),
    )


def body(
    tokens,
    lengths,
    cotangent,
    q_weight,
    q_bias,
    k_weight,
    k_bias,
    v_weight,
    v_bias,
    o_weight,
    attn_gain,
    ffn_gain,
    gate_weight,
    up_weight,
    down_weight,
):
    rows, local, width = tokens.shape
    total = rows * local
    half = total // 2
    heads = q_weight.shape[1] // HD
    ranks = lax.axis_size("tensor")
    seqs = lax.axis_size("seq")
    rank = lax.axis_index("tensor")
    dp_index = lax.axis_index("dp")
    seq_index = lax.axis_index("seq")
    core = lax.rem(rank, 2)
    head = lax.div(rank, 2)
    core_one = core.reshape(1)
    hops = min(seqs - 1, -(-(MOST - 1) // local))
    reach = hops * local

    def own_first(value):
        turned = jnp.concatenate([value[rows // 2 :], value[: rows // 2]], axis=0)
        return jnp.where(core == 0, value, turned)

    slots = jnp.arange(lengths.shape[1], dtype=jnp.int32)
    lens = own_first(lengths)
    ends = jnp.sum(jnp.where(slots[None, :] <= slots[:, None], lens[:, None, :], 0), axis=2)
    spot = seq_index * local + jnp.arange(local, dtype=jnp.int32)
    begun = jnp.max(
        jnp.where(ends[:, None, :] <= spot[None, :, None], ends[:, None, :], 0), axis=2
    )
    valid = to_f(spot[None, :] < ends[:, -2:-1])
    position = (spot[None, :] - begun).reshape(total, 1)
    freqs = ROPE_BASE ** (-(jnp.arange(HD // 2, dtype=jnp.float32) * 2.0) / HD)
    angles = to_f(position) * freqs[None, :]
    cosine, sine = jnp.cos(angles), jnp.sin(angles)
    cosine = jnp.concatenate([cosine, cosine], axis=1)
    sine = jnp.concatenate([-sine, sine], axis=1)
    start = begun - (seq_index * local - reach)
    low = jnp.maximum(lax.div(jnp.maximum(start[:, ::Q_BLOCK], 0), K_BLOCK), 0)
    start = start.reshape(rows, 1, local)

    key_side = core == 0
    kv_weight = jnp.where(
        key_side,
        lax.dynamic_slice_in_dim(k_weight, head * HD, HD, 1),
        lax.dynamic_slice_in_dim(v_weight, head * HD, HD, 1),
    )
    kv_bias = jnp.where(
        key_side,
        lax.dynamic_slice_in_dim(k_bias, head * HD, HD, 0),
        lax.dynamic_slice_in_dim(v_bias, head * HD, HD, 0),
    )
    weight = jnp.concatenate([q_weight, kv_weight], axis=1)
    bias = to_f(jnp.concatenate([q_bias, kv_bias])).reshape(1, -1)
    gain_one = to_f(attn_gain).reshape(1, width)
    gain_two = to_f(ffn_gain).reshape(1, width)

    h_one, q_rot, kv = first(
        core_one, tokens.reshape(total, width), gain_one, weight, bias, cosine, sine
    )
    kv = kv.reshape(rows, local, HD)
    span = [shifted(kv, h) for h in range(hops, 0, -1)] + [kv]
    mate = [core_swap(piece) for piece in span]
    q_rows = q_rot.reshape(rows, local, heads * HD)
    mixed_rows, lse = attend(low, core_one, q_rows, start, span, mate)
    mixed = mixed_rows.reshape(total, heads * HD)

    order = Order()
    flat_tokens = tokens.reshape(total, width)
    dps = lax.axis_size("dp")
    near_pair = dps == 2 and seqs == 4
    part = width // dps
    share = part // seqs
    gate_t, up_t, down_t = gate_weight.T, up_weight.T, down_weight.T
    units = gate_t.shape[0]
    tiles = -(-units // TILE)
    cut = (tiles + 1) // 2
    long = -(-2 * tiles // 3)
    one, two = seq_index ^ 1, seq_index ^ 2
    three = seq_index ^ 3
    quad = jnp.stack([one, three, seq_index, two])

    begin = (dp_index * seqs + seq_index) * share

    def rows_of(value):
        return lax.dynamic_slice_in_dim(value, begin, share, 0)

    class Rows:
        def __init__(self, lefts, rights, parts, tile=TILE, sent=None):
            self.args = (order, lefts, rights, parts)
            self.tile = tile
            if not near_pair:
                (whole,) = share_of(*self.args, width, 0, tile)
                self.whole = lax.psum_scatter(whole, ("dp", "seq"), scatter_dimension=0, tiled=True)
                return
            if sent is None:
                (sent,) = share_of(*self.args, part, 1 - dp_index, tile)
            self.come = lax.ppermute(sent, "dp", flipped("dp", 0))

        def own(self):
            if near_pair:
                send, self.keep = share_of(*self.args, part, dp_index, self.tile, self.come, quad)
                self.come = lax.ppermute(send, "seq", flipped("seq", 0))

        def relay(self):
            if near_pair:
                sent = relay(order, self.keep, self.come, share)
                self.last = lax.ppermute(sent, "seq", flipped("seq", 1))

        def settled(self):
            if near_pair:
                order.arrived(self.last)

        def result(self):
            return [self.keep, self.come, self.last] if near_pair else [self.whole]

    class SeqFirst(Rows):
        def __init__(self, lefts, rights, parts, tile=TILE):
            if not near_pair:
                super().__init__(lefts, rights, parts, tile)
                return
            (whole,) = share_of(order, lefts, rights, parts, width, 0, tile, None, None, (dps, seqs))
            self.mine = lax.psum_scatter(whole, "seq", scatter_dimension=0, tiled=True)

        def across(self):
            if near_pair:
                sent = lax.dynamic_slice_in_dim(self.mine, (1 - dp_index) * share, share, 0)
                self.mine = lax.dynamic_slice_in_dim(self.mine, dp_index * share, share, 0)
                order.arrived(sent, self.mine)
                self.come = lax.ppermute(sent, "dp", flipped("dp", 0))

        def settled(self):
            if near_pair:
                order.arrived(self.come)

        def result(self):
            return [self.mine, self.come] if near_pair else [self.whole]

    class Scattered(Rows):
        def own(self):
            if near_pair:
                (mine,) = share_of(*self.args, part, dp_index, self.tile, self.come)
                self.whole = lax.psum_scatter(mine, "seq", scatter_dimension=0, tiled=True)

        def settled(self):
            order.arrived(self.whole)

        def result(self):
            return [self.whole]

    sent = core_swaps(narrow(order, [(mixed, o_weight)], 1, (), 1))
    mine = narrow(order, [(mixed, o_weight)], 0, sent, 1)
    come = chip_swaps(mine)
    grad_ffn, grad_ffn_t = grad_out_of(
        order, core_one, cotangent.reshape(total, width), valid.reshape(total, 1)
    )
    gate_rows, up_rows = rows_of(gate_weight), rows_of(up_weight)
    order.arrived(gate_rows, up_rows)
    grad_hidden = grad_hidden_of(order, grad_ffn, down_t)
    h_one_t = turn(order, [h_one])
    middle, h_two = middle_of(order, core_one, flat_tokens, mine, come, gain_two)
    h_two += core_swaps(h_two)
    hidden, grad_gate, grad_up = gated(order, h_two, grad_hidden, gate_t, up_t)

    down_b = SeqFirst([grad_ffn_t], [hidden], [(0, 0, cut, tiles - cut, 0)])
    down_a = Rows([grad_ffn_t], [hidden], [(0, 0, 0, cut, 0)])
    pairs = [(grad_gate, gate_t), (grad_up, up_t)]
    sent = core_swaps(narrow(order, pairs, 1))
    mine = narrow(order, pairs, 0, sent)
    come = chip_swaps(mine)
    h_two_t = turn(order, h_two)
    if near_pair:
        sends = share_of(
            order,
            [h_two_t],
            [grad_gate, grad_up],
            [(0, 0, 0, tiles, 0), (0, 1, 0, long, 1), (0, 1, long, tiles - long, 2)],
            part,
            1 - dp_index,
            TILE,
        )
    else:
        sends = [None] * 3

    def half_rows(kind, right, begin, end, sent):
        return kind([h_two_t], [right], [(0, 0, begin, end - begin, 0)], TILE, sent)

    gate = half_rows(Scattered, grad_gate, 0, tiles, sends[0])
    up_a = half_rows(Rows, grad_up, 0, long, sends[1])
    up_b = half_rows(Rows, grad_up, long, tiles, sends[2])
    down_a.own()
    grad_middle, *branch = norm_back(order, core_one, mine, come, middle, gain_two, grad_ffn, False)
    branch += core_swaps(branch)
    grad_mixed = mixed_back(order, branch, o_weight).reshape(rows, local, heads * HD)
    grad_q_rows, keep, sent = attend_back(
        order, low, core_one, q_rows, start, span, mate, grad_mixed, mixed_rows, lse, cosine, sine
    )
    both_come = core_swap(sent)
    branch_t = turn(order, branch)
    down_a.relay()
    own_kv, *pieces = fold(order, keep, both_come, local)
    moving = shifted(pieces[-1], -1) if pieces else None
    ffn_sent = core_swaps(narrow(order, [(hidden, down_t)], 1))
    for piece in pieces[-2::-1]:
        moving = shifted(carry(order, piece, moving), -1)
    grad_qkv, bias_sum = join(
        order, core_one, grad_q_rows, own_kv, [] if moving is None else [moving], cosine, sine
    )
    sent = core_swaps(narrow(order, [(grad_qkv, weight)], 1, (), 1))
    down_b.across()
    mine = narrow(order, [(grad_qkv, weight)], 0, sent, 1)
    come = chip_swaps(mine)
    gate.own()
    last_parts = [(0, 0, 0, grad_qkv.shape[1] // HD, 0), (1, 1, 0, heads, 0)]
    last = Rows([h_one_t, branch_t], [grad_qkv, mixed], last_parts, HD)
    ffn_mine = narrow(order, [(hidden, down_t)], 0, ffn_sent)
    token = norm_back(order, core_one, mine, come, flat_tokens, gain_one, grad_middle, True)
    token += core_swaps(token)
    ffn_come = chip_swaps(ffn_mine)
    up_a.own()
    token_grad = place(order, core_one, token).reshape(rows, local, width)
    layer = layer_of(order, middle, ffn_mine, ffn_come)
    layer += core_swaps(layer)
    last.own()
    layer_out = place(order, core_one, layer).reshape(rows, local, width)
    up_a.relay()
    down_a.settled()
    up_b.own()
    last.relay()
    if near_pair:
        bias_come = lax.ppermute(bias_sum, "dp", flipped("dp", 0))
        bias_all = bias_add(order, bias_sum, bias_come)
        bias_come = lax.ppermute(bias_all, "seq", flipped("seq", 0))
    up_a.settled()
    up_b.relay()
    (down_grad,) = finish(order, [down_a.result(), down_b.result()], share, units, TILE)
    gate_grad, gate_term = finish(order, [gate.result()], share, units, TILE, gate_rows)
    wide_columns = grad_qkv.shape[1]
    (last_grad,) = finish(order, [last.result()], share, wide_columns + heads * HD, HD)
    if near_pair:
        bias_all = bias_add(order, bias_all, bias_come)
        bias_come = lax.ppermute(bias_all, "seq", flipped("seq", 1))
        bias_all = (bias_all + bias_come)[:1]
    else:
        bias_all = lax.psum(bias_sum[:1], ("dp", "seq"))
    up_grad, up_term = finish(order, [up_a.result(), up_b.result()], share, units, TILE, up_rows)
    qkv_grad, o_grad = last_grad[:, :wide_columns], last_grad[:, wide_columns:]

    attn_term = jnp.sum(to_f(rows_of(weight)) * qkv_grad, axis=1)
    ffn_term = jnp.sum(gate_term + up_term, axis=1)
    columns = heads * HD
    room = -(-share // HD) * HD - share
    terms = jnp.pad(jnp.stack([ffn_term, attn_term]), ((0, 0), (0, room))).reshape(-1, HD)
    packed = jnp.concatenate([qkv_grad[:, columns:], bias_all.reshape(-1, HD), terms], axis=0)
    gathered = tensor_gather(packed, rank)
    term_rows = terms.shape[0]
    bias_count = bias_all.shape[1] // HD
    terms = gathered[:, share + bias_count :].reshape(ranks, 2, -1)[:, :, :share]
    ffn_gain_grad, attn_gain_grad = terms[0] + terms[1] + (terms[2] + terms[3])
    attn_gain_grad = attn_gain_grad / lax.dynamic_slice_in_dim(gain_one[0], begin, share, 0)
    ffn_gain_grad = ffn_gain_grad / lax.dynamic_slice_in_dim(gain_two[0], begin, share, 0)
    q_grad = qkv_grad[:, :columns]
    kv_parts = lax.dynamic_slice_in_dim(gathered, rank * (share // ranks), share // ranks, 1)
    k_grad = jnp.concatenate([kv_parts[2 * i] for i in range(KVH)], axis=1)
    v_grad = jnp.concatenate([kv_parts[2 * i + 1] for i in range(KVH)], axis=1)
    biases = gathered[:, share : share + bias_count]
    q_bias_grad = biases[:, :heads].reshape(-1)
    k_bias_grad = biases[0::2, heads].reshape(-1)
    v_bias_grad = biases[1::2, heads].reshape(-1)
    return (
        layer_out,
        token_grad,
        q_grad,
        q_bias_grad,
        k_grad,
        k_bias_grad,
        v_grad,
        v_bias_grad,
        o_grad,
        attn_gain_grad,
        ffn_gain_grad,
        gate_grad,
        up_grad,
        down_grad,
    )


def solution(mesh):
    in_specs = (
        P("dp", "seq", None),
        P("dp", None),
        P("dp", "seq", None),
        P(None, "tensor"),
        P("tensor"),
        P(),
        P(),
        P(),
        P(),
        P(None, "tensor"),
        P(),
        P(),
        P(None, "tensor"),
        P(None, "tensor"),
        P(None, "tensor"),
    )
    out_specs = (
        P("dp", "seq", None),
        P("dp", "seq", None),
        P(("dp", "seq"), "tensor"),
        P(),
        P(("dp", "seq", "tensor"), None),
        P(),
        P(("dp", "seq", "tensor"), None),
        P(),
        P(("dp", "seq"), "tensor"),
        P(("dp", "seq")),
        P(("dp", "seq")),
        P(("dp", "seq"), "tensor"),
        P(("dp", "seq"), "tensor"),
        P(("dp", "seq"), "tensor"),
    )
    return jax.shard_map(body, mesh=mesh, in_specs=in_specs, out_specs=out_specs, check_vma=False)
```

```python
import functools
import math

import jax
import jax.numpy as jnp
from jax import lax
from jax.experimental import pallas as pl
from jax.experimental.pallas import tpu as pltpu
from jax.sharding import PartitionSpec as P

KVH = 2
HD = 128
MOST = 1024
EPS = 1e-06
ROPE_BASE = 10000.0
NEG_FILL = -1e30
Q_BLOCK = 256
K_BLOCK = 256
MIB = 1 << 20
LIGHT = 1000
TILE = 256
PIECES = 2
SCALE = 1.0 / math.sqrt(HD)


def to_bf(value):
    return value.astype(jnp.bfloat16)


def to_f(value):
    return value.astype(jnp.float32)


def dot(left, right, left_dim=1, right_dim=0):
    return lax.dot_general(
        left,
        right,
        (((left_dim,), (right_dim,)), ((), ())),
        preferred_element_type=jnp.float32,
    )


def flipped(axis, bit):
    return [(i, i ^ (1 << bit)) for i in range(lax.axis_size(axis))]


def core_swap(value):
    return lax.ppermute(value, "tensor", flipped("tensor", 0))


def chip_swap(value):
    return lax.ppermute(value, "tensor", flipped("tensor", 1))


def core_swaps(values):
    return [core_swap(value) for value in values]


def chip_swaps(values):
    return [chip_swap(value) for value in values]


def shifted(value, hops):
    count = lax.axis_size("seq")
    route = [(i, i + hops) for i in range(count) if 0 <= i + hops < count]
    return lax.ppermute(value, "seq", route)


def cost(flops, read):
    return pl.CostEstimate(flops=flops // LIGHT, bytes_accessed=read // LIGHT, transcendentals=0)


class Order:
    def __init__(self):
        self.mark = None
        self.touched = []

    def arrived(self, *values):
        self.touched.extend(values)

    def __call__(self, kernel, args, in_specs, out_specs, out_shape, grid, flops, read, name, scalars=(), scratch=()):
        anchor = ([] if self.mark is None else [self.mark]) + self.touched
        self.touched = []
        count = len(scalars) + len(args)
        outs = len(out_shape)

        def run(*refs):
            rest = refs[count + len(anchor) :]
            kernel(*refs[:count], *rest[:outs], *rest[outs + 1 :])
            rest[outs][...] = jnp.zeros(rest[outs].shape, jnp.float32)

        *results, self.mark = pl.pallas_call(
            run,
            grid_spec=pltpu.PrefetchScalarGridSpec(
                num_scalar_prefetch=len(scalars),
                grid=grid,
                in_specs=list(in_specs) + anchors(len(anchor)),
                out_specs=list(out_specs) + [mark_spec()],
                scratch_shapes=list(scratch),
            ),
            out_shape=list(out_shape) + [MARK],
            compiler_params=pltpu.CompilerParams(vmem_limit_bytes=32 * MIB),
            cost_estimate=cost(flops, read),
            name=name,
        )(*scalars, *args, *anchor)
        return results


def first_kernel(core_ref, tok_ref, gain_ref, w_ref, b_ref, cos_ref, sin_ref, h_ref, q_ref, kv_ref):
    x = to_f(tok_ref[...])
    factor = lax.rsqrt(jnp.mean(x * x, axis=-1, keepdims=True) + EPS)
    h = to_bf(x * factor * gain_ref[...])
    h_ref[...] = h
    lin = dot(h, w_ref[...]) + b_ref[...]
    cosine = cos_ref[...]
    sine = sin_ref[...]
    heads = q_ref.shape[1] // HD
    for head in range(heads):
        part = lin[:, head * HD : (head + 1) * HD]
        q_ref[:, head * HD : (head + 1) * HD] = to_bf(
            part * cosine + pltpu.roll(part, HD // 2, 1) * sine
        )
    part = lin[:, heads * HD :]
    is_key = core_ref[0] == 0
    kv_ref[...] = to_bf(
        part * jnp.where(is_key, cosine, 1.0)
        + pltpu.roll(part, HD // 2, 1) * jnp.where(is_key, sine, 0.0)
    )


def first(core, tokens, gain, weight, bias, cosine, sine):
    total, width = tokens.shape
    columns = weight.shape[1]
    block = total // 4
    half = 2

    def flip(i, core_ref):
        return (lax.rem(i + core_ref[0] * half, 4), 0)

    def at(i, core_ref):
        return (i, 0)

    def whole(i, core_ref):
        return (0, 0)

    return pl.pallas_call(
        first_kernel,
        grid_spec=pltpu.PrefetchScalarGridSpec(
            num_scalar_prefetch=1,
            grid=(4,),
            in_specs=[
                pl.BlockSpec((block, width), flip),
                pl.BlockSpec((1, width), whole),
                pl.BlockSpec((width, columns), whole),
                pl.BlockSpec((1, columns), whole),
                pl.BlockSpec((block, HD), at),
                pl.BlockSpec((block, HD), at),
            ],
            out_specs=[
                pl.BlockSpec((block, width), at),
                pl.BlockSpec((block, columns - HD), at),
                pl.BlockSpec((block, HD), at),
            ],
        ),
        out_shape=[
            jax.ShapeDtypeStruct((total, width), jnp.bfloat16),
            jax.ShapeDtypeStruct((total, columns - HD), jnp.bfloat16),
            jax.ShapeDtypeStruct((total, HD), jnp.bfloat16),
        ],
        compiler_params=pltpu.CompilerParams(vmem_limit_bytes=32 * MIB),
        cost_estimate=cost(2 * total * width * columns, 9 * MIB),
        name="first",
    )(core, tokens, gain, weight, bias, cosine, sine)


def stacked(ref, start, count, heads):
    return jnp.concatenate(
        [ref[0, pl.ds(start, count), h * HD : (h + 1) * HD] for h in range(heads)], axis=0
    )


def bounds(start_ref, index, heads, reach):
    first_key = jnp.concatenate(
        [start_ref[0, :, pl.ds(index * Q_BLOCK, Q_BLOCK)]] * heads, axis=1
    )
    place = reach + index * Q_BLOCK + lax.broadcasted_iota(jnp.int32, (1, Q_BLOCK), 1)
    return first_key, jnp.concatenate([place] * heads, axis=1)


def gather_span(core, refs, span):
    count = len(refs) // 2
    local = refs[0].shape[1]
    for i in range(count):
        here = slice(i * local, (i + 1) * local)
        span[core, here] = refs[i][0]
        span[1 - core, here] = refs[count + i][0]


def attend_kernel(heads, blocks, pieces, low_ref, core_ref, q_ref, start_ref, *refs):
    o_ref, lse_ref, acc, span = refs[2 * pieces :]
    row = pl.program_id(0)
    wide = heads * Q_BLOCK
    reach = (pieces - 1) * q_ref.shape[1]
    gather_span(core_ref[0], refs[: 2 * pieces], span)
    for index in range(blocks):
        q = stacked(q_ref, index * Q_BLOCK, Q_BLOCK, heads)
        first_key, place = bounds(start_ref, index, heads, reach)
        acc[...] = jnp.zeros_like(acc)

        def step(j, carry):
            top, total = carry
            keys = pl.ds(pl.multiple_of(j * K_BLOCK, K_BLOCK), K_BLOCK)
            s = dot(span[0, keys], q, 1, 1) * SCALE
            key = j * K_BLOCK + lax.broadcasted_iota(jnp.int32, (K_BLOCK, wide), 0)
            s = jnp.where((key >= first_key) & (key <= place), s, NEG_FILL)
            later = jnp.maximum(top, jnp.max(s, axis=0, keepdims=True))
            p = jnp.exp(s - later)
            fade = jnp.exp(top - later)
            total = total * fade + jnp.sum(p, axis=0, keepdims=True)
            acc[...] = acc[...] * fade + dot(span[1, keys], to_bf(p), 0, 0)
            return later, total

        last = (reach + (index + 1) * Q_BLOCK - 1) // K_BLOCK + 1
        top, total = lax.fori_loop(
            low_ref[row, index],
            last,
            step,
            (jnp.full((1, wide), NEG_FILL, jnp.float32), jnp.zeros((1, wide), jnp.float32)),
        )
        out = to_bf((acc[...] / total).T)
        for h in range(heads):
            o_ref[0, index * Q_BLOCK : (index + 1) * Q_BLOCK, h * HD : (h + 1) * HD] = out[
                h * Q_BLOCK : (h + 1) * Q_BLOCK
            ]
        lse_ref[0, index : index + 1, :] = top + jnp.log(total)


def span_specs(rows, local, pieces):
    near = pl.BlockSpec((1, local, HD), lambda i, *refs: (i, 0, 0))
    far = pl.BlockSpec((1, local, HD), lambda i, *refs: (lax.rem(i + rows // 2, rows), 0, 0))
    return [near] * pieces + [far] * pieces


def attend(low, core, q, start, span, mate):
    rows, local, columns = q.shape
    pieces = len(span)
    heads = columns // HD
    blocks = local // Q_BLOCK

    def at(i, *refs):
        return (i, 0, 0)

    return pl.pallas_call(
        functools.partial(attend_kernel, heads, blocks, pieces),
        grid_spec=pltpu.PrefetchScalarGridSpec(
            num_scalar_prefetch=2,
            grid=(rows,),
            in_specs=[pl.BlockSpec((1, local, columns), at), pl.BlockSpec((1, 1, local), at)]
            + span_specs(rows, local, pieces),
            out_specs=[
                pl.BlockSpec((1, local, columns), at),
                pl.BlockSpec((1, blocks, heads * Q_BLOCK), at),
            ],
            scratch_shapes=[
                pltpu.VMEM((HD, heads * Q_BLOCK), jnp.float32),
                pltpu.VMEM((2, pieces * local, HD), jnp.bfloat16),
            ],
        ),
        out_shape=[
            jax.ShapeDtypeStruct((rows, local, columns), jnp.bfloat16),
            jax.ShapeDtypeStruct((rows, blocks, heads * Q_BLOCK), jnp.float32),
        ],
        compiler_params=pltpu.CompilerParams(vmem_limit_bytes=32 * MIB),
        cost_estimate=cost(8_000_000_000, 4 * MIB),
        name="attend",
    )(low, core, q, start, *span, *mate)


def attend_back_kernel(
    heads, blocks, pieces, low_ref, core_ref, q_ref, start_ref, g_ref, o_ref, lse_ref, cos_ref, sin_ref, *refs
):
    gq_ref, keep_ref, send_ref, acc, gk, gv, span = refs[2 * pieces :]
    row = pl.program_id(0)
    wide = heads * Q_BLOCK
    reach = (pieces - 1) * q_ref.shape[1]
    core = core_ref[0]
    gather_span(core, refs[: 2 * pieces], span)
    gk[...] = jnp.zeros_like(gk)
    gv[...] = jnp.zeros_like(gv)
    for index in range(blocks):
        q = stacked(q_ref, index * Q_BLOCK, Q_BLOCK, heads)
        g = stacked(g_ref, index * Q_BLOCK, Q_BLOCK, heads)
        o = stacked(o_ref, index * Q_BLOCK, Q_BLOCK, heads)
        inner = jnp.sum((to_f(g) * to_f(o)).T, axis=0, keepdims=True)
        lse = lse_ref[0, index : index + 1, :]
        first_key, place = bounds(start_ref, index, heads, reach)
        acc[...] = jnp.zeros_like(acc)

        def step(j, carry):
            keys = pl.ds(pl.multiple_of(j * K_BLOCK, K_BLOCK), K_BLOCK)
            k = span[0, keys]
            s = dot(k, q, 1, 1) * SCALE
            key = j * K_BLOCK + lax.broadcasted_iota(jnp.int32, (K_BLOCK, wide), 0)
            p = jnp.where((key >= first_key) & (key <= place), jnp.exp(s - lse), 0.0)
            gp = dot(span[1, keys], g, 1, 1)
            gs = to_bf(p * (gp - inner))
            gv[keys] += dot(to_bf(p), g)
            gk[keys] += dot(gs, q)
            acc[...] += dot(k, gs, 0, 0)
            return carry

        last = (reach + (index + 1) * Q_BLOCK - 1) // K_BLOCK + 1
        lax.fori_loop(low_ref[row, index], last, step, 0)
        gq = acc[...].T * SCALE
        here = slice(index * Q_BLOCK, (index + 1) * Q_BLOCK)
        cosine, sine = cos_ref[here], sin_ref[here]
        for h in range(heads):
            part = gq[h * Q_BLOCK : (h + 1) * Q_BLOCK]
            gq_ref[0, here, h * HD : (h + 1) * HD] = to_bf(
                part * cosine + pltpu.roll(part * sine, HD // 2, 1)
            )
    is_key = core == 0
    keys, values = gk[...] * SCALE, gv[...]
    keep_ref[0] = to_bf(jnp.where(is_key, keys, values))
    send_ref[0] = to_bf(jnp.where(is_key, values, keys))


def attend_back(order, low, core, q, start, span, mate, grad, out, lse, cosine, sine):
    rows, local, columns = q.shape
    pieces = len(span)
    window = pieces * local
    heads = columns // HD
    blocks = local // Q_BLOCK

    def at(i, *refs):
        return (i, 0, 0)

    table = pl.BlockSpec((local, HD), lambda i, *refs: (i, 0))
    tokens = pl.BlockSpec((1, local, columns), at)
    return order(
        functools.partial(attend_back_kernel, heads, blocks, pieces),
        [q, start, grad, out, lse, cosine, sine, *span, *mate],
        [
            tokens,
            pl.BlockSpec((1, 1, local), at),
            tokens,
            tokens,
            pl.BlockSpec((1, blocks, heads * Q_BLOCK), at),
            table,
            table,
        ]
        + span_specs(rows, local, pieces),
        [tokens, pl.BlockSpec((1, window, HD), at), pl.BlockSpec((1, window, HD), at)],
        [
            jax.ShapeDtypeStruct((rows, local, columns), jnp.bfloat16),
            jax.ShapeDtypeStruct((rows, window, HD), jnp.bfloat16),
            jax.ShapeDtypeStruct((rows, window, HD), jnp.bfloat16),
        ],
        (rows,),
        20_000_000_000,
        6 * MIB,
        "attend_back",
        scalars=(low, core),
        scratch=[
            pltpu.VMEM((HD, heads * Q_BLOCK), jnp.float32),
            pltpu.VMEM((window, HD), jnp.float32),
            pltpu.VMEM((window, HD), jnp.float32),
            pltpu.VMEM((2, window, HD), jnp.bfloat16),
        ],
    )


def fold_kernel(keep_ref, come_ref, own_ref, *send_refs):
    local = own_ref.shape[1]
    total = to_f(keep_ref[0]) + to_f(come_ref[0])
    reach = total.shape[0] - local
    own_ref[0] = total[reach:]
    for hop, ref in enumerate(send_refs, 1):
        ref[0] = to_bf(total[reach - hop * local : reach - (hop - 1) * local])


def fold(order, keep, come, local):
    rows, window = keep.shape[:2]
    hops = window // local - 1
    out = pl.BlockSpec((1, local, HD), lambda i: (i, 0, 0))
    return order(
        fold_kernel,
        [keep, come],
        [
            pl.BlockSpec((1, window, HD), lambda i: (i, 0, 0)),
            pl.BlockSpec((1, window, HD), lambda i: (lax.rem(i + rows // 2, rows), 0, 0)),
        ],
        [out] * (hops + 1),
        [jax.ShapeDtypeStruct((rows, local, HD), jnp.float32)]
        + [jax.ShapeDtypeStruct((rows, local, HD), jnp.bfloat16)] * hops,
        (rows,),
        0,
        4 * MIB,
        "fold",
    )


def carry_kernel(piece_ref, come_ref, out_ref):
    out_ref[...] = to_bf(to_f(piece_ref[...]) + to_f(come_ref[...]))


def carry(order, piece, come):
    rows, local, columns = piece.shape
    at = pl.BlockSpec((1, local, columns), lambda i: (i, 0, 0))
    return order(
        carry_kernel,
        [piece, come],
        [at, at],
        [at],
        [jax.ShapeDtypeStruct(piece.shape, jnp.bfloat16)],
        (rows,),
        0,
        2 * MIB,
        "carry",
    )[0]


def bias_kernel(left_ref, right_ref, out_ref):
    out_ref[...] = left_ref[...] + right_ref[...]


def bias_add(order, left, right):
    whole = pl.BlockSpec(left.shape, lambda i: (0, 0))
    return order(
        bias_kernel,
        [left, right],
        [whole, whole],
        [whole],
        [jax.ShapeDtypeStruct(left.shape, jnp.float32)],
        (1,),
        0,
        MIB,
        "bias",
    )[0]


def join_kernel(hops, core_ref, gq_ref, cos_ref, sin_ref, own_ref, *refs):
    out_ref, sum_ref = refs[-2:]
    columns = gq_ref.shape[2]
    grad = own_ref[0]
    for ref in refs[:hops]:
        grad = grad + to_f(ref[0])
    is_key = core_ref[0] == 0
    cosine = jnp.where(is_key, cos_ref[...], 1.0)
    sine = jnp.where(is_key, sin_ref[...], 0.0)
    kv = to_bf(grad * cosine + pltpu.roll(grad * sine, HD // 2, 1))
    q = gq_ref[0]
    out_ref[:, :columns] = q
    out_ref[:, columns:] = kv

    @pl.when(pl.program_id(0) == 0)
    def _():
        sum_ref[...] = jnp.zeros(sum_ref.shape, jnp.float32)

    sum_ref[:, :columns] += jnp.sum(to_f(q), axis=0, keepdims=True)
    sum_ref[:, columns:] += jnp.sum(to_f(kv), axis=0, keepdims=True)


def join(order, core, grad_q, own, comes, cosine, sine):
    rows, local, columns = grad_q.shape
    wide = columns + HD

    def at(i, *refs):
        return (i, 0, 0)

    piece = pl.BlockSpec((1, local, HD), at)
    table = pl.BlockSpec((local, HD), lambda i, *refs: (i, 0))
    return order(
        functools.partial(join_kernel, len(comes)),
        [grad_q, cosine, sine, own, *comes],
        [pl.BlockSpec((1, local, columns), at), table, table, piece] + [piece] * len(comes),
        [
            pl.BlockSpec((local, wide), lambda i, *refs: (i, 0)),
            pl.BlockSpec((8, wide), lambda i, *refs: (0, 0)),
        ],
        [
            jax.ShapeDtypeStruct((rows * local, wide), jnp.bfloat16),
            jax.ShapeDtypeStruct((8, wide), jnp.float32),
        ],
        (rows,),
        0,
        4 * MIB,
        "join",
        scalars=(core,),
    )


def mixed_back_kernel(w_ref, *refs):
    rows = refs[0].shape[0]
    for i, ref in enumerate(refs[:-1]):
        refs[-1][i * rows : (i + 1) * rows] = to_bf(dot(ref[...], w_ref[...]))


def mixed_back(order, pieces, weight):
    rows, width = pieces[0].shape
    total = rows * len(pieces)
    columns = weight.shape[1]

    def whole(i):
        return (0, 0)

    return order(
        mixed_back_kernel,
        [weight, *pieces],
        [pl.BlockSpec((width, columns), whole)] + [pl.BlockSpec((rows, width), whole)] * len(pieces),
        [pl.BlockSpec((total, columns), whole)],
        [jax.ShapeDtypeStruct((total, columns), jnp.bfloat16)],
        (1,),
        2 * total * width * columns,
        6 * MIB,
        "mixed_back",
    )[0]


def place_kernel(core_ref, *refs):
    for i, ref in enumerate(refs[:-1]):

        @pl.when(pl.program_id(0) == i)
        def _(ref=ref):
            refs[-1][...] = ref[...]


def place(order, core, pieces):
    rows, width = pieces[0].shape
    count = len(pieces)
    return order(
        place_kernel,
        list(pieces),
        [pl.BlockSpec((rows, width), lambda i, core_ref: (0, 0))] * count,
        [pl.BlockSpec((rows, width), lambda i, core_ref: (lax.rem(i + core_ref[0] * (count // 2), count), 0))],
        [jax.ShapeDtypeStruct((rows * count, width), pieces[0].dtype)],
        (count,),
        0,
        8 * rows * width,
        "place",
        scalars=(core,),
    )[0]


def anchors(count):
    return [pl.BlockSpec(memory_space=pl.ANY)] * count


MARK = jax.ShapeDtypeStruct((8, HD), jnp.float32)


def mark_spec():
    return pl.BlockSpec((8, HD), lambda *refs: (0, 0))


def grad_hidden_kernel(g_ref, w_ref, out_ref):
    out_ref[...] = to_bf(dot(g_ref[...], w_ref[...], 1, 1))


def grad_hidden_of(order, grad, weight):
    total, width = grad.shape
    hidden = weight.shape[0]
    return order(
        grad_hidden_kernel,
        [grad, weight],
        [pl.BlockSpec((total, width), lambda i: (0, 0)), pl.BlockSpec((TILE, width), lambda i: (i, 0))],
        [pl.BlockSpec((total, TILE), lambda i: (0, i))],
        [jax.ShapeDtypeStruct((total, hidden), jnp.bfloat16)],
        (pl.cdiv(hidden, TILE),),
        2 * total * width * hidden,
        15 * MIB,
        "grad_hidden",
    )[0]


def gated_kernel(gh_ref, gw_ref, uw_ref, *refs):
    hid_ref, gg_ref, gu_ref = refs[-3:]
    rows = refs[0].shape[0]
    for part, ref in enumerate(refs[:-3]):
        here = slice(part * rows, (part + 1) * rows)
        h = ref[...]
        gate = dot(h, gw_ref[...], 1, 1)
        up = dot(h, uw_ref[...], 1, 1)
        grad = to_f(gh_ref[here])
        sigma = 1.0 / (1.0 + jnp.exp(-gate))
        swish = gate * sigma
        hid_ref[here] = to_bf(swish * up)
        gu_ref[here] = to_bf(grad * swish)
        gg_ref[here] = to_bf(grad * up * sigma * (1.0 + gate * (1.0 - sigma)))


def gated(order, pieces, grad_hidden, gate_weight, up_weight):
    rows, width = pieces[0].shape
    total = rows * len(pieces)
    hidden = gate_weight.shape[0]
    column = pl.BlockSpec((total, TILE), lambda i: (0, i))
    weight = pl.BlockSpec((TILE, width), lambda i: (i, 0))
    shape = pltpu.HBM((total, hidden), jnp.bfloat16)
    return order(
        gated_kernel,
        [grad_hidden, gate_weight, up_weight, *pieces],
        [column, weight, weight] + [pl.BlockSpec((rows, width), lambda i: (0, 0))] * len(pieces),
        [column] * 3,
        [shape] * 3,
        (pl.cdiv(hidden, TILE),),
        4 * total * width * hidden,
        30 * MIB,
        "gated",
    )


def share_kernel(plan, lefts, rights, extra, halves, groups, pick_ref, blocks_ref, *refs):
    step = pl.program_id(0)
    left_refs, right_refs = refs[:lefts], refs[lefts : lefts + rights]
    refs = refs[lefts + rights :]
    if extra:
        extra_ref, refs = refs[0], refs[1:]
    for left, right, begin, end, shift, columns, target in plan:

        @pl.when((step >= begin) & (step < end))
        def _(left=left, right=right, shift=shift, columns=columns, target=target):
            out = dot(left_refs[left][...], right_refs[right][...])
            if extra:
                out = out + to_f(extra_ref[...])
            tile = out.shape[1]
            spot = (step + shift) * tile + lax.broadcasted_iota(jnp.int32, (1, tile), 1)
            out = to_bf(jnp.where(spot < columns, out, 0.0))
            if groups:
                share = out.shape[0] // (groups[0] * groups[1])
                for i in range(groups[0]):
                    for j in range(groups[1]):
                        here = (j * groups[0] + i) * share
                        there = (i * groups[1] + j) * share
                        refs[target][here : here + share] = out[there : there + share]
                return
            if not halves:
                refs[target][...] = out
                return
            send_ref, keep_ref, rows = refs
            rows[...] = out
            share = send_ref.shape[0] // (2 * halves)
            for i in range(2 * halves):
                here = slice(i * share, (i + 1) * share)
                send_ref[here] = rows[pl.ds(pl.multiple_of(blocks_ref[i] * share, share), share)]
                keep_ref[here] = rows[pl.ds(pl.multiple_of(blocks_ref[2 * halves + i] * share, share), share)]


def clipped(rows, tile, begin, count, shift=0):
    return pl.BlockSpec((rows, tile), lambda i, *refs: (0, jnp.clip(i - begin, 0, count - 1) + shift))


def share_of(order, lefts, rights, parts, part, pick, tile, extra=None, blocks=None, groups=None):
    tokens = lefts[0].shape[1]
    plan, at = [], 0
    starts, sizes, right_at = {}, {}, {}
    for left, right, skip, count, target in parts:
        plan.append((left, right, at, at + count, skip - at, rights[right].shape[1], target))
        starts.setdefault(target, at)
        sizes[target] = sizes.get(target, 0) + count
        first, tiles, low = right_at.get(right, (at, 0, skip))
        right_at[right] = (first, tiles + count, low)
        at += count
    halves = 0
    extras = [] if extra is None else [extra]
    scratch = []
    if blocks is None:
        blocks = jnp.zeros((1,), jnp.int32)
        outs = [clipped(part, tile, starts[t], sizes[t]) for t in sorted(sizes)]
        shapes = [jax.ShapeDtypeStruct((part, sizes[t] * tile), jnp.bfloat16) for t in sorted(sizes)]
    else:
        halves = blocks.shape[0] // 4
        outs = [clipped(part // 2, tile, 0, at)] * 2
        shapes = [jax.ShapeDtypeStruct((part // 2, at * tile), jnp.bfloat16)] * 2
        scratch = [pltpu.VMEM((part, tile), jnp.bfloat16)]
    return order(
        functools.partial(share_kernel, plan, len(lefts), len(rights), len(extras), halves, groups),
        [*lefts, *rights, *extras],
        [pl.BlockSpec((part, tokens), lambda i, pick_ref, blocks_ref: (pick_ref[0], 0))] * len(lefts)
        + [clipped(tokens, tile, *right_at[r]) for r in range(len(rights))]
        + [clipped(part, tile, 0, at)] * len(extras),
        outs,
        shapes,
        (at,),
        2 * part * tokens * at * tile,
        2 * (part * tokens + (part + tokens) * at * tile),
        "share",
        scalars=(jnp.asarray(pick, jnp.int32).reshape(1), blocks),
        scratch=scratch,
    )


def relay_kernel(keep_ref, come_ref, out_ref):
    out_ref[...] = to_bf(to_f(keep_ref[...]) + to_f(come_ref[...]))


def relay(order, keep, come, share):
    rows, columns = keep.shape
    pair = pl.BlockSpec((share, columns), lambda i: (2 * i + 1, 0))
    return order(
        relay_kernel,
        [keep, come],
        [pair, pair],
        [pl.BlockSpec((share, columns), lambda i: (i, 0))],
        [jax.ShapeDtypeStruct((rows // 2, columns), jnp.bfloat16)],
        (rows // (2 * share),),
        0,
        3 * rows * columns,
        "relay",
    )[0]


def finish_kernel(plan, columns, gains, *refs):
    out_ref = refs[-2] if gains else refs[-1]
    step = pl.program_id(0)
    tile = out_ref.shape[1]
    for begin, end, first, count in plan:

        @pl.when((step >= begin) & (step < end))
        def _(first=first, count=count):
            out = to_f(refs[first][...])
            for ref in refs[first + 1 : first + count]:
                out = out + to_f(ref[...])
            out_ref[...] = out
            if gains:
                spot = step * tile + lax.broadcasted_iota(jnp.int32, (1, tile), 1)
                terms = jnp.where(spot < columns, out * to_f(refs[-3][...]), 0.0)
                total = terms[:, :HD]
                for i in range(HD, tile, HD):
                    total = total + terms[:, i : i + HD]

                @pl.when(step == 0)
                def _():
                    refs[-1][...] = total

                @pl.when(step > 0)
                def _():
                    refs[-1][...] += total


def finish(order, chunks, share, columns, tile, weight=None):
    plan, specs, args, at = [], [], [], 0
    for chunk in chunks:
        count = chunk[0].shape[1] // tile
        plan.append((at, at + count, len(args), len(chunk)))
        specs += [clipped(share, tile, at, count)] * len(chunk)
        args += chunk
        at += count
    column = pl.BlockSpec((share, tile), lambda i: (0, i))
    outs, shapes = [column], [jax.ShapeDtypeStruct((share, columns), jnp.float32)]
    if weight is not None:
        args.append(weight)
        specs.append(column)
        outs.append(pl.BlockSpec((share, HD), lambda i: (0, 0)))
        shapes.append(jax.ShapeDtypeStruct((share, HD), jnp.float32))
    return order(
        functools.partial(finish_kernel, plan, columns, weight is not None),
        args,
        specs,
        outs,
        shapes,
        (at,),
        0,
        14 * share * columns,
        "finish",
    )


def narrow_kernel(pairs, extras, right_dim, *refs):
    out = dot(refs[0][...], refs[1][...], 1, right_dim)
    for i in range(1, pairs):
        out = out + dot(refs[2 * i][...], refs[2 * i + 1][...], 1, right_dim)
    extra = refs[2 * pairs : 2 * pairs + extras]
    outs = refs[2 * pairs + extras :]
    if extras:
        out = out + jnp.concatenate([to_f(ref[...]) for ref in extra], axis=0)
    rows = outs[0].shape[0]
    for i, ref in enumerate(outs):
        ref[...] = to_bf(out[i * rows : (i + 1) * rows])


def narrow(order, pairs, index, extra=(), right_dim=0):
    total, hidden = pairs[0][0].shape
    width = pairs[0][1].shape[1 - right_dim]
    half = total // 2
    piece = half // PIECES
    column = pl.BlockSpec((piece, TILE), lambda i: (0, i))
    right = (
        pl.BlockSpec((TILE, hidden), lambda i: (i, 0))
        if right_dim
        else pl.BlockSpec((hidden, TILE), lambda i: (0, i))
    )
    return order(
        functools.partial(narrow_kernel, len(pairs), len(extra), right_dim),
        [item for pair in pairs for item in pair] + list(extra),
        [pl.BlockSpec((half, hidden), lambda i: (index, 0)), right] * len(pairs) + [column] * len(extra),
        [column] * PIECES,
        [jax.ShapeDtypeStruct((piece, width), jnp.bfloat16)] * PIECES,
        (width // TILE,),
        2 * len(pairs) * half * width * hidden,
        2 * len(pairs) * (half + width) * hidden + 2 * half * width,
        "narrow",
    )


def piece_specs(piece, width, block):
    steps = piece // block
    return [
        pl.BlockSpec((block, width), lambda i, *refs, j=j: (jnp.clip(i - j * steps, 0, steps - 1), 0))
        for j in range(PIECES)
    ]


def pick_piece(refs):
    value = refs[0][...]
    for j, ref in enumerate(refs[1:], 1):
        value = jnp.where(pl.program_id(0) >= 4 * j // len(refs), ref[...], value)
    return value


def put_piece(refs, value):
    steps = 4 // len(refs)
    for j, ref in enumerate(refs):

        @pl.when(lax.div(pl.program_id(0), steps) == j)
        def _(ref=ref):
            ref[...] = value


def turn_kernel(*refs):
    rows = refs[0].shape[0]
    for i, ref in enumerate(refs[:-1]):
        refs[-1][:, i * rows : (i + 1) * rows] = ref[...].T


def turn(order, pieces):
    rows, width = pieces[0].shape
    total = rows * len(pieces)
    return order(
        turn_kernel,
        list(pieces),
        [pl.BlockSpec((rows, TILE), lambda i: (0, i))] * len(pieces),
        [pl.BlockSpec((TILE, total), lambda i: (i, 0))],
        [jax.ShapeDtypeStruct((width, total), jnp.bfloat16)],
        (width // TILE,),
        0,
        4 * total * width,
        "turn",
    )[0]


def grad_out_kernel(core_ref, cot_ref, valid_ref, out_ref, turned_ref):
    out = to_bf(to_f(cot_ref[...]) * valid_ref[...])
    out_ref[...] = out
    turned_ref[...] = out.T


def grad_out_of(order, core, cotangent, valid):
    total, width = cotangent.shape
    block = total // 4
    return order(
        grad_out_kernel,
        [cotangent, valid],
        [
            pl.BlockSpec((block, width), lambda i, core_ref: (lax.rem(i + core_ref[0] * 2, 4), 0)),
            pl.BlockSpec((block, 1), lambda i, core_ref: (i, 0)),
        ],
        [
            pl.BlockSpec((block, width), lambda i, core_ref: (i, 0)),
            pl.BlockSpec((width, block), lambda i, core_ref: (0, i)),
        ],
        [
            jax.ShapeDtypeStruct((total, width), jnp.bfloat16),
            jax.ShapeDtypeStruct((width, total), jnp.bfloat16),
        ],
        (4,),
        0,
        6 * total * width,
        "grad_out",
        scalars=(core,),
    )


def middle_kernel(core_ref, tok_ref, gain_ref, *refs):
    mine, come = pick_piece(refs[:PIECES]), pick_piece(refs[PIECES : 2 * PIECES])
    mid_ref, *h_refs = refs[2 * PIECES :]
    middle = to_f(tok_ref[...]) + (to_f(mine) + to_f(come))
    factor = lax.rsqrt(jnp.mean(middle * middle, axis=-1, keepdims=True) + EPS)
    mid_ref[...] = middle
    put_piece(h_refs, to_bf(middle * factor * gain_ref[...]))


def middle_of(order, core, tokens, mine, come, gain):
    piece, width = mine[0].shape
    half = piece * PIECES
    block = half // 4
    specs = piece_specs(piece, width, block)
    middle, *h = order(
        middle_kernel,
        [tokens, gain, *mine, *come],
        [
            pl.BlockSpec((block, width), lambda i, core_ref: (core_ref[0] * 4 + i, 0)),
            pl.BlockSpec((1, width), lambda i, core_ref: (0, 0)),
        ]
        + specs * 2,
        [pl.BlockSpec((block, width), lambda i, core_ref: (i, 0))] + specs,
        [jax.ShapeDtypeStruct((half, width), jnp.float32)]
        + [jax.ShapeDtypeStruct((piece, width), jnp.bfloat16)] * PIECES,
        (4,),
        0,
        9 * MIB,
        "middle",
        scalars=(core,),
    )
    return middle, h


def norm_back_kernel(core_ref, x_ref, gain_ref, up_ref, *refs):
    mine, come = pick_piece(refs[:PIECES]), pick_piece(refs[PIECES : 2 * PIECES])
    outs = refs[2 * PIECES :]
    grad = to_f(mine) + to_f(come)
    x = to_f(x_ref[...])
    factor = lax.rsqrt(jnp.mean(x * x, axis=-1, keepdims=True) + EPS)
    normed = x * factor
    weighted = grad * gain_ref[...]
    inner = jnp.mean(weighted * normed, axis=-1, keepdims=True)
    out = to_f(up_ref[...]) + factor * (weighted - normed * inner)
    if len(outs) > PIECES:
        outs[0][...] = out
        put_piece(outs[1:], to_bf(out))
    else:
        put_piece(outs, out)


def norm_back(order, core, mine, come, x, gain, up, by_core):
    piece, width = mine[0].shape
    half = piece * PIECES
    block = half // 4
    at = pl.BlockSpec((block, width), lambda i, core_ref: (i, 0))
    picked = pl.BlockSpec((block, width), lambda i, core_ref: (core_ref[0] * 4 + i, 0))
    specs = piece_specs(piece, width, block)
    if by_core:
        shapes = [jax.ShapeDtypeStruct((piece, width), jnp.float32)] * PIECES
    else:
        shapes = [jax.ShapeDtypeStruct((half, width), jnp.float32)]
        shapes += [jax.ShapeDtypeStruct((piece, width), jnp.bfloat16)] * PIECES
    return order(
        norm_back_kernel,
        [x, gain, up, *mine, *come],
        [picked if by_core else at, pl.BlockSpec((1, width), lambda i, core_ref: (0, 0)), at] + specs * 2,
        specs if by_core else [at] + specs,
        shapes,
        (4,),
        0,
        10 * MIB,
        "norm_back",
        scalars=(core,),
    )


def layer_kernel(middle_ref, *refs):
    mine, come = pick_piece(refs[:PIECES]), pick_piece(refs[PIECES : 2 * PIECES])
    put_piece(refs[2 * PIECES :], to_bf(middle_ref[...] + (to_f(mine) + to_f(come))))


def layer_of(order, middle, mine, come):
    piece, width = mine[0].shape
    block = piece * PIECES // 4
    specs = piece_specs(piece, width, block)
    return order(
        layer_kernel,
        [middle, *mine, *come],
        [pl.BlockSpec((block, width), lambda i: (i, 0))] + specs * 2,
        specs,
        [jax.ShapeDtypeStruct((piece, width), jnp.bfloat16)] * PIECES,
        (4,),
        0,
        5 * MIB,
        "layer",
    )


def tensor_gather(value, rank):
    mate = core_swap(value)
    pair = jnp.where(lax.rem(rank, 2) == 0, jnp.stack([value, mate]), jnp.stack([mate, value]))
    come = chip_swap(pair)
    return jnp.where(
        lax.div(rank, 2) == 0,
        jnp.concatenate([pair, come], axis=0),
        jnp.concatenate([come, pair], axis=0),
    )


def body(
    tokens,
    lengths,
    cotangent,
    q_weight,
    q_bias,
    k_weight,
    k_bias,
    v_weight,
    v_bias,
    o_weight,
    attn_gain,
    ffn_gain,
    gate_weight,
    up_weight,
    down_weight,
):
    rows, local, width = tokens.shape
    total = rows * local
    half = total // 2
    heads = q_weight.shape[1] // HD
    ranks = lax.axis_size("tensor")
    seqs = lax.axis_size("seq")
    rank = lax.axis_index("tensor")
    dp_index = lax.axis_index("dp")
    seq_index = lax.axis_index("seq")
    core = lax.rem(rank, 2)
    head = lax.div(rank, 2)
    core_one = core.reshape(1)
    hops = min(seqs - 1, -(-(MOST - 1) // local))
    reach = hops * local

    def own_first(value):
        turned = jnp.concatenate([value[rows // 2 :], value[: rows // 2]], axis=0)
        return jnp.where(core == 0, value, turned)

    slots = jnp.arange(lengths.shape[1], dtype=jnp.int32)
    lens = own_first(lengths)
    ends = jnp.sum(jnp.where(slots[None, :] <= slots[:, None], lens[:, None, :], 0), axis=2)
    spot = seq_index * local + jnp.arange(local, dtype=jnp.int32)
    begun = jnp.max(
        jnp.where(ends[:, None, :] <= spot[None, :, None], ends[:, None, :], 0), axis=2
    )
    valid = to_f(spot[None, :] < ends[:, -2:-1])
    position = (spot[None, :] - begun).reshape(total, 1)
    freqs = ROPE_BASE ** (-(jnp.arange(HD // 2, dtype=jnp.float32) * 2.0) / HD)
    angles = to_f(position) * freqs[None, :]
    cosine, sine = jnp.cos(angles), jnp.sin(angles)
    cosine = jnp.concatenate([cosine, cosine], axis=1)
    sine = jnp.concatenate([-sine, sine], axis=1)
    start = begun - (seq_index * local - reach)
    low = jnp.maximum(lax.div(jnp.maximum(start[:, ::Q_BLOCK], 0), K_BLOCK), 0)
    start = start.reshape(rows, 1, local)

    key_side = core == 0
    kv_weight = jnp.where(
        key_side,
        lax.dynamic_slice_in_dim(k_weight, head * HD, HD, 1),
        lax.dynamic_slice_in_dim(v_weight, head * HD, HD, 1),
    )
    kv_bias = jnp.where(
        key_side,
        lax.dynamic_slice_in_dim(k_bias, head * HD, HD, 0),
        lax.dynamic_slice_in_dim(v_bias, head * HD, HD, 0),
    )
    weight = jnp.concatenate([q_weight, kv_weight], axis=1)
    bias = to_f(jnp.concatenate([q_bias, kv_bias])).reshape(1, -1)
    gain_one = to_f(attn_gain).reshape(1, width)
    gain_two = to_f(ffn_gain).reshape(1, width)

    h_one, q_rot, kv = first(
        core_one, tokens.reshape(total, width), gain_one, weight, bias, cosine, sine
    )
    kv = kv.reshape(rows, local, HD)
    span = [shifted(kv, h) for h in range(hops, 0, -1)] + [kv]
    mate = [core_swap(piece) for piece in span]
    q_rows = q_rot.reshape(rows, local, heads * HD)
    mixed_rows, lse = attend(low, core_one, q_rows, start, span, mate)
    mixed = mixed_rows.reshape(total, heads * HD)

    order = Order()
    flat_tokens = tokens.reshape(total, width)
    dps = lax.axis_size("dp")
    near_pair = dps == 2 and seqs == 4
    part = width // dps
    share = part // seqs
    gate_t, up_t, down_t = gate_weight.T, up_weight.T, down_weight.T
    units = gate_t.shape[0]
    tiles = -(-units // TILE)
    cut = (tiles + 1) // 2
    long = -(-2 * tiles // 3)
    one, two = seq_index ^ 1, seq_index ^ 2
    three = seq_index ^ 3
    quad = jnp.stack([one, three, seq_index, two])

    begin = (dp_index * seqs + seq_index) * share

    def rows_of(value):
        return lax.dynamic_slice_in_dim(value, begin, share, 0)

    class Rows:
        def __init__(self, lefts, rights, parts, tile=TILE, sent=None):
            self.args = (order, lefts, rights, parts)
            self.tile = tile
            if not near_pair:
                (whole,) = share_of(*self.args, width, 0, tile)
                self.whole = lax.psum_scatter(whole, ("dp", "seq"), scatter_dimension=0, tiled=True)
                return
            if sent is None:
                (sent,) = share_of(*self.args, part, 1 - dp_index, tile)
            self.come = lax.ppermute(sent, "dp", flipped("dp", 0))

        def own(self):
            if near_pair:
                send, self.keep = share_of(*self.args, part, dp_index, self.tile, self.come, quad)
                self.come = lax.ppermute(send, "seq", flipped("seq", 0))

        def relay(self):
            if near_pair:
                sent = relay(order, self.keep, self.come, share)
                self.last = lax.ppermute(sent, "seq", flipped("seq", 1))

        def settled(self):
            if near_pair:
                order.arrived(self.last)

        def result(self):
            return [self.keep, self.come, self.last] if near_pair else [self.whole]

    class SeqFirst(Rows):
        def __init__(self, lefts, rights, parts, tile=TILE):
            if not near_pair:
                super().__init__(lefts, rights, parts, tile)
                return
            (whole,) = share_of(order, lefts, rights, parts, width, 0, tile, None, None, (dps, seqs))
            self.mine = lax.psum_scatter(whole, "seq", scatter_dimension=0, tiled=True)

        def across(self):
            if near_pair:
                sent = lax.dynamic_slice_in_dim(self.mine, (1 - dp_index) * share, share, 0)
                self.mine = lax.dynamic_slice_in_dim(self.mine, dp_index * share, share, 0)
                order.arrived(sent, self.mine)
                self.come = lax.ppermute(sent, "dp", flipped("dp", 0))

        def settled(self):
            if near_pair:
                order.arrived(self.come)

        def result(self):
            return [self.mine, self.come] if near_pair else [self.whole]

    class Scattered(Rows):
        def own(self):
            if near_pair:
                (mine,) = share_of(*self.args, part, dp_index, self.tile, self.come)
                self.whole = lax.psum_scatter(mine, "seq", scatter_dimension=0, tiled=True)

        def settled(self):
            order.arrived(self.whole)

        def result(self):
            return [self.whole]

    sent = core_swaps(narrow(order, [(mixed, o_weight)], 1, (), 1))
    mine = narrow(order, [(mixed, o_weight)], 0, sent, 1)
    come = chip_swaps(mine)
    grad_ffn, grad_ffn_t = grad_out_of(
        order, core_one, cotangent.reshape(total, width), valid.reshape(total, 1)
    )
    gate_rows, up_rows = rows_of(gate_weight), rows_of(up_weight)
    order.arrived(gate_rows, up_rows)
    grad_hidden = grad_hidden_of(order, grad_ffn, down_t)
    h_one_t = turn(order, [h_one])
    middle, h_two = middle_of(order, core_one, flat_tokens, mine, come, gain_two)
    h_two += core_swaps(h_two)
    hidden, grad_gate, grad_up = gated(order, h_two, grad_hidden, gate_t, up_t)

    down_b = SeqFirst([grad_ffn_t], [hidden], [(0, 0, cut, tiles - cut, 0)])
    down_a = Rows([grad_ffn_t], [hidden], [(0, 0, 0, cut, 0)])
    pairs = [(grad_gate, gate_t), (grad_up, up_t)]
    sent = core_swaps(narrow(order, pairs, 1))
    mine = narrow(order, pairs, 0, sent)
    come = chip_swaps(mine)
    h_two_t = turn(order, h_two)
    if near_pair:
        sends = share_of(
            order,
            [h_two_t],
            [grad_gate, grad_up],
            [(0, 0, 0, tiles, 0), (0, 1, 0, long, 1), (0, 1, long, tiles - long, 2)],
            part,
            1 - dp_index,
            TILE,
        )
    else:
        sends = [None] * 3

    def half_rows(kind, right, begin, end, sent):
        return kind([h_two_t], [right], [(0, 0, begin, end - begin, 0)], TILE, sent)

    gate = half_rows(Scattered, grad_gate, 0, tiles, sends[0])
    up_a = half_rows(Rows, grad_up, 0, long, sends[1])
    up_b = half_rows(Rows, grad_up, long, tiles, sends[2])
    down_a.own()
    grad_middle, *branch = norm_back(order, core_one, mine, come, middle, gain_two, grad_ffn, False)
    branch += core_swaps(branch)
    grad_mixed = mixed_back(order, branch, o_weight).reshape(rows, local, heads * HD)
    grad_q_rows, keep, sent = attend_back(
        order, low, core_one, q_rows, start, span, mate, grad_mixed, mixed_rows, lse, cosine, sine
    )
    both_come = core_swap(sent)
    branch_t = turn(order, branch)
    down_a.relay()
    own_kv, *pieces = fold(order, keep, both_come, local)
    moving = shifted(pieces[-1], -1) if pieces else None
    ffn_sent = core_swaps(narrow(order, [(hidden, down_t)], 1))
    for piece in pieces[-2::-1]:
        moving = shifted(carry(order, piece, moving), -1)
    grad_qkv, bias_sum = join(
        order, core_one, grad_q_rows, own_kv, [] if moving is None else [moving], cosine, sine
    )
    sent = core_swaps(narrow(order, [(grad_qkv, weight)], 1, (), 1))
    down_b.across()
    mine = narrow(order, [(grad_qkv, weight)], 0, sent, 1)
    come = chip_swaps(mine)
    gate.own()
    last_parts = [(0, 0, 0, grad_qkv.shape[1] // HD, 0), (1, 1, 0, heads, 0)]
    last = Rows([h_one_t, branch_t], [grad_qkv, mixed], last_parts, HD)
    ffn_mine = narrow(order, [(hidden, down_t)], 0, ffn_sent)
    token = norm_back(order, core_one, mine, come, flat_tokens, gain_one, grad_middle, True)
    token += core_swaps(token)
    ffn_come = chip_swaps(ffn_mine)
    up_a.own()
    token_grad = place(order, core_one, token).reshape(rows, local, width)
    layer = layer_of(order, middle, ffn_mine, ffn_come)
    layer += core_swaps(layer)
    last.own()
    layer_out = place(order, core_one, layer).reshape(rows, local, width)
    up_a.relay()
    down_a.settled()
    up_b.own()
    down_b.settled()
    up_a.settled()
    last.relay()
    (down_grad,) = finish(order, [down_a.result(), down_b.result()], share, units, TILE)
    if near_pair:
        bias_come = lax.ppermute(bias_sum, "dp", flipped("dp", 0))
        bias_all = bias_add(order, bias_sum, bias_come)
        bias_come = lax.ppermute(bias_all, "seq", flipped("seq", 0))
    up_b.relay()
    gate_grad, gate_term = finish(order, [gate.result()], share, units, TILE, gate_rows)
    wide_columns = grad_qkv.shape[1]
    (last_grad,) = finish(order, [last.result()], share, wide_columns + heads * HD, HD)
    if near_pair:
        bias_all = bias_add(order, bias_all, bias_come)
        bias_come = lax.ppermute(bias_all, "seq", flipped("seq", 1))
        bias_all = (bias_all + bias_come)[:1]
    else:
        bias_all = lax.psum(bias_sum[:1], ("dp", "seq"))
    up_grad, up_term = finish(order, [up_a.result(), up_b.result()], share, units, TILE, up_rows)
    qkv_grad, o_grad = last_grad[:, :wide_columns], last_grad[:, wide_columns:]

    attn_term = jnp.sum(to_f(rows_of(weight)) * qkv_grad, axis=1)
    ffn_term = jnp.sum(gate_term + up_term, axis=1)
    columns = heads * HD
    room = -(-share // HD) * HD - share
    terms = jnp.pad(jnp.stack([ffn_term, attn_term]), ((0, 0), (0, room))).reshape(-1, HD)
    packed = jnp.concatenate([qkv_grad[:, columns:], bias_all.reshape(-1, HD), terms], axis=0)
    gathered = tensor_gather(packed, rank)
    term_rows = terms.shape[0]
    bias_count = bias_all.shape[1] // HD
    terms = gathered[:, share + bias_count :].reshape(ranks, 2, -1)[:, :, :share]
    ffn_gain_grad, attn_gain_grad = terms[0] + terms[1] + (terms[2] + terms[3])
    attn_gain_grad = attn_gain_grad / lax.dynamic_slice_in_dim(gain_one[0], begin, share, 0)
    ffn_gain_grad = ffn_gain_grad / lax.dynamic_slice_in_dim(gain_two[0], begin, share, 0)
    q_grad = qkv_grad[:, :columns]
    kv_parts = lax.dynamic_slice_in_dim(gathered, rank * (share // ranks), share // ranks, 1)
    k_grad = jnp.concatenate([kv_parts[2 * i] for i in range(KVH)], axis=1)
    v_grad = jnp.concatenate([kv_parts[2 * i + 1] for i in range(KVH)], axis=1)
    biases = gathered[:, share : share + bias_count]
    q_bias_grad = biases[:, :heads].reshape(-1)
    k_bias_grad = biases[0::2, heads].reshape(-1)
    v_bias_grad = biases[1::2, heads].reshape(-1)
    return (
        layer_out,
        token_grad,
        q_grad,
        q_bias_grad,
        k_grad,
        k_bias_grad,
        v_grad,
        v_bias_grad,
        o_grad,
        attn_gain_grad,
        ffn_gain_grad,
        gate_grad,
        up_grad,
        down_grad,
    )


def solution(mesh):
    in_specs = (
        P("dp", "seq", None),
        P("dp", None),
        P("dp", "seq", None),
        P(None, "tensor"),
        P("tensor"),
        P(),
        P(),
        P(),
        P(),
        P(None, "tensor"),
        P(),
        P(),
        P(None, "tensor"),
        P(None, "tensor"),
        P(None, "tensor"),
    )
    out_specs = (
        P("dp", "seq", None),
        P("dp", "seq", None),
        P(("dp", "seq"), "tensor"),
        P(),
        P(("dp", "seq", "tensor"), None),
        P(),
        P(("dp", "seq", "tensor"), None),
        P(),
        P(("dp", "seq"), "tensor"),
        P(("dp", "seq")),
        P(("dp", "seq")),
        P(("dp", "seq"), "tensor"),
        P(("dp", "seq"), "tensor"),
        P(("dp", "seq"), "tensor"),
    )
    return jax.shard_map(body, mesh=mesh, in_specs=in_specs, out_specs=out_specs, check_vma=False)
```
